32 devices in a mesh: dp: 16 (over z, x, core), sp: 2 (over y).
Axes of the slice: x: 2, y: 2, z: 4, core: 2. Of those that a mesh axis runs over, the one named last changes fastest.
Arguments:
- inputs: bfloat16 [16, 1024, 768], P('dp', 'sp'), may hold values from -6 to 6
- memory: bfloat16 [16, 1024, 768], P('dp', 'sp'), may hold values from -6 to 6
- target_docs: int32 [16, 1024], P('dp', 'sp'), may hold values from 0 to 3, as said below
- memory_docs: int32 [16, 1024], P('dp', 'sp'), may hold values from 0 to 3, as said below
- cotangent: bfloat16 [16, 1024, 768], P('dp', 'sp'), may hold values from -6 to 6
- self_query_key_value_weight: bfloat16 [768, 2304], replicated, may hold values from -0.21875 to 0.21875
- self_query_bias: bfloat16 [768], replicated, may hold values from -1.25 to 1.25
- self_value_bias: bfloat16 [768], replicated, may hold values from -1.25 to 1.25
- self_output_weight: bfloat16 [768, 768], replicated, may hold values from -0.875 to 0.875
- self_out_bias: bfloat16 [768], replicated, may hold values from -1.25 to 1.25
- norm_one_gain: bfloat16 [768], replicated, may hold values from 0.5 to 1.5
- norm_one_shift: bfloat16 [768], replicated, may hold values from -1.25 to 1.25
- cross_query_matrix: bfloat16 [768, 768], replicated, may hold values from -0.21875 to 0.21875
- cross_query_bias: bfloat16 [768], replicated, may hold values from -1.25 to 1.25
- cross_key_value_weight: bfloat16 [768, 1536], replicated, may hold values from -0.21875 to 0.21875
- cross_value_bias: bfloat16 [768], replicated, may hold values from -1.25 to 1.25
- cross_output_weight: bfloat16 [768, 768], replicated, may hold values from -0.875 to 0.875
- cross_out_bias: bfloat16 [768], replicated, may hold values from -1.25 to 1.25
- norm_two_gain: bfloat16 [768], replicated, may hold values from 0.5 to 1.5
- norm_two_shift: bfloat16 [768], replicated, may hold values from -1.25 to 1.25
- feed_input_weight: bfloat16 [768, 3072], replicated, may hold values from -0.21875 to 0.21875
- feed_in_bias: bfloat16 [3072], replicated, may hold values from -1.25 to 1.25
- feed_output_weight: bfloat16 [3072, 768], replicated, may hold values from -0.109375 to 0.109375
- feed_out_bias: bfloat16 [768], replicated, may hold values from -1.25 to 1.25
- norm_three_gain: bfloat16 [768], replicated, may hold values from 0.5 to 1.5
- norm_three_shift: bfloat16 [768], replicated, may hold values from -1.25 to 1.25
Outputs:
- output: bfloat16 [16, 1024, 768], P('dp', 'sp')
- derivative_arguments: bfloat16 [16, 1024, 768], P('dp', 'sp')
- grad_memory: bfloat16 [16, 1024, 768], P('dp', 'sp')
- grad_self_qkv_weight: float32 [768, 2304], P('dp')
- grad_self_query_bias: float32 [768], P('dp')
- grad_self_value_bias: float32 [768], P('dp')
- grad_self_out_weight: float32 [768, 768], P('dp')
- grad_self_out_bias: float32 [768], P('dp')
- grad_norm_one_gain: float32 [768], P('dp')
- grad_norm_one_shift: float32 [768], P('dp')
- grad_cross_query_weight: float32 [768, 768], P('dp')
- grad_cross_query_bias: float32 [768], P('dp')
- grad_cross_memory_weight: float32 [768, 1536], P('dp')
- grad_cross_value_bias: float32 [768], P('dp')
- grad_cross_out_weight: float32 [768, 768], P('dp')
- derivative_encoder_exit_offset: float32 [768], P('dp')
- grad_norm_two_gain: float32 [768], P('dp')
- grad_norm_two_shift: float32 [768], P('dp')
- grad_feed_in_weight: float32 [768, 3072], P('dp')
- grad_feed_in_bias: float32 [3072], P('dp')
- grad_feed_out_weight: float32 [3072, 768], P('dp')
- grad_feed_out_bias: float32 [768], P('dp')
- grad_norm_three_gain: float32 [768], P('dp')
- grad_norm_three_shift: float32 [768], P('dp')
The draws below stay inside these ranges and needn't reach their ends.
Inputs may be any that keep to these rules, and one draw needn't show every extreme that they name: `target_docs`: each row's document numbers never fall and take every value from 0 to 3 at one or more positions; the document at positions 511 and 512 is the same. `memory_docs`: each row's document numbers never fall and take every value from 0 to 3 at one or more positions; the document at positions 511 and 512 is the same.
All inputs are finite; a program needn't handle non-finite values.
Results may differ from the reference program's by a relative error of at most 0.023.
Values may be sent and summed in bfloat16 or wider, within the bound.
A program may use at most 256 MiB of HBM per device.

```python
import jax
import jax.numpy as jnp
from jax import lax

D = 768
H = 12
HD = 64
FF = 3072
LEN = 1024
MLEN = 1024
DOCS = 4
BATCH = 16


def document_rows(key, rows, length, docs):
    middle = length // 2
    keys = jax.random.split(key, rows)

    def single(row_key):
        order = jax.random.permutation(row_key, length - 2)[:docs - 1] + 1
        cuts = jnp.where(order >= middle, order + 1, order)
        places = jnp.arange(length, dtype=jnp.int32)
        return jnp.sum((cuts[None, :] <= places[:, None]).astype(jnp.int32), axis=1)
    return jax.vmap(single)(keys).astype(jnp.int32)


def draw_target_docs(key, part):
    key = jax.random.fold_in(key, 11)
    return document_rows(key, BATCH, LEN, DOCS)


def draw_memory_docs(key, part):
    key = jax.random.fold_in(key, 12)
    return document_rows(key, BATCH, MLEN, DOCS)


def steps_of(key, dims, shards, smallest, largest):
    def one(axis_at, parts):
        heights = jax.random.uniform(jax.random.fold_in(jax.random.fold_in(key, 6), axis_at), (parts,), jnp.float32, smallest / len(shards), largest / len(shards))
        return jnp.repeat(jnp.exp(heights), dims[axis_at] // parts).reshape((-1,) + (1,) * (len(dims) - axis_at - 1))

    level = one(*shards[0])
    for cut in shards[1:]:
        level = level * one(*cut)
    return level


def scatter_about(own_key, extent, scale, limit, shards=(), held_as=jnp.bfloat16):
    factor_of = steps_of(own_key, extent, shards, -0.22, 0.18) if shards else 1.0
    values = jax.random.normal(own_key, extent, jnp.float32) * scale * factor_of
    return jnp.minimum(jnp.maximum(values, -limit), limit).astype(held_as)


def setup_inputs(seed: int = 0) -> dict:
    key_list = jax.random.split(jax.random.key(seed), 27)
    return {
        "inputs": scatter_about(key_list[0], (BATCH, LEN, D), 1.0, 6.0, ((0, 16), (1, 2))),
        "memory": scatter_about(key_list[1], (BATCH, MLEN, D), 1.0, 6.0, ((0, 16), (1, 2))),
        "target_docs": draw_target_docs(jax.random.fold_in(key_list[26], 71), 0),
        "memory_docs": draw_memory_docs(jax.random.fold_in(key_list[26], 71), 0),
        "cotangent": scatter_about(key_list[4], (BATCH, LEN, D), 1.0, 6.0, ((0, 16), (1, 2))),
        "self_query_key_value_weight": scatter_about(key_list[5], (D, 3 * D), D ** -0.5, 0.21875),
        "self_query_bias": scatter_about(key_list[6], (D,), 0.2, 1.25),
        "self_value_bias": scatter_about(key_list[7], (D,), 0.2, 1.25),
        "self_output_weight": scatter_about(key_list[8], (D, D), (D // 16) ** -0.5, 0.875),
        "self_out_bias": scatter_about(key_list[9], (D,), 0.2, 1.25),
        "norm_one_gain": jnp.clip(1.0 + 0.1 * jax.random.normal(key_list[10], (D,), jnp.float32), 0.5, 1.5).astype(jnp.bfloat16),
        "norm_one_shift": scatter_about(key_list[11], (D,), 0.2, 1.25),
        "cross_query_matrix": scatter_about(key_list[12], (D, D), D ** -0.5, 0.21875),
        "cross_query_bias": scatter_about(key_list[13], (D,), 0.2, 1.25),
        "cross_key_value_weight": scatter_about(key_list[14], (D, 2 * D), D ** -0.5, 0.21875),
        "cross_value_bias": scatter_about(key_list[15], (D,), 0.2, 1.25),
        "cross_output_weight": scatter_about(key_list[16], (D, D), (D // 16) ** -0.5, 0.875),
        "cross_out_bias": scatter_about(key_list[17], (D,), 0.2, 1.25),
        "norm_two_gain": jnp.clip(1.0 + 0.1 * jax.random.normal(key_list[18], (D,), jnp.float32), 0.5, 1.5).astype(jnp.bfloat16),
        "norm_two_shift": scatter_about(key_list[19], (D,), 0.2, 1.25),
        "feed_input_weight": scatter_about(key_list[20], (D, FF), D ** -0.5, 0.21875),
        "feed_in_bias": scatter_about(key_list[21], (FF,), 0.2, 1.25),
        "feed_output_weight": scatter_about(key_list[22], (FF, D), FF ** -0.5, 0.109375),
        "feed_out_bias": scatter_about(key_list[23], (D,), 0.2, 1.25),
        "norm_three_gain": jnp.clip(1.0 + 0.1 * jax.random.normal(key_list[24], (D,), jnp.float32), 0.5, 1.5).astype(jnp.bfloat16),
        "norm_three_shift": scatter_about(key_list[25], (D,), 0.2, 1.25),
    }


@jax.custom_vjp
def low(v):
    return lax.optimization_barrier(v.astype(jnp.bfloat16)).astype(jnp.float32)

@jax.custom_vjp
def low_back(v):
    return v

def low_keep(v):
    return (low(v), None)

def narrow_precision_forward(kept, grad):
    return (grad,)

def back_keep(v):
    return (v, None)

def back_low(kept, grad):
    return (low(grad),)
low.defvjp(low_keep, narrow_precision_forward)
low_back.defvjp(back_keep, back_low)

def project(left, right):
    return jnp.dot(left, right, precision=lax.Precision.HIGHEST, preferred_element_type=jnp.float32)

def both_low(value):
    return low_back(low(value))

def layer_norm(latent_activation, gain, shift):
    centred = latent_activation - lax.optimization_barrier(jnp.mean(latent_activation, axis=-1, keepdims=True))
    spread = lax.optimization_barrier(jnp.mean(centred * centred, axis=-1, keepdims=True))
    return centred * lax.rsqrt(spread + 1e-05) * gain + shift

def attend(queries, keys, values, allowed):
    qheads = queries.reshape(queries.shape[0], H, HD)
    kheads = keys.reshape(keys.shape[0], H, HD)
    valued_attender_splits = values.reshape(values.shape[0], H, HD)
    raw = jnp.einsum('qhd,khd->hqk', qheads, kheads, precision=lax.Precision.HIGHEST) * HD ** (-0.5)
    scores = jnp.where(allowed[None], low_back(raw), -1000000000.0)
    probs = jax.nn.softmax(scores, axis=-1)
    result = jnp.einsum('hqk,khd->qhd', low(probs), valued_attender_splits, precision=lax.Precision.HIGHEST)
    return result.reshape(queries.shape[0], D)

def sequence_layer(params, inputs, memory, tdocs, mdocs):
    self_query_key_value_weight, self_query_bias, self_value_bias, self_output_weight, self_out_bias, norm_one_gain, norm_one_shift, cross_query_matrix, cross_query_bias, cross_key_value_weight, cross_value_bias, cross_output_weight, cross_out_bias, norm_two_gain, norm_two_shift, feed_input_weight, feed_in_bias, feed_output_weight, feed_out_bias, norm_three_gain, norm_three_shift = params
    places = jnp.arange(LEN, dtype=jnp.int32)
    packed_rows = project(inputs, self_query_key_value_weight)
    query = both_low(packed_rows[:, :D] + self_query_bias)
    key = both_low(packed_rows[:, D:2 * D])
    value = both_low(packed_rows[:, 2 * D:] + self_value_bias)
    self_mask = jnp.logical_and(tdocs[:, None] == tdocs[None, :], places[:, None] >= places[None, :])
    attention_context = both_low(attend(query, key, value, self_mask))
    residual_branch = low_back(project(attention_context, self_output_weight) + self_out_bias)
    first = layer_norm(inputs + residual_branch, norm_one_gain, norm_one_shift)
    cross_query = both_low(project(low(first), cross_query_matrix) + cross_query_bias)
    mem_packed = project(memory, cross_key_value_weight)
    mem_key = both_low(mem_packed[:, :D])
    mem_value = both_low(mem_packed[:, D:] + cross_value_bias)
    cross_mask = tdocs[:, None] == mdocs[None, :]
    cross_attention_context = both_low(attend(cross_query, mem_key, mem_value, cross_mask))
    cross_branch = low_back(project(cross_attention_context, cross_output_weight) + cross_out_bias)
    second = layer_norm(first + cross_branch, norm_two_gain, norm_two_shift)
    inner = low_back(project(low(second), feed_input_weight) + feed_in_bias)
    latent_activation = low(jax.nn.gelu(inner, approximate=False))
    feed = low_back(project(latent_activation, feed_output_weight) + feed_out_bias)
    return layer_norm(second + feed, norm_three_gain, norm_three_shift)

def reference(inputs, memory, target_docs, memory_docs, cotangent, self_query_key_value_weight, self_query_bias, self_value_bias, self_output_weight, self_out_bias, norm_one_gain, norm_one_shift, cross_query_matrix, cross_query_bias, cross_key_value_weight, cross_value_bias, cross_output_weight, cross_out_bias, norm_two_gain, norm_two_shift, feed_input_weight, feed_in_bias, feed_output_weight, feed_out_bias, norm_three_gain, norm_three_shift):
    weights = (self_query_key_value_weight, self_query_bias, self_value_bias, self_output_weight, self_out_bias, norm_one_gain, norm_one_shift, cross_query_matrix, cross_query_bias, cross_key_value_weight, cross_value_bias, cross_output_weight, cross_out_bias, norm_two_gain, norm_two_shift, feed_input_weight, feed_in_bias, feed_output_weight, feed_out_bias, norm_three_gain, norm_three_shift)
    params = tuple((weight.astype(jnp.float32) for weight in weights))

    def forward(params, inputs_f, memory_f):

        def single(items):
            return sequence_layer(params, items[0], items[1], items[2], items[3])
        return lax.map(jax.checkpoint(single), (inputs_f, memory_f, target_docs, memory_docs))
    result, pullback = jax.vjp(forward, params, inputs.astype(jnp.float32), memory.astype(jnp.float32))
    grads, grad_in, grad_mem = pullback(cotangent.astype(jnp.float32))
    query_key_value_gradient, g_qbias, g_vbias, self_output_gradient, g_obias, g_gone, g_sone, cross_query_weight_gradient, g_cqbias, cross_key_value_gradient, g_cvbias, cross_output_gradient, g_cobias, g_gtwo, g_stwo, feed_input_gradient, g_fibias, feed_output_gradient, g_fobias, g_gthree, g_sthree = grads
    return (result.astype(jnp.bfloat16), grad_in.astype(jnp.bfloat16), grad_mem.astype(jnp.bfloat16), query_key_value_gradient, g_qbias, g_vbias, self_output_gradient, g_obias, g_gone, g_sone, cross_query_weight_gradient, g_cqbias, cross_key_value_gradient, g_cvbias, cross_output_gradient, g_cobias, g_gtwo, g_stwo, feed_input_gradient, g_fibias, feed_output_gradient, g_fobias, g_gthree, g_sthree)
```

```python
import functools

import jax
import jax.numpy as jnp
from jax import lax
from jax.experimental import pallas as pl
from jax.experimental.pallas import tpu as pltpu
from jax.sharding import PartitionSpec as P

HD = 64
PAIR = 2 * HD
EPS = 1e-05
FAR = 1.0e9
VMEM = 60 * 1024 * 1024
F32 = jnp.float32
BF16 = jnp.bfloat16


def nn(a, b):
    return lax.dot_general(a, b, (((1,), (0,)), ((), ())), preferred_element_type=F32)


def nt(a, b):
    return lax.dot_general(a, b, (((1,), (1,)), ((), ())), preferred_element_type=F32)


def tn(a, b):
    return lax.dot_general(a, b, (((0,), (0,)), ((), ())), preferred_element_type=F32)


def params():
    return pltpu.CompilerParams(vmem_limit_bytes=VMEM)


def cost(flops, moved):
    return pl.CostEstimate(flops=int(flops), bytes_accessed=int(moved), transcendentals=0)


def normed(h):
    centred = h - jnp.mean(h, axis=-1, keepdims=True)
    rstd = lax.rsqrt(jnp.mean(centred * centred, axis=-1, keepdims=True) + EPS)
    return centred * rstd, rstd


def norm_back(grad, n, rstd, gain):
    scaled = grad * gain
    centre = jnp.mean(scaled, axis=-1, keepdims=True)
    along = jnp.mean(scaled * n, axis=-1, keepdims=True)
    return rstd * (scaled - centre - n * along)


def total(a):
    return jnp.sum(a.astype(F32), axis=0, keepdims=True)


def project_kernel(with_query, x_ref, w_ref, qb_ref, vb_ref, o_ref):
    step = pl.program_id(0)
    last = pl.num_programs(0) - 1
    bias = jnp.where(step == last, vb_ref[...].astype(F32), 0.0)
    if with_query:
        bias = bias + jnp.where(step == 0, qb_ref[...].astype(F32), 0.0)
    o_ref[...] = (nn(x_ref[...], w_ref[...]) + bias).astype(BF16)


def project(x, w, qbias, vbias, first):
    rows, width = x.shape
    count = w.shape[1] // width - first
    return pl.pallas_call(
        functools.partial(project_kernel, first == 0 and qbias is not vbias),
        grid=(count,),
        in_specs=[
            pl.BlockSpec((rows, width), lambda j: (0, 0)),
            pl.BlockSpec((width, width), lambda j: (0, j + first)),
            pl.BlockSpec((1, width), lambda j: (0, 0)),
            pl.BlockSpec((1, width), lambda j: (0, 0)),
        ],
        out_specs=pl.BlockSpec((rows, width), lambda j: (0, j)),
        out_shape=jax.ShapeDtypeStruct((rows, width * count), BF16),
        compiler_params=params(),
        cost_estimate=cost(2 * rows * width * width * count, 2 * width * count * (width + rows)),
        name="project",
    )(x, w, qbias, vbias)


def head_masks(dtype):
    lane = lax.broadcasted_iota(jnp.int32, (1, PAIR), 1)
    low = jnp.where(lane < HD, 1.0, 0.0)
    return low.astype(dtype), (1.0 - low).astype(dtype)


def query_code(code):
    lane = lax.broadcasted_iota(jnp.int32, code.shape, 1)
    return jnp.where(lane < 4, (code.astype(F32) - 1.0) * FAR, 0.0).astype(BF16)


def softmax_pieces(scores, values):
    peak = functools.reduce(jnp.maximum, [jnp.max(s, axis=-1, keepdims=True) for s in scores])
    expd = [jnp.exp(s - peak) for s in scores]
    norm = sum(jnp.sum(e, axis=-1, keepdims=True) for e in expd)
    out = sum(nn(e.astype(BF16), v) for e, v in zip(expd, values))
    return out / norm, peak + jnp.log(norm)


def self_pieces(block, size, both, own, other):
    pieces = []
    if both:
        pieces.append((other, False))
    if block:
        pieces.append((own[: block * size], False))
    pieces.append((own[block * size : (block + 1) * size], True))
    return pieces


def store_lse(lse_ref, block, size, low, high):
    lane = lax.broadcasted_iota(jnp.int32, (size, PAIR), 1)
    both = jnp.where(lane == 0, low, high)
    lse_ref[:, block * size : (block + 1) * size] = jnp.transpose(both)[:8]


def self_forward_kernel(size, q_ref, k_ref, v_ref, ko_ref, vo_ref, own_ref, oth_ref, o_ref, lse_ref):
    second = lax.axis_index("sp") == 1
    rows = q_ref.shape[0]
    masks = head_masks(BF16)
    outs = head_masks(F32)

    def run(both):
        qcode = query_code(own_ref[...])
        own = jnp.concatenate([k_ref[...], own_ref[...]], axis=1)
        oth = jnp.concatenate([ko_ref[...], oth_ref[...]], axis=1) if both else None
        vown = v_ref[...]
        voth = vo_ref[...] if both else None
        for block in range(rows // size):
            at = slice(block * size, (block + 1) * size)
            lses, result = [], 0.0
            for mask, keep in zip(masks, outs):
                q = jnp.concatenate([q_ref[at] * (mask * BF16(HD**-0.5)), qcode[at]], axis=1)
                scores = []
                for keys, diagonal in self_pieces(block, size, both, own, oth):
                    s = nt(q, keys)
                    if diagonal:
                        row = lax.broadcasted_iota(jnp.int32, s.shape, 0)
                        col = lax.broadcasted_iota(jnp.int32, s.shape, 1)
                        s = jnp.where(row >= col, s, -FAR)
                    scores.append(s)
                values = [v for v, _ in self_pieces(block, size, both, vown, voth)]
                out, lse = softmax_pieces(scores, values)
                result = result + out * keep
                lses.append(lse)
            o_ref[at] = result.astype(BF16)
            store_lse(lse_ref, block, size, *lses)

    pl.when(second)(lambda: run(True))
    pl.when(jnp.logical_not(second))(lambda: run(False))


def pair_spec(rows, offset):
    return pl.BlockSpec((rows, PAIR), lambda p: (0, p + offset))


def whole(shape):
    return pl.BlockSpec(shape, lambda *_: (0,) * len(shape))


def self_forward(qkv, kvo, own, oth):
    rows = qkv.shape[0]
    width = qkv.shape[1] // 3
    pairs = width // PAIR
    return pl.pallas_call(
        functools.partial(self_forward_kernel, 256),
        grid=(pairs,),
        in_specs=[
            pair_spec(rows, 0),
            pair_spec(rows, pairs),
            pair_spec(rows, 2 * pairs),
            pair_spec(rows, 0),
            pair_spec(rows, pairs),
            whole((rows, 128)),
            whole((rows, 128)),
        ],
        out_specs=[pair_spec(rows, 0), pl.BlockSpec((8, rows), lambda p: (p, 0))],
        out_shape=[
            jax.ShapeDtypeStruct((rows, width), BF16),
            jax.ShapeDtypeStruct((8 * pairs, rows), F32),
        ],
        compiler_params=params(),
        cost_estimate=cost(16 * rows * rows * width, 16 * rows * width),
        name="self_forward",
    )(qkv, qkv, qkv, kvo, kvo, own, oth)


def cross_forward_kernel(size, q_ref, k_ref, v_ref, ko_ref, vo_ref, t_ref, own_ref, oth_ref, o_ref, lse_ref):
    rows = q_ref.shape[0]
    masks = head_masks(BF16)
    outs = head_masks(F32)
    qcode = query_code(t_ref[...])
    keys = [
        jnp.concatenate([k_ref[...], own_ref[...]], axis=1),
        jnp.concatenate([ko_ref[...], oth_ref[...]], axis=1),
    ]
    values = [v_ref[...], vo_ref[...]]
    for block in range(rows // size):
        at = slice(block * size, (block + 1) * size)
        lses, result = [], 0.0
        for mask, keep in zip(masks, outs):
            q = jnp.concatenate([q_ref[at] * (mask * BF16(HD**-0.5)), qcode[at]], axis=1)
            out, lse = softmax_pieces([nt(q, k) for k in keys], values)
            result = result + out * keep
            lses.append(lse)
        o_ref[at] = result.astype(BF16)
        store_lse(lse_ref, block, size, *lses)


def cross_forward(cq, kv, kvo, t, own, oth):
    rows, width = cq.shape
    pairs = width // PAIR
    return pl.pallas_call(
        functools.partial(cross_forward_kernel, 256),
        grid=(pairs,),
        in_specs=[
            pair_spec(rows, 0),
            pair_spec(rows, 0),
            pair_spec(rows, pairs),
            pair_spec(rows, 0),
            pair_spec(rows, pairs),
            whole((rows, 128)),
            whole((rows, 128)),
            whole((rows, 128)),
        ],
        out_specs=[pair_spec(rows, 0), pl.BlockSpec((8, rows), lambda p: (p, 0))],
        out_shape=[
            jax.ShapeDtypeStruct((rows, width), BF16),
            jax.ShapeDtypeStruct((8 * pairs, rows), F32),
        ],
        compiler_params=params(),
        cost_estimate=cost(24 * rows * rows * width, 16 * rows * width),
        name="cross_forward",
    )(cq, kv, kv, kvo, kvo, t, own, oth)


def delta_rows(g, o):
    prod = g.astype(F32) * o.astype(F32)
    upper = prod.astype(BF16)
    lower = (prod - upper.astype(F32)).astype(BF16)
    row = lax.broadcasted_iota(jnp.int32, (8, PAIR), 0)
    lane = lax.broadcasted_iota(jnp.int32, (8, PAIR), 1)
    pick = jnp.where(row == lane // HD, 1.0, 0.0).astype(BF16)
    return nt(pick, upper) + nt(pick, lower)


def back_piece(keys, values, q, g, lse, delta, causal):
    s = nt(keys, q)
    if causal:
        row = lax.broadcasted_iota(jnp.int32, s.shape, 0)
        col = lax.broadcasted_iota(jnp.int32, s.shape, 1)
        s = jnp.where(row <= col, s, -FAR)
    p = jnp.exp(s - lse)
    ds = p * (nt(values, g) - delta)
    return p.astype(BF16), ds.astype(BF16)


def cross_backward_kernel(
    size, q_ref, k_ref, v_ref, ko_ref, vo_ref, g_ref, o_ref, lse_ref, t_ref, own_ref, oth_ref,
    dq_ref, dk_ref, dv_ref, dko_ref, dvo_ref,
):
    rows = q_ref.shape[0]
    masks = head_masks(BF16)
    scale = BF16(HD**-0.5)
    qcode = query_code(t_ref[...])
    delta = delta_rows(g_ref[...], o_ref[...])
    lse = lse_ref[...]
    halves = [(k_ref, v_ref, own_ref, dk_ref, dv_ref), (ko_ref, vo_ref, oth_ref, dko_ref, dvo_ref)]
    dq = [0.0] * (rows // size)
    for kr, vr, code, dkr, dvr in halves:
        keys = jnp.concatenate([kr[...], code[...]], axis=1)
        values = vr[...]
        dk = dv = 0.0
        for block in range(rows // size):
            at = slice(block * size, (block + 1) * size)
            for head, mask in enumerate(masks):
                qm = q_ref[at] * (mask * scale)
                gm = g_ref[at] * mask
                q = jnp.concatenate([qm, qcode[at]], axis=1)
                p, ds = back_piece(
                    keys, values, q, gm, lse[head : head + 1, at], delta[head : head + 1, at], False
                )
                dk = dk + nn(ds, qm)
                dv = dv + nn(p, gm)
                dq[block] = dq[block] + tn(ds, kr[...] * (mask * scale))
        dkr[...] = dk.astype(BF16)
        dvr[...] = dv.astype(BF16)
    for block in range(rows // size):
        dq_ref[block * size : (block + 1) * size] = dq[block].astype(BF16)


def cross_backward(cq, kv, kvo, g, o, lse, t, own, oth):
    rows, width = cq.shape
    pairs = width // PAIR
    flat = jax.ShapeDtypeStruct((rows, width), BF16)
    return pl.pallas_call(
        functools.partial(cross_backward_kernel, 256),
        grid=(pairs,),
        in_specs=[
            pair_spec(rows, 0),
            pair_spec(rows, 0),
            pair_spec(rows, pairs),
            pair_spec(rows, 0),
            pair_spec(rows, pairs),
            pair_spec(rows, 0),
            pair_spec(rows, 0),
            pl.BlockSpec((8, rows), lambda p: (p, 0)),
            whole((rows, 128)),
            whole((rows, 128)),
            whole((rows, 128)),
        ],
        out_specs=[pair_spec(rows, 0)] * 5,
        out_shape=[flat] * 5,
        compiler_params=params(),
        cost_estimate=cost(64 * rows * rows * width, 24 * rows * width),
        name="cross_backward",
    )(cq, kv, kv, kvo, kvo, g, o, lse, t, own, oth)


def self_backward_kernel(
    size, q_ref, k_ref, v_ref, ko_ref, vo_ref, g_ref, o_ref, lse_ref, own_ref, oth_ref,
    dq_ref, dk_ref, dv_ref, dko_ref, dvo_ref,
):
    second = lax.axis_index("sp") == 1
    rows = q_ref.shape[0]
    masks = head_masks(BF16)
    scale = BF16(HD**-0.5)

    def run(both):
        qcode = query_code(own_ref[...])
        delta = delta_rows(g_ref[...], o_ref[...])
        lse = lse_ref[...]
        count = rows // size
        dk, dv = [0.0] * count, [0.0] * count
        dko = dvo = 0.0
        for block in range(count):
            at = slice(block * size, (block + 1) * size)
            dq = 0.0
            for head, mask in enumerate(masks):
                qm = q_ref[at] * (mask * scale)
                gm = g_ref[at] * mask
                q = jnp.concatenate([qm, qcode[at]], axis=1)
                rest = (q, gm, lse[head : head + 1, at], delta[head : head + 1, at])
                for part in range(block + 1):
                    of = slice(part * size, (part + 1) * size)
                    keys = jnp.concatenate([k_ref[of], own_ref[of]], axis=1)
                    p, ds = back_piece(keys, v_ref[of], *rest, part == block)
                    dk[part] = dk[part] + nn(ds, qm)
                    dv[part] = dv[part] + nn(p, gm)
                    dq = dq + tn(ds, k_ref[of] * (mask * scale))
                if both:
                    keys = jnp.concatenate([ko_ref[...], oth_ref[...]], axis=1)
                    p, ds = back_piece(keys, vo_ref[...], *rest, False)
                    dko = dko + nn(ds, qm)
                    dvo = dvo + nn(p, gm)
                    dq = dq + tn(ds, ko_ref[...] * (mask * scale))
            dq_ref[at] = dq.astype(BF16)
        for part in range(count):
            of = slice(part * size, (part + 1) * size)
            dk_ref[of] = dk[part].astype(BF16)
            dv_ref[of] = dv[part].astype(BF16)
        if both:
            dko_ref[...] = dko.astype(BF16)
            dvo_ref[...] = dvo.astype(BF16)
        else:
            dko_ref[...] = jnp.zeros(dko_ref.shape, BF16)
            dvo_ref[...] = jnp.zeros(dvo_ref.shape, BF16)

    pl.when(second)(lambda: run(True))
    pl.when(jnp.logical_not(second))(lambda: run(False))


def self_backward(qkv, kvo, g, o, lse, own, oth):
    rows = qkv.shape[0]
    width = qkv.shape[1] // 3
    pairs = width // PAIR
    flat = jax.ShapeDtypeStruct((rows, width), BF16)
    return pl.pallas_call(
        functools.partial(self_backward_kernel, 256),
        grid=(pairs,),
        in_specs=[
            pair_spec(rows, 0),
            pair_spec(rows, pairs),
            pair_spec(rows, 2 * pairs),
            pair_spec(rows, 0),
            pair_spec(rows, pairs),
            pair_spec(rows, 0),
            pair_spec(rows, 0),
            pl.BlockSpec((8, rows), lambda p: (p, 0)),
            whole((rows, 128)),
            whole((rows, 128)),
        ],
        out_specs=[pair_spec(rows, 0)] * 5,
        out_shape=[flat] * 5,
        compiler_params=params(),
        cost_estimate=cost(48 * rows * rows * width, 24 * rows * width),
        name="self_backward",
    )(qkv, qkv, qkv, kvo, kvo, g, o, lse, own, oth)


def first_norm_kernel(x_ref, ctx_ref, wo_ref, ob_ref, g_ref, s_ref, wq_ref, qb_ref, h_ref, cq_ref):
    h = x_ref[...].astype(F32) + nn(ctx_ref[...], wo_ref[...]) + ob_ref[...].astype(F32)
    h_ref[...] = h
    n, _ = normed(h)
    a = (n * g_ref[...].astype(F32) + s_ref[...].astype(F32)).astype(BF16)
    cq_ref[...] = (nn(a, wq_ref[...]) + qb_ref[...].astype(F32)).astype(BF16)


def first_norm(x, ctx, wo, ob, g, s, wq, qb):
    rows, width = x.shape
    return pl.pallas_call(
        first_norm_kernel,
        out_shape=[
            jax.ShapeDtypeStruct((rows, width), F32),
            jax.ShapeDtypeStruct((rows, width), BF16),
        ],
        compiler_params=params(),
        cost_estimate=cost(4 * rows * width * width, 4 * width * width + 10 * rows * width),
        name="first_norm",
    )(x, ctx, wo, ob, g, s, wq, qb)


def feed_kernel(
    count, h1_ref, cc_ref, ct_ref, wco_ref, cob_ref, g1_ref, s1_ref, g2_ref, s2_ref, g3_ref, s3_ref,
    wi_ref, ib_ref, wo_ref, fob_ref,
    out_ref, dh2_ref, dcc_ref, gco_ref, gwi_ref, gwo_ref, small_ref, gib_ref,
    hid_ref, slope_ref, n2_ref, r2_ref, a2b_ref, acc_ref, df_ref,
):
    step = pl.program_id(0)

    @pl.when(step == 0)
    def _():
        n1, _ = normed(h1_ref[...])
        a1 = n1 * g1_ref[...].astype(F32) + s1_ref[...].astype(F32)
        h2 = a1 + nn(cc_ref[...], wco_ref[...]) + cob_ref[...].astype(F32)
        n2, r2 = normed(h2)
        n2_ref[...] = n2
        r2_ref[...] = jnp.broadcast_to(r2, r2_ref.shape)
        a2 = n2 * g2_ref[...].astype(F32) + s2_ref[...].astype(F32)
        a2b_ref[...] = a2.astype(BF16)
        acc_ref[...] = a2 + fob_ref[...].astype(F32)

    @pl.when(step < count)
    def _():
        u = nn(a2b_ref[...], wi_ref[...]) + ib_ref[...].astype(F32)
        cumul = 0.5 * (1.0 + lax.erf(u * 0.7071067811865476))
        density = jnp.exp(-0.5 * u * u) * 0.3989422804014327
        hid = (u * cumul).astype(BF16)
        hid_ref[step] = hid
        slope_ref[step] = cumul + u * density
        acc_ref[...] += nn(hid, wo_ref[...])

    @pl.when(step == count - 1)
    def _():
        n3, r3 = normed(acc_ref[...])
        gain = g3_ref[...].astype(F32)
        out_ref[...] = (n3 * gain + s3_ref[...].astype(F32)).astype(BF16)
        e = ct_ref[...].astype(F32)
        d3 = norm_back(e, n3, r3, gain)
        df = d3.astype(BF16)
        df_ref[...] = df
        acc_ref[...] = d3
        small_ref[0:1] = total(e * n3)
        small_ref[1:2] = total(e)
        small_ref[2:3] = total(df)

    @pl.when(step >= count)
    def _():
        j = step - count
        df = df_ref[...]
        du = (nt(df, wo_ref[...]) * slope_ref[j]).astype(BF16)
        gib_ref[...] = total(du)
        acc_ref[...] += nt(du, wi_ref[...])
        gwo_ref[...] = tn(hid_ref[j], df).astype(BF16)
        gwi_ref[...] = tn(a2b_ref[...], du).astype(BF16)

    @pl.when(step == 2 * count - 1)
    def _():
        d2 = acc_ref[...]
        n2 = n2_ref[...]
        dh2 = norm_back(d2, n2, r2_ref[:, :1], g2_ref[...].astype(F32))
        dh2_ref[...] = dh2
        dco = dh2.astype(BF16)
        dcc_ref[...] = nt(dco, wco_ref[...]).astype(BF16)
        gco_ref[...] = tn(cc_ref[...], dco).astype(BF16)
        small_ref[3:4] = total(d2 * n2)
        small_ref[4:5] = total(d2)
        small_ref[5:6] = total(dco)
        small_ref[6:8] = jnp.zeros((2, d2.shape[1]), F32)


def feed(h1, cc, ct, wco, cob, g1, s1, g2, s2, g3, s3, wi, ib, wo, fob):
    rows, width = h1.shape
    wide = wi.shape[1]
    chunk = width
    count = wide // chunk

    def fwd_bwd(s):
        return jnp.where(s < count, s, s - count)

    def later(s):
        return jnp.maximum(s - count, 0)

    row = whole((1, width))
    flat = whole((rows, width))
    square = whole((width, width))
    return pl.pallas_call(
        functools.partial(feed_kernel, count),
        grid=(2 * count,),
        in_specs=[
            flat, flat, flat, square, row, row, row, row, row, row, row,
            pl.BlockSpec((width, chunk), lambda s: (0, fwd_bwd(s))),
            pl.BlockSpec((1, chunk), lambda s: (0, fwd_bwd(s))),
            pl.BlockSpec((chunk, width), lambda s: (fwd_bwd(s), 0)),
            row,
        ],
        out_specs=[
            flat, flat, flat, square,
            pl.BlockSpec((width, chunk), lambda s: (0, later(s))),
            pl.BlockSpec((chunk, width), lambda s: (later(s), 0)),
            whole((8, width)),
            pl.BlockSpec((1, chunk), lambda s: (0, later(s))),
        ],
        out_shape=[
            jax.ShapeDtypeStruct((rows, width), BF16),
            jax.ShapeDtypeStruct((rows, width), F32),
            jax.ShapeDtypeStruct((rows, width), BF16),
            jax.ShapeDtypeStruct((width, width), BF16),
            jax.ShapeDtypeStruct((width, wide), BF16),
            jax.ShapeDtypeStruct((wide, width), BF16),
            jax.ShapeDtypeStruct((8, width), F32),
            jax.ShapeDtypeStruct((1, wide), F32),
        ],
        scratch_shapes=[
            pltpu.VMEM((count, rows, chunk), BF16),
            pltpu.VMEM((count, rows, chunk), F32),
            pltpu.VMEM((rows, width), F32),
            pltpu.VMEM((rows, 128), F32),
            pltpu.VMEM((rows, width), BF16),
            pltpu.VMEM((rows, width), F32),
            pltpu.VMEM((rows, width), BF16),
        ],
        compiler_params=params(),
        cost_estimate=cost(
            12 * rows * width * wide + 6 * rows * width * width, 12 * width * wide + 16 * rows * width
        ),
        name="feed",
    )(h1, cc, ct, wco, cob, g1, s1, g2, s2, g3, s3, wi, ib, wo, fob)


def memory_back_kernel(m_ref, mo_ref, dk_ref, dv_ref, dko_ref, dvo_ref, w_ref, dm_ref, dmo_ref, gw_ref, gb_ref):
    width = m_ref.shape[1]
    wk, wv = w_ref[:, :width], w_ref[:, width:]
    dk, dv, dko, dvo = dk_ref[...], dv_ref[...], dko_ref[...], dvo_ref[...]
    dmo_ref[...] = (nt(dko, wk) + nt(dvo, wv)).astype(BF16)
    dm_ref[...] = nt(dk, wk) + nt(dv, wv)
    m, mo = m_ref[...], mo_ref[...]
    gw_ref[:, :width] = (tn(m, dk) + tn(mo, dko)).astype(BF16)
    gw_ref[:, width:] = (tn(m, dv) + tn(mo, dvo)).astype(BF16)
    gb_ref[...] = total(dv) + total(dvo)


def memory_back(m, mo, dk, dv, dko, dvo, w):
    rows, width = m.shape
    return pl.pallas_call(
        memory_back_kernel,
        out_shape=[
            jax.ShapeDtypeStruct((rows, width), F32),
            jax.ShapeDtypeStruct((rows, width), BF16),
            jax.ShapeDtypeStruct((width, 2 * width), BF16),
            jax.ShapeDtypeStruct((1, width), F32),
        ],
        compiler_params=params(),
        cost_estimate=cost(16 * rows * width * width, 8 * width * width + 18 * rows * width),
        name="memory_back",
    )(m, mo, dk, dv, dko, dvo, w)


def first_back_kernel(
    dcq_ref, dh2_ref, h1_ref, ctx_ref, wcq_ref, wso_ref, g_ref, s_ref,
    dh1_ref, dsc_ref, gcq_ref, gso_ref, small_ref,
):
    gain = g_ref[...].astype(F32)
    n1, r1 = normed(h1_ref[...])
    a1b = (n1 * gain + s_ref[...].astype(F32)).astype(BF16)
    dcq = dcq_ref[...]
    d1 = dh2_ref[...] + nt(dcq, wcq_ref[...])
    dh1 = norm_back(d1, n1, r1, gain)
    dh1_ref[...] = dh1
    dso = dh1.astype(BF16)
    dsc_ref[...] = nt(dso, wso_ref[...]).astype(BF16)
    gcq_ref[...] = tn(a1b, dcq).astype(BF16)
    gso_ref[...] = tn(ctx_ref[...], dso).astype(BF16)
    small_ref[0:1] = total(dcq)
    small_ref[1:2] = total(d1 * n1)
    small_ref[2:3] = total(d1)
    small_ref[3:4] = total(dso)
    small_ref[4:8] = jnp.zeros((4, dh1.shape[1]), F32)


def first_back(dcq, dh2, h1, ctx, wcq, wso, g, s):
    rows, width = dcq.shape
    return pl.pallas_call(
        first_back_kernel,
        out_shape=[
            jax.ShapeDtypeStruct((rows, width), F32),
            jax.ShapeDtypeStruct((rows, width), BF16),
            jax.ShapeDtypeStruct((width, width), BF16),
            jax.ShapeDtypeStruct((width, width), BF16),
            jax.ShapeDtypeStruct((8, width), F32),
        ],
        compiler_params=params(),
        cost_estimate=cost(8 * rows * width * width, 8 * width * width + 18 * rows * width),
        name="first_back",
    )(dcq, dh2, h1, ctx, wcq, wso, g, s)


def other_input_kernel(dko_ref, dvo_ref, w_ref, dxo_ref):
    width = dko_ref.shape[1]

    @pl.when(lax.axis_index("sp") == 1)
    def _():
        dxo = nt(dko_ref[...], w_ref[:, width : 2 * width]) + nt(dvo_ref[...], w_ref[:, 2 * width :])
        dxo_ref[...] = dxo.astype(BF16)

    @pl.when(lax.axis_index("sp") == 0)
    def _():
        dxo_ref[...] = jnp.zeros(dxo_ref.shape, BF16)


def other_input(dko, dvo, w):
    rows, width = dko.shape
    return pl.pallas_call(
        other_input_kernel,
        out_shape=jax.ShapeDtypeStruct((rows, width), BF16),
        compiler_params=params(),
        cost_estimate=cost(4 * rows * width * width, 6 * width * width + 6 * rows * width),
        name="other_input",
    )(dko, dvo, w)


def input_weight_kernel(x_ref, xo_ref, dq_ref, dk_ref, dv_ref, dko_ref, dvo_ref, gw_ref, gb_ref):
    width = x_ref.shape[1]
    x = x_ref[...]
    gw_ref[:, :width] = tn(x, dq_ref[...]).astype(BF16)
    gb_ref[0:1] = total(dq_ref[...])
    gb_ref[2:8] = jnp.zeros((6, width), F32)

    @pl.when(lax.axis_index("sp") == 1)
    def _():
        xo = xo_ref[...]
        gw_ref[:, width : 2 * width] = (tn(x, dk_ref[...]) + tn(xo, dko_ref[...])).astype(BF16)
        gw_ref[:, 2 * width :] = (tn(x, dv_ref[...]) + tn(xo, dvo_ref[...])).astype(BF16)
        gb_ref[1:2] = total(dv_ref[...]) + total(dvo_ref[...])

    @pl.when(lax.axis_index("sp") == 0)
    def _():
        gw_ref[:, width : 2 * width] = tn(x, dk_ref[...]).astype(BF16)
        gw_ref[:, 2 * width :] = tn(x, dv_ref[...]).astype(BF16)
        gb_ref[1:2] = total(dv_ref[...])


def input_weight(x, xo, dq, dk, dv, dko, dvo):
    rows, width = x.shape
    return pl.pallas_call(
        input_weight_kernel,
        out_shape=[
            jax.ShapeDtypeStruct((width, 3 * width), BF16),
            jax.ShapeDtypeStruct((8, width), F32),
        ],
        compiler_params=params(),
        cost_estimate=cost(10 * rows * width * width, 6 * width * width + 14 * rows * width),
        name="input_weight",
    )(x, xo, dq, dk, dv, dko, dvo)


def input_back_kernel(dh1_ref, dq_ref, dk_ref, dv_ref, w_ref, dx_ref):
    width = dq_ref.shape[1]
    dx_ref[...] = (
        dh1_ref[...]
        + nt(dq_ref[...], w_ref[:, :width])
        + nt(dk_ref[...], w_ref[:, width : 2 * width])
        + nt(dv_ref[...], w_ref[:, 2 * width :])
    )


def input_back(dh1, dq, dk, dv, w):
    rows, width = dq.shape
    return pl.pallas_call(
        input_back_kernel,
        out_shape=jax.ShapeDtypeStruct((rows, width), F32),
        compiler_params=params(),
        cost_estimate=cost(6 * rows * width * width, 6 * width * width + 14 * rows * width),
        name="input_back",
    )(dh1, dq, dk, dv, w)


def sum_scatter(grad, size, order):
    rows, cols = grad.shape
    bits = size.bit_length() - 1
    me = lax.axis_index("dp")
    now = grad.reshape((2,) * bits + (rows // size, cols))
    left = list(range(bits))[::-1]
    for bit in [b for b in order if b < bits] + [b for b in range(bits) if b not in order]:
        axis = left.index(bit)
        mine = (me >> bit) & 1
        keep = lax.dynamic_index_in_dim(now, mine, axis, keepdims=False)
        send = lax.dynamic_index_in_dim(now, 1 - mine, axis, keepdims=False)
        came = lax.ppermute(send, "dp", [(i, i ^ (1 << bit)) for i in range(size)])
        now = (keep.astype(F32) + came.astype(F32)).astype(BF16)
        left.pop(axis)
    came = lax.ppermute(now, "sp", [(0, 1), (1, 0)])
    return now.astype(F32) + came.astype(F32)


def document_code(docs):
    lane = jnp.arange(128, dtype=jnp.int32)
    return (docs[:, None] == lane[None, :]).astype(BF16)


def per_device(
    size,
    inputs,
    memory,
    target_docs,
    memory_docs,
    cotangent,
    w_qkv,
    b_q,
    b_v,
    w_so,
    b_so,
    g_one,
    s_one,
    w_cq,
    b_cq,
    w_ckv,
    b_cv,
    w_co,
    b_co,
    g_two,
    s_two,
    w_fi,
    b_fi,
    w_fo,
    b_fo,
    g_three,
    s_three,
):
    rows, width = inputs.shape[1:]
    swap = [(0, 1), (1, 0)]
    x, mem, ct = inputs[0], memory[0], cotangent[0]
    b_q, b_v, b_so, g_one, s_one, b_cq, b_cv, b_co, g_two, s_two, b_fi, b_fo, g_three, s_three = (
        v.reshape(1, -1)
        for v in (
            b_q, b_v, b_so, g_one, s_one, b_cq, b_cv, b_co, g_two, s_two, b_fi, b_fo, g_three, s_three
        )
    )
    docs = jnp.concatenate([target_docs, memory_docs], axis=0)
    docs_o = lax.ppermute(docs, "sp", swap)
    x_o = lax.ppermute(x, "sp", [(0, 1)])
    mem_o = lax.ppermute(mem, "sp", swap)
    t_own, m_own = document_code(docs[0]), document_code(docs[1])
    t_oth, m_oth = document_code(docs_o[0]), document_code(docs_o[1])

    qkv = project(x, w_qkv, b_q, b_v, 0)
    mkv = project(mem, w_ckv, b_cv, b_cv, 0)
    kvo = project(x_o, w_qkv, b_v, b_v, 1)
    ctx, lse = self_forward(qkv, kvo, t_own, t_oth)
    h1, cq = first_norm(x, ctx, w_so, b_so, g_one, s_one, w_cq, b_cq)
    mkvo = project(mem_o, w_ckv, b_cv, b_cv, 0)
    cc, clse = cross_forward(cq, mkv, mkvo, t_own, m_own, m_oth)
    output, dh2, dcc, gco, gwi, gwo, small_a, gib = feed(
        h1, cc, ct, w_co, b_co, g_one, s_one, g_two, s_two, g_three, s_three, w_fi, b_fi, w_fo, b_fo
    )
    t_fin = sum_scatter(gwi, size, (0, 1, 2, 3))
    t_fout = sum_scatter(gwo, size, (0, 2, 3, 1))
    dcq, dmk, dmv, dmko, dmvo = cross_backward(cq, mkv, mkvo, dcc, cc, clse, t_own, m_own, m_oth)
    dm, dmo, gckv, gcv = memory_back(mem, mem_o, dmk, dmv, dmko, dmvo, w_ckv)
    dm_in = lax.ppermute(dmo, "sp", swap)
    dh1, dsc, gcq, gso, small_b = first_back(dcq, dh2, h1, ctx, w_cq, w_so, g_one, s_one)
    t_cout = sum_scatter(gco, size, (0, 1, 2, 3))
    t_cmem = sum_scatter(gckv, size, (0, 1, 2, 3))
    t_cquery = sum_scatter(gcq, size, (0, 2, 3, 1))
    t_out = sum_scatter(gso, size, (0, 1, 2, 3))
    dq, dk, dv, dko, dvo = self_backward(qkv, kvo, dsc, ctx, lse, t_own, t_oth)
    dxo = other_input(dko, dvo, w_qkv)
    dx_in = lax.ppermute(dxo, "sp", [(1, 0)])
    gqkv, small_c = input_weight(x, x_o, dq, dk, dv, dko, dvo)
    t_qkv = sum_scatter(gqkv, size, (0, 1, 2, 3))
    dx = input_back(dh1, dq, dk, dv, w_qkv)
    grad_memory = (dm + dm_in.astype(F32)).astype(BF16)
    derivative = (dx + dx_in.astype(F32)).astype(BF16)

    small = jnp.concatenate([small_a[:6], small_b[:4], gcv, small_c[:2], gib.reshape(-1, width)], axis=0)
    small = lax.psum(small, ("dp", "sp"))
    me = lax.axis_index("dp")
    share = width // size
    lines = lax.dynamic_slice_in_dim(small, me * share, share, 1)
    (t_gthree, t_sthree, t_fobias, t_gtwo, t_stwo, t_cobias, t_cqbias, t_gone, t_sone, t_obias,
     t_cvbias, t_qbias, t_vbias) = (lines[i] for i in range(13))
    wide = gib.shape[1] // size
    t_fibias = lax.dynamic_slice_in_dim(small[13:].reshape(-1), me * wide, wide, 0)
    return (
        output[None],
        derivative[None],
        grad_memory[None],
        t_qkv,
        t_qbias,
        t_vbias,
        t_out,
        t_obias,
        t_gone,
        t_sone,
        t_cquery,
        t_cqbias,
        t_cmem,
        t_cvbias,
        t_cout,
        t_cobias,
        t_gtwo,
        t_stwo,
        t_fin,
        t_fibias,
        t_fout,
        t_fobias,
        t_gthree,
        t_sthree,
    )


def solution(mesh):
    split = P("dp", "sp", None)
    in_specs = (split, split, P("dp", "sp"), P("dp", "sp"), split) + (P(),) * 21
    matrix, vector = P("dp", None), P("dp")
    out_specs = (
        split, split, split,
        matrix, vector, vector,
        matrix, vector, vector, vector,
        matrix, vector,
        matrix, vector,
        matrix, vector, vector, vector,
        matrix, vector,
        matrix, vector, vector, vector,
    )
    return jax.shard_map(
        functools.partial(per_device, mesh.shape["dp"]),
        mesh=mesh, in_specs=in_specs, out_specs=out_specs, check_vma=False,
    )
```

```python
import functools

import jax
import jax.numpy as jnp
from jax import lax
from jax.experimental import pallas as pl
from jax.experimental.pallas import tpu as pltpu
from jax.sharding import PartitionSpec as P

HD = 64
PAIR = 2 * HD
EPS = 1e-05
FAR = 1.0e9
VMEM = 60 * 1024 * 1024
F32 = jnp.float32
BF16 = jnp.bfloat16


def nn(a, b):
    return lax.dot_general(a, b, (((1,), (0,)), ((), ())), preferred_element_type=F32)


def nt(a, b):
    return lax.dot_general(a, b, (((1,), (1,)), ((), ())), preferred_element_type=F32)


def tn(a, b):
    return lax.dot_general(a, b, (((0,), (0,)), ((), ())), preferred_element_type=F32)


def params(collective=None):
    if collective is None:
        return pltpu.CompilerParams(vmem_limit_bytes=VMEM)
    return pltpu.CompilerParams(
        vmem_limit_bytes=VMEM, collective_id=collective, has_side_effects=True
    )


def cost(flops, moved):
    return pl.CostEstimate(flops=int(flops), bytes_accessed=int(moved), transcendentals=0)


def normed(h):
    centred = h - jnp.mean(h, axis=-1, keepdims=True)
    rstd = lax.rsqrt(jnp.mean(centred * centred, axis=-1, keepdims=True) + EPS)
    return centred * rstd, rstd


def norm_back(grad, n, rstd, gain):
    scaled = grad * gain
    centre = jnp.mean(scaled, axis=-1, keepdims=True)
    along = jnp.mean(scaled * n, axis=-1, keepdims=True)
    return rstd * (scaled - centre - n * along)


def total(a):
    return jnp.sum(a.astype(F32), axis=0, keepdims=True)


def place():
    me = lax.axis_index("dp")
    return me, me % 2, (me // 2) % 2, me // 4


def partner(hop):
    me, c, x, z = place()
    if hop == "core":
        return {"dp": me + 1 - 2 * c}
    if hop == "x":
        return {"dp": me + 2 - 4 * x}
    if hop == "z1":
        return {"dp": me + 4 - 8 * (z % 2)}
    if hop == "z3":
        return {"dp": me + 4 * (3 - 2 * z)}
    return {"sp": 1 - lax.axis_index("sp")}


def beside(z, mask):
    if mask == 0:
        return z
    if mask == 1:
        return z + 1 - 2 * (z % 2)
    if mask == 2:
        return (z + 2) % 4
    return 3 - z


def greet(hops):
    barrier = pltpu.get_barrier_semaphore()
    for hop in hops:
        pl.semaphore_signal(barrier, inc=1, device_id=partner(hop), device_id_type=pl.DeviceIdType.MESH)
    pl.semaphore_wait(barrier, len(hops))


def remote(src, dst, send, recv, hop):
    return pltpu.make_async_remote_copy(
        src_ref=src, dst_ref=dst, send_sem=send, recv_sem=recv,
        device_id=partner(hop), device_id_type=pl.DeviceIdType.MESH,
    )


def first_z(hop, keep):
    kept = (0, 3) if hop == "z1" else (0, 1)
    return kept if keep else tuple(m ^ (1 if hop == "z1" else 3) for m in kept)


def exchange(hop, src, cols, into, kept, send, recv, local):
    _, _, x, z = place()
    at = pl.ds(*cols)
    rest = (slice(None),) * (len(src.shape) - 2)
    tail = rest + (at,)
    if hop == "x":
        lead = (slice(None),) * (len(src.shape) - 3)
        mine, yours = [(lead + (x,), ())], [(lead + (1 - x,), ())]
        tail = (slice(None), at)
    elif src.shape[0] == 4:
        mine = [((beside(z, m),), (i,)) for i, m in enumerate(first_z(hop, True))]
        yours = [((beside(z, m),), (i,)) for i, m in enumerate(first_z(hop, False))]
    else:
        mine, yours = [((0,), ())], [((1,), ())]
    away = [
        remote(src.at[frm + tail], into.at[to] if to else into, send.at[i], recv.at[i], hop)
        for i, (frm, to) in enumerate(yours)
    ]
    near = [
        pltpu.make_async_copy(src.at[frm + tail], kept.at[to] if to else kept, local.at[i])
        for i, (frm, to) in enumerate(mine)
    ]
    return away, near


def code_of(docs_ref):
    row = lax.broadcasted_iota(jnp.int32, (128, docs_ref.shape[1]), 0)
    return jnp.transpose(jnp.where(docs_ref[...] == row, 1.0, 0.0)).astype(BF16)


def project_kernel(
    x_ref, m_ref, td_ref, md_ref, wx_ref, wm_ref, b_ref,
    qkv_ref, mkv_ref, kvo_ref, xo_ref, mem_ref, to_ref, mo_ref, tt_ref, mt_ref,
    came_ref, tdo_ref, mdo_ref, send_ref, recv_ref,
):
    step = pl.program_id(0)
    sp = lax.axis_index("sp")
    peer = "sp"
    rows_out = remote(x_ref, came_ref, send_ref.at[0], recv_ref.at[0], peer)
    docs = [
        remote(td_ref, tdo_ref, send_ref.at[1], recv_ref.at[1], peer),
        remote(md_ref, mdo_ref, send_ref.at[2], recv_ref.at[2], peer),
    ]

    @pl.when(step == 0)
    def _():
        greet([peer])
        for copy in docs:
            copy.start()
        pl.when(sp == 0)(rows_out.start)
        to_ref[...] = code_of(td_ref)
        mo_ref[...] = code_of(md_ref)
        mem_ref[...] = m_ref[...]

    @pl.when(step < 3)
    def _():
        bias = jnp.where(step == 0, b_ref[0:1], 0.0) + jnp.where(step == 2, b_ref[1:2], 0.0)
        qkv_ref[...] = (nn(x_ref[...], wx_ref[...]) + bias).astype(BF16)

    @pl.when(jnp.logical_and(step >= 3, step < 5))
    def _():
        bias = jnp.where(step == 4, b_ref[2:3], 0.0)
        mkv_ref[...] = (nn(m_ref[...], wm_ref[...]) + bias).astype(BF16)

    @pl.when(step == 4)
    def _():
        for copy in docs:
            copy.wait()
        tt_ref[...] = code_of(tdo_ref)
        mt_ref[...] = code_of(mdo_ref)
        pl.when(sp == 0)(rows_out.wait_send)

        @pl.when(sp == 1)
        def _():
            rows_out.wait_recv()
            xo_ref[...] = came_ref[...]

    @pl.when(jnp.logical_and(step >= 5, sp == 1))
    def _():
        bias = jnp.where(step == 6, b_ref[1:2], 0.0)
        kvo_ref[...] = (nn(came_ref[...], wx_ref[...]) + bias).astype(BF16)

    @pl.when(jnp.logical_and(step >= 5, sp == 0))
    def _():
        kvo_ref[...] = jnp.zeros(kvo_ref.shape, BF16)
        xo_ref[...] = jnp.zeros(xo_ref.shape, BF16)


def project_first(x, mem, td, md, wx, wm, biases):
    rows, width = x.shape
    code = jax.ShapeDtypeStruct((rows, 128), BF16)

    def flat(cols):
        return jax.ShapeDtypeStruct((rows, cols), BF16)

    return pl.pallas_call(
        project_kernel,
        grid=(7,),
        in_specs=[
            whole((rows, width)), whole((rows, width)), whole((1, rows)), whole((1, rows)),
            pl.BlockSpec((width, width), lambda s: (0, jnp.where(s < 3, s, jnp.maximum(s - 4, 1)))),
            pl.BlockSpec((width, width), lambda s: (0, jnp.clip(s - 3, 0, 1))),
            whole(biases.shape),
        ],
        out_specs=[
            pl.BlockSpec((rows, width), lambda s: (0, jnp.minimum(s, 2))),
            pl.BlockSpec((rows, width), lambda s: (0, jnp.clip(s - 3, 0, 1))),
            pl.BlockSpec((rows, width), lambda s: (0, jnp.clip(s - 5, 0, 1))),
            whole((rows, width)), whole((rows, width)),
            whole((rows, 128)), whole((rows, 128)), whole((rows, 128)), whole((rows, 128)),
        ],
        out_shape=[flat(3 * width), flat(2 * width), flat(2 * width), flat(width), flat(width)] + [code] * 4,
        scratch_shapes=[
            pltpu.VMEM((rows, width), BF16),
            pltpu.VMEM((1, rows), jnp.int32),
            pltpu.VMEM((1, rows), jnp.int32),
            pltpu.SemaphoreType.DMA((3,)),
            pltpu.SemaphoreType.DMA((3,)),
        ],
        compiler_params=params(1),
        cost_estimate=cost(14 * rows * width * width, 20 * width * width),
        name="project_first",
    )(x, mem, td, md, wx, wm, biases)


def project_memory_kernel(x_ref, w_ref, b_ref, o_ref):
    bias = jnp.where(pl.program_id(0) == 1, b_ref[2:3], 0.0)
    o_ref[...] = (nn(x_ref[...], w_ref[...]) + bias).astype(BF16)


def project_memory(x, w, biases):
    rows, width = x.shape
    return pl.pallas_call(
        project_memory_kernel,
        grid=(2,),
        in_specs=[
            whole((rows, width)),
            pl.BlockSpec((width, width), lambda j: (0, j)),
            whole(biases.shape),
        ],
        out_specs=pl.BlockSpec((rows, width), lambda j: (0, j)),
        out_shape=jax.ShapeDtypeStruct((rows, 2 * width), BF16),
        compiler_params=params(),
        cost_estimate=cost(4 * rows * width * width, 4 * width * (width + rows)),
        name="project_memory",
    )(x, w, biases)


def head_masks(dtype):
    lane = lax.broadcasted_iota(jnp.int32, (1, PAIR), 1)
    low = jnp.where(lane < HD, 1.0, 0.0)
    return low.astype(dtype), (1.0 - low).astype(dtype)


def query_code(code):
    lane = lax.broadcasted_iota(jnp.int32, code.shape, 1)
    return jnp.where(lane < 4, (code.astype(F32) - 1.0) * FAR, 0.0).astype(BF16)


def softmax_pieces(scores, values):
    peak = functools.reduce(jnp.maximum, [jnp.max(s, axis=-1, keepdims=True) for s in scores])
    expd = [jnp.exp(s - peak) for s in scores]
    norm = sum(jnp.sum(e, axis=-1, keepdims=True) for e in expd)
    out = sum(nn(e.astype(BF16), v) for e, v in zip(expd, values))
    return out / norm, peak + jnp.log(norm)


def self_pieces(block, size, both, own, other):
    pieces = []
    if both:
        pieces.append((other, False))
    if block:
        pieces.append((own[: block * size], False))
    pieces.append((own[block * size : (block + 1) * size], True))
    return pieces


def store_lse(lse_ref, block, size, low, high):
    lane = lax.broadcasted_iota(jnp.int32, (size, PAIR), 1)
    both = jnp.where(lane == 0, low, high)
    lse_ref[:, block * size : (block + 1) * size] = jnp.transpose(both)[:8]


def self_forward_kernel(size, q_ref, k_ref, v_ref, ko_ref, vo_ref, own_ref, oth_ref, o_ref, lse_ref):
    second = lax.axis_index("sp") == 1
    rows = q_ref.shape[0]
    masks = head_masks(BF16)
    outs = head_masks(F32)

    def run(both):
        qcode = query_code(own_ref[...])
        own = jnp.concatenate([k_ref[...], own_ref[...]], axis=1)
        oth = jnp.concatenate([ko_ref[...], oth_ref[...]], axis=1) if both else None
        vown = v_ref[...]
        voth = vo_ref[...] if both else None
        for block in range(rows // size):
            at = slice(block * size, (block + 1) * size)
            lses, result = [], 0.0
            for mask, keep in zip(masks, outs):
                q = jnp.concatenate([q_ref[at] * (mask * BF16(HD**-0.5)), qcode[at]], axis=1)
                scores = []
                for keys, diagonal in self_pieces(block, size, both, own, oth):
                    s = nt(q, keys)
                    if diagonal:
                        row = lax.broadcasted_iota(jnp.int32, s.shape, 0)
                        col = lax.broadcasted_iota(jnp.int32, s.shape, 1)
                        s = jnp.where(row >= col, s, -FAR)
                    scores.append(s)
                values = [v for v, _ in self_pieces(block, size, both, vown, voth)]
                out, lse = softmax_pieces(scores, values)
                result = result + out * keep
                lses.append(lse)
            o_ref[at] = result.astype(BF16)
            store_lse(lse_ref, block, size, *lses)

    pl.when(second)(lambda: run(True))
    pl.when(jnp.logical_not(second))(lambda: run(False))


def pair_spec(rows, offset):
    return pl.BlockSpec((rows, PAIR), lambda p: (0, p + offset))


def whole(shape):
    return pl.BlockSpec(shape, lambda *_: (0,) * len(shape))


def self_forward(qkv, kvo, own, oth):
    rows = qkv.shape[0]
    width = qkv.shape[1] // 3
    pairs = width // PAIR
    return pl.pallas_call(
        functools.partial(self_forward_kernel, 256),
        grid=(pairs,),
        in_specs=[
            pair_spec(rows, 0),
            pair_spec(rows, pairs),
            pair_spec(rows, 2 * pairs),
            pair_spec(rows, 0),
            pair_spec(rows, pairs),
            whole((rows, 128)),
            whole((rows, 128)),
        ],
        out_specs=[pair_spec(rows, 0), pl.BlockSpec((8, rows), lambda p: (p, 0))],
        out_shape=[
            jax.ShapeDtypeStruct((rows, width), BF16),
            jax.ShapeDtypeStruct((8 * pairs, rows), F32),
        ],
        compiler_params=params(),
        cost_estimate=cost(16 * rows * rows * width, 16 * rows * width),
        name="self_forward",
    )(qkv, qkv, qkv, kvo, kvo, own, oth)


def cross_forward_kernel(size, q_ref, k_ref, v_ref, ko_ref, vo_ref, t_ref, own_ref, oth_ref, o_ref, lse_ref):
    rows = q_ref.shape[0]
    masks = head_masks(BF16)
    outs = head_masks(F32)
    qcode = query_code(t_ref[...])
    keys = [
        jnp.concatenate([k_ref[...], own_ref[...]], axis=1),
        jnp.concatenate([ko_ref[...], oth_ref[...]], axis=1),
    ]
    values = [v_ref[...], vo_ref[...]]
    for block in range(rows // size):
        at = slice(block * size, (block + 1) * size)
        lses, result = [], 0.0
        for mask, keep in zip(masks, outs):
            q = jnp.concatenate([q_ref[at] * (mask * BF16(HD**-0.5)), qcode[at]], axis=1)
            out, lse = softmax_pieces([nt(q, k) for k in keys], values)
            result = result + out * keep
            lses.append(lse)
        o_ref[at] = result.astype(BF16)
        store_lse(lse_ref, block, size, *lses)


def cross_forward(cq, kv, kvo, t, own, oth):
    rows, width = cq.shape
    pairs = width // PAIR
    return pl.pallas_call(
        functools.partial(cross_forward_kernel, 256),
        grid=(pairs,),
        in_specs=[
            pair_spec(rows, 0),
            pair_spec(rows, 0),
            pair_spec(rows, pairs),
            pair_spec(rows, 0),
            pair_spec(rows, pairs),
            whole((rows, 128)),
            whole((rows, 128)),
            whole((rows, 128)),
        ],
        out_specs=[pair_spec(rows, 0), pl.BlockSpec((8, rows), lambda p: (p, 0))],
        out_shape=[
            jax.ShapeDtypeStruct((rows, width), BF16),
            jax.ShapeDtypeStruct((8 * pairs, rows), F32),
        ],
        compiler_params=params(),
        cost_estimate=cost(24 * rows * rows * width, 16 * rows * width),
        name="cross_forward",
    )(cq, kv, kv, kvo, kvo, t, own, oth)


def delta_rows(g, o):
    prod = g.astype(F32) * o.astype(F32)
    upper = prod.astype(BF16)
    lower = (prod - upper.astype(F32)).astype(BF16)
    row = lax.broadcasted_iota(jnp.int32, (8, PAIR), 0)
    lane = lax.broadcasted_iota(jnp.int32, (8, PAIR), 1)
    pick = jnp.where(row == lane // HD, 1.0, 0.0).astype(BF16)
    return nt(pick, upper) + nt(pick, lower)


def back_piece(keys, values, q, g, lse, delta, causal):
    s = nt(keys, q)
    if causal:
        row = lax.broadcasted_iota(jnp.int32, s.shape, 0)
        col = lax.broadcasted_iota(jnp.int32, s.shape, 1)
        s = jnp.where(row <= col, s, -FAR)
    p = jnp.exp(s - lse)
    ds = p * (nt(values, g) - delta)
    return p.astype(BF16), ds.astype(BF16)


FEED_PARTS = (
    (0, (0, 1024), "x", "z1"),
    (0, (1024, 1024), "x", "z3"),
    (0, (2048, 512), "z1", "z3"),
    (0, (2560, 512), "z3", "z1"),
    (1, (0, 384), "z1", "z3"),
    (1, (384, 384), "z3", "z1"),
)


def part_shapes(shape, cols, first):
    rows = shape[2]
    if first == "x":
        return (4, rows, cols[1]), (2, rows, cols[1])
    return (2, 2, rows, cols[1]), (2, rows, cols[1])


def cross_backward_kernel(size, parts, *refs):
    (q_ref, k_ref, v_ref, ko_ref, vo_ref, g_ref, o_ref, lse_ref, t_ref, own_ref, oth_ref,
     m_ref, mo_ref, wk_ref, wv_ref) = refs[:15]
    refs = refs[15:]
    grads, refs = refs[:2 if parts else 0], refs[2 if parts else 0 :]
    dq_ref, dm_ref, dmo_ref, gk_ref, gv_ref, gb_ref = refs[:6]
    refs = refs[6:]
    count = len(parts)
    done, refs = refs[:count], refs[count:]
    dm_acc, dmo_acc, refs = refs[0], refs[1], refs[2:]
    if parts:
        came1, kept1, came2 = refs[:count], refs[count : 2 * count], refs[2 * count : 3 * count]
        send, recv, local = refs[3 * count :]
    step = pl.program_id(0)
    rows = q_ref.shape[0]
    masks = head_masks(BF16)
    scale = BF16(HD**-0.5)

    if parts:
        one, two = [], []
        for i, (array, cols, first, second) in enumerate(parts):
            one.append(
                exchange(first, grads[array], cols, came1[i], kept1[i], send.at[i], recv.at[i], local.at[i])
            )
            two.append(
                exchange(
                    second, kept1[i], (0, cols[1]), came2[i], done[i],
                    send.at[count + i], recv.at[count + i], local.at[count + i],
                )
            )

        @pl.when(step == 0)
        def _():
            greet(["x", "z1", "z3"])
            for away, near in one:
                for copy in away + near:
                    copy.start()

        @pl.when(step == 3)
        def _():
            for i, (away, near) in enumerate(one):
                for copy in away + near:
                    copy.wait()
                kept1[i][...] += came1[i][...]
                for copy in two[i][0] + two[i][1]:
                    copy.start()

    qcode = query_code(t_ref[...])
    delta = delta_rows(g_ref[...], o_ref[...])
    lse = lse_ref[...]
    halves = [(k_ref, v_ref, own_ref, m_ref, dm_acc), (ko_ref, vo_ref, oth_ref, mo_ref, dmo_acc)]
    dq = [0.0] * (rows // size)
    gk = gv = gb = 0.0
    for kr, vr, code, mem, acc in halves:
        keys = jnp.concatenate([kr[...], code[...]], axis=1)
        values = vr[...]
        dk = dv = 0.0
        for block in range(rows // size):
            at = slice(block * size, (block + 1) * size)
            for head, mask in enumerate(masks):
                qm = q_ref[at] * (mask * scale)
                gm = g_ref[at] * mask
                q = jnp.concatenate([qm, qcode[at]], axis=1)
                p, ds = back_piece(
                    keys, values, q, gm, lse[head : head + 1, at], delta[head : head + 1, at], False
                )
                dk = dk + nn(ds, qm)
                dv = dv + nn(p, gm)
                dq[block] = dq[block] + tn(ds, kr[...] * (mask * scale))
        both = jnp.concatenate([dk.astype(BF16), dv.astype(BF16)], axis=1)
        grad = tn(mem[...], both)
        gk, gv = gk + grad[:, :PAIR], gv + grad[:, PAIR:]
        gb = gb + total(both[:, PAIR:])
        dm = nt(both, jnp.concatenate([wk_ref[...], wv_ref[...]], axis=1))

        @pl.when(step == 0)
        def _():
            acc[...] = dm

        @pl.when(step > 0)
        def _():
            acc[...] += dm
    for block in range(rows // size):
        dq_ref[block * size : (block + 1) * size] = dq[block].astype(BF16)
    gk_ref[...] = gk.astype(BF16)
    gv_ref[...] = gv.astype(BF16)
    gb_ref[...] = gb

    @pl.when(step == pl.num_programs(0) - 1)
    def _():
        dm_ref[...] = dm_acc[...]
        dmo_ref[...] = dmo_acc[...].astype(BF16)
        if parts:
            for i, (away, near) in enumerate(two):
                for copy in away + near:
                    copy.wait()
                done[i][...] += came2[i][...]


def cross_backward(cq, kv, kvo, g, o, lse, t, own, oth, m, mo, w, grads):
    rows, width = cq.shape
    pairs = width // PAIR
    parts = FEED_PARTS if grads else ()
    shapes = [part_shapes(grads[array].shape, cols, first) for array, cols, first, _ in parts]
    ones, after = [a for a, _ in shapes], [b for _, b in shapes]
    scratch = [pltpu.VMEM((rows, width), F32)] * 2
    if parts:
        scratch += [pltpu.VMEM(a, BF16) for a in ones + ones + after]
        sems = pltpu.SemaphoreType.DMA((2 * len(parts), 2))
        scratch += [sems, sems, sems]
    flat = jax.ShapeDtypeStruct((rows, width), BF16)
    square = jax.ShapeDtypeStruct((width, width), BF16)
    return pl.pallas_call(
        functools.partial(cross_backward_kernel, 256, parts),
        grid=(pairs,),
        in_specs=[
            pair_spec(rows, 0),
            pair_spec(rows, 0),
            pair_spec(rows, pairs),
            pair_spec(rows, 0),
            pair_spec(rows, pairs),
            pair_spec(rows, 0),
            pair_spec(rows, 0),
            pl.BlockSpec((8, rows), lambda p: (p, 0)),
            whole((rows, 128)),
            whole((rows, 128)),
            whole((rows, 128)),
            whole((rows, width)),
            whole((rows, width)),
            pair_spec(width, 0),
            pair_spec(width, pairs),
        ]
        + [pl.BlockSpec(memory_space=pl.ANY)] * len(grads),
        out_specs=[pair_spec(rows, 0)]
        + [whole((rows, width))] * 2
        + [pair_spec(width, 0)] * 2
        + [pair_spec(1, 0)]
        + [whole(a) for a in after],
        out_shape=[flat, jax.ShapeDtypeStruct((rows, width), F32), flat, square, square, jax.ShapeDtypeStruct((1, width), F32)]
        + [jax.ShapeDtypeStruct(a, BF16) for a in after],
        scratch_shapes=scratch,
        compiler_params=params(3 if parts else None),
        cost_estimate=cost(64 * rows * rows * width + 16 * rows * width * width, 24 * rows * width),
        name="cross_backward",
    )(cq, kv, kv, kvo, kvo, g, o, lse, t, own, oth, m, mo, w, w, *grads)


def self_backward_kernel(
    size, q_ref, k_ref, v_ref, ko_ref, vo_ref, g_ref, o_ref, lse_ref, own_ref, oth_ref,
    dq_ref, dk_ref, dv_ref, dko_ref, dvo_ref,
):
    second = lax.axis_index("sp") == 1
    rows = q_ref.shape[0]
    masks = head_masks(BF16)
    scale = BF16(HD**-0.5)

    def run(both):
        qcode = query_code(own_ref[...])
        delta = delta_rows(g_ref[...], o_ref[...])
        lse = lse_ref[...]
        count = rows // size
        dk, dv = [0.0] * count, [0.0] * count
        dko = dvo = 0.0
        for block in range(count):
            at = slice(block * size, (block + 1) * size)
            dq = 0.0
            for head, mask in enumerate(masks):
                qm = q_ref[at] * (mask * scale)
                gm = g_ref[at] * mask
                q = jnp.concatenate([qm, qcode[at]], axis=1)
                rest = (q, gm, lse[head : head + 1, at], delta[head : head + 1, at])
                for part in range(block + 1):
                    of = slice(part * size, (part + 1) * size)
                    keys = jnp.concatenate([k_ref[of], own_ref[of]], axis=1)
                    p, ds = back_piece(keys, v_ref[of], *rest, part == block)
                    dk[part] = dk[part] + nn(ds, qm)
                    dv[part] = dv[part] + nn(p, gm)
                    dq = dq + tn(ds, k_ref[of] * (mask * scale))
                if both:
                    keys = jnp.concatenate([ko_ref[...], oth_ref[...]], axis=1)
                    p, ds = back_piece(keys, vo_ref[...], *rest, False)
                    dko = dko + nn(ds, qm)
                    dvo = dvo + nn(p, gm)
                    dq = dq + tn(ds, ko_ref[...] * (mask * scale))
            dq_ref[at] = dq.astype(BF16)
        for part in range(count):
            of = slice(part * size, (part + 1) * size)
            dk_ref[of] = dk[part].astype(BF16)
            dv_ref[of] = dv[part].astype(BF16)
        if both:
            dko_ref[...] = dko.astype(BF16)
            dvo_ref[...] = dvo.astype(BF16)
        else:
            dko_ref[...] = jnp.zeros(dko_ref.shape, BF16)
            dvo_ref[...] = jnp.zeros(dvo_ref.shape, BF16)

    pl.when(second)(lambda: run(True))
    pl.when(jnp.logical_not(second))(lambda: run(False))


def self_backward(qkv, kvo, g, o, lse, own, oth):
    rows = qkv.shape[0]
    width = qkv.shape[1] // 3
    pairs = width // PAIR
    flat = jax.ShapeDtypeStruct((rows, width), BF16)
    return pl.pallas_call(
        functools.partial(self_backward_kernel, 256),
        grid=(pairs,),
        in_specs=[
            pair_spec(rows, 0),
            pair_spec(rows, pairs),
            pair_spec(rows, 2 * pairs),
            pair_spec(rows, 0),
            pair_spec(rows, pairs),
            pair_spec(rows, 0),
            pair_spec(rows, 0),
            pl.BlockSpec((8, rows), lambda p: (p, 0)),
            whole((rows, 128)),
            whole((rows, 128)),
        ],
        out_specs=[pair_spec(rows, 0)] * 5,
        out_shape=[flat] * 5,
        compiler_params=params(),
        cost_estimate=cost(48 * rows * rows * width, 24 * rows * width),
        name="self_backward",
    )(qkv, qkv, qkv, kvo, kvo, g, o, lse, own, oth)


def first_norm_kernel(x_ref, ctx_ref, wo_ref, wq_ref, b_ref, h_ref, cq_ref):
    h = x_ref[...].astype(F32) + nn(ctx_ref[...], wo_ref[...]) + b_ref[3:4]
    h_ref[...] = h
    n, _ = normed(h)
    a = (n * b_ref[4:5] + b_ref[5:6]).astype(BF16)
    cq_ref[...] = (nn(a, wq_ref[...]) + b_ref[6:7]).astype(BF16)


def first_norm(x, ctx, wo, wq, biases):
    rows, width = x.shape
    return pl.pallas_call(
        first_norm_kernel,
        out_shape=[
            jax.ShapeDtypeStruct((rows, width), F32),
            jax.ShapeDtypeStruct((rows, width), BF16),
        ],
        compiler_params=params(),
        cost_estimate=cost(4 * rows * width * width, 4 * width * width + 10 * rows * width),
        name="first_norm",
    )(x, ctx, wo, wq, biases)


def feed_kernel(
    count, comm, h1_ref, cc_ref, ct_ref, wco_ref, b_ref, wi_ref, wo_ref,
    out_ref, dh2_ref, dcc_ref, gco_ref, gwi_ref, gwo_ref, small_ref, gib_ref,
    hid_ref, slope_ref, n2_ref, r2_ref, a2b_ref, acc_ref, df_ref, *refs,
):
    step = pl.program_id(0)
    width = acc_ref.shape[1]

    if comm:
        mi_ref, mo_ref, ci_ref, co_ref, send_ref, recv_ref = refs
        _, c, _, _ = place()

        def chunk_copies(j):
            at = pl.ds(pl.multiple_of(j * width, width), width)
            return [
                remote(
                    mi_ref.at[:, 1 - c, :, at], ci_ref.at[:, :, at], send_ref.at[0, j], recv_ref.at[0, j], "core"
                ),
                remote(mo_ref.at[j, :, 1 - c], co_ref.at[j], send_ref.at[1, j], recv_ref.at[1, j], "core"),
            ]

    @pl.when(step == 0)
    def _():
        if comm:
            greet(["core"])
        n1, _ = normed(h1_ref[...])
        a1 = n1 * b_ref[4:5] + b_ref[5:6]
        h2 = a1 + nn(cc_ref[...], wco_ref[...]) + b_ref[7:8]
        n2, r2 = normed(h2)
        n2_ref[...] = n2
        r2_ref[...] = jnp.broadcast_to(r2, r2_ref.shape)
        a2 = n2 * b_ref[8:9] + b_ref[9:10]
        a2b_ref[...] = a2.astype(BF16)
        acc_ref[...] = a2 + b_ref[10:11]

    @pl.when(step < count)
    def _():
        u = nn(a2b_ref[...], wi_ref[...]) + b_ref[pl.ds(13 + step, 1)]
        cumul = 0.5 * (1.0 + lax.erf(u * 0.7071067811865476))
        density = jnp.exp(-0.5 * u * u) * 0.3989422804014327
        hid = (u * cumul).astype(BF16)
        hid_ref[step] = hid
        slope_ref[step] = cumul + u * density
        acc_ref[...] += nn(hid, wo_ref[...])

    @pl.when(step == count - 1)
    def _():
        n3, r3 = normed(acc_ref[...])
        gain = b_ref[11:12]
        out_ref[...] = (n3 * gain + b_ref[12:13]).astype(BF16)
        e = ct_ref[...].astype(F32)
        d3 = norm_back(e, n3, r3, gain)
        df = d3.astype(BF16)
        df_ref[...] = df
        acc_ref[...] = d3
        small_ref[0:1] = total(e * n3)
        small_ref[1:2] = total(e)
        small_ref[2:3] = total(df)

    @pl.when(jnp.logical_and(step >= count, step < 2 * count))
    def _():
        j = step - count
        df = df_ref[...]
        du = (nt(df, wo_ref[...]) * slope_ref[j]).astype(BF16)
        gib_ref[...] = total(du)
        acc_ref[...] += nt(du, wi_ref[...])
        go = tn(hid_ref[j], df).astype(BF16)
        gi = tn(a2b_ref[...], du).astype(BF16)
        if comm:
            at = pl.ds(pl.multiple_of(j * width, width), width)
            mo_ref[j] = go.reshape(mo_ref.shape[1:])
            mi_ref[:, :, :, at] = gi.reshape(mi_ref.shape[:3] + (width,))
            for copy in chunk_copies(j):
                copy.start()
        else:
            gwo_ref[...] = go
            gwi_ref[...] = gi

    @pl.when(step == 2 * count)
    def _():
        d2 = acc_ref[...]
        n2 = n2_ref[...]
        dh2 = norm_back(d2, n2, r2_ref[:, :1], b_ref[8:9])
        dh2_ref[...] = dh2
        dco = dh2.astype(BF16)
        dcc_ref[...] = nt(dco, wco_ref[...]).astype(BF16)
        gco_ref[...] = tn(cc_ref[...], dco).astype(BF16)
        small_ref[3:4] = total(d2 * n2)
        small_ref[4:5] = total(d2)
        small_ref[5:6] = total(dco)
        small_ref[6:8] = jnp.zeros((2, d2.shape[1]), F32)

    if comm:

        @pl.when(step > count)
        def _():
            j = step - count - 1
            at = pl.ds(pl.multiple_of(j * width, width), width)
            for copy in chunk_copies(j):
                copy.wait()
            gwi_ref[...] = mi_ref[:, c, :, at] + ci_ref[:, :, at]
            gwo_ref[0] = mo_ref[j, :, c] + co_ref[j]


def feed(size, comm, h1, cc, ct, wco, biases, wi, wo):
    rows, width = h1.shape
    wide = wi.shape[1]
    chunk = width
    count = wide // chunk

    def weight(s):
        return jnp.where(s < count, s, jnp.minimum(s - count, count - 1))

    def early(s):
        return jnp.clip(s - count, 0, count - 1)

    def late(s):
        return jnp.clip(s - count - 1, 0, count - 1)

    flat = whole((rows, width))
    square = whole((width, width))
    scratch = [
        pltpu.VMEM((count, rows, chunk), BF16),
        pltpu.VMEM((count, rows, chunk), F32),
        pltpu.VMEM((rows, width), F32),
        pltpu.VMEM((rows, 128), F32),
        pltpu.VMEM((rows, width), BF16),
        pltpu.VMEM((rows, width), F32),
        pltpu.VMEM((rows, width), BF16),
    ]
    if comm:
        narrow, broad = width // size, wide // size
        grad_specs = [
            pl.BlockSpec((size // 2, narrow, chunk), lambda s: (0, 0, late(s))),
            pl.BlockSpec((1, 2, broad, width), lambda s: (late(s), 0, 0, 0)),
        ]
        grad_shapes = [(size // 2, narrow, wide), (count, 2, broad, width)]
        scratch += [
            pltpu.VMEM((size // 2, 2, narrow, wide), BF16),
            pltpu.VMEM((count, 2, 2, broad, width), BF16),
            pltpu.VMEM((size // 2, narrow, wide), BF16),
            pltpu.VMEM((count, 2, broad, width), BF16),
            pltpu.SemaphoreType.DMA((2, count)),
            pltpu.SemaphoreType.DMA((2, count)),
        ]
    else:
        grad_specs = [
            pl.BlockSpec((width, chunk), lambda s: (0, early(s))),
            pl.BlockSpec((chunk, width), lambda s: (early(s), 0)),
        ]
        grad_shapes = [(width, wide), (wide, width)]
    return pl.pallas_call(
        functools.partial(feed_kernel, count, comm),
        grid=(2 * count + 1,),
        in_specs=[
            flat, flat, flat, square, whole(biases.shape),
            pl.BlockSpec((width, chunk), lambda s: (0, weight(s))),
            pl.BlockSpec((chunk, width), lambda s: (weight(s), 0)),
        ],
        out_specs=[flat, flat, flat, square]
        + grad_specs
        + [whole((8, width)), pl.BlockSpec((1, chunk), lambda s: (0, early(s)))],
        out_shape=[
            jax.ShapeDtypeStruct((rows, width), BF16),
            jax.ShapeDtypeStruct((rows, width), F32),
            jax.ShapeDtypeStruct((rows, width), BF16),
            jax.ShapeDtypeStruct((width, width), BF16),
        ]
        + [jax.ShapeDtypeStruct(a, BF16) for a in grad_shapes]
        + [
            jax.ShapeDtypeStruct((8, width), F32),
            jax.ShapeDtypeStruct((1, wide), F32),
        ],
        scratch_shapes=scratch,
        compiler_params=params(2 if comm else None),
        cost_estimate=cost(
            12 * rows * width * wide + 6 * rows * width * width, 12 * width * wide + 16 * rows * width
        ),
        name="feed",
    )(h1, cc, ct, wco, biases, wi, wo)


def first_back_kernel(
    dcq_ref, dh2_ref, h1_ref, ctx_ref, wcq_ref, wso_ref, b_ref,
    dh1_ref, dsc_ref, gcq_ref, gso_ref, small_ref,
):
    gain = b_ref[4:5]
    n1, r1 = normed(h1_ref[...])
    a1b = (n1 * gain + b_ref[5:6]).astype(BF16)
    dcq = dcq_ref[...]
    d1 = dh2_ref[...] + nt(dcq, wcq_ref[...])
    dh1 = norm_back(d1, n1, r1, gain)
    dh1_ref[...] = dh1
    dso = dh1.astype(BF16)
    dsc_ref[...] = nt(dso, wso_ref[...]).astype(BF16)
    gcq_ref[...] = tn(a1b, dcq).astype(BF16)
    gso_ref[...] = tn(ctx_ref[...], dso).astype(BF16)
    small_ref[0:1] = total(dcq)
    small_ref[1:2] = total(d1 * n1)
    small_ref[2:3] = total(d1)
    small_ref[3:4] = total(dso)
    small_ref[4:8] = jnp.zeros((4, dh1.shape[1]), F32)


def first_back(dcq, dh2, h1, ctx, wcq, wso, biases):
    rows, width = dcq.shape
    return pl.pallas_call(
        first_back_kernel,
        out_shape=[
            jax.ShapeDtypeStruct((rows, width), F32),
            jax.ShapeDtypeStruct((rows, width), BF16),
            jax.ShapeDtypeStruct((width, width), BF16),
            jax.ShapeDtypeStruct((width, width), BF16),
            jax.ShapeDtypeStruct((8, width), F32),
        ],
        compiler_params=params(),
        cost_estimate=cost(8 * rows * width * width, 8 * width * width + 18 * rows * width),
        name="first_back",
    )(dcq, dh2, h1, ctx, wcq, wso, biases)


def other_input_kernel(dko_ref, dvo_ref, w_ref, dxo_ref):
    width = dko_ref.shape[1]

    @pl.when(lax.axis_index("sp") == 1)
    def _():
        dxo = nt(dko_ref[...], w_ref[:, width : 2 * width]) + nt(dvo_ref[...], w_ref[:, 2 * width :])
        dxo_ref[...] = dxo.astype(BF16)

    @pl.when(lax.axis_index("sp") == 0)
    def _():
        dxo_ref[...] = jnp.zeros(dxo_ref.shape, BF16)


def other_input(dko, dvo, w):
    rows, width = dko.shape
    return pl.pallas_call(
        other_input_kernel,
        out_shape=jax.ShapeDtypeStruct((rows, width), BF16),
        compiler_params=params(),
        cost_estimate=cost(4 * rows * width * width, 6 * width * width + 6 * rows * width),
        name="other_input",
    )(dko, dvo, w)


def input_weight_kernel(x_ref, xo_ref, dq_ref, dk_ref, dv_ref, dko_ref, dvo_ref, gw_ref, gb_ref):
    width = x_ref.shape[1]
    x = x_ref[...]
    gw_ref[:, :width] = tn(x, dq_ref[...]).astype(BF16)
    gb_ref[0:1] = total(dq_ref[...])
    gb_ref[2:8] = jnp.zeros((6, width), F32)

    @pl.when(lax.axis_index("sp") == 1)
    def _():
        xo = xo_ref[...]
        gw_ref[:, width : 2 * width] = (tn(x, dk_ref[...]) + tn(xo, dko_ref[...])).astype(BF16)
        gw_ref[:, 2 * width :] = (tn(x, dv_ref[...]) + tn(xo, dvo_ref[...])).astype(BF16)
        gb_ref[1:2] = total(dv_ref[...]) + total(dvo_ref[...])

    @pl.when(lax.axis_index("sp") == 0)
    def _():
        gw_ref[:, width : 2 * width] = tn(x, dk_ref[...]).astype(BF16)
        gw_ref[:, 2 * width :] = tn(x, dv_ref[...]).astype(BF16)
        gb_ref[1:2] = total(dv_ref[...])


def input_weight(x, xo, dq, dk, dv, dko, dvo):
    rows, width = x.shape
    return pl.pallas_call(
        input_weight_kernel,
        out_shape=[
            jax.ShapeDtypeStruct((width, 3 * width), BF16),
            jax.ShapeDtypeStruct((8, width), F32),
        ],
        compiler_params=params(),
        cost_estimate=cost(10 * rows * width * width, 6 * width * width + 14 * rows * width),
        name="input_weight",
    )(x, xo, dq, dk, dv, dko, dvo)


def input_back_kernel(dh1_ref, dq_ref, dk_ref, dv_ref, w_ref, dx_ref):
    width = dq_ref.shape[1]
    dx_ref[...] = (
        dh1_ref[...]
        + nt(dq_ref[...], w_ref[:, :width])
        + nt(dk_ref[...], w_ref[:, width : 2 * width])
        + nt(dv_ref[...], w_ref[:, 2 * width :])
    )


def input_back(dh1, dq, dk, dv, w):
    rows, width = dq.shape
    return pl.pallas_call(
        input_back_kernel,
        out_shape=jax.ShapeDtypeStruct((rows, width), F32),
        compiler_params=params(),
        cost_estimate=cost(6 * rows * width * width, 6 * width * width + 14 * rows * width),
        name="input_back",
    )(dh1, dq, dk, dv, w)


def swap_sum(part, axis, pairs):
    came = lax.ppermute(part, axis, pairs)
    return part.astype(F32) + came.astype(F32)


def sum_scatter(grad, size, order):
    rows, cols = grad.shape
    bits = size.bit_length() - 1
    me = lax.axis_index("dp")
    now = grad.reshape((2,) * bits + (rows // size, cols))
    left = list(range(bits))[::-1]
    for bit in [b for b in order if b < bits] + [b for b in range(bits) if b not in order]:
        axis = left.index(bit)
        mine = (me >> bit) & 1
        keep = lax.dynamic_index_in_dim(now, mine, axis, keepdims=False)
        send = lax.dynamic_index_in_dim(now, 1 - mine, axis, keepdims=False)
        came = lax.ppermute(send, "dp", [(i, i ^ (1 << bit)) for i in range(size)])
        now = (keep.astype(F32) + came.astype(F32)).astype(BF16)
        left.pop(axis)
    return swap_sum(now, "sp", [(0, 1), (1, 0)])


def finish_part(part, second, size):
    me = lax.axis_index("dp")
    if part[2] == "x":
        mask, keep, send = 12 if part[3] == "z1" else 4, second[0], second[1]
    else:
        mine = (me >> 1) & 1
        mask = 2
        keep = lax.dynamic_index_in_dim(second, mine, 0, keepdims=False)
        send = lax.dynamic_index_in_dim(second, 1 - mine, 0, keepdims=False)
    came = lax.ppermute(send, "dp", [(i, i ^ mask) for i in range(size)])
    now = (keep.astype(F32) + came.astype(F32)).astype(BF16)
    return swap_sum(now, "sp", [(0, 1), (1, 0)])


def per_device(
    size,
    inputs,
    memory,
    target_docs,
    memory_docs,
    cotangent,
    w_qkv,
    b_q,
    b_v,
    w_so,
    b_so,
    g_one,
    s_one,
    w_cq,
    b_cq,
    w_ckv,
    b_cv,
    w_co,
    b_co,
    g_two,
    s_two,
    w_fi,
    b_fi,
    w_fo,
    b_fo,
    g_three,
    s_three,
):
    rows, width = inputs.shape[1:]
    comm = size == 16
    swap = [(0, 1), (1, 0)]
    x, mem, ct = inputs[0], memory[0], cotangent[0]
    vectors = (b_q, b_v, b_cv, b_so, g_one, s_one, b_cq, b_co, g_two, s_two, b_fo, g_three, s_three, b_fi)
    biases = jnp.concatenate(vectors + (jnp.zeros(7 * width, BF16),)).astype(F32).reshape(24, width)

    qkv, mkv, kvo, x_o, mem_s, t_own, m_own, t_oth, m_oth = project_first(
        x, mem, target_docs, memory_docs, w_qkv, w_ckv, biases
    )
    mem_o = lax.ppermute(mem_s, "sp", swap)
    ctx, lse = self_forward(qkv, kvo, t_own, t_oth)
    h1, cq = first_norm(x, ctx, w_so, w_cq, biases)
    mkvo = project_memory(mem_o, w_ckv, biases)
    cc, clse = cross_forward(cq, mkv, mkvo, t_own, m_own, m_oth)
    output, dh2, dcc, gco, gwi, gwo, small_a, gib = feed(
        size, comm, h1, cc, ct, w_co, biases, w_fi, w_fo
    )
    if comm:
        grads = [gwi.reshape(4, 2, width // size, -1), gwo]
    else:
        grads = []
        t_fin = sum_scatter(gwi, size, (0, 1, 2, 3))
        t_fout = sum_scatter(gwo, size, (0, 2, 3, 1))
    dcq, dm, dmo, gck, gcv, gcvb, *second = cross_backward(
        cq, mkv, mkvo, dcc, cc, clse, t_own, m_own, m_oth, mem, mem_o, w_ckv, grads
    )
    dm_in = lax.ppermute(dmo, "sp", swap)
    dh1, dsc, gcq, gso, small_b = first_back(dcq, dh2, h1, ctx, w_cq, w_so, biases)
    if comm:
        shares = [finish_part(part, got, size) for part, got in zip(FEED_PARTS, second)]
        t_fin = jnp.concatenate(shares[:4], axis=1)
        t_fout = jnp.concatenate(shares[4:], axis=1)
    t_cout = sum_scatter(gco, size, (0, 1, 2, 3))
    t_cmem = sum_scatter(jnp.concatenate([gck, gcv], axis=1), size, (0, 1, 2, 3))
    t_cquery = sum_scatter(gcq, size, (0, 2, 3, 1))
    t_out = sum_scatter(gso, size, (0, 1, 2, 3))
    dq, dk, dv, dko, dvo = self_backward(qkv, kvo, dsc, ctx, lse, t_own, t_oth)
    dxo = other_input(dko, dvo, w_qkv)
    dx_in = lax.ppermute(dxo, "sp", [(1, 0)])
    gqkv, small_c = input_weight(x, x_o, dq, dk, dv, dko, dvo)
    t_qkv = sum_scatter(gqkv, size, (0, 1, 2, 3))
    dx = input_back(dh1, dq, dk, dv, w_qkv)
    grad_memory = (dm + dm_in.astype(F32)).astype(BF16)
    derivative = (dx + dx_in.astype(F32)).astype(BF16)

    small = jnp.concatenate([small_a[:6], small_b[:4], gcvb, small_c[:2], gib.reshape(-1, width)], axis=0)
    small = lax.psum(small, ("dp", "sp"))
    me = lax.axis_index("dp")
    share = width // size
    lines = lax.dynamic_slice_in_dim(small, me * share, share, 1)
    (t_gthree, t_sthree, t_fobias, t_gtwo, t_stwo, t_cobias, t_cqbias, t_gone, t_sone, t_obias,
     t_cvbias, t_qbias, t_vbias) = (lines[i] for i in range(13))
    wide = gib.shape[1] // size
    t_fibias = lax.dynamic_slice_in_dim(small[13:].reshape(-1), me * wide, wide, 0)
    return (
        output[None],
        derivative[None],
        grad_memory[None],
        t_qkv,
        t_qbias,
        t_vbias,
        t_out,
        t_obias,
        t_gone,
        t_sone,
        t_cquery,
        t_cqbias,
        t_cmem,
        t_cvbias,
        t_cout,
        t_cobias,
        t_gtwo,
        t_stwo,
        t_fin,
        t_fibias,
        t_fout,
        t_fobias,
        t_gthree,
        t_sthree,
    )


def solution(mesh):
    split = P("dp", "sp", None)
    in_specs = (split, split, P("dp", "sp"), P("dp", "sp"), split) + (P(),) * 21
    matrix, vector = P("dp", None), P("dp")
    out_specs = (
        split, split, split,
        matrix, vector, vector,
        matrix, vector, vector, vector,
        matrix, vector,
        matrix, vector,
        matrix, vector, vector, vector,
        matrix, vector,
        matrix, vector, vector, vector,
    )
    return jax.shard_map(
        functools.partial(per_device, mesh.shape["dp"]),
        mesh=mesh, in_specs=in_specs, out_specs=out_specs, check_vma=False,
    )
```

```python
import functools

import jax
import jax.numpy as jnp
from jax import lax
from jax.experimental import pallas as pl
from jax.experimental.pallas import tpu as pltpu
from jax.sharding import PartitionSpec as P

HD = 64
PAIR = 2 * HD
EPS = 1e-05
FAR = 1.0e9
VMEM = 60 * 1024 * 1024
F32 = jnp.float32
BF16 = jnp.bfloat16


def nn(a, b):
    return lax.dot_general(a, b, (((1,), (0,)), ((), ())), preferred_element_type=F32)


def nt(a, b):
    return lax.dot_general(a, b, (((1,), (1,)), ((), ())), preferred_element_type=F32)


def tn(a, b):
    return lax.dot_general(a, b, (((0,), (0,)), ((), ())), preferred_element_type=F32)


def params(collective=None):
    if collective is None:
        return pltpu.CompilerParams(vmem_limit_bytes=VMEM)
    return pltpu.CompilerParams(
        vmem_limit_bytes=VMEM, collective_id=collective, has_side_effects=True
    )


def cost(flops, moved):
    return pl.CostEstimate(flops=int(flops), bytes_accessed=int(moved), transcendentals=0)


def normed(h):
    centred = h - jnp.mean(h, axis=-1, keepdims=True)
    rstd = lax.rsqrt(jnp.mean(centred * centred, axis=-1, keepdims=True) + EPS)
    return centred * rstd, rstd


def norm_back(grad, n, rstd, gain):
    scaled = grad * gain
    centre = jnp.mean(scaled, axis=-1, keepdims=True)
    along = jnp.mean(scaled * n, axis=-1, keepdims=True)
    return rstd * (scaled - centre - n * along)


def total(a):
    return jnp.sum(a.astype(F32), axis=0, keepdims=True)


def place():
    me = lax.axis_index("dp")
    return me, me % 2, (me // 2) % 2, me // 4


def partner(hop):
    me, c, x, z = place()
    if hop == "core":
        return {"dp": me + 1 - 2 * c}
    if hop == "x":
        return {"dp": me + 2 - 4 * x}
    if hop == "z1":
        return {"dp": me + 4 - 8 * (z % 2)}
    if hop == "z3":
        return {"dp": me + 4 * (3 - 2 * z)}
    return {"sp": 1 - lax.axis_index("sp")}


def beside(z, mask):
    if mask == 0:
        return z
    if mask == 1:
        return z + 1 - 2 * (z % 2)
    if mask == 2:
        return (z + 2) % 4
    return 3 - z


def greet(hops):
    barrier = pltpu.get_barrier_semaphore()
    for hop in hops:
        pl.semaphore_signal(barrier, inc=1, device_id=partner(hop), device_id_type=pl.DeviceIdType.MESH)
    pl.semaphore_wait(barrier, len(hops))


def remote(src, dst, send, recv, hop):
    return pltpu.make_async_remote_copy(
        src_ref=src, dst_ref=dst, send_sem=send, recv_sem=recv,
        device_id=partner(hop), device_id_type=pl.DeviceIdType.MESH,
    )


def first_z(hop, keep):
    kept = (0, 3) if hop == "z1" else (0, 1)
    return kept if keep else tuple(m ^ (1 if hop == "z1" else 3) for m in kept)


class Part:
    def __init__(self, hop, shape, cols=None):
        self.hop = hop
        self.cols = cols or (0, shape[-1])
        shape = tuple(shape[:-1]) + (self.cols[1],)
        self.shape = shape
        if hop in ("core", "x"):
            self.after = shape[:-3] + shape[-2:]
        elif hop == "y":
            self.after = shape
        else:
            self.after = ((2,) if shape[0] == 4 else ()) + shape[1:]
        self.dtype = F32 if hop == "y" else BF16

    def copies(self, src, kept, came, send, recv, local):
        _, c, x, z = place()
        at = pl.ds(*self.cols)
        rest = (slice(None),) * (len(self.shape) - 2)
        if self.hop in ("core", "x"):
            mine = c if self.hop == "core" else x
            lead = (slice(None),) * (len(self.shape) - 3)
            tail = (slice(None), at)
            stay, away = [(lead + (mine,), ())], [(lead + (1 - mine,), ())]
        elif self.hop == "y":
            tail = rest + (slice(None), at)
            stay = away = [((), ())]
        elif self.shape[0] == 4:
            tail = rest + (at,)
            stay = [((beside(z, m),), (i,)) for i, m in enumerate(first_z(self.hop, True))]
            away = [((beside(z, m),), (i,)) for i, m in enumerate(first_z(self.hop, False))]
        else:
            tail = rest + (at,)
            stay, away = [((0,), ())], [((1,), ())]
        return [
            remote(src.at[frm + tail], came.at[to] if to else came, send.at[i], recv.at[i], self.hop)
            for i, (frm, to) in enumerate(away)
        ] + [
            pltpu.make_async_copy(src.at[frm + tail], kept.at[to] if to else kept, local.at[i])
            for i, (frm, to) in enumerate(stay)
        ]


class Window:
    def __init__(self, parts, sources, start, stop, keep="out", joined=None):
        self.parts, self.sources, self.start, self.stop = parts, sources, start, stop
        self.keep, self.joined = keep, joined


def carrying(body, own, windows, arrays, grid, also):
    ins, outs, held = own

    def kernel(*refs):
        refs = list(refs)

        def take(n):
            got = refs[:n]
            del refs[:n]
            return got

        my_in, arr = take(ins), take(arrays)
        my_out = take(outs)
        given = []
        for w in windows:
            if w.joined:
                whole_refs = take(len(w.joined[0]))
                given.append(
                    [whole_refs[i].at[:, pl.ds(c, q.after[1])] for q, (i, c) in zip(w.parts, w.joined[1])]
                )
            else:
                given.append(take(len(w.parts)) if w.keep == "out" else None)
        my_held = take(held)
        made, kept, came = [], [], []
        for w, g in zip(windows, given):
            made.append(take(len(w.parts)) if g is None else g)
            kept.append([take(1)[0] if q.dtype == F32 else m for q, m in zip(w.parts, made[-1])])
            came.append(take(len(w.parts)))
        mine = my_in + my_out + my_held
        step = pl.program_id(0)
        hops = sorted({q.hop for w in windows for q in w.parts} | set(also))
        if hops:
            pl.when(step == 0)(lambda: greet(hops))
        copies = []
        if windows:
            send, recv, local = refs
        base = 0
        for w, k, c in zip(windows, kept, came):
            now = []
            for i, q in enumerate(w.parts):
                kind = w.sources[i]
                if kind[0] == "in":
                    src = arr[kind[1]]
                elif kind[0] == "ref":
                    src = mine[kind[1]]
                    src = src.at[kind[2]] if len(kind) > 2 else src
                else:
                    src = made[kind[1]][kind[2]]
                now += q.copies(src, k[i], c[i], send.at[base], recv.at[base], local.at[base])
                base += 1
            copies.append(now)

        def phase(number):
            for n, w in enumerate(windows):
                if w.stop == number:
                    for copy in copies[n]:
                        copy.wait()
                    for m, k, c, q in zip(made[n], kept[n], came[n], w.parts):
                        if q.dtype == F32:
                            m[...] = k[...].astype(F32) + c[...].astype(F32)
                        else:
                            m[...] += c[...]
            for n, w in enumerate(windows):
                if w.start == number:
                    for copy in copies[n]:
                        copy.start()

        used = sorted({w.start for w in windows} | {w.stop for w in windows})
        for number in used:
            if number < grid:
                pl.when(step == number)(functools.partial(phase, number))
        body(*mine)
        for number in used:
            if number >= grid:
                pl.when(step == grid - 1)(functools.partial(phase, number))

    return kernel


def run(
    body, name, grid, ins, in_specs, outs, out_specs, held=(), windows=(), arrays=(), collective=None,
    flops=0, moved=0, also=(),
):
    in_specs, outs, out_specs, held = list(in_specs), list(outs), list(out_specs), list(held)
    kernel = carrying(body, (len(ins), len(outs), len(held)), windows, len(arrays), grid, also)
    in_specs += [pl.BlockSpec(memory_space=pl.ANY)] * len(arrays)
    count = 0
    for w in windows:
        if w.joined:
            outs += [jax.ShapeDtypeStruct(shape, F32) for shape in w.joined[0]]
            out_specs += [whole(shape) for shape in w.joined[0]]
        elif w.keep == "out":
            outs += [jax.ShapeDtypeStruct(q.after, q.dtype) for q in w.parts]
            out_specs += [whole(q.after) for q in w.parts]
        else:
            held += [pltpu.VMEM(q.after, q.dtype) for q in w.parts]
        held += [pltpu.VMEM(q.after, BF16) for q in w.parts if q.dtype == F32]
        held += [pltpu.VMEM(q.after, BF16) for q in w.parts]
        count += len(w.parts)
    if windows:
        held += [pltpu.SemaphoreType.DMA((count, 2))] * 3
    return pl.pallas_call(
        kernel,
        grid=(grid,),
        in_specs=in_specs,
        out_specs=out_specs,
        out_shape=outs,
        scratch_shapes=held,
        compiler_params=params(collective if windows or also else None),
        cost_estimate=cost(flops, moved),
        name=name,
    )(*ins, *arrays)


FEED_PATHS = (
    (0, (0, 1024), ("x", "z1", "z3", "y")),
    (0, (1024, 1024), ("x", "z3", "z1", "y")),
    (0, (2048, 512), ("z1", "z3", "x", "y")),
    (0, (2560, 512), ("z3", "z1", "x", "y")),
    (1, (0, 384), ("z1", "z3", "x", "y")),
    (1, (384, 384), ("z3", "z1", "x", "y")),
)
MIDDLE_PATHS = (
    (0, (0, 768), ("x", "z1", "z3", "y")),
    (1, (0, 768), ("x", "z3", "z1", "y")),
    (2, (0, 768), ("z1", "z3", "x", "y")),
    (3, (0, 768), ("z3", "z1", "x", "y")),
    (4, (0, 384), ("z1", "z3", "x", "y")),
    (4, (384, 384), ("z3", "z1", "x", "y")),
)
LAST_PATHS = (
    (0, (0, 768), ("x", "z1", "z3", "y")),
    (1, (0, 768), ("z1", "z3", "x", "y")),
    (2, (0, 768), ("z3", "z1", "x", "y")),
    (3, (0, 128), ("x", "z1", "z3", "y")),
)


def hop(paths, number, shapes, source, start, stop, keep="out", joined=None):
    if number == 0:
        parts = [Part(hops[0], shapes[i], cols) for i, cols, hops in paths]
        sources = [source(i) for i, _, _ in paths]
    else:
        parts = [Part(hops[number], shape) for (_, _, hops), shape in zip(paths, shapes)]
        sources = [source(i) for i in range(len(parts))]
    return Window(parts, sources, start, stop, keep, joined)


def afters(window):
    return [q.after for q in window.parts]


def given(i):
    return ("in", i)


def code_of(docs_ref):
    row = lax.broadcasted_iota(jnp.int32, (128, docs_ref.shape[1]), 0)
    return jnp.transpose(jnp.where(docs_ref[...] == row, 1.0, 0.0)).astype(BF16)


def project_kernel(
    x_ref, m_ref, td_ref, md_ref, wx_ref, wm_ref, b_ref,
    qkv_ref, mkv_ref, kvo_ref, xo_ref, mem_ref, to_ref, mo_ref, tt_ref, mt_ref,
    came_ref, tdo_ref, mdo_ref, send_ref, recv_ref,
):
    step = pl.program_id(0)
    sp = lax.axis_index("sp")
    peer = "sp"
    rows_out = remote(x_ref, came_ref, send_ref.at[0], recv_ref.at[0], peer)
    docs = [
        remote(td_ref, tdo_ref, send_ref.at[1], recv_ref.at[1], peer),
        remote(md_ref, mdo_ref, send_ref.at[2], recv_ref.at[2], peer),
    ]

    @pl.when(step == 0)
    def _():
        greet([peer])
        for copy in docs:
            copy.start()
        pl.when(sp == 0)(rows_out.start)
        to_ref[...] = code_of(td_ref)
        mo_ref[...] = code_of(md_ref)
        mem_ref[...] = m_ref[...]

    @pl.when(step < 3)
    def _():
        bias = jnp.where(step == 0, b_ref[0:1], 0.0) + jnp.where(step == 2, b_ref[1:2], 0.0)
        qkv_ref[...] = (nn(x_ref[...], wx_ref[...]) + bias).astype(BF16)

    @pl.when(jnp.logical_and(step >= 3, step < 5))
    def _():
        bias = jnp.where(step == 4, b_ref[2:3], 0.0)
        mkv_ref[...] = (nn(m_ref[...], wm_ref[...]) + bias).astype(BF16)

    @pl.when(step == 4)
    def _():
        for copy in docs:
            copy.wait()
        tt_ref[...] = code_of(tdo_ref)
        mt_ref[...] = code_of(mdo_ref)
        pl.when(sp == 0)(rows_out.wait_send)

        @pl.when(sp == 1)
        def _():
            rows_out.wait_recv()
            xo_ref[...] = came_ref[...]

    @pl.when(jnp.logical_and(step >= 5, sp == 1))
    def _():
        bias = jnp.where(step == 6, b_ref[1:2], 0.0)
        kvo_ref[...] = (nn(came_ref[...], wx_ref[...]) + bias).astype(BF16)

    @pl.when(jnp.logical_and(step >= 5, sp == 0))
    def _():
        kvo_ref[...] = jnp.zeros(kvo_ref.shape, BF16)
        xo_ref[...] = jnp.zeros(xo_ref.shape, BF16)


def project_first(x, mem, td, md, wx, wm, biases):
    rows, width = x.shape
    code = jax.ShapeDtypeStruct((rows, 128), BF16)

    def flat(cols):
        return jax.ShapeDtypeStruct((rows, cols), BF16)

    return pl.pallas_call(
        project_kernel,
        grid=(7,),
        in_specs=[
            whole((rows, width)), whole((rows, width)), whole((1, rows)), whole((1, rows)),
            pl.BlockSpec((width, width), lambda s: (0, jnp.where(s < 3, s, jnp.maximum(s - 4, 1)))),
            pl.BlockSpec((width, width), lambda s: (0, jnp.clip(s - 3, 0, 1))),
            whole(biases.shape),
        ],
        out_specs=[
            pl.BlockSpec((rows, width), lambda s: (0, jnp.minimum(s, 2))),
            pl.BlockSpec((rows, width), lambda s: (0, jnp.clip(s - 3, 0, 1))),
            pl.BlockSpec((rows, width), lambda s: (0, jnp.clip(s - 5, 0, 1))),
            whole((rows, width)), whole((rows, width)),
            whole((rows, 128)), whole((rows, 128)), whole((rows, 128)), whole((rows, 128)),
        ],
        out_shape=[flat(3 * width), flat(2 * width), flat(2 * width), flat(width), flat(width)] + [code] * 4,
        scratch_shapes=[
            pltpu.VMEM((rows, width), BF16),
            pltpu.VMEM((1, rows), jnp.int32),
            pltpu.VMEM((1, rows), jnp.int32),
            pltpu.SemaphoreType.DMA((3,)),
            pltpu.SemaphoreType.DMA((3,)),
        ],
        compiler_params=params(1),
        cost_estimate=cost(14 * rows * width * width, 20 * width * width),
        name="project_first",
    )(x, mem, td, md, wx, wm, biases)


def project_memory_kernel(x_ref, w_ref, b_ref, o_ref):
    bias = jnp.where(pl.program_id(0) == 1, b_ref[2:3], 0.0)
    o_ref[...] = (nn(x_ref[...], w_ref[...]) + bias).astype(BF16)


def project_memory(x, w, biases):
    rows, width = x.shape
    return pl.pallas_call(
        project_memory_kernel,
        grid=(2,),
        in_specs=[
            whole((rows, width)),
            pl.BlockSpec((width, width), lambda j: (0, j)),
            whole(biases.shape),
        ],
        out_specs=pl.BlockSpec((rows, width), lambda j: (0, j)),
        out_shape=jax.ShapeDtypeStruct((rows, 2 * width), BF16),
        compiler_params=params(),
        cost_estimate=cost(4 * rows * width * width, 4 * width * (width + rows)),
        name="project_memory",
    )(x, w, biases)


def head_masks(dtype):
    lane = lax.broadcasted_iota(jnp.int32, (1, PAIR), 1)
    low = jnp.where(lane < HD, 1.0, 0.0)
    return low.astype(dtype), (1.0 - low).astype(dtype)


def query_code(code):
    lane = lax.broadcasted_iota(jnp.int32, code.shape, 1)
    return jnp.where(lane < 4, (code.astype(F32) - 1.0) * FAR, 0.0).astype(BF16)


def softmax_pieces(scores, values):
    peak = functools.reduce(jnp.maximum, [jnp.max(s, axis=-1, keepdims=True) for s in scores])
    expd = [jnp.exp(s - peak) for s in scores]
    norm = sum(jnp.sum(e, axis=-1, keepdims=True) for e in expd)
    out = sum(nn(e.astype(BF16), v) for e, v in zip(expd, values))
    return out / norm, peak + jnp.log(norm)


def self_pieces(block, size, both, own, other):
    pieces = []
    if both:
        pieces.append((other, False))
    if block:
        pieces.append((own[: block * size], False))
    pieces.append((own[block * size : (block + 1) * size], True))
    return pieces


def store_lse(lse_ref, block, size, low, high):
    lane = lax.broadcasted_iota(jnp.int32, (size, PAIR), 1)
    both = jnp.where(lane == 0, low, high)
    lse_ref[:, block * size : (block + 1) * size] = jnp.transpose(both)[:8]


def self_forward_kernel(size, q_ref, k_ref, v_ref, ko_ref, vo_ref, own_ref, oth_ref, o_ref, lse_ref):
    second = lax.axis_index("sp") == 1
    rows = q_ref.shape[0]
    masks = head_masks(BF16)
    outs = head_masks(F32)

    def run(both):
        qcode = query_code(own_ref[...])
        own = jnp.concatenate([k_ref[...], own_ref[...]], axis=1)
        oth = jnp.concatenate([ko_ref[...], oth_ref[...]], axis=1) if both else None
        vown = v_ref[...]
        voth = vo_ref[...] if both else None
        for block in range(rows // size):
            at = slice(block * size, (block + 1) * size)
            lses, result = [], 0.0
            for mask, keep in zip(masks, outs):
                q = jnp.concatenate([q_ref[at] * (mask * BF16(HD**-0.5)), qcode[at]], axis=1)
                scores = []
                for keys, diagonal in self_pieces(block, size, both, own, oth):
                    s = nt(q, keys)
                    if diagonal:
                        row = lax.broadcasted_iota(jnp.int32, s.shape, 0)
                        col = lax.broadcasted_iota(jnp.int32, s.shape, 1)
                        s = jnp.where(row >= col, s, -FAR)
                    scores.append(s)
                values = [v for v, _ in self_pieces(block, size, both, vown, voth)]
                out, lse = softmax_pieces(scores, values)
                result = result + out * keep
                lses.append(lse)
            o_ref[at] = result.astype(BF16)
            store_lse(lse_ref, block, size, *lses)

    pl.when(second)(lambda: run(True))
    pl.when(jnp.logical_not(second))(lambda: run(False))


def pair_spec(rows, offset):
    return pl.BlockSpec((rows, PAIR), lambda p: (0, p + offset))


def whole(shape):
    return pl.BlockSpec(shape, lambda *_: (0,) * len(shape))


def self_forward(qkv, kvo, own, oth):
    rows = qkv.shape[0]
    width = qkv.shape[1] // 3
    pairs = width // PAIR
    return pl.pallas_call(
        functools.partial(self_forward_kernel, 256),
        grid=(pairs,),
        in_specs=[
            pair_spec(rows, 0),
            pair_spec(rows, pairs),
            pair_spec(rows, 2 * pairs),
            pair_spec(rows, 0),
            pair_spec(rows, pairs),
            whole((rows, 128)),
            whole((rows, 128)),
        ],
        out_specs=[pair_spec(rows, 0), pl.BlockSpec((8, rows), lambda p: (p, 0))],
        out_shape=[
            jax.ShapeDtypeStruct((rows, width), BF16),
            jax.ShapeDtypeStruct((8 * pairs, rows), F32),
        ],
        compiler_params=params(),
        cost_estimate=cost(16 * rows * rows * width, 16 * rows * width),
        name="self_forward",
    )(qkv, qkv, qkv, kvo, kvo, own, oth)


def cross_forward_kernel(size, q_ref, k_ref, v_ref, ko_ref, vo_ref, t_ref, own_ref, oth_ref, o_ref, lse_ref):
    rows = q_ref.shape[0]
    masks = head_masks(BF16)
    outs = head_masks(F32)
    qcode = query_code(t_ref[...])
    keys = [
        jnp.concatenate([k_ref[...], own_ref[...]], axis=1),
        jnp.concatenate([ko_ref[...], oth_ref[...]], axis=1),
    ]
    values = [v_ref[...], vo_ref[...]]
    for block in range(rows // size):
        at = slice(block * size, (block + 1) * size)
        lses, result = [], 0.0
        for mask, keep in zip(masks, outs):
            q = jnp.concatenate([q_ref[at] * (mask * BF16(HD**-0.5)), qcode[at]], axis=1)
            out, lse = softmax_pieces([nt(q, k) for k in keys], values)
            result = result + out * keep
            lses.append(lse)
        o_ref[at] = result.astype(BF16)
        store_lse(lse_ref, block, size, *lses)


def cross_forward(cq, kv, kvo, t, own, oth):
    rows, width = cq.shape
    pairs = width // PAIR
    return pl.pallas_call(
        functools.partial(cross_forward_kernel, 256),
        grid=(pairs,),
        in_specs=[
            pair_spec(rows, 0),
            pair_spec(rows, 0),
            pair_spec(rows, pairs),
            pair_spec(rows, 0),
            pair_spec(rows, pairs),
            whole((rows, 128)),
            whole((rows, 128)),
            whole((rows, 128)),
        ],
        out_specs=[pair_spec(rows, 0), pl.BlockSpec((8, rows), lambda p: (p, 0))],
        out_shape=[
            jax.ShapeDtypeStruct((rows, width), BF16),
            jax.ShapeDtypeStruct((8 * pairs, rows), F32),
        ],
        compiler_params=params(),
        cost_estimate=cost(24 * rows * rows * width, 16 * rows * width),
        name="cross_forward",
    )(cq, kv, kv, kvo, kvo, t, own, oth)


def delta_rows(g, o):
    prod = g.astype(F32) * o.astype(F32)
    upper = prod.astype(BF16)
    lower = (prod - upper.astype(F32)).astype(BF16)
    row = lax.broadcasted_iota(jnp.int32, (8, PAIR), 0)
    lane = lax.broadcasted_iota(jnp.int32, (8, PAIR), 1)
    pick = jnp.where(row == lane // HD, 1.0, 0.0).astype(BF16)
    return nt(pick, upper) + nt(pick, lower)


def back_piece(keys, values, q, g, lse, delta, causal):
    s = nt(keys, q)
    if causal:
        row = lax.broadcasted_iota(jnp.int32, s.shape, 0)
        col = lax.broadcasted_iota(jnp.int32, s.shape, 1)
        s = jnp.where(row <= col, s, -FAR)
    p = jnp.exp(s - lse)
    ds = p * (nt(values, g) - delta)
    return p.astype(BF16), ds.astype(BF16)


def cross_backward_kernel(
    size, q_ref, k_ref, v_ref, ko_ref, vo_ref, g_ref, o_ref, lse_ref, t_ref, own_ref, oth_ref,
    m_ref, mo_ref, wk_ref, wv_ref,
    dq_ref, dm_ref, dmo_ref, gk_ref, gv_ref, gb_ref, dm_acc, dmo_acc,
):
    step = pl.program_id(0)
    rows = q_ref.shape[0]
    masks = head_masks(BF16)
    scale = BF16(HD**-0.5)
    qcode = query_code(t_ref[...])
    delta = delta_rows(g_ref[...], o_ref[...])
    lse = lse_ref[...]
    halves = [(k_ref, v_ref, own_ref, m_ref, dm_acc), (ko_ref, vo_ref, oth_ref, mo_ref, dmo_acc)]
    dq = [0.0] * (rows // size)
    gk = gv = gb = 0.0
    for kr, vr, code, mem, acc in halves:
        keys = jnp.concatenate([kr[...], code[...]], axis=1)
        values = vr[...]
        dk = dv = 0.0
        for block in range(rows // size):
            at = slice(block * size, (block + 1) * size)
            for head, mask in enumerate(masks):
                qm = q_ref[at] * (mask * scale)
                gm = g_ref[at] * mask
                q = jnp.concatenate([qm, qcode[at]], axis=1)
                p, ds = back_piece(
                    keys, values, q, gm, lse[head : head + 1, at], delta[head : head + 1, at], False
                )
                dk = dk + nn(ds, qm)
                dv = dv + nn(p, gm)
                dq[block] = dq[block] + tn(ds, kr[...] * (mask * scale))
        both = jnp.concatenate([dk.astype(BF16), dv.astype(BF16)], axis=1)
        grad = tn(mem[...], both)
        gk, gv = gk + grad[:, :PAIR], gv + grad[:, PAIR:]
        gb = gb + total(both[:, PAIR:])
        dm = nt(both, jnp.concatenate([wk_ref[...], wv_ref[...]], axis=1))

        @pl.when(step == 0)
        def _():
            acc[...] = dm

        @pl.when(step > 0)
        def _():
            acc[...] += dm
    for block in range(rows // size):
        dq_ref[block * size : (block + 1) * size] = dq[block].astype(BF16)
    gk_ref[...] = gk.astype(BF16)
    gv_ref[...] = gv.astype(BF16)
    gb_ref[...] = gb

    @pl.when(step == pl.num_programs(0) - 1)
    def _():
        dm_ref[...] = dm_acc[...]
        dmo_ref[...] = dmo_acc[...].astype(BF16)


def cross_backward(cq, kv, kvo, g, o, lse, t, own, oth, m, mo, w, windows, arrays):
    rows, width = cq.shape
    pairs = width // PAIR
    flat = jax.ShapeDtypeStruct((rows, width), BF16)
    square = jax.ShapeDtypeStruct((width, width), BF16)
    return run(
        functools.partial(cross_backward_kernel, 256), "cross_backward", pairs,
        (cq, kv, kv, kvo, kvo, g, o, lse, t, own, oth, m, mo, w, w),
        [
            pair_spec(rows, 0),
            pair_spec(rows, 0),
            pair_spec(rows, pairs),
            pair_spec(rows, 0),
            pair_spec(rows, pairs),
            pair_spec(rows, 0),
            pair_spec(rows, 0),
            pl.BlockSpec((8, rows), lambda p: (p, 0)),
            whole((rows, 128)),
            whole((rows, 128)),
            whole((rows, 128)),
            whole((rows, width)),
            whole((rows, width)),
            pair_spec(width, 0),
            pair_spec(width, pairs),
        ],
        [flat, jax.ShapeDtypeStruct((rows, width), F32), flat, square, square, jax.ShapeDtypeStruct((1, width), F32)],
        [pair_spec(rows, 0)] + [whole((rows, width))] * 2 + [pair_spec(width, 0)] * 2 + [pair_spec(1, 0)],
        [pltpu.VMEM((rows, width), F32)] * 2,
        windows, arrays, 3,
        64 * rows * rows * width + 16 * rows * width * width, 24 * rows * width,
    )


def self_backward_kernel(
    size, q_ref, k_ref, v_ref, ko_ref, vo_ref, g_ref, o_ref, lse_ref, own_ref, oth_ref,
    dq_ref, dk_ref, dv_ref, dko_ref, dvo_ref,
):
    second = lax.axis_index("sp") == 1
    rows = q_ref.shape[0]
    masks = head_masks(BF16)
    scale = BF16(HD**-0.5)

    def run(both):
        qcode = query_code(own_ref[...])
        delta = delta_rows(g_ref[...], o_ref[...])
        lse = lse_ref[...]
        count = rows // size
        dk, dv = [0.0] * count, [0.0] * count
        dko = dvo = 0.0
        for block in range(count):
            at = slice(block * size, (block + 1) * size)
            dq = 0.0
            for head, mask in enumerate(masks):
                qm = q_ref[at] * (mask * scale)
                gm = g_ref[at] * mask
                q = jnp.concatenate([qm, qcode[at]], axis=1)
                rest = (q, gm, lse[head : head + 1, at], delta[head : head + 1, at])
                for part in range(block + 1):
                    of = slice(part * size, (part + 1) * size)
                    keys = jnp.concatenate([k_ref[of], own_ref[of]], axis=1)
                    p, ds = back_piece(keys, v_ref[of], *rest, part == block)
                    dk[part] = dk[part] + nn(ds, qm)
                    dv[part] = dv[part] + nn(p, gm)
                    dq = dq + tn(ds, k_ref[of] * (mask * scale))
                if both:
                    keys = jnp.concatenate([ko_ref[...], oth_ref[...]], axis=1)
                    p, ds = back_piece(keys, vo_ref[...], *rest, False)
                    dko = dko + nn(ds, qm)
                    dvo = dvo + nn(p, gm)
                    dq = dq + tn(ds, ko_ref[...] * (mask * scale))
            dq_ref[at] = dq.astype(BF16)
        for part in range(count):
            of = slice(part * size, (part + 1) * size)
            dk_ref[of] = dk[part].astype(BF16)
            dv_ref[of] = dv[part].astype(BF16)
        if both:
            dko_ref[...] = dko.astype(BF16)
            dvo_ref[...] = dvo.astype(BF16)
        else:
            dko_ref[...] = jnp.zeros(dko_ref.shape, BF16)
            dvo_ref[...] = jnp.zeros(dvo_ref.shape, BF16)

    pl.when(second)(lambda: run(True))
    pl.when(jnp.logical_not(second))(lambda: run(False))


def self_backward(qkv, kvo, g, o, lse, own, oth, windows, arrays):
    rows = qkv.shape[0]
    width = qkv.shape[1] // 3
    pairs = width // PAIR
    flat = jax.ShapeDtypeStruct((rows, width), BF16)
    return run(
        functools.partial(self_backward_kernel, 256), "self_backward", pairs,
        (qkv, qkv, qkv, kvo, kvo, g, o, lse, own, oth),
        [
            pair_spec(rows, 0),
            pair_spec(rows, pairs),
            pair_spec(rows, 2 * pairs),
            pair_spec(rows, 0),
            pair_spec(rows, pairs),
            pair_spec(rows, 0),
            pair_spec(rows, 0),
            pl.BlockSpec((8, rows), lambda p: (p, 0)),
            whole((rows, 128)),
            whole((rows, 128)),
        ],
        [flat] * 5,
        [pair_spec(rows, 0)] * 5,
        (), windows, arrays, 5,
        48 * rows * rows * width, 24 * rows * width,
    )


def first_norm_kernel(x_ref, ctx_ref, wo_ref, wq_ref, b_ref, h_ref, cq_ref):
    h = x_ref[...].astype(F32) + nn(ctx_ref[...], wo_ref[...]) + b_ref[3:4]
    h_ref[...] = h
    n, _ = normed(h)
    a = (n * b_ref[4:5] + b_ref[5:6]).astype(BF16)
    cq_ref[...] = (nn(a, wq_ref[...]) + b_ref[6:7]).astype(BF16)


def first_norm(x, ctx, wo, wq, biases):
    rows, width = x.shape
    return pl.pallas_call(
        first_norm_kernel,
        out_shape=[
            jax.ShapeDtypeStruct((rows, width), F32),
            jax.ShapeDtypeStruct((rows, width), BF16),
        ],
        compiler_params=params(),
        cost_estimate=cost(4 * rows * width * width, 4 * width * width + 10 * rows * width),
        name="first_norm",
    )(x, ctx, wo, wq, biases)


def feed_kernel(
    count, comm, h1_ref, cc_ref, ct_ref, wco_ref, b_ref, wi_ref, wo_ref,
    out_ref, dh2_ref, dcc_ref, gco_ref, gwi_ref, gwo_ref, small_ref, gib_ref,
    hid_ref, slope_ref, n2_ref, r2_ref, a2b_ref, acc_ref, df_ref, *refs,
):
    step = pl.program_id(0)
    width = acc_ref.shape[1]

    if comm:
        mi_ref, mo_ref, ci_ref, co_ref, send_ref, recv_ref = refs
        _, c, _, _ = place()

        def chunk_copies(j):
            at = pl.ds(pl.multiple_of(j * width, width), width)
            return [
                remote(
                    mi_ref.at[:, 1 - c, :, at], ci_ref.at[:, :, at], send_ref.at[0, j], recv_ref.at[0, j], "core"
                ),
                remote(mo_ref.at[j, :, 1 - c], co_ref.at[j], send_ref.at[1, j], recv_ref.at[1, j], "core"),
            ]

    @pl.when(step == 0)
    def _():
        if comm:
            greet(["core"])
        n1, _ = normed(h1_ref[...])
        a1 = n1 * b_ref[4:5] + b_ref[5:6]
        h2 = a1 + nn(cc_ref[...], wco_ref[...]) + b_ref[7:8]
        n2, r2 = normed(h2)
        n2_ref[...] = n2
        r2_ref[...] = jnp.broadcast_to(r2, r2_ref.shape)
        a2 = n2 * b_ref[8:9] + b_ref[9:10]
        a2b_ref[...] = a2.astype(BF16)
        acc_ref[...] = a2 + b_ref[10:11]

    @pl.when(step < count)
    def _():
        u = nn(a2b_ref[...], wi_ref[...]) + b_ref[pl.ds(13 + step, 1)]
        cumul = 0.5 * (1.0 + lax.erf(u * 0.7071067811865476))
        density = jnp.exp(-0.5 * u * u) * 0.3989422804014327
        hid = (u * cumul).astype(BF16)
        hid_ref[step] = hid
        slope_ref[step] = cumul + u * density
        acc_ref[...] += nn(hid, wo_ref[...])

    @pl.when(step == count - 1)
    def _():
        n3, r3 = normed(acc_ref[...])
        gain = b_ref[11:12]
        out_ref[...] = (n3 * gain + b_ref[12:13]).astype(BF16)
        e = ct_ref[...].astype(F32)
        d3 = norm_back(e, n3, r3, gain)
        df = d3.astype(BF16)
        df_ref[...] = df
        acc_ref[...] = d3
        small_ref[0:1] = total(e * n3)
        small_ref[1:2] = total(e)
        small_ref[2:3] = total(df)

    @pl.when(jnp.logical_and(step >= count, step < 2 * count))
    def _():
        j = step - count
        df = df_ref[...]
        du = (nt(df, wo_ref[...]) * slope_ref[j]).astype(BF16)
        gib_ref[...] = total(du)
        acc_ref[...] += nt(du, wi_ref[...])
        go = tn(hid_ref[j], df).astype(BF16)
        gi = tn(a2b_ref[...], du).astype(BF16)
        if comm:
            at = pl.ds(pl.multiple_of(j * width, width), width)
            mo_ref[j] = go.reshape(mo_ref.shape[1:])
            mi_ref[:, :, :, at] = gi.reshape(mi_ref.shape[:3] + (width,))
            for copy in chunk_copies(j):
                copy.start()
        else:
            gwo_ref[...] = go
            gwi_ref[...] = gi

    @pl.when(step == 2 * count)
    def _():
        d2 = acc_ref[...]
        n2 = n2_ref[...]
        dh2 = norm_back(d2, n2, r2_ref[:, :1], b_ref[8:9])
        dh2_ref[...] = dh2
        dco = dh2.astype(BF16)
        dcc_ref[...] = nt(dco, wco_ref[...]).astype(BF16)
        gco_ref[...] = tn(cc_ref[...], dco).astype(BF16)
        small_ref[3:4] = total(d2 * n2)
        small_ref[4:5] = total(d2)
        small_ref[5:6] = total(dco)
        small_ref[6:8] = jnp.zeros((2, d2.shape[1]), F32)

    if comm:

        @pl.when(step > count)
        def _():
            j = step - count - 1
            at = pl.ds(pl.multiple_of(j * width, width), width)
            for copy in chunk_copies(j):
                copy.wait()
            gwi_ref[...] = mi_ref[:, c, :, at] + ci_ref[:, :, at]
            gwo_ref[0] = mo_ref[j, :, c] + co_ref[j]


def feed(size, comm, h1, cc, ct, wco, biases, wi, wo):
    rows, width = h1.shape
    wide = wi.shape[1]
    chunk = width
    count = wide // chunk

    def weight(s):
        return jnp.where(s < count, s, jnp.minimum(s - count, count - 1))

    def early(s):
        return jnp.clip(s - count, 0, count - 1)

    def late(s):
        return jnp.clip(s - count - 1, 0, count - 1)

    flat = whole((rows, width))
    square = whole((width, width))
    scratch = [
        pltpu.VMEM((count, rows, chunk), BF16),
        pltpu.VMEM((count, rows, chunk), F32),
        pltpu.VMEM((rows, width), F32),
        pltpu.VMEM((rows, 128), F32),
        pltpu.VMEM((rows, width), BF16),
        pltpu.VMEM((rows, width), F32),
        pltpu.VMEM((rows, width), BF16),
    ]
    if comm:
        narrow, broad = width // size, wide // size
        grad_specs = [
            pl.BlockSpec((size // 2, narrow, chunk), lambda s: (0, 0, late(s))),
            pl.BlockSpec((1, 2, broad, width), lambda s: (late(s), 0, 0, 0)),
        ]
        grad_shapes = [(size // 2, narrow, wide), (count, 2, broad, width)]
        scratch += [
            pltpu.VMEM((size // 2, 2, narrow, wide), BF16),
            pltpu.VMEM((count, 2, 2, broad, width), BF16),
            pltpu.VMEM((size // 2, narrow, wide), BF16),
            pltpu.VMEM((count, 2, broad, width), BF16),
            pltpu.SemaphoreType.DMA((2, count)),
            pltpu.SemaphoreType.DMA((2, count)),
        ]
    else:
        grad_specs = [
            pl.BlockSpec((width, chunk), lambda s: (0, early(s))),
            pl.BlockSpec((chunk, width), lambda s: (early(s), 0)),
        ]
        grad_shapes = [(width, wide), (wide, width)]
    return pl.pallas_call(
        functools.partial(feed_kernel, count, comm),
        grid=(2 * count + 1,),
        in_specs=[
            flat, flat, flat, square, whole(biases.shape),
            pl.BlockSpec((width, chunk), lambda s: (0, weight(s))),
            pl.BlockSpec((chunk, width), lambda s: (weight(s), 0)),
        ],
        out_specs=[flat, flat, flat, square]
        + grad_specs
        + [whole((8, width)), pl.BlockSpec((1, chunk), lambda s: (0, early(s)))],
        out_shape=[
            jax.ShapeDtypeStruct((rows, width), BF16),
            jax.ShapeDtypeStruct((rows, width), F32),
            jax.ShapeDtypeStruct((rows, width), BF16),
            jax.ShapeDtypeStruct((width, width), BF16),
        ]
        + [jax.ShapeDtypeStruct(a, BF16) for a in grad_shapes]
        + [
            jax.ShapeDtypeStruct((8, width), F32),
            jax.ShapeDtypeStruct((1, wide), F32),
        ],
        scratch_shapes=scratch,
        compiler_params=params(2 if comm else None),
        cost_estimate=cost(
            12 * rows * width * wide + 6 * rows * width * width, 12 * width * wide + 16 * rows * width
        ),
        name="feed",
    )(h1, cc, ct, wco, biases, wi, wo)


def first_back_kernel(
    dcq_ref, dh2_ref, h1_ref, ctx_ref, wcq_ref, wso_ref, b_ref,
    dh1_ref, dsc_ref, gcq_ref, gso_ref, small_ref,
):
    gain = b_ref[4:5]
    n1, r1 = normed(h1_ref[...])
    a1b = (n1 * gain + b_ref[5:6]).astype(BF16)
    dcq = dcq_ref[...]
    d1 = dh2_ref[...] + nt(dcq, wcq_ref[...])
    dh1 = norm_back(d1, n1, r1, gain)
    dh1_ref[...] = dh1
    dso = dh1.astype(BF16)
    dsc_ref[...] = nt(dso, wso_ref[...]).astype(BF16)
    gcq_ref[...] = tn(a1b, dcq).astype(BF16)
    gso_ref[...] = tn(ctx_ref[...], dso).astype(BF16)
    small_ref[0:1] = total(dcq)
    small_ref[1:2] = total(d1 * n1)
    small_ref[2:3] = total(d1)
    small_ref[3:4] = total(dso)
    small_ref[4:8] = jnp.zeros((4, dh1.shape[1]), F32)


def first_back(dcq, dh2, h1, ctx, wcq, wso, biases, windows, arrays):
    rows, width = dcq.shape
    flat, square = whole((rows, width)), whole((width, width))
    return run(
        first_back_kernel, "first_back", 1,
        (dcq, dh2, h1, ctx, wcq, wso, biases),
        [flat, flat, flat, flat, square, square, whole(biases.shape)],
        [
            jax.ShapeDtypeStruct((rows, width), F32),
            jax.ShapeDtypeStruct((rows, width), BF16),
            jax.ShapeDtypeStruct((width, width), BF16),
            jax.ShapeDtypeStruct((width, width), BF16),
            jax.ShapeDtypeStruct((8, width), F32),
        ],
        [flat, flat, square, square, whole((8, width))],
        (), windows, arrays, 4,
        8 * rows * width * width, 8 * width * width + 18 * rows * width,
    )


def input_back_kernel(
    x_ref, xo_ref, dq_ref, dk_ref, dv_ref, dko_ref, dvo_ref, w_ref, dh1_ref, sa_ref, sb_ref, sc_ref, sd_ref,
    dx_ref, g_ref, sm_ref, dxo_ref, came_ref, turn_ref, send_ref, recv_ref,
):
    step = pl.program_id(0)
    sp = lax.axis_index("sp")
    width = x_ref.shape[1]
    over = remote(dxo_ref, came_ref, send_ref.at[0], recv_ref.at[0], "y")

    @pl.when(step == 0)
    def _():
        @pl.when(sp == 1)
        def _():
            dxo = nt(dko_ref[...], w_ref[:, width : 2 * width]) + nt(dvo_ref[...], w_ref[:, 2 * width :])
            dxo_ref[...] = dxo.astype(BF16)
            over.start()

        g_ref[0] = tn(x_ref[...], dq_ref[...]).astype(BF16).reshape(g_ref.shape[1:])
        turn_ref[...] = jnp.zeros(turn_ref.shape, F32)
        turn_ref[0:8] = sa_ref[...]
        turn_ref[8:16] = sb_ref[...]
        turn_ref[16:17] = sc_ref[...]
        turn_ref[17:21] = sd_ref[...]
        turn_ref[21:22] = total(dq_ref[...])

    for n, (own, oth) in enumerate(((dk_ref, dko_ref), (dv_ref, dvo_ref)), start=1):

        @pl.when(jnp.logical_and(step == n, sp == 1))
        def _():
            grad = tn(x_ref[...], own[...]) + tn(xo_ref[...], oth[...])
            g_ref[n] = grad.astype(BF16).reshape(g_ref.shape[1:])

        @pl.when(jnp.logical_and(step == n, sp == 0))
        def _():
            g_ref[n] = tn(x_ref[...], own[...]).astype(BF16).reshape(g_ref.shape[1:])

    @pl.when(step == 2)
    def _():
        sums = total(dv_ref[...])
        turn_ref[22:23] = jnp.where(sp == 1, sums + total(dvo_ref[...]), sums)
        sm_ref[...] = jnp.transpose(turn_ref[...]).astype(BF16).reshape(sm_ref.shape)

    @pl.when(step == 3)
    def _():
        dx = (
            dh1_ref[...]
            + nt(dq_ref[...], w_ref[:, :width])
            + nt(dk_ref[...], w_ref[:, width : 2 * width])
            + nt(dv_ref[...], w_ref[:, 2 * width :])
        )

        @pl.when(sp == 0)
        def _():
            over.wait_recv()
            dx_ref[...] = (dx + came_ref[...].astype(F32)).astype(BF16)

        @pl.when(sp == 1)
        def _():
            over.wait_send()
            dx_ref[...] = dx.astype(BF16)


def input_back(block, x, xo, dq, dk, dv, dko, dvo, w, dh1, small, windows, arrays):
    rows, width = x.shape
    flat = whole((rows, width))
    ins = (x, xo, dq, dk, dv, dko, dvo, w, dh1) + tuple(small)
    made = [(3,) + block + (width,), block + (128,)]
    outs = [jax.ShapeDtypeStruct((rows, width), BF16)]
    specs = [flat]
    held = []
    if windows:
        held += [pltpu.VMEM(a, BF16) for a in made]
    else:
        outs += [jax.ShapeDtypeStruct(a, BF16) for a in made]
        specs += [whole(a) for a in made]
    held += [
        pltpu.VMEM((rows, width), BF16),
        pltpu.VMEM((rows, width), BF16),
        pltpu.VMEM((128, width), F32),
        pltpu.SemaphoreType.DMA((1,)),
        pltpu.SemaphoreType.DMA((1,)),
    ]
    return run(
        input_back_kernel, "input_back", 4, ins, [whole(a.shape) for a in ins], outs, specs, held,
        windows, arrays, 6, 20 * rows * width * width, 12 * width * width + 28 * rows * width, ("y",),
    )


def exchange_only(windows, arrays, collective, name):
    return run(lambda: None, name, 1, (), [], [], [], (), windows, arrays, collective, 0, 1 << 20)


def swap_sum(part, axis, pairs):
    came = lax.ppermute(part, axis, pairs)
    return part.astype(F32) + came.astype(F32)


def sum_scatter(grad, size, order):
    rows, cols = grad.shape
    bits = size.bit_length() - 1
    me = lax.axis_index("dp")
    now = grad.reshape((2,) * bits + (rows // size, cols))
    left = list(range(bits))[::-1]
    for bit in [b for b in order if b < bits] + [b for b in range(bits) if b not in order]:
        axis = left.index(bit)
        mine = (me >> bit) & 1
        keep = lax.dynamic_index_in_dim(now, mine, axis, keepdims=False)
        send = lax.dynamic_index_in_dim(now, 1 - mine, axis, keepdims=False)
        came = lax.ppermute(send, "dp", [(i, i ^ (1 << bit)) for i in range(size)])
        now = (keep.astype(F32) + came.astype(F32)).astype(BF16)
        left.pop(axis)
    return swap_sum(now, "sp", [(0, 1), (1, 0)])


def per_device(
    size,
    inputs,
    memory,
    target_docs,
    memory_docs,
    cotangent,
    w_qkv,
    b_q,
    b_v,
    w_so,
    b_so,
    g_one,
    s_one,
    w_cq,
    b_cq,
    w_ckv,
    b_cv,
    w_co,
    b_co,
    g_two,
    s_two,
    w_fi,
    b_fi,
    w_fo,
    b_fo,
    g_three,
    s_three,
):
    rows, width = inputs.shape[1:]
    comm = size == 16
    narrow = width // size
    swap = [(0, 1), (1, 0)]
    x, mem, ct = inputs[0], memory[0], cotangent[0]
    line = lax.broadcasted_iota(jnp.int32, (24, width), 0)
    vectors = (b_q, b_v, b_cv, b_so, g_one, s_one, b_cq, b_co, g_two, s_two, b_fo, g_three, s_three)
    vectors += tuple(b_fi[i : i + width] for i in range(0, b_fi.shape[0], width))
    biases = jnp.zeros((24, width), F32)
    for i, v in enumerate(vectors):
        biases = jnp.where(line == i, v.astype(F32)[None], biases)

    qkv, mkv, kvo, x_o, mem_s, t_own, m_own, t_oth, m_oth = project_first(
        x, mem, target_docs, memory_docs, w_qkv, w_ckv, biases
    )
    mem_o = lax.ppermute(mem_s, "sp", swap)
    ctx, lse = self_forward(qkv, kvo, t_own, t_oth)
    h1, cq = first_norm(x, ctx, w_so, w_cq, biases)
    mkvo = project_memory(mem_o, w_ckv, biases)
    cc, clse = cross_forward(cq, mkv, mkvo, t_own, m_own, m_oth)
    output, dh2, dcc, gco, gwi, gwo, small_a, gib = feed(
        size, comm, h1, cc, ct, w_co, biases, w_fi, w_fo
    )
    turned = gib.reshape(width, -1).T

    block = (4, 2, 2, narrow)
    after = block[:2] + block[3:]
    if comm:
        feeds = [gwi.reshape(after + (-1,)), gwo]
        w1 = hop(FEED_PATHS, 0, [a.shape for a in feeds], given, 0, 6)
        w2 = hop(FEED_PATHS, 1, afters(w1), given, 0, 1)
        w3 = hop(FEED_PATHS, 2, afters(w2), given, 0, 6)
        wide = b_fi.shape[0]
        w4 = hop(
            FEED_PATHS, 3, afters(w3), given, 0, 4,
            joined=(((narrow, wide), (wide // size, width)), ((0, 0), (0, 1024), (0, 2048), (0, 2560), (1, 0), (1, 384))),
        )
    dcq, dm, dmo, gck, gcv, gcvb, *feeds = cross_backward(
        cq, mkv, mkvo, dcc, cc, clse, t_own, m_own, m_oth, mem, mem_o, w_ckv,
        *(([w1], feeds) if comm else ((), ())),
    )
    dm_in = lax.ppermute(dmo, "sp", swap)
    dh1, dsc, gcq, gso, small_b, *feeds = first_back(
        dcq, dh2, h1, ctx, w_cq, w_so, biases, *(([w2], feeds) if comm else ((), ()))
    )
    middle = [gck, gcv, gco, gcq, gso]
    if comm:
        count = len(FEED_PATHS)
        middle = [a.reshape(block + (width,)) for a in middle]
        core = Window(
            [Part("core", a.shape) for a in middle], [("in", count + i) for i in range(len(middle))], 0, 6
        )
        carry = [w3, core], feeds + middle
    else:
        carry = (), ()
    dq, dk, dv, dko, dvo, *rest = self_backward(qkv, kvo, dsc, ctx, lse, t_own, t_oth, *carry)
    if comm:
        feeds, middle = rest[:count], rest[count:]
        m1 = hop(MIDDLE_PATHS, 0, afters(core), lambda i: ("in", count + i), 0, 4)
        c1 = Window([Part("core", block + (width,))], [("ref", 14, 0)], 1, 4)
        c2 = Window([Part("core", block + (width,))], [("ref", 14, 1)], 2, 4)
        c3 = Window(
            [Part("core", block + (width,)), Part("core", block + (128,))], [("ref", 14, 2), ("ref", 15)], 3, 4
        )
        carry = [w4, m1, c1, c2, c3], feeds + middle
    derivative, *rest = input_back(
        block if comm else (width,), x, x_o, dq, dk, dv, dko, dvo, w_qkv, dh1,
        (small_a, small_b, gcvb, turned), *carry,
    )
    if comm:
        t_fin, t_fout, *rest = rest
        middle, ends = rest[: len(MIDDLE_PATHS)], rest[len(MIDDLE_PATHS) :]
        count = len(middle)
        m2 = hop(MIDDLE_PATHS, 1, afters(m1), given, 0, 1, "held")
        l1 = hop(LAST_PATHS, 0, [a.shape for a in ends], lambda i: ("in", count + i), 0, 1, "held")
        m3 = hop(MIDDLE_PATHS, 2, afters(m2), lambda i: ("part", 0, i), 1, 2, "held")
        l2 = hop(LAST_PATHS, 1, afters(l1), lambda i: ("part", 1, i), 1, 2, "held")
        m4 = hop(
            MIDDLE_PATHS, 3, afters(m3), lambda i: ("part", 2, i), 2, 3,
            joined=(
                ((narrow, 2 * width),) + ((narrow, width),) * 3,
                ((0, 0), (0, width), (1, 0), (2, 0), (3, 0), (3, 384)),
            ),
        )
        l3 = hop(LAST_PATHS, 2, afters(l2), lambda i: ("part", 3, i), 2, 3, "held")
        l4 = hop(
            LAST_PATHS, 3, afters(l3), lambda i: ("part", 5, i), 3, 4,
            joined=(((narrow, 3 * width), (narrow, 128)), ((0, 0), (0, width), (0, 2 * width), (1, 0))),
        )
        t_cmem, t_cout, t_cquery, t_out, t_qkv, lines = exchange_only(
            [m2, l1, m3, l2, m4, l3, l4], middle + ends, 7, "exchange_last"
        )
    else:
        gqkv, columns = rest
        t_fin, t_fout, t_cout, t_cquery, t_out, t_cmem, t_qkv, lines = (
            sum_scatter(g, size, (0, 1, 2, 3))
            for g in (
                gwi, gwo, gco, gcq, gso, jnp.concatenate([gck, gcv], axis=1),
                jnp.concatenate([gqkv[0], gqkv[1], gqkv[2]], axis=1), columns,
            )
        )
    grad_memory = (dm + dm_in.astype(F32)).astype(BF16)
    lines = lines.T
    t_gthree, t_sthree, t_fobias, t_gtwo, t_stwo, t_cobias = (lines[i] for i in range(6))
    t_cqbias, t_gone, t_sone, t_obias = (lines[i] for i in range(8, 12))
    t_cvbias, t_qbias, t_vbias = lines[16], lines[21], lines[22]
    t_fibias = lines[17:21].T.reshape(-1)
    return (
        output[None],
        derivative[None],
        grad_memory[None],
        t_qkv,
        t_qbias,
        t_vbias,
        t_out,
        t_obias,
        t_gone,
        t_sone,
        t_cquery,
        t_cqbias,
        t_cmem,
        t_cvbias,
        t_cout,
        t_cobias,
        t_gtwo,
        t_stwo,
        t_fin,
        t_fibias,
        t_fout,
        t_fobias,
        t_gthree,
        t_sthree,
    )


def solution(mesh):
    split = P("dp", "sp", None)
    in_specs = (split, split, P("dp", "sp"), P("dp", "sp"), split) + (P(),) * 21
    matrix, vector = P("dp", None), P("dp")
    out_specs = (
        split, split, split,
        matrix, vector, vector,
        matrix, vector, vector, vector,
        matrix, vector,
        matrix, vector,
        matrix, vector, vector, vector,
        matrix, vector,
        matrix, vector, vector, vector,
    )
    return jax.shard_map(
        functools.partial(per_device, mesh.shape["dp"]),
        mesh=mesh, in_specs=in_specs, out_specs=out_specs, check_vma=False,
    )
```

```python
import functools

import jax
import jax.numpy as jnp
from jax import lax
from jax.experimental import pallas as pl
from jax.experimental.pallas import tpu as pltpu
from jax.sharding import PartitionSpec as P

HD = 64
PAIR = 2 * HD
EPS = 1e-05
FAR = 1.0e9
VMEM = 60 * 1024 * 1024
F32 = jnp.float32
BF16 = jnp.bfloat16


def nn(a, b):
    return lax.dot_general(a, b, (((1,), (0,)), ((), ())), preferred_element_type=F32)


def nt(a, b):
    return lax.dot_general(a, b, (((1,), (1,)), ((), ())), preferred_element_type=F32)


def tn(a, b):
    return lax.dot_general(a, b, (((0,), (0,)), ((), ())), preferred_element_type=F32)


def params(collective=None):
    if collective is None:
        return pltpu.CompilerParams(vmem_limit_bytes=VMEM)
    return pltpu.CompilerParams(
        vmem_limit_bytes=VMEM, collective_id=collective, has_side_effects=True
    )


def cost(flops, moved):
    return pl.CostEstimate(flops=int(flops), bytes_accessed=int(moved), transcendentals=0)


def normed(h):
    centred = h - jnp.mean(h, axis=-1, keepdims=True)
    rstd = lax.rsqrt(jnp.mean(centred * centred, axis=-1, keepdims=True) + EPS)
    return centred * rstd, rstd


def norm_back(grad, n, rstd, gain):
    scaled = grad * gain
    centre = jnp.mean(scaled, axis=-1, keepdims=True)
    along = jnp.mean(scaled * n, axis=-1, keepdims=True)
    return rstd * (scaled - centre - n * along)


def total(a):
    return jnp.sum(a.astype(F32), axis=0, keepdims=True)


def place():
    me = lax.axis_index("dp")
    return me, me % 2, (me // 2) % 2, me // 4


def partner(hop):
    me, c, x, z = place()
    if hop == "core":
        return {"dp": me + 1 - 2 * c}
    if hop == "x":
        return {"dp": me + 2 - 4 * x}
    if hop == "z1":
        return {"dp": me + 4 - 8 * (z % 2)}
    if hop == "z2":
        return {"dp": me + 8 - 16 * (z // 2)}
    return {"sp": 1 - lax.axis_index("sp")}


def greet(hops):
    hops = sorted({"y" if h[0] == "y" else h for h in hops})
    barrier = pltpu.get_barrier_semaphore()
    for hop in hops:
        pl.semaphore_signal(barrier, inc=1, device_id=partner(hop), device_id_type=pl.DeviceIdType.MESH)
    pl.semaphore_wait(barrier, len(hops))


def remote(src, dst, send, recv, hop):
    return pltpu.make_async_remote_copy(
        src_ref=src, dst_ref=dst, send_sem=send, recv_sem=recv,
        device_id=partner(hop), device_id_type=pl.DeviceIdType.MESH,
    )


class Part:
    def __init__(self, hop, shape, dims, cols=None):
        self.hop, self.dims = hop, dims
        self.cols = cols or (0, shape[-1])
        self.shape = shape = tuple(shape[:-1]) + (self.cols[1],)
        if hop in dims:
            at = dims.index(hop)
            self.after, self.left = shape[:at] + shape[at + 1 :], dims[:at] + dims[at + 1 :]
        else:
            wide = shape[-1]
            wide = wide // 2 if hop == "yr" else 2 * wide if hop == "yg" else wide
            self.after, self.left = shape[:-1] + (wide,), dims
        self.came = shape if hop == "yg" else self.after

    def copies(self, src, made, came, send, recv, local):
        _, c, x, z = place()
        sp = lax.axis_index("sp")
        first, wide = self.cols
        full = (slice(None),) * (len(self.shape) - 1)
        stay = away = full + (pl.ds(first, wide),)
        to = made
        if self.hop in self.dims:
            at = self.dims.index(self.hop)
            mine = {"core": c, "x": x, "z1": z % 2, "z2": z // 2}[self.hop]
            stay = stay[:at] + (mine,) + stay[at + 1 :]
            away = away[:at] + (1 - mine,) + away[at + 1 :]
        elif self.hop == "yr":
            half = wide // 2
            stay = full + (pl.ds(pl.multiple_of(first + sp * half, 128), half),)
            away = full + (pl.ds(pl.multiple_of(first + (1 - sp) * half, 128), half),)
        elif self.hop == "yg":
            to = made.at[full + (pl.ds(pl.multiple_of(sp * wide, 128), wide),)]
        return [
            remote(src.at[away], came, send, recv, self.hop),
            pltpu.make_async_copy(src.at[stay], to, local),
        ]

    def add(self, made, came):
        if self.hop == "yg":
            wide = self.shape[-1]
            at = pl.ds(pl.multiple_of((1 - lax.axis_index("sp")) * wide, 128), wide)
            made[(slice(None),) * (len(self.shape) - 1) + (at,)] = came[...]
        else:
            made[...] += came[...]


class Flow:
    def __init__(self, array, shape, hops, dims, cols=None):
        self.array, self.shape, self.dims, self.cols = array, tuple(shape), dims, cols
        self.hops = list(hops)

    def step(self):
        part = Part(self.hops.pop(0), self.shape, self.dims, self.cols)
        self.shape, self.dims, self.cols = part.after, part.left, None
        return part


class Window:
    def __init__(self, start, stop):
        self.start, self.stop = start, stop
        self.parts, self.sources, self.keeps = [], [], []


def plan(schedule):
    windows, arrays, latest = [], [], {}
    for n, (flows, start, stop) in enumerate(schedule):
        window = Window(start, stop)
        for i, flow in enumerate(flows):
            if flow in latest:
                source = ("part",) + latest[flow]
                before = windows[latest[flow][0]]
                before.keeps[latest[flow][1]] = False
            elif isinstance(flow.array, tuple):
                source = flow.array
            else:
                known = [k for k, a in enumerate(arrays) if a is flow.array]
                if not known:
                    arrays.append(flow.array)
                source = ("in", known[0] if known else len(arrays) - 1)
            window.parts.append(flow.step())
            window.sources.append(source)
            window.keeps.append(True)
            latest[flow] = (n, i)
        windows.append(window)
    return windows, arrays, latest


def carrying(body, own, windows, arrays, grid, also):
    ins, outs, held = own

    def kernel(*refs):
        refs = list(refs)

        def take(n):
            got = refs[:n]
            del refs[:n]
            return got

        my_in, arr = take(ins), take(arrays)
        my_out = take(outs)
        given = [[take(1)[0] if k else None for k in w.keeps] for w in windows]
        my_held = take(held)
        made, came = [], []
        for w, g in zip(windows, given):
            made.append([ref if ref is not None else take(1)[0] for ref in g])
            came.append(take(len(w.parts)))
        mine = my_in + my_out + my_held
        step = pl.program_id(0)
        hops = [q.hop for w in windows for q in w.parts] + list(also)
        if hops:
            pl.when(step == 0)(lambda: greet(hops))
        if windows:
            send, recv, local = refs
        copies, base = [], 0
        for w, m, c in zip(windows, made, came):
            now = []
            for i, q in enumerate(w.parts):
                kind = w.sources[i]
                if kind[0] == "in":
                    src = arr[kind[1]]
                elif kind[0] == "ref":
                    src = mine[kind[1]]
                    src = src.at[kind[2]] if len(kind) > 2 else src
                else:
                    src = made[kind[1]][kind[2]]
                now += q.copies(src, m[i], c[i], send.at[base], recv.at[base], local.at[base])
                base += 1
            copies.append(now)

        def phase(number):
            for n, w in enumerate(windows):
                if w.stop == number:
                    for copy in copies[n]:
                        copy.wait()
                    for q, m, c in zip(w.parts, made[n], came[n]):
                        q.add(m, c)
            for n, w in enumerate(windows):
                if w.start == number:
                    for copy in copies[n]:
                        copy.start()

        used = sorted({w.start for w in windows} | {w.stop for w in windows})
        for number in used:
            if number < grid:
                pl.when(step == number)(functools.partial(phase, number))
        body(*mine)
        for number in used:
            if number >= grid:
                pl.when(step == grid - 1)(functools.partial(phase, number))

    return kernel


def run(
    body, name, grid, ins, in_specs, outs, out_specs, held=(), schedule=(), collective=None,
    flops=0, moved=0, also=(),
):
    in_specs, outs, out_specs, held = list(in_specs), list(outs), list(out_specs), list(held)
    windows, arrays, latest = plan(schedule)
    own = len(outs)
    kernel = carrying(body, (len(ins), own, len(held)), windows, len(arrays), grid, also)
    in_specs += [pl.BlockSpec(memory_space=pl.ANY)] * len(arrays)
    order, count = [], 0
    for n, w in enumerate(windows):
        for i, (q, k) in enumerate(zip(w.parts, w.keeps)):
            if k:
                outs.append(jax.ShapeDtypeStruct(q.after, BF16))
                out_specs.append(whole(q.after))
                order.append((n, i))
            else:
                held.append(pltpu.VMEM(q.after, BF16))
        held += [pltpu.VMEM(q.came, BF16) for q in w.parts]
        count += len(w.parts)
    if windows:
        held += [pltpu.SemaphoreType.DMA((count,))] * 3
    results = pl.pallas_call(
        kernel,
        grid=(grid,),
        in_specs=in_specs,
        out_specs=out_specs,
        out_shape=outs,
        scratch_shapes=held,
        compiler_params=params(collective if windows or also else None),
        cost_estimate=cost(flops, moved),
        name=name,
    )(*ins, *arrays)
    for flow, where in latest.items():
        flow.array = results[own + order.index(where)]
    return results[:own]


VIA_X = ("x", "z1", "z2", "y")
VIA_Y = ("yr", "x", "z1", "z2", "yg")
VIA_Z = ("z1", "yr", "x", "z2", "yg")
BLOCK = ("z2", "z1", "x", "core")


def code_of(docs_ref):
    row = lax.broadcasted_iota(jnp.int32, (128, docs_ref.shape[1]), 0)
    return jnp.transpose(jnp.where(docs_ref[...] == row, 1.0, 0.0)).astype(BF16)


def project_own_kernel(x_ref, m_ref, td_ref, md_ref, wx_ref, wm_ref, b_ref, qkv_ref, mkv_ref, to_ref, mo_ref):
    step = pl.program_id(0)

    @pl.when(step == 0)
    def _():
        to_ref[...] = code_of(td_ref)
        mo_ref[...] = code_of(md_ref)

    @pl.when(step < 3)
    def _():
        bias = jnp.where(step == 0, b_ref[0:1], 0.0) + jnp.where(step == 2, b_ref[1:2], 0.0)
        qkv_ref[...] = (nn(x_ref[...], wx_ref[...]) + bias).astype(BF16)

    @pl.when(step >= 3)
    def _():
        bias = jnp.where(step == 4, b_ref[2:3], 0.0)
        mkv_ref[...] = (nn(m_ref[...], wm_ref[...]) + bias).astype(BF16)


def project_own(x, mem, td, md, wx, wm, biases):
    rows, width = x.shape
    code = jax.ShapeDtypeStruct((rows, 128), BF16)
    return pl.pallas_call(
        project_own_kernel,
        grid=(5,),
        in_specs=[
            whole((rows, width)), whole((rows, width)), whole((1, rows)), whole((1, rows)),
            pl.BlockSpec((width, width), lambda s: (0, jnp.minimum(s, 2))),
            pl.BlockSpec((width, width), lambda s: (0, jnp.maximum(s - 3, 0))),
            whole(biases.shape),
        ],
        out_specs=[
            pl.BlockSpec((rows, width), lambda s: (0, jnp.minimum(s, 2))),
            pl.BlockSpec((rows, width), lambda s: (0, jnp.maximum(s - 3, 0))),
            whole((rows, 128)), whole((rows, 128)),
        ],
        out_shape=[
            jax.ShapeDtypeStruct((rows, 3 * width), BF16), jax.ShapeDtypeStruct((rows, 2 * width), BF16), code, code,
        ],
        compiler_params=params(),
        cost_estimate=cost(10 * rows * width * width, 20 * width * width),
        name="project_own",
    )(x, mem, td, md, wx, wm, biases)


def project_other_kernel(x_ref, m_ref, td_ref, md_ref, wx_ref, b_ref, kvo_ref, mem_ref, tt_ref, mt_ref):
    step = pl.program_id(0)

    @pl.when(step == 0)
    def _():
        mem_ref[...] = m_ref[...]
        tt_ref[...] = code_of(td_ref)
        mt_ref[...] = code_of(md_ref)

    @pl.when(lax.axis_index("sp") == 1)
    def _():
        bias = jnp.where(step == 1, b_ref[1:2], 0.0)
        kvo_ref[...] = (nn(x_ref[...], wx_ref[...]) + bias).astype(BF16)

    @pl.when(lax.axis_index("sp") == 0)
    def _():
        kvo_ref[...] = jnp.zeros(kvo_ref.shape, BF16)


def project_other(x, mem, td, md, wx, biases):
    rows, width = x.shape
    code = jax.ShapeDtypeStruct((rows, 128), BF16)
    return pl.pallas_call(
        project_other_kernel,
        grid=(2,),
        in_specs=[
            whole((rows, width)), whole((rows, width)), whole((1, rows)), whole((1, rows)),
            pl.BlockSpec((width, width), lambda s: (0, s + 1)),
            whole(biases.shape),
        ],
        out_specs=[
            pl.BlockSpec((rows, width), lambda s: (0, s)),
            whole((rows, width)), whole((rows, 128)), whole((rows, 128)),
        ],
        out_shape=[
            jax.ShapeDtypeStruct((rows, 2 * width), BF16), jax.ShapeDtypeStruct((rows, width), BF16), code, code,
        ],
        compiler_params=params(),
        cost_estimate=cost(4 * rows * width * width, 10 * width * width),
        name="project_other",
    )(x, mem, td, md, wx, biases)


def project_memory_kernel(x_ref, w_ref, b_ref, o_ref):
    bias = jnp.where(pl.program_id(0) == 1, b_ref[2:3], 0.0)
    o_ref[...] = (nn(x_ref[...], w_ref[...]) + bias).astype(BF16)


def project_memory(x, w, biases):
    rows, width = x.shape
    return pl.pallas_call(
        project_memory_kernel,
        grid=(2,),
        in_specs=[
            whole((rows, width)),
            pl.BlockSpec((width, width), lambda j: (0, j)),
            whole(biases.shape),
        ],
        out_specs=pl.BlockSpec((rows, width), lambda j: (0, j)),
        out_shape=jax.ShapeDtypeStruct((rows, 2 * width), BF16),
        compiler_params=params(),
        cost_estimate=cost(4 * rows * width * width, 4 * width * (width + rows)),
        name="project_memory",
    )(x, w, biases)


def head_masks(dtype):
    lane = lax.broadcasted_iota(jnp.int32, (1, PAIR), 1)
    low = jnp.where(lane < HD, 1.0, 0.0)
    return low.astype(dtype), (1.0 - low).astype(dtype)


def query_code(code):
    lane = lax.broadcasted_iota(jnp.int32, code.shape, 1)
    return jnp.where(lane < 4, (code.astype(F32) - 1.0) * FAR, 0.0).astype(BF16)


def softmax_pieces(scores, values):
    peak = functools.reduce(jnp.maximum, [jnp.max(s, axis=-1, keepdims=True) for s in scores])
    expd = [jnp.exp(s - peak) for s in scores]
    norm = sum(jnp.sum(e, axis=-1, keepdims=True) for e in expd)
    out = sum(nn(e.astype(BF16), v) for e, v in zip(expd, values))
    return out / norm, peak + jnp.log(norm)


def self_pieces(block, size, both, own, other):
    pieces = []
    if both:
        pieces.append((other, False))
    if block:
        pieces.append((own[: block * size], False))
    pieces.append((own[block * size : (block + 1) * size], True))
    return pieces


def store_lse(lse_ref, block, size, low, high):
    lane = lax.broadcasted_iota(jnp.int32, (size, PAIR), 1)
    both = jnp.where(lane == 0, low, high)
    lse_ref[:, block * size : (block + 1) * size] = jnp.transpose(both)[:8]


def self_forward_kernel(size, q_ref, k_ref, v_ref, ko_ref, vo_ref, own_ref, oth_ref, o_ref, lse_ref):
    second = lax.axis_index("sp") == 1
    rows = q_ref.shape[0]
    masks = head_masks(BF16)
    outs = head_masks(F32)

    def run(both):
        qcode = query_code(own_ref[...])
        own = jnp.concatenate([k_ref[...], own_ref[...]], axis=1)
        oth = jnp.concatenate([ko_ref[...], oth_ref[...]], axis=1) if both else None
        vown = v_ref[...]
        voth = vo_ref[...] if both else None
        for block in range(rows // size):
            at = slice(block * size, (block + 1) * size)
            lses, result = [], 0.0
            for mask, keep in zip(masks, outs):
                q = jnp.concatenate([q_ref[at] * (mask * BF16(HD**-0.5)), qcode[at]], axis=1)
                scores = []
                for keys, diagonal in self_pieces(block, size, both, own, oth):
                    s = nt(q, keys)
                    if diagonal:
                        row = lax.broadcasted_iota(jnp.int32, s.shape, 0)
                        col = lax.broadcasted_iota(jnp.int32, s.shape, 1)
                        s = jnp.where(row >= col, s, -FAR)
                    scores.append(s)
                values = [v for v, _ in self_pieces(block, size, both, vown, voth)]
                out, lse = softmax_pieces(scores, values)
                result = result + out * keep
                lses.append(lse)
            o_ref[at] = result.astype(BF16)
            store_lse(lse_ref, block, size, *lses)

    pl.when(second)(lambda: run(True))
    pl.when(jnp.logical_not(second))(lambda: run(False))


def pair_spec(rows, offset):
    return pl.BlockSpec((rows, PAIR), lambda p: (0, p + offset))


def whole(shape):
    return pl.BlockSpec(shape, lambda *_: (0,) * len(shape))


def self_forward(qkv, kvo, own, oth):
    rows = qkv.shape[0]
    width = qkv.shape[1] // 3
    pairs = width // PAIR
    return pl.pallas_call(
        functools.partial(self_forward_kernel, 256),
        grid=(pairs,),
        in_specs=[
            pair_spec(rows, 0),
            pair_spec(rows, pairs),
            pair_spec(rows, 2 * pairs),
            pair_spec(rows, 0),
            pair_spec(rows, pairs),
            whole((rows, 128)),
            whole((rows, 128)),
        ],
        out_specs=[pair_spec(rows, 0), pl.BlockSpec((8, rows), lambda p: (p, 0))],
        out_shape=[
            jax.ShapeDtypeStruct((rows, width), BF16),
            jax.ShapeDtypeStruct((8 * pairs, rows), F32),
        ],
        compiler_params=params(),
        cost_estimate=cost(16 * rows * rows * width, 16 * rows * width),
        name="self_forward",
    )(qkv, qkv, qkv, kvo, kvo, own, oth)


def cross_forward_kernel(size, q_ref, k_ref, v_ref, ko_ref, vo_ref, t_ref, own_ref, oth_ref, o_ref, lse_ref):
    rows = q_ref.shape[0]
    masks = head_masks(BF16)
    outs = head_masks(F32)
    qcode = query_code(t_ref[...])
    keys = [
        jnp.concatenate([k_ref[...], own_ref[...]], axis=1),
        jnp.concatenate([ko_ref[...], oth_ref[...]], axis=1),
    ]
    values = [v_ref[...], vo_ref[...]]
    for block in range(rows // size):
        at = slice(block * size, (block + 1) * size)
        lses, result = [], 0.0
        for mask, keep in zip(masks, outs):
            q = jnp.concatenate([q_ref[at] * (mask * BF16(HD**-0.5)), qcode[at]], axis=1)
            out, lse = softmax_pieces([nt(q, k) for k in keys], values)
            result = result + out * keep
            lses.append(lse)
        o_ref[at] = result.astype(BF16)
        store_lse(lse_ref, block, size, *lses)


def cross_forward(cq, kv, kvo, t, own, oth):
    rows, width = cq.shape
    pairs = width // PAIR
    return pl.pallas_call(
        functools.partial(cross_forward_kernel, 256),
        grid=(pairs,),
        in_specs=[
            pair_spec(rows, 0),
            pair_spec(rows, 0),
            pair_spec(rows, pairs),
            pair_spec(rows, 0),
            pair_spec(rows, pairs),
            whole((rows, 128)),
            whole((rows, 128)),
            whole((rows, 128)),
        ],
        out_specs=[pair_spec(rows, 0), pl.BlockSpec((8, rows), lambda p: (p, 0))],
        out_shape=[
            jax.ShapeDtypeStruct((rows, width), BF16),
            jax.ShapeDtypeStruct((8 * pairs, rows), F32),
        ],
        compiler_params=params(),
        cost_estimate=cost(24 * rows * rows * width, 16 * rows * width),
        name="cross_forward",
    )(cq, kv, kv, kvo, kvo, t, own, oth)


def delta_rows(g, o):
    prod = g.astype(F32) * o.astype(F32)
    upper = prod.astype(BF16)
    lower = (prod - upper.astype(F32)).astype(BF16)
    row = lax.broadcasted_iota(jnp.int32, (8, PAIR), 0)
    lane = lax.broadcasted_iota(jnp.int32, (8, PAIR), 1)
    pick = jnp.where(row == lane // HD, 1.0, 0.0).astype(BF16)
    return nt(pick, upper) + nt(pick, lower)


def back_piece(keys, values, q, g, lse, delta, causal):
    s = nt(keys, q)
    if causal:
        row = lax.broadcasted_iota(jnp.int32, s.shape, 0)
        col = lax.broadcasted_iota(jnp.int32, s.shape, 1)
        s = jnp.where(row <= col, s, -FAR)
    p = jnp.exp(s - lse)
    ds = p * (nt(values, g) - delta)
    return p.astype(BF16), ds.astype(BF16)


def cross_backward_kernel(
    size, q_ref, k_ref, v_ref, ko_ref, vo_ref, g_ref, o_ref, lse_ref, t_ref, own_ref, oth_ref,
    m_ref, mo_ref, wk_ref, wv_ref,
    dq_ref, dm_ref, dmo_ref, gk_ref, gv_ref, gb_ref, dm_acc, dmo_acc,
):
    step = pl.program_id(0)
    rows = q_ref.shape[0]
    masks = head_masks(BF16)
    scale = BF16(HD**-0.5)
    qcode = query_code(t_ref[...])
    delta = delta_rows(g_ref[...], o_ref[...])
    lse = lse_ref[...]
    halves = [(k_ref, v_ref, own_ref, m_ref, dm_acc), (ko_ref, vo_ref, oth_ref, mo_ref, dmo_acc)]
    dq = [0.0] * (rows // size)
    gk = gv = gb = 0.0
    for kr, vr, code, mem, acc in halves:
        keys = jnp.concatenate([kr[...], code[...]], axis=1)
        values = vr[...]
        dk = dv = 0.0
        for block in range(rows // size):
            at = slice(block * size, (block + 1) * size)
            for head, mask in enumerate(masks):
                qm = q_ref[at] * (mask * scale)
                gm = g_ref[at] * mask
                q = jnp.concatenate([qm, qcode[at]], axis=1)
                p, ds = back_piece(
                    keys, values, q, gm, lse[head : head + 1, at], delta[head : head + 1, at], False
                )
                dk = dk + nn(ds, qm)
                dv = dv + nn(p, gm)
                dq[block] = dq[block] + tn(ds, kr[...] * (mask * scale))
        both = jnp.concatenate([dk.astype(BF16), dv.astype(BF16)], axis=1)
        grad = tn(mem[...], both)
        gk, gv = gk + grad[:, :PAIR], gv + grad[:, PAIR:]
        gb = gb + total(both[:, PAIR:])
        dm = nt(both, jnp.concatenate([wk_ref[...], wv_ref[...]], axis=1))

        @pl.when(step == 0)
        def _():
            acc[...] = dm

        @pl.when(step > 0)
        def _():
            acc[...] += dm
    for block in range(rows // size):
        dq_ref[block * size : (block + 1) * size] = dq[block].astype(BF16)
    gk_ref[...] = gk.astype(BF16)
    gv_ref[...] = gv.astype(BF16)
    gb_ref[...] = gb

    @pl.when(step == pl.num_programs(0) - 1)
    def _():
        dm_ref[...] = dm_acc[...]
        dmo_ref[...] = dmo_acc[...].astype(BF16)


def cross_backward(cq, kv, kvo, g, o, lse, t, own, oth, m, mo, w, schedule):
    rows, width = cq.shape
    pairs = width // PAIR
    flat = jax.ShapeDtypeStruct((rows, width), BF16)
    square = jax.ShapeDtypeStruct((width, width), BF16)
    return run(
        functools.partial(cross_backward_kernel, 256), "cross_backward", pairs,
        (cq, kv, kv, kvo, kvo, g, o, lse, t, own, oth, m, mo, w, w),
        [
            pair_spec(rows, 0),
            pair_spec(rows, 0),
            pair_spec(rows, pairs),
            pair_spec(rows, 0),
            pair_spec(rows, pairs),
            pair_spec(rows, 0),
            pair_spec(rows, 0),
            pl.BlockSpec((8, rows), lambda p: (p, 0)),
            whole((rows, 128)),
            whole((rows, 128)),
            whole((rows, 128)),
            whole((rows, width)),
            whole((rows, width)),
            pair_spec(width, 0),
            pair_spec(width, pairs),
        ],
        [flat, jax.ShapeDtypeStruct((rows, width), F32), flat, square, square, jax.ShapeDtypeStruct((1, width), F32)],
        [pair_spec(rows, 0)] + [whole((rows, width))] * 2 + [pair_spec(width, 0)] * 2 + [pair_spec(1, 0)],
        [pltpu.VMEM((rows, width), F32)] * 2,
        schedule, 3,
        64 * rows * rows * width + 16 * rows * width * width, 24 * rows * width,
    )


def self_backward_kernel(
    size, q_ref, k_ref, v_ref, ko_ref, vo_ref, g_ref, o_ref, lse_ref, own_ref, oth_ref,
    dq_ref, dk_ref, dv_ref, dko_ref, dvo_ref,
):
    second = lax.axis_index("sp") == 1
    rows = q_ref.shape[0]
    masks = head_masks(BF16)
    scale = BF16(HD**-0.5)

    def run(both):
        qcode = query_code(own_ref[...])
        delta = delta_rows(g_ref[...], o_ref[...])
        lse = lse_ref[...]
        count = rows // size
        dk, dv = [0.0] * count, [0.0] * count
        dko = dvo = 0.0
        for block in range(count):
            at = slice(block * size, (block + 1) * size)
            dq = 0.0
            for head, mask in enumerate(masks):
                qm = q_ref[at] * (mask * scale)
                gm = g_ref[at] * mask
                q = jnp.concatenate([qm, qcode[at]], axis=1)
                rest = (q, gm, lse[head : head + 1, at], delta[head : head + 1, at])
                for part in range(block + 1):
                    of = slice(part * size, (part + 1) * size)
                    keys = jnp.concatenate([k_ref[of], own_ref[of]], axis=1)
                    p, ds = back_piece(keys, v_ref[of], *rest, part == block)
                    dk[part] = dk[part] + nn(ds, qm)
                    dv[part] = dv[part] + nn(p, gm)
                    dq = dq + tn(ds, k_ref[of] * (mask * scale))
                if both:
                    keys = jnp.concatenate([ko_ref[...], oth_ref[...]], axis=1)
                    p, ds = back_piece(keys, vo_ref[...], *rest, False)
                    dko = dko + nn(ds, qm)
                    dvo = dvo + nn(p, gm)
                    dq = dq + tn(ds, ko_ref[...] * (mask * scale))
            dq_ref[at] = dq.astype(BF16)
        for part in range(count):
            of = slice(part * size, (part + 1) * size)
            dk_ref[of] = dk[part].astype(BF16)
            dv_ref[of] = dv[part].astype(BF16)
        if both:
            dko_ref[...] = dko.astype(BF16)
            dvo_ref[...] = dvo.astype(BF16)
        else:
            dko_ref[...] = jnp.zeros(dko_ref.shape, BF16)
            dvo_ref[...] = jnp.zeros(dvo_ref.shape, BF16)

    pl.when(second)(lambda: run(True))
    pl.when(jnp.logical_not(second))(lambda: run(False))


def self_backward(qkv, kvo, g, o, lse, own, oth, schedule):
    rows = qkv.shape[0]
    width = qkv.shape[1] // 3
    pairs = width // PAIR
    flat = jax.ShapeDtypeStruct((rows, width), BF16)
    return run(
        functools.partial(self_backward_kernel, 256), "self_backward", pairs,
        (qkv, qkv, qkv, kvo, kvo, g, o, lse, own, oth),
        [
            pair_spec(rows, 0),
            pair_spec(rows, pairs),
            pair_spec(rows, 2 * pairs),
            pair_spec(rows, 0),
            pair_spec(rows, pairs),
            pair_spec(rows, 0),
            pair_spec(rows, 0),
            pl.BlockSpec((8, rows), lambda p: (p, 0)),
            whole((rows, 128)),
            whole((rows, 128)),
        ],
        [flat] * 5,
        [pair_spec(rows, 0)] * 5,
        (), schedule, 5,
        48 * rows * rows * width, 24 * rows * width,
    )


def first_norm_kernel(x_ref, ctx_ref, wo_ref, wq_ref, b_ref, h_ref, cq_ref):
    h = x_ref[...].astype(F32) + nn(ctx_ref[...], wo_ref[...]) + b_ref[3:4]
    h_ref[...] = h
    n, _ = normed(h)
    a = (n * b_ref[4:5] + b_ref[5:6]).astype(BF16)
    cq_ref[...] = (nn(a, wq_ref[...]) + b_ref[6:7]).astype(BF16)


def first_norm(x, ctx, wo, wq, biases):
    rows, width = x.shape
    return pl.pallas_call(
        first_norm_kernel,
        out_shape=[
            jax.ShapeDtypeStruct((rows, width), F32),
            jax.ShapeDtypeStruct((rows, width), BF16),
        ],
        compiler_params=params(),
        cost_estimate=cost(4 * rows * width * width, 4 * width * width + 10 * rows * width),
        name="first_norm",
    )(x, ctx, wo, wq, biases)


def feed_kernel(
    count, comm, h1_ref, cc_ref, ct_ref, wco_ref, b_ref, wi_ref, wo_ref,
    out_ref, dh2_ref, dcc_ref, gco_ref, gwi_ref, gwo_ref, small_ref, gib_ref,
    hid_ref, slope_ref, n2_ref, r2_ref, a2b_ref, acc_ref, df_ref, *refs,
):
    step = pl.program_id(0)
    width = acc_ref.shape[1]

    if comm:
        mi_ref, mo_ref, ci_ref, co_ref, send_ref, recv_ref = refs
        _, c, _, _ = place()

        def chunk_copies(j):
            at = pl.ds(pl.multiple_of(j * width, width), width)
            return [
                remote(
                    mi_ref.at[:, 1 - c, :, at], ci_ref.at[:, :, at], send_ref.at[0, j], recv_ref.at[0, j], "core"
                ),
                remote(mo_ref.at[j, :, 1 - c], co_ref.at[j], send_ref.at[1, j], recv_ref.at[1, j], "core"),
            ]

    @pl.when(step == 0)
    def _():
        if comm:
            greet(["core"])
        n1, _ = normed(h1_ref[...])
        a1 = n1 * b_ref[4:5] + b_ref[5:6]
        h2 = a1 + nn(cc_ref[...], wco_ref[...]) + b_ref[7:8]
        n2, r2 = normed(h2)
        n2_ref[...] = n2
        r2_ref[...] = jnp.broadcast_to(r2, r2_ref.shape)
        a2 = n2 * b_ref[8:9] + b_ref[9:10]
        a2b_ref[...] = a2.astype(BF16)
        acc_ref[...] = a2 + b_ref[10:11]

    @pl.when(step < count)
    def _():
        u = nn(a2b_ref[...], wi_ref[...]) + b_ref[pl.ds(13 + step, 1)]
        cumul = 0.5 * (1.0 + lax.erf(u * 0.7071067811865476))
        density = jnp.exp(-0.5 * u * u) * 0.3989422804014327
        hid = (u * cumul).astype(BF16)
        hid_ref[step] = hid
        slope_ref[step] = cumul + u * density
        acc_ref[...] += nn(hid, wo_ref[...])

    @pl.when(step == count - 1)
    def _():
        n3, r3 = normed(acc_ref[...])
        gain = b_ref[11:12]
        out_ref[...] = (n3 * gain + b_ref[12:13]).astype(BF16)
        e = ct_ref[...].astype(F32)
        d3 = norm_back(e, n3, r3, gain)
        df = d3.astype(BF16)
        df_ref[...] = df
        acc_ref[...] = d3
        small_ref[0:1] = total(e * n3)
        small_ref[1:2] = total(e)
        small_ref[2:3] = total(df)

    @pl.when(jnp.logical_and(step >= count, step < 2 * count))
    def _():
        j = step - count
        df = df_ref[...]
        du = (nt(df, wo_ref[...]) * slope_ref[j]).astype(BF16)
        gib_ref[...] = total(du)
        acc_ref[...] += nt(du, wi_ref[...])
        go = tn(hid_ref[j], df).astype(BF16)
        gi = tn(a2b_ref[...], du).astype(BF16)
        if comm:
            at = pl.ds(pl.multiple_of(j * width, width), width)
            mo_ref[j] = go.reshape(mo_ref.shape[1:])
            mi_ref[:, :, :, at] = gi.reshape(mi_ref.shape[:3] + (width,))
            for copy in chunk_copies(j):
                copy.start()
        else:
            gwo_ref[...] = go
            gwi_ref[...] = gi

    @pl.when(step == 2 * count)
    def _():
        d2 = acc_ref[...]
        n2 = n2_ref[...]
        dh2 = norm_back(d2, n2, r2_ref[:, :1], b_ref[8:9])
        dh2_ref[...] = dh2
        dco = dh2.astype(BF16)
        dcc_ref[...] = nt(dco, wco_ref[...]).astype(BF16)
        gco_ref[...] = tn(cc_ref[...], dco).astype(BF16)
        small_ref[3:4] = total(d2 * n2)
        small_ref[4:5] = total(d2)
        small_ref[5:6] = total(dco)
        small_ref[6:8] = jnp.zeros((2, d2.shape[1]), F32)

    if comm:

        @pl.when(step > count)
        def _():
            j = step - count - 1
            at = pl.ds(pl.multiple_of(j * width, width), width)
            for copy in chunk_copies(j):
                copy.wait()
            gwi_ref[...] = mi_ref[:, c, :, at] + ci_ref[:, :, at]
            gwo_ref[0] = mo_ref[j, :, c] + co_ref[j]


def feed(size, comm, h1, cc, ct, wco, biases, wi, wo):
    rows, width = h1.shape
    wide = wi.shape[1]
    chunk = width
    count = wide // chunk

    def weight(s):
        return jnp.where(s < count, s, jnp.minimum(s - count, count - 1))

    def early(s):
        return jnp.clip(s - count, 0, count - 1)

    def late(s):
        return jnp.clip(s - count - 1, 0, count - 1)

    flat = whole((rows, width))
    square = whole((width, width))
    scratch = [
        pltpu.VMEM((count, rows, chunk), BF16),
        pltpu.VMEM((count, rows, chunk), F32),
        pltpu.VMEM((rows, width), F32),
        pltpu.VMEM((rows, 128), F32),
        pltpu.VMEM((rows, width), BF16),
        pltpu.VMEM((rows, width), F32),
        pltpu.VMEM((rows, width), BF16),
    ]
    if comm:
        narrow, broad = width // size, wide // size
        grad_specs = [
            pl.BlockSpec((size // 2, narrow, chunk), lambda s: (0, 0, late(s))),
            pl.BlockSpec((1, 2, broad, width), lambda s: (late(s), 0, 0, 0)),
        ]
        grad_shapes = [(size // 2, narrow, wide), (count, 2, broad, width)]
        scratch += [
            pltpu.VMEM((size // 2, 2, narrow, wide), BF16),
            pltpu.VMEM((count, 2, 2, broad, width), BF16),
            pltpu.VMEM((size // 2, narrow, wide), BF16),
            pltpu.VMEM((count, 2, broad, width), BF16),
            pltpu.SemaphoreType.DMA((2, count)),
            pltpu.SemaphoreType.DMA((2, count)),
        ]
    else:
        grad_specs = [
            pl.BlockSpec((width, chunk), lambda s: (0, early(s))),
            pl.BlockSpec((chunk, width), lambda s: (early(s), 0)),
        ]
        grad_shapes = [(width, wide), (wide, width)]
    return pl.pallas_call(
        functools.partial(feed_kernel, count, comm),
        grid=(2 * count + 1,),
        in_specs=[
            flat, flat, flat, square, whole(biases.shape),
            pl.BlockSpec((width, chunk), lambda s: (0, weight(s))),
            pl.BlockSpec((chunk, width), lambda s: (weight(s), 0)),
        ],
        out_specs=[flat, flat, flat, square]
        + grad_specs
        + [whole((8, width)), pl.BlockSpec((1, chunk), lambda s: (0, early(s)))],
        out_shape=[
            jax.ShapeDtypeStruct((rows, width), BF16),
            jax.ShapeDtypeStruct((rows, width), F32),
            jax.ShapeDtypeStruct((rows, width), BF16),
            jax.ShapeDtypeStruct((width, width), BF16),
        ]
        + [jax.ShapeDtypeStruct(a, BF16) for a in grad_shapes]
        + [
            jax.ShapeDtypeStruct((8, width), F32),
            jax.ShapeDtypeStruct((1, wide), F32),
        ],
        scratch_shapes=scratch,
        compiler_params=params(2 if comm else None),
        cost_estimate=cost(
            12 * rows * width * wide + 6 * rows * width * width, 12 * width * wide + 16 * rows * width
        ),
        name="feed",
    )(h1, cc, ct, wco, biases, wi, wo)


def first_back_kernel(
    dcq_ref, dh2_ref, h1_ref, ctx_ref, wcq_ref, wso_ref, b_ref,
    dh1_ref, dsc_ref, gcq_ref, gso_ref, small_ref,
):
    gain = b_ref[4:5]
    n1, r1 = normed(h1_ref[...])
    a1b = (n1 * gain + b_ref[5:6]).astype(BF16)
    dcq = dcq_ref[...]
    d1 = dh2_ref[...] + nt(dcq, wcq_ref[...])
    dh1 = norm_back(d1, n1, r1, gain)
    dh1_ref[...] = dh1
    dso = dh1.astype(BF16)
    dsc_ref[...] = nt(dso, wso_ref[...]).astype(BF16)
    gcq_ref[...] = tn(a1b, dcq).astype(BF16)
    gso_ref[...] = tn(ctx_ref[...], dso).astype(BF16)
    small_ref[0:1] = total(dcq)
    small_ref[1:2] = total(d1 * n1)
    small_ref[2:3] = total(d1)
    small_ref[3:4] = total(dso)
    small_ref[4:8] = jnp.zeros((4, dh1.shape[1]), F32)


def first_back(dcq, dh2, h1, ctx, wcq, wso, biases, schedule):
    rows, width = dcq.shape
    flat, square = whole((rows, width)), whole((width, width))
    return run(
        first_back_kernel, "first_back", 1,
        (dcq, dh2, h1, ctx, wcq, wso, biases),
        [flat, flat, flat, flat, square, square, whole(biases.shape)],
        [
            jax.ShapeDtypeStruct((rows, width), F32),
            jax.ShapeDtypeStruct((rows, width), BF16),
            jax.ShapeDtypeStruct((width, width), BF16),
            jax.ShapeDtypeStruct((width, width), BF16),
            jax.ShapeDtypeStruct((8, width), F32),
        ],
        [flat, flat, square, square, whole((8, width))],
        (), schedule, 4,
        8 * rows * width * width, 8 * width * width + 18 * rows * width,
    )


def input_back_kernel(
    x_ref, xo_ref, dq_ref, dk_ref, dv_ref, dko_ref, dvo_ref, w_ref, dh1_ref, sa_ref, sb_ref, sc_ref, sd_ref,
    dx_ref, g_ref, sm_ref, dxo_ref, came_ref, turn_ref, send_ref, recv_ref,
):
    step = pl.program_id(0)
    sp = lax.axis_index("sp")
    width = x_ref.shape[1]
    over = remote(dxo_ref, came_ref, send_ref.at[0], recv_ref.at[0], "y")

    @pl.when(step == 0)
    def _():
        @pl.when(sp == 1)
        def _():
            dxo = nt(dko_ref[...], w_ref[:, width : 2 * width]) + nt(dvo_ref[...], w_ref[:, 2 * width :])
            dxo_ref[...] = dxo.astype(BF16)
            over.start()

        g_ref[0] = tn(x_ref[...], dq_ref[...]).astype(BF16).reshape(g_ref.shape[1:])
        turn_ref[...] = jnp.zeros(turn_ref.shape, F32)
        turn_ref[0:8] = sa_ref[...]
        turn_ref[8:16] = sb_ref[...]
        turn_ref[16:17] = sc_ref[...]
        turn_ref[17:21] = sd_ref[...]
        turn_ref[21:22] = total(dq_ref[...])

    for n, (own, oth) in enumerate(((dk_ref, dko_ref), (dv_ref, dvo_ref)), start=1):

        @pl.when(jnp.logical_and(step == n, sp == 1))
        def _():
            grad = tn(x_ref[...], own[...]) + tn(xo_ref[...], oth[...])
            g_ref[n] = grad.astype(BF16).reshape(g_ref.shape[1:])

        @pl.when(jnp.logical_and(step == n, sp == 0))
        def _():
            g_ref[n] = tn(x_ref[...], own[...]).astype(BF16).reshape(g_ref.shape[1:])

    @pl.when(step == 2)
    def _():
        sums = total(dv_ref[...])
        turn_ref[22:23] = jnp.where(sp == 1, sums + total(dvo_ref[...]), sums)
        sm_ref[...] = jnp.transpose(turn_ref[...]).astype(BF16).reshape(sm_ref.shape)

    @pl.when(step == 3)
    def _():
        dx = (
            dh1_ref[...]
            + nt(dq_ref[...], w_ref[:, :width])
            + nt(dk_ref[...], w_ref[:, width : 2 * width])
            + nt(dv_ref[...], w_ref[:, 2 * width :])
        )

        @pl.when(sp == 0)
        def _():
            over.wait_recv()
            dx_ref[...] = (dx + came_ref[...].astype(F32)).astype(BF16)

        @pl.when(sp == 1)
        def _():
            over.wait_send()
            dx_ref[...] = dx.astype(BF16)


def input_back(block, x, xo, dq, dk, dv, dko, dvo, w, dh1, small, schedule):
    rows, width = x.shape
    flat = whole((rows, width))
    ins = (x, xo, dq, dk, dv, dko, dvo, w, dh1) + tuple(small)
    made = [(3,) + block + (width,), block + (128,)]
    outs = [jax.ShapeDtypeStruct((rows, width), BF16)]
    specs = [flat]
    held = []
    if schedule:
        held += [pltpu.VMEM(a, BF16) for a in made]
    else:
        outs += [jax.ShapeDtypeStruct(a, BF16) for a in made]
        specs += [whole(a) for a in made]
    held += [
        pltpu.VMEM((rows, width), BF16),
        pltpu.VMEM((rows, width), BF16),
        pltpu.VMEM((128, width), F32),
        pltpu.SemaphoreType.DMA((1,)),
        pltpu.SemaphoreType.DMA((1,)),
    ]
    return run(
        input_back_kernel, "input_back", 4, ins, [whole(a.shape) for a in ins], outs, specs, held,
        schedule, 6, 20 * rows * width * width, 12 * width * width + 28 * rows * width, ("y",),
    )


def outputs_kernel(places, count, *refs):
    pieces, rest = refs[:count], refs[count:]
    lines_ref, out_ref, dx_ref, dm_ref, dmi_ref = rest[:5]
    outs = rest[5:]
    for ref, (which, col) in zip(pieces, places):
        outs[which][:, col : col + ref.shape[1]] = ref[...].astype(F32)
    turned, result, dx, dm = outs[-4:]
    turned[...] = jnp.transpose(lines_ref[...].astype(F32))
    result[...] = out_ref[...]
    dx[...] = dx_ref[...]
    dm[...] = (dm_ref[...] + dmi_ref[...].astype(F32)).astype(BF16)


def outputs(pieces, places, shapes, lines, out, dx, dm, dmi):
    ins = tuple(pieces) + (lines, out, dx, dm, dmi)
    result = jax.ShapeDtypeStruct(out.shape, BF16)
    return pl.pallas_call(
        functools.partial(outputs_kernel, places, len(pieces)),
        out_shape=[jax.ShapeDtypeStruct(a, F32) for a in shapes]
        + [jax.ShapeDtypeStruct((128, lines.shape[0]), F32), result, result, result],
        compiler_params=params(),
        cost_estimate=cost(0, 12 << 20),
        name="outputs",
    )(*ins)


def swap_sum(part, axis, pairs):
    came = lax.ppermute(part, axis, pairs)
    return part.astype(F32) + came.astype(F32)


def sum_scatter(grad, size, order):
    rows, cols = grad.shape
    bits = size.bit_length() - 1
    me = lax.axis_index("dp")
    now = grad.reshape((2,) * bits + (rows // size, cols))
    left = list(range(bits))[::-1]
    for bit in [b for b in order if b < bits] + [b for b in range(bits) if b not in order]:
        axis = left.index(bit)
        mine = (me >> bit) & 1
        keep = lax.dynamic_index_in_dim(now, mine, axis, keepdims=False)
        send = lax.dynamic_index_in_dim(now, 1 - mine, axis, keepdims=False)
        came = lax.ppermute(send, "dp", [(i, i ^ (1 << bit)) for i in range(size)])
        now = (keep.astype(F32) + came.astype(F32)).astype(BF16)
        left.pop(axis)
    return swap_sum(now, "sp", [(0, 1), (1, 0)])


def per_device(
    size,
    inputs,
    memory,
    target_docs,
    memory_docs,
    cotangent,
    w_qkv,
    b_q,
    b_v,
    w_so,
    b_so,
    g_one,
    s_one,
    w_cq,
    b_cq,
    w_ckv,
    b_cv,
    w_co,
    b_co,
    g_two,
    s_two,
    w_fi,
    b_fi,
    w_fo,
    b_fo,
    g_three,
    s_three,
):
    rows, width = inputs.shape[1:]
    wide = b_fi.shape[0]
    comm = size == 16
    narrow, broad = width // size, wide // size
    swap = [(0, 1), (1, 0)]
    x, mem, ct = inputs[0], memory[0], cotangent[0]
    x_o = lax.ppermute(x, "sp", [(0, 1)])
    docs_o = lax.ppermute(jnp.concatenate([target_docs, memory_docs], axis=0), "sp", swap)
    line = lax.broadcasted_iota(jnp.int32, (24, width), 0)
    vectors = (b_q, b_v, b_cv, b_so, g_one, s_one, b_cq, b_co, g_two, s_two, b_fo, g_three, s_three)
    vectors += tuple(b_fi[i : i + width] for i in range(0, wide, width))
    biases = jnp.zeros((24, width), F32)
    for i, v in enumerate(vectors):
        biases = jnp.where(line == i, v.astype(F32)[None], biases)

    qkv, mkv, t_own, m_own = project_own(x, mem, target_docs, memory_docs, w_qkv, w_ckv, biases)
    kvo, mem_s, t_oth, m_oth = project_other(x_o, mem, docs_o[:1], docs_o[1:], w_qkv, biases)
    mem_o = lax.ppermute(mem_s, "sp", swap)
    ctx, lse = self_forward(qkv, kvo, t_own, t_oth)
    h1, cq = first_norm(x, ctx, w_so, w_cq, biases)
    mkvo = project_memory(mem_o, w_ckv, biases)
    cc, clse = cross_forward(cq, mkv, mkvo, t_own, m_own, m_oth)
    output, dh2, dcc, gco, gwi, gwo, small_a, gib = feed(
        size, comm, h1, cc, ct, w_co, biases, w_fi, w_fo
    )
    turned = gib.reshape(width, -1).T

    def flow(array, hops, first=0, cols=None, before=("core",)):
        shape = (2, 2, 2, 2, narrow, array.shape[1])
        return Flow(array.reshape(shape), shape, before + hops, BLOCK, (first, cols or array.shape[1]))

    at_cross, at_first, at_self, at_input = (), (), (), ()
    if comm:
        gwi = gwi.reshape(2, 2, 2, narrow, wide)
        gwo = gwo.reshape(2, 2, 2, broad, width)
        third = wide // 3
        t0 = [
            Flow(gwi, gwi.shape, hops, BLOCK[:3], (i * third, third)) for i, hops in enumerate((VIA_X, VIA_Y, VIA_Z))
        ] + [
            Flow(gwo, gwo.shape, hops, BLOCK[:3], (i * 256, 256)) for i, hops in enumerate((VIA_X, VIA_Y, VIA_Z))
        ]
        late = [f for f in t0 if "yg" in f.hops]
        early = [flow(gco, VIA_Y)]
        at_cross = ((t0, 0, 3), (t0, 3, 5), (t0, 5, 6), (early, 0, 6))
    dcq, dm, dmo, gck, gcv, gcvb = cross_backward(
        cq, mkv, mkvo, dcc, cc, clse, t_own, m_own, m_oth, mem, mem_o, w_ckv, at_cross
    )
    dm_in = lax.ppermute(dmo, "sp", swap)
    if comm:
        at_first = ((t0, 0, 1),)
    dh1, dsc, gcq, gso, small_b = first_back(dcq, dh2, h1, ctx, w_cq, w_so, biases, at_first)
    if comm:
        fresh = [flow(gck, VIA_X), flow(gcv, VIA_Z)] + [
            flow(g, hops, 256 * i, 256) for g in (gcq, gso) for i, hops in enumerate((VIA_X, VIA_Y, VIA_Z))
        ]
        t1 = early + fresh
        at_self = ((late, 0, 2), (fresh, 0, 2), (t1, 2, 5), (t1, 5, 6))
    dq, dk, dv, dko, dvo = self_backward(qkv, kvo, dsc, ctx, lse, t_own, t_oth, at_self)
    block = (width,)
    if comm:
        block = (2, 2, 2, 2, narrow)
        last = [
            Flow(("ref", 14, i), block + (width,), ("core",) + hops, BLOCK) for i, hops in enumerate((VIA_X, VIA_Z, VIA_Y))
        ]
        last.append(Flow(("ref", 15), block + (128,), ("core",) + VIA_X, BLOCK))
        t1_late = [f for f in t1 if "yg" in f.hops]
        gq, gk, gv, sm = last
        at_input = (
            (t1, 0, 2), (t1, 2, 4), (t1_late, 4, 6),
            ([gq], 1, 2), ([gk], 2, 3), ([gv, sm], 3, 4),
            ([gq], 2, 4), ([gk], 3, 5), ([gv, sm], 4, 5),
            ([gq], 4, 5), (last, 5, 6), ([gk, gv, sm], 6, 7), (last, 7, 8), ([gk, gv], 8, 9),
        )
    dx, *rest = input_back(
        block, x, x_o, dq, dk, dv, dko, dvo, w_qkv, dh1, (small_a, small_b, gcvb, turned), at_input
    )
    if comm:
        pieces, places = [], []
        for flows, which in (
            ([gq, gk, gv], 0), (t1[1:3], 1), (t0[:3], 2), (t0[3:], 3), (t1[:1], 4), (t1[3:6], 5), (t1[6:], 6)
        ):
            col = 0
            for f in flows:
                pieces.append(f.array)
                places.append((which, col))
                col += f.shape[-1]
        shapes = [(narrow, 3 * width), (narrow, 2 * width), (narrow, wide), (broad, width)] + [(narrow, width)] * 3
        t_qkv, t_cmem, t_fin, t_fout, t_cout, t_cquery, t_out, lines, output, derivative, grad_memory = outputs(
            pieces, places, shapes, sm.array, output, dx, dm, dm_in
        )
    else:
        gqkv, columns = rest
        t_fin, t_fout, t_cout, t_cquery, t_out, t_cmem, t_qkv, lines = (
            sum_scatter(g, size, (0, 1, 2, 3))
            for g in (
                gwi, gwo, gco, gcq, gso, jnp.concatenate([gck, gcv], axis=1),
                jnp.concatenate([gqkv[0], gqkv[1], gqkv[2]], axis=1), columns,
            )
        )
        lines, derivative = lines.T, dx
        grad_memory = (dm + dm_in.astype(F32)).astype(BF16)
    t_gthree, t_sthree, t_fobias, t_gtwo, t_stwo, t_cobias = (lines[i] for i in range(6))
    t_cqbias, t_gone, t_sone, t_obias = (lines[i] for i in range(8, 12))
    t_cvbias, t_qbias, t_vbias = lines[16], lines[21], lines[22]
    t_fibias = lines[17:21].T.reshape(-1)
    return (
        output[None],
        derivative[None],
        grad_memory[None],
        t_qkv,
        t_qbias,
        t_vbias,
        t_out,
        t_obias,
        t_gone,
        t_sone,
        t_cquery,
        t_cqbias,
        t_cmem,
        t_cvbias,
        t_cout,
        t_cobias,
        t_gtwo,
        t_stwo,
        t_fin,
        t_fibias,
        t_fout,
        t_fobias,
        t_gthree,
        t_sthree,
    )


def solution(mesh):
    split = P("dp", "sp", None)
    in_specs = (split, split, P("dp", "sp"), P("dp", "sp"), split) + (P(),) * 21
    matrix, vector = P("dp", None), P("dp")
    out_specs = (
        split, split, split,
        matrix, vector, vector,
        matrix, vector, vector, vector,
        matrix, vector,
        matrix, vector,
        matrix, vector, vector, vector,
        matrix, vector,
        matrix, vector, vector, vector,
    )
    return jax.shard_map(
        functools.partial(per_device, mesh.shape["dp"]),
        mesh=mesh, in_specs=in_specs, out_specs=out_specs, check_vma=False,
    )
```

```python
import functools

import jax
import jax.numpy as jnp
from jax import lax
from jax.experimental import pallas as pl
from jax.experimental.pallas import tpu as pltpu
from jax.sharding import PartitionSpec as P

HD = 64
PAIR = 2 * HD
EPS = 1e-05
FAR = 1.0e9
VMEM = 60 * 1024 * 1024
F32 = jnp.float32
BF16 = jnp.bfloat16


def nn(a, b):
    return lax.dot_general(a, b, (((1,), (0,)), ((), ())), preferred_element_type=F32)


def nt(a, b):
    return lax.dot_general(a, b, (((1,), (1,)), ((), ())), preferred_element_type=F32)


def tn(a, b):
    return lax.dot_general(a, b, (((0,), (0,)), ((), ())), preferred_element_type=F32)


def params(collective=None):
    if collective is None:
        return pltpu.CompilerParams(vmem_limit_bytes=VMEM, fuse_transposed_lhs_in_matmul=True)
    return pltpu.CompilerParams(
        vmem_limit_bytes=VMEM, collective_id=collective, has_side_effects=True, fuse_transposed_lhs_in_matmul=True
    )


def cost(flops, moved):
    return pl.CostEstimate(flops=int(flops), bytes_accessed=int(moved), transcendentals=0)


def normed(h):
    centred = h - jnp.mean(h, axis=-1, keepdims=True)
    rstd = lax.rsqrt(jnp.mean(centred * centred, axis=-1, keepdims=True) + EPS)
    return centred * rstd, rstd


def norm_back(grad, n, rstd, gain):
    scaled = grad * gain
    centre = jnp.mean(scaled, axis=-1, keepdims=True)
    along = jnp.mean(scaled * n, axis=-1, keepdims=True)
    return rstd * (scaled - centre - n * along)


def total(a):
    return jnp.sum(a.astype(F32), axis=0, keepdims=True)


def place():
    me = lax.axis_index("dp")
    return me, me % 2, (me // 2) % 2, me // 4


def partner(hop, at=None):
    me, c, x, z = at or place()
    if hop == "core":
        return {"dp": me + 1 - 2 * c}
    if hop == "x":
        return {"dp": me + 2 - 4 * x}
    if hop == "z1":
        return {"dp": me + 4 - 8 * (z % 2)}
    if hop == "z2":
        return {"dp": me + 8 - 16 * (z // 2)}
    return {"sp": 1 - lax.axis_index("sp")}


def greet(hops, at=None):
    hops = sorted({"y" if h[0] == "y" else h for h in hops})
    barrier = pltpu.get_barrier_semaphore()
    for hop in hops:
        pl.semaphore_signal(barrier, inc=1, device_id=partner(hop, at), device_id_type=pl.DeviceIdType.MESH)
    pl.semaphore_wait(barrier, len(hops))


def remote(src, dst, send, recv, hop, at=None):
    return pltpu.make_async_remote_copy(
        src_ref=src, dst_ref=dst, send_sem=send, recv_sem=recv,
        device_id=partner(hop, at), device_id_type=pl.DeviceIdType.MESH,
    )


class Part:
    def __init__(self, hop, shape, dims, cols=None):
        self.hop, self.dims = hop, dims
        self.cols = cols or (0, shape[-1])
        self.shape = shape = tuple(shape[:-1]) + (self.cols[1],)
        if hop in dims:
            at = dims.index(hop)
            self.after, self.left = shape[:at] + shape[at + 1 :], dims[:at] + dims[at + 1 :]
        else:
            wide = shape[-1]
            wide = wide // 2 if hop == "yr" else 2 * wide if hop == "yg" else wide
            self.after, self.left = shape[:-1] + (wide,), dims
        self.came = shape if hop == "yg" else self.after

    def copies(self, src, made, came, send, recv, local, at_dp, sp):
        _, c, x, z = at_dp
        first, wide = self.cols
        full = (slice(None),) * (len(self.shape) - 1)
        stay = away = full + (pl.ds(first, wide),)
        to = made
        if self.hop in self.dims:
            at = self.dims.index(self.hop)
            mine = {"core": c, "x": x, "z1": z % 2, "z2": z // 2}[self.hop]
            stay = stay[:at] + (mine,) + stay[at + 1 :]
            away = away[:at] + (1 - mine,) + away[at + 1 :]
        elif self.hop == "yr":
            half = wide // 2
            stay = full + (pl.ds(pl.multiple_of(first + sp * half, 128), half),)
            away = full + (pl.ds(pl.multiple_of(first + (1 - sp) * half, 128), half),)
        elif self.hop == "yg":
            to = made.at[full + (pl.ds(pl.multiple_of(sp * wide, 128), wide),)]
        return [
            remote(src.at[away], came, send, recv, self.hop, at_dp),
            pltpu.make_async_copy(src.at[stay], to, local),
        ]

    def add(self, made, came, sp):
        if self.hop == "yg":
            wide = self.shape[-1]
            at = pl.ds(pl.multiple_of((1 - sp) * wide, 128), wide)
            made[(slice(None),) * (len(self.shape) - 1) + (at,)] = came[...]
        else:
            made[...] += came[...]


class Flow:
    def __init__(self, array, shape, hops, dims, cols=None):
        self.array, self.shape, self.dims, self.cols = array, tuple(shape), dims, cols
        self.hops = list(hops)

    def step(self):
        part = Part(self.hops.pop(0), self.shape, self.dims, self.cols)
        self.shape, self.dims, self.cols = part.after, part.left, None
        return part


class Window:
    def __init__(self, start, stop):
        self.start, self.stop = start, stop
        self.parts, self.sources, self.keeps = [], [], []


def plan(schedule):
    windows, arrays, latest = [], [], {}
    for n, (flows, start, stop) in enumerate(schedule):
        window = Window(start, stop)
        for i, flow in enumerate(flows):
            if flow in latest:
                source = ("part",) + latest[flow]
                before = windows[latest[flow][0]]
                before.keeps[latest[flow][1]] = False
            elif isinstance(flow.array, tuple):
                source = flow.array
            else:
                known = [k for k, a in enumerate(arrays) if a is flow.array]
                if not known:
                    arrays.append(flow.array)
                source = ("in", known[0] if known else len(arrays) - 1)
            window.parts.append(flow.step())
            window.sources.append(source)
            window.keeps.append(True)
            latest[flow] = (n, i)
        windows.append(window)
    return windows, arrays, latest


def carrying(body, own, windows, arrays, grid, also):
    ins, outs, held = own

    def kernel(*refs):
        refs = list(refs)

        def take(n):
            got = refs[:n]
            del refs[:n]
            return got

        my_in, arr = take(ins), take(arrays)
        my_out = take(outs)
        given = [[take(1)[0] if k else None for k in w.keeps] for w in windows]
        my_held = take(held)
        made, came = [], []
        for w, g in zip(windows, given):
            made.append([ref if ref is not None else take(1)[0] for ref in g])
            came.append(take(len(w.parts)))
        mine = my_in + my_out + my_held
        step = pl.program_id(0)
        hops = [q.hop for w in windows for q in w.parts] + list(also)
        if hops:
            at_dp, sp = place(), lax.axis_index("sp")
            pl.when(step == 0)(lambda: greet(hops, at_dp))
        if windows:
            send, recv, local = refs
        copies, base = [], 0
        for w, m, c in zip(windows, made, came):
            now = []
            for i, q in enumerate(w.parts):
                kind = w.sources[i]
                if kind[0] == "in":
                    src = arr[kind[1]]
                elif kind[0] == "ref":
                    src = mine[kind[1]]
                    src = src.at[kind[2]] if len(kind) > 2 else src
                else:
                    src = made[kind[1]][kind[2]]
                now += q.copies(
                    src, m[i], c[i], send.at[base], recv.at[base], local.at[base], at_dp, sp
                )
                base += 1
            copies.append(now)

        def phase(number):
            for n, w in enumerate(windows):
                if w.stop == number:
                    for copy in copies[n]:
                        copy.wait()
                    for q, m, c in zip(w.parts, made[n], came[n]):
                        q.add(m, c, sp)
            for n, w in enumerate(windows):
                if w.start == number:
                    for copy in copies[n]:
                        copy.start()

        used = sorted({w.start for w in windows} | {w.stop for w in windows})
        for number in used:
            if number < grid:
                pl.when(step == number)(functools.partial(phase, number))
        body(*mine)
        for number in used:
            if number >= grid:
                pl.when(step == grid - 1)(functools.partial(phase, number))

    return kernel


def run(
    body, name, grid, ins, in_specs, outs, out_specs, held=(), schedule=(), collective=None,
    flops=0, moved=0, also=(),
):
    in_specs, outs, out_specs, held = list(in_specs), list(outs), list(out_specs), list(held)
    windows, arrays, latest = plan(schedule)
    own = len(outs)
    kernel = carrying(body, (len(ins), own, len(held)), windows, len(arrays), grid, also)
    in_specs += [pl.BlockSpec(memory_space=pl.ANY)] * len(arrays)
    order, count = [], 0
    for n, w in enumerate(windows):
        for i, (q, k) in enumerate(zip(w.parts, w.keeps)):
            if k:
                outs.append(jax.ShapeDtypeStruct(q.after, BF16))
                out_specs.append(whole(q.after))
                order.append((n, i))
            else:
                held.append(pltpu.VMEM(q.after, BF16))
        held += [pltpu.VMEM(q.came, BF16) for q in w.parts]
        count += len(w.parts)
    if windows:
        held += [pltpu.SemaphoreType.DMA((count,))] * 3
    results = pl.pallas_call(
        kernel,
        grid=(grid,),
        in_specs=in_specs,
        out_specs=out_specs,
        out_shape=outs,
        scratch_shapes=held,
        compiler_params=params(collective if windows or also else None),
        cost_estimate=cost(flops, moved),
        name=name,
    )(*ins, *arrays)
    for flow, where in latest.items():
        flow.array = results[own + order.index(where)]
    return results[:own]


VIA_X = ("x", "z1", "z2", "y")
VIA_Y = ("yr", "x", "z1", "z2", "yg")
VIA_Z = ("z1", "yr", "x", "z2", "yg")
BLOCK = ("z2", "z1", "x", "core")


def code_of(docs_ref):
    row = lax.broadcasted_iota(jnp.int32, (128, docs_ref.shape[1]), 0)
    return jnp.transpose(jnp.where(docs_ref[...] == row, 1.0, 0.0)).astype(BF16)


def project_own_kernel(x_ref, m_ref, td_ref, md_ref, wx_ref, wm_ref, b_ref, qkv_ref, mkv_ref, to_ref, mo_ref):
    step = pl.program_id(0)

    @pl.when(step == 0)
    def _():
        to_ref[...] = code_of(td_ref)
        mo_ref[...] = code_of(md_ref)

    @pl.when(step < 3)
    def _():
        bias = jnp.where(step == 0, b_ref[0:1], 0.0) + jnp.where(step == 2, b_ref[1:2], 0.0)
        qkv_ref[...] = (nn(x_ref[...], wx_ref[...]) + bias).astype(BF16)

    @pl.when(step >= 3)
    def _():
        bias = jnp.where(step == 4, b_ref[2:3], 0.0)
        mkv_ref[...] = (nn(m_ref[...], wm_ref[...]) + bias).astype(BF16)


def project_own(x, mem, td, md, wx, wm, biases):
    rows, width = x.shape
    code = jax.ShapeDtypeStruct((rows, 128), BF16)
    return pl.pallas_call(
        project_own_kernel,
        grid=(5,),
        in_specs=[
            whole((rows, width)), whole((rows, width)), whole((1, rows)), whole((1, rows)),
            pl.BlockSpec((width, width), lambda s: (0, jnp.minimum(s, 2))),
            pl.BlockSpec((width, width), lambda s: (0, jnp.maximum(s - 3, 0))),
            whole(biases.shape),
        ],
        out_specs=[
            pl.BlockSpec((rows, width), lambda s: (0, jnp.minimum(s, 2))),
            pl.BlockSpec((rows, width), lambda s: (0, jnp.maximum(s - 3, 0))),
            whole((rows, 128)), whole((rows, 128)),
        ],
        out_shape=[
            jax.ShapeDtypeStruct((rows, 3 * width), BF16), jax.ShapeDtypeStruct((rows, 2 * width), BF16), code, code,
        ],
        compiler_params=params(),
        cost_estimate=cost(10 * rows * width * width, 20 * width * width),
        name="project_own",
    )(x, mem, td, md, wx, wm, biases)


def project_other_kernel(x_ref, m_ref, td_ref, md_ref, wx_ref, b_ref, after_ref, kvo_ref, mem_ref, tt_ref, mt_ref):
    step = pl.program_id(0)

    @pl.when(step == 0)
    def _():
        mem_ref[...] = m_ref[...]
        tt_ref[...] = code_of(td_ref)
        mt_ref[...] = code_of(md_ref)

    @pl.when(lax.axis_index("sp") == 1)
    def _():
        bias = jnp.where(step == 1, b_ref[1:2], 0.0)
        kvo_ref[...] = (nn(x_ref[...], wx_ref[...]) + bias).astype(BF16)

    @pl.when(lax.axis_index("sp") == 0)
    def _():
        kvo_ref[...] = jnp.zeros(kvo_ref.shape, BF16)


def project_other(x, mem, td, md, wx, biases, after):
    rows, width = x.shape
    code = jax.ShapeDtypeStruct((rows, 128), BF16)
    return pl.pallas_call(
        project_other_kernel,
        grid=(2,),
        in_specs=[
            whole((rows, width)), whole((rows, width)), whole((1, rows)), whole((1, rows)),
            pl.BlockSpec((width, width), lambda s: (0, s + 1)),
            whole(biases.shape),
            pl.BlockSpec(memory_space=pl.ANY),
        ],
        out_specs=[
            pl.BlockSpec((rows, width), lambda s: (0, s)),
            whole((rows, width)), whole((rows, 128)), whole((rows, 128)),
        ],
        out_shape=[
            jax.ShapeDtypeStruct((rows, 2 * width), BF16), jax.ShapeDtypeStruct((rows, width), BF16), code, code,
        ],
        compiler_params=params(),
        cost_estimate=cost(4 * rows * width * width, 10 * width * width),
        name="project_other",
    )(x, mem, td, md, wx, biases, after)


def project_memory_kernel(x_ref, w_ref, b_ref, o_ref):
    bias = jnp.where(pl.program_id(0) == 1, b_ref[2:3], 0.0)
    o_ref[...] = (nn(x_ref[...], w_ref[...]) + bias).astype(BF16)


def project_memory(x, w, biases):
    rows, width = x.shape
    return pl.pallas_call(
        project_memory_kernel,
        grid=(2,),
        in_specs=[
            whole((rows, width)),
            pl.BlockSpec((width, width), lambda j: (0, j)),
            whole(biases.shape),
        ],
        out_specs=pl.BlockSpec((rows, width), lambda j: (0, j)),
        out_shape=jax.ShapeDtypeStruct((rows, 2 * width), BF16),
        compiler_params=params(),
        cost_estimate=cost(4 * rows * width * width, 4 * width * (width + rows)),
        name="project_memory",
    )(x, w, biases)


def head_masks(dtype):
    lane = lax.broadcasted_iota(jnp.int32, (1, PAIR), 1)
    low = jnp.where(lane < HD, 1.0, 0.0)
    return low.astype(dtype), (1.0 - low).astype(dtype)


def query_code(code):
    lane = lax.broadcasted_iota(jnp.int32, code.shape, 1)
    return jnp.where(lane < 4, (code.astype(F32) - 1.0) * FAR, 0.0).astype(BF16)


def softmax_pieces(scores, values):
    peak = functools.reduce(jnp.maximum, [jnp.max(s, axis=-1, keepdims=True) for s in scores])
    expd = [jnp.exp(s - peak) for s in scores]
    norm = sum(jnp.sum(e, axis=-1, keepdims=True) for e in expd)
    out = sum(nn(e.astype(BF16), v) for e, v in zip(expd, values))
    return out / norm, peak + jnp.log(norm)


def self_pieces(block, size, both, own, other):
    pieces = []
    if both:
        pieces.append((other, False))
    if block:
        pieces.append((own[: block * size], False))
    pieces.append((own[block * size : (block + 1) * size], True))
    return pieces


def store_lse(lse_ref, block, size, low, high):
    lane = lax.broadcasted_iota(jnp.int32, (size, PAIR), 1)
    both = jnp.where(lane == 0, low, high)
    lse_ref[:, block * size : (block + 1) * size] = jnp.transpose(both)[:8]


def self_forward_kernel(size, q_ref, k_ref, v_ref, ko_ref, vo_ref, own_ref, oth_ref, o_ref, lse_ref):
    second = lax.axis_index("sp") == 1
    rows = q_ref.shape[0]
    masks = head_masks(BF16)
    outs = head_masks(F32)

    def run(both):
        qcode = query_code(own_ref[...])
        own = jnp.concatenate([k_ref[...], own_ref[...]], axis=1)
        oth = jnp.concatenate([ko_ref[...], oth_ref[...]], axis=1) if both else None
        vown = v_ref[...]
        voth = vo_ref[...] if both else None
        for block in range(rows // size):
            at = slice(block * size, (block + 1) * size)
            lses, result = [], 0.0
            for mask, keep in zip(masks, outs):
                q = jnp.concatenate([q_ref[at] * (mask * BF16(HD**-0.5)), qcode[at]], axis=1)
                scores = []
                for keys, diagonal in self_pieces(block, size, both, own, oth):
                    s = nt(q, keys)
                    if diagonal:
                        row = lax.broadcasted_iota(jnp.int32, s.shape, 0)
                        col = lax.broadcasted_iota(jnp.int32, s.shape, 1)
                        s = jnp.where(row >= col, s, -FAR)
                    scores.append(s)
                values = [v for v, _ in self_pieces(block, size, both, vown, voth)]
                out, lse = softmax_pieces(scores, values)
                result = result + out * keep
                lses.append(lse)
            o_ref[at] = result.astype(BF16)
            store_lse(lse_ref, block, size, *lses)

    pl.when(second)(lambda: run(True))
    pl.when(jnp.logical_not(second))(lambda: run(False))


def pair_spec(rows, offset):
    return pl.BlockSpec((rows, PAIR), lambda p: (0, p + offset))


def whole(shape):
    return pl.BlockSpec(shape, lambda *_: (0,) * len(shape))


def self_forward(qkv, kvo, own, oth):
    rows = qkv.shape[0]
    width = qkv.shape[1] // 3
    pairs = width // PAIR
    return pl.pallas_call(
        functools.partial(self_forward_kernel, 256),
        grid=(pairs,),
        in_specs=[
            pair_spec(rows, 0),
            pair_spec(rows, pairs),
            pair_spec(rows, 2 * pairs),
            pair_spec(rows, 0),
            pair_spec(rows, pairs),
            whole((rows, 128)),
            whole((rows, 128)),
        ],
        out_specs=[pair_spec(rows, 0), pl.BlockSpec((8, rows), lambda p: (p, 0))],
        out_shape=[
            jax.ShapeDtypeStruct((rows, width), BF16),
            jax.ShapeDtypeStruct((8 * pairs, rows), F32),
        ],
        compiler_params=params(),
        cost_estimate=cost(16 * rows * rows * width, 16 * rows * width),
        name="self_forward",
    )(qkv, qkv, qkv, kvo, kvo, own, oth)


def cross_forward_kernel(size, q_ref, k_ref, v_ref, ko_ref, vo_ref, t_ref, own_ref, oth_ref, o_ref, lse_ref):
    rows = q_ref.shape[0]
    masks = head_masks(BF16)
    outs = head_masks(F32)
    qcode = query_code(t_ref[...])
    keys = [
        jnp.concatenate([k_ref[...], own_ref[...]], axis=1),
        jnp.concatenate([ko_ref[...], oth_ref[...]], axis=1),
    ]
    values = [v_ref[...], vo_ref[...]]
    for block in range(rows // size):
        at = slice(block * size, (block + 1) * size)
        lses, result = [], 0.0
        for mask, keep in zip(masks, outs):
            q = jnp.concatenate([q_ref[at] * (mask * BF16(HD**-0.5)), qcode[at]], axis=1)
            out, lse = softmax_pieces([nt(q, k) for k in keys], values)
            result = result + out * keep
            lses.append(lse)
        o_ref[at] = result.astype(BF16)
        store_lse(lse_ref, block, size, *lses)


def cross_forward(cq, kv, kvo, t, own, oth):
    rows, width = cq.shape
    pairs = width // PAIR
    return pl.pallas_call(
        functools.partial(cross_forward_kernel, 256),
        grid=(pairs,),
        in_specs=[
            pair_spec(rows, 0),
            pair_spec(rows, 0),
            pair_spec(rows, pairs),
            pair_spec(rows, 0),
            pair_spec(rows, pairs),
            whole((rows, 128)),
            whole((rows, 128)),
            whole((rows, 128)),
        ],
        out_specs=[pair_spec(rows, 0), pl.BlockSpec((8, rows), lambda p: (p, 0))],
        out_shape=[
            jax.ShapeDtypeStruct((rows, width), BF16),
            jax.ShapeDtypeStruct((8 * pairs, rows), F32),
        ],
        compiler_params=params(),
        cost_estimate=cost(24 * rows * rows * width, 16 * rows * width),
        name="cross_forward",
    )(cq, kv, kv, kvo, kvo, t, own, oth)


def delta_rows(g, o):
    prod = g.astype(F32) * o.astype(F32)
    upper = prod.astype(BF16)
    lower = (prod - upper.astype(F32)).astype(BF16)
    row = lax.broadcasted_iota(jnp.int32, (8, PAIR), 0)
    lane = lax.broadcasted_iota(jnp.int32, (8, PAIR), 1)
    pick = jnp.where(row == lane // HD, 1.0, 0.0).astype(BF16)
    return nt(pick, upper) + nt(pick, lower)


def back_piece(keys, values, q, g, lse, delta, causal):
    s = nt(keys, q)
    if causal:
        row = lax.broadcasted_iota(jnp.int32, s.shape, 0)
        col = lax.broadcasted_iota(jnp.int32, s.shape, 1)
        s = jnp.where(row <= col, s, -FAR)
    p = jnp.exp(s - lse)
    ds = p * (nt(values, g) - delta)
    return p.astype(BF16), ds.astype(BF16)


def cross_backward_kernel(
    size, q_ref, k_ref, v_ref, ko_ref, vo_ref, g_ref, o_ref, lse_ref, t_ref, own_ref, oth_ref,
    m_ref, mo_ref, wk_ref, wv_ref,
    dq_ref, dm_ref, dmo_ref, gk_ref, gv_ref, gb_ref, dm_acc, dmo_acc,
):
    step = pl.program_id(0)
    rows = q_ref.shape[0]
    masks = head_masks(BF16)
    scale = BF16(HD**-0.5)
    qcode = query_code(t_ref[...])
    delta = delta_rows(g_ref[...], o_ref[...])
    lse = lse_ref[...]
    halves = [(k_ref, v_ref, own_ref, m_ref, dm_acc), (ko_ref, vo_ref, oth_ref, mo_ref, dmo_acc)]
    dq = [0.0] * (rows // size)
    gk = gv = gb = 0.0
    for kr, vr, code, mem, acc in halves:
        keys = jnp.concatenate([kr[...], code[...]], axis=1)
        values = vr[...]
        dk = dv = 0.0
        for block in range(rows // size):
            at = slice(block * size, (block + 1) * size)
            for head, mask in enumerate(masks):
                qm = q_ref[at] * (mask * scale)
                gm = g_ref[at] * mask
                q = jnp.concatenate([qm, qcode[at]], axis=1)
                p, ds = back_piece(
                    keys, values, q, gm, lse[head : head + 1, at], delta[head : head + 1, at], False
                )
                dk = dk + nn(ds, qm)
                dv = dv + nn(p, gm)
                dq[block] = dq[block] + tn(ds, kr[...] * (mask * scale))
        both = jnp.concatenate([dk.astype(BF16), dv.astype(BF16)], axis=1)
        grad = tn(mem[...], both)
        gk, gv = gk + grad[:, :PAIR], gv + grad[:, PAIR:]
        gb = gb + total(both[:, PAIR:])
        dm = nt(both, jnp.concatenate([wk_ref[...], wv_ref[...]], axis=1))

        @pl.when(step == 0)
        def _():
            acc[...] = dm

        @pl.when(step > 0)
        def _():
            acc[...] += dm
    for block in range(rows // size):
        dq_ref[block * size : (block + 1) * size] = dq[block].astype(BF16)
    gk_ref[...] = gk.astype(BF16)
    gv_ref[...] = gv.astype(BF16)
    gb_ref[...] = gb

    @pl.when(step == pl.num_programs(0) - 1)
    def _():
        dm_ref[...] = dm_acc[...]
        dmo_ref[...] = dmo_acc[...].astype(BF16)


def cross_backward(cq, kv, kvo, g, o, lse, t, own, oth, m, mo, w, schedule):
    rows, width = cq.shape
    pairs = width // PAIR
    flat = jax.ShapeDtypeStruct((rows, width), BF16)
    square = jax.ShapeDtypeStruct((width, width), BF16)
    return run(
        functools.partial(cross_backward_kernel, 256), "cross_backward", pairs,
        (cq, kv, kv, kvo, kvo, g, o, lse, t, own, oth, m, mo, w, w),
        [
            pair_spec(rows, 0),
            pair_spec(rows, 0),
            pair_spec(rows, pairs),
            pair_spec(rows, 0),
            pair_spec(rows, pairs),
            pair_spec(rows, 0),
            pair_spec(rows, 0),
            pl.BlockSpec((8, rows), lambda p: (p, 0)),
            whole((rows, 128)),
            whole((rows, 128)),
            whole((rows, 128)),
            whole((rows, width)),
            whole((rows, width)),
            pair_spec(width, 0),
            pair_spec(width, pairs),
        ],
        [flat, jax.ShapeDtypeStruct((rows, width), F32), flat, square, square, jax.ShapeDtypeStruct((1, width), F32)],
        [pair_spec(rows, 0)] + [whole((rows, width))] * 2 + [pair_spec(width, 0)] * 2 + [pair_spec(1, 0)],
        [pltpu.VMEM((rows, width), F32)] * 2,
        schedule, 3,
        64 * rows * rows * width + 16 * rows * width * width, 24 * rows * width,
    )


def self_backward_kernel(
    size, q_ref, k_ref, v_ref, ko_ref, vo_ref, g_ref, o_ref, lse_ref, own_ref, oth_ref,
    dq_ref, dk_ref, dv_ref, dko_ref, dvo_ref,
):
    second = lax.axis_index("sp") == 1
    rows = q_ref.shape[0]
    masks = head_masks(BF16)
    scale = BF16(HD**-0.5)

    def run(both):
        qcode = query_code(own_ref[...])
        delta = delta_rows(g_ref[...], o_ref[...])
        lse = lse_ref[...]
        count = rows // size
        dk, dv = [0.0] * count, [0.0] * count
        dko = dvo = 0.0
        for block in range(count):
            at = slice(block * size, (block + 1) * size)
            dq = 0.0
            for head, mask in enumerate(masks):
                qm = q_ref[at] * (mask * scale)
                gm = g_ref[at] * mask
                q = jnp.concatenate([qm, qcode[at]], axis=1)
                rest = (q, gm, lse[head : head + 1, at], delta[head : head + 1, at])
                for part in range(block + 1):
                    of = slice(part * size, (part + 1) * size)
                    keys = jnp.concatenate([k_ref[of], own_ref[of]], axis=1)
                    p, ds = back_piece(keys, v_ref[of], *rest, part == block)
                    dk[part] = dk[part] + nn(ds, qm)
                    dv[part] = dv[part] + nn(p, gm)
                    dq = dq + tn(ds, k_ref[of] * (mask * scale))
                if both:
                    keys = jnp.concatenate([ko_ref[...], oth_ref[...]], axis=1)
                    p, ds = back_piece(keys, vo_ref[...], *rest, False)
                    dko = dko + nn(ds, qm)
                    dvo = dvo + nn(p, gm)
                    dq = dq + tn(ds, ko_ref[...] * (mask * scale))
            dq_ref[at] = dq.astype(BF16)
        for part in range(count):
            of = slice(part * size, (part + 1) * size)
            dk_ref[of] = dk[part].astype(BF16)
            dv_ref[of] = dv[part].astype(BF16)
        if both:
            dko_ref[...] = dko.astype(BF16)
            dvo_ref[...] = dvo.astype(BF16)
        else:
            dko_ref[...] = jnp.zeros(dko_ref.shape, BF16)
            dvo_ref[...] = jnp.zeros(dvo_ref.shape, BF16)

    pl.when(second)(lambda: run(True))
    pl.when(jnp.logical_not(second))(lambda: run(False))


def self_backward(qkv, kvo, g, o, lse, own, oth, schedule):
    rows = qkv.shape[0]
    width = qkv.shape[1] // 3
    pairs = width // PAIR
    flat = jax.ShapeDtypeStruct((rows, width), BF16)
    return run(
        functools.partial(self_backward_kernel, 256), "self_backward", pairs,
        (qkv, qkv, qkv, kvo, kvo, g, o, lse, own, oth),
        [
            pair_spec(rows, 0),
            pair_spec(rows, pairs),
            pair_spec(rows, 2 * pairs),
            pair_spec(rows, 0),
            pair_spec(rows, pairs),
            pair_spec(rows, 0),
            pair_spec(rows, 0),
            pl.BlockSpec((8, rows), lambda p: (p, 0)),
            whole((rows, 128)),
            whole((rows, 128)),
        ],
        [flat] * 5,
        [pair_spec(rows, 0)] * 5,
        (), schedule, 5,
        48 * rows * rows * width, 24 * rows * width,
    )


def first_norm_kernel(x_ref, ctx_ref, wo_ref, wq_ref, b_ref, h_ref, cq_ref):
    h = x_ref[...].astype(F32) + nn(ctx_ref[...], wo_ref[...]) + b_ref[3:4]
    h_ref[...] = h
    n, _ = normed(h)
    a = (n * b_ref[4:5] + b_ref[5:6]).astype(BF16)
    cq_ref[...] = (nn(a, wq_ref[...]) + b_ref[6:7]).astype(BF16)


def first_norm(x, ctx, wo, wq, biases):
    rows, width = x.shape
    return pl.pallas_call(
        first_norm_kernel,
        out_shape=[
            jax.ShapeDtypeStruct((rows, width), F32),
            jax.ShapeDtypeStruct((rows, width), BF16),
        ],
        compiler_params=params(),
        cost_estimate=cost(4 * rows * width * width, 4 * width * width + 10 * rows * width),
        name="first_norm",
    )(x, ctx, wo, wq, biases)


def feed_kernel(
    count, comm, h1_ref, cc_ref, ct_ref, wco_ref, b_ref, wi_ref, wo_ref,
    out_ref, dh2_ref, dcc_ref, gco_ref, gwi_ref, gwo_ref, small_ref, gib_ref,
    hid_ref, slope_ref, n2_ref, r2_ref, a2b_ref, acc_ref, df_ref, *refs,
):
    step = pl.program_id(0)
    width = acc_ref.shape[1]

    if comm:
        mi_ref, mo_ref, ci_ref, co_ref, send_ref, recv_ref = refs
        _, c, _, _ = place()

        def chunk_copies(j):
            at = pl.ds(pl.multiple_of(j * width, width), width)
            return [
                remote(
                    mi_ref.at[:, 1 - c, :, at], ci_ref.at[:, :, at], send_ref.at[0, j], recv_ref.at[0, j], "core"
                ),
                remote(mo_ref.at[j, :, 1 - c], co_ref.at[j], send_ref.at[1, j], recv_ref.at[1, j], "core"),
            ]

    @pl.when(step == 0)
    def _():
        if comm:
            greet(["core"])
        n1, _ = normed(h1_ref[...])
        a1 = n1 * b_ref[4:5] + b_ref[5:6]
        h2 = a1 + nn(cc_ref[...], wco_ref[...]) + b_ref[7:8]
        n2, r2 = normed(h2)
        n2_ref[...] = n2
        r2_ref[...] = jnp.broadcast_to(r2, r2_ref.shape)
        a2 = n2 * b_ref[8:9] + b_ref[9:10]
        a2b_ref[...] = a2.astype(BF16)
        acc_ref[...] = a2 + b_ref[10:11]

    @pl.when(step < count)
    def _():
        u = nn(a2b_ref[...], wi_ref[...]) + b_ref[pl.ds(13 + step, 1)]
        cumul = 0.5 * (1.0 + lax.erf(u * 0.7071067811865476))
        density = jnp.exp(-0.5 * u * u) * 0.3989422804014327
        hid = (u * cumul).astype(BF16)
        hid_ref[step] = hid
        slope_ref[step] = cumul + u * density
        acc_ref[...] += nn(hid, wo_ref[...])

    @pl.when(step == count - 1)
    def _():
        n3, r3 = normed(acc_ref[...])
        gain = b_ref[11:12]
        out_ref[...] = (n3 * gain + b_ref[12:13]).astype(BF16)
        e = ct_ref[...].astype(F32)
        d3 = norm_back(e, n3, r3, gain)
        df = d3.astype(BF16)
        df_ref[...] = df
        acc_ref[...] = d3
        small_ref[0:1] = total(e * n3)
        small_ref[1:2] = total(e)
        small_ref[2:3] = total(df)

    @pl.when(jnp.logical_and(step >= count, step < 2 * count))
    def _():
        j = step - count
        df = df_ref[...]
        du = (nt(df, wo_ref[...]) * slope_ref[j]).astype(BF16)
        gib_ref[...] = total(du)
        acc_ref[...] += nt(du, wi_ref[...])
        go = tn(hid_ref[j], df).astype(BF16)
        gi = tn(a2b_ref[...], du).astype(BF16)
        if comm:
            at = pl.ds(pl.multiple_of(j * width, width), width)
            mo_ref[j] = go.reshape(mo_ref.shape[1:])
            mi_ref[:, :, :, at] = gi.reshape(mi_ref.shape[:3] + (width,))
            for copy in chunk_copies(j):
                copy.start()
        else:
            gwo_ref[...] = go
            gwi_ref[...] = gi

    @pl.when(step == 2 * count)
    def _():
        d2 = acc_ref[...]
        n2 = n2_ref[...]
        dh2 = norm_back(d2, n2, r2_ref[:, :1], b_ref[8:9])
        dh2_ref[...] = dh2
        dco = dh2.astype(BF16)
        dcc_ref[...] = nt(dco, wco_ref[...]).astype(BF16)
        gco_ref[...] = tn(cc_ref[...], dco).astype(BF16)
        small_ref[3:4] = total(d2 * n2)
        small_ref[4:5] = total(d2)
        small_ref[5:6] = total(dco)
        small_ref[6:8] = jnp.zeros((2, d2.shape[1]), F32)

    if comm:

        @pl.when(step > count)
        def _():
            j = step - count - 1
            at = pl.ds(pl.multiple_of(j * width, width), width)
            for copy in chunk_copies(j):
                copy.wait()
            gwi_ref[...] = mi_ref[:, c, :, at] + ci_ref[:, :, at]
            gwo_ref[0] = mo_ref[j, :, c] + co_ref[j]


def feed(size, comm, h1, cc, ct, wco, biases, wi, wo):
    rows, width = h1.shape
    wide = wi.shape[1]
    chunk = width
    count = wide // chunk

    def weight(s):
        return jnp.where(s < count, s, jnp.minimum(s - count, count - 1))

    def early(s):
        return jnp.clip(s - count, 0, count - 1)

    def late(s):
        return jnp.clip(s - count - 1, 0, count - 1)

    flat = whole((rows, width))
    square = whole((width, width))
    scratch = [
        pltpu.VMEM((count, rows, chunk), BF16),
        pltpu.VMEM((count, rows, chunk), F32),
        pltpu.VMEM((rows, width), F32),
        pltpu.VMEM((rows, 128), F32),
        pltpu.VMEM((rows, width), BF16),
        pltpu.VMEM((rows, width), F32),
        pltpu.VMEM((rows, width), BF16),
    ]
    if comm:
        narrow, broad = width // size, wide // size
        grad_specs = [
            pl.BlockSpec((size // 2, narrow, chunk), lambda s: (0, 0, late(s))),
            pl.BlockSpec((1, 2, broad, width), lambda s: (late(s), 0, 0, 0)),
        ]
        grad_shapes = [(size // 2, narrow, wide), (count, 2, broad, width)]
        scratch += [
            pltpu.VMEM((size // 2, 2, narrow, wide), BF16),
            pltpu.VMEM((count, 2, 2, broad, width), BF16),
            pltpu.VMEM((size // 2, narrow, wide), BF16),
            pltpu.VMEM((count, 2, broad, width), BF16),
            pltpu.SemaphoreType.DMA((2, count)),
            pltpu.SemaphoreType.DMA((2, count)),
        ]
    else:
        grad_specs = [
            pl.BlockSpec((width, chunk), lambda s: (0, early(s))),
            pl.BlockSpec((chunk, width), lambda s: (early(s), 0)),
        ]
        grad_shapes = [(width, wide), (wide, width)]
    return pl.pallas_call(
        functools.partial(feed_kernel, count, comm),
        grid=(2 * count + 1,),
        in_specs=[
            flat, flat, flat, square, whole(biases.shape),
            pl.BlockSpec((width, chunk), lambda s: (0, weight(s))),
            pl.BlockSpec((chunk, width), lambda s: (weight(s), 0)),
        ],
        out_specs=[flat, flat, flat, square]
        + grad_specs
        + [whole((8, width)), pl.BlockSpec((1, chunk), lambda s: (0, early(s)))],
        out_shape=[
            jax.ShapeDtypeStruct((rows, width), BF16),
            jax.ShapeDtypeStruct((rows, width), F32),
            jax.ShapeDtypeStruct((rows, width), BF16),
            jax.ShapeDtypeStruct((width, width), BF16),
        ]
        + [jax.ShapeDtypeStruct(a, BF16) for a in grad_shapes]
        + [
            jax.ShapeDtypeStruct((8, width), F32),
            jax.ShapeDtypeStruct((1, wide), F32),
        ],
        scratch_shapes=scratch,
        compiler_params=params(2 if comm else None),
        cost_estimate=cost(
            12 * rows * width * wide + 6 * rows * width * width, 12 * width * wide + 16 * rows * width
        ),
        name="feed",
    )(h1, cc, ct, wco, biases, wi, wo)


def first_back_kernel(
    dcq_ref, dh2_ref, h1_ref, ctx_ref, wcq_ref, wso_ref, b_ref,
    dh1_ref, dsc_ref, gcq_ref, gso_ref, small_ref,
):
    gain = b_ref[4:5]
    n1, r1 = normed(h1_ref[...])
    a1b = (n1 * gain + b_ref[5:6]).astype(BF16)
    dcq = dcq_ref[...]
    d1 = dh2_ref[...] + nt(dcq, wcq_ref[...])
    dh1 = norm_back(d1, n1, r1, gain)
    dh1_ref[...] = dh1
    dso = dh1.astype(BF16)
    dsc_ref[...] = nt(dso, wso_ref[...]).astype(BF16)
    gcq_ref[...] = tn(a1b, dcq).astype(BF16)
    gso_ref[...] = tn(ctx_ref[...], dso).astype(BF16)
    small_ref[0:1] = total(dcq)
    small_ref[1:2] = total(d1 * n1)
    small_ref[2:3] = total(d1)
    small_ref[3:4] = total(dso)
    small_ref[4:8] = jnp.zeros((4, dh1.shape[1]), F32)


def first_back(dcq, dh2, h1, ctx, wcq, wso, biases, schedule):
    rows, width = dcq.shape
    flat, square = whole((rows, width)), whole((width, width))
    return run(
        first_back_kernel, "first_back", 1,
        (dcq, dh2, h1, ctx, wcq, wso, biases),
        [flat, flat, flat, flat, square, square, whole(biases.shape)],
        [
            jax.ShapeDtypeStruct((rows, width), F32),
            jax.ShapeDtypeStruct((rows, width), BF16),
            jax.ShapeDtypeStruct((width, width), BF16),
            jax.ShapeDtypeStruct((width, width), BF16),
            jax.ShapeDtypeStruct((8, width), F32),
        ],
        [flat, flat, square, square, whole((8, width))],
        (), schedule, 4,
        8 * rows * width * width, 8 * width * width + 18 * rows * width,
    )


def input_back_kernel(
    x_ref, xo_ref, dq_ref, dk_ref, dv_ref, dko_ref, dvo_ref, w_ref, dh1_ref, sa_ref, sb_ref, sc_ref, sd_ref,
    dx_ref, g_ref, sm_ref, dxo_ref, came_ref, turn_ref, send_ref, recv_ref,
):
    step = pl.program_id(0)
    sp = lax.axis_index("sp")
    width = x_ref.shape[1]
    over = remote(dxo_ref, came_ref, send_ref.at[0], recv_ref.at[0], "y")

    @pl.when(step == 0)
    def _():
        @pl.when(sp == 1)
        def _():
            dxo = nt(dko_ref[...], w_ref[:, width : 2 * width]) + nt(dvo_ref[...], w_ref[:, 2 * width :])
            dxo_ref[...] = dxo.astype(BF16)
            over.start()

        g_ref[0] = tn(x_ref[...], dq_ref[...]).astype(BF16).reshape(g_ref.shape[1:])
        turn_ref[...] = jnp.zeros(turn_ref.shape, F32)
        turn_ref[0:8] = sa_ref[...]
        turn_ref[8:16] = sb_ref[...]
        turn_ref[16:17] = sc_ref[...]
        turn_ref[17:21] = sd_ref[...]
        turn_ref[21:22] = total(dq_ref[...])

    for n, (own, oth) in enumerate(((dk_ref, dko_ref), (dv_ref, dvo_ref)), start=1):

        @pl.when(jnp.logical_and(step == n, sp == 1))
        def _():
            grad = tn(x_ref[...], own[...]) + tn(xo_ref[...], oth[...])
            g_ref[n] = grad.astype(BF16).reshape(g_ref.shape[1:])

        @pl.when(jnp.logical_and(step == n, sp == 0))
        def _():
            g_ref[n] = tn(x_ref[...], own[...]).astype(BF16).reshape(g_ref.shape[1:])

    @pl.when(step == 2)
    def _():
        sums = total(dv_ref[...])
        turn_ref[22:23] = jnp.where(sp == 1, sums + total(dvo_ref[...]), sums)
        sm_ref[...] = jnp.transpose(turn_ref[...]).astype(BF16).reshape(sm_ref.shape)

    @pl.when(step == 3)
    def _():
        dx = (
            dh1_ref[...]
            + nt(dq_ref[...], w_ref[:, :width])
            + nt(dk_ref[...], w_ref[:, width : 2 * width])
            + nt(dv_ref[...], w_ref[:, 2 * width :])
        )

        @pl.when(sp == 0)
        def _():
            over.wait_recv()
            dx_ref[...] = (dx + came_ref[...].astype(F32)).astype(BF16)

        @pl.when(sp == 1)
        def _():
            over.wait_send()
            dx_ref[...] = dx.astype(BF16)


def input_back(block, x, xo, dq, dk, dv, dko, dvo, w, dh1, small, schedule):
    rows, width = x.shape
    flat = whole((rows, width))
    ins = (x, xo, dq, dk, dv, dko, dvo, w, dh1) + tuple(small)
    made = [(3,) + block + (width,), block + (128,)]
    outs = [jax.ShapeDtypeStruct((rows, width), BF16)]
    specs = [flat]
    held = []
    if schedule:
        held += [pltpu.VMEM(a, BF16) for a in made]
    else:
        outs += [jax.ShapeDtypeStruct(a, BF16) for a in made]
        specs += [whole(a) for a in made]
    held += [
        pltpu.VMEM((rows, width), BF16),
        pltpu.VMEM((rows, width), BF16),
        pltpu.VMEM((128, width), F32),
        pltpu.SemaphoreType.DMA((1,)),
        pltpu.SemaphoreType.DMA((1,)),
    ]
    return run(
        input_back_kernel, "input_back", 4, ins, [whole(a.shape) for a in ins], outs, specs, held,
        schedule, 6, 20 * rows * width * width, 12 * width * width + 28 * rows * width, ("y",),
    )


def outputs_kernel(places, count, *refs):
    pieces, rest = refs[:count], refs[count:]
    lines_ref, out_ref, dx_ref, dm_ref, dmi_ref = rest[:5]
    outs = rest[5:]
    for ref, (which, col) in zip(pieces, places):
        outs[which][:, col : col + ref.shape[1]] = ref[...].astype(F32)
    turned, result, dx, dm = outs[-4:]
    turned[...] = jnp.transpose(lines_ref[...].astype(F32))
    result[...] = out_ref[...]
    dx[...] = dx_ref[...]
    dm[...] = (dm_ref[...] + dmi_ref[...].astype(F32)).astype(BF16)


def outputs(pieces, places, shapes, lines, out, dx, dm, dmi):
    ins = tuple(pieces) + (lines, out, dx, dm, dmi)
    result = jax.ShapeDtypeStruct(out.shape, BF16)
    return pl.pallas_call(
        functools.partial(outputs_kernel, places, len(pieces)),
        out_shape=[jax.ShapeDtypeStruct(a, F32) for a in shapes]
        + [jax.ShapeDtypeStruct((128, lines.shape[0]), F32), result, result, result],
        compiler_params=params(),
        cost_estimate=cost(0, 12 << 20),
        name="outputs",
    )(*ins)


def swap_sum(part, axis, pairs):
    came = lax.ppermute(part, axis, pairs)
    return part.astype(F32) + came.astype(F32)


def sum_scatter(grad, size, order):
    rows, cols = grad.shape
    bits = size.bit_length() - 1
    me = lax.axis_index("dp")
    now = grad.reshape((2,) * bits + (rows // size, cols))
    left = list(range(bits))[::-1]
    for bit in [b for b in order if b < bits] + [b for b in range(bits) if b not in order]:
        axis = left.index(bit)
        mine = (me >> bit) & 1
        keep = lax.dynamic_index_in_dim(now, mine, axis, keepdims=False)
        send = lax.dynamic_index_in_dim(now, 1 - mine, axis, keepdims=False)
        came = lax.ppermute(send, "dp", [(i, i ^ (1 << bit)) for i in range(size)])
        now = (keep.astype(F32) + came.astype(F32)).astype(BF16)
        left.pop(axis)
    return swap_sum(now, "sp", [(0, 1), (1, 0)])


def per_device(
    size,
    inputs,
    memory,
    target_docs,
    memory_docs,
    cotangent,
    w_qkv,
    b_q,
    b_v,
    w_so,
    b_so,
    g_one,
    s_one,
    w_cq,
    b_cq,
    w_ckv,
    b_cv,
    w_co,
    b_co,
    g_two,
    s_two,
    w_fi,
    b_fi,
    w_fo,
    b_fo,
    g_three,
    s_three,
):
    rows, width = inputs.shape[1:]
    wide = b_fi.shape[0]
    comm = size == 16
    narrow, broad = width // size, wide // size
    swap = [(0, 1), (1, 0)]
    x, mem, ct = inputs[0], memory[0], cotangent[0]
    x_o = lax.ppermute(x, "sp", [(0, 1)])
    docs_o = lax.ppermute(jnp.concatenate([target_docs, memory_docs], axis=0), "sp", swap)
    line = lax.broadcasted_iota(jnp.int32, (24, width), 0)
    vectors = (b_q, b_v, b_cv, b_so, g_one, s_one, b_cq, b_co, g_two, s_two, b_fo, g_three, s_three)
    vectors += tuple(b_fi[i : i + width] for i in range(0, wide, width))
    biases = jnp.zeros((24, width), F32)
    for i, v in enumerate(vectors):
        biases = jnp.where(line == i, v.astype(F32)[None], biases)

    qkv, mkv, t_own, m_own = project_own(x, mem, target_docs, memory_docs, w_qkv, w_ckv, biases)
    kvo, mem_s, t_oth, m_oth = project_other(x_o, mem, docs_o[:1], docs_o[1:], w_qkv, biases, t_own)
    mem_o = lax.ppermute(mem_s, "sp", swap)
    ctx, lse = self_forward(qkv, kvo, t_own, t_oth)
    h1, cq = first_norm(x, ctx, w_so, w_cq, biases)
    mkvo = project_memory(mem_o, w_ckv, biases)
    cc, clse = cross_forward(cq, mkv, mkvo, t_own, m_own, m_oth)
    output, dh2, dcc, gco, gwi, gwo, small_a, gib = feed(
        size, comm, h1, cc, ct, w_co, biases, w_fi, w_fo
    )
    turned = gib.reshape(width, -1).T

    def flow(array, hops, first=0, cols=None, before=("core",)):
        shape = (2, 2, 2, 2, narrow, array.shape[1])
        return Flow(array.reshape(shape), shape, before + hops, BLOCK, (first, cols or array.shape[1]))

    at_cross, at_first, at_self, at_input = (), (), (), ()
    if comm:
        gwi = gwi.reshape(2, 2, 2, narrow, wide)
        gwo = gwo.reshape(2, 2, 2, broad, width)
        third = wide // 3
        t0 = [
            Flow(gwi, gwi.shape, hops, BLOCK[:3], (i * third, third)) for i, hops in enumerate((VIA_X, VIA_Y, VIA_Z))
        ] + [
            Flow(gwo, gwo.shape, hops, BLOCK[:3], (i * 256, 256)) for i, hops in enumerate((VIA_X, VIA_Y, VIA_Z))
        ]
        late = [f for f in t0 if "yg" in f.hops]
        early = [flow(gco, VIA_Y)]
        at_cross = ((t0, 0, 3), (t0, 3, 5), (t0, 5, 6), (early, 0, 6))
    dcq, dm, dmo, gck, gcv, gcvb = cross_backward(
        cq, mkv, mkvo, dcc, cc, clse, t_own, m_own, m_oth, mem, mem_o, w_ckv, at_cross
    )
    dm_in = lax.ppermute(dmo, "sp", swap)
    if comm:
        at_first = ((late, 0, 1),)
    dh1, dsc, gcq, gso, small_b = first_back(dcq, dh2, h1, ctx, w_cq, w_so, biases, at_first)
    if comm:
        fresh = [flow(gck, VIA_X), flow(gcv, VIA_Z)] + [
            flow(g, hops, 256 * i, 256) for g in (gcq, gso) for i, hops in enumerate((VIA_X, VIA_Y, VIA_Z))
        ]
        t1 = early + fresh
        at_self = ((t0, 0, 2), (fresh, 0, 2), (t1, 2, 5), (t1, 5, 6))
    dq, dk, dv, dko, dvo = self_backward(qkv, kvo, dsc, ctx, lse, t_own, t_oth, at_self)
    block = (width,)
    if comm:
        block = (2, 2, 2, 2, narrow)
        last = [
            Flow(("ref", 14, i), block + (width,), ("core",) + hops, BLOCK) for i, hops in enumerate((VIA_X, VIA_Z, VIA_Y))
        ]
        last.append(Flow(("ref", 15), block + (128,), ("core",) + VIA_X, BLOCK))
        t1_late = [f for f in t1 if "yg" in f.hops]
        gq, gk, gv, sm = last
        at_input = (
            (t1, 0, 2), (t1, 2, 4), (t1_late, 4, 6),
            ([gq], 1, 2), ([gk], 2, 3), ([gv, sm], 3, 4),
            ([gq], 2, 4), ([gk], 3, 5), ([gv, sm], 4, 5),
            ([gq], 4, 5), (last, 5, 6), ([gk, gv, sm], 6, 7), (last, 7, 8), ([gk, gv], 8, 9),
        )
    dx, *rest = input_back(
        block, x, x_o, dq, dk, dv, dko, dvo, w_qkv, dh1, (small_a, small_b, gcvb, turned), at_input
    )
    if comm:
        pieces, places = [], []
        for flows, which in (
            ([gq, gk, gv], 0), (t1[1:3], 1), (t0[:3], 2), (t0[3:], 3), (t1[:1], 4), (t1[3:6], 5), (t1[6:], 6)
        ):
            col = 0
            for f in flows:
                pieces.append(f.array)
                places.append((which, col))
                col += f.shape[-1]
        shapes = [(narrow, 3 * width), (narrow, 2 * width), (narrow, wide), (broad, width)] + [(narrow, width)] * 3
        t_qkv, t_cmem, t_fin, t_fout, t_cout, t_cquery, t_out, lines, output, derivative, grad_memory = outputs(
            pieces, places, shapes, sm.array, output, dx, dm, dm_in
        )
    else:
        gqkv, columns = rest
        t_fin, t_fout, t_cout, t_cquery, t_out, t_cmem, t_qkv, lines = (
            sum_scatter(g, size, (0, 1, 2, 3))
            for g in (
                gwi, gwo, gco, gcq, gso, jnp.concatenate([gck, gcv], axis=1),
                jnp.concatenate([gqkv[0], gqkv[1], gqkv[2]], axis=1), columns,
            )
        )
        lines, derivative = lines.T, dx
        grad_memory = (dm + dm_in.astype(F32)).astype(BF16)
    t_gthree, t_sthree, t_fobias, t_gtwo, t_stwo, t_cobias = (lines[i] for i in range(6))
    t_cqbias, t_gone, t_sone, t_obias = (lines[i] for i in range(8, 12))
    t_cvbias, t_qbias, t_vbias = lines[16], lines[21], lines[22]
    t_fibias = lines[17:21].T.reshape(-1)
    return (
        output[None],
        derivative[None],
        grad_memory[None],
        t_qkv,
        t_qbias,
        t_vbias,
        t_out,
        t_obias,
        t_gone,
        t_sone,
        t_cquery,
        t_cqbias,
        t_cmem,
        t_cvbias,
        t_cout,
        t_cobias,
        t_gtwo,
        t_stwo,
        t_fin,
        t_fibias,
        t_fout,
        t_fobias,
        t_gthree,
        t_sthree,
    )


def solution(mesh):
    split = P("dp", "sp", None)
    in_specs = (split, split, P("dp", "sp"), P("dp", "sp"), split) + (P(),) * 21
    matrix, vector = P("dp", None), P("dp")
    out_specs = (
        split, split, split,
        matrix, vector, vector,
        matrix, vector, vector, vector,
        matrix, vector,
        matrix, vector,
        matrix, vector, vector, vector,
        matrix, vector,
        matrix, vector, vector, vector,
    )
    return jax.shard_map(
        functools.partial(per_device, mesh.shape["dp"]),
        mesh=mesh, in_specs=in_specs, out_specs=out_specs, check_vma=False,
    )
```

```python
import functools

import jax
import jax.numpy as jnp
from jax import lax
from jax.experimental import pallas as pl
from jax.experimental.pallas import tpu as pltpu
from jax.sharding import PartitionSpec as P

HD = 64
PAIR = 2 * HD
EPS = 1e-05
FAR = 1.0e9
VMEM = 60 * 1024 * 1024
F32 = jnp.float32
BF16 = jnp.bfloat16


def nn(a, b):
    return lax.dot_general(a, b, (((1,), (0,)), ((), ())), preferred_element_type=F32)


def nt(a, b):
    return lax.dot_general(a, b, (((1,), (1,)), ((), ())), preferred_element_type=F32)


def tn(a, b):
    return lax.dot_general(a, b, (((0,), (0,)), ((), ())), preferred_element_type=F32)


def params(collective=None):
    if collective is None:
        return pltpu.CompilerParams(vmem_limit_bytes=VMEM)
    return pltpu.CompilerParams(
        vmem_limit_bytes=VMEM, collective_id=collective, has_side_effects=True
    )


def cost(flops, moved):
    return pl.CostEstimate(flops=int(flops), bytes_accessed=int(moved), transcendentals=0)


def normed(h):
    centred = h - jnp.mean(h, axis=-1, keepdims=True)
    rstd = lax.rsqrt(jnp.mean(centred * centred, axis=-1, keepdims=True) + EPS)
    return centred * rstd, rstd


def norm_back(grad, n, rstd, gain):
    scaled = grad * gain
    centre = jnp.mean(scaled, axis=-1, keepdims=True)
    along = jnp.mean(scaled * n, axis=-1, keepdims=True)
    return rstd * (scaled - centre - n * along)


def total(a):
    return jnp.sum(a.astype(F32), axis=0, keepdims=True)


def place():
    me = lax.axis_index("dp")
    return me, me % 2, (me // 2) % 2, me // 4


def partner(hop, at=None):
    me, c, x, z = at or place()
    if hop == "core":
        return {"dp": me + 1 - 2 * c}
    if hop == "x":
        return {"dp": me + 2 - 4 * x}
    if hop == "z1":
        return {"dp": me + 4 - 8 * (z % 2)}
    if hop == "z2":
        return {"dp": me + 8 - 16 * (z // 2)}
    return {"sp": 1 - lax.axis_index("sp")}


def greet(hops, at=None):
    hops = sorted({"y" if h[0] == "y" else h for h in hops})
    barrier = pltpu.get_barrier_semaphore()
    for hop in hops:
        pl.semaphore_signal(barrier, inc=1, device_id=partner(hop, at), device_id_type=pl.DeviceIdType.MESH)
    pl.semaphore_wait(barrier, len(hops))


def remote(src, dst, send, recv, hop, at=None):
    return pltpu.make_async_remote_copy(
        src_ref=src, dst_ref=dst, send_sem=send, recv_sem=recv,
        device_id=partner(hop, at), device_id_type=pl.DeviceIdType.MESH,
    )


class Part:
    def __init__(self, hop, shape, dims, cols=None):
        self.hop, self.dims = hop, dims
        self.cols = cols or (0, shape[-1])
        self.shape = shape = tuple(shape[:-1]) + (self.cols[1],)
        if hop in dims:
            at = dims.index(hop)
            self.after, self.left = shape[:at] + shape[at + 1 :], dims[:at] + dims[at + 1 :]
        else:
            wide = shape[-1]
            wide = wide // 2 if hop == "yr" else 2 * wide if hop == "yg" else wide
            self.after, self.left = shape[:-1] + (wide,), dims
        self.came = shape if hop == "yg" else self.after

    def copies(self, src, made, came, send, recv, local, at_dp, sp):
        _, c, x, z = at_dp
        first, wide = self.cols
        full = (slice(None),) * (len(self.shape) - 1)
        stay = away = full + (pl.ds(first, wide),)
        to = made
        if self.hop in self.dims:
            at = self.dims.index(self.hop)
            mine = {"core": c, "x": x, "z1": z % 2, "z2": z // 2}[self.hop]
            stay = stay[:at] + (mine,) + stay[at + 1 :]
            away = away[:at] + (1 - mine,) + away[at + 1 :]
        elif self.hop == "yr":
            half = wide // 2
            stay = full + (pl.ds(pl.multiple_of(first + sp * half, 128), half),)
            away = full + (pl.ds(pl.multiple_of(first + (1 - sp) * half, 128), half),)
        elif self.hop == "yg":
            to = made.at[full + (pl.ds(pl.multiple_of(sp * wide, 128), wide),)]
        return [
            remote(src.at[away], came, send, recv, self.hop, at_dp),
            pltpu.make_async_copy(src.at[stay], to, local),
        ]

    def add(self, made, came, sp):
        if self.hop == "yg":
            wide = self.shape[-1]
            at = pl.ds(pl.multiple_of((1 - sp) * wide, 128), wide)
            made[(slice(None),) * (len(self.shape) - 1) + (at,)] = came[...]
        else:
            made[...] += came[...]


class Flow:
    def __init__(self, array, shape, hops, dims, cols=None):
        self.array, self.shape, self.dims, self.cols = array, tuple(shape), dims, cols
        self.hops = list(hops)

    def step(self):
        part = Part(self.hops.pop(0), self.shape, self.dims, self.cols)
        self.shape, self.dims, self.cols = part.after, part.left, None
        return part


class Window:
    def __init__(self, start, stop):
        self.start, self.stop = start, stop
        self.parts, self.sources, self.keeps = [], [], []


def plan(schedule):
    windows, arrays, latest = [], [], {}
    for n, (flows, start, stop) in enumerate(schedule):
        window = Window(start, stop)
        for i, flow in enumerate(flows):
            if flow in latest:
                source = ("part",) + latest[flow]
                before = windows[latest[flow][0]]
                before.keeps[latest[flow][1]] = False
            elif isinstance(flow.array, tuple):
                source = flow.array
            else:
                known = [k for k, a in enumerate(arrays) if a is flow.array]
                if not known:
                    arrays.append(flow.array)
                source = ("in", known[0] if known else len(arrays) - 1)
            window.parts.append(flow.step())
            window.sources.append(source)
            window.keeps.append(True)
            latest[flow] = (n, i)
        windows.append(window)
    return windows, arrays, latest


def carrying(body, own, windows, arrays, grid, also, finale):
    ins, outs, held = own

    def kernel(*refs):
        refs = list(refs)

        def take(n):
            got = refs[:n]
            del refs[:n]
            return got

        my_in, arr = take(ins), take(arrays)
        my_out = take(outs)
        given = [[take(1)[0] if k else None for k in w.keeps] for w in windows]
        my_held = take(held)
        made, came = [], []
        for w, g in zip(windows, given):
            made.append([ref if ref is not None else take(1)[0] for ref in g])
            came.append(take(len(w.parts)))
        mine = my_in + my_out + my_held
        step = pl.program_id(0)
        hops = [q.hop for w in windows for q in w.parts] + list(also)
        if hops:
            at_dp, sp = place(), lax.axis_index("sp")
            pl.when(step == 0)(lambda: greet(hops, at_dp))
        if windows:
            send, recv, local = refs
        copies, base = [], 0
        for w, m, c in zip(windows, made, came):
            now = []
            for i, q in enumerate(w.parts):
                kind = w.sources[i]
                if kind[0] == "in":
                    src = arr[kind[1]]
                elif kind[0] == "ref":
                    src = mine[kind[1]]
                    src = src.at[kind[2]] if len(kind) > 2 else src
                else:
                    src = made[kind[1]][kind[2]]
                now += q.copies(
                    src, m[i], c[i], send.at[base], recv.at[base], local.at[base], at_dp, sp
                )
                base += 1
            copies.append(now)

        def phase(number):
            for n, w in enumerate(windows):
                if w.stop == number:
                    for copy in copies[n]:
                        copy.wait()
                    for q, m, c in zip(w.parts, made[n], came[n]):
                        q.add(m, c, sp)
            for n, w in enumerate(windows):
                if w.start == number:
                    for copy in copies[n]:
                        copy.start()

        used = sorted({w.start for w in windows} | {w.stop for w in windows})
        for number in used:
            if number < grid:
                pl.when(step == number)(functools.partial(phase, number))
        body(*mine)
        for number in used:
            if number >= grid:
                pl.when(step == grid - 1)(functools.partial(phase, number))
        if finale:
            pl.when(step == grid - 1)(lambda: finale(*mine))

    return kernel


def run(
    body, name, grid, ins, in_specs, outs, out_specs, held=(), schedule=(), collective=None,
    flops=0, moved=0, also=(), finale=None,
):
    in_specs, outs, out_specs, held = list(in_specs), list(outs), list(out_specs), list(held)
    windows, arrays, latest = plan(schedule)
    own = len(outs)
    kernel = carrying(body, (len(ins), own, len(held)), windows, len(arrays), grid, also, finale)
    in_specs += [pl.BlockSpec(memory_space=pl.ANY)] * len(arrays)
    order, count = [], 0
    for n, w in enumerate(windows):
        for i, (q, k) in enumerate(zip(w.parts, w.keeps)):
            if k:
                outs.append(jax.ShapeDtypeStruct(q.after, BF16))
                out_specs.append(whole(q.after))
                order.append((n, i))
            else:
                held.append(pltpu.VMEM(q.after, BF16))
        held += [pltpu.VMEM(q.came, BF16) for q in w.parts]
        count += len(w.parts)
    if windows:
        held += [pltpu.SemaphoreType.DMA((count,))] * 3
    results = pl.pallas_call(
        kernel,
        grid=(grid,),
        in_specs=in_specs,
        out_specs=out_specs,
        out_shape=outs,
        scratch_shapes=held,
        compiler_params=params(collective if windows or also else None),
        cost_estimate=cost(flops, moved),
        name=name,
    )(*ins, *arrays)
    for flow, where in latest.items():
        flow.array = results[own + order.index(where)]
    return results[:own]


VIA_X = ("x", "z1", "z2", "y")
VIA_Y = ("yr", "x", "z1", "z2", "yg")
VIA_Z = ("z1", "yr", "x", "z2", "yg")
BLOCK = ("z2", "z1", "x", "core")


def code_of(docs_ref):
    row = lax.broadcasted_iota(jnp.int32, (128, docs_ref.shape[1]), 0)
    return jnp.transpose(jnp.where(docs_ref[...] == row, 1.0, 0.0)).astype(BF16)


def project_own_kernel(x_ref, m_ref, td_ref, md_ref, wx_ref, wm_ref, b_ref, qkv_ref, mkv_ref, to_ref, mo_ref):
    step = pl.program_id(0)

    @pl.when(step == 0)
    def _():
        to_ref[...] = code_of(td_ref)
        mo_ref[...] = code_of(md_ref)

    @pl.when(step < 3)
    def _():
        bias = jnp.where(step == 0, b_ref[0:1], 0.0) + jnp.where(step == 2, b_ref[1:2], 0.0)
        qkv_ref[...] = (nn(x_ref[...], wx_ref[...]) + bias).astype(BF16)

    @pl.when(step >= 3)
    def _():
        bias = jnp.where(step == 4, b_ref[2:3], 0.0)
        mkv_ref[...] = (nn(m_ref[...], wm_ref[...]) + bias).astype(BF16)


def project_own(x, mem, td, md, wx, wm, biases):
    rows, width = x.shape
    code = jax.ShapeDtypeStruct((rows, 128), BF16)
    return pl.pallas_call(
        project_own_kernel,
        grid=(5,),
        in_specs=[
            whole((rows, width)), whole((rows, width)), whole((1, rows)), whole((1, rows)),
            pl.BlockSpec((width, width), lambda s: (0, jnp.minimum(s, 2))),
            pl.BlockSpec((width, width), lambda s: (0, jnp.maximum(s - 3, 0))),
            whole(biases.shape),
        ],
        out_specs=[
            pl.BlockSpec((rows, width), lambda s: (0, jnp.minimum(s, 2))),
            pl.BlockSpec((rows, width), lambda s: (0, jnp.maximum(s - 3, 0))),
            whole((rows, 128)), whole((rows, 128)),
        ],
        out_shape=[
            jax.ShapeDtypeStruct((rows, 3 * width), BF16), jax.ShapeDtypeStruct((rows, 2 * width), BF16), code, code,
        ],
        compiler_params=params(),
        cost_estimate=cost(10 * rows * width * width, 20 * width * width),
        name="project_own",
    )(x, mem, td, md, wx, wm, biases)


def project_other_kernel(x_ref, m_ref, td_ref, md_ref, wx_ref, b_ref, after_ref, kvo_ref, mem_ref, tt_ref, mt_ref):
    step = pl.program_id(0)

    @pl.when(step == 0)
    def _():
        mem_ref[...] = m_ref[...]
        tt_ref[...] = code_of(td_ref)
        mt_ref[...] = code_of(md_ref)

    @pl.when(lax.axis_index("sp") == 1)
    def _():
        bias = jnp.where(step == 1, b_ref[1:2], 0.0)
        kvo_ref[...] = (nn(x_ref[...], wx_ref[...]) + bias).astype(BF16)

    @pl.when(lax.axis_index("sp") == 0)
    def _():
        kvo_ref[...] = jnp.zeros(kvo_ref.shape, BF16)


def project_other(x, mem, td, md, wx, biases, after):
    rows, width = x.shape
    code = jax.ShapeDtypeStruct((rows, 128), BF16)
    return pl.pallas_call(
        project_other_kernel,
        grid=(2,),
        in_specs=[
            whole((rows, width)), whole((rows, width)), whole((1, rows)), whole((1, rows)),
            pl.BlockSpec((width, width), lambda s: (0, s + 1)),
            whole(biases.shape),
            pl.BlockSpec(memory_space=pl.ANY),
        ],
        out_specs=[
            pl.BlockSpec((rows, width), lambda s: (0, s)),
            whole((rows, width)), whole((rows, 128)), whole((rows, 128)),
        ],
        out_shape=[
            jax.ShapeDtypeStruct((rows, 2 * width), BF16), jax.ShapeDtypeStruct((rows, width), BF16), code, code,
        ],
        compiler_params=params(),
        cost_estimate=cost(4 * rows * width * width, 10 * width * width),
        name="project_other",
    )(x, mem, td, md, wx, biases, after)


def project_memory_kernel(x_ref, w_ref, b_ref, o_ref):
    bias = jnp.where(pl.program_id(0) == 1, b_ref[2:3], 0.0)
    o_ref[...] = (nn(x_ref[...], w_ref[...]) + bias).astype(BF16)


def project_memory(x, w, biases):
    rows, width = x.shape
    return pl.pallas_call(
        project_memory_kernel,
        grid=(2,),
        in_specs=[
            whole((rows, width)),
            pl.BlockSpec((width, width), lambda j: (0, j)),
            whole(biases.shape),
        ],
        out_specs=pl.BlockSpec((rows, width), lambda j: (0, j)),
        out_shape=jax.ShapeDtypeStruct((rows, 2 * width), BF16),
        compiler_params=params(),
        cost_estimate=cost(4 * rows * width * width, 4 * width * (width + rows)),
        name="project_memory",
    )(x, w, biases)


def head_masks(dtype):
    lane = lax.broadcasted_iota(jnp.int32, (1, PAIR), 1)
    low = jnp.where(lane < HD, 1.0, 0.0)
    return low.astype(dtype), (1.0 - low).astype(dtype)


def query_code(code):
    lane = lax.broadcasted_iota(jnp.int32, code.shape, 1)
    return jnp.where(lane < 4, (code.astype(F32) - 1.0) * FAR, 0.0).astype(BF16)


def softmax_pieces(scores, values):
    peak = functools.reduce(jnp.maximum, [jnp.max(s, axis=-1, keepdims=True) for s in scores])
    expd = [jnp.exp(s - peak) for s in scores]
    norm = sum(jnp.sum(e, axis=-1, keepdims=True) for e in expd)
    out = sum(nn(e.astype(BF16), v) for e, v in zip(expd, values))
    return out / norm, peak + jnp.log(norm)


def self_pieces(block, size, both, own, other):
    pieces = []
    if both:
        pieces.append((other, False))
    if block:
        pieces.append((own[: block * size], False))
    pieces.append((own[block * size : (block + 1) * size], True))
    return pieces


def store_lse(lse_ref, block, size, low, high):
    lane = lax.broadcasted_iota(jnp.int32, (size, PAIR), 1)
    both = jnp.where(lane == 0, low, high)
    lse_ref[:, block * size : (block + 1) * size] = jnp.transpose(both)[:8]


def self_forward_kernel(size, q_ref, k_ref, v_ref, ko_ref, vo_ref, own_ref, oth_ref, o_ref, lse_ref):
    second = lax.axis_index("sp") == 1
    rows = q_ref.shape[0]
    masks = head_masks(BF16)
    outs = head_masks(F32)

    def run(both):
        qcode = query_code(own_ref[...])
        own = jnp.concatenate([k_ref[...], own_ref[...]], axis=1)
        oth = jnp.concatenate([ko_ref[...], oth_ref[...]], axis=1) if both else None
        vown = v_ref[...]
        voth = vo_ref[...] if both else None
        for block in range(rows // size):
            at = slice(block * size, (block + 1) * size)
            lses, result = [], 0.0
            for mask, keep in zip(masks, outs):
                q = jnp.concatenate([q_ref[at] * (mask * BF16(HD**-0.5)), qcode[at]], axis=1)
                scores = []
                for keys, diagonal in self_pieces(block, size, both, own, oth):
                    s = nt(q, keys)
                    if diagonal:
                        row = lax.broadcasted_iota(jnp.int32, s.shape, 0)
                        col = lax.broadcasted_iota(jnp.int32, s.shape, 1)
                        s = jnp.where(row >= col, s, -FAR)
                    scores.append(s)
                values = [v for v, _ in self_pieces(block, size, both, vown, voth)]
                out, lse = softmax_pieces(scores, values)
                result = result + out * keep
                lses.append(lse)
            o_ref[at] = result.astype(BF16)
            store_lse(lse_ref, block, size, *lses)

    pl.when(second)(lambda: run(True))
    pl.when(jnp.logical_not(second))(lambda: run(False))


def pair_spec(rows, offset):
    return pl.BlockSpec((rows, PAIR), lambda p: (0, p + offset))


def whole(shape):
    return pl.BlockSpec(shape, lambda *_: (0,) * len(shape))


def self_forward(qkv, kvo, own, oth):
    rows = qkv.shape[0]
    width = qkv.shape[1] // 3
    pairs = width // PAIR
    return pl.pallas_call(
        functools.partial(self_forward_kernel, 256),
        grid=(pairs,),
        in_specs=[
            pair_spec(rows, 0),
            pair_spec(rows, pairs),
            pair_spec(rows, 2 * pairs),
            pair_spec(rows, 0),
            pair_spec(rows, pairs),
            whole((rows, 128)),
            whole((rows, 128)),
        ],
        out_specs=[pair_spec(rows, 0), pl.BlockSpec((8, rows), lambda p: (p, 0))],
        out_shape=[
            jax.ShapeDtypeStruct((rows, width), BF16),
            jax.ShapeDtypeStruct((8 * pairs, rows), F32),
        ],
        compiler_params=params(),
        cost_estimate=cost(16 * rows * rows * width, 16 * rows * width),
        name="self_forward",
    )(qkv, qkv, qkv, kvo, kvo, own, oth)


def cross_forward_kernel(size, q_ref, k_ref, v_ref, ko_ref, vo_ref, t_ref, own_ref, oth_ref, o_ref, lse_ref):
    rows = q_ref.shape[0]
    masks = head_masks(BF16)
    outs = head_masks(F32)
    qcode = query_code(t_ref[...])
    keys = [
        jnp.concatenate([k_ref[...], own_ref[...]], axis=1),
        jnp.concatenate([ko_ref[...], oth_ref[...]], axis=1),
    ]
    values = [v_ref[...], vo_ref[...]]
    for block in range(rows // size):
        at = slice(block * size, (block + 1) * size)
        lses, result = [], 0.0
        for mask, keep in zip(masks, outs):
            q = jnp.concatenate([q_ref[at] * (mask * BF16(HD**-0.5)), qcode[at]], axis=1)
            out, lse = softmax_pieces([nt(q, k) for k in keys], values)
            result = result + out * keep
            lses.append(lse)
        o_ref[at] = result.astype(BF16)
        store_lse(lse_ref, block, size, *lses)


def cross_forward(cq, kv, kvo, t, own, oth):
    rows, width = cq.shape
    pairs = width // PAIR
    return pl.pallas_call(
        functools.partial(cross_forward_kernel, 256),
        grid=(pairs,),
        in_specs=[
            pair_spec(rows, 0),
            pair_spec(rows, 0),
            pair_spec(rows, pairs),
            pair_spec(rows, 0),
            pair_spec(rows, pairs),
            whole((rows, 128)),
            whole((rows, 128)),
            whole((rows, 128)),
        ],
        out_specs=[pair_spec(rows, 0), pl.BlockSpec((8, rows), lambda p: (p, 0))],
        out_shape=[
            jax.ShapeDtypeStruct((rows, width), BF16),
            jax.ShapeDtypeStruct((8 * pairs, rows), F32),
        ],
        compiler_params=params(),
        cost_estimate=cost(24 * rows * rows * width, 16 * rows * width),
        name="cross_forward",
    )(cq, kv, kv, kvo, kvo, t, own, oth)


def delta_rows(g, o):
    prod = g.astype(F32) * o.astype(F32)
    upper = prod.astype(BF16)
    lower = (prod - upper.astype(F32)).astype(BF16)
    row = lax.broadcasted_iota(jnp.int32, (8, PAIR), 0)
    lane = lax.broadcasted_iota(jnp.int32, (8, PAIR), 1)
    pick = jnp.where(row == lane // HD, 1.0, 0.0).astype(BF16)
    return nt(pick, upper) + nt(pick, lower)


def back_piece(keys, values, q, g, lse, delta, causal):
    s = nt(keys, q)
    if causal:
        row = lax.broadcasted_iota(jnp.int32, s.shape, 0)
        col = lax.broadcasted_iota(jnp.int32, s.shape, 1)
        s = jnp.where(row <= col, s, -FAR)
    p = jnp.exp(s - lse)
    ds = p * (nt(values, g) - delta)
    return p.astype(BF16), ds.astype(BF16)


def cross_backward_kernel(
    size, q_ref, k_ref, v_ref, ko_ref, vo_ref, g_ref, o_ref, lse_ref, t_ref, own_ref, oth_ref,
    m_ref, mo_ref, wk_ref, wv_ref,
    dq_ref, dm_ref, dmo_ref, gk_ref, gv_ref, gb_ref, dm_acc, dmo_acc, mt_ref, mot_ref,
):
    step = pl.program_id(0)

    @pl.when(step == 0)
    def _():
        mt_ref[...] = jnp.transpose(m_ref[...])
        mot_ref[...] = jnp.transpose(mo_ref[...])

    rows = q_ref.shape[0]
    masks = head_masks(BF16)
    scale = BF16(HD**-0.5)
    qcode = query_code(t_ref[...])
    delta = delta_rows(g_ref[...], o_ref[...])
    lse = lse_ref[...]
    halves = [(k_ref, v_ref, own_ref, mt_ref, dm_acc), (ko_ref, vo_ref, oth_ref, mot_ref, dmo_acc)]
    dq = [0.0] * (rows // size)
    gk = gv = gb = 0.0
    for kr, vr, code, mem, acc in halves:
        keys = jnp.concatenate([kr[...], code[...]], axis=1)
        values = vr[...]
        dk = dv = 0.0
        for block in range(rows // size):
            at = slice(block * size, (block + 1) * size)
            for head, mask in enumerate(masks):
                qm = q_ref[at] * (mask * scale)
                gm = g_ref[at] * mask
                q = jnp.concatenate([qm, qcode[at]], axis=1)
                p, ds = back_piece(
                    keys, values, q, gm, lse[head : head + 1, at], delta[head : head + 1, at], False
                )
                dk = dk + nn(ds, qm)
                dv = dv + nn(p, gm)
                dq[block] = dq[block] + tn(ds, kr[...] * (mask * scale))
        both = jnp.concatenate([dk.astype(BF16), dv.astype(BF16)], axis=1)
        grad = nn(mem[...], both)
        gk, gv = gk + grad[:, :PAIR], gv + grad[:, PAIR:]
        gb = gb + total(both[:, PAIR:])
        dm = nt(both, jnp.concatenate([wk_ref[...], wv_ref[...]], axis=1))

        @pl.when(step == 0)
        def _():
            acc[...] = dm

        @pl.when(step > 0)
        def _():
            acc[...] += dm
    for block in range(rows // size):
        dq_ref[block * size : (block + 1) * size] = dq[block].astype(BF16)
    gk_ref[...] = gk.astype(BF16)
    gv_ref[...] = gv.astype(BF16)
    gb_ref[...] = gb

    @pl.when(step == pl.num_programs(0) - 1)
    def _():
        dm_ref[...] = dm_acc[...]
        dmo_ref[...] = dmo_acc[...].astype(BF16)


def cross_backward(cq, kv, kvo, g, o, lse, t, own, oth, m, mo, w, schedule):
    rows, width = cq.shape
    pairs = width // PAIR
    flat = jax.ShapeDtypeStruct((rows, width), BF16)
    square = jax.ShapeDtypeStruct((width, width), BF16)
    return run(
        functools.partial(cross_backward_kernel, 256), "cross_backward", pairs,
        (cq, kv, kv, kvo, kvo, g, o, lse, t, own, oth, m, mo, w, w),
        [
            pair_spec(rows, 0),
            pair_spec(rows, 0),
            pair_spec(rows, pairs),
            pair_spec(rows, 0),
            pair_spec(rows, pairs),
            pair_spec(rows, 0),
            pair_spec(rows, 0),
            pl.BlockSpec((8, rows), lambda p: (p, 0)),
            whole((rows, 128)),
            whole((rows, 128)),
            whole((rows, 128)),
            whole((rows, width)),
            whole((rows, width)),
            pair_spec(width, 0),
            pair_spec(width, pairs),
        ],
        [flat, jax.ShapeDtypeStruct((rows, width), F32), flat, square, square, jax.ShapeDtypeStruct((1, width), F32)],
        [pair_spec(rows, 0)] + [whole((rows, width))] * 2 + [pair_spec(width, 0)] * 2 + [pair_spec(1, 0)],
        [pltpu.VMEM((rows, width), F32)] * 2 + [pltpu.VMEM((width, rows), BF16)] * 2,
        schedule, 3,
        64 * rows * rows * width + 16 * rows * width * width, 24 * rows * width,
    )


def self_backward_kernel(
    size, q_ref, k_ref, v_ref, ko_ref, vo_ref, g_ref, o_ref, lse_ref, own_ref, oth_ref,
    x_ref, xo_ref, wq_ref, wk_ref, wv_ref, dh1_ref, sa_ref, sb_ref, sc_ref, sd_ref,
    dx_ref, grad_ref, sm_ref,
    dq_acc, dx_acc, dxo_acc, dkv_acc, xt_ref, xot_ref, dxo_ref, came_ref, turn_ref, send_ref, recv_ref,
):
    step = pl.program_id(0)
    sp = lax.axis_index("sp")
    second = sp == 1
    rows, width = x_ref.shape
    pairs = width // PAIR
    pair = lax.rem(step, pairs)
    cols = pl.ds(pl.multiple_of(pair * PAIR, PAIR), PAIR)
    masks = head_masks(BF16)
    scale = BF16(HD**-0.5)
    count = rows // size
    over = remote(dxo_ref, came_ref, send_ref.at[0], recv_ref.at[0], "y")

    def pieces():
        qcode = query_code(own_ref[...])
        delta = delta_rows(g_ref[...], o_ref[...])
        for block in range(count):
            at = slice(block * size, (block + 1) * size)
            for head, mask in enumerate(masks):
                qm = q_ref[at] * (mask * scale)
                gm = g_ref[at] * mask
                q = jnp.concatenate([qm, qcode[at]], axis=1)
                yield block, mask, qm, gm, q, lse_ref[head : head + 1, at], delta[head : head + 1, at]

    @pl.when(step == 0)
    def _():
        xt_ref[...] = jnp.transpose(x_ref[...])
        turn_ref[...] = jnp.zeros(turn_ref.shape, F32)
        turn_ref[0:8] = sa_ref[...]
        turn_ref[8:16] = sb_ref[...]
        turn_ref[16:17] = sc_ref[...]
        turn_ref[17:21] = sd_ref[...]

    @pl.when(jnp.logical_and(step == 0, second))
    def _():
        xot_ref[...] = jnp.transpose(xo_ref[...])

    @pl.when(jnp.logical_and(step < pairs, second))
    def _():
        keys = jnp.concatenate([ko_ref[...], oth_ref[...]], axis=1)
        values = vo_ref[...]
        dk = dv = 0.0
        dq = [0.0] * count
        for block, mask, qm, gm, q, lse, delta in pieces():
            p, ds = back_piece(keys, values, q, gm, lse, delta, False)
            dk = dk + nn(ds, qm)
            dv = dv + nn(p, gm)
            dq[block] = dq[block] + tn(ds, ko_ref[...] * (mask * scale))
        for block in range(count):
            dq_acc[pair, block * size : (block + 1) * size] = dq[block]
        both = jnp.concatenate([dk.astype(BF16), dv.astype(BF16)], axis=1)
        dkv_acc[pair] = both
        dxo = nt(both, jnp.concatenate([wk_ref[...], wv_ref[...]], axis=1))

        @pl.when(step == 0)
        def _():
            dxo_acc[...] = dxo

        @pl.when(step > 0)
        def _():
            dxo_acc[...] += dxo

    @pl.when(jnp.logical_and(step == pairs - 1, second))
    def _():
        dxo_ref[...] = dxo_acc[...].astype(BF16)
        over.start()

    @pl.when(step >= pairs)
    def _():
        dq, dk, dv = [0.0] * count, [0.0] * count, [0.0] * count
        for block, mask, qm, gm, q, lse, delta in pieces():
            for part in range(block + 1):
                of = slice(part * size, (part + 1) * size)
                keys = jnp.concatenate([k_ref[of], own_ref[of]], axis=1)
                p, ds = back_piece(keys, v_ref[of], q, gm, lse, delta, part == block)
                dk[part] = dk[part] + nn(ds, qm)
                dv[part] = dv[part] + nn(p, gm)
                dq[block] = dq[block] + tn(ds, k_ref[of] * (mask * scale))
        dq, dk, dv = (jnp.concatenate(a, axis=0) for a in (dq, dk, dv))
        dq = jnp.where(second, dq + dq_acc[pair], dq)
        dqk = jnp.concatenate([dq.astype(BF16), dk.astype(BF16)], axis=1)
        dv = dv.astype(BF16)
        grad_qk = nn(xt_ref[...], dqk)
        grad_v = nn(xt_ref[...], dv)
        shape = grad_ref.shape[1:-1] + (PAIR,)
        lead = (slice(None),) * (len(shape) - 1)

        def put(n, grad):
            grad_ref[(n,) + lead + (cols,)] = grad.astype(BF16).reshape(shape)

        put(0, grad_qk[:, :PAIR])
        turn_ref[21:22, cols] = total(dqk[:, :PAIR])

        @pl.when(second)
        def _():
            grad_o = nn(xot_ref[...], dkv_acc[pair])
            put(1, grad_qk[:, PAIR:] + grad_o[:, :PAIR])
            put(2, grad_v + grad_o[:, PAIR:])
            turn_ref[22:23, cols] = total(dv) + total(dkv_acc[pair, :, PAIR:])

        @pl.when(jnp.logical_not(second))
        def _():
            put(1, grad_qk[:, PAIR:])
            put(2, grad_v)
            turn_ref[22:23, cols] = total(dv)

        dx = nt(dqk, jnp.concatenate([wq_ref[...], wk_ref[...]], axis=1)) + nt(dv, wv_ref[...])

        @pl.when(step == pairs)
        def _():
            dx_acc[...] = dh1_ref[...] + dx

        @pl.when(step > pairs)
        def _():
            dx_acc[...] += dx

    @pl.when(step == 2 * pairs - 1)
    def _():
        sm_ref[...] = jnp.transpose(turn_ref[...]).astype(BF16).reshape(sm_ref.shape)


def self_backward_finale(*refs):
    dx_ref, dx_acc, dxo_ref, came_ref, send_ref, recv_ref = (refs[i] for i in (20, 24, 29, 30, 32, 33))
    over = remote(dxo_ref, came_ref, send_ref.at[0], recv_ref.at[0], "y")

    @pl.when(lax.axis_index("sp") == 0)
    def _():
        over.wait_recv()
        dx_ref[...] = (dx_acc[...] + came_ref[...].astype(F32)).astype(BF16)

    @pl.when(lax.axis_index("sp") == 1)
    def _():
        over.wait_send()
        dx_ref[...] = dx_acc[...].astype(BF16)


GRADS = 21


def self_backward(block, qkv, kvo, g, o, lse, own, oth, x, xo, w, dh1, small, schedule):
    rows, width = x.shape
    pairs = width // PAIR

    def pair_of(offset):
        return pl.BlockSpec((rows, PAIR), lambda s: (0, lax.rem(s, pairs) + offset))

    def weight(offset):
        return pl.BlockSpec((width, PAIR), lambda s: (0, lax.rem(s, pairs) + offset))

    made = [(3,) + block + (width,), block + (128,)]
    outs = [jax.ShapeDtypeStruct((rows, width), BF16)]
    specs = [whole((rows, width))]
    held = []
    if schedule:
        held += [pltpu.VMEM(a, BF16) for a in made]
    else:
        outs += [jax.ShapeDtypeStruct(a, BF16) for a in made]
        specs += [whole(a) for a in made]
    held += [
        pltpu.VMEM((pairs, rows, PAIR), F32),
        pltpu.VMEM((rows, width), F32),
        pltpu.VMEM((rows, width), F32),
        pltpu.VMEM((pairs, rows, 2 * PAIR), BF16),
        pltpu.VMEM((width, rows), BF16),
        pltpu.VMEM((width, rows), BF16),
        pltpu.VMEM((rows, width), BF16),
        pltpu.VMEM((rows, width), BF16),
        pltpu.VMEM((128, width), F32),
        pltpu.SemaphoreType.DMA((1,)),
        pltpu.SemaphoreType.DMA((1,)),
    ]
    return run(
        functools.partial(self_backward_kernel, 256), "self_backward", 2 * pairs,
        (qkv, qkv, qkv, kvo, kvo, g, o, lse, own, oth, x, xo, w, w, w, dh1) + tuple(small),
        [
            pair_of(0),
            pair_of(pairs),
            pair_of(2 * pairs),
            pair_of(0),
            pair_of(pairs),
            pair_of(0),
            pair_of(0),
            pl.BlockSpec((8, rows), lambda s: (lax.rem(s, pairs), 0)),
            whole((rows, 128)),
            whole((rows, 128)),
            whole((rows, width)),
            whole((rows, width)),
            weight(0),
            weight(pairs),
            weight(2 * pairs),
            whole((rows, width)),
        ] + [whole(a.shape) for a in small],
        outs, specs, held, schedule, 5,
        48 * rows * rows * width + 20 * rows * width * width, 12 * width * width + 40 * rows * width,
        ("y",), self_backward_finale,
    )


def first_norm_kernel(x_ref, ctx_ref, wo_ref, wq_ref, b_ref, h_ref, cq_ref):
    h = x_ref[...].astype(F32) + nn(ctx_ref[...], wo_ref[...]) + b_ref[3:4]
    h_ref[...] = h
    n, _ = normed(h)
    a = (n * b_ref[4:5] + b_ref[5:6]).astype(BF16)
    cq_ref[...] = (nn(a, wq_ref[...]) + b_ref[6:7]).astype(BF16)


def first_norm(x, ctx, wo, wq, biases):
    rows, width = x.shape
    return pl.pallas_call(
        first_norm_kernel,
        out_shape=[
            jax.ShapeDtypeStruct((rows, width), F32),
            jax.ShapeDtypeStruct((rows, width), BF16),
        ],
        compiler_params=params(),
        cost_estimate=cost(4 * rows * width * width, 4 * width * width + 10 * rows * width),
        name="first_norm",
    )(x, ctx, wo, wq, biases)


def feed_kernel(
    count, comm, h1_ref, cc_ref, ct_ref, wco_ref, b_ref, wi_ref, wo_ref,
    out_ref, dh2_ref, dcc_ref, gco_ref, gwi_ref, gwo_ref, small_ref, gib_ref,
    hid_ref, slope_ref, n2_ref, r2_ref, a2b_ref, acc_ref, df_ref, *refs,
):
    step = pl.program_id(0)
    width = acc_ref.shape[1]

    if comm:
        mi_ref, mo_ref, ci_ref, co_ref, send_ref, recv_ref = refs
        _, c, _, _ = place()

        def chunk_copies(j):
            at = pl.ds(pl.multiple_of(j * width, width), width)
            return [
                remote(
                    mi_ref.at[:, 1 - c, :, at], ci_ref.at[:, :, at], send_ref.at[0, j], recv_ref.at[0, j], "core"
                ),
                remote(mo_ref.at[j, :, 1 - c], co_ref.at[j], send_ref.at[1, j], recv_ref.at[1, j], "core"),
            ]

    @pl.when(step == 0)
    def _():
        if comm:
            greet(["core"])
        n1, _ = normed(h1_ref[...])
        a1 = n1 * b_ref[4:5] + b_ref[5:6]
        h2 = a1 + nn(cc_ref[...], wco_ref[...]) + b_ref[7:8]
        n2, r2 = normed(h2)
        n2_ref[...] = n2
        r2_ref[...] = jnp.broadcast_to(r2, r2_ref.shape)
        a2 = n2 * b_ref[8:9] + b_ref[9:10]
        a2b_ref[...] = a2.astype(BF16)
        acc_ref[...] = a2 + b_ref[10:11]

    @pl.when(step < count)
    def _():
        u = nn(a2b_ref[...], wi_ref[...]) + b_ref[pl.ds(13 + step, 1)]
        cumul = 0.5 * (1.0 + lax.erf(u * 0.7071067811865476))
        density = jnp.exp(-0.5 * u * u) * 0.3989422804014327
        hid = (u * cumul).astype(BF16)
        hid_ref[step] = hid
        slope_ref[step] = cumul + u * density
        acc_ref[...] += nn(hid, wo_ref[...])

    @pl.when(step == count - 1)
    def _():
        n3, r3 = normed(acc_ref[...])
        gain = b_ref[11:12]
        out_ref[...] = (n3 * gain + b_ref[12:13]).astype(BF16)
        e = ct_ref[...].astype(F32)
        d3 = norm_back(e, n3, r3, gain)
        df = d3.astype(BF16)
        df_ref[...] = df
        acc_ref[...] = d3
        small_ref[0:1] = total(e * n3)
        small_ref[1:2] = total(e)
        small_ref[2:3] = total(df)

    @pl.when(jnp.logical_and(step >= count, step < 2 * count))
    def _():
        j = step - count
        df = df_ref[...]
        du = (nt(df, wo_ref[...]) * slope_ref[j]).astype(BF16)
        gib_ref[...] = total(du)
        acc_ref[...] += nt(du, wi_ref[...])
        go = tn(hid_ref[j], df).astype(BF16)
        gi = tn(a2b_ref[...], du).astype(BF16)
        if comm:
            at = pl.ds(pl.multiple_of(j * width, width), width)
            mo_ref[j] = go.reshape(mo_ref.shape[1:])
            mi_ref[:, :, :, at] = gi.reshape(mi_ref.shape[:3] + (width,))
            for copy in chunk_copies(j):
                copy.start()
        else:
            gwo_ref[...] = go
            gwi_ref[...] = gi

    @pl.when(step == 2 * count)
    def _():
        d2 = acc_ref[...]
        n2 = n2_ref[...]
        dh2 = norm_back(d2, n2, r2_ref[:, :1], b_ref[8:9])
        dh2_ref[...] = dh2
        dco = dh2.astype(BF16)
        dcc_ref[...] = nt(dco, wco_ref[...]).astype(BF16)
        gco_ref[...] = tn(cc_ref[...], dco).astype(BF16)
        small_ref[3:4] = total(d2 * n2)
        small_ref[4:5] = total(d2)
        small_ref[5:6] = total(dco)
        small_ref[6:8] = jnp.zeros((2, d2.shape[1]), F32)

    if comm:

        @pl.when(step > count)
        def _():
            j = step - count - 1
            at = pl.ds(pl.multiple_of(j * width, width), width)
            for copy in chunk_copies(j):
                copy.wait()
            gwi_ref[...] = mi_ref[:, c, :, at] + ci_ref[:, :, at]
            gwo_ref[0] = mo_ref[j, :, c] + co_ref[j]


def feed(size, comm, h1, cc, ct, wco, biases, wi, wo):
    rows, width = h1.shape
    wide = wi.shape[1]
    chunk = width
    count = wide // chunk

    def weight(s):
        return jnp.where(s < count, s, jnp.minimum(s - count, count - 1))

    def early(s):
        return jnp.clip(s - count, 0, count - 1)

    def late(s):
        return jnp.clip(s - count - 1, 0, count - 1)

    flat = whole((rows, width))
    square = whole((width, width))
    scratch = [
        pltpu.VMEM((count, rows, chunk), BF16),
        pltpu.VMEM((count, rows, chunk), F32),
        pltpu.VMEM((rows, width), F32),
        pltpu.VMEM((rows, 128), F32),
        pltpu.VMEM((rows, width), BF16),
        pltpu.VMEM((rows, width), F32),
        pltpu.VMEM((rows, width), BF16),
    ]
    if comm:
        narrow, broad = width // size, wide // size
        grad_specs = [
            pl.BlockSpec((size // 2, narrow, chunk), lambda s: (0, 0, late(s))),
            pl.BlockSpec((1, 2, broad, width), lambda s: (late(s), 0, 0, 0)),
        ]
        grad_shapes = [(size // 2, narrow, wide), (count, 2, broad, width)]
        scratch += [
            pltpu.VMEM((size // 2, 2, narrow, wide), BF16),
            pltpu.VMEM((count, 2, 2, broad, width), BF16),
            pltpu.VMEM((size // 2, narrow, wide), BF16),
            pltpu.VMEM((count, 2, broad, width), BF16),
            pltpu.SemaphoreType.DMA((2, count)),
            pltpu.SemaphoreType.DMA((2, count)),
        ]
    else:
        grad_specs = [
            pl.BlockSpec((width, chunk), lambda s: (0, early(s))),
            pl.BlockSpec((chunk, width), lambda s: (early(s), 0)),
        ]
        grad_shapes = [(width, wide), (wide, width)]
    return pl.pallas_call(
        functools.partial(feed_kernel, count, comm),
        grid=(2 * count + 1,),
        in_specs=[
            flat, flat, flat, square, whole(biases.shape),
            pl.BlockSpec((width, chunk), lambda s: (0, weight(s))),
            pl.BlockSpec((chunk, width), lambda s: (weight(s), 0)),
        ],
        out_specs=[flat, flat, flat, square]
        + grad_specs
        + [whole((8, width)), pl.BlockSpec((1, chunk), lambda s: (0, early(s)))],
        out_shape=[
            jax.ShapeDtypeStruct((rows, width), BF16),
            jax.ShapeDtypeStruct((rows, width), F32),
            jax.ShapeDtypeStruct((rows, width), BF16),
            jax.ShapeDtypeStruct((width, width), BF16),
        ]
        + [jax.ShapeDtypeStruct(a, BF16) for a in grad_shapes]
        + [
            jax.ShapeDtypeStruct((8, width), F32),
            jax.ShapeDtypeStruct((1, wide), F32),
        ],
        scratch_shapes=scratch,
        compiler_params=params(2 if comm else None),
        cost_estimate=cost(
            12 * rows * width * wide + 6 * rows * width * width, 12 * width * wide + 16 * rows * width
        ),
        name="feed",
    )(h1, cc, ct, wco, biases, wi, wo)


def first_back_kernel(
    dcq_ref, dh2_ref, h1_ref, ctx_ref, wcq_ref, wso_ref, b_ref,
    dh1_ref, dsc_ref, gcq_ref, gso_ref, small_ref,
):
    gain = b_ref[4:5]
    n1, r1 = normed(h1_ref[...])
    a1b = (n1 * gain + b_ref[5:6]).astype(BF16)
    dcq = dcq_ref[...]
    d1 = dh2_ref[...] + nt(dcq, wcq_ref[...])
    dh1 = norm_back(d1, n1, r1, gain)
    dh1_ref[...] = dh1
    dso = dh1.astype(BF16)
    dsc_ref[...] = nt(dso, wso_ref[...]).astype(BF16)
    gcq_ref[...] = tn(a1b, dcq).astype(BF16)
    gso_ref[...] = tn(ctx_ref[...], dso).astype(BF16)
    small_ref[0:1] = total(dcq)
    small_ref[1:2] = total(d1 * n1)
    small_ref[2:3] = total(d1)
    small_ref[3:4] = total(dso)
    small_ref[4:8] = jnp.zeros((4, dh1.shape[1]), F32)


def first_back(dcq, dh2, h1, ctx, wcq, wso, biases, schedule):
    rows, width = dcq.shape
    flat, square = whole((rows, width)), whole((width, width))
    return run(
        first_back_kernel, "first_back", 1,
        (dcq, dh2, h1, ctx, wcq, wso, biases),
        [flat, flat, flat, flat, square, square, whole(biases.shape)],
        [
            jax.ShapeDtypeStruct((rows, width), F32),
            jax.ShapeDtypeStruct((rows, width), BF16),
            jax.ShapeDtypeStruct((width, width), BF16),
            jax.ShapeDtypeStruct((width, width), BF16),
            jax.ShapeDtypeStruct((8, width), F32),
        ],
        [flat, flat, square, square, whole((8, width))],
        (), schedule, 4,
        8 * rows * width * width, 8 * width * width + 18 * rows * width,
    )


def outputs_kernel(places, count, *refs):
    pieces, rest = refs[:count], refs[count:]
    lines_ref, out_ref, dx_ref, dm_ref, dmi_ref = rest[:5]
    outs = rest[5:]
    for ref, (which, col) in zip(pieces, places):
        outs[which][:, col : col + ref.shape[1]] = ref[...].astype(F32)
    turned, result, dx, dm = outs[-4:]
    turned[...] = jnp.transpose(lines_ref[...].astype(F32))
    result[...] = out_ref[...]
    dx[...] = dx_ref[...]
    dm[...] = (dm_ref[...] + dmi_ref[...].astype(F32)).astype(BF16)


def outputs(pieces, places, shapes, lines, out, dx, dm, dmi):
    ins = tuple(pieces) + (lines, out, dx, dm, dmi)
    result = jax.ShapeDtypeStruct(out.shape, BF16)
    return pl.pallas_call(
        functools.partial(outputs_kernel, places, len(pieces)),
        out_shape=[jax.ShapeDtypeStruct(a, F32) for a in shapes]
        + [jax.ShapeDtypeStruct((128, lines.shape[0]), F32), result, result, result],
        compiler_params=params(),
        cost_estimate=cost(0, 12 << 20),
        name="outputs",
    )(*ins)


def swap_sum(part, axis, pairs):
    came = lax.ppermute(part, axis, pairs)
    return part.astype(F32) + came.astype(F32)


def sum_scatter(grad, size, order):
    rows, cols = grad.shape
    bits = size.bit_length() - 1
    me = lax.axis_index("dp")
    now = grad.reshape((2,) * bits + (rows // size, cols))
    left = list(range(bits))[::-1]
    for bit in [b for b in order if b < bits] + [b for b in range(bits) if b not in order]:
        axis = left.index(bit)
        mine = (me >> bit) & 1
        keep = lax.dynamic_index_in_dim(now, mine, axis, keepdims=False)
        send = lax.dynamic_index_in_dim(now, 1 - mine, axis, keepdims=False)
        came = lax.ppermute(send, "dp", [(i, i ^ (1 << bit)) for i in range(size)])
        now = (keep.astype(F32) + came.astype(F32)).astype(BF16)
        left.pop(axis)
    return swap_sum(now, "sp", [(0, 1), (1, 0)])


def per_device(
    size,
    inputs,
    memory,
    target_docs,
    memory_docs,
    cotangent,
    w_qkv,
    b_q,
    b_v,
    w_so,
    b_so,
    g_one,
    s_one,
    w_cq,
    b_cq,
    w_ckv,
    b_cv,
    w_co,
    b_co,
    g_two,
    s_two,
    w_fi,
    b_fi,
    w_fo,
    b_fo,
    g_three,
    s_three,
):
    rows, width = inputs.shape[1:]
    wide = b_fi.shape[0]
    comm = size == 16
    narrow, broad = width // size, wide // size
    swap = [(0, 1), (1, 0)]
    x, mem, ct = inputs[0], memory[0], cotangent[0]
    x_o = lax.ppermute(x, "sp", [(0, 1)])
    docs_o = lax.ppermute(jnp.concatenate([target_docs, memory_docs], axis=0), "sp", swap)
    line = lax.broadcasted_iota(jnp.int32, (24, width), 0)
    vectors = (b_q, b_v, b_cv, b_so, g_one, s_one, b_cq, b_co, g_two, s_two, b_fo, g_three, s_three)
    vectors += tuple(b_fi[i : i + width] for i in range(0, wide, width))
    biases = jnp.zeros((24, width), F32)
    for i, v in enumerate(vectors):
        biases = jnp.where(line == i, v.astype(F32)[None], biases)

    qkv, mkv, t_own, m_own = project_own(x, mem, target_docs, memory_docs, w_qkv, w_ckv, biases)
    kvo, mem_s, t_oth, m_oth = project_other(x_o, mem, docs_o[:1], docs_o[1:], w_qkv, biases, t_own)
    mem_o = lax.ppermute(mem_s, "sp", swap)
    ctx, lse = self_forward(qkv, kvo, t_own, t_oth)
    h1, cq = first_norm(x, ctx, w_so, w_cq, biases)
    mkvo = project_memory(mem_o, w_ckv, biases)
    cc, clse = cross_forward(cq, mkv, mkvo, t_own, m_own, m_oth)
    output, dh2, dcc, gco, gwi, gwo, small_a, gib = feed(
        size, comm, h1, cc, ct, w_co, biases, w_fi, w_fo
    )
    turned = gib.reshape(width, -1).T

    def flow(array, hops, first=0, cols=None, before=("core",)):
        shape = (2, 2, 2, 2, narrow, array.shape[1])
        return Flow(array.reshape(shape), shape, before + hops, BLOCK, (first, cols or array.shape[1]))

    at_cross, at_first, at_self = (), (), ()
    if comm:
        gwi = gwi.reshape(2, 2, 2, narrow, wide)
        gwo = gwo.reshape(2, 2, 2, broad, width)
        third = wide // 3
        t0 = [
            Flow(gwi, gwi.shape, hops, BLOCK[:3], (i * third, third)) for i, hops in enumerate((VIA_X, VIA_Y, VIA_Z))
        ] + [
            Flow(gwo, gwo.shape, hops, BLOCK[:3], (i * 256, 256)) for i, hops in enumerate((VIA_X, VIA_Y, VIA_Z))
        ]
        late = [f for f in t0 if "yg" in f.hops]
        early = [flow(gco, VIA_Y)]
        at_cross = ((t0, 0, 4), (t0, 4, 6), (early, 0, 6))
    dcq, dm, dmo, gck, gcv, gcvb = cross_backward(
        cq, mkv, mkvo, dcc, cc, clse, t_own, m_own, m_oth, mem, mem_o, w_ckv, at_cross
    )
    dm_in = lax.ppermute(dmo, "sp", swap)
    if comm:
        at_first = ((t0, 0, 1),)
    dh1, dsc, gcq, gso, small_b = first_back(dcq, dh2, h1, ctx, w_cq, w_so, biases, at_first)
    if comm:
        fresh = [flow(gck, VIA_X), flow(gcv, VIA_Z)] + [
            flow(g, hops, 256 * i, 256) for g in (gcq, gso) for i, hops in enumerate((VIA_X, VIA_Y, VIA_Z))
        ]
        t1 = early + fresh
    block = (2, 2, 2, 2, narrow) if comm else (width,)
    if comm:

        def group(first, cols):
            return [
                Flow(("ref", GRADS, i), block + (width,), ("core",) + hops, BLOCK, (first, cols))
                for i, hops in enumerate((VIA_X, VIA_Z, VIA_Y))
            ]

        cut = 2 * width // 3
        front, back = group(0, cut), group(cut, width - cut)
        sm = Flow(("ref", GRADS + 1), block + (128,), ("core",) + VIA_X, BLOCK)
        rest = back + [sm]
        t1_late = [f for f in t1 if "yg" in f.hops]
        front_late, back_late = front[1:], back[1:]
        at_self = (
            (t0, 0, 3), (late, 3, 6),
            (fresh, 0, 2), (t1, 2, 7), (t1, 7, 9), (t1, 9, 10), (t1, 10, 11), (t1_late, 11, 12),
            (front, 10, 11), (front, 11, 12), (front, 12, 13), (front, 13, 14), (front, 14, 15), (front_late, 15, 16),
            (rest, 12, 13), (rest, 13, 14), (rest, 14, 15), (rest, 15, 16), (rest, 16, 17), (back_late, 17, 18),
        )
    dx, *made = self_backward(
        block, qkv, kvo, dsc, ctx, lse, t_own, t_oth, x, x_o, w_qkv, dh1, (small_a, small_b, gcvb, turned), at_self
    )
    if comm:
        pieces, places = [], []
        for flows, which in (
            ([f for both in zip(front, back) for f in both], 0), (t1[1:3], 1), (t0[:3], 2), (t0[3:], 3), (t1[:1], 4), (t1[3:6], 5), (t1[6:], 6)
        ):
            col = 0
            for f in flows:
                pieces.append(f.array)
                places.append((which, col))
                col += f.shape[-1]
        shapes = [(narrow, 3 * width), (narrow, 2 * width), (narrow, wide), (broad, width)] + [(narrow, width)] * 3
        t_qkv, t_cmem, t_fin, t_fout, t_cout, t_cquery, t_out, lines, output, derivative, grad_memory = outputs(
            pieces, places, shapes, sm.array, output, dx, dm, dm_in
        )
    else:
        gqkv, columns = made
        t_fin, t_fout, t_cout, t_cquery, t_out, t_cmem, t_qkv, lines = (
            sum_scatter(g, size, (0, 1, 2, 3))
            for g in (
                gwi, gwo, gco, gcq, gso, jnp.concatenate([gck, gcv], axis=1),
                jnp.concatenate([gqkv[0], gqkv[1], gqkv[2]], axis=1), columns,
            )
        )
        lines, derivative = lines.T, dx
        grad_memory = (dm + dm_in.astype(F32)).astype(BF16)
    t_gthree, t_sthree, t_fobias, t_gtwo, t_stwo, t_cobias = (lines[i] for i in range(6))
    t_cqbias, t_gone, t_sone, t_obias = (lines[i] for i in range(8, 12))
    t_cvbias, t_qbias, t_vbias = lines[16], lines[21], lines[22]
    t_fibias = lines[17:21].T.reshape(-1)
    return (
        output[None],
        derivative[None],
        grad_memory[None],
        t_qkv,
        t_qbias,
        t_vbias,
        t_out,
        t_obias,
        t_gone,
        t_sone,
        t_cquery,
        t_cqbias,
        t_cmem,
        t_cvbias,
        t_cout,
        t_cobias,
        t_gtwo,
        t_stwo,
        t_fin,
        t_fibias,
        t_fout,
        t_fobias,
        t_gthree,
        t_sthree,
    )


def solution(mesh):
    split = P("dp", "sp", None)
    in_specs = (split, split, P("dp", "sp"), P("dp", "sp"), split) + (P(),) * 21
    matrix, vector = P("dp", None), P("dp")
    out_specs = (
        split, split, split,
        matrix, vector, vector,
        matrix, vector, vector, vector,
        matrix, vector,
        matrix, vector,
        matrix, vector, vector, vector,
        matrix, vector,
        matrix, vector, vector, vector,
    )
    return jax.shard_map(
        functools.partial(per_device, mesh.shape["dp"]),
        mesh=mesh, in_specs=in_specs, out_specs=out_specs, check_vma=False,
    )
```

```python
import functools

import jax
import jax.numpy as jnp
from jax import lax
from jax.experimental import pallas as pl
from jax.experimental.pallas import tpu as pltpu
from jax.sharding import PartitionSpec as P

HD = 64
PAIR = 2 * HD
EPS = 1e-05
FAR = 1.0e9
VMEM = 60 * 1024 * 1024
F32 = jnp.float32
BF16 = jnp.bfloat16


def nn(a, b):
    return lax.dot_general(a, b, (((1,), (0,)), ((), ())), preferred_element_type=F32)


def nt(a, b):
    return lax.dot_general(a, b, (((1,), (1,)), ((), ())), preferred_element_type=F32)


def tn(a, b):
    return lax.dot_general(a, b, (((0,), (0,)), ((), ())), preferred_element_type=F32)


def params(collective=None):
    if collective is None:
        return pltpu.CompilerParams(vmem_limit_bytes=VMEM)
    return pltpu.CompilerParams(
        vmem_limit_bytes=VMEM, collective_id=collective, has_side_effects=True
    )


def cost(flops, moved):
    return pl.CostEstimate(flops=int(flops), bytes_accessed=int(moved), transcendentals=0)


def normed(h):
    centred = h - jnp.mean(h, axis=-1, keepdims=True)
    rstd = lax.rsqrt(jnp.mean(centred * centred, axis=-1, keepdims=True) + EPS)
    return centred * rstd, rstd


def norm_back(grad, n, rstd, gain):
    scaled = grad * gain
    centre = jnp.mean(scaled, axis=-1, keepdims=True)
    along = jnp.mean(scaled * n, axis=-1, keepdims=True)
    return rstd * (scaled - centre - n * along)


def total(a):
    return jnp.sum(a.astype(F32), axis=0, keepdims=True)


def place():
    me = lax.axis_index("dp")
    return me, me % 2, (me // 2) % 2, me // 4


def partner(hop, at=None):
    me, c, x, z = at or place()
    if hop == "core":
        return {"dp": me + 1 - 2 * c}
    if hop == "x":
        return {"dp": me + 2 - 4 * x}
    if hop == "z1":
        return {"dp": me + 4 - 8 * (z % 2)}
    if hop == "z2":
        return {"dp": me + 8 - 16 * (z // 2)}
    return {"sp": 1 - lax.axis_index("sp")}


def greet(hops, at=None):
    hops = sorted({"y" if h[0] == "y" else h for h in hops})
    barrier = pltpu.get_barrier_semaphore()
    for hop in hops:
        pl.semaphore_signal(barrier, inc=1, device_id=partner(hop, at), device_id_type=pl.DeviceIdType.MESH)
    pl.semaphore_wait(barrier, len(hops))


def remote(src, dst, send, recv, hop, at=None):
    return pltpu.make_async_remote_copy(
        src_ref=src, dst_ref=dst, send_sem=send, recv_sem=recv,
        device_id=partner(hop, at), device_id_type=pl.DeviceIdType.MESH,
    )


VIA_X = ("x", "z1", "z2", "y")
VIA_Y = ("yr", "x", "z1", "z2", "yg")
VIA_Z = ("z1", "yr", "x", "z2", "yg")
BLOCK = ("z2", "z1", "x", "core")


class Part:
    def __init__(self, hop, shape, dims, cols=None):
        self.hop, self.dims = hop, dims
        self.cols = cols or (0, shape[-1])
        self.shape = shape = tuple(shape[:-1]) + (self.cols[1],)
        if hop in dims:
            at = dims.index(hop)
            self.after, self.left = shape[:at] + shape[at + 1 :], dims[:at] + dims[at + 1 :]
        else:
            wide = shape[-1]
            wide = wide // 2 if hop == "yr" else 2 * wide if hop == "yg" else wide
            self.after, self.left = shape[:-1] + (wide,), dims
        self.came = shape if hop == "yg" else self.after

    def stay(self, at_dp, sp):
        _, c, x, z = at_dp
        first, wide = self.cols
        index = [slice(None)] * (len(self.shape) - 1) + [pl.ds(first, wide)]
        if self.hop in self.dims:
            mine = {"core": c, "x": x, "z1": z % 2, "z2": z // 2}[self.hop]
            index[self.dims.index(self.hop)] = mine
        elif self.hop == "yr":
            half = wide // 2
            index[-1] = pl.ds(pl.multiple_of(first + sp * half, 128), half)
        return tuple(index)

    def away(self, at_dp, sp):
        me, c, x, z = at_dp
        if self.hop in self.dims or self.hop == "yr":
            return self.stay((me, 1 - c, 1 - x, (1 - z // 2) * 2 + 1 - z % 2), 1 - sp)
        return self.stay(at_dp, sp)

    def copies(self, src, held, made, came, send, recv, local, at_dp, sp):
        out = [remote(src.at[self.away(at_dp, sp)], came, send, recv, self.hop, at_dp)]
        if not held:
            out.append(pltpu.make_async_copy(src.at[self.stay(at_dp, sp)], made, local))
        return out

    def add(self, src, held, made, came, at_dp, sp):
        if self.hop == "yg":
            wide = self.shape[-1]
            lead = (slice(None),) * (len(self.shape) - 1)
            made[lead + (pl.ds(pl.multiple_of(sp * wide, 128), wide),)] = src[self.stay(at_dp, sp)]
            made[lead + (pl.ds(pl.multiple_of((1 - sp) * wide, 128), wide),)] = came[...]
        elif held:
            made[...] = src[self.stay(at_dp, sp)] + came[...]
        else:
            made[...] += came[...]


class Flow:
    def __init__(self, array, shape, hops, dims=BLOCK, cols=None):
        self.array, self.shape, self.dims, self.cols = array, tuple(shape), dims, cols
        self.hops = list(hops)

    def step(self):
        part = Part(self.hops.pop(0), self.shape, self.dims, self.cols)
        self.shape, self.dims, self.cols = part.after, part.left, None
        return part


class Window:
    def __init__(self, start, stop, joint):
        self.start, self.stop, self.joint = start, stop, joint
        self.parts, self.sources, self.keeps = [], [], []


class Joint:
    def __init__(self):
        self.window = None


def plan(schedule):
    windows, arrays, latest = [], [], {}
    for n, (flows, start, stop, *joint) in enumerate(schedule):
        window = Window(start, stop, bool(joint))
        if joint:
            joint[0].window = n
        for i, flow in enumerate(flows):
            if flow in latest:
                source = ("part",) + latest[flow]
                before = windows[latest[flow][0]]
                before.keeps[latest[flow][1]] = False
            elif isinstance(flow.array, Joint):
                source = ("joint", flow.array.window)
            elif isinstance(flow.array, tuple):
                source = flow.array
            else:
                known = [k for k, a in enumerate(arrays) if a is flow.array]
                if not known:
                    arrays.append(flow.array)
                source = ("in", known[0] if known else len(arrays) - 1)
            window.parts.append(flow.step())
            window.sources.append(source)
            window.keeps.append(not joint)
            if not joint:
                latest[flow] = (n, i)
        windows.append(window)
    return windows, arrays, latest


def carrying(body, own, windows, arrays, grid, also, finale):
    ins, outs, held = own

    def kernel(*refs):
        refs = list(refs)

        def take(n):
            got = refs[:n]
            del refs[:n]
            return got

        my_in, arr = take(ins), take(arrays)
        my_out = take(outs)
        given = [[take(1)[0] if k else None for k in w.keeps] for w in windows]
        my_held = take(held)
        made, came, joints = [], [], []
        for w, g in zip(windows, given):
            if w.joint:
                joint, col, views = take(1)[0], 0, []
                for q in w.parts:
                    views.append(joint.at[(slice(None),) * (len(q.after) - 1) + (pl.ds(col, q.after[-1]),)])
                    col += q.after[-1]
                joints.append(joint)
                made.append(views)
            else:
                joints.append(None)
                made.append([ref if ref is not None else take(1)[0] for ref in g])
            came.append(take(len(w.parts)))
        mine = my_in + my_out + my_held
        step = pl.program_id(0)
        hops = [q.hop for w in windows for q in w.parts] + list(also)
        if hops:
            at_dp, sp = place(), lax.axis_index("sp")
            pl.when(step == 0)(lambda: greet(hops, at_dp))
        if windows:
            send, recv, local = refs
        copies, sources, base = [], [], 0
        for w, m, c in zip(windows, made, came):
            now, froms = [], []
            for i, q in enumerate(w.parts):
                kind = w.sources[i]
                if kind[0] == "in":
                    src = arr[kind[1]]
                elif kind[0] == "ref":
                    src = mine[kind[1]]
                elif kind[0] == "joint":
                    src = joints[kind[1]]
                else:
                    src = made[kind[1]][kind[2]]
                held_here = kind[0] != "in"
                froms.append((src, held_here))
                now += q.copies(
                    src, held_here, m[i], c[i], send.at[base], recv.at[base], local.at[base], at_dp, sp
                )
                base += 1
            copies.append(now)
            sources.append(froms)

        def phase(number):
            for n, w in enumerate(windows):
                if w.stop == number:
                    for copy in copies[n]:
                        copy.wait()
                    for q, (src, here), m, c in zip(w.parts, sources[n], made[n], came[n]):
                        q.add(src, here, m, c, at_dp, sp)
            for n, w in enumerate(windows):
                if w.start == number:
                    for copy in copies[n]:
                        copy.start()

        used = sorted({w.start for w in windows} | {w.stop for w in windows})
        for number in used:
            if number < grid:
                pl.when(step == number)(functools.partial(phase, number))
        body(*mine)
        for number in used:
            if number >= grid:
                pl.when(step == grid - 1)(functools.partial(phase, number))
        if finale:
            pl.when(step == grid - 1)(lambda: finale(*mine))

    return kernel


def run(
    body, name, grid, ins, in_specs, outs, out_specs, held=(), schedule=(), collective=None,
    flops=0, moved=0, also=(), finale=None,
):
    in_specs, outs, out_specs, held = list(in_specs), list(outs), list(out_specs), list(held)
    windows, arrays, latest = plan(schedule)
    own = len(outs)
    kernel = carrying(body, (len(ins), own, len(held)), windows, len(arrays), grid, also, finale)
    in_specs += [pl.BlockSpec(memory_space=pl.ANY)] * len(arrays)
    order, count = [], 0
    for n, w in enumerate(windows):
        if w.joint:
            shape = w.parts[0].after[:-1] + (sum(q.after[-1] for q in w.parts),)
            held.append(pltpu.VMEM(shape, BF16))
        for i, (q, k) in enumerate(zip(w.parts, w.keeps)):
            if w.joint:
                continue
            if k:
                outs.append(jax.ShapeDtypeStruct(q.after, BF16))
                out_specs.append(whole(q.after))
                order.append((n, i))
            else:
                held.append(pltpu.VMEM(q.after, BF16))
        held += [pltpu.VMEM(q.came, BF16) for q in w.parts]
        count += len(w.parts)
    if windows:
        held += [pltpu.SemaphoreType.DMA((count,))] * 3
    results = pl.pallas_call(
        kernel,
        grid=(grid,),
        in_specs=in_specs,
        out_specs=out_specs,
        out_shape=outs,
        scratch_shapes=held,
        compiler_params=params(collective if windows or also else None),
        cost_estimate=cost(flops, moved),
        name=name,
    )(*ins, *arrays)
    for flow, where in latest.items():
        flow.array = results[own + order.index(where)]
    return results[:own]


def code_of(docs_ref):
    row = lax.broadcasted_iota(jnp.int32, (128, docs_ref.shape[1]), 0)
    return jnp.transpose(jnp.where(docs_ref[...] == row, 1.0, 0.0)).astype(BF16)


def project_own_kernel(x_ref, m_ref, td_ref, md_ref, wx_ref, wm_ref, b_ref, qkv_ref, mkv_ref, to_ref, mo_ref):
    step = pl.program_id(0)

    @pl.when(step == 0)
    def _():
        to_ref[...] = code_of(td_ref)
        mo_ref[...] = code_of(md_ref)

    @pl.when(step < 3)
    def _():
        bias = jnp.where(step == 0, b_ref[0:1], 0.0) + jnp.where(step == 2, b_ref[1:2], 0.0)
        qkv_ref[...] = (nn(x_ref[...], wx_ref[...]) + bias).astype(BF16)

    @pl.when(step >= 3)
    def _():
        bias = jnp.where(step == 4, b_ref[2:3], 0.0)
        mkv_ref[...] = (nn(m_ref[...], wm_ref[...]) + bias).astype(BF16)


def project_own(x, mem, td, md, wx, wm, biases):
    rows, width = x.shape
    code = jax.ShapeDtypeStruct((rows, 128), BF16)
    return pl.pallas_call(
        project_own_kernel,
        grid=(5,),
        in_specs=[
            whole((rows, width)), whole((rows, width)), whole((1, rows)), whole((1, rows)),
            pl.BlockSpec((width, width), lambda s: (0, jnp.minimum(s, 2))),
            pl.BlockSpec((width, width), lambda s: (0, jnp.maximum(s - 3, 0))),
            whole(biases.shape),
        ],
        out_specs=[
            pl.BlockSpec((rows, width), lambda s: (0, jnp.minimum(s, 2))),
            pl.BlockSpec((rows, width), lambda s: (0, jnp.maximum(s - 3, 0))),
            whole((rows, 128)), whole((rows, 128)),
        ],
        out_shape=[
            jax.ShapeDtypeStruct((rows, 3 * width), BF16), jax.ShapeDtypeStruct((rows, 2 * width), BF16), code, code,
        ],
        compiler_params=params(),
        cost_estimate=cost(10 * rows * width * width, 20 * width * width),
        name="project_own",
    )(x, mem, td, md, wx, wm, biases)


def project_other_kernel(x_ref, m_ref, td_ref, md_ref, wx_ref, b_ref, after_ref, kvo_ref, mem_ref, tt_ref, mt_ref):
    step = pl.program_id(0)

    @pl.when(step == 0)
    def _():
        mem_ref[...] = m_ref[...]
        tt_ref[...] = code_of(td_ref)
        mt_ref[...] = code_of(md_ref)

    @pl.when(lax.axis_index("sp") == 1)
    def _():
        bias = jnp.where(step == 1, b_ref[1:2], 0.0)
        kvo_ref[...] = (nn(x_ref[...], wx_ref[...]) + bias).astype(BF16)

    @pl.when(lax.axis_index("sp") == 0)
    def _():
        kvo_ref[...] = jnp.zeros(kvo_ref.shape, BF16)


def project_other(x, mem, td, md, wx, biases, after):
    rows, width = x.shape
    code = jax.ShapeDtypeStruct((rows, 128), BF16)
    return pl.pallas_call(
        project_other_kernel,
        grid=(2,),
        in_specs=[
            whole((rows, width)), whole((rows, width)), whole((1, rows)), whole((1, rows)),
            pl.BlockSpec((width, width), lambda s: (0, s + 1)),
            whole(biases.shape),
            pl.BlockSpec(memory_space=pl.ANY),
        ],
        out_specs=[
            pl.BlockSpec((rows, width), lambda s: (0, s)),
            whole((rows, width)), whole((rows, 128)), whole((rows, 128)),
        ],
        out_shape=[
            jax.ShapeDtypeStruct((rows, 2 * width), BF16), jax.ShapeDtypeStruct((rows, width), BF16), code, code,
        ],
        compiler_params=params(),
        cost_estimate=cost(4 * rows * width * width, 10 * width * width),
        name="project_other",
    )(x, mem, td, md, wx, biases, after)


def project_memory_kernel(x_ref, w_ref, b_ref, o_ref):
    bias = jnp.where(pl.program_id(0) == 1, b_ref[2:3], 0.0)
    o_ref[...] = (nn(x_ref[...], w_ref[...]) + bias).astype(BF16)


def project_memory(x, w, biases):
    rows, width = x.shape
    return pl.pallas_call(
        project_memory_kernel,
        grid=(2,),
        in_specs=[
            whole((rows, width)),
            pl.BlockSpec((width, width), lambda j: (0, j)),
            whole(biases.shape),
        ],
        out_specs=pl.BlockSpec((rows, width), lambda j: (0, j)),
        out_shape=jax.ShapeDtypeStruct((rows, 2 * width), BF16),
        compiler_params=params(),
        cost_estimate=cost(4 * rows * width * width, 4 * width * (width + rows)),
        name="project_memory",
    )(x, w, biases)


def head_masks(dtype):
    lane = lax.broadcasted_iota(jnp.int32, (1, PAIR), 1)
    low = jnp.where(lane < HD, 1.0, 0.0)
    return low.astype(dtype), (1.0 - low).astype(dtype)


def query_code(code):
    lane = lax.broadcasted_iota(jnp.int32, code.shape, 1)
    return jnp.where(lane < 4, (code.astype(F32) - 1.0) * FAR, 0.0).astype(BF16)


def softmax_pieces(scores, values):
    peak = functools.reduce(jnp.maximum, [jnp.max(s, axis=-1, keepdims=True) for s in scores])
    expd = [jnp.exp(s - peak) for s in scores]
    norm = sum(jnp.sum(e, axis=-1, keepdims=True) for e in expd)
    out = sum(nn(e.astype(BF16), v) for e, v in zip(expd, values))
    return out / norm, peak + jnp.log(norm)


def self_pieces(block, size, both, own, other):
    pieces = []
    if both:
        pieces.append((other, False))
    if block:
        pieces.append((own[: block * size], False))
    pieces.append((own[block * size : (block + 1) * size], True))
    return pieces


def store_lse(lse_ref, block, size, low, high):
    lane = lax.broadcasted_iota(jnp.int32, (size, PAIR), 1)
    both = jnp.where(lane == 0, low, high)
    lse_ref[:, block * size : (block + 1) * size] = jnp.transpose(both)[:8]


def self_forward_kernel(size, q_ref, k_ref, v_ref, ko_ref, vo_ref, own_ref, oth_ref, o_ref, lse_ref):
    second = lax.axis_index("sp") == 1
    rows = q_ref.shape[0]
    masks = head_masks(BF16)
    outs = head_masks(F32)

    def run(both):
        qcode = query_code(own_ref[...])
        own = jnp.concatenate([k_ref[...], own_ref[...]], axis=1)
        oth = jnp.concatenate([ko_ref[...], oth_ref[...]], axis=1) if both else None
        vown = v_ref[...]
        voth = vo_ref[...] if both else None
        for block in range(rows // size):
            at = slice(block * size, (block + 1) * size)
            lses, result = [], 0.0
            for mask, keep in zip(masks, outs):
                q = jnp.concatenate([q_ref[at] * (mask * BF16(HD**-0.5)), qcode[at]], axis=1)
                scores = []
                for keys, diagonal in self_pieces(block, size, both, own, oth):
                    s = nt(q, keys)
                    if diagonal:
                        row = lax.broadcasted_iota(jnp.int32, s.shape, 0)
                        col = lax.broadcasted_iota(jnp.int32, s.shape, 1)
                        s = jnp.where(row >= col, s, -FAR)
                    scores.append(s)
                values = [v for v, _ in self_pieces(block, size, both, vown, voth)]
                out, lse = softmax_pieces(scores, values)
                result = result + out * keep
                lses.append(lse)
            o_ref[at] = result.astype(BF16)
            store_lse(lse_ref, block, size, *lses)

    pl.when(second)(lambda: run(True))
    pl.when(jnp.logical_not(second))(lambda: run(False))


def pair_spec(rows, offset):
    return pl.BlockSpec((rows, PAIR), lambda p: (0, p + offset))


def whole(shape):
    return pl.BlockSpec(shape, lambda *_: (0,) * len(shape))


def self_forward(qkv, kvo, own, oth):
    rows = qkv.shape[0]
    width = qkv.shape[1] // 3
    pairs = width // PAIR
    return pl.pallas_call(
        functools.partial(self_forward_kernel, 256),
        grid=(pairs,),
        in_specs=[
            pair_spec(rows, 0),
            pair_spec(rows, pairs),
            pair_spec(rows, 2 * pairs),
            pair_spec(rows, 0),
            pair_spec(rows, pairs),
            whole((rows, 128)),
            whole((rows, 128)),
        ],
        out_specs=[pair_spec(rows, 0), pl.BlockSpec((8, rows), lambda p: (p, 0))],
        out_shape=[
            jax.ShapeDtypeStruct((rows, width), BF16),
            jax.ShapeDtypeStruct((8 * pairs, rows), F32),
        ],
        compiler_params=params(),
        cost_estimate=cost(16 * rows * rows * width, 16 * rows * width),
        name="self_forward",
    )(qkv, qkv, qkv, kvo, kvo, own, oth)


def cross_forward_kernel(size, q_ref, k_ref, v_ref, ko_ref, vo_ref, t_ref, own_ref, oth_ref, o_ref, lse_ref):
    rows = q_ref.shape[0]
    masks = head_masks(BF16)
    outs = head_masks(F32)
    qcode = query_code(t_ref[...])
    keys = [
        jnp.concatenate([k_ref[...], own_ref[...]], axis=1),
        jnp.concatenate([ko_ref[...], oth_ref[...]], axis=1),
    ]
    values = [v_ref[...], vo_ref[...]]
    for block in range(rows // size):
        at = slice(block * size, (block + 1) * size)
        lses, result = [], 0.0
        for mask, keep in zip(masks, outs):
            q = jnp.concatenate([q_ref[at] * (mask * BF16(HD**-0.5)), qcode[at]], axis=1)
            out, lse = softmax_pieces([nt(q, k) for k in keys], values)
            result = result + out * keep
            lses.append(lse)
        o_ref[at] = result.astype(BF16)
        store_lse(lse_ref, block, size, *lses)


def cross_forward(cq, kv, kvo, t, own, oth):
    rows, width = cq.shape
    pairs = width // PAIR
    return pl.pallas_call(
        functools.partial(cross_forward_kernel, 256),
        grid=(pairs,),
        in_specs=[
            pair_spec(rows, 0),
            pair_spec(rows, 0),
            pair_spec(rows, pairs),
            pair_spec(rows, 0),
            pair_spec(rows, pairs),
            whole((rows, 128)),
            whole((rows, 128)),
            whole((rows, 128)),
        ],
        out_specs=[pair_spec(rows, 0), pl.BlockSpec((8, rows), lambda p: (p, 0))],
        out_shape=[
            jax.ShapeDtypeStruct((rows, width), BF16),
            jax.ShapeDtypeStruct((8 * pairs, rows), F32),
        ],
        compiler_params=params(),
        cost_estimate=cost(24 * rows * rows * width, 16 * rows * width),
        name="cross_forward",
    )(cq, kv, kv, kvo, kvo, t, own, oth)


def delta_rows(g, o):
    prod = g.astype(F32) * o.astype(F32)
    upper = prod.astype(BF16)
    lower = (prod - upper.astype(F32)).astype(BF16)
    row = lax.broadcasted_iota(jnp.int32, (8, PAIR), 0)
    lane = lax.broadcasted_iota(jnp.int32, (8, PAIR), 1)
    pick = jnp.where(row == lane // HD, 1.0, 0.0).astype(BF16)
    return nt(pick, upper) + nt(pick, lower)


def back_piece(keys, values, q, g, lse, delta, causal):
    s = nt(keys, q)
    if causal:
        row = lax.broadcasted_iota(jnp.int32, s.shape, 0)
        col = lax.broadcasted_iota(jnp.int32, s.shape, 1)
        s = jnp.where(row <= col, s, -FAR)
    p = jnp.exp(s - lse)
    ds = p * (nt(values, g) - delta)
    return p.astype(BF16), ds.astype(BF16)


def cross_backward_kernel(
    size, q_ref, k_ref, v_ref, ko_ref, vo_ref, g_ref, o_ref, lse_ref, t_ref, own_ref, oth_ref,
    m_ref, mo_ref, wk_ref, wv_ref,
    dq_ref, dm_ref, dmo_ref, gk_ref, gv_ref, gb_ref, dm_acc, dmo_acc, mt_ref, mot_ref,
):
    step = pl.program_id(0)

    @pl.when(step == 0)
    def _():
        mt_ref[...] = jnp.transpose(m_ref[...])
        mot_ref[...] = jnp.transpose(mo_ref[...])

    rows = q_ref.shape[0]
    masks = head_masks(BF16)
    scale = BF16(HD**-0.5)
    qcode = query_code(t_ref[...])
    delta = delta_rows(g_ref[...], o_ref[...])
    lse = lse_ref[...]
    halves = [(k_ref, v_ref, own_ref, mt_ref, dm_acc), (ko_ref, vo_ref, oth_ref, mot_ref, dmo_acc)]
    dq = [0.0] * (rows // size)
    gk = gv = gb = 0.0
    for kr, vr, code, mem, acc in halves:
        keys = jnp.concatenate([kr[...], code[...]], axis=1)
        values = vr[...]
        dk = dv = 0.0
        for block in range(rows // size):
            at = slice(block * size, (block + 1) * size)
            for head, mask in enumerate(masks):
                qm = q_ref[at] * (mask * scale)
                gm = g_ref[at] * mask
                q = jnp.concatenate([qm, qcode[at]], axis=1)
                p, ds = back_piece(
                    keys, values, q, gm, lse[head : head + 1, at], delta[head : head + 1, at], False
                )
                dk = dk + nn(ds, qm)
                dv = dv + nn(p, gm)
                dq[block] = dq[block] + tn(ds, kr[...] * (mask * scale))
        both = jnp.concatenate([dk.astype(BF16), dv.astype(BF16)], axis=1)
        grad = nn(mem[...], both)
        gk, gv = gk + grad[:, :PAIR], gv + grad[:, PAIR:]
        gb = gb + total(both[:, PAIR:])
        dm = nt(both, jnp.concatenate([wk_ref[...], wv_ref[...]], axis=1))

        @pl.when(step == 0)
        def _():
            acc[...] = dm

        @pl.when(step > 0)
        def _():
            acc[...] += dm
    for block in range(rows // size):
        dq_ref[block * size : (block + 1) * size] = dq[block].astype(BF16)
    gk_ref[...] = gk.astype(BF16)
    gv_ref[...] = gv.astype(BF16)
    gb_ref[...] = gb

    @pl.when(step == pl.num_programs(0) - 1)
    def _():
        dm_ref[...] = dm_acc[...]
        dmo_ref[...] = dmo_acc[...].astype(BF16)


def cross_backward(cq, kv, kvo, g, o, lse, t, own, oth, m, mo, w, schedule):
    rows, width = cq.shape
    pairs = width // PAIR
    flat = jax.ShapeDtypeStruct((rows, width), BF16)
    square = jax.ShapeDtypeStruct((width, width), BF16)
    return run(
        functools.partial(cross_backward_kernel, 256), "cross_backward", pairs,
        (cq, kv, kv, kvo, kvo, g, o, lse, t, own, oth, m, mo, w, w),
        [
            pair_spec(rows, 0),
            pair_spec(rows, 0),
            pair_spec(rows, pairs),
            pair_spec(rows, 0),
            pair_spec(rows, pairs),
            pair_spec(rows, 0),
            pair_spec(rows, 0),
            pl.BlockSpec((8, rows), lambda p: (p, 0)),
            whole((rows, 128)),
            whole((rows, 128)),
            whole((rows, 128)),
            whole((rows, width)),
            whole((rows, width)),
            pair_spec(width, 0),
            pair_spec(width, pairs),
        ],
        [flat, jax.ShapeDtypeStruct((rows, width), F32), flat, square, square, jax.ShapeDtypeStruct((1, width), F32)],
        [pair_spec(rows, 0)] + [whole((rows, width))] * 2 + [pair_spec(width, 0)] * 2 + [pair_spec(1, 0)],
        [pltpu.VMEM((rows, width), F32)] * 2 + [pltpu.VMEM((width, rows), BF16)] * 2,
        schedule, 3,
        64 * rows * rows * width + 16 * rows * width * width, 24 * rows * width,
    )


def front_pairs(pairs):
    return 2 * pairs // 3


def self_backward_kernel(
    size, q_ref, k_ref, v_ref, ko_ref, vo_ref, g_ref, o_ref, lse_ref, own_ref, oth_ref,
    x_ref, xo_ref, wq_ref, wk_ref, wv_ref, dh1_ref, sa_ref, sb_ref, sc_ref, sd_ref,
    dx_ref, grad_ref,
    dq_acc, dx_acc, dxo_acc, dkv_acc, xt_ref, xot_ref, dxo_ref, came_ref, turn_ref, send_ref, recv_ref,
):
    step = pl.program_id(0)
    sp = lax.axis_index("sp")
    second = sp == 1
    rows, width = x_ref.shape
    pairs = width // PAIR
    pair = lax.rem(step, pairs)
    cols = pl.ds(pl.multiple_of(pair * PAIR, PAIR), PAIR)
    masks = head_masks(BF16)
    scale = BF16(HD**-0.5)
    count = rows // size
    over = remote(dxo_ref, came_ref, send_ref.at[0], recv_ref.at[0], "y")

    def pieces():
        qcode = query_code(own_ref[...])
        delta = delta_rows(g_ref[...], o_ref[...])
        for block in range(count):
            at = slice(block * size, (block + 1) * size)
            for head, mask in enumerate(masks):
                qm = q_ref[at] * (mask * scale)
                gm = g_ref[at] * mask
                q = jnp.concatenate([qm, qcode[at]], axis=1)
                yield block, mask, qm, gm, q, lse_ref[head : head + 1, at], delta[head : head + 1, at]

    @pl.when(step == 0)
    def _():
        xt_ref[...] = jnp.transpose(x_ref[...])
        turn_ref[...] = jnp.zeros(turn_ref.shape, F32)
        turn_ref[0:8] = sa_ref[...]
        turn_ref[8:16] = sb_ref[...]
        turn_ref[16:17] = sc_ref[...]
        turn_ref[17:21] = sd_ref[...]

    @pl.when(jnp.logical_and(step == 0, second))
    def _():
        xot_ref[...] = jnp.transpose(xo_ref[...])

    @pl.when(jnp.logical_and(step < pairs, second))
    def _():
        keys = jnp.concatenate([ko_ref[...], oth_ref[...]], axis=1)
        values = vo_ref[...]
        dk = dv = 0.0
        dq = [0.0] * count
        for block, mask, qm, gm, q, lse, delta in pieces():
            p, ds = back_piece(keys, values, q, gm, lse, delta, False)
            dk = dk + nn(ds, qm)
            dv = dv + nn(p, gm)
            dq[block] = dq[block] + tn(ds, ko_ref[...] * (mask * scale))
        for block in range(count):
            dq_acc[pair, block * size : (block + 1) * size] = dq[block]
        both = jnp.concatenate([dk.astype(BF16), dv.astype(BF16)], axis=1)
        dkv_acc[pair] = both
        dxo = nt(both, jnp.concatenate([wk_ref[...], wv_ref[...]], axis=1))

        @pl.when(step == 0)
        def _():
            dxo_acc[...] = dxo

        @pl.when(step > 0)
        def _():
            dxo_acc[...] += dxo

    @pl.when(jnp.logical_and(step == pairs - 1, second))
    def _():
        dxo_ref[...] = dxo_acc[...].astype(BF16)
        over.start()

    @pl.when(step >= pairs)
    def _():
        dq, dk, dv = [0.0] * count, [0.0] * count, [0.0] * count
        for block, mask, qm, gm, q, lse, delta in pieces():
            for part in range(block + 1):
                of = slice(part * size, (part + 1) * size)
                keys = jnp.concatenate([k_ref[of], own_ref[of]], axis=1)
                p, ds = back_piece(keys, v_ref[of], q, gm, lse, delta, part == block)
                dk[part] = dk[part] + nn(ds, qm)
                dv[part] = dv[part] + nn(p, gm)
                dq[block] = dq[block] + tn(ds, k_ref[of] * (mask * scale))
        dq, dk, dv = (jnp.concatenate(a, axis=0) for a in (dq, dk, dv))
        dq = jnp.where(second, dq + dq_acc[pair], dq)
        dqk = jnp.concatenate([dq.astype(BF16), dk.astype(BF16)], axis=1)
        dv = dv.astype(BF16)
        grad_qk = nn(xt_ref[...], dqk)
        grad_v = nn(xt_ref[...], dv)
        shape = grad_ref.shape[:-1] + (PAIR,)
        lead = (slice(None),) * (len(shape) - 1)
        cut = front_pairs(pairs)

        def put(n, grad):
            col = jnp.where(pair < cut, n * cut + pair, 3 * cut + n * (pairs - cut) + pair - cut + (n > 0))
            to = pl.ds(pl.multiple_of(col * PAIR, PAIR), PAIR)
            grad_ref[lead + (to,)] = grad.astype(BF16).reshape(shape)

        put(0, grad_qk[:, :PAIR])
        turn_ref[21:22, cols] = total(dqk[:, :PAIR])

        @pl.when(second)
        def _():
            grad_o = nn(xot_ref[...], dkv_acc[pair])
            put(1, grad_qk[:, PAIR:] + grad_o[:, :PAIR])
            put(2, grad_v + grad_o[:, PAIR:])
            turn_ref[22:23, cols] = total(dv) + total(dkv_acc[pair, :, PAIR:])

        @pl.when(jnp.logical_not(second))
        def _():
            put(1, grad_qk[:, PAIR:])
            put(2, grad_v)
            turn_ref[22:23, cols] = total(dv)

        dx = nt(dqk, jnp.concatenate([wq_ref[...], wk_ref[...]], axis=1)) + nt(dv, wv_ref[...])

        @pl.when(step == pairs)
        def _():
            dx_acc[...] = dh1_ref[...] + dx

        @pl.when(step > pairs)
        def _():
            dx_acc[...] += dx

    @pl.when(step == 2 * pairs - 1)
    def _():
        shape = grad_ref.shape[:-1] + (PAIR,)
        lead = (slice(None),) * (len(shape) - 1)
        col = (2 * front_pairs(pairs) + pairs) * PAIR
        grad_ref[lead + (slice(col, col + PAIR),)] = jnp.transpose(turn_ref[...]).astype(BF16).reshape(shape)


def self_backward_finale(*refs):
    dx_ref, dx_acc, dxo_ref, came_ref, send_ref, recv_ref = (refs[i] for i in (20, 23, 28, 29, 31, 32))
    over = remote(dxo_ref, came_ref, send_ref.at[0], recv_ref.at[0], "y")

    @pl.when(lax.axis_index("sp") == 0)
    def _():
        over.wait_recv()
        dx_ref[...] = (dx_acc[...] + came_ref[...].astype(F32)).astype(BF16)

    @pl.when(lax.axis_index("sp") == 1)
    def _():
        over.wait_send()
        dx_ref[...] = dx_acc[...].astype(BF16)


GRADS = 21


def self_backward(block, qkv, kvo, g, o, lse, own, oth, x, xo, w, dh1, small, schedule):
    rows, width = x.shape
    pairs = width // PAIR

    def pair_of(offset):
        return pl.BlockSpec((rows, PAIR), lambda s: (0, lax.rem(s, pairs) + offset))

    def weight(offset):
        return pl.BlockSpec((width, PAIR), lambda s: (0, lax.rem(s, pairs) + offset))

    made = block + (3 * width + PAIR,)
    outs = [jax.ShapeDtypeStruct((rows, width), BF16)]
    specs = [whole((rows, width))]
    held = []
    if schedule:
        held += [pltpu.VMEM(made, BF16)]
    else:
        outs += [jax.ShapeDtypeStruct(made, BF16)]
        specs += [whole(made)]
    held += [
        pltpu.VMEM((pairs, rows, PAIR), F32),
        pltpu.VMEM((rows, width), F32),
        pltpu.VMEM((rows, width), F32),
        pltpu.VMEM((pairs, rows, 2 * PAIR), BF16),
        pltpu.VMEM((width, rows), BF16),
        pltpu.VMEM((width, rows), BF16),
        pltpu.VMEM((rows, width), BF16),
        pltpu.VMEM((rows, width), BF16),
        pltpu.VMEM((128, width), F32),
        pltpu.SemaphoreType.DMA((1,)),
        pltpu.SemaphoreType.DMA((1,)),
    ]
    return run(
        functools.partial(self_backward_kernel, 256), "self_backward", 2 * pairs,
        (qkv, qkv, qkv, kvo, kvo, g, o, lse, own, oth, x, xo, w, w, w, dh1) + tuple(small),
        [
            pair_of(0),
            pair_of(pairs),
            pair_of(2 * pairs),
            pair_of(0),
            pair_of(pairs),
            pair_of(0),
            pair_of(0),
            pl.BlockSpec((8, rows), lambda s: (lax.rem(s, pairs), 0)),
            whole((rows, 128)),
            whole((rows, 128)),
            whole((rows, width)),
            whole((rows, width)),
            weight(0),
            weight(pairs),
            weight(2 * pairs),
            whole((rows, width)),
        ] + [whole(a.shape) for a in small],
        outs, specs, held, schedule, 5,
        48 * rows * rows * width + 20 * rows * width * width, 12 * width * width + 40 * rows * width,
        ("y",), self_backward_finale,
    )


def first_norm_kernel(x_ref, ctx_ref, wo_ref, wq_ref, b_ref, h_ref, cq_ref):
    h = x_ref[...].astype(F32) + nn(ctx_ref[...], wo_ref[...]) + b_ref[3:4]
    h_ref[...] = h
    n, _ = normed(h)
    a = (n * b_ref[4:5] + b_ref[5:6]).astype(BF16)
    cq_ref[...] = (nn(a, wq_ref[...]) + b_ref[6:7]).astype(BF16)


def first_norm(x, ctx, wo, wq, biases):
    rows, width = x.shape
    return pl.pallas_call(
        first_norm_kernel,
        out_shape=[
            jax.ShapeDtypeStruct((rows, width), F32),
            jax.ShapeDtypeStruct((rows, width), BF16),
        ],
        compiler_params=params(),
        cost_estimate=cost(4 * rows * width * width, 4 * width * width + 10 * rows * width),
        name="first_norm",
    )(x, ctx, wo, wq, biases)


def feed_kernel(
    count, comm, h1_ref, cc_ref, ct_ref, wco_ref, b_ref, wi_ref, wo_ref,
    out_ref, dh2_ref, dcc_ref, gco_ref, *refs,
):
    if comm:
        gwi_ref, refs = refs[0], refs[1:]
    else:
        gwi_ref, gwo_ref, refs = refs[0], refs[1], refs[2:]
    small_ref, gib_ref, hid_ref, slope_ref, n2_ref, r2_ref, a2b_ref, acc_ref, df_ref, *refs = refs
    step = pl.program_id(0)
    width = acc_ref.shape[1]

    if comm:
        mi_ref, mo_ref, ci_ref, co_ref, send_ref, recv_ref = refs
        wide = ci_ref.shape[-1]
        _, c, _, _ = place()

        def chunk_copies(j):
            at = pl.ds(pl.multiple_of(j * width, width), width)
            return [
                remote(mi_ref.at[:, :, at], ci_ref.at[:, :, at], send_ref.at[0, j], recv_ref.at[0, j], "core"),
                remote(mo_ref.at[j], co_ref.at[j], send_ref.at[1, j], recv_ref.at[1, j], "core"),
            ]

    @pl.when(step == 0)
    def _():
        if comm:
            greet(["core"])
        n1, _ = normed(h1_ref[...])
        a1 = n1 * b_ref[4:5] + b_ref[5:6]
        h2 = a1 + nn(cc_ref[...], wco_ref[...]) + b_ref[7:8]
        n2, r2 = normed(h2)
        n2_ref[...] = n2
        r2_ref[...] = jnp.broadcast_to(r2, r2_ref.shape)
        a2 = n2 * b_ref[8:9] + b_ref[9:10]
        a2b_ref[...] = a2.astype(BF16)
        acc_ref[...] = a2 + b_ref[10:11]

    @pl.when(step < count)
    def _():
        u = nn(a2b_ref[...], wi_ref[...]) + b_ref[pl.ds(13 + step, 1)]
        cumul = 0.5 * (1.0 + lax.erf(u * 0.7071067811865476))
        density = jnp.exp(-0.5 * u * u) * 0.3989422804014327
        hid = (u * cumul).astype(BF16)
        hid_ref[step] = hid
        slope_ref[step] = cumul + u * density
        acc_ref[...] += nn(hid, wo_ref[...])

    @pl.when(step == count - 1)
    def _():
        n3, r3 = normed(acc_ref[...])
        gain = b_ref[11:12]
        out_ref[...] = (n3 * gain + b_ref[12:13]).astype(BF16)
        e = ct_ref[...].astype(F32)
        d3 = norm_back(e, n3, r3, gain)
        df = d3.astype(BF16)
        df_ref[...] = df
        acc_ref[...] = d3
        small_ref[0:1] = total(e * n3)
        small_ref[1:2] = total(e)
        small_ref[2:3] = total(df)

    @pl.when(jnp.logical_and(step >= count, step < 2 * count))
    def _():
        j = step - count
        df = df_ref[...]
        du = (nt(df, wo_ref[...]) * slope_ref[j]).astype(BF16)
        gib_ref[...] = total(du)
        acc_ref[...] += nt(du, wi_ref[...])
        go = tn(hid_ref[j], df).astype(BF16)
        gi = tn(a2b_ref[...], du).astype(BF16)
        if comm:
            at = pl.ds(pl.multiple_of(j * width, width), width)
            eight, narrow = gwi_ref.shape[:2]
            gi = gi.reshape(eight, 2, narrow, width)
            go = go.reshape(2, 2, 4, narrow, width)
            gwi_ref[:, :, at] = jnp.where(c == 0, gi[:, 0], gi[:, 1])
            mi_ref[:, :, at] = jnp.where(c == 0, gi[:, 1], gi[:, 0])
            mo_ref[j] = jnp.where(c == 0, go[:, 1], go[:, 0])
            for i in range(4):
                gwi_ref[pl.ds(2 * j, 2), :, pl.ds(wide + i * width, width)] = jnp.where(c == 0, go[:, 0, i], go[:, 1, i])
            for copy in chunk_copies(j):
                copy.start()
        else:
            gwo_ref[...] = go
            gwi_ref[...] = gi

    @pl.when(step == 2 * count)
    def _():
        d2 = acc_ref[...]
        n2 = n2_ref[...]
        dh2 = norm_back(d2, n2, r2_ref[:, :1], b_ref[8:9])
        dh2_ref[...] = dh2
        dco = dh2.astype(BF16)
        dcc_ref[...] = nt(dco, wco_ref[...]).astype(BF16)
        gco_ref[...] = tn(cc_ref[...], dco).astype(BF16)
        small_ref[3:4] = total(d2 * n2)
        small_ref[4:5] = total(d2)
        small_ref[5:6] = total(dco)
        small_ref[6:8] = jnp.zeros((2, d2.shape[1]), F32)

    if comm:

        @pl.when(step > count)
        def _():
            j = step - count - 1
            at = pl.ds(pl.multiple_of(j * width, width), width)
            for copy in chunk_copies(j):
                copy.wait()
            gwi_ref[:, :, at] += ci_ref[:, :, at]
            for i in range(4):
                gwi_ref[pl.ds(2 * j, 2), :, pl.ds(wide + i * width, width)] += co_ref[j, :, i]


def feed(size, comm, h1, cc, ct, wco, biases, wi, wo):
    rows, width = h1.shape
    wide = wi.shape[1]
    chunk = width
    count = wide // chunk

    def weight(s):
        return jnp.where(s < count, s, jnp.minimum(s - count, count - 1))

    def early(s):
        return jnp.clip(s - count, 0, count - 1)

    flat = whole((rows, width))
    square = whole((width, width))
    scratch = [
        pltpu.VMEM((count, rows, chunk), BF16),
        pltpu.VMEM((count, rows, chunk), F32),
        pltpu.VMEM((rows, width), F32),
        pltpu.VMEM((rows, 128), F32),
        pltpu.VMEM((rows, width), BF16),
        pltpu.VMEM((rows, width), F32),
        pltpu.VMEM((rows, width), BF16),
    ]
    if comm:
        narrow = width // size
        grad_specs = [whole((size // 2, narrow, 2 * wide))]
        grad_shapes = [(size // 2, narrow, 2 * wide)]
        scratch += [
            pltpu.VMEM((size // 2, narrow, wide), BF16),
            pltpu.VMEM((count, 2, 4, narrow, width), BF16),
            pltpu.VMEM((size // 2, narrow, wide), BF16),
            pltpu.VMEM((count, 2, 4, narrow, width), BF16),
            pltpu.SemaphoreType.DMA((2, count)),
            pltpu.SemaphoreType.DMA((2, count)),
        ]
    else:
        grad_specs = [
            pl.BlockSpec((width, chunk), lambda s: (0, early(s))),
            pl.BlockSpec((chunk, width), lambda s: (early(s), 0)),
        ]
        grad_shapes = [(width, wide), (wide, width)]
    return pl.pallas_call(
        functools.partial(feed_kernel, count, comm),
        grid=(2 * count + 1,),
        in_specs=[
            flat, flat, flat, square, whole(biases.shape),
            pl.BlockSpec((width, chunk), lambda s: (0, weight(s))),
            pl.BlockSpec((chunk, width), lambda s: (weight(s), 0)),
        ],
        out_specs=[flat, flat, flat, square]
        + grad_specs
        + [whole((8, width)), pl.BlockSpec((1, chunk), lambda s: (0, early(s)))],
        out_shape=[
            jax.ShapeDtypeStruct((rows, width), BF16),
            jax.ShapeDtypeStruct((rows, width), F32),
            jax.ShapeDtypeStruct((rows, width), BF16),
            jax.ShapeDtypeStruct((width, width), BF16),
        ]
        + [jax.ShapeDtypeStruct(a, BF16) for a in grad_shapes]
        + [
            jax.ShapeDtypeStruct((8, width), F32),
            jax.ShapeDtypeStruct((1, wide), F32),
        ],
        scratch_shapes=scratch,
        compiler_params=params(2 if comm else None),
        cost_estimate=cost(
            12 * rows * width * wide + 6 * rows * width * width, 12 * width * wide + 16 * rows * width
        ),
        name="feed",
    )(h1, cc, ct, wco, biases, wi, wo)


def first_back_kernel(
    dcq_ref, dh2_ref, h1_ref, ctx_ref, wcq_ref, wso_ref, b_ref,
    dh1_ref, dsc_ref, gcq_ref, gso_ref, small_ref,
):
    gain = b_ref[4:5]
    n1, r1 = normed(h1_ref[...])
    a1b = (n1 * gain + b_ref[5:6]).astype(BF16)
    dcq = dcq_ref[...]
    d1 = dh2_ref[...] + nt(dcq, wcq_ref[...])
    dh1 = norm_back(d1, n1, r1, gain)
    dh1_ref[...] = dh1
    dso = dh1.astype(BF16)
    dsc_ref[...] = nt(dso, wso_ref[...]).astype(BF16)
    gcq_ref[...] = tn(a1b, dcq).astype(BF16)
    gso_ref[...] = tn(ctx_ref[...], dso).astype(BF16)
    small_ref[0:1] = total(dcq)
    small_ref[1:2] = total(d1 * n1)
    small_ref[2:3] = total(d1)
    small_ref[3:4] = total(dso)
    small_ref[4:8] = jnp.zeros((4, dh1.shape[1]), F32)


def first_back(dcq, dh2, h1, ctx, wcq, wso, biases, schedule):
    rows, width = dcq.shape
    flat, square = whole((rows, width)), whole((width, width))
    return run(
        first_back_kernel, "first_back", 1,
        (dcq, dh2, h1, ctx, wcq, wso, biases),
        [flat, flat, flat, flat, square, square, whole(biases.shape)],
        [
            jax.ShapeDtypeStruct((rows, width), F32),
            jax.ShapeDtypeStruct((rows, width), BF16),
            jax.ShapeDtypeStruct((width, width), BF16),
            jax.ShapeDtypeStruct((width, width), BF16),
            jax.ShapeDtypeStruct((8, width), F32),
        ],
        [flat, flat, square, square, whole((8, width))],
        (), schedule, 4,
        8 * rows * width * width, 8 * width * width + 18 * rows * width,
    )


def outputs_kernel(moves, count, line, *refs):
    pieces, rest = refs[:count], refs[count:]
    out_ref, dx_ref, dm_ref, dmi_ref = rest[:4]
    outs = rest[4:]
    for piece, first, wide, which, row, col in moves:
        ref = pieces[piece]
        outs[which][row : row + ref.shape[0], col : col + wide] = ref[:, first : first + wide].astype(F32)
    turned, result, dx, dm = outs[-4:]
    turned[...] = jnp.transpose(pieces[line[0]][:, line[1] : line[1] + PAIR].astype(F32))
    result[...] = out_ref[...]
    dx[...] = dx_ref[...]
    dm[...] = (dm_ref[...] + dmi_ref[...].astype(F32)).astype(BF16)


def outputs(pieces, moves, line, shapes, out, dx, dm, dmi):
    ins = tuple(pieces) + (out, dx, dm, dmi)
    result = jax.ShapeDtypeStruct(out.shape, BF16)
    return pl.pallas_call(
        functools.partial(outputs_kernel, moves, len(pieces), line),
        out_shape=[jax.ShapeDtypeStruct(a, F32) for a in shapes]
        + [jax.ShapeDtypeStruct((PAIR, pieces[0].shape[0]), F32), result, result, result],
        compiler_params=params(),
        cost_estimate=cost(0, 12 << 20),
        name="outputs",
    )(*ins)


def moved(pieces, targets):
    out = []
    for n, (start, wide) in enumerate(pieces):
        for first, cols, which, row, col in targets:
            low, high = max(start, first), min(start + wide, first + cols)
            if low < high:
                out.append((n, low - start, high - low, which, row, col + low - first))
    return out


def swap_sum(part, axis, pairs):
    came = lax.ppermute(part, axis, pairs)
    return part.astype(F32) + came.astype(F32)


def sum_scatter(grad, size, order):
    rows, cols = grad.shape
    bits = size.bit_length() - 1
    me = lax.axis_index("dp")
    now = grad.reshape((2,) * bits + (rows // size, cols))
    left = list(range(bits))[::-1]
    for bit in [b for b in order if b < bits] + [b for b in range(bits) if b not in order]:
        axis = left.index(bit)
        mine = (me >> bit) & 1
        keep = lax.dynamic_index_in_dim(now, mine, axis, keepdims=False)
        send = lax.dynamic_index_in_dim(now, 1 - mine, axis, keepdims=False)
        came = lax.ppermute(send, "dp", [(i, i ^ (1 << bit)) for i in range(size)])
        now = (keep.astype(F32) + came.astype(F32)).astype(BF16)
        left.pop(axis)
    return swap_sum(now, "sp", [(0, 1), (1, 0)])


def per_device(
    size,
    inputs,
    memory,
    target_docs,
    memory_docs,
    cotangent,
    w_qkv,
    b_q,
    b_v,
    w_so,
    b_so,
    g_one,
    s_one,
    w_cq,
    b_cq,
    w_ckv,
    b_cv,
    w_co,
    b_co,
    g_two,
    s_two,
    w_fi,
    b_fi,
    w_fo,
    b_fo,
    g_three,
    s_three,
):
    rows, width = inputs.shape[1:]
    wide = b_fi.shape[0]
    comm = size == 16
    narrow, broad = width // size, wide // size
    swap = [(0, 1), (1, 0)]
    x, mem, ct = inputs[0], memory[0], cotangent[0]
    x_o = lax.ppermute(x, "sp", [(0, 1)])
    docs_o = lax.ppermute(jnp.concatenate([target_docs, memory_docs], axis=0), "sp", swap)
    line = lax.broadcasted_iota(jnp.int32, (24, width), 0)
    vectors = (b_q, b_v, b_cv, b_so, g_one, s_one, b_cq, b_co, g_two, s_two, b_fo, g_three, s_three)
    vectors += tuple(b_fi[i : i + width] for i in range(0, wide, width))
    biases = jnp.zeros((24, width), F32)
    for i, v in enumerate(vectors):
        biases = jnp.where(line == i, v.astype(F32)[None], biases)

    qkv, mkv, t_own, m_own = project_own(x, mem, target_docs, memory_docs, w_qkv, w_ckv, biases)
    kvo, mem_s, t_oth, m_oth = project_other(x_o, mem, docs_o[:1], docs_o[1:], w_qkv, biases, t_own)
    mem_o = lax.ppermute(mem_s, "sp", swap)
    ctx, lse = self_forward(qkv, kvo, t_own, t_oth)
    h1, cq = first_norm(x, ctx, w_so, w_cq, biases)
    mkvo = project_memory(mem_o, w_ckv, biases)
    cc, clse = cross_forward(cq, mkv, mkvo, t_own, m_own, m_oth)
    output, dh2, dcc, gco, gwi, *gwo, small_a, gib = feed(size, comm, h1, cc, ct, w_co, biases, w_fi, w_fo)
    turned = gib.reshape(width, -1).T

    block = (2, 2, 2, 2, narrow) if comm else (width,)
    at_cross, at_first, at_self = (), (), ()
    ways = (VIA_X, VIA_Y, VIA_Z)

    def thirds(array, shape, dims):
        wide = shape[-1] // 3
        return [Flow(array, shape, hops, dims, (i * wide, wide)) for i, hops in enumerate(ways)]

    if comm:
        gwi = gwi.reshape(block[:3] + gwi.shape[1:])
        t0 = thirds(gwi, gwi.shape, BLOCK[:3])
        at_cross = ((t0, 0, 4), (t0, 4, 6))
    dcq, dm, dmo, gck, gcv, gcvb = cross_backward(
        cq, mkv, mkvo, dcc, cc, clse, t_own, m_own, m_oth, mem, mem_o, w_ckv, at_cross
    )
    dm_in = lax.ppermute(dmo, "sp", swap)
    if comm:
        at_first = ((t0, 0, 1),)
    dh1, dsc, gcq, gso, small_b = first_back(dcq, dh2, h1, ctx, w_cq, w_so, biases, at_first)
    if comm:
        fresh = [
            Flow(g.reshape(block + (width,)), block + (width,), ("core",)) for g in (gck, gcv, gco, gcq, gso)
        ]
        joint = Joint()
        t1 = thirds(joint, block[:3] + (narrow, 5 * width), BLOCK[:3])
        cut = front_pairs(width // PAIR) * PAIR
        shape = block + (3 * width + PAIR,)

        def group(starts, widths):
            return [
                Flow(("ref", GRADS), shape, ("core",) + hops, BLOCK, (first, cols))
                for hops, first, cols in zip((VIA_X, VIA_Z, VIA_Y), starts, widths)
            ]

        back_width = width - cut
        starts = [0, cut, 2 * cut, 3 * cut, 3 * cut + back_width + PAIR, 3 * cut + 2 * back_width + PAIR]
        widths = [cut] * 3 + [back_width + PAIR] + [back_width] * 2
        front, back = group(starts[:3], widths[:3]), group(starts[3:], widths[3:])
        at_self = (
            (fresh, 0, 2, joint), (t0, 0, 3), (t0[1:], 3, 6),
            (t1, 2, 7), (t1, 7, 9), (t1, 9, 10), (t1, 10, 11), (t1[1:], 11, 12),
            (front, 10, 11), (front, 11, 12), (front, 12, 13), (front, 13, 14), (front, 14, 15), (front[1:], 15, 16),
            (back, 12, 13), (back, 13, 14), (back, 14, 15), (back, 15, 16), (back, 16, 17), (back[1:], 17, 18),
        )
    dx, *made = self_backward(
        block, qkv, kvo, dsc, ctx, lse, t_own, t_oth, x, x_o, w_qkv, dh1, (small_a, small_b, gcvb, turned), at_self
    )
    if comm:
        spans = [(i * 2 * wide // 3, 2 * wide // 3) for i in range(3)]
        moves = moved(spans, [(0, wide, 2, 0, 0)] + [(wide + i * width, width, 3, i * narrow, 0) for i in range(4)])
        spans = [(i * 5 * width // 3, 5 * width // 3) for i in range(3)]
        targets = [(0, 2 * width, 1, 0, 0)] + [((2 + i) * width, width, 4 + i, 0, 0) for i in range(3)]
        moves += [(m[0] + 3,) + m[1:] for m in moved(spans, targets)]
        for i in range(3):
            moves.append((6 + i, 0, cut, 0, 0, i * width))
            moves.append((9 + i, 0, back_width, 0, 0, i * width + cut))
        shapes = [(narrow, 3 * width), (narrow, 2 * width), (narrow, wide), (broad, width)] + [(narrow, width)] * 3
        t_qkv, t_cmem, t_fin, t_fout, t_cout, t_cquery, t_out, lines, output, derivative, grad_memory = outputs(
            [f.array for f in t0 + t1 + front + back], moves, (9, back_width), shapes, output, dx, dm, dm_in
        )
    else:
        cut = front_pairs(width // PAIR) * PAIR
        rest = width - cut
        (gqkv,) = made
        at = [0, cut, 2 * cut, 3 * cut, 3 * cut + rest + PAIR, 3 * cut + 2 * rest + PAIR]
        columns = gqkv[:, 3 * cut + rest : 3 * cut + rest + PAIR]
        gqkv = jnp.concatenate(
            [gqkv[:, a : a + n] for i in range(3) for a, n in ((at[i], cut), (at[3 + i], rest))], axis=1
        )
        t_fin, t_fout, t_cout, t_cquery, t_out, t_cmem, t_qkv, lines = (
            sum_scatter(g, size, (0, 1, 2, 3))
            for g in (
                gwi, gwo[0], gco, gcq, gso, jnp.concatenate([gck, gcv], axis=1),
                gqkv, columns,
            )
        )
        lines, derivative = lines.T, dx
        grad_memory = (dm + dm_in.astype(F32)).astype(BF16)
    t_gthree, t_sthree, t_fobias, t_gtwo, t_stwo, t_cobias = (lines[i] for i in range(6))
    t_cqbias, t_gone, t_sone, t_obias = (lines[i] for i in range(8, 12))
    t_cvbias, t_qbias, t_vbias = lines[16], lines[21], lines[22]
    t_fibias = lines[17:21].T.reshape(-1)
    return (
        output[None],
        derivative[None],
        grad_memory[None],
        t_qkv,
        t_qbias,
        t_vbias,
        t_out,
        t_obias,
        t_gone,
        t_sone,
        t_cquery,
        t_cqbias,
        t_cmem,
        t_cvbias,
        t_cout,
        t_cobias,
        t_gtwo,
        t_stwo,
        t_fin,
        t_fibias,
        t_fout,
        t_fobias,
        t_gthree,
        t_sthree,
    )


def solution(mesh):
    split = P("dp", "sp", None)
    in_specs = (split, split, P("dp", "sp"), P("dp", "sp"), split) + (P(),) * 21
    matrix, vector = P("dp", None), P("dp")
    out_specs = (
        split, split, split,
        matrix, vector, vector,
        matrix, vector, vector, vector,
        matrix, vector,
        matrix, vector,
        matrix, vector, vector, vector,
        matrix, vector,
        matrix, vector, vector, vector,
    )
    return jax.shard_map(
        functools.partial(per_device, mesh.shape["dp"]),
        mesh=mesh, in_specs=in_specs, out_specs=out_specs, check_vma=False,
    )
```

```python
import functools

import jax
import jax.numpy as jnp
from jax import lax
from jax.experimental import pallas as pl
from jax.experimental.pallas import tpu as pltpu
from jax.sharding import PartitionSpec as P

HD = 64
PAIR = 2 * HD
EPS = 1e-05
FAR = 1.0e9
VMEM = 60 * 1024 * 1024
F32 = jnp.float32
BF16 = jnp.bfloat16


def nn(a, b):
    return lax.dot_general(a, b, (((1,), (0,)), ((), ())), preferred_element_type=F32)


def nt(a, b):
    return lax.dot_general(a, b, (((1,), (1,)), ((), ())), preferred_element_type=F32)


def tn(a, b):
    return lax.dot_general(a, b, (((0,), (0,)), ((), ())), preferred_element_type=F32)


def params(collective=None):
    if collective is None:
        return pltpu.CompilerParams(vmem_limit_bytes=VMEM)
    return pltpu.CompilerParams(
        vmem_limit_bytes=VMEM, collective_id=collective, has_side_effects=True
    )


def cost(flops, moved):
    return pl.CostEstimate(flops=int(flops), bytes_accessed=int(moved), transcendentals=0)


def normed(h):
    centred = h - jnp.mean(h, axis=-1, keepdims=True)
    rstd = lax.rsqrt(jnp.mean(centred * centred, axis=-1, keepdims=True) + EPS)
    return centred * rstd, rstd


def norm_back(grad, n, rstd, gain):
    scaled = grad * gain
    centre = jnp.mean(scaled, axis=-1, keepdims=True)
    along = jnp.mean(scaled * n, axis=-1, keepdims=True)
    return rstd * (scaled - centre - n * along)


def total(a):
    return jnp.sum(a.astype(F32), axis=0, keepdims=True)


def place():
    me = lax.axis_index("dp")
    return me, me % 2, (me // 2) % 2, me // 4, lax.axis_index("sp")


def flipped(at, hops):
    me, c, x, z, sp = at
    for hop in hops:
        if hop == "core":
            me, c = me + 1 - 2 * c, 1 - c
        elif hop == "x":
            me, x = me + 2 - 4 * x, 1 - x
        elif hop == "z1":
            me, z = me + 4 - 8 * (z % 2), z + 1 - 2 * (z % 2)
        elif hop == "z2":
            me, z = me + 8 - 16 * (z // 2), z + 2 - 4 * (z // 2)
        else:
            sp = 1 - sp
    return me, c, x, z, sp


def partner(hops, at=None):
    there = flipped(at or place(), hops)
    return {"dp": there[0], "sp": there[4]}


def greet(groups, at=None):
    groups = sorted({tuple("y" if h[0] == "y" else h for h in hops) for hops in groups})
    barrier = pltpu.get_barrier_semaphore()
    for hops in groups:
        pl.semaphore_signal(barrier, inc=1, device_id=partner(hops, at), device_id_type=pl.DeviceIdType.MESH)
    pl.semaphore_wait(barrier, len(groups))


def remote(src, dst, send, recv, hops, at=None):
    return pltpu.make_async_remote_copy(
        src_ref=src, dst_ref=dst, send_sem=send, recv_sem=recv,
        device_id=partner(hops, at), device_id_type=pl.DeviceIdType.MESH,
    )


VIA_X = ("x", "z1", "z2", "y")
VIA_Y = ("yr", "x", "z1", "z2", "yg")
VIA_Z = ("z1", "yr", "x", "z2", "yg")
X_FIRST = ("x", "z1", ("yr", "z2"), "yg")
Z_FIRST = ("z1", "x", ("yr", "z2"), "yg")
AT_ONCE = (("x", "z1"), ("yr", "z2"), "yg")
BLOCK = ("z2", "z1", "x", "core")


class Part:
    def __init__(self, hop, shape, dims, cols=None):
        self.hops = hops = hop if isinstance(hop, tuple) else (hop,)
        self.groups = [(h,) for h in hops] + ([hops] if len(hops) > 1 else [])
        self.dims = dims
        self.cols = cols or (0, shape[-1])
        self.shape = shape = tuple(shape[:-1]) + (self.cols[1],)
        for h in hops:
            if h in dims:
                at = dims.index(h)
                shape, dims = shape[:at] + shape[at + 1 :], dims[:at] + dims[at + 1 :]
            elif h != "y":
                shape = shape[:-1] + (shape[-1] // 2 if h == "yr" else 2 * shape[-1],)
        self.after, self.left = shape, dims
        self.came = self.shape if hops == ("yg",) else shape

    def share(self, at):
        _, c, x, z, sp = at
        first, wide = self.cols
        index = [slice(None)] * (len(self.shape) - 1) + [pl.ds(first, wide)]
        for h in self.hops:
            if h in self.dims:
                index[self.dims.index(h)] = {"core": c, "x": x, "z1": z % 2, "z2": z // 2}[h]
            elif h == "yr":
                half = wide // 2
                index[-1] = pl.ds(pl.multiple_of(first + sp * half, 128), half)
        return tuple(index)

    def copies(self, src, held, made, came, send, recv, local, at):
        out = [
            remote(src.at[self.share(flipped(at, g))], came[i], send.at[i], recv.at[i], g, at)
            for i, g in enumerate(self.groups)
        ]
        if not held:
            out.append(pltpu.make_async_copy(src.at[self.share(at)], made, local))
        return out

    def add(self, src, held, made, came, at):
        if self.hops == ("yg",):
            wide, sp = self.shape[-1], at[4]
            lead = (slice(None),) * (len(self.shape) - 1)
            made[lead + (pl.ds(pl.multiple_of(sp * wide, 128), wide),)] = src[self.share(at)]
            made[lead + (pl.ds(pl.multiple_of((1 - sp) * wide, 128), wide),)] = came[0][...]
        elif len(came) > 1:
            mine = src[self.share(at)] if held else made[...]
            made[...] = sum((c[...].astype(F32) for c in came), mine.astype(F32)).astype(BF16)
        elif held:
            made[...] = src[self.share(at)] + came[0][...]
        else:
            made[...] += came[0][...]


class Flow:
    def __init__(self, array, shape, hops, dims=BLOCK, cols=None):
        self.array, self.shape, self.dims, self.cols = array, tuple(shape), dims, cols
        self.hops = list(hops)

    def step(self):
        part = Part(self.hops.pop(0), self.shape, self.dims, self.cols)
        self.shape, self.dims, self.cols = part.after, part.left, None
        return part


class Window:
    def __init__(self, start, stop, joint):
        self.start, self.stop, self.joint = start, stop, joint
        self.parts, self.sources, self.keeps = [], [], []


class Joint:
    def __init__(self):
        self.window = None


def plan(schedule):
    windows, arrays, latest = [], [], {}
    for n, (flows, start, stop, *joint) in enumerate(schedule):
        window = Window(start, stop, bool(joint))
        if joint:
            joint[0].window = n
        for i, flow in enumerate(flows):
            if flow in latest:
                source = ("part",) + latest[flow]
                before = windows[latest[flow][0]]
                before.keeps[latest[flow][1]] = False
            elif isinstance(flow.array, Joint):
                source = ("joint", flow.array.window)
            elif isinstance(flow.array, tuple):
                source = flow.array
            else:
                known = [k for k, a in enumerate(arrays) if a is flow.array]
                if not known:
                    arrays.append(flow.array)
                source = ("in", known[0] if known else len(arrays) - 1)
            window.parts.append(flow.step())
            window.sources.append(source)
            window.keeps.append(not joint)
            if not joint:
                latest[flow] = (n, i)
        windows.append(window)
    return windows, arrays, latest


def carrying(body, own, windows, arrays, grid, also, finale):
    ins, outs, held = own

    def kernel(*refs):
        refs = list(refs)

        def take(n):
            got = refs[:n]
            del refs[:n]
            return got

        my_in, arr = take(ins), take(arrays)
        my_out = take(outs)
        given = [[take(1)[0] if k else None for k in w.keeps] for w in windows]
        my_held = take(held)
        made, came, joints = [], [], []
        for w, g in zip(windows, given):
            if w.joint:
                joint, col, views = take(1)[0], 0, []
                for q in w.parts:
                    views.append(joint.at[(slice(None),) * (len(q.after) - 1) + (pl.ds(col, q.after[-1]),)])
                    col += q.after[-1]
                joints.append(joint)
                made.append(views)
            else:
                joints.append(None)
                made.append([ref if ref is not None else take(1)[0] for ref in g])
            came.append([take(len(q.groups)) for q in w.parts])
        mine = my_in + my_out + my_held
        step = pl.program_id(0)
        groups = [g for w in windows for q in w.parts for g in q.groups] + list(also)
        if groups:
            here = place()
            pl.when(step == 0)(lambda: greet(groups, here))
        if windows:
            send, recv, local = refs
        copies, sources, base = [], [], 0
        for w, m, c in zip(windows, made, came):
            now, froms = [], []
            for i, q in enumerate(w.parts):
                kind = w.sources[i]
                if kind[0] == "in":
                    src = arr[kind[1]]
                elif kind[0] == "ref":
                    src = mine[kind[1]]
                elif kind[0] == "joint":
                    src = joints[kind[1]]
                else:
                    src = made[kind[1]][kind[2]]
                held_here = kind[0] != "in"
                froms.append((src, held_here))
                now += q.copies(
                    src, held_here, m[i], c[i], send.at[base], recv.at[base], local.at[base], here
                )
                base += 1
            copies.append(now)
            sources.append(froms)

        def phase(number):
            for n, w in enumerate(windows):
                if w.stop == number:
                    for copy in copies[n]:
                        copy.wait()
                    for q, (src, held_here), m, c in zip(w.parts, sources[n], made[n], came[n]):
                        q.add(src, held_here, m, c, here)
            for n, w in enumerate(windows):
                if w.start == number:
                    for copy in copies[n]:
                        copy.start()

        used = sorted({w.start for w in windows} | {w.stop for w in windows})
        for number in used:
            if number < grid:
                pl.when(step == number)(functools.partial(phase, number))
        body(*mine)
        for number in used:
            if number >= grid:
                pl.when(step == grid - 1)(functools.partial(phase, number))
        if finale:
            pl.when(step == grid - 1)(lambda: finale(*mine))

    return kernel


def run(
    body, name, grid, ins, in_specs, outs, out_specs, held=(), schedule=(), collective=None,
    flops=0, moved=0, also=(), finale=None,
):
    in_specs, outs, out_specs, held = list(in_specs), list(outs), list(out_specs), list(held)
    windows, arrays, latest = plan(schedule)
    own = len(outs)
    kernel = carrying(body, (len(ins), own, len(held)), windows, len(arrays), grid, also, finale)
    in_specs += [pl.BlockSpec(memory_space=pl.ANY)] * len(arrays)
    order, count = [], 0
    for n, w in enumerate(windows):
        if w.joint:
            shape = w.parts[0].after[:-1] + (sum(q.after[-1] for q in w.parts),)
            held.append(pltpu.VMEM(shape, BF16))
        for i, (q, k) in enumerate(zip(w.parts, w.keeps)):
            if w.joint:
                continue
            if k:
                outs.append(jax.ShapeDtypeStruct(q.after, BF16))
                out_specs.append(whole(q.after))
                order.append((n, i))
            else:
                held.append(pltpu.VMEM(q.after, BF16))
        held += [pltpu.VMEM(q.came, BF16) for q in w.parts for _ in q.groups]
        count += len(w.parts)
    if windows:
        held += [pltpu.SemaphoreType.DMA((count, 3))] * 2 + [pltpu.SemaphoreType.DMA((count,))]
    results = pl.pallas_call(
        kernel,
        grid=(grid,),
        in_specs=in_specs,
        out_specs=out_specs,
        out_shape=outs,
        scratch_shapes=held,
        compiler_params=params(collective if windows or also else None),
        cost_estimate=cost(flops, moved),
        name=name,
    )(*ins, *arrays)
    for flow, where in latest.items():
        flow.array = results[own + order.index(where)]
    return results[:own]


def code_of(docs_ref):
    row = lax.broadcasted_iota(jnp.int32, (128, docs_ref.shape[1]), 0)
    return jnp.transpose(jnp.where(docs_ref[...] == row, 1.0, 0.0)).astype(BF16)


def project_own_kernel(x_ref, m_ref, td_ref, md_ref, wx_ref, wm_ref, b_ref, qkv_ref, mkv_ref, to_ref, mo_ref):
    step = pl.program_id(0)

    @pl.when(step == 0)
    def _():
        to_ref[...] = code_of(td_ref)
        mo_ref[...] = code_of(md_ref)

    @pl.when(step < 3)
    def _():
        bias = jnp.where(step == 0, b_ref[0:1], 0.0) + jnp.where(step == 2, b_ref[1:2], 0.0)
        qkv_ref[...] = (nn(x_ref[...], wx_ref[...]) + bias).astype(BF16)

    @pl.when(step >= 3)
    def _():
        bias = jnp.where(step == 4, b_ref[2:3], 0.0)
        mkv_ref[...] = (nn(m_ref[...], wm_ref[...]) + bias).astype(BF16)


def project_own(x, mem, td, md, wx, wm, biases):
    rows, width = x.shape
    code = jax.ShapeDtypeStruct((rows, 128), BF16)
    return pl.pallas_call(
        project_own_kernel,
        grid=(5,),
        in_specs=[
            whole((rows, width)), whole((rows, width)), whole((1, rows)), whole((1, rows)),
            pl.BlockSpec((width, width), lambda s: (0, jnp.minimum(s, 2))),
            pl.BlockSpec((width, width), lambda s: (0, jnp.maximum(s - 3, 0))),
            whole(biases.shape),
        ],
        out_specs=[
            pl.BlockSpec((rows, width), lambda s: (0, jnp.minimum(s, 2))),
            pl.BlockSpec((rows, width), lambda s: (0, jnp.maximum(s - 3, 0))),
            whole((rows, 128)), whole((rows, 128)),
        ],
        out_shape=[
            jax.ShapeDtypeStruct((rows, 3 * width), BF16), jax.ShapeDtypeStruct((rows, 2 * width), BF16), code, code,
        ],
        compiler_params=params(),
        cost_estimate=cost(10 * rows * width * width, 20 * width * width),
        name="project_own",
    )(x, mem, td, md, wx, wm, biases)


def project_other_kernel(x_ref, m_ref, td_ref, md_ref, wx_ref, b_ref, after_ref, kvo_ref, mem_ref, tt_ref, mt_ref):
    step = pl.program_id(0)

    @pl.when(step == 0)
    def _():
        mem_ref[...] = m_ref[...]
        tt_ref[...] = code_of(td_ref)
        mt_ref[...] = code_of(md_ref)

    @pl.when(lax.axis_index("sp") == 1)
    def _():
        bias = jnp.where(step == 1, b_ref[1:2], 0.0)
        kvo_ref[...] = (nn(x_ref[...], wx_ref[...]) + bias).astype(BF16)

    @pl.when(lax.axis_index("sp") == 0)
    def _():
        kvo_ref[...] = jnp.zeros(kvo_ref.shape, BF16)


def project_other(x, mem, td, md, wx, biases, after):
    rows, width = x.shape
    code = jax.ShapeDtypeStruct((rows, 128), BF16)
    return pl.pallas_call(
        project_other_kernel,
        grid=(2,),
        in_specs=[
            whole((rows, width)), whole((rows, width)), whole((1, rows)), whole((1, rows)),
            pl.BlockSpec((width, width), lambda s: (0, s + 1)),
            whole(biases.shape),
            pl.BlockSpec(memory_space=pl.ANY),
        ],
        out_specs=[
            pl.BlockSpec((rows, width), lambda s: (0, s)),
            whole((rows, width)), whole((rows, 128)), whole((rows, 128)),
        ],
        out_shape=[
            jax.ShapeDtypeStruct((rows, 2 * width), BF16), jax.ShapeDtypeStruct((rows, width), BF16), code, code,
        ],
        compiler_params=params(),
        cost_estimate=cost(4 * rows * width * width, 10 * width * width),
        name="project_other",
    )(x, mem, td, md, wx, biases, after)


def project_memory_kernel(x_ref, w_ref, b_ref, o_ref):
    bias = jnp.where(pl.program_id(0) == 1, b_ref[2:3], 0.0)
    o_ref[...] = (nn(x_ref[...], w_ref[...]) + bias).astype(BF16)


def project_memory(x, w, biases):
    rows, width = x.shape
    return pl.pallas_call(
        project_memory_kernel,
        grid=(2,),
        in_specs=[
            whole((rows, width)),
            pl.BlockSpec((width, width), lambda j: (0, j)),
            whole(biases.shape),
        ],
        out_specs=pl.BlockSpec((rows, width), lambda j: (0, j)),
        out_shape=jax.ShapeDtypeStruct((rows, 2 * width), BF16),
        compiler_params=params(),
        cost_estimate=cost(4 * rows * width * width, 4 * width * (width + rows)),
        name="project_memory",
    )(x, w, biases)


def head_masks(dtype):
    lane = lax.broadcasted_iota(jnp.int32, (1, PAIR), 1)
    low = jnp.where(lane < HD, 1.0, 0.0)
    return low.astype(dtype), (1.0 - low).astype(dtype)


def query_code(code):
    lane = lax.broadcasted_iota(jnp.int32, code.shape, 1)
    return jnp.where(lane < 4, (code.astype(F32) - 1.0) * FAR, 0.0).astype(BF16)


def softmax_pieces(scores, values):
    peak = functools.reduce(jnp.maximum, [jnp.max(s, axis=-1, keepdims=True) for s in scores])
    expd = [jnp.exp(s - peak) for s in scores]
    norm = sum(jnp.sum(e, axis=-1, keepdims=True) for e in expd)
    out = sum(nn(e.astype(BF16), v) for e, v in zip(expd, values))
    return out / norm, peak + jnp.log(norm)


def self_pieces(block, size, both, own, other):
    pieces = []
    if both:
        pieces.append((other, False))
    if block:
        pieces.append((own[: block * size], False))
    pieces.append((own[block * size : (block + 1) * size], True))
    return pieces


def store_lse(lse_ref, block, size, low, high):
    lane = lax.broadcasted_iota(jnp.int32, (size, PAIR), 1)
    both = jnp.where(lane == 0, low, high)
    lse_ref[:, block * size : (block + 1) * size] = jnp.transpose(both)[:8]


def self_forward_kernel(size, q_ref, k_ref, v_ref, ko_ref, vo_ref, own_ref, oth_ref, o_ref, lse_ref):
    second = lax.axis_index("sp") == 1
    rows = q_ref.shape[0]
    masks = head_masks(BF16)
    outs = head_masks(F32)

    def run(both):
        qcode = query_code(own_ref[...])
        own = jnp.concatenate([k_ref[...], own_ref[...]], axis=1)
        oth = jnp.concatenate([ko_ref[...], oth_ref[...]], axis=1) if both else None
        vown = v_ref[...]
        voth = vo_ref[...] if both else None
        for block in range(rows // size):
            at = slice(block * size, (block + 1) * size)
            lses, result = [], 0.0
            for mask, keep in zip(masks, outs):
                q = jnp.concatenate([q_ref[at] * (mask * BF16(HD**-0.5)), qcode[at]], axis=1)
                scores = []
                for keys, diagonal in self_pieces(block, size, both, own, oth):
                    s = nt(q, keys)
                    if diagonal:
                        row = lax.broadcasted_iota(jnp.int32, s.shape, 0)
                        col = lax.broadcasted_iota(jnp.int32, s.shape, 1)
                        s = jnp.where(row >= col, s, -FAR)
                    scores.append(s)
                values = [v for v, _ in self_pieces(block, size, both, vown, voth)]
                out, lse = softmax_pieces(scores, values)
                result = result + out * keep
                lses.append(lse)
            o_ref[at] = result.astype(BF16)
            store_lse(lse_ref, block, size, *lses)

    pl.when(second)(lambda: run(True))
    pl.when(jnp.logical_not(second))(lambda: run(False))


def pair_spec(rows, offset):
    return pl.BlockSpec((rows, PAIR), lambda p: (0, p + offset))


def whole(shape):
    return pl.BlockSpec(shape, lambda *_: (0,) * len(shape))


def self_forward(qkv, kvo, own, oth):
    rows = qkv.shape[0]
    width = qkv.shape[1] // 3
    pairs = width // PAIR
    return pl.pallas_call(
        functools.partial(self_forward_kernel, 256),
        grid=(pairs,),
        in_specs=[
            pair_spec(rows, 0),
            pair_spec(rows, pairs),
            pair_spec(rows, 2 * pairs),
            pair_spec(rows, 0),
            pair_spec(rows, pairs),
            whole((rows, 128)),
            whole((rows, 128)),
        ],
        out_specs=[pair_spec(rows, 0), pl.BlockSpec((8, rows), lambda p: (p, 0))],
        out_shape=[
            jax.ShapeDtypeStruct((rows, width), BF16),
            jax.ShapeDtypeStruct((8 * pairs, rows), F32),
        ],
        compiler_params=params(),
        cost_estimate=cost(16 * rows * rows * width, 16 * rows * width),
        name="self_forward",
    )(qkv, qkv, qkv, kvo, kvo, own, oth)


def cross_forward_kernel(size, q_ref, k_ref, v_ref, ko_ref, vo_ref, t_ref, own_ref, oth_ref, o_ref, lse_ref):
    rows = q_ref.shape[0]
    masks = head_masks(BF16)
    outs = head_masks(F32)
    qcode = query_code(t_ref[...])
    keys = [
        jnp.concatenate([k_ref[...], own_ref[...]], axis=1),
        jnp.concatenate([ko_ref[...], oth_ref[...]], axis=1),
    ]
    values = [v_ref[...], vo_ref[...]]
    for block in range(rows // size):
        at = slice(block * size, (block + 1) * size)
        lses, result = [], 0.0
        for mask, keep in zip(masks, outs):
            q = jnp.concatenate([q_ref[at] * (mask * BF16(HD**-0.5)), qcode[at]], axis=1)
            out, lse = softmax_pieces([nt(q, k) for k in keys], values)
            result = result + out * keep
            lses.append(lse)
        o_ref[at] = result.astype(BF16)
        store_lse(lse_ref, block, size, *lses)


def cross_forward(cq, kv, kvo, t, own, oth):
    rows, width = cq.shape
    pairs = width // PAIR
    return pl.pallas_call(
        functools.partial(cross_forward_kernel, 256),
        grid=(pairs,),
        in_specs=[
            pair_spec(rows, 0),
            pair_spec(rows, 0),
            pair_spec(rows, pairs),
            pair_spec(rows, 0),
            pair_spec(rows, pairs),
            whole((rows, 128)),
            whole((rows, 128)),
            whole((rows, 128)),
        ],
        out_specs=[pair_spec(rows, 0), pl.BlockSpec((8, rows), lambda p: (p, 0))],
        out_shape=[
            jax.ShapeDtypeStruct((rows, width), BF16),
            jax.ShapeDtypeStruct((8 * pairs, rows), F32),
        ],
        compiler_params=params(),
        cost_estimate=cost(24 * rows * rows * width, 16 * rows * width),
        name="cross_forward",
    )(cq, kv, kv, kvo, kvo, t, own, oth)


def delta_rows(g, o):
    prod = g.astype(F32) * o.astype(F32)
    upper = prod.astype(BF16)
    lower = (prod - upper.astype(F32)).astype(BF16)
    row = lax.broadcasted_iota(jnp.int32, (8, PAIR), 0)
    lane = lax.broadcasted_iota(jnp.int32, (8, PAIR), 1)
    pick = jnp.where(row == lane // HD, 1.0, 0.0).astype(BF16)
    return nt(pick, upper) + nt(pick, lower)


def back_piece(keys, values, q, g, lse, delta, causal):
    s = nt(keys, q)
    if causal:
        row = lax.broadcasted_iota(jnp.int32, s.shape, 0)
        col = lax.broadcasted_iota(jnp.int32, s.shape, 1)
        s = jnp.where(row <= col, s, -FAR)
    p = jnp.exp(s - lse)
    ds = p * (nt(values, g) - delta)
    return p.astype(BF16), ds.astype(BF16)


def cross_backward_kernel(
    size, q_ref, k_ref, v_ref, ko_ref, vo_ref, g_ref, o_ref, lse_ref, t_ref, own_ref, oth_ref,
    m_ref, mo_ref, wk_ref, wv_ref,
    dq_ref, dm_ref, dmo_ref, gk_ref, gv_ref, gb_ref, dm_acc, dmo_acc, mt_ref, mot_ref,
):
    step = pl.program_id(0)

    @pl.when(step == 0)
    def _():
        mt_ref[...] = jnp.transpose(m_ref[...])
        mot_ref[...] = jnp.transpose(mo_ref[...])

    rows = q_ref.shape[0]
    masks = head_masks(BF16)
    scale = BF16(HD**-0.5)
    qcode = query_code(t_ref[...])
    delta = delta_rows(g_ref[...], o_ref[...])
    lse = lse_ref[...]
    halves = [(k_ref, v_ref, own_ref, mt_ref, dm_acc), (ko_ref, vo_ref, oth_ref, mot_ref, dmo_acc)]
    dq = [0.0] * (rows // size)
    gk = gv = gb = 0.0
    for kr, vr, code, mem, acc in halves:
        keys = jnp.concatenate([kr[...], code[...]], axis=1)
        values = vr[...]
        dk = dv = 0.0
        for block in range(rows // size):
            at = slice(block * size, (block + 1) * size)
            for head, mask in enumerate(masks):
                qm = q_ref[at] * (mask * scale)
                gm = g_ref[at] * mask
                q = jnp.concatenate([qm, qcode[at]], axis=1)
                p, ds = back_piece(
                    keys, values, q, gm, lse[head : head + 1, at], delta[head : head + 1, at], False
                )
                dk = dk + nn(ds, qm)
                dv = dv + nn(p, gm)
                dq[block] = dq[block] + tn(ds, kr[...] * (mask * scale))
        both = jnp.concatenate([dk.astype(BF16), dv.astype(BF16)], axis=1)
        grad = nn(mem[...], both)
        gk, gv = gk + grad[:, :PAIR], gv + grad[:, PAIR:]
        gb = gb + total(both[:, PAIR:])
        dm = nt(both, jnp.concatenate([wk_ref[...], wv_ref[...]], axis=1))

        @pl.when(step == 0)
        def _():
            acc[...] = dm

        @pl.when(step > 0)
        def _():
            acc[...] += dm
    for block in range(rows // size):
        dq_ref[block * size : (block + 1) * size] = dq[block].astype(BF16)
    gk_ref[...] = gk.astype(BF16)
    gv_ref[...] = gv.astype(BF16)
    gb_ref[...] = gb

    @pl.when(step == pl.num_programs(0) - 1)
    def _():
        dm_ref[...] = dm_acc[...]
        dmo_ref[...] = dmo_acc[...].astype(BF16)


def cross_backward(cq, kv, kvo, g, o, lse, t, own, oth, m, mo, w, schedule):
    rows, width = cq.shape
    pairs = width // PAIR
    flat = jax.ShapeDtypeStruct((rows, width), BF16)
    square = jax.ShapeDtypeStruct((width, width), BF16)
    return run(
        functools.partial(cross_backward_kernel, 256), "cross_backward", pairs,
        (cq, kv, kv, kvo, kvo, g, o, lse, t, own, oth, m, mo, w, w),
        [
            pair_spec(rows, 0),
            pair_spec(rows, 0),
            pair_spec(rows, pairs),
            pair_spec(rows, 0),
            pair_spec(rows, pairs),
            pair_spec(rows, 0),
            pair_spec(rows, 0),
            pl.BlockSpec((8, rows), lambda p: (p, 0)),
            whole((rows, 128)),
            whole((rows, 128)),
            whole((rows, 128)),
            whole((rows, width)),
            whole((rows, width)),
            pair_spec(width, 0),
            pair_spec(width, pairs),
        ],
        [flat, jax.ShapeDtypeStruct((rows, width), F32), flat, square, square, jax.ShapeDtypeStruct((1, width), F32)],
        [pair_spec(rows, 0)] + [whole((rows, width))] * 2 + [pair_spec(width, 0)] * 2 + [pair_spec(1, 0)],
        [pltpu.VMEM((rows, width), F32)] * 2 + [pltpu.VMEM((width, rows), BF16)] * 2,
        schedule, 3,
        64 * rows * rows * width + 16 * rows * width * width, 24 * rows * width,
    )


def front_pairs(pairs):
    return 2 * pairs // 3


def self_backward_kernel(
    size, q_ref, k_ref, v_ref, ko_ref, vo_ref, g_ref, o_ref, lse_ref, own_ref, oth_ref,
    x_ref, xo_ref, wq_ref, wk_ref, wv_ref, dh1_ref, sa_ref, sb_ref, sc_ref, sd_ref,
    dx_ref, grad_ref,
    dq_acc, dx_acc, dxo_acc, dkv_acc, xt_ref, xot_ref, dxo_ref, came_ref, turn_ref, send_ref, recv_ref,
):
    step = pl.program_id(0)
    sp = lax.axis_index("sp")
    second = sp == 1
    rows, width = x_ref.shape
    pairs = width // PAIR
    pair = lax.rem(step, pairs)
    cols = pl.ds(pl.multiple_of(pair * PAIR, PAIR), PAIR)
    masks = head_masks(BF16)
    scale = BF16(HD**-0.5)
    count = rows // size
    over = remote(dxo_ref, came_ref, send_ref.at[0], recv_ref.at[0], ("y",))

    def pieces():
        qcode = query_code(own_ref[...])
        delta = delta_rows(g_ref[...], o_ref[...])
        for block in range(count):
            at = slice(block * size, (block + 1) * size)
            for head, mask in enumerate(masks):
                qm = q_ref[at] * (mask * scale)
                gm = g_ref[at] * mask
                q = jnp.concatenate([qm, qcode[at]], axis=1)
                yield block, mask, qm, gm, q, lse_ref[head : head + 1, at], delta[head : head + 1, at]

    @pl.when(step == 0)
    def _():
        xt_ref[...] = jnp.transpose(x_ref[...])
        turn_ref[...] = jnp.zeros(turn_ref.shape, F32)
        turn_ref[0:8] = sa_ref[...]
        turn_ref[8:16] = sb_ref[...]
        turn_ref[16:17] = sc_ref[...]
        turn_ref[17:21] = sd_ref[...]

    @pl.when(jnp.logical_and(step == 0, second))
    def _():
        xot_ref[...] = jnp.transpose(xo_ref[...])

    @pl.when(jnp.logical_and(step < pairs, second))
    def _():
        keys = jnp.concatenate([ko_ref[...], oth_ref[...]], axis=1)
        values = vo_ref[...]
        dk = dv = 0.0
        dq = [0.0] * count
        for block, mask, qm, gm, q, lse, delta in pieces():
            p, ds = back_piece(keys, values, q, gm, lse, delta, False)
            dk = dk + nn(ds, qm)
            dv = dv + nn(p, gm)
            dq[block] = dq[block] + tn(ds, ko_ref[...] * (mask * scale))
        for block in range(count):
            dq_acc[pair, block * size : (block + 1) * size] = dq[block]
        both = jnp.concatenate([dk.astype(BF16), dv.astype(BF16)], axis=1)
        dkv_acc[pair] = both
        dxo = nt(both, jnp.concatenate([wk_ref[...], wv_ref[...]], axis=1))

        @pl.when(step == 0)
        def _():
            dxo_acc[...] = dxo

        @pl.when(step > 0)
        def _():
            dxo_acc[...] += dxo

    @pl.when(jnp.logical_and(step == pairs - 1, second))
    def _():
        dxo_ref[...] = dxo_acc[...].astype(BF16)
        over.start()

    @pl.when(step >= pairs)
    def _():
        dq, dk, dv = [0.0] * count, [0.0] * count, [0.0] * count
        for block, mask, qm, gm, q, lse, delta in pieces():
            for part in range(block + 1):
                of = slice(part * size, (part + 1) * size)
                keys = jnp.concatenate([k_ref[of], own_ref[of]], axis=1)
                p, ds = back_piece(keys, v_ref[of], q, gm, lse, delta, part == block)
                dk[part] = dk[part] + nn(ds, qm)
                dv[part] = dv[part] + nn(p, gm)
                dq[block] = dq[block] + tn(ds, k_ref[of] * (mask * scale))
        dq, dk, dv = (jnp.concatenate(a, axis=0) for a in (dq, dk, dv))
        dq = jnp.where(second, dq + dq_acc[pair], dq)
        dqk = jnp.concatenate([dq.astype(BF16), dk.astype(BF16)], axis=1)
        dv = dv.astype(BF16)
        grad_qk = nn(xt_ref[...], dqk)
        grad_v = nn(xt_ref[...], dv)
        shape = grad_ref.shape[:-1] + (PAIR,)
        lead = (slice(None),) * (len(shape) - 1)
        cut = front_pairs(pairs)

        def put(n, grad):
            col = jnp.where(pair < cut, n * cut + pair, 3 * cut + n * (pairs - cut) + pair - cut + 2 * (n > 0))
            to = pl.ds(pl.multiple_of(col * PAIR, PAIR), PAIR)
            grad_ref[lead + (to,)] = grad.astype(BF16).reshape(shape)

        put(0, grad_qk[:, :PAIR])
        turn_ref[21:22, cols] = total(dqk[:, :PAIR])

        @pl.when(second)
        def _():
            grad_o = nn(xot_ref[...], dkv_acc[pair])
            put(1, grad_qk[:, PAIR:] + grad_o[:, :PAIR])
            put(2, grad_v + grad_o[:, PAIR:])
            turn_ref[22:23, cols] = total(dv) + total(dkv_acc[pair, :, PAIR:])

        @pl.when(jnp.logical_not(second))
        def _():
            put(1, grad_qk[:, PAIR:])
            put(2, grad_v)
            turn_ref[22:23, cols] = total(dv)

        dx = nt(dqk, jnp.concatenate([wq_ref[...], wk_ref[...]], axis=1)) + nt(dv, wv_ref[...])

        @pl.when(step == pairs)
        def _():
            dx_acc[...] = dh1_ref[...] + dx

        @pl.when(step > pairs)
        def _():
            dx_acc[...] += dx

    @pl.when(step == 2 * pairs - 1)
    def _():
        shape = grad_ref.shape[:-1] + (2 * PAIR,)
        lead = (slice(None),) * (len(shape) - 1)
        col = (2 * front_pairs(pairs) + pairs) * PAIR
        grad_ref[lead + (slice(col, col + 2 * PAIR),)] = jnp.transpose(turn_ref[...]).astype(BF16).reshape(shape)


def self_backward_finale(*refs):
    dx_ref, dx_acc, dxo_ref, came_ref, send_ref, recv_ref = (refs[i] for i in (20, 23, 28, 29, 31, 32))
    over = remote(dxo_ref, came_ref, send_ref.at[0], recv_ref.at[0], ("y",))

    @pl.when(lax.axis_index("sp") == 0)
    def _():
        over.wait_recv()
        dx_ref[...] = (dx_acc[...] + came_ref[...].astype(F32)).astype(BF16)

    @pl.when(lax.axis_index("sp") == 1)
    def _():
        over.wait_send()
        dx_ref[...] = dx_acc[...].astype(BF16)


GRADS = 21


def self_backward(block, qkv, kvo, g, o, lse, own, oth, x, xo, w, dh1, small, schedule):
    rows, width = x.shape
    pairs = width // PAIR

    def pair_of(offset):
        return pl.BlockSpec((rows, PAIR), lambda s: (0, lax.rem(s, pairs) + offset))

    def weight(offset):
        return pl.BlockSpec((width, PAIR), lambda s: (0, lax.rem(s, pairs) + offset))

    made = block + (3 * width + 2 * PAIR,)
    outs = [jax.ShapeDtypeStruct((rows, width), BF16)]
    specs = [whole((rows, width))]
    held = []
    if schedule:
        held += [pltpu.VMEM(made, BF16)]
    else:
        outs += [jax.ShapeDtypeStruct(made, BF16)]
        specs += [whole(made)]
    held += [
        pltpu.VMEM((pairs, rows, PAIR), F32),
        pltpu.VMEM((rows, width), F32),
        pltpu.VMEM((rows, width), F32),
        pltpu.VMEM((pairs, rows, 2 * PAIR), BF16),
        pltpu.VMEM((width, rows), BF16),
        pltpu.VMEM((width, rows), BF16),
        pltpu.VMEM((rows, width), BF16),
        pltpu.VMEM((rows, width), BF16),
        pltpu.VMEM((2 * PAIR, width), F32),
        pltpu.SemaphoreType.DMA((1,)),
        pltpu.SemaphoreType.DMA((1,)),
    ]
    return run(
        functools.partial(self_backward_kernel, 256), "self_backward", 2 * pairs,
        (qkv, qkv, qkv, kvo, kvo, g, o, lse, own, oth, x, xo, w, w, w, dh1) + tuple(small),
        [
            pair_of(0),
            pair_of(pairs),
            pair_of(2 * pairs),
            pair_of(0),
            pair_of(pairs),
            pair_of(0),
            pair_of(0),
            pl.BlockSpec((8, rows), lambda s: (lax.rem(s, pairs), 0)),
            whole((rows, 128)),
            whole((rows, 128)),
            whole((rows, width)),
            whole((rows, width)),
            weight(0),
            weight(pairs),
            weight(2 * pairs),
            whole((rows, width)),
        ] + [whole(a.shape) for a in small],
        outs, specs, held, schedule, 5,
        48 * rows * rows * width + 20 * rows * width * width, 12 * width * width + 40 * rows * width,
        (("y",),), self_backward_finale,
    )


def first_norm_kernel(x_ref, ctx_ref, wo_ref, wq_ref, b_ref, h_ref, cq_ref):
    h = x_ref[...].astype(F32) + nn(ctx_ref[...], wo_ref[...]) + b_ref[3:4]
    h_ref[...] = h
    n, _ = normed(h)
    a = (n * b_ref[4:5] + b_ref[5:6]).astype(BF16)
    cq_ref[...] = (nn(a, wq_ref[...]) + b_ref[6:7]).astype(BF16)


def first_norm(x, ctx, wo, wq, biases):
    rows, width = x.shape
    return pl.pallas_call(
        first_norm_kernel,
        out_shape=[
            jax.ShapeDtypeStruct((rows, width), F32),
            jax.ShapeDtypeStruct((rows, width), BF16),
        ],
        compiler_params=params(),
        cost_estimate=cost(4 * rows * width * width, 4 * width * width + 10 * rows * width),
        name="first_norm",
    )(x, ctx, wo, wq, biases)


def feed_kernel(
    count, comm, h1_ref, cc_ref, ct_ref, wco_ref, b_ref, wi_ref, wo_ref,
    out_ref, dh2_ref, dcc_ref, gco_ref, *refs,
):
    if comm:
        gwi_ref, refs = refs[0], refs[1:]
    else:
        gwi_ref, gwo_ref, refs = refs[0], refs[1], refs[2:]
    small_ref, gib_ref, hid_ref, slope_ref, n2_ref, r2_ref, a2b_ref, acc_ref, df_ref, *refs = refs
    step = pl.program_id(0)
    width = acc_ref.shape[1]

    if comm:
        mi_ref, mo_ref, ci_ref, co_ref, send_ref, recv_ref = refs
        wide = ci_ref.shape[-1]
        here = place()
        c = here[1]

        def chunk_copies(j):
            at = pl.ds(pl.multiple_of(j * width, width), width)
            return [
                remote(mi_ref.at[:, :, at], ci_ref.at[:, :, at], send_ref.at[0, j], recv_ref.at[0, j], ("core",), here),
                remote(mo_ref.at[j], co_ref.at[j], send_ref.at[1, j], recv_ref.at[1, j], ("core",), here),
            ]

    @pl.when(step == 0)
    def _():
        if comm:
            greet([("core",)])
        n1, _ = normed(h1_ref[...])
        a1 = n1 * b_ref[4:5] + b_ref[5:6]
        h2 = a1 + nn(cc_ref[...], wco_ref[...]) + b_ref[7:8]
        n2, r2 = normed(h2)
        n2_ref[...] = n2
        r2_ref[...] = jnp.broadcast_to(r2, r2_ref.shape)
        a2 = n2 * b_ref[8:9] + b_ref[9:10]
        a2b_ref[...] = a2.astype(BF16)
        acc_ref[...] = a2 + b_ref[10:11]

    @pl.when(step < count)
    def _():
        u = nn(a2b_ref[...], wi_ref[...]) + b_ref[pl.ds(13 + step, 1)]
        cumul = 0.5 * (1.0 + lax.erf(u * 0.7071067811865476))
        density = jnp.exp(-0.5 * u * u) * 0.3989422804014327
        hid = (u * cumul).astype(BF16)
        hid_ref[step] = hid
        slope_ref[step] = cumul + u * density
        acc_ref[...] += nn(hid, wo_ref[...])

    @pl.when(step == count - 1)
    def _():
        n3, r3 = normed(acc_ref[...])
        gain = b_ref[11:12]
        out_ref[...] = (n3 * gain + b_ref[12:13]).astype(BF16)
        e = ct_ref[...].astype(F32)
        d3 = norm_back(e, n3, r3, gain)
        df = d3.astype(BF16)
        df_ref[...] = df
        acc_ref[...] = d3
        small_ref[0:1] = total(e * n3)
        small_ref[1:2] = total(e)
        small_ref[2:3] = total(df)

    @pl.when(jnp.logical_and(step >= count, step < 2 * count))
    def _():
        j = step - count
        df = df_ref[...]
        du = (nt(df, wo_ref[...]) * slope_ref[j]).astype(BF16)
        gib_ref[...] = total(du)
        acc_ref[...] += nt(du, wi_ref[...])
        go = tn(hid_ref[j], df).astype(BF16)
        gi = tn(a2b_ref[...], du).astype(BF16)
        if comm:
            at = pl.ds(pl.multiple_of(j * width, width), width)
            eight, narrow = gwi_ref.shape[:2]
            gi = gi.reshape(eight, 2, narrow, width)
            go = go.reshape(2, 2, 4, narrow, width)
            gwi_ref[:, :, at] = jnp.where(c == 0, gi[:, 0], gi[:, 1])
            mi_ref[:, :, at] = jnp.where(c == 0, gi[:, 1], gi[:, 0])
            mo_ref[j] = jnp.where(c == 0, go[:, 1], go[:, 0])
            for i in range(4):
                gwi_ref[pl.ds(2 * j, 2), :, pl.ds(wide + i * width, width)] = jnp.where(c == 0, go[:, 0, i], go[:, 1, i])
            for copy in chunk_copies(j):
                copy.start()
        else:
            gwo_ref[...] = go
            gwi_ref[...] = gi

    @pl.when(step == 2 * count)
    def _():
        d2 = acc_ref[...]
        n2 = n2_ref[...]
        dh2 = norm_back(d2, n2, r2_ref[:, :1], b_ref[8:9])
        dh2_ref[...] = dh2
        dco = dh2.astype(BF16)
        dcc_ref[...] = nt(dco, wco_ref[...]).astype(BF16)
        gco_ref[...] = tn(cc_ref[...], dco).astype(BF16)
        small_ref[3:4] = total(d2 * n2)
        small_ref[4:5] = total(d2)
        small_ref[5:6] = total(dco)
        small_ref[6:8] = jnp.zeros((2, d2.shape[1]), F32)

    if comm:

        @pl.when(step > count)
        def _():
            j = step - count - 1
            at = pl.ds(pl.multiple_of(j * width, width), width)
            for copy in chunk_copies(j):
                copy.wait()
            gwi_ref[:, :, at] += ci_ref[:, :, at]
            for i in range(4):
                gwi_ref[pl.ds(2 * j, 2), :, pl.ds(wide + i * width, width)] += co_ref[j, :, i]


def feed(size, comm, h1, cc, ct, wco, biases, wi, wo):
    rows, width = h1.shape
    wide = wi.shape[1]
    chunk = width
    count = wide // chunk

    def weight(s):
        return jnp.where(s < count, s, jnp.minimum(s - count, count - 1))

    def early(s):
        return jnp.clip(s - count, 0, count - 1)

    flat = whole((rows, width))
    square = whole((width, width))
    scratch = [
        pltpu.VMEM((count, rows, chunk), BF16),
        pltpu.VMEM((count, rows, chunk), F32),
        pltpu.VMEM((rows, width), F32),
        pltpu.VMEM((rows, 128), F32),
        pltpu.VMEM((rows, width), BF16),
        pltpu.VMEM((rows, width), F32),
        pltpu.VMEM((rows, width), BF16),
    ]
    if comm:
        narrow = width // size
        grad_specs = [whole((size // 2, narrow, 2 * wide))]
        grad_shapes = [(size // 2, narrow, 2 * wide)]
        scratch += [
            pltpu.VMEM((size // 2, narrow, wide), BF16),
            pltpu.VMEM((count, 2, 4, narrow, width), BF16),
            pltpu.VMEM((size // 2, narrow, wide), BF16),
            pltpu.VMEM((count, 2, 4, narrow, width), BF16),
            pltpu.SemaphoreType.DMA((2, count)),
            pltpu.SemaphoreType.DMA((2, count)),
        ]
    else:
        grad_specs = [
            pl.BlockSpec((width, chunk), lambda s: (0, early(s))),
            pl.BlockSpec((chunk, width), lambda s: (early(s), 0)),
        ]
        grad_shapes = [(width, wide), (wide, width)]
    return pl.pallas_call(
        functools.partial(feed_kernel, count, comm),
        grid=(2 * count + 1,),
        in_specs=[
            flat, flat, flat, square, whole(biases.shape),
            pl.BlockSpec((width, chunk), lambda s: (0, weight(s))),
            pl.BlockSpec((chunk, width), lambda s: (weight(s), 0)),
        ],
        out_specs=[flat, flat, flat, square]
        + grad_specs
        + [whole((8, width)), pl.BlockSpec((1, chunk), lambda s: (0, early(s)))],
        out_shape=[
            jax.ShapeDtypeStruct((rows, width), BF16),
            jax.ShapeDtypeStruct((rows, width), F32),
            jax.ShapeDtypeStruct((rows, width), BF16),
            jax.ShapeDtypeStruct((width, width), BF16),
        ]
        + [jax.ShapeDtypeStruct(a, BF16) for a in grad_shapes]
        + [
            jax.ShapeDtypeStruct((8, width), F32),
            jax.ShapeDtypeStruct((1, wide), F32),
        ],
        scratch_shapes=scratch,
        compiler_params=params(2 if comm else None),
        cost_estimate=cost(
            12 * rows * width * wide + 6 * rows * width * width, 12 * width * wide + 16 * rows * width
        ),
        name="feed",
    )(h1, cc, ct, wco, biases, wi, wo)


def first_back_kernel(
    dcq_ref, dh2_ref, h1_ref, ctx_ref, wcq_ref, wso_ref, b_ref,
    dh1_ref, dsc_ref, gcq_ref, gso_ref, small_ref,
):
    gain = b_ref[4:5]
    n1, r1 = normed(h1_ref[...])
    a1b = (n1 * gain + b_ref[5:6]).astype(BF16)
    dcq = dcq_ref[...]
    d1 = dh2_ref[...] + nt(dcq, wcq_ref[...])
    dh1 = norm_back(d1, n1, r1, gain)
    dh1_ref[...] = dh1
    dso = dh1.astype(BF16)
    dsc_ref[...] = nt(dso, wso_ref[...]).astype(BF16)
    gcq_ref[...] = tn(a1b, dcq).astype(BF16)
    gso_ref[...] = tn(ctx_ref[...], dso).astype(BF16)
    small_ref[0:1] = total(dcq)
    small_ref[1:2] = total(d1 * n1)
    small_ref[2:3] = total(d1)
    small_ref[3:4] = total(dso)
    small_ref[4:8] = jnp.zeros((4, dh1.shape[1]), F32)


def first_back(dcq, dh2, h1, ctx, wcq, wso, biases, schedule):
    rows, width = dcq.shape
    flat, square = whole((rows, width)), whole((width, width))
    return run(
        first_back_kernel, "first_back", 1,
        (dcq, dh2, h1, ctx, wcq, wso, biases),
        [flat, flat, flat, flat, square, square, whole(biases.shape)],
        [
            jax.ShapeDtypeStruct((rows, width), F32),
            jax.ShapeDtypeStruct((rows, width), BF16),
            jax.ShapeDtypeStruct((width, width), BF16),
            jax.ShapeDtypeStruct((width, width), BF16),
            jax.ShapeDtypeStruct((8, width), F32),
        ],
        [flat, flat, square, square, whole((8, width))],
        (), schedule, 4,
        8 * rows * width * width, 8 * width * width + 18 * rows * width,
    )


def outputs_kernel(moves, count, line, *refs):
    pieces, rest = refs[:count], refs[count:]
    out_ref, dx_ref, dm_ref, dmi_ref = rest[:4]
    outs = rest[4:]
    for piece, first, wide, which, row, col in moves:
        ref = pieces[piece]
        outs[which][row : row + ref.shape[0], col : col + wide] = ref[:, first : first + wide].astype(F32)
    turned, result, dx, dm = outs[-4:]
    turned[...] = jnp.transpose(pieces[line[0]][:, line[1] : line[1] + PAIR].astype(F32))
    result[...] = out_ref[...]
    dx[...] = dx_ref[...]
    dm[...] = (dm_ref[...] + dmi_ref[...].astype(F32)).astype(BF16)


def outputs(pieces, moves, line, shapes, out, dx, dm, dmi):
    ins = tuple(pieces) + (out, dx, dm, dmi)
    result = jax.ShapeDtypeStruct(out.shape, BF16)
    return pl.pallas_call(
        functools.partial(outputs_kernel, moves, len(pieces), line),
        out_shape=[jax.ShapeDtypeStruct(a, F32) for a in shapes]
        + [jax.ShapeDtypeStruct((PAIR, pieces[0].shape[0]), F32), result, result, result],
        compiler_params=params(),
        cost_estimate=cost(0, 12 << 20),
        name="outputs",
    )(*ins)


def moved(pieces, targets):
    out = []
    for n, (start, wide) in enumerate(pieces):
        for first, cols, which, row, col in targets:
            low, high = max(start, first), min(start + wide, first + cols)
            if low < high:
                out.append((n, low - start, high - low, which, row, col + low - first))
    return out


def swap_sum(part, axis, pairs):
    came = lax.ppermute(part, axis, pairs)
    return part.astype(F32) + came.astype(F32)


def sum_scatter(grad, size, order):
    rows, cols = grad.shape
    bits = size.bit_length() - 1
    me = lax.axis_index("dp")
    now = grad.reshape((2,) * bits + (rows // size, cols))
    left = list(range(bits))[::-1]
    for bit in [b for b in order if b < bits] + [b for b in range(bits) if b not in order]:
        axis = left.index(bit)
        mine = (me >> bit) & 1
        keep = lax.dynamic_index_in_dim(now, mine, axis, keepdims=False)
        send = lax.dynamic_index_in_dim(now, 1 - mine, axis, keepdims=False)
        came = lax.ppermute(send, "dp", [(i, i ^ (1 << bit)) for i in range(size)])
        now = (keep.astype(F32) + came.astype(F32)).astype(BF16)
        left.pop(axis)
    return swap_sum(now, "sp", [(0, 1), (1, 0)])


def per_device(
    size,
    inputs,
    memory,
    target_docs,
    memory_docs,
    cotangent,
    w_qkv,
    b_q,
    b_v,
    w_so,
    b_so,
    g_one,
    s_one,
    w_cq,
    b_cq,
    w_ckv,
    b_cv,
    w_co,
    b_co,
    g_two,
    s_two,
    w_fi,
    b_fi,
    w_fo,
    b_fo,
    g_three,
    s_three,
):
    rows, width = inputs.shape[1:]
    wide = b_fi.shape[0]
    comm = size == 16
    narrow, broad = width // size, wide // size
    swap = [(0, 1), (1, 0)]
    x, mem, ct = inputs[0], memory[0], cotangent[0]
    x_o = lax.ppermute(x, "sp", [(0, 1)])
    docs_o = lax.ppermute(jnp.concatenate([target_docs, memory_docs], axis=0), "sp", swap)
    line = lax.broadcasted_iota(jnp.int32, (24, width), 0)
    vectors = (b_q, b_v, b_cv, b_so, g_one, s_one, b_cq, b_co, g_two, s_two, b_fo, g_three, s_three)
    vectors += tuple(b_fi[i : i + width] for i in range(0, wide, width))
    biases = jnp.zeros((24, width), F32)
    for i, v in enumerate(vectors):
        biases = jnp.where(line == i, v.astype(F32)[None], biases)

    qkv, mkv, t_own, m_own = project_own(x, mem, target_docs, memory_docs, w_qkv, w_ckv, biases)
    kvo, mem_s, t_oth, m_oth = project_other(x_o, mem, docs_o[:1], docs_o[1:], w_qkv, biases, t_own)
    mem_o = lax.ppermute(mem_s, "sp", swap)
    ctx, lse = self_forward(qkv, kvo, t_own, t_oth)
    h1, cq = first_norm(x, ctx, w_so, w_cq, biases)
    mkvo = project_memory(mem_o, w_ckv, biases)
    cc, clse = cross_forward(cq, mkv, mkvo, t_own, m_own, m_oth)
    output, dh2, dcc, gco, gwi, *gwo, small_a, gib = feed(size, comm, h1, cc, ct, w_co, biases, w_fi, w_fo)
    turned = gib.reshape(width, -1).T

    block = (2, 2, 2, 2, narrow) if comm else (width,)
    at_cross, at_first, at_self = (), (), ()
    ways = (VIA_X, VIA_Y, VIA_Z)

    def thirds(array, shape, dims):
        wide = shape[-1] // 3
        return [Flow(array, shape, hops, dims, (i * wide, wide)) for i, hops in enumerate(ways)]

    if comm:
        gwi = gwi.reshape(block[:3] + gwi.shape[1:])
        t0 = thirds(gwi, gwi.shape, BLOCK[:3])
        at_cross = ((t0, 0, 4), (t0, 4, 6))
    dcq, dm, dmo, gck, gcv, gcvb = cross_backward(
        cq, mkv, mkvo, dcc, cc, clse, t_own, m_own, m_oth, mem, mem_o, w_ckv, at_cross
    )
    dm_in = lax.ppermute(dmo, "sp", swap)
    if comm:
        at_first = ((t0, 0, 1),)
    dh1, dsc, gcq, gso, small_b = first_back(dcq, dh2, h1, ctx, w_cq, w_so, biases, at_first)
    if comm:
        fresh = [
            Flow(g.reshape(block + (width,)), block + (width,), ("core",)) for g in (gck, gcv, gco, gcq, gso)
        ]
        joint = Joint()
        mid = block[:3] + (narrow, 5 * width)
        t1_cols = ((0, 2048), (2048, 5 * width - 2048))
        t1 = [Flow(joint, mid, hops, BLOCK[:3], cols) for hops, cols in zip((X_FIRST, Z_FIRST), t1_cols)]
        cut = front_pairs(width // PAIR) * PAIR
        end = 3 * width + 2 * PAIR
        t2_cols = ((0, 3 * cut // 2), (3 * cut // 2, 3 * cut // 2), (3 * cut, end - 3 * cut))
        t2 = [
            Flow(("ref", GRADS), block + (end,), ("core",) + hops, BLOCK, cols)
            for hops, cols in zip((X_FIRST, Z_FIRST, AT_ONCE), t2_cols)
        ]
        front, back = t2[:2], t2[2:]
        at_self = (
            (fresh, 0, 2, joint), (t0, 0, 3), (t0[1:], 3, 6),
            (t1, 2, 8), (t1, 8, 10), (t1, 10, 11), (t1, 11, 12),
            (front, 10, 11), (front, 11, 12), (front, 12, 13), (front, 13, 14), (front, 14, 15),
            (back, 12, 13), (back, 13, 14), (back, 14, 15), (back, 15, 16),
        )
    dx, *made = self_backward(
        block, qkv, kvo, dsc, ctx, lse, t_own, t_oth, x, x_o, w_qkv, dh1, (small_a, small_b, gcvb, turned), at_self
    )
    if comm:
        spans = [(i * 2 * wide // 3, 2 * wide // 3) for i in range(3)]
        moves = moved(spans, [(0, wide, 2, 0, 0)] + [(wide + i * width, width, 3, i * narrow, 0) for i in range(4)])
        targets = [(0, 2 * width, 1, 0, 0)] + [((2 + i) * width, width, 4 + i, 0, 0) for i in range(3)]
        moves += [(m[0] + 3,) + m[1:] for m in moved(t1_cols, targets)]
        rest = width - cut
        targets = []
        for i in range(3):
            targets += [(i * cut, cut, 0, 0, i * width)]
            targets += [(3 * cut + i * rest + 2 * PAIR * (i > 0), rest, 0, 0, i * width + cut)]
        moves += [(m[0] + 5,) + m[1:] for m in moved(t2_cols, targets)]
        shapes = [(narrow, 3 * width), (narrow, 2 * width), (narrow, wide), (broad, width)] + [(narrow, width)] * 3
        t_qkv, t_cmem, t_fin, t_fout, t_cout, t_cquery, t_out, lines, output, derivative, grad_memory = outputs(
            [f.array for f in t0 + t1 + t2], moves, (7, rest), shapes, output, dx, dm, dm_in
        )
    else:
        cut = front_pairs(width // PAIR) * PAIR
        rest = width - cut
        (gqkv,) = made
        at = [0, cut, 2 * cut, 3 * cut, 3 * cut + rest + 2 * PAIR, 3 * cut + 2 * rest + 2 * PAIR]
        columns = gqkv[:, 3 * cut + rest : 3 * cut + rest + PAIR]
        gqkv = jnp.concatenate(
            [gqkv[:, a : a + n] for i in range(3) for a, n in ((at[i], cut), (at[3 + i], rest))], axis=1
        )
        t_fin, t_fout, t_cout, t_cquery, t_out, t_cmem, t_qkv, lines = (
            sum_scatter(g, size, (0, 1, 2, 3))
            for g in (
                gwi, gwo[0], gco, gcq, gso, jnp.concatenate([gck, gcv], axis=1),
                gqkv, columns,
            )
        )
        lines, derivative = lines.T, dx
        grad_memory = (dm + dm_in.astype(F32)).astype(BF16)
    t_gthree, t_sthree, t_fobias, t_gtwo, t_stwo, t_cobias = (lines[i] for i in range(6))
    t_cqbias, t_gone, t_sone, t_obias = (lines[i] for i in range(8, 12))
    t_cvbias, t_qbias, t_vbias = lines[16], lines[21], lines[22]
    t_fibias = lines[17:21].T.reshape(-1)
    return (
        output[None],
        derivative[None],
        grad_memory[None],
        t_qkv,
        t_qbias,
        t_vbias,
        t_out,
        t_obias,
        t_gone,
        t_sone,
        t_cquery,
        t_cqbias,
        t_cmem,
        t_cvbias,
        t_cout,
        t_cobias,
        t_gtwo,
        t_stwo,
        t_fin,
        t_fibias,
        t_fout,
        t_fobias,
        t_gthree,
        t_sthree,
    )


def solution(mesh):
    split = P("dp", "sp", None)
    in_specs = (split, split, P("dp", "sp"), P("dp", "sp"), split) + (P(),) * 21
    matrix, vector = P("dp", None), P("dp")
    out_specs = (
        split, split, split,
        matrix, vector, vector,
        matrix, vector, vector, vector,
        matrix, vector,
        matrix, vector,
        matrix, vector, vector, vector,
        matrix, vector,
        matrix, vector, vector, vector,
    )
    return jax.shard_map(
        functools.partial(per_device, mesh.shape["dp"]),
        mesh=mesh, in_specs=in_specs, out_specs=out_specs, check_vma=False,
    )
```

```python
import functools

import jax
import jax.numpy as jnp
from jax import lax
from jax.experimental import pallas as pl
from jax.experimental.pallas import tpu as pltpu
from jax.sharding import PartitionSpec as P

HD = 64
PAIR = 2 * HD
EPS = 1e-05
FAR = 1.0e9
VMEM = 60 * 1024 * 1024
F32 = jnp.float32
BF16 = jnp.bfloat16


def nn(a, b):
    return lax.dot_general(a, b, (((1,), (0,)), ((), ())), preferred_element_type=F32)


def nt(a, b):
    return lax.dot_general(a, b, (((1,), (1,)), ((), ())), preferred_element_type=F32)


def tn(a, b):
    return lax.dot_general(a, b, (((0,), (0,)), ((), ())), preferred_element_type=F32)


def params(collective=None):
    if collective is None:
        return pltpu.CompilerParams(vmem_limit_bytes=VMEM)
    return pltpu.CompilerParams(
        vmem_limit_bytes=VMEM, collective_id=collective, has_side_effects=True
    )


def cost(flops, moved):
    return pl.CostEstimate(flops=int(flops), bytes_accessed=int(moved), transcendentals=0)


def normed(h):
    centred = h - jnp.mean(h, axis=-1, keepdims=True)
    rstd = lax.rsqrt(jnp.mean(centred * centred, axis=-1, keepdims=True) + EPS)
    return centred * rstd, rstd


def norm_back(grad, n, rstd, gain):
    scaled = grad * gain
    centre = jnp.mean(scaled, axis=-1, keepdims=True)
    along = jnp.mean(scaled * n, axis=-1, keepdims=True)
    return rstd * (scaled - centre - n * along)


def total(a):
    return jnp.sum(a.astype(F32), axis=0, keepdims=True)


def place():
    me = lax.axis_index("dp")
    return me, me % 2, (me // 2) % 2, me // 4, lax.axis_index("sp")


def flipped(at, hops):
    me, c, x, z, sp = at
    for hop in hops:
        if hop == "core":
            me, c = me + 1 - 2 * c, 1 - c
        elif hop == "x":
            me, x = me + 2 - 4 * x, 1 - x
        elif hop == "z1":
            me, z = me + 4 - 8 * (z % 2), z + 1 - 2 * (z % 2)
        elif hop == "z2":
            me, z = me + 8 - 16 * (z // 2), z + 2 - 4 * (z // 2)
        else:
            sp = 1 - sp
    return me, c, x, z, sp


def partner(hops, at=None):
    there = flipped(at or place(), hops)
    return {"dp": there[0], "sp": there[4]}


def greet(groups, at=None):
    groups = sorted({tuple("y" if h[0] == "y" else h for h in hops) for hops in groups})
    barrier = pltpu.get_barrier_semaphore()
    for hops in groups:
        pl.semaphore_signal(barrier, inc=1, device_id=partner(hops, at), device_id_type=pl.DeviceIdType.MESH)
    pl.semaphore_wait(barrier, len(groups))


def remote(src, dst, send, recv, hops, at=None):
    return pltpu.make_async_remote_copy(
        src_ref=src, dst_ref=dst, send_sem=send, recv_sem=recv,
        device_id=partner(hops, at), device_id_type=pl.DeviceIdType.MESH,
    )


VIA_X = ("x", "z1", "z2", "y")
VIA_Y = ("yr", "x", "z1", "z2", "yg")
VIA_Z = ("z1", "yr", "x", "z2", "yg")
X_FIRST = ("x", "z1", ("yr", "z2"), "yg")
Z_FIRST = ("z1", "x", ("yr", "z2"), "yg")
AT_ONCE = (("x", "z1"), ("yr", "z2"), "yg")
BLOCK = ("z2", "z1", "x", "core")


class Part:
    def __init__(self, hop, shape, dims, cols=None):
        self.hops = hops = hop if isinstance(hop, tuple) else (hop,)
        self.groups = [(h,) for h in hops] + ([hops] if len(hops) > 1 else [])
        self.dims = dims
        self.cols = cols or (0, shape[-1])
        self.shape = shape = tuple(shape[:-1]) + (self.cols[1],)
        for h in hops:
            if h in dims:
                at = dims.index(h)
                shape, dims = shape[:at] + shape[at + 1 :], dims[:at] + dims[at + 1 :]
            elif h != "y":
                shape = shape[:-1] + (shape[-1] // 2 if h == "yr" else 2 * shape[-1],)
        self.after, self.left = shape, dims
        self.came = self.shape if hops == ("yg",) else shape

    def share(self, at):
        _, c, x, z, sp = at
        first, wide = self.cols
        index = [slice(None)] * (len(self.shape) - 1) + [pl.ds(first, wide)]
        for h in self.hops:
            if h in self.dims:
                index[self.dims.index(h)] = {"core": c, "x": x, "z1": z % 2, "z2": z // 2}[h]
            elif h == "yr":
                half = wide // 2
                index[-1] = pl.ds(pl.multiple_of(first + sp * half, 128), half)
        return tuple(index)

    def copies(self, src, held, made, came, send, recv, local, at):
        out = [
            remote(src.at[self.share(flipped(at, g))], came[i], send.at[i], recv.at[i], g, at)
            for i, g in enumerate(self.groups)
        ]
        if not held:
            out.append(pltpu.make_async_copy(src.at[self.share(at)], made, local))
        return out

    def add(self, src, held, made, came, at):
        if self.hops == ("yg",):
            wide, sp = self.shape[-1], at[4]
            lead = (slice(None),) * (len(self.shape) - 1)
            made[lead + (pl.ds(pl.multiple_of(sp * wide, 128), wide),)] = src[self.share(at)]
            made[lead + (pl.ds(pl.multiple_of((1 - sp) * wide, 128), wide),)] = came[0][...]
        elif len(came) > 1:
            mine = src[self.share(at)] if held else made[...]
            made[...] = sum((c[...].astype(F32) for c in came), mine.astype(F32)).astype(BF16)
        elif held:
            made[...] = src[self.share(at)] + came[0][...]
        else:
            made[...] += came[0][...]


class Flow:
    def __init__(self, array, shape, hops, dims=BLOCK, cols=None):
        self.array, self.shape, self.dims, self.cols = array, tuple(shape), dims, cols
        self.hops = list(hops)

    def step(self):
        part = Part(self.hops.pop(0), self.shape, self.dims, self.cols)
        self.shape, self.dims, self.cols = part.after, part.left, None
        return part


class Window:
    def __init__(self, start, stop, joint):
        self.start, self.stop, self.joint = start, stop, joint
        self.parts, self.sources, self.keeps = [], [], []


class Joint:
    def __init__(self):
        self.window = None


def plan(schedule):
    windows, arrays, latest = [], [], {}
    for n, (flows, start, stop, *joint) in enumerate(schedule):
        window = Window(start, stop, bool(joint))
        if joint:
            joint[0].window = n
        for i, flow in enumerate(flows):
            if flow in latest:
                source = ("part",) + latest[flow]
                before = windows[latest[flow][0]]
                before.keeps[latest[flow][1]] = False
            elif isinstance(flow.array, Joint):
                source = ("joint", flow.array.window)
            elif isinstance(flow.array, tuple):
                source = flow.array
            else:
                known = [k for k, a in enumerate(arrays) if a is flow.array]
                if not known:
                    arrays.append(flow.array)
                source = ("in", known[0] if known else len(arrays) - 1)
            window.parts.append(flow.step())
            window.sources.append(source)
            window.keeps.append(not joint)
            if not joint:
                latest[flow] = (n, i)
        windows.append(window)
    return windows, arrays, latest


def carrying(body, own, windows, arrays, grid, also, finale):
    ins, outs, held = own

    def kernel(*refs):
        refs = list(refs)

        def take(n):
            got = refs[:n]
            del refs[:n]
            return got

        my_in, arr = take(ins), take(arrays)
        my_out = take(outs)
        given = [[take(1)[0] if k else None for k in w.keeps] for w in windows]
        my_held = take(held)
        made, came, joints = [], [], []
        for w, g in zip(windows, given):
            if w.joint:
                joint, col, views = take(1)[0], 0, []
                for q in w.parts:
                    views.append(joint.at[(slice(None),) * (len(q.after) - 1) + (pl.ds(col, q.after[-1]),)])
                    col += q.after[-1]
                joints.append(joint)
                made.append(views)
            else:
                joints.append(None)
                made.append([ref if ref is not None else take(1)[0] for ref in g])
            came.append([take(len(q.groups)) for q in w.parts])
        mine = my_in + my_out + my_held
        step = pl.program_id(0)
        groups = [g for w in windows for q in w.parts for g in q.groups] + list(also)
        if groups:
            here = place()
            pl.when(step == 0)(lambda: greet(groups, here))
        if windows:
            send, recv, local = refs
        copies, sources, base = [], [], 0
        for w, m, c in zip(windows, made, came):
            now, froms = [], []
            for i, q in enumerate(w.parts):
                kind = w.sources[i]
                if kind[0] == "in":
                    src = arr[kind[1]]
                elif kind[0] == "ref":
                    src = mine[kind[1]]
                elif kind[0] == "joint":
                    src = joints[kind[1]]
                else:
                    src = made[kind[1]][kind[2]]
                held_here = kind[0] != "in"
                froms.append((src, held_here))
                now += q.copies(
                    src, held_here, m[i], c[i], send.at[base], recv.at[base], local.at[base], here
                )
                base += 1
            copies.append(now)
            sources.append(froms)

        def phase(number):
            for n, w in enumerate(windows):
                if w.stop == number:
                    for copy in copies[n]:
                        copy.wait()
                    for q, (src, held_here), m, c in zip(w.parts, sources[n], made[n], came[n]):
                        q.add(src, held_here, m, c, here)
            for n, w in enumerate(windows):
                if w.start == number:
                    for copy in copies[n]:
                        copy.start()

        used = sorted({w.start for w in windows} | {w.stop for w in windows})
        for number in used:
            if number < grid:
                pl.when(step == number)(functools.partial(phase, number))
        body(*mine)
        for number in used:
            if number >= grid:
                pl.when(step == grid - 1)(functools.partial(phase, number))
        if finale:
            pl.when(step == grid - 1)(lambda: finale(*mine))

    return kernel


def run(
    body, name, grid, ins, in_specs, outs, out_specs, held=(), schedule=(), collective=None,
    flops=0, moved=0, also=(), finale=None,
):
    in_specs, outs, out_specs, held = list(in_specs), list(outs), list(out_specs), list(held)
    windows, arrays, latest = plan(schedule)
    own = len(outs)
    kernel = carrying(body, (len(ins), own, len(held)), windows, len(arrays), grid, also, finale)
    in_specs += [pl.BlockSpec(memory_space=pl.ANY)] * len(arrays)
    order, count = [], 0
    for n, w in enumerate(windows):
        if w.joint:
            shape = w.parts[0].after[:-1] + (sum(q.after[-1] for q in w.parts),)
            held.append(pltpu.VMEM(shape, BF16))
        for i, (q, k) in enumerate(zip(w.parts, w.keeps)):
            if w.joint:
                continue
            if k:
                outs.append(jax.ShapeDtypeStruct(q.after, BF16))
                out_specs.append(whole(q.after))
                order.append((n, i))
            else:
                held.append(pltpu.VMEM(q.after, BF16))
        held += [pltpu.VMEM(q.came, BF16) for q in w.parts for _ in q.groups]
        count += len(w.parts)
    if windows:
        held += [pltpu.SemaphoreType.DMA((count, 3))] * 2 + [pltpu.SemaphoreType.DMA((count,))]
    results = pl.pallas_call(
        kernel,
        grid=(grid,),
        in_specs=in_specs,
        out_specs=out_specs,
        out_shape=outs,
        scratch_shapes=held,
        compiler_params=params(collective if windows or also else None),
        cost_estimate=cost(flops, moved),
        name=name,
    )(*ins, *arrays)
    for flow, where in latest.items():
        flow.array = results[own + order.index(where)]
    return results[:own]


def code_of(docs_ref):
    row = lax.broadcasted_iota(jnp.int32, (128, docs_ref.shape[1]), 0)
    return jnp.transpose(jnp.where(docs_ref[...] == row, 1.0, 0.0)).astype(BF16)


def project_own_kernel(x_ref, m_ref, td_ref, md_ref, wx_ref, wm_ref, b_ref, qkv_ref, mkv_ref, to_ref, mo_ref):
    step = pl.program_id(0)

    @pl.when(step == 0)
    def _():
        to_ref[...] = code_of(td_ref)
        mo_ref[...] = code_of(md_ref)

    @pl.when(step < 3)
    def _():
        bias = jnp.where(step == 0, b_ref[0:1], 0.0) + jnp.where(step == 2, b_ref[1:2], 0.0)
        qkv_ref[...] = (nn(x_ref[...], wx_ref[...]) + bias).astype(BF16)

    @pl.when(step >= 3)
    def _():
        bias = jnp.where(step == 4, b_ref[2:3], 0.0)
        mkv_ref[...] = (nn(m_ref[...], wm_ref[...]) + bias).astype(BF16)


def project_own(x, mem, td, md, wx, wm, biases):
    rows, width = x.shape
    code = jax.ShapeDtypeStruct((rows, 128), BF16)
    return pl.pallas_call(
        project_own_kernel,
        grid=(5,),
        in_specs=[
            whole((rows, width)), whole((rows, width)), whole((1, rows)), whole((1, rows)),
            pl.BlockSpec((width, width), lambda s: (0, jnp.minimum(s, 2))),
            pl.BlockSpec((width, width), lambda s: (0, jnp.maximum(s - 3, 0))),
            whole(biases.shape),
        ],
        out_specs=[
            pl.BlockSpec((rows, width), lambda s: (0, jnp.minimum(s, 2))),
            pl.BlockSpec((rows, width), lambda s: (0, jnp.maximum(s - 3, 0))),
            whole((rows, 128)), whole((rows, 128)),
        ],
        out_shape=[
            jax.ShapeDtypeStruct((rows, 3 * width), BF16), jax.ShapeDtypeStruct((rows, 2 * width), BF16), code, code,
        ],
        compiler_params=params(),
        cost_estimate=cost(10 * rows * width * width, 20 * width * width),
        name="project_own",
    )(x, mem, td, md, wx, wm, biases)


def project_other_kernel(x_ref, m_ref, td_ref, md_ref, wx_ref, b_ref, after_ref, kvo_ref, mem_ref, tt_ref, mt_ref):
    step = pl.program_id(0)

    @pl.when(step == 0)
    def _():
        mem_ref[...] = m_ref[...]
        tt_ref[...] = code_of(td_ref)
        mt_ref[...] = code_of(md_ref)

    @pl.when(lax.axis_index("sp") == 1)
    def _():
        bias = jnp.where(step == 1, b_ref[1:2], 0.0)
        kvo_ref[...] = (nn(x_ref[...], wx_ref[...]) + bias).astype(BF16)

    @pl.when(lax.axis_index("sp") == 0)
    def _():
        kvo_ref[...] = jnp.zeros(kvo_ref.shape, BF16)


def project_other(x, mem, td, md, wx, biases, after):
    rows, width = x.shape
    code = jax.ShapeDtypeStruct((rows, 128), BF16)
    return pl.pallas_call(
        project_other_kernel,
        grid=(2,),
        in_specs=[
            whole((rows, width)), whole((rows, width)), whole((1, rows)), whole((1, rows)),
            pl.BlockSpec((width, width), lambda s: (0, s + 1)),
            whole(biases.shape),
            pl.BlockSpec(memory_space=pl.ANY),
        ],
        out_specs=[
            pl.BlockSpec((rows, width), lambda s: (0, s)),
            whole((rows, width)), whole((rows, 128)), whole((rows, 128)),
        ],
        out_shape=[
            jax.ShapeDtypeStruct((rows, 2 * width), BF16), jax.ShapeDtypeStruct((rows, width), BF16), code, code,
        ],
        compiler_params=params(),
        cost_estimate=cost(4 * rows * width * width, 10 * width * width),
        name="project_other",
    )(x, mem, td, md, wx, biases, after)


def project_memory_kernel(x_ref, w_ref, b_ref, o_ref):
    bias = jnp.where(pl.program_id(0) == 1, b_ref[2:3], 0.0)
    o_ref[...] = (nn(x_ref[...], w_ref[...]) + bias).astype(BF16)


def project_memory(x, w, biases):
    rows, width = x.shape
    return pl.pallas_call(
        project_memory_kernel,
        grid=(2,),
        in_specs=[
            whole((rows, width)),
            pl.BlockSpec((width, width), lambda j: (0, j)),
            whole(biases.shape),
        ],
        out_specs=pl.BlockSpec((rows, width), lambda j: (0, j)),
        out_shape=jax.ShapeDtypeStruct((rows, 2 * width), BF16),
        compiler_params=params(),
        cost_estimate=cost(4 * rows * width * width, 4 * width * (width + rows)),
        name="project_memory",
    )(x, w, biases)


def head_masks(dtype):
    lane = lax.broadcasted_iota(jnp.int32, (1, PAIR), 1)
    low = jnp.where(lane < HD, 1.0, 0.0)
    return low.astype(dtype), (1.0 - low).astype(dtype)


def query_code(code):
    lane = lax.broadcasted_iota(jnp.int32, code.shape, 1)
    return jnp.where(lane < 4, (code.astype(F32) - 1.0) * FAR, 0.0).astype(BF16)


def softmax_pieces(scores, values):
    peak = functools.reduce(jnp.maximum, [jnp.max(s, axis=-1, keepdims=True) for s in scores])
    expd = [jnp.exp(s - peak) for s in scores]
    norm = sum(jnp.sum(e, axis=-1, keepdims=True) for e in expd)
    out = sum(nn(e.astype(BF16), v) for e, v in zip(expd, values))
    return out / norm, peak + jnp.log(norm)


def self_pieces(block, size, both, own, other):
    pieces = []
    if both:
        pieces.append((other, False))
    if block:
        pieces.append((own[: block * size], False))
    pieces.append((own[block * size : (block + 1) * size], True))
    return pieces


def store_lse(lse_ref, block, size, low, high):
    lane = lax.broadcasted_iota(jnp.int32, (size, PAIR), 1)
    both = jnp.where(lane == 0, low, high)
    lse_ref[:, block * size : (block + 1) * size] = jnp.transpose(both)[:8]


def self_forward_kernel(size, q_ref, k_ref, v_ref, ko_ref, vo_ref, own_ref, oth_ref, o_ref, lse_ref):
    second = lax.axis_index("sp") == 1
    rows = q_ref.shape[0]
    masks = head_masks(BF16)
    outs = head_masks(F32)

    def run(both):
        qcode = query_code(own_ref[...])
        own = jnp.concatenate([k_ref[...], own_ref[...]], axis=1)
        oth = jnp.concatenate([ko_ref[...], oth_ref[...]], axis=1) if both else None
        vown = v_ref[...]
        voth = vo_ref[...] if both else None
        for block in range(rows // size):
            at = slice(block * size, (block + 1) * size)
            lses, result = [], 0.0
            for mask, keep in zip(masks, outs):
                q = jnp.concatenate([q_ref[at] * (mask * BF16(HD**-0.5)), qcode[at]], axis=1)
                scores = []
                for keys, diagonal in self_pieces(block, size, both, own, oth):
                    s = nt(q, keys)
                    if diagonal:
                        row = lax.broadcasted_iota(jnp.int32, s.shape, 0)
                        col = lax.broadcasted_iota(jnp.int32, s.shape, 1)
                        s = jnp.where(row >= col, s, -FAR)
                    scores.append(s)
                values = [v for v, _ in self_pieces(block, size, both, vown, voth)]
                out, lse = softmax_pieces(scores, values)
                result = result + out * keep
                lses.append(lse)
            o_ref[at] = result.astype(BF16)
            store_lse(lse_ref, block, size, *lses)

    pl.when(second)(lambda: run(True))
    pl.when(jnp.logical_not(second))(lambda: run(False))


def pair_spec(rows, offset):
    return pl.BlockSpec((rows, PAIR), lambda p: (0, p + offset))


def whole(shape):
    return pl.BlockSpec(shape, lambda *_: (0,) * len(shape))


def self_forward(qkv, kvo, own, oth):
    rows = qkv.shape[0]
    width = qkv.shape[1] // 3
    pairs = width // PAIR
    return pl.pallas_call(
        functools.partial(self_forward_kernel, 256),
        grid=(pairs,),
        in_specs=[
            pair_spec(rows, 0),
            pair_spec(rows, pairs),
            pair_spec(rows, 2 * pairs),
            pair_spec(rows, 0),
            pair_spec(rows, pairs),
            whole((rows, 128)),
            whole((rows, 128)),
        ],
        out_specs=[pair_spec(rows, 0), pl.BlockSpec((8, rows), lambda p: (p, 0))],
        out_shape=[
            jax.ShapeDtypeStruct((rows, width), BF16),
            jax.ShapeDtypeStruct((8 * pairs, rows), F32),
        ],
        compiler_params=params(),
        cost_estimate=cost(16 * rows * rows * width, 16 * rows * width),
        name="self_forward",
    )(qkv, qkv, qkv, kvo, kvo, own, oth)


def cross_forward_kernel(size, q_ref, k_ref, v_ref, ko_ref, vo_ref, t_ref, own_ref, oth_ref, o_ref, lse_ref):
    rows = q_ref.shape[0]
    masks = head_masks(BF16)
    outs = head_masks(F32)
    qcode = query_code(t_ref[...])
    keys = [
        jnp.concatenate([k_ref[...], own_ref[...]], axis=1),
        jnp.concatenate([ko_ref[...], oth_ref[...]], axis=1),
    ]
    values = [v_ref[...], vo_ref[...]]
    for block in range(rows // size):
        at = slice(block * size, (block + 1) * size)
        lses, result = [], 0.0
        for mask, keep in zip(masks, outs):
            q = jnp.concatenate([q_ref[at] * (mask * BF16(HD**-0.5)), qcode[at]], axis=1)
            out, lse = softmax_pieces([nt(q, k) for k in keys], values)
            result = result + out * keep
            lses.append(lse)
        o_ref[at] = result.astype(BF16)
        store_lse(lse_ref, block, size, *lses)


def cross_forward(cq, kv, kvo, t, own, oth):
    rows, width = cq.shape
    pairs = width // PAIR
    return pl.pallas_call(
        functools.partial(cross_forward_kernel, 256),
        grid=(pairs,),
        in_specs=[
            pair_spec(rows, 0),
            pair_spec(rows, 0),
            pair_spec(rows, pairs),
            pair_spec(rows, 0),
            pair_spec(rows, pairs),
            whole((rows, 128)),
            whole((rows, 128)),
            whole((rows, 128)),
        ],
        out_specs=[pair_spec(rows, 0), pl.BlockSpec((8, rows), lambda p: (p, 0))],
        out_shape=[
            jax.ShapeDtypeStruct((rows, width), BF16),
            jax.ShapeDtypeStruct((8 * pairs, rows), F32),
        ],
        compiler_params=params(),
        cost_estimate=cost(24 * rows * rows * width, 16 * rows * width),
        name="cross_forward",
    )(cq, kv, kv, kvo, kvo, t, own, oth)


def delta_rows(g, o):
    prod = g.astype(F32) * o.astype(F32)
    upper = prod.astype(BF16)
    lower = (prod - upper.astype(F32)).astype(BF16)
    row = lax.broadcasted_iota(jnp.int32, (8, PAIR), 0)
    lane = lax.broadcasted_iota(jnp.int32, (8, PAIR), 1)
    pick = jnp.where(row == lane // HD, 1.0, 0.0).astype(BF16)
    return nt(pick, upper) + nt(pick, lower)


def back_piece(keys, values, q, g, lse, delta, causal):
    s = nt(keys, q)
    if causal:
        row = lax.broadcasted_iota(jnp.int32, s.shape, 0)
        col = lax.broadcasted_iota(jnp.int32, s.shape, 1)
        s = jnp.where(row <= col, s, -FAR)
    p = jnp.exp(s - lse)
    ds = p * (nt(values, g) - delta)
    return p.astype(BF16), ds.astype(BF16)


def cross_backward_kernel(
    size, q_ref, k_ref, v_ref, ko_ref, vo_ref, g_ref, o_ref, lse_ref, t_ref, own_ref, oth_ref,
    m_ref, mo_ref, wk_ref, wv_ref,
    dq_ref, dm_ref, dmo_ref, gk_ref, gv_ref, gb_ref, dm_acc, dmo_acc, mt_ref, mot_ref,
):
    step = pl.program_id(0)

    @pl.when(step == 0)
    def _():
        mt_ref[...] = jnp.transpose(m_ref[...])
        mot_ref[...] = jnp.transpose(mo_ref[...])

    rows = q_ref.shape[0]
    masks = head_masks(BF16)
    scale = BF16(HD**-0.5)
    qcode = query_code(t_ref[...])
    delta = delta_rows(g_ref[...], o_ref[...])
    lse = lse_ref[...]
    halves = [(k_ref, v_ref, own_ref, mt_ref, dm_acc), (ko_ref, vo_ref, oth_ref, mot_ref, dmo_acc)]
    dq = [0.0] * (rows // size)
    gk = gv = gb = 0.0
    for kr, vr, code, mem, acc in halves:
        keys = jnp.concatenate([kr[...], code[...]], axis=1)
        values = vr[...]
        dk = dv = 0.0
        for block in range(rows // size):
            at = slice(block * size, (block + 1) * size)
            for head, mask in enumerate(masks):
                qm = q_ref[at] * (mask * scale)
                gm = g_ref[at] * mask
                q = jnp.concatenate([qm, qcode[at]], axis=1)
                p, ds = back_piece(
                    keys, values, q, gm, lse[head : head + 1, at], delta[head : head + 1, at], False
                )
                dk = dk + nn(ds, qm)
                dv = dv + nn(p, gm)
                dq[block] = dq[block] + tn(ds, kr[...] * (mask * scale))
        both = jnp.concatenate([dk.astype(BF16), dv.astype(BF16)], axis=1)
        grad = nn(mem[...], both)
        gk, gv = gk + grad[:, :PAIR], gv + grad[:, PAIR:]
        gb = gb + total(both[:, PAIR:])
        dm = nt(both, jnp.concatenate([wk_ref[...], wv_ref[...]], axis=1))

        @pl.when(step == 0)
        def _():
            acc[...] = dm

        @pl.when(step > 0)
        def _():
            acc[...] += dm
    for block in range(rows // size):
        dq_ref[block * size : (block + 1) * size] = dq[block].astype(BF16)
    gk_ref[...] = gk.astype(BF16)
    gv_ref[...] = gv.astype(BF16)
    gb_ref[...] = gb

    @pl.when(step == pl.num_programs(0) - 1)
    def _():
        dm_ref[...] = dm_acc[...]
        dmo_ref[...] = dmo_acc[...].astype(BF16)


def cross_backward(cq, kv, kvo, g, o, lse, t, own, oth, m, mo, w, schedule):
    rows, width = cq.shape
    pairs = width // PAIR
    flat = jax.ShapeDtypeStruct((rows, width), BF16)
    square = jax.ShapeDtypeStruct((width, width), BF16)
    return run(
        functools.partial(cross_backward_kernel, 256), "cross_backward", pairs,
        (cq, kv, kv, kvo, kvo, g, o, lse, t, own, oth, m, mo, w, w),
        [
            pair_spec(rows, 0),
            pair_spec(rows, 0),
            pair_spec(rows, pairs),
            pair_spec(rows, 0),
            pair_spec(rows, pairs),
            pair_spec(rows, 0),
            pair_spec(rows, 0),
            pl.BlockSpec((8, rows), lambda p: (p, 0)),
            whole((rows, 128)),
            whole((rows, 128)),
            whole((rows, 128)),
            whole((rows, width)),
            whole((rows, width)),
            pair_spec(width, 0),
            pair_spec(width, pairs),
        ],
        [flat, jax.ShapeDtypeStruct((rows, width), F32), flat, square, square, jax.ShapeDtypeStruct((1, width), F32)],
        [pair_spec(rows, 0)] + [whole((rows, width))] * 2 + [pair_spec(width, 0)] * 2 + [pair_spec(1, 0)],
        [pltpu.VMEM((rows, width), F32)] * 2 + [pltpu.VMEM((width, rows), BF16)] * 2,
        schedule, 3,
        64 * rows * rows * width + 16 * rows * width * width, 24 * rows * width,
    )


def front_pairs(pairs):
    return 2 * pairs // 3


def backward_pieces(size, q_ref, g_ref, o_ref, lse_ref, own_ref):
    masks = head_masks(BF16)
    scale = BF16(HD**-0.5)
    qcode = query_code(own_ref[...])
    delta = delta_rows(g_ref[...], o_ref[...])
    for block in range(q_ref.shape[0] // size):
        at = slice(block * size, (block + 1) * size)
        for head, mask in enumerate(masks):
            qm = q_ref[at] * (mask * scale)
            gm = g_ref[at] * mask
            q = jnp.concatenate([qm, qcode[at]], axis=1)
            yield block, mask * scale, qm, gm, q, lse_ref[head : head + 1, at], delta[head : head + 1, at]


def other_backward_kernel(
    size, q_ref, ko_ref, vo_ref, g_ref, o_ref, lse_ref, own_ref, oth_ref, wk_ref, wv_ref,
    dq_ref, dkv_ref, dxo_ref, dxo_acc,
):
    step = pl.program_id(0)

    @pl.when(lax.axis_index("sp") == 1)
    def _():
        keys = jnp.concatenate([ko_ref[...], oth_ref[...]], axis=1)
        values = vo_ref[...]
        dk = dv = 0.0
        dq = [0.0] * (q_ref.shape[0] // size)
        for block, mask, qm, gm, q, lse, delta in backward_pieces(size, q_ref, g_ref, o_ref, lse_ref, own_ref):
            p, ds = back_piece(keys, values, q, gm, lse, delta, False)
            dk = dk + nn(ds, qm)
            dv = dv + nn(p, gm)
            dq[block] = dq[block] + tn(ds, ko_ref[...] * mask)
        for block, part in enumerate(dq):
            dq_ref[block * size : (block + 1) * size] = part
        both = jnp.concatenate([dk.astype(BF16), dv.astype(BF16)], axis=1)
        dkv_ref[...] = both
        dxo = nt(both, jnp.concatenate([wk_ref[...], wv_ref[...]], axis=1))

        @pl.when(step == 0)
        def _():
            dxo_acc[...] = dxo

        @pl.when(step > 0)
        def _():
            dxo_acc[...] += dxo

        @pl.when(step == pl.num_programs(0) - 1)
        def _():
            dxo_ref[...] = dxo_acc[...].astype(BF16)

    @pl.when(lax.axis_index("sp") == 0)
    def _():
        dq_ref[...] = jnp.zeros(dq_ref.shape, F32)
        dkv_ref[...] = jnp.zeros(dkv_ref.shape, BF16)
        dxo_ref[...] = jnp.zeros(dxo_ref.shape, BF16)


def other_backward(qkv, kvo, g, o, lse, own, oth, w, schedule):
    rows = qkv.shape[0]
    width = qkv.shape[1] // 3
    pairs = width // PAIR
    return run(
        functools.partial(other_backward_kernel, 256), "other_backward", pairs,
        (qkv, kvo, kvo, g, o, lse, own, oth, w, w),
        [
            pair_spec(rows, 0), pair_spec(rows, 0), pair_spec(rows, pairs), pair_spec(rows, 0), pair_spec(rows, 0),
            pl.BlockSpec((8, rows), lambda p: (p, 0)), whole((rows, 128)), whole((rows, 128)),
            pair_spec(width, pairs), pair_spec(width, 2 * pairs),
        ],
        [
            jax.ShapeDtypeStruct((rows, width), F32),
            jax.ShapeDtypeStruct((rows, 2 * width), BF16),
            jax.ShapeDtypeStruct((rows, width), BF16),
        ],
        [pair_spec(rows, 0), pl.BlockSpec((rows, 2 * PAIR), lambda p: (0, p)), whole((rows, width))],
        [pltpu.VMEM((rows, width), F32)],
        schedule, 5, 32 * rows * rows * width, 24 * rows * width,
    )


def front_pairs(pairs):
    return 2 * pairs // 3


def self_backward_kernel(
    size, q_ref, k_ref, v_ref, g_ref, o_ref, lse_ref, own_ref, dqo_ref, dkvo_ref,
    x_ref, xo_ref, wq_ref, wk_ref, wv_ref, dh1_ref, sa_ref, sb_ref, sc_ref, sd_ref,
    dx_ref, grad_ref, xt_ref, xot_ref, turn_ref,
):
    step = pl.program_id(0)
    second = lax.axis_index("sp") == 1
    width = x_ref.shape[1]
    pairs = width // PAIR
    count = q_ref.shape[0] // size
    cut = front_pairs(pairs)
    lead = (slice(None),) * (len(grad_ref.shape) - 1)

    @pl.when(step == 0)
    def _():
        xt_ref[...] = jnp.transpose(x_ref[...])
        turn_ref[...] = jnp.zeros(turn_ref.shape, F32)
        turn_ref[0:8] = sa_ref[...]
        turn_ref[8:16] = sb_ref[...]
        turn_ref[16:17] = sc_ref[...]
        turn_ref[17:21] = sd_ref[...]

    @pl.when(jnp.logical_and(step == 0, second))
    def _():
        xot_ref[...] = jnp.transpose(xo_ref[...])

    dq = [dqo_ref[block * size : (block + 1) * size] for block in range(count)]
    dk, dv = [0.0] * count, [0.0] * count
    for block, mask, qm, gm, q, lse, delta in backward_pieces(size, q_ref, g_ref, o_ref, lse_ref, own_ref):
        for part in range(block + 1):
            of = slice(part * size, (part + 1) * size)
            keys = jnp.concatenate([k_ref[of], own_ref[of]], axis=1)
            p, ds = back_piece(keys, v_ref[of], q, gm, lse, delta, part == block)
            dk[part] = dk[part] + nn(ds, qm)
            dv[part] = dv[part] + nn(p, gm)
            dq[block] = dq[block] + tn(ds, k_ref[of] * mask)
    dq, dk, dv = (jnp.concatenate(a, axis=0).astype(BF16) for a in (dq, dk, dv))
    dqk = jnp.concatenate([dq, dk], axis=1)
    grad_qk = nn(xt_ref[...], dqk)
    grad_v = nn(xt_ref[...], dv)

    def put(n, grad):
        col = jnp.where(step < cut, n * cut + step, 3 * cut + n * (pairs - cut) + step - cut + 2 * (n > 0))
        to = pl.ds(pl.multiple_of(col * PAIR, PAIR), PAIR)
        grad_ref[lead + (to,)] = grad.astype(BF16).reshape(grad_ref.shape[:-1] + (PAIR,))

    cols = pl.ds(pl.multiple_of(step * PAIR, PAIR), PAIR)
    put(0, grad_qk[:, :PAIR])
    turn_ref[21:22, cols] = total(dq)

    @pl.when(second)
    def _():
        dkvo = dkvo_ref[...]
        grad_o = nn(xot_ref[...], dkvo)
        put(1, grad_qk[:, PAIR:] + grad_o[:, :PAIR])
        put(2, grad_v + grad_o[:, PAIR:])
        turn_ref[22:23, cols] = total(dv) + total(dkvo[:, PAIR:])

    @pl.when(jnp.logical_not(second))
    def _():
        put(1, grad_qk[:, PAIR:])
        put(2, grad_v)
        turn_ref[22:23, cols] = total(dv)

    dx = nt(dqk, jnp.concatenate([wq_ref[...], wk_ref[...]], axis=1)) + nt(dv, wv_ref[...])

    @pl.when(step == 0)
    def _():
        dx_ref[...] = dh1_ref[...] + dx

    @pl.when(step > 0)
    def _():
        dx_ref[...] += dx

    @pl.when(step == pairs - 1)
    def _():
        col = (2 * cut + pairs) * PAIR
        shape = grad_ref.shape[:-1] + (2 * PAIR,)
        grad_ref[lead + (slice(col, col + 2 * PAIR),)] = jnp.transpose(turn_ref[...]).astype(BF16).reshape(shape)


GRADS = 20


def self_backward(block, qkv, g, o, lse, own, dqo, dkvo, x, xo, w, dh1, small, schedule):
    rows, width = x.shape
    pairs = width // PAIR
    made = block + (3 * width + 2 * PAIR,)
    outs = [jax.ShapeDtypeStruct((rows, width), F32)]
    specs = [whole((rows, width))]
    held = []
    if schedule:
        held += [pltpu.VMEM(made, BF16)]
    else:
        outs += [jax.ShapeDtypeStruct(made, BF16)]
        specs += [whole(made)]
    held += [
        pltpu.VMEM((width, rows), BF16),
        pltpu.VMEM((width, rows), BF16),
        pltpu.VMEM((2 * PAIR, width), F32),
    ]
    return run(
        functools.partial(self_backward_kernel, 256), "self_backward", pairs,
        (qkv, qkv, qkv, g, o, lse, own, dqo, dkvo, x, xo, w, w, w, dh1) + tuple(small),
        [
            pair_spec(rows, 0), pair_spec(rows, pairs), pair_spec(rows, 2 * pairs), pair_spec(rows, 0), pair_spec(rows, 0),
            pl.BlockSpec((8, rows), lambda p: (p, 0)), whole((rows, 128)),
            pair_spec(rows, 0), pl.BlockSpec((rows, 2 * PAIR), lambda p: (0, p)),
            whole((rows, width)), whole((rows, width)),
            pair_spec(width, 0), pair_spec(width, pairs), pair_spec(width, 2 * pairs), whole((rows, width)),
        ] + [whole(a.shape) for a in small],
        outs, specs, held, schedule, 6,
        24 * rows * rows * width + 16 * rows * width * width, 12 * width * width + 40 * rows * width,
    )


def first_norm_kernel(x_ref, ctx_ref, wo_ref, wq_ref, b_ref, h_ref, cq_ref):
    h = x_ref[...].astype(F32) + nn(ctx_ref[...], wo_ref[...]) + b_ref[3:4]
    h_ref[...] = h
    n, _ = normed(h)
    a = (n * b_ref[4:5] + b_ref[5:6]).astype(BF16)
    cq_ref[...] = (nn(a, wq_ref[...]) + b_ref[6:7]).astype(BF16)


def first_norm(x, ctx, wo, wq, biases):
    rows, width = x.shape
    return pl.pallas_call(
        first_norm_kernel,
        out_shape=[
            jax.ShapeDtypeStruct((rows, width), F32),
            jax.ShapeDtypeStruct((rows, width), BF16),
        ],
        compiler_params=params(),
        cost_estimate=cost(4 * rows * width * width, 4 * width * width + 10 * rows * width),
        name="first_norm",
    )(x, ctx, wo, wq, biases)


def feed_kernel(
    count, comm, h1_ref, cc_ref, ct_ref, wco_ref, b_ref, wi_ref, wo_ref,
    out_ref, dh2_ref, dcc_ref, gco_ref, *refs,
):
    if comm:
        gwi_ref, refs = refs[0], refs[1:]
    else:
        gwi_ref, gwo_ref, refs = refs[0], refs[1], refs[2:]
    small_ref, gib_ref, hid_ref, slope_ref, n2_ref, r2_ref, a2b_ref, acc_ref, df_ref, *refs = refs
    step = pl.program_id(0)
    width = acc_ref.shape[1]

    if comm:
        mi_ref, mo_ref, ci_ref, co_ref, send_ref, recv_ref = refs
        wide = ci_ref.shape[-1]
        here = place()
        c = here[1]

        def chunk_copies(j):
            at = pl.ds(pl.multiple_of(j * width, width), width)
            return [
                remote(mi_ref.at[:, :, at], ci_ref.at[:, :, at], send_ref.at[0, j], recv_ref.at[0, j], ("core",), here),
                remote(mo_ref.at[j], co_ref.at[j], send_ref.at[1, j], recv_ref.at[1, j], ("core",), here),
            ]

    @pl.when(step == 0)
    def _():
        if comm:
            greet([("core",)])
        n1, _ = normed(h1_ref[...])
        a1 = n1 * b_ref[4:5] + b_ref[5:6]
        h2 = a1 + nn(cc_ref[...], wco_ref[...]) + b_ref[7:8]
        n2, r2 = normed(h2)
        n2_ref[...] = n2
        r2_ref[...] = jnp.broadcast_to(r2, r2_ref.shape)
        a2 = n2 * b_ref[8:9] + b_ref[9:10]
        a2b_ref[...] = a2.astype(BF16)
        acc_ref[...] = a2 + b_ref[10:11]

    @pl.when(step < count)
    def _():
        u = nn(a2b_ref[...], wi_ref[...]) + b_ref[pl.ds(13 + step, 1)]
        cumul = 0.5 * (1.0 + lax.erf(u * 0.7071067811865476))
        density = jnp.exp(-0.5 * u * u) * 0.3989422804014327
        hid = (u * cumul).astype(BF16)
        hid_ref[step] = hid
        slope_ref[step] = cumul + u * density
        acc_ref[...] += nn(hid, wo_ref[...])

    @pl.when(step == count - 1)
    def _():
        n3, r3 = normed(acc_ref[...])
        gain = b_ref[11:12]
        out_ref[...] = (n3 * gain + b_ref[12:13]).astype(BF16)
        e = ct_ref[...].astype(F32)
        d3 = norm_back(e, n3, r3, gain)
        df = d3.astype(BF16)
        df_ref[...] = df
        acc_ref[...] = d3
        small_ref[0:1] = total(e * n3)
        small_ref[1:2] = total(e)
        small_ref[2:3] = total(df)

    @pl.when(jnp.logical_and(step >= count, step < 2 * count))
    def _():
        j = step - count
        df = df_ref[...]
        du = (nt(df, wo_ref[...]) * slope_ref[j]).astype(BF16)
        gib_ref[...] = total(du)
        acc_ref[...] += nt(du, wi_ref[...])
        go = tn(hid_ref[j], df).astype(BF16)
        gi = tn(a2b_ref[...], du).astype(BF16)
        if comm:
            at = pl.ds(pl.multiple_of(j * width, width), width)
            eight, narrow = gwi_ref.shape[:2]
            gi = gi.reshape(eight, 2, narrow, width)
            go = go.reshape(2, 2, 4, narrow, width)
            gwi_ref[:, :, at] = jnp.where(c == 0, gi[:, 0], gi[:, 1])
            mi_ref[:, :, at] = jnp.where(c == 0, gi[:, 1], gi[:, 0])
            mo_ref[j] = jnp.where(c == 0, go[:, 1], go[:, 0])
            for i in range(4):
                gwi_ref[pl.ds(2 * j, 2), :, pl.ds(wide + i * width, width)] = jnp.where(c == 0, go[:, 0, i], go[:, 1, i])
            for copy in chunk_copies(j):
                copy.start()
        else:
            gwo_ref[...] = go
            gwi_ref[...] = gi

    @pl.when(step == 2 * count)
    def _():
        d2 = acc_ref[...]
        n2 = n2_ref[...]
        dh2 = norm_back(d2, n2, r2_ref[:, :1], b_ref[8:9])
        dh2_ref[...] = dh2
        dco = dh2.astype(BF16)
        dcc_ref[...] = nt(dco, wco_ref[...]).astype(BF16)
        gco_ref[...] = tn(cc_ref[...], dco).astype(BF16)
        small_ref[3:4] = total(d2 * n2)
        small_ref[4:5] = total(d2)
        small_ref[5:6] = total(dco)
        small_ref[6:8] = jnp.zeros((2, d2.shape[1]), F32)

    if comm:

        @pl.when(step > count)
        def _():
            j = step - count - 1
            at = pl.ds(pl.multiple_of(j * width, width), width)
            for copy in chunk_copies(j):
                copy.wait()
            gwi_ref[:, :, at] += ci_ref[:, :, at]
            for i in range(4):
                gwi_ref[pl.ds(2 * j, 2), :, pl.ds(wide + i * width, width)] += co_ref[j, :, i]


def feed(size, comm, h1, cc, ct, wco, biases, wi, wo):
    rows, width = h1.shape
    wide = wi.shape[1]
    chunk = width
    count = wide // chunk

    def weight(s):
        return jnp.where(s < count, s, jnp.minimum(s - count, count - 1))

    def early(s):
        return jnp.clip(s - count, 0, count - 1)

    flat = whole((rows, width))
    square = whole((width, width))
    scratch = [
        pltpu.VMEM((count, rows, chunk), BF16),
        pltpu.VMEM((count, rows, chunk), F32),
        pltpu.VMEM((rows, width), F32),
        pltpu.VMEM((rows, 128), F32),
        pltpu.VMEM((rows, width), BF16),
        pltpu.VMEM((rows, width), F32),
        pltpu.VMEM((rows, width), BF16),
    ]
    if comm:
        narrow = width // size
        grad_specs = [whole((size // 2, narrow, 2 * wide))]
        grad_shapes = [(size // 2, narrow, 2 * wide)]
        scratch += [
            pltpu.VMEM((size // 2, narrow, wide), BF16),
            pltpu.VMEM((count, 2, 4, narrow, width), BF16),
            pltpu.VMEM((size // 2, narrow, wide), BF16),
            pltpu.VMEM((count, 2, 4, narrow, width), BF16),
            pltpu.SemaphoreType.DMA((2, count)),
            pltpu.SemaphoreType.DMA((2, count)),
        ]
    else:
        grad_specs = [
            pl.BlockSpec((width, chunk), lambda s: (0, early(s))),
            pl.BlockSpec((chunk, width), lambda s: (early(s), 0)),
        ]
        grad_shapes = [(width, wide), (wide, width)]
    return pl.pallas_call(
        functools.partial(feed_kernel, count, comm),
        grid=(2 * count + 1,),
        in_specs=[
            flat, flat, flat, square, whole(biases.shape),
            pl.BlockSpec((width, chunk), lambda s: (0, weight(s))),
            pl.BlockSpec((chunk, width), lambda s: (weight(s), 0)),
        ],
        out_specs=[flat, flat, flat, square]
        + grad_specs
        + [whole((8, width)), pl.BlockSpec((1, chunk), lambda s: (0, early(s)))],
        out_shape=[
            jax.ShapeDtypeStruct((rows, width), BF16),
            jax.ShapeDtypeStruct((rows, width), F32),
            jax.ShapeDtypeStruct((rows, width), BF16),
            jax.ShapeDtypeStruct((width, width), BF16),
        ]
        + [jax.ShapeDtypeStruct(a, BF16) for a in grad_shapes]
        + [
            jax.ShapeDtypeStruct((8, width), F32),
            jax.ShapeDtypeStruct((1, wide), F32),
        ],
        scratch_shapes=scratch,
        compiler_params=params(2 if comm else None),
        cost_estimate=cost(
            12 * rows * width * wide + 6 * rows * width * width, 12 * width * wide + 16 * rows * width
        ),
        name="feed",
    )(h1, cc, ct, wco, biases, wi, wo)


def first_back_kernel(
    dcq_ref, dh2_ref, h1_ref, ctx_ref, wcq_ref, wso_ref, b_ref,
    dh1_ref, dsc_ref, gcq_ref, gso_ref, small_ref,
):
    gain = b_ref[4:5]
    n1, r1 = normed(h1_ref[...])
    a1b = (n1 * gain + b_ref[5:6]).astype(BF16)
    dcq = dcq_ref[...]
    d1 = dh2_ref[...] + nt(dcq, wcq_ref[...])
    dh1 = norm_back(d1, n1, r1, gain)
    dh1_ref[...] = dh1
    dso = dh1.astype(BF16)
    dsc_ref[...] = nt(dso, wso_ref[...]).astype(BF16)
    gcq_ref[...] = tn(a1b, dcq).astype(BF16)
    gso_ref[...] = tn(ctx_ref[...], dso).astype(BF16)
    small_ref[0:1] = total(dcq)
    small_ref[1:2] = total(d1 * n1)
    small_ref[2:3] = total(d1)
    small_ref[3:4] = total(dso)
    small_ref[4:8] = jnp.zeros((4, dh1.shape[1]), F32)


def first_back(dcq, dh2, h1, ctx, wcq, wso, biases, schedule):
    rows, width = dcq.shape
    flat, square = whole((rows, width)), whole((width, width))
    return run(
        first_back_kernel, "first_back", 1,
        (dcq, dh2, h1, ctx, wcq, wso, biases),
        [flat, flat, flat, flat, square, square, whole(biases.shape)],
        [
            jax.ShapeDtypeStruct((rows, width), F32),
            jax.ShapeDtypeStruct((rows, width), BF16),
            jax.ShapeDtypeStruct((width, width), BF16),
            jax.ShapeDtypeStruct((width, width), BF16),
            jax.ShapeDtypeStruct((8, width), F32),
        ],
        [flat, flat, square, square, whole((8, width))],
        (), schedule, 4,
        8 * rows * width * width, 8 * width * width + 18 * rows * width,
    )


def outputs_kernel(moves, count, line, *refs):
    pieces, rest = refs[:count], refs[count:]
    out_ref, dx_ref, dxi_ref, dm_ref, dmi_ref = rest[:5]
    outs = rest[5:]
    for piece, first, wide, which, row, col in moves:
        ref = pieces[piece]
        outs[which][row : row + ref.shape[0], col : col + wide] = ref[:, first : first + wide].astype(F32)
    turned, result, dx, dm = outs[-4:]
    turned[...] = jnp.transpose(pieces[line[0]][:, line[1] : line[1] + PAIR].astype(F32))
    result[...] = out_ref[...]
    dx[...] = (dx_ref[...] + dxi_ref[...].astype(F32)).astype(BF16)
    dm[...] = (dm_ref[...] + dmi_ref[...].astype(F32)).astype(BF16)


def outputs(pieces, moves, line, shapes, out, dx, dxi, dm, dmi):
    ins = tuple(pieces) + (out, dx, dxi, dm, dmi)
    result = jax.ShapeDtypeStruct(out.shape, BF16)
    return pl.pallas_call(
        functools.partial(outputs_kernel, moves, len(pieces), line),
        out_shape=[jax.ShapeDtypeStruct(a, F32) for a in shapes]
        + [jax.ShapeDtypeStruct((PAIR, pieces[0].shape[0]), F32), result, result, result],
        compiler_params=params(),
        cost_estimate=cost(0, 12 << 20),
        name="outputs",
    )(*ins)


def moved(pieces, targets):
    out = []
    for n, (start, wide) in enumerate(pieces):
        for first, cols, which, row, col in targets:
            low, high = max(start, first), min(start + wide, first + cols)
            if low < high:
                out.append((n, low - start, high - low, which, row, col + low - first))
    return out


def swap_sum(part, axis, pairs):
    came = lax.ppermute(part, axis, pairs)
    return part.astype(F32) + came.astype(F32)


def sum_scatter(grad, size, order):
    rows, cols = grad.shape
    bits = size.bit_length() - 1
    me = lax.axis_index("dp")
    now = grad.reshape((2,) * bits + (rows // size, cols))
    left = list(range(bits))[::-1]
    for bit in [b for b in order if b < bits] + [b for b in range(bits) if b not in order]:
        axis = left.index(bit)
        mine = (me >> bit) & 1
        keep = lax.dynamic_index_in_dim(now, mine, axis, keepdims=False)
        send = lax.dynamic_index_in_dim(now, 1 - mine, axis, keepdims=False)
        came = lax.ppermute(send, "dp", [(i, i ^ (1 << bit)) for i in range(size)])
        now = (keep.astype(F32) + came.astype(F32)).astype(BF16)
        left.pop(axis)
    return swap_sum(now, "sp", [(0, 1), (1, 0)])


def per_device(
    size,
    inputs,
    memory,
    target_docs,
    memory_docs,
    cotangent,
    w_qkv,
    b_q,
    b_v,
    w_so,
    b_so,
    g_one,
    s_one,
    w_cq,
    b_cq,
    w_ckv,
    b_cv,
    w_co,
    b_co,
    g_two,
    s_two,
    w_fi,
    b_fi,
    w_fo,
    b_fo,
    g_three,
    s_three,
):
    rows, width = inputs.shape[1:]
    wide = b_fi.shape[0]
    comm = size == 16
    narrow, broad = width // size, wide // size
    swap = [(0, 1), (1, 0)]
    x, mem, ct = inputs[0], memory[0], cotangent[0]
    x_o = lax.ppermute(x, "sp", [(0, 1)])
    docs_o = lax.ppermute(jnp.concatenate([target_docs, memory_docs], axis=0), "sp", swap)
    line = lax.broadcasted_iota(jnp.int32, (24, width), 0)
    vectors = (b_q, b_v, b_cv, b_so, g_one, s_one, b_cq, b_co, g_two, s_two, b_fo, g_three, s_three)
    vectors += tuple(b_fi[i : i + width] for i in range(0, wide, width))
    biases = jnp.zeros((24, width), F32)
    for i, v in enumerate(vectors):
        biases = jnp.where(line == i, v.astype(F32)[None], biases)

    qkv, mkv, t_own, m_own = project_own(x, mem, target_docs, memory_docs, w_qkv, w_ckv, biases)
    kvo, mem_s, t_oth, m_oth = project_other(x_o, mem, docs_o[:1], docs_o[1:], w_qkv, biases, t_own)
    mem_o = lax.ppermute(mem_s, "sp", swap)
    ctx, lse = self_forward(qkv, kvo, t_own, t_oth)
    h1, cq = first_norm(x, ctx, w_so, w_cq, biases)
    mkvo = project_memory(mem_o, w_ckv, biases)
    cc, clse = cross_forward(cq, mkv, mkvo, t_own, m_own, m_oth)
    output, dh2, dcc, gco, gwi, *gwo, small_a, gib = feed(size, comm, h1, cc, ct, w_co, biases, w_fi, w_fo)
    turned = gib.reshape(width, -1).T

    block = (2, 2, 2, 2, narrow) if comm else (width,)
    at_cross, at_first, at_other, at_self = (), (), (), ()
    ways = (VIA_X, VIA_Y, VIA_Z)

    def thirds(array, shape, dims):
        wide = shape[-1] // 3
        return [Flow(array, shape, hops, dims, (i * wide, wide)) for i, hops in enumerate(ways)]

    if comm:
        gwi = gwi.reshape(block[:3] + gwi.shape[1:])
        t0 = thirds(gwi, gwi.shape, BLOCK[:3])
        at_cross = ((t0, 0, 4), (t0, 4, 6))
    dcq, dm, dmo, gck, gcv, gcvb = cross_backward(
        cq, mkv, mkvo, dcc, cc, clse, t_own, m_own, m_oth, mem, mem_o, w_ckv, at_cross
    )
    dm_in = lax.ppermute(dmo, "sp", swap)
    if comm:
        at_first = ((t0, 0, 1),)
    dh1, dsc, gcq, gso, small_b = first_back(dcq, dh2, h1, ctx, w_cq, w_so, biases, at_first)
    if comm:
        fresh = [
            Flow(g.reshape(block + (width,)), block + (width,), ("core",)) for g in (gck, gcv, gco, gcq, gso)
        ]
        joint = Joint()
        mid = block[:3] + (narrow, 5 * width)
        t1_cols = ((0, 2048), (2048, 5 * width - 2048))
        t1 = [Flow(joint, mid, hops, BLOCK[:3], cols) for hops, cols in zip((X_FIRST, Z_FIRST), t1_cols)]
        cut = front_pairs(width // PAIR) * PAIR
        end = 3 * width + 2 * PAIR
        t2_cols = ((0, 3 * cut // 2), (3 * cut // 2, 3 * cut // 2), (3 * cut, end - 3 * cut))
        t2 = [
            Flow(("ref", GRADS), block + (end,), ("core",) + hops, BLOCK, cols)
            for hops, cols in zip((X_FIRST, Z_FIRST, AT_ONCE), t2_cols)
        ]
        front, back = t2[:2], t2[2:]
        at_other = ((fresh, 0, 2, joint), (t0, 0, 3), (t0[1:], 3, 6), (t1, 2, 6))
    dqo, dkvo, dxo = other_backward(qkv, kvo, dsc, ctx, lse, t_own, t_oth, w_qkv, at_other)
    dx_in = lax.ppermute(dxo, "sp", [(1, 0)])
    if comm:
        at_self = (
            (t1, 0, 2), (t1, 2, 4), (t1, 4, 5),
            (front, 4, 5), (front, 5, 6), (front, 6, 7), (front, 7, 8), (front, 8, 9),
            (back, 6, 7), (back, 7, 8), (back, 8, 9), (back, 9, 10),
        )
    dx, *made = self_backward(
        block, qkv, dsc, ctx, lse, t_own, dqo, dkvo, x, x_o, w_qkv, dh1, (small_a, small_b, gcvb, turned), at_self
    )
    if comm:
        spans = [(i * 2 * wide // 3, 2 * wide // 3) for i in range(3)]
        moves = moved(spans, [(0, wide, 2, 0, 0)] + [(wide + i * width, width, 3, i * narrow, 0) for i in range(4)])
        targets = [(0, 2 * width, 1, 0, 0)] + [((2 + i) * width, width, 4 + i, 0, 0) for i in range(3)]
        moves += [(m[0] + 3,) + m[1:] for m in moved(t1_cols, targets)]
        rest = width - cut
        targets = []
        for i in range(3):
            targets += [(i * cut, cut, 0, 0, i * width)]
            targets += [(3 * cut + i * rest + 2 * PAIR * (i > 0), rest, 0, 0, i * width + cut)]
        moves += [(m[0] + 5,) + m[1:] for m in moved(t2_cols, targets)]
        shapes = [(narrow, 3 * width), (narrow, 2 * width), (narrow, wide), (broad, width)] + [(narrow, width)] * 3
        t_qkv, t_cmem, t_fin, t_fout, t_cout, t_cquery, t_out, lines, output, derivative, grad_memory = outputs(
            [f.array for f in t0 + t1 + t2], moves, (7, rest), shapes, output, dx, dx_in, dm, dm_in
        )
    else:
        cut = front_pairs(width // PAIR) * PAIR
        rest = width - cut
        (gqkv,) = made
        at = [0, cut, 2 * cut, 3 * cut, 3 * cut + rest + 2 * PAIR, 3 * cut + 2 * rest + 2 * PAIR]
        columns = gqkv[:, 3 * cut + rest : 3 * cut + rest + PAIR]
        gqkv = jnp.concatenate(
            [gqkv[:, a : a + n] for i in range(3) for a, n in ((at[i], cut), (at[3 + i], rest))], axis=1
        )
        t_fin, t_fout, t_cout, t_cquery, t_out, t_cmem, t_qkv, lines = (
            sum_scatter(g, size, (0, 1, 2, 3))
            for g in (
                gwi, gwo[0], gco, gcq, gso, jnp.concatenate([gck, gcv], axis=1),
                gqkv, columns,
            )
        )
        lines, derivative = lines.T, (dx + dx_in.astype(F32)).astype(BF16)
        grad_memory = (dm + dm_in.astype(F32)).astype(BF16)
    t_gthree, t_sthree, t_fobias, t_gtwo, t_stwo, t_cobias = (lines[i] for i in range(6))
    t_cqbias, t_gone, t_sone, t_obias = (lines[i] for i in range(8, 12))
    t_cvbias, t_qbias, t_vbias = lines[16], lines[21], lines[22]
    t_fibias = lines[17:21].T.reshape(-1)
    return (
        output[None],
        derivative[None],
        grad_memory[None],
        t_qkv,
        t_qbias,
        t_vbias,
        t_out,
        t_obias,
        t_gone,
        t_sone,
        t_cquery,
        t_cqbias,
        t_cmem,
        t_cvbias,
        t_cout,
        t_cobias,
        t_gtwo,
        t_stwo,
        t_fin,
        t_fibias,
        t_fout,
        t_fobias,
        t_gthree,
        t_sthree,
    )


def solution(mesh):
    split = P("dp", "sp", None)
    in_specs = (split, split, P("dp", "sp"), P("dp", "sp"), split) + (P(),) * 21
    matrix, vector = P("dp", None), P("dp")
    out_specs = (
        split, split, split,
        matrix, vector, vector,
        matrix, vector, vector, vector,
        matrix, vector,
        matrix, vector,
        matrix, vector, vector, vector,
        matrix, vector,
        matrix, vector, vector, vector,
    )
    return jax.shard_map(
        functools.partial(per_device, mesh.shape["dp"]),
        mesh=mesh, in_specs=in_specs, out_specs=out_specs, check_vma=False,
    )
```

```python
import functools

import jax
import jax.numpy as jnp
from jax import lax
from jax.experimental import pallas as pl
from jax.experimental.pallas import tpu as pltpu
from jax.sharding import PartitionSpec as P

HD = 64
PAIR = 2 * HD
EPS = 1e-05
FAR = 1.0e9
VMEM = 60 * 1024 * 1024
F32 = jnp.float32
BF16 = jnp.bfloat16


def nn(a, b):
    return lax.dot_general(a, b, (((1,), (0,)), ((), ())), preferred_element_type=F32)


def nt(a, b):
    return lax.dot_general(a, b, (((1,), (1,)), ((), ())), preferred_element_type=F32)


def tn(a, b):
    return lax.dot_general(a, b, (((0,), (0,)), ((), ())), preferred_element_type=F32)


def params(collective=None):
    if collective is None:
        return pltpu.CompilerParams(vmem_limit_bytes=VMEM)
    return pltpu.CompilerParams(
        vmem_limit_bytes=VMEM, collective_id=collective, has_side_effects=True
    )


def cost(flops, moved):
    return pl.CostEstimate(flops=int(flops), bytes_accessed=int(moved), transcendentals=0)


def normed(h):
    centred = h - jnp.mean(h, axis=-1, keepdims=True)
    rstd = lax.rsqrt(jnp.mean(centred * centred, axis=-1, keepdims=True) + EPS)
    return centred * rstd, rstd


def norm_back(grad, n, rstd, gain):
    scaled = grad * gain
    centre = jnp.mean(scaled, axis=-1, keepdims=True)
    along = jnp.mean(scaled * n, axis=-1, keepdims=True)
    return rstd * (scaled - centre - n * along)


def total(a):
    return jnp.sum(a.astype(F32), axis=0, keepdims=True)


def place():
    me = lax.axis_index("dp")
    return me, me % 2, (me // 2) % 2, me // 4, lax.axis_index("sp")


def flipped(at, hops):
    me, c, x, z, sp = at
    for hop in hops:
        if hop == "core":
            me, c = me + 1 - 2 * c, 1 - c
        elif hop == "x":
            me, x = me + 2 - 4 * x, 1 - x
        elif hop == "z1":
            me, z = me + 4 - 8 * (z % 2), z + 1 - 2 * (z % 2)
        elif hop == "z2":
            me, z = me + 8 - 16 * (z // 2), z + 2 - 4 * (z // 2)
        else:
            sp = 1 - sp
    return me, c, x, z, sp


def partner(hops, at=None):
    there = flipped(at or place(), hops)
    return {"dp": there[0], "sp": there[4]}


def greet(groups, at=None):
    groups = sorted({tuple("y" if h[0] == "y" else h for h in hops) for hops in groups})
    barrier = pltpu.get_barrier_semaphore()
    for hops in groups:
        pl.semaphore_signal(barrier, inc=1, device_id=partner(hops, at), device_id_type=pl.DeviceIdType.MESH)
    pl.semaphore_wait(barrier, len(groups))


def remote(src, dst, send, recv, hops, at=None):
    return pltpu.make_async_remote_copy(
        src_ref=src, dst_ref=dst, send_sem=send, recv_sem=recv,
        device_id=partner(hops, at), device_id_type=pl.DeviceIdType.MESH,
    )


PLAN = {
    "T00": ("T0", (0, 2304), ("x", "yr", "z1", "z2", "yg"), ((0, 5), (5, 7)), ((0, 6), (6, 8), (8, 11))),
    "T01": ("T0", (2304, 1280), ("z1", "x", "z2", "y"), ((0, 3), (3, 6), (6, 7)), ((0, 3),)),
    "T02": ("T0", (3584, 2560), ("yr", "x", "z1", "z2", "yg"), ((0, 5), (5, 7)), ((0, 7), (7, 9), (9, 12))),
    "T1a0": ("T1a", (0, 1280), ("core", "x", "yr", "z1", "z2", "yg"), ((6, 7),), ((0, 5), (5, 10), (10, 12), (12, 18), (18, 22))),
    "T1a1": ("T1a", (1280, 1024), ("core", "z1", "x", "z2", "y"), ((6, 7),), ((0, 8), (8, 10), (10, 12), (12, 17))),
    "T1b0": ("T1b", (0, 1536), ("core", "x", "z1", "yr", "z2", "yg"), (), ((0, 3), (3, 8), (8, 10), (10, 13), (13, 20), (20, 25))),
    "G10": ("G", (0, 768), ("core", "x", "z1", "z2", "y"), (), ((8, 9), (9, 11), (11, 13), (13, 20), (20, 25))),
    "G20": ("G", (768, 256), ("core", "x", "z1", "z2", "y"), (), ((10, 11), (11, 12), (12, 15), (15, 19), (19, 24))),
    "G21": ("G", (1024, 512), ("core", "x", "yr", "z1", "z2", "yg"), (), ((10, 12), (12, 17), (17, 23), (23, 26), (26, 28), (28, 30))),
    "G30": ("G", (1536, 640), ("core", "x", "z1", ("z2", "y")), (), ((12, 16), (16, 21), (21, 27), (27, 32))),
    "G31": ("G", (2176, 384), ("core", "z1", "x", "z2", "y"), (), ((12, 14), (14, 24), (24, 25), (25, 29), (29, 31))),
}
BLOCK = ("z2", "z1", "x", "core")


class Part:
    def __init__(self, hop, shape, dims, cols=None):
        self.hops = hops = hop if isinstance(hop, tuple) else (hop,)
        self.groups = [(h,) for h in hops] + ([hops] if len(hops) > 1 else [])
        self.dims = dims
        self.cols = cols or (0, shape[-1])
        self.shape = shape = tuple(shape[:-1]) + (self.cols[1],)
        for h in hops:
            if h in dims:
                at = dims.index(h)
                shape, dims = shape[:at] + shape[at + 1 :], dims[:at] + dims[at + 1 :]
            elif h != "y":
                shape = shape[:-1] + (shape[-1] // 2 if h == "yr" else 2 * shape[-1],)
        self.after, self.left = shape, dims
        self.came = self.shape if hops == ("yg",) else shape

    def share(self, at):
        _, c, x, z, sp = at
        first, wide = self.cols
        index = [slice(None)] * (len(self.shape) - 1) + [pl.ds(first, wide)]
        for h in self.hops:
            if h in self.dims:
                index[self.dims.index(h)] = {"core": c, "x": x, "z1": z % 2, "z2": z // 2}[h]
            elif h == "yr":
                half = wide // 2
                index[-1] = pl.ds(pl.multiple_of(first + sp * half, 128), half)
        return tuple(index)

    def copies(self, src, held, made, came, send, recv, local, at):
        out = [
            remote(src.at[self.share(flipped(at, g))], came[i], send.at[i], recv.at[i], g, at)
            for i, g in enumerate(self.groups)
        ]
        if not held:
            out.append(pltpu.make_async_copy(src.at[self.share(at)], made, local))
        return out

    def add(self, src, held, made, came, at):
        if self.hops == ("yg",):
            wide, sp = self.shape[-1], at[4]
            lead = (slice(None),) * (len(self.shape) - 1)
            made[lead + (pl.ds(pl.multiple_of(sp * wide, 128), wide),)] = src[self.share(at)]
            made[lead + (pl.ds(pl.multiple_of((1 - sp) * wide, 128), wide),)] = came[0][...]
        elif len(came) > 1:
            mine = src[self.share(at)] if held else made[...]
            one, two, three = (c[...].astype(F32) for c in came)
            made[...] = ((mine.astype(F32) + one) + (two + three)).astype(BF16)
        elif held:
            made[...] = src[self.share(at)] + came[0][...]
        else:
            made[...] += came[0][...]


class Flow:
    def __init__(self, array, shape, hops, dims=BLOCK, cols=None):
        self.array, self.shape, self.dims, self.cols = array, tuple(shape), dims, cols
        self.hops = list(hops)

    def step(self):
        part = Part(self.hops.pop(0), self.shape, self.dims, self.cols)
        self.shape, self.dims, self.cols = part.after, part.left, None
        return part


class Window:
    def __init__(self, start, stop, joint):
        self.start, self.stop, self.joint = start, stop, joint
        self.parts, self.sources, self.keeps = [], [], []


class Joint:
    def __init__(self):
        self.window = None


def plan(schedule):
    windows, arrays, latest = [], [], {}
    for n, (flows, start, stop, *joint) in enumerate(schedule):
        window = Window(start, stop, bool(joint))
        if joint:
            joint[0].window = n
        for i, flow in enumerate(flows):
            if flow in latest:
                source = ("part",) + latest[flow]
                before = windows[latest[flow][0]]
                before.keeps[latest[flow][1]] = False
            elif isinstance(flow.array, Joint):
                source = ("joint", flow.array.window)
            elif isinstance(flow.array, tuple):
                source = flow.array
            else:
                known = [k for k, a in enumerate(arrays) if a is flow.array]
                if not known:
                    arrays.append(flow.array)
                source = ("in", known[0] if known else len(arrays) - 1)
            window.parts.append(flow.step())
            window.sources.append(source)
            window.keeps.append(not joint)
            if not joint:
                latest[flow] = (n, i)
        windows.append(window)
    return windows, arrays, latest


def carrying(body, own, windows, arrays, grid, also, finale):
    ins, outs, held = own

    def kernel(*refs):
        refs = list(refs)

        def take(n):
            got = refs[:n]
            del refs[:n]
            return got

        my_in, arr = take(ins), take(arrays)
        my_out = take(outs)
        given = [[take(1)[0] if k else None for k in w.keeps] for w in windows]
        my_held = take(held)
        made, came, joints = [], [], []
        for w, g in zip(windows, given):
            if w.joint:
                joint, col, views = take(1)[0], 0, []
                for q in w.parts:
                    views.append(joint.at[(slice(None),) * (len(q.after) - 1) + (pl.ds(col, q.after[-1]),)])
                    col += q.after[-1]
                joints.append(joint)
                made.append(views)
            else:
                joints.append(None)
                made.append([ref if ref is not None else take(1)[0] for ref in g])
            came.append([take(len(q.groups)) for q in w.parts])
        mine = my_in + my_out + my_held
        step = pl.program_id(0)
        groups = [g for w in windows for q in w.parts for g in q.groups] + list(also)
        if groups:
            here = place()
            pl.when(step == 0)(lambda: greet(groups, here))
        if windows:
            send, recv, local = refs
        copies, sources, base = [], [], 0
        for w, m, c in zip(windows, made, came):
            now, froms = [], []
            for i, q in enumerate(w.parts):
                kind = w.sources[i]
                if kind[0] == "in":
                    src = arr[kind[1]]
                elif kind[0] == "ref":
                    src = mine[kind[1]]
                elif kind[0] == "joint":
                    src = joints[kind[1]]
                else:
                    src = made[kind[1]][kind[2]]
                held_here = kind[0] != "in"
                froms.append((src, held_here))
                now += q.copies(
                    src, held_here, m[i], c[i], send.at[base], recv.at[base], local.at[base], here
                )
                base += 1
            copies.append(now)
            sources.append(froms)

        def phase(number):
            for n, w in enumerate(windows):
                if w.stop == number:
                    for copy in copies[n]:
                        copy.wait()
                    for q, (src, held_here), m, c in zip(w.parts, sources[n], made[n], came[n]):
                        q.add(src, held_here, m, c, here)
            for n, w in enumerate(windows):
                if w.start == number:
                    for copy in copies[n]:
                        copy.start()

        used = sorted({w.start for w in windows} | {w.stop for w in windows})
        for number in used:
            if number < grid:
                pl.when(step == number)(functools.partial(phase, number))
        body(*mine)
        for number in used:
            if number >= grid:
                pl.when(step == grid - 1)(functools.partial(phase, number))
        if finale:
            pl.when(step == grid - 1)(lambda: finale(*mine))

    return kernel


def run(
    body, name, grid, ins, in_specs, outs, out_specs, held=(), schedule=(), collective=None,
    flops=0, moved=0, also=(), finale=None,
):
    in_specs, outs, out_specs, held = list(in_specs), list(outs), list(out_specs), list(held)
    windows, arrays, latest = plan(schedule)
    own = len(outs)
    kernel = carrying(body, (len(ins), own, len(held)), windows, len(arrays), grid, also, finale)
    in_specs += [pl.BlockSpec(memory_space=pl.ANY)] * len(arrays)
    order, count = [], 0
    for n, w in enumerate(windows):
        if w.joint:
            shape = w.parts[0].after[:-1] + (sum(q.after[-1] for q in w.parts),)
            held.append(pltpu.VMEM(shape, BF16))
        for i, (q, k) in enumerate(zip(w.parts, w.keeps)):
            if w.joint:
                continue
            if k:
                outs.append(jax.ShapeDtypeStruct(q.after, BF16))
                out_specs.append(whole(q.after))
                order.append((n, i))
            else:
                held.append(pltpu.VMEM(q.after, BF16))
        held += [pltpu.VMEM(q.came, BF16) for q in w.parts for _ in q.groups]
        count += len(w.parts)
    if windows:
        held += [pltpu.SemaphoreType.DMA((count, 3))] * 2 + [pltpu.SemaphoreType.DMA((count,))]
    results = pl.pallas_call(
        kernel,
        grid=(grid,),
        in_specs=in_specs,
        out_specs=out_specs,
        out_shape=outs,
        scratch_shapes=held,
        compiler_params=params(collective if windows or also else None),
        cost_estimate=cost(flops, moved),
        name=name,
    )(*ins, *arrays)
    for flow, where in latest.items():
        flow.array = results[own + order.index(where)]
    return results[:own]


def code_of(docs_ref):
    row = lax.broadcasted_iota(jnp.int32, (128, docs_ref.shape[1]), 0)
    return jnp.transpose(jnp.where(docs_ref[...] == row, 1.0, 0.0)).astype(BF16)


def project_own_kernel(x_ref, m_ref, td_ref, md_ref, wx_ref, wm_ref, b_ref, qkv_ref, mkv_ref, to_ref, mo_ref):
    step = pl.program_id(0)

    @pl.when(step == 0)
    def _():
        to_ref[...] = code_of(td_ref)
        mo_ref[...] = code_of(md_ref)

    @pl.when(step < 3)
    def _():
        bias = jnp.where(step == 0, b_ref[0:1], 0.0) + jnp.where(step == 2, b_ref[1:2], 0.0)
        qkv_ref[...] = (nn(x_ref[...], wx_ref[...]) + bias).astype(BF16)

    @pl.when(step >= 3)
    def _():
        bias = jnp.where(step == 4, b_ref[2:3], 0.0)
        mkv_ref[...] = (nn(m_ref[...], wm_ref[...]) + bias).astype(BF16)


def project_own(x, mem, td, md, wx, wm, biases):
    rows, width = x.shape
    code = jax.ShapeDtypeStruct((rows, 128), BF16)
    return pl.pallas_call(
        project_own_kernel,
        grid=(5,),
        in_specs=[
            whole((rows, width)), whole((rows, width)), whole((1, rows)), whole((1, rows)),
            pl.BlockSpec((width, width), lambda s: (0, jnp.minimum(s, 2))),
            pl.BlockSpec((width, width), lambda s: (0, jnp.maximum(s - 3, 0))),
            whole(biases.shape),
        ],
        out_specs=[
            pl.BlockSpec((rows, width), lambda s: (0, jnp.minimum(s, 2))),
            pl.BlockSpec((rows, width), lambda s: (0, jnp.maximum(s - 3, 0))),
            whole((rows, 128)), whole((rows, 128)),
        ],
        out_shape=[
            jax.ShapeDtypeStruct((rows, 3 * width), BF16), jax.ShapeDtypeStruct((rows, 2 * width), BF16), code, code,
        ],
        compiler_params=params(),
        cost_estimate=cost(10 * rows * width * width, 20 * width * width),
        name="project_own",
    )(x, mem, td, md, wx, wm, biases)


def project_other_kernel(x_ref, m_ref, td_ref, md_ref, wx_ref, b_ref, after_ref, kvo_ref, mem_ref, tt_ref, mt_ref):
    step = pl.program_id(0)

    @pl.when(step == 0)
    def _():
        mem_ref[...] = m_ref[...]
        tt_ref[...] = code_of(td_ref)
        mt_ref[...] = code_of(md_ref)

    @pl.when(lax.axis_index("sp") == 1)
    def _():
        bias = jnp.where(step == 1, b_ref[1:2], 0.0)
        kvo_ref[...] = (nn(x_ref[...], wx_ref[...]) + bias).astype(BF16)

    @pl.when(lax.axis_index("sp") == 0)
    def _():
        kvo_ref[...] = jnp.zeros(kvo_ref.shape, BF16)


def project_other(x, mem, td, md, wx, biases, after):
    rows, width = x.shape
    code = jax.ShapeDtypeStruct((rows, 128), BF16)
    return pl.pallas_call(
        project_other_kernel,
        grid=(2,),
        in_specs=[
            whole((rows, width)), whole((rows, width)), whole((1, rows)), whole((1, rows)),
            pl.BlockSpec((width, width), lambda s: (0, s + 1)),
            whole(biases.shape),
            pl.BlockSpec(memory_space=pl.ANY),
        ],
        out_specs=[
            pl.BlockSpec((rows, width), lambda s: (0, s)),
            whole((rows, width)), whole((rows, 128)), whole((rows, 128)),
        ],
        out_shape=[
            jax.ShapeDtypeStruct((rows, 2 * width), BF16), jax.ShapeDtypeStruct((rows, width), BF16), code, code,
        ],
        compiler_params=params(),
        cost_estimate=cost(4 * rows * width * width, 10 * width * width),
        name="project_other",
    )(x, mem, td, md, wx, biases, after)


def project_memory_kernel(x_ref, w_ref, b_ref, o_ref):
    bias = jnp.where(pl.program_id(0) == 1, b_ref[2:3], 0.0)
    o_ref[...] = (nn(x_ref[...], w_ref[...]) + bias).astype(BF16)


def project_memory(x, w, biases):
    rows, width = x.shape
    return pl.pallas_call(
        project_memory_kernel,
        grid=(2,),
        in_specs=[
            whole((rows, width)),
            pl.BlockSpec((width, width), lambda j: (0, j)),
            whole(biases.shape),
        ],
        out_specs=pl.BlockSpec((rows, width), lambda j: (0, j)),
        out_shape=jax.ShapeDtypeStruct((rows, 2 * width), BF16),
        compiler_params=params(),
        cost_estimate=cost(4 * rows * width * width, 4 * width * (width + rows)),
        name="project_memory",
    )(x, w, biases)


def head_masks(dtype):
    lane = lax.broadcasted_iota(jnp.int32, (1, PAIR), 1)
    low = jnp.where(lane < HD, 1.0, 0.0)
    return low.astype(dtype), (1.0 - low).astype(dtype)


def query_code(code):
    lane = lax.broadcasted_iota(jnp.int32, code.shape, 1)
    return jnp.where(lane < 4, (code.astype(F32) - 1.0) * FAR, 0.0).astype(BF16)


def softmax_pieces(scores, values):
    peak = functools.reduce(jnp.maximum, [jnp.max(s, axis=-1, keepdims=True) for s in scores])
    expd = [jnp.exp(s - peak) for s in scores]
    norm = sum(jnp.sum(e, axis=-1, keepdims=True) for e in expd)
    out = sum(nn(e.astype(BF16), v) for e, v in zip(expd, values))
    return out / norm, peak + jnp.log(norm)


def self_pieces(block, size, both, own, other):
    pieces = []
    if both:
        pieces.append((other, False))
    if block:
        pieces.append((own[: block * size], False))
    pieces.append((own[block * size : (block + 1) * size], True))
    return pieces


def store_lse(lse_ref, block, size, low, high):
    lane = lax.broadcasted_iota(jnp.int32, (size, PAIR), 1)
    both = jnp.where(lane == 0, low, high)
    lse_ref[:, block * size : (block + 1) * size] = jnp.transpose(both)[:8]


def self_forward_kernel(size, q_ref, k_ref, v_ref, ko_ref, vo_ref, own_ref, oth_ref, o_ref, lse_ref):
    second = lax.axis_index("sp") == 1
    rows = q_ref.shape[0]
    masks = head_masks(BF16)
    outs = head_masks(F32)

    def run(both):
        qcode = query_code(own_ref[...])
        own = jnp.concatenate([k_ref[...], own_ref[...]], axis=1)
        oth = jnp.concatenate([ko_ref[...], oth_ref[...]], axis=1) if both else None
        vown = v_ref[...]
        voth = vo_ref[...] if both else None
        for block in range(rows // size):
            at = slice(block * size, (block + 1) * size)
            lses, result = [], 0.0
            for mask, keep in zip(masks, outs):
                q = jnp.concatenate([q_ref[at] * (mask * BF16(HD**-0.5)), qcode[at]], axis=1)
                scores = []
                for keys, diagonal in self_pieces(block, size, both, own, oth):
                    s = nt(q, keys)
                    if diagonal:
                        row = lax.broadcasted_iota(jnp.int32, s.shape, 0)
                        col = lax.broadcasted_iota(jnp.int32, s.shape, 1)
                        s = jnp.where(row >= col, s, -FAR)
                    scores.append(s)
                values = [v for v, _ in self_pieces(block, size, both, vown, voth)]
                out, lse = softmax_pieces(scores, values)
                result = result + out * keep
                lses.append(lse)
            o_ref[at] = result.astype(BF16)
            store_lse(lse_ref, block, size, *lses)

    pl.when(second)(lambda: run(True))
    pl.when(jnp.logical_not(second))(lambda: run(False))


def pair_spec(rows, offset):
    return pl.BlockSpec((rows, PAIR), lambda p: (0, p + offset))


def whole(shape):
    return pl.BlockSpec(shape, lambda *_: (0,) * len(shape))


def self_forward(qkv, kvo, own, oth):
    rows = qkv.shape[0]
    width = qkv.shape[1] // 3
    pairs = width // PAIR
    return pl.pallas_call(
        functools.partial(self_forward_kernel, 256),
        grid=(pairs,),
        in_specs=[
            pair_spec(rows, 0),
            pair_spec(rows, pairs),
            pair_spec(rows, 2 * pairs),
            pair_spec(rows, 0),
            pair_spec(rows, pairs),
            whole((rows, 128)),
            whole((rows, 128)),
        ],
        out_specs=[pair_spec(rows, 0), pl.BlockSpec((8, rows), lambda p: (p, 0))],
        out_shape=[
            jax.ShapeDtypeStruct((rows, width), BF16),
            jax.ShapeDtypeStruct((8 * pairs, rows), F32),
        ],
        compiler_params=params(),
        cost_estimate=cost(16 * rows * rows * width, 16 * rows * width),
        name="self_forward",
    )(qkv, qkv, qkv, kvo, kvo, own, oth)


def cross_forward_kernel(size, q_ref, k_ref, v_ref, ko_ref, vo_ref, t_ref, own_ref, oth_ref, o_ref, lse_ref):
    rows = q_ref.shape[0]
    masks = head_masks(BF16)
    outs = head_masks(F32)
    qcode = query_code(t_ref[...])
    keys = [
        jnp.concatenate([k_ref[...], own_ref[...]], axis=1),
        jnp.concatenate([ko_ref[...], oth_ref[...]], axis=1),
    ]
    values = [v_ref[...], vo_ref[...]]
    for block in range(rows // size):
        at = slice(block * size, (block + 1) * size)
        lses, result = [], 0.0
        for mask, keep in zip(masks, outs):
            q = jnp.concatenate([q_ref[at] * (mask * BF16(HD**-0.5)), qcode[at]], axis=1)
            out, lse = softmax_pieces([nt(q, k) for k in keys], values)
            result = result + out * keep
            lses.append(lse)
        o_ref[at] = result.astype(BF16)
        store_lse(lse_ref, block, size, *lses)


def cross_forward(cq, kv, kvo, t, own, oth):
    rows, width = cq.shape
    pairs = width // PAIR
    return pl.pallas_call(
        functools.partial(cross_forward_kernel, 256),
        grid=(pairs,),
        in_specs=[
            pair_spec(rows, 0),
            pair_spec(rows, 0),
            pair_spec(rows, pairs),
            pair_spec(rows, 0),
            pair_spec(rows, pairs),
            whole((rows, 128)),
            whole((rows, 128)),
            whole((rows, 128)),
        ],
        out_specs=[pair_spec(rows, 0), pl.BlockSpec((8, rows), lambda p: (p, 0))],
        out_shape=[
            jax.ShapeDtypeStruct((rows, width), BF16),
            jax.ShapeDtypeStruct((8 * pairs, rows), F32),
        ],
        compiler_params=params(),
        cost_estimate=cost(24 * rows * rows * width, 16 * rows * width),
        name="cross_forward",
    )(cq, kv, kv, kvo, kvo, t, own, oth)


def delta_rows(g, o):
    prod = g.astype(F32) * o.astype(F32)
    upper = prod.astype(BF16)
    lower = (prod - upper.astype(F32)).astype(BF16)
    row = lax.broadcasted_iota(jnp.int32, (8, PAIR), 0)
    lane = lax.broadcasted_iota(jnp.int32, (8, PAIR), 1)
    pick = jnp.where(row == lane // HD, 1.0, 0.0).astype(BF16)
    return nt(pick, upper) + nt(pick, lower)


def back_piece(keys, values, q, g, lse, delta, causal):
    s = nt(keys, q)
    if causal:
        row = lax.broadcasted_iota(jnp.int32, s.shape, 0)
        col = lax.broadcasted_iota(jnp.int32, s.shape, 1)
        s = jnp.where(row <= col, s, -FAR)
    p = jnp.exp(s - lse)
    ds = p * (nt(values, g) - delta)
    return p.astype(BF16), ds.astype(BF16)


def cross_backward_kernel(
    size, pairs, q_ref, k_ref, v_ref, ko_ref, vo_ref, g_ref, o_ref, lse_ref, t_ref, own_ref, oth_ref,
    m_ref, mo_ref, wk_ref, wv_ref, gco_ref, dh2_ref, h1_ref, ctx_ref, wcq_ref, wso_ref, b_ref,
    dm_ref, dmo_ref, gb_ref, dh1_ref, dsc_ref, late_ref, small_ref, grad_ref,
    dmo_acc, mt_ref, mot_ref, dcq_ref,
):
    step = pl.program_id(0)
    rows, width = m_ref.shape
    lead = (slice(None),) * (len(grad_ref.shape) - 1)

    def put(ref, col, grad):
        to = pl.ds(pl.multiple_of(col, PAIR), grad.shape[1])
        ref[lead + (to,)] = grad.astype(BF16).reshape(ref.shape[:-1] + (grad.shape[1],))

    @pl.when(step == 0)
    def _():
        mt_ref[...] = jnp.transpose(m_ref[...])
        mot_ref[...] = jnp.transpose(mo_ref[...])
        put(grad_ref, 0, gco_ref[...])

    @pl.when(step < pairs)
    def _():
        count = rows // size
        halves = [(k_ref, v_ref, own_ref, mt_ref, dm_ref), (ko_ref, vo_ref, oth_ref, mot_ref, dmo_acc)]
        cols = pl.ds(pl.multiple_of(step * PAIR, PAIR), PAIR)
        dq = [0.0] * count
        gk = gv = gb = 0.0
        for kr, vr, code, mem, acc in halves:
            keys = jnp.concatenate([kr[...], code[...]], axis=1)
            values = vr[...]
            dk = dv = 0.0
            for block, mask, qm, gm, q, lse, delta in backward_pieces(size, q_ref, g_ref, o_ref, lse_ref, t_ref):
                p, ds = back_piece(keys, values, q, gm, lse, delta, False)
                dk = dk + nn(ds, qm)
                dv = dv + nn(p, gm)
                dq[block] = dq[block] + tn(ds, kr[...] * mask)
            both = jnp.concatenate([dk.astype(BF16), dv.astype(BF16)], axis=1)
            grad = nn(mem[...], both)
            gk, gv = gk + grad[:, :PAIR], gv + grad[:, PAIR:]
            gb = gb + total(both[:, PAIR:])
            dm = nt(both, jnp.concatenate([wk_ref[...], wv_ref[...]], axis=1))

            @pl.when(step == 0)
            def _():
                acc[...] = dm

            @pl.when(step > 0)
            def _():
                acc[...] += dm

        for block in range(count):
            dcq_ref[block * size : (block + 1) * size, cols] = dq[block].astype(BF16)
        put(grad_ref, width + step * PAIR, gk)
        put(grad_ref, 2 * width + step * PAIR, gv)
        gb_ref[:, cols] = gb

    @pl.when(step == pairs)
    def _():
        dmo_ref[...] = dmo_acc[...].astype(BF16)
        gain = b_ref[4:5]
        n1, r1 = normed(h1_ref[...])
        a1b = (n1 * gain + b_ref[5:6]).astype(BF16)
        dcq = dcq_ref[...]
        d1 = dh2_ref[...] + nt(dcq, wcq_ref[...])
        dh1 = norm_back(d1, n1, r1, gain)
        dh1_ref[...] = dh1
        dso = dh1.astype(BF16)
        dsc_ref[...] = nt(dso, wso_ref[...]).astype(BF16)
        put(late_ref, 0, tn(a1b, dcq))
        put(late_ref, width, tn(ctx_ref[...], dso))
        small_ref[0:1] = total(dcq)
        small_ref[1:2] = total(d1 * n1)
        small_ref[2:3] = total(d1)
        small_ref[3:4] = total(dso)
        small_ref[4:8] = jnp.zeros((4, width), F32)


MIDDLE = 29


def cross_backward(block, cq, kv, kvo, g, o, lse, t, own, oth, m, mo, w, gco, dh2, h1, ctx, wcq, wso, biases, schedule):
    rows, width = cq.shape
    pairs = width // PAIR

    def pair_of(size, offset):
        return pl.BlockSpec((size, PAIR), lambda s: (0, jnp.minimum(s, pairs - 1) + offset))

    flat, square = whole((rows, width)), whole((width, width))
    outs = [
        jax.ShapeDtypeStruct((rows, width), F32),
        jax.ShapeDtypeStruct((rows, width), BF16),
        jax.ShapeDtypeStruct((1, width), F32),
        jax.ShapeDtypeStruct((rows, width), F32),
        jax.ShapeDtypeStruct((rows, width), BF16),
        jax.ShapeDtypeStruct(block + (2 * width,), BF16),
        jax.ShapeDtypeStruct((8, width), F32),
    ]
    specs = [flat, flat, whole((1, width)), flat, flat, whole(block + (2 * width,)), whole((8, width))]
    held = []
    if schedule:
        held.append(pltpu.VMEM(block + (3 * width,), BF16))
    else:
        outs.append(jax.ShapeDtypeStruct(block + (3 * width,), BF16))
        specs.append(whole(block + (3 * width,)))
    held += [
        pltpu.VMEM((rows, width), F32),
        pltpu.VMEM((width, rows), BF16),
        pltpu.VMEM((width, rows), BF16),
        pltpu.VMEM((rows, width), BF16),
    ]
    return run(
        functools.partial(cross_backward_kernel, 256, pairs), "cross_backward", pairs + 1,
        (cq, kv, kv, kvo, kvo, g, o, lse, t, own, oth, m, mo, w, w, gco, dh2, h1, ctx, wcq, wso, biases),
        [
            pair_of(rows, 0), pair_of(rows, 0), pair_of(rows, pairs), pair_of(rows, 0), pair_of(rows, pairs),
            pair_of(rows, 0), pair_of(rows, 0),
            pl.BlockSpec((8, rows), lambda s: (jnp.minimum(s, pairs - 1), 0)),
            whole((rows, 128)), whole((rows, 128)), whole((rows, 128)), flat, flat,
            pair_of(width, 0), pair_of(width, pairs),
            square, flat, flat, flat, square, square, whole(biases.shape),
        ],
        outs, specs, held, schedule, 3,
        64 * rows * rows * width + 24 * rows * width * width, 40 * rows * width,
    )


def backward_pieces(size, q_ref, g_ref, o_ref, lse_ref, own_ref):
    masks = head_masks(BF16)
    scale = BF16(HD**-0.5)
    qcode = query_code(own_ref[...])
    delta = delta_rows(g_ref[...], o_ref[...])
    for block in range(q_ref.shape[0] // size):
        at = slice(block * size, (block + 1) * size)
        for head, mask in enumerate(masks):
            qm = q_ref[at] * (mask * scale)
            gm = g_ref[at] * mask
            q = jnp.concatenate([qm, qcode[at]], axis=1)
            yield block, mask * scale, qm, gm, q, lse_ref[head : head + 1, at], delta[head : head + 1, at]


def self_backward_kernel(
    size, q_ref, k_ref, v_ref, ko_ref, vo_ref, g_ref, o_ref, lse_ref, own_ref, oth_ref,
    x_ref, xo_ref, wq_ref, wk_ref, wv_ref, dh1_ref, sa_ref, sb_ref, sc_ref, sd_ref, dmo_ref,
    dx_ref, dmi_ref, grad_ref,
    dq_acc, dx_acc, dxo_acc, dkv_acc, xt_ref, xot_ref, dxo_ref, came_ref, memory_ref, turn_ref, send_ref, recv_ref,
):
    step = pl.program_id(0)
    sp = lax.axis_index("sp")
    second = sp == 1
    rows, width = x_ref.shape
    pairs = width // PAIR
    pair = lax.rem(step, pairs)
    cols = pl.ds(pl.multiple_of(pair * PAIR, PAIR), PAIR)
    count = rows // size
    over = remote(dxo_ref, came_ref, send_ref.at[0], recv_ref.at[0], ("y",))

    def pieces():
        return backward_pieces(size, q_ref, g_ref, o_ref, lse_ref, own_ref)

    @pl.when(step == 0)
    def _():
        remote(dmo_ref, memory_ref, send_ref.at[1], recv_ref.at[1], ("y",)).start()
        xt_ref[...] = jnp.transpose(x_ref[...])
        turn_ref[...] = jnp.zeros(turn_ref.shape, F32)
        turn_ref[0:8] = sa_ref[...]
        turn_ref[8:16] = sb_ref[...]
        turn_ref[16:17] = sc_ref[...]
        turn_ref[17:21] = sd_ref[...]

    @pl.when(jnp.logical_and(step == 0, second))
    def _():
        xot_ref[...] = jnp.transpose(xo_ref[...])

    @pl.when(jnp.logical_and(step < pairs, second))
    def _():
        keys = jnp.concatenate([ko_ref[...], oth_ref[...]], axis=1)
        values = vo_ref[...]
        dk = dv = 0.0
        dq = [0.0] * count
        for block, mask, qm, gm, q, lse, delta in pieces():
            p, ds = back_piece(keys, values, q, gm, lse, delta, False)
            dk = dk + nn(ds, qm)
            dv = dv + nn(p, gm)
            dq[block] = dq[block] + tn(ds, ko_ref[...] * mask)
        for block in range(count):
            dq_acc[pair, block * size : (block + 1) * size] = dq[block]
        both = jnp.concatenate([dk.astype(BF16), dv.astype(BF16)], axis=1)
        dkv_acc[pair] = both
        dxo = nt(both, jnp.concatenate([wk_ref[...], wv_ref[...]], axis=1))

        @pl.when(step == 0)
        def _():
            dxo_acc[...] = dxo

        @pl.when(step > 0)
        def _():
            dxo_acc[...] += dxo

    @pl.when(jnp.logical_and(step == pairs - 1, second))
    def _():
        dxo_ref[...] = dxo_acc[...].astype(BF16)
        over.start()

    @pl.when(step >= pairs)
    def _():
        dq, dk, dv = [0.0] * count, [0.0] * count, [0.0] * count
        for block, mask, qm, gm, q, lse, delta in pieces():
            for part in range(block + 1):
                of = slice(part * size, (part + 1) * size)
                keys = jnp.concatenate([k_ref[of], own_ref[of]], axis=1)
                p, ds = back_piece(keys, v_ref[of], q, gm, lse, delta, part == block)
                dk[part] = dk[part] + nn(ds, qm)
                dv[part] = dv[part] + nn(p, gm)
                dq[block] = dq[block] + tn(ds, k_ref[of] * mask)
        dq, dk, dv = (jnp.concatenate(a, axis=0) for a in (dq, dk, dv))
        dq = jnp.where(second, dq + dq_acc[pair], dq)
        dqk = jnp.concatenate([dq.astype(BF16), dk.astype(BF16)], axis=1)
        dv = dv.astype(BF16)
        grad_qk = nn(xt_ref[...], dqk)
        grad_v = nn(xt_ref[...], dv)
        shape = grad_ref.shape[:-1] + (PAIR,)
        lead = (slice(None),) * (len(shape) - 1)

        def put(n, grad):
            col = pair // 2 * 6 + 2 * n + pair % 2
            to = pl.ds(pl.multiple_of(col * PAIR, PAIR), PAIR)
            grad_ref[lead + (to,)] = grad.astype(BF16).reshape(shape)

        put(0, grad_qk[:, :PAIR])
        turn_ref[21:22, cols] = total(dqk[:, :PAIR])

        @pl.when(second)
        def _():
            grad_o = nn(xot_ref[...], dkv_acc[pair])
            put(1, grad_qk[:, PAIR:] + grad_o[:, :PAIR])
            put(2, grad_v + grad_o[:, PAIR:])
            turn_ref[22:23, cols] = total(dv) + total(dkv_acc[pair, :, PAIR:])

        @pl.when(jnp.logical_not(second))
        def _():
            put(1, grad_qk[:, PAIR:])
            put(2, grad_v)
            turn_ref[22:23, cols] = total(dv)

        dx = nt(dqk, jnp.concatenate([wq_ref[...], wk_ref[...]], axis=1)) + nt(dv, wv_ref[...])

        @pl.when(step == pairs)
        def _():
            dx_acc[...] = dh1_ref[...] + dx

        @pl.when(step > pairs)
        def _():
            dx_acc[...] += dx

    @pl.when(step == 2 * pairs - 1)
    def _():
        shape = grad_ref.shape[:-1] + (2 * PAIR,)
        lead = (slice(None),) * (len(shape) - 1)
        col = 3 * width
        grad_ref[lead + (slice(col, col + 2 * PAIR),)] = jnp.transpose(turn_ref[...]).astype(BF16).reshape(shape)


def self_backward_finale(*refs):
    dmo_ref, dx_ref, dmi_ref = refs[20:23]
    dx_acc, dxo_ref, came_ref, memory_ref, send_ref, recv_ref = (refs[i] for i in (25, 30, 31, 32, 34, 35))
    remote(dmo_ref, memory_ref, send_ref.at[1], recv_ref.at[1], ("y",)).wait()
    dmi_ref[...] = memory_ref[...]
    over = remote(dxo_ref, came_ref, send_ref.at[0], recv_ref.at[0], ("y",))

    @pl.when(lax.axis_index("sp") == 0)
    def _():
        over.wait_recv()
        dx_ref[...] = (dx_acc[...] + came_ref[...].astype(F32)).astype(BF16)

    @pl.when(lax.axis_index("sp") == 1)
    def _():
        over.wait_send()
        dx_ref[...] = dx_acc[...].astype(BF16)


GRADS = 23


def self_backward(block, qkv, kvo, g, o, lse, own, oth, x, xo, w, dh1, small, dmo, schedule):
    rows, width = x.shape
    pairs = width // PAIR

    def pair_of(offset):
        return pl.BlockSpec((rows, PAIR), lambda s: (0, lax.rem(s, pairs) + offset))

    def weight(offset):
        return pl.BlockSpec((width, PAIR), lambda s: (0, lax.rem(s, pairs) + offset))

    made = block + (3 * width + 2 * PAIR,)
    outs = [jax.ShapeDtypeStruct((rows, width), BF16)] * 2
    specs = [whole((rows, width))] * 2
    held = []
    if schedule:
        held += [pltpu.VMEM(made, BF16)]
    else:
        outs += [jax.ShapeDtypeStruct(made, BF16)]
        specs += [whole(made)]
    held += [
        pltpu.VMEM((pairs, rows, PAIR), F32),
        pltpu.VMEM((rows, width), F32),
        pltpu.VMEM((rows, width), F32),
        pltpu.VMEM((pairs, rows, 2 * PAIR), BF16),
        pltpu.VMEM((width, rows), BF16),
        pltpu.VMEM((width, rows), BF16),
        pltpu.VMEM((rows, width), BF16),
        pltpu.VMEM((rows, width), BF16),
        pltpu.VMEM((rows, width), BF16),
        pltpu.VMEM((2 * PAIR, width), F32),
        pltpu.SemaphoreType.DMA((2,)),
        pltpu.SemaphoreType.DMA((2,)),
    ]
    return run(
        functools.partial(self_backward_kernel, 256), "self_backward", 2 * pairs,
        (qkv, qkv, qkv, kvo, kvo, g, o, lse, own, oth, x, xo, w, w, w, dh1) + tuple(small) + (dmo,),
        [
            pair_of(0),
            pair_of(pairs),
            pair_of(2 * pairs),
            pair_of(0),
            pair_of(pairs),
            pair_of(0),
            pair_of(0),
            pl.BlockSpec((8, rows), lambda s: (lax.rem(s, pairs), 0)),
            whole((rows, 128)),
            whole((rows, 128)),
            whole((rows, width)),
            whole((rows, width)),
            weight(0),
            weight(pairs),
            weight(2 * pairs),
            whole((rows, width)),
        ] + [whole(a.shape) for a in small] + [pl.BlockSpec(memory_space=pl.ANY)],
        outs, specs, held, schedule, 5,
        48 * rows * rows * width + 20 * rows * width * width, 12 * width * width + 40 * rows * width,
        (("y",),), self_backward_finale,
    )


def first_norm_kernel(x_ref, ctx_ref, wo_ref, wq_ref, b_ref, h_ref, cq_ref):
    h = x_ref[...].astype(F32) + nn(ctx_ref[...], wo_ref[...]) + b_ref[3:4]
    h_ref[...] = h
    n, _ = normed(h)
    a = (n * b_ref[4:5] + b_ref[5:6]).astype(BF16)
    cq_ref[...] = (nn(a, wq_ref[...]) + b_ref[6:7]).astype(BF16)


def first_norm(x, ctx, wo, wq, biases):
    rows, width = x.shape
    return pl.pallas_call(
        first_norm_kernel,
        out_shape=[
            jax.ShapeDtypeStruct((rows, width), F32),
            jax.ShapeDtypeStruct((rows, width), BF16),
        ],
        compiler_params=params(),
        cost_estimate=cost(4 * rows * width * width, 4 * width * width + 10 * rows * width),
        name="first_norm",
    )(x, ctx, wo, wq, biases)


def feed_kernel(
    count, comm, h1_ref, cc_ref, ct_ref, wco_ref, b_ref, wi_ref, wo_ref,
    out_ref, dh2_ref, dcc_ref, gco_ref, *refs,
):
    if comm:
        gwi_ref, refs = refs[0], refs[1:]
    else:
        gwi_ref, gwo_ref, refs = refs[0], refs[1], refs[2:]
    small_ref, gib_ref, hid_ref, slope_ref, n2_ref, r2_ref, a2b_ref, acc_ref, df_ref, *refs = refs
    step = pl.program_id(0)
    width = acc_ref.shape[1]

    if comm:
        mi_ref, mo_ref, ci_ref, co_ref, send_ref, recv_ref = refs
        wide = ci_ref.shape[-1]
        here = place()
        c = here[1]

        def chunk_copies(j):
            at = pl.ds(pl.multiple_of(j * width, width), width)
            return [
                remote(mi_ref.at[:, :, at], ci_ref.at[:, :, at], send_ref.at[0, j], recv_ref.at[0, j], ("core",), here),
                remote(mo_ref.at[j], co_ref.at[j], send_ref.at[1, j], recv_ref.at[1, j], ("core",), here),
            ]

    @pl.when(step == 0)
    def _():
        if comm:
            greet([("core",)])
        n1, _ = normed(h1_ref[...])
        a1 = n1 * b_ref[4:5] + b_ref[5:6]
        h2 = a1 + nn(cc_ref[...], wco_ref[...]) + b_ref[7:8]
        n2, r2 = normed(h2)
        n2_ref[...] = n2
        r2_ref[...] = jnp.broadcast_to(r2, r2_ref.shape)
        a2 = n2 * b_ref[8:9] + b_ref[9:10]
        a2b_ref[...] = a2.astype(BF16)
        acc_ref[...] = a2 + b_ref[10:11]

    @pl.when(step < count)
    def _():
        u = nn(a2b_ref[...], wi_ref[...]) + b_ref[pl.ds(13 + step, 1)]
        cumul = 0.5 * (1.0 + lax.erf(u * 0.7071067811865476))
        density = jnp.exp(-0.5 * u * u) * 0.3989422804014327
        hid = (u * cumul).astype(BF16)
        hid_ref[step] = hid
        slope_ref[step] = cumul + u * density
        acc_ref[...] += nn(hid, wo_ref[...])

    @pl.when(step == count - 1)
    def _():
        n3, r3 = normed(acc_ref[...])
        gain = b_ref[11:12]
        out_ref[...] = (n3 * gain + b_ref[12:13]).astype(BF16)
        e = ct_ref[...].astype(F32)
        d3 = norm_back(e, n3, r3, gain)
        df = d3.astype(BF16)
        df_ref[...] = df
        acc_ref[...] = d3
        small_ref[0:1] = total(e * n3)
        small_ref[1:2] = total(e)
        small_ref[2:3] = total(df)

    @pl.when(jnp.logical_and(step >= count, step < 2 * count))
    def _():
        j = step - count
        df = df_ref[...]
        du = (nt(df, wo_ref[...]) * slope_ref[j]).astype(BF16)
        gib_ref[...] = total(du)
        acc_ref[...] += nt(du, wi_ref[...])
        go = tn(hid_ref[j], df).astype(BF16)
        gi = tn(a2b_ref[...], du).astype(BF16)
        if comm:
            at = pl.ds(pl.multiple_of(j * width, width), width)
            eight, narrow = gwi_ref.shape[:2]
            gi = gi.reshape(eight, 2, narrow, width)
            go = go.reshape(2, 2, 4, narrow, width)
            gwi_ref[:, :, at] = jnp.where(c == 0, gi[:, 0], gi[:, 1])
            mi_ref[:, :, at] = jnp.where(c == 0, gi[:, 1], gi[:, 0])
            mo_ref[j] = jnp.where(c == 0, go[:, 1], go[:, 0])
            for i in range(4):
                gwi_ref[pl.ds(2 * j, 2), :, pl.ds(wide + i * width, width)] = jnp.where(c == 0, go[:, 0, i], go[:, 1, i])
            for copy in chunk_copies(j):
                copy.start()
        else:
            gwo_ref[...] = go
            gwi_ref[...] = gi

    @pl.when(step == 2 * count)
    def _():
        d2 = acc_ref[...]
        n2 = n2_ref[...]
        dh2 = norm_back(d2, n2, r2_ref[:, :1], b_ref[8:9])
        dh2_ref[...] = dh2
        dco = dh2.astype(BF16)
        dcc_ref[...] = nt(dco, wco_ref[...]).astype(BF16)
        gco_ref[...] = tn(cc_ref[...], dco).astype(BF16)
        small_ref[3:4] = total(d2 * n2)
        small_ref[4:5] = total(d2)
        small_ref[5:6] = total(dco)
        small_ref[6:8] = jnp.zeros((2, d2.shape[1]), F32)

    if comm:

        @pl.when(step > count)
        def _():
            j = step - count - 1
            at = pl.ds(pl.multiple_of(j * width, width), width)
            for copy in chunk_copies(j):
                copy.wait()
            gwi_ref[:, :, at] += ci_ref[:, :, at]
            for i in range(4):
                gwi_ref[pl.ds(2 * j, 2), :, pl.ds(wide + i * width, width)] += co_ref[j, :, i]


def feed(size, comm, h1, cc, ct, wco, biases, wi, wo):
    rows, width = h1.shape
    wide = wi.shape[1]
    chunk = width
    count = wide // chunk

    def weight(s):
        return jnp.where(s < count, s, jnp.minimum(s - count, count - 1))

    def early(s):
        return jnp.clip(s - count, 0, count - 1)

    flat = whole((rows, width))
    square = whole((width, width))
    scratch = [
        pltpu.VMEM((count, rows, chunk), BF16),
        pltpu.VMEM((count, rows, chunk), F32),
        pltpu.VMEM((rows, width), F32),
        pltpu.VMEM((rows, 128), F32),
        pltpu.VMEM((rows, width), BF16),
        pltpu.VMEM((rows, width), F32),
        pltpu.VMEM((rows, width), BF16),
    ]
    if comm:
        narrow = width // size
        grad_specs = [whole((size // 2, narrow, 2 * wide))]
        grad_shapes = [(size // 2, narrow, 2 * wide)]
        scratch += [
            pltpu.VMEM((size // 2, narrow, wide), BF16),
            pltpu.VMEM((count, 2, 4, narrow, width), BF16),
            pltpu.VMEM((size // 2, narrow, wide), BF16),
            pltpu.VMEM((count, 2, 4, narrow, width), BF16),
            pltpu.SemaphoreType.DMA((2, count)),
            pltpu.SemaphoreType.DMA((2, count)),
        ]
    else:
        grad_specs = [
            pl.BlockSpec((width, chunk), lambda s: (0, early(s))),
            pl.BlockSpec((chunk, width), lambda s: (early(s), 0)),
        ]
        grad_shapes = [(width, wide), (wide, width)]
    return pl.pallas_call(
        functools.partial(feed_kernel, count, comm),
        grid=(2 * count + 1,),
        in_specs=[
            flat, flat, flat, square, whole(biases.shape),
            pl.BlockSpec((width, chunk), lambda s: (0, weight(s))),
            pl.BlockSpec((chunk, width), lambda s: (weight(s), 0)),
        ],
        out_specs=[flat, flat, flat, square]
        + grad_specs
        + [whole((8, width)), pl.BlockSpec((1, chunk), lambda s: (0, early(s)))],
        out_shape=[
            jax.ShapeDtypeStruct((rows, width), BF16),
            jax.ShapeDtypeStruct((rows, width), F32),
            jax.ShapeDtypeStruct((rows, width), BF16),
            jax.ShapeDtypeStruct((width, width), BF16),
        ]
        + [jax.ShapeDtypeStruct(a, BF16) for a in grad_shapes]
        + [
            jax.ShapeDtypeStruct((8, width), F32),
            jax.ShapeDtypeStruct((1, wide), F32),
        ],
        scratch_shapes=scratch,
        compiler_params=params(2 if comm else None),
        cost_estimate=cost(
            12 * rows * width * wide + 6 * rows * width * width, 12 * width * wide + 16 * rows * width
        ),
        name="feed",
    )(h1, cc, ct, wco, biases, wi, wo)


def outputs_kernel(moves, count, line, *refs):
    pieces, rest = refs[:count], refs[count:]
    out_ref, dx_ref, dm_ref, dmi_ref = rest[:4]
    outs = rest[4:]
    for piece, first, wide, which, row, col in moves:
        ref = pieces[piece]
        outs[which][row : row + ref.shape[0], col : col + wide] = ref[:, first : first + wide].astype(F32)
    turned, result, dx, dm = outs[-4:]
    turned[...] = jnp.transpose(pieces[line[0]][:, line[1] : line[1] + PAIR].astype(F32))
    result[...] = out_ref[...]
    dx[...] = dx_ref[...]
    dm[...] = (dm_ref[...] + dmi_ref[...].astype(F32)).astype(BF16)


def outputs(pieces, moves, line, shapes, out, dx, dm, dmi):
    ins = tuple(pieces) + (out, dx, dm, dmi)
    result = jax.ShapeDtypeStruct(out.shape, BF16)
    return pl.pallas_call(
        functools.partial(outputs_kernel, moves, len(pieces), line),
        out_shape=[jax.ShapeDtypeStruct(a, F32) for a in shapes]
        + [jax.ShapeDtypeStruct((PAIR, pieces[0].shape[0]), F32), result, result, result],
        compiler_params=params(),
        cost_estimate=cost(0, 12 << 20),
        name="outputs",
    )(*ins)


def moved(pieces, targets):
    out = []
    for n, (start, wide) in enumerate(pieces):
        for first, cols, which, row, col in targets:
            low, high = max(start, first), min(start + wide, first + cols)
            if low < high:
                out.append((n, low - start, high - low, which, row, col + low - first))
    return out


def schedule_of(flows, kernel):
    entries = [
        (start, order, name, start, stop)
        for order, name in enumerate(flows)
        for start, stop in PLAN[name][kernel]
    ]
    return tuple(([flows[name]], start, stop) for _, _, name, start, stop in sorted(entries))


def swap_sum(part, axis, pairs):
    came = lax.ppermute(part, axis, pairs)
    return part.astype(F32) + came.astype(F32)


def sum_scatter(grad, size, order):
    rows, cols = grad.shape
    bits = size.bit_length() - 1
    me = lax.axis_index("dp")
    now = grad.reshape((2,) * bits + (rows // size, cols))
    left = list(range(bits))[::-1]
    for bit in [b for b in order if b < bits] + [b for b in range(bits) if b not in order]:
        axis = left.index(bit)
        mine = (me >> bit) & 1
        keep = lax.dynamic_index_in_dim(now, mine, axis, keepdims=False)
        send = lax.dynamic_index_in_dim(now, 1 - mine, axis, keepdims=False)
        came = lax.ppermute(send, "dp", [(i, i ^ (1 << bit)) for i in range(size)])
        now = (keep.astype(F32) + came.astype(F32)).astype(BF16)
        left.pop(axis)
    return swap_sum(now, "sp", [(0, 1), (1, 0)])


def per_device(
    size,
    inputs,
    memory,
    target_docs,
    memory_docs,
    cotangent,
    w_qkv,
    b_q,
    b_v,
    w_so,
    b_so,
    g_one,
    s_one,
    w_cq,
    b_cq,
    w_ckv,
    b_cv,
    w_co,
    b_co,
    g_two,
    s_two,
    w_fi,
    b_fi,
    w_fo,
    b_fo,
    g_three,
    s_three,
):
    rows, width = inputs.shape[1:]
    wide = b_fi.shape[0]
    comm = size == 16
    narrow, broad = width // size, wide // size
    swap = [(0, 1), (1, 0)]
    x, mem, ct = inputs[0], memory[0], cotangent[0]
    x_o = lax.ppermute(x, "sp", [(0, 1)])
    docs_o = lax.ppermute(jnp.concatenate([target_docs, memory_docs], axis=0), "sp", swap)
    line = lax.broadcasted_iota(jnp.int32, (24, width), 0)
    vectors = (b_q, b_v, b_cv, b_so, g_one, s_one, b_cq, b_co, g_two, s_two, b_fo, g_three, s_three)
    vectors += tuple(b_fi[i : i + width] for i in range(0, wide, width))
    biases = jnp.zeros((24, width), F32)
    for i, v in enumerate(vectors):
        biases = jnp.where(line == i, v.astype(F32)[None], biases)

    qkv, mkv, t_own, m_own = project_own(x, mem, target_docs, memory_docs, w_qkv, w_ckv, biases)
    kvo, mem_s, t_oth, m_oth = project_other(x_o, mem, docs_o[:1], docs_o[1:], w_qkv, biases, t_own)
    mem_o = lax.ppermute(mem_s, "sp", swap)
    ctx, lse = self_forward(qkv, kvo, t_own, t_oth)
    h1, cq = first_norm(x, ctx, w_so, w_cq, biases)
    mkvo = project_memory(mem_o, w_ckv, biases)
    cc, clse = cross_forward(cq, mkv, mkvo, t_own, m_own, m_oth)
    output, dh2, dcc, gco, gwi, *gwo, small_a, gib = feed(size, comm, h1, cc, ct, w_co, biases, w_fi, w_fo)
    turned = gib.reshape(width, -1).T

    block = (2, 2, 2, 2, narrow) if comm else (width,)
    at_cross, at_self, flows = (), (), {}
    if comm:
        late_shape = block + (2 * width,)
        sources = {
            "T0": (gwi.reshape(block[:3] + gwi.shape[1:]), block[:3] + gwi.shape[1:], BLOCK[:3]),
            "T1a": (("ref", MIDDLE), block + (3 * width,), BLOCK),
            "T1b": (None, late_shape, BLOCK),
            "G": (("ref", GRADS), block + (3 * width + 2 * PAIR,), BLOCK),
        }
        for name, (source, cols, hops, _, _) in PLAN.items():
            array, shape, dims = sources[source]
            flows[name] = Flow(array, shape, hops, dims, cols)
        at_cross = schedule_of(flows, 3)
        at_self = schedule_of(flows, 4)
    dm, dmo, gcvb, dh1, dsc, late, small_b, *early = cross_backward(
        block, cq, mkv, mkvo, dcc, cc, clse, t_own, m_own, m_oth, mem, mem_o, w_ckv,
        gco, dh2, h1, ctx, w_cq, w_so, biases, at_cross,
    )
    for name, flow in flows.items():
        if PLAN[name][0] == "T1b":
            flow.array = late
    dx, dm_in, *made = self_backward(
        block, qkv, kvo, dsc, ctx, lse, t_own, t_oth, x, x_o, w_qkv, dh1, (small_a, small_b, gcvb, turned), dmo, at_self
    )
    if comm:
        targets = {
            "T0": [(0, wide, 2, 0, 0)] + [(wide + i * width, width, 3, i * narrow, 0) for i in range(4)],
            "T1a": [(0, width, 4, 0, 0), (width, 2 * width, 1, 0, 0)],
            "T1b": [(0, width, 5, 0, 0), (width, width, 6, 0, 0)],
            "G": [
                (g * 6 * PAIR + i * 2 * PAIR, 2 * PAIR, 0, 0, i * width + g * 2 * PAIR)
                for g in range(width // PAIR // 2)
                for i in range(3)
            ],
        }
        moves, line = [], None
        for n, (source, cols, *_) in enumerate(PLAN.values()):
            moves += [(n,) + m[1:] for m in moved([cols], targets[source])]
            if source == "G" and cols[0] <= 3 * width < sum(cols):
                line = n, 3 * width - cols[0]
        shapes = [(narrow, 3 * width), (narrow, 2 * width), (narrow, wide), (broad, width)] + [(narrow, width)] * 3
        t_qkv, t_cmem, t_fin, t_fout, t_cout, t_cquery, t_out, lines, output, derivative, grad_memory = outputs(
            [f.array for f in flows.values()], moves, line, shapes, output, dx, dm, dm_in
        )
    else:
        (early,), (made,) = early, made
        columns = made[:, 3 * width : 3 * width + PAIR]
        groups = range(width // PAIR // 2)
        gqkv = jnp.concatenate(
            [made[:, (g * 6 + 2 * i) * PAIR : (g * 6 + 2 * i + 2) * PAIR] for i in range(3) for g in groups], axis=1
        )
        t_fin, t_fout, t_cout, t_cquery, t_out, t_cmem, t_qkv, lines = (
            sum_scatter(g, size, (0, 1, 2, 3))
            for g in (
                gwi, gwo[0], early[:, :width], late[:, :width], late[:, width:], early[:, width:], gqkv, columns
            )
        )
        lines, derivative = lines.T, dx
        grad_memory = (dm + dm_in.astype(F32)).astype(BF16)
    t_gthree, t_sthree, t_fobias, t_gtwo, t_stwo, t_cobias = (lines[i] for i in range(6))
    t_cqbias, t_gone, t_sone, t_obias = (lines[i] for i in range(8, 12))
    t_cvbias, t_qbias, t_vbias = lines[16], lines[21], lines[22]
    t_fibias = lines[17:21].T.reshape(-1)
    return (
        output[None],
        derivative[None],
        grad_memory[None],
        t_qkv,
        t_qbias,
        t_vbias,
        t_out,
        t_obias,
        t_gone,
        t_sone,
        t_cquery,
        t_cqbias,
        t_cmem,
        t_cvbias,
        t_cout,
        t_cobias,
        t_gtwo,
        t_stwo,
        t_fin,
        t_fibias,
        t_fout,
        t_fobias,
        t_gthree,
        t_sthree,
    )


def solution(mesh):
    split = P("dp", "sp", None)
    in_specs = (split, split, P("dp", "sp"), P("dp", "sp"), split) + (P(),) * 21
    matrix, vector = P("dp", None), P("dp")
    out_specs = (
        split, split, split,
        matrix, vector, vector,
        matrix, vector, vector, vector,
        matrix, vector,
        matrix, vector,
        matrix, vector, vector, vector,
        matrix, vector,
        matrix, vector, vector, vector,
    )
    return jax.shard_map(
        functools.partial(per_device, mesh.shape["dp"]),
        mesh=mesh, in_specs=in_specs, out_specs=out_specs, check_vma=False,
    )
```

```python
import functools

import jax
import jax.numpy as jnp
from jax import lax
from jax.experimental import pallas as pl
from jax.experimental.pallas import tpu as pltpu
from jax.sharding import PartitionSpec as P

HD = 64
PAIR = 2 * HD
EPS = 1e-05
FAR = 1.0e9
VMEM = 60 * 1024 * 1024
F32 = jnp.float32
BF16 = jnp.bfloat16


def nn(a, b):
    return lax.dot_general(a, b, (((1,), (0,)), ((), ())), preferred_element_type=F32)


def nt(a, b):
    return lax.dot_general(a, b, (((1,), (1,)), ((), ())), preferred_element_type=F32)


def tn(a, b):
    return lax.dot_general(a, b, (((0,), (0,)), ((), ())), preferred_element_type=F32)


def params(collective=None):
    if collective is None:
        return pltpu.CompilerParams(vmem_limit_bytes=VMEM)
    return pltpu.CompilerParams(
        vmem_limit_bytes=VMEM, collective_id=collective, has_side_effects=True
    )


def cost(flops, moved):
    return pl.CostEstimate(flops=int(flops), bytes_accessed=int(moved), transcendentals=0)


def normed(h):
    centred = h - jnp.mean(h, axis=-1, keepdims=True)
    rstd = lax.rsqrt(jnp.mean(centred * centred, axis=-1, keepdims=True) + EPS)
    return centred * rstd, rstd


def norm_back(grad, n, rstd, gain):
    scaled = grad * gain
    centre = jnp.mean(scaled, axis=-1, keepdims=True)
    along = jnp.mean(scaled * n, axis=-1, keepdims=True)
    return rstd * (scaled - centre - n * along)


def total(a):
    return jnp.sum(a.astype(F32), axis=0, keepdims=True)


def place():
    me = lax.axis_index("dp")
    return me, me % 2, (me // 2) % 2, me // 4, lax.axis_index("sp")


def flipped(at, hops):
    me, c, x, z, sp = at
    for hop in hops:
        if hop == "core":
            me, c = me + 1 - 2 * c, 1 - c
        elif hop == "x":
            me, x = me + 2 - 4 * x, 1 - x
        elif hop == "z1":
            me, z = me + 4 - 8 * (z % 2), z + 1 - 2 * (z % 2)
        elif hop == "z2":
            me, z = me + 8 - 16 * (z // 2), z + 2 - 4 * (z // 2)
        else:
            sp = 1 - sp
    return me, c, x, z, sp


def partner(hops, at=None):
    there = flipped(at or place(), hops)
    return {"dp": there[0], "sp": there[4]}


def greet(groups, at=None):
    groups = sorted({tuple("y" if h[0] == "y" else h for h in hops) for hops in groups})
    barrier = pltpu.get_barrier_semaphore()
    for hops in groups:
        pl.semaphore_signal(barrier, inc=1, device_id=partner(hops, at), device_id_type=pl.DeviceIdType.MESH)
    pl.semaphore_wait(barrier, len(groups))


def remote(src, dst, send, recv, hops, at=None):
    return pltpu.make_async_remote_copy(
        src_ref=src, dst_ref=dst, send_sem=send, recv_sem=recv,
        device_id=partner(hops, at), device_id_type=pl.DeviceIdType.MESH,
    )


PLAN = {
    "T00": ("T0", (0, 2304), ("x", "yr", "z1", "z2", "yg"), ((0, 5), (5, 7)), ((0, 6), (6, 8), (8, 11))),
    "T01": ("T0", (2304, 1280), ("z1", "x", "z2", "y"), ((0, 3), (3, 6), (6, 7)), ((0, 3),)),
    "T02": ("T0", (3584, 2560), ("yr", "x", "z1", "z2", "yg"), ((0, 5), (5, 7)), ((0, 7), (7, 9), (9, 12))),
    "T1a0": ("T1a", (0, 1280), ("core", "x", "yr", "z1", "z2", "yg"), ((6, 7),), ((0, 5), (5, 10), (10, 12), (12, 18), (18, 22))),
    "T1a1": ("T1a", (1280, 1024), ("core", "z1", "x", "z2", "y"), ((6, 7),), ((0, 8), (8, 10), (10, 12), (12, 17))),
    "T1b0": ("T1b", (0, 1536), ("core", "x", "z1", "yr", "z2", "yg"), (), ((0, 3), (3, 8), (8, 10), (10, 13), (13, 20), (20, 25))),
    "G10": ("G", (0, 768), ("core", "x", "z1", "z2", "y"), (), ((8, 9), (9, 11), (11, 13), (13, 20), (20, 25))),
    "G20": ("G", (768, 256), ("core", "x", "z1", "z2", "y"), (), ((10, 11), (11, 12), (12, 15), (15, 19), (19, 24))),
    "G21": ("G", (1024, 512), ("core", "x", "yr", "z1", "z2", "yg"), (), ((10, 12), (12, 17), (17, 23), (23, 26), (26, 28), (28, 30))),
    "G30": ("G", (1536, 640), ("core", "x", "z1", ("z2", "y")), (), ((12, 16), (16, 21), (21, 27), (27, 32))),
    "G31": ("G", (2176, 384), ("core", "z1", "x", "z2", "y"), (), ((12, 14), (14, 24), (24, 25), (25, 29), (29, 31))),
}
BLOCK = ("z2", "z1", "x", "core")


class Part:
    def __init__(self, hop, shape, dims, cols=None):
        self.hops = hops = hop if isinstance(hop, tuple) else (hop,)
        self.groups = [(h,) for h in hops] + ([hops] if len(hops) > 1 else [])
        self.dims = dims
        self.cols = cols or (0, shape[-1])
        self.shape = shape = tuple(shape[:-1]) + (self.cols[1],)
        for h in hops:
            if h in dims:
                at = dims.index(h)
                shape, dims = shape[:at] + shape[at + 1 :], dims[:at] + dims[at + 1 :]
            elif h != "y":
                shape = shape[:-1] + (shape[-1] // 2 if h == "yr" else 2 * shape[-1],)
        self.after, self.left = shape, dims
        self.came = self.shape if hops == ("yg",) else shape

    def share(self, at):
        _, c, x, z, sp = at
        first, wide = self.cols
        index = [slice(None)] * (len(self.shape) - 1) + [pl.ds(first, wide)]
        for h in self.hops:
            if h in self.dims:
                index[self.dims.index(h)] = {"core": c, "x": x, "z1": z % 2, "z2": z // 2}[h]
            elif h == "yr":
                half = wide // 2
                index[-1] = pl.ds(pl.multiple_of(first + sp * half, 128), half)
        return tuple(index)

    def copies(self, src, held, made, came, send, recv, local, at):
        out = [
            remote(src.at[self.share(flipped(at, g))], came[i], send.at[i], recv.at[i], g, at)
            for i, g in enumerate(self.groups)
        ]
        if not held:
            out.append(pltpu.make_async_copy(src.at[self.share(at)], made, local))
        return out

    def add(self, src, held, made, came, at):
        if self.hops == ("yg",):
            wide, sp = self.shape[-1], at[4]
            lead = (slice(None),) * (len(self.shape) - 1)
            made[lead + (pl.ds(pl.multiple_of(sp * wide, 128), wide),)] = src[self.share(at)]
            made[lead + (pl.ds(pl.multiple_of((1 - sp) * wide, 128), wide),)] = came[0][...]
        elif len(came) > 1:
            mine = src[self.share(at)] if held else made[...]
            one, two, three = (c[...].astype(F32) for c in came)
            made[...] = ((mine.astype(F32) + one) + (two + three)).astype(BF16)
        elif held:
            made[...] = src[self.share(at)] + came[0][...]
        else:
            made[...] += came[0][...]


class Flow:
    def __init__(self, array, shape, hops, dims=BLOCK, cols=None):
        self.array, self.shape, self.dims, self.cols = array, tuple(shape), dims, cols
        self.hops = list(hops)

    def step(self):
        part = Part(self.hops.pop(0), self.shape, self.dims, self.cols)
        self.shape, self.dims, self.cols = part.after, part.left, None
        return part


class Window:
    def __init__(self, start, stop, joint):
        self.start, self.stop, self.joint = start, stop, joint
        self.parts, self.sources, self.keeps = [], [], []


class Joint:
    def __init__(self):
        self.window = None


def plan(schedule):
    windows, arrays, latest = [], [], {}
    for n, (flows, start, stop, *joint) in enumerate(schedule):
        window = Window(start, stop, bool(joint))
        if joint:
            joint[0].window = n
        for i, flow in enumerate(flows):
            if flow in latest:
                source = ("part",) + latest[flow]
                before = windows[latest[flow][0]]
                before.keeps[latest[flow][1]] = False
            elif isinstance(flow.array, Joint):
                source = ("joint", flow.array.window)
            elif isinstance(flow.array, tuple):
                source = flow.array
            else:
                known = [k for k, a in enumerate(arrays) if a is flow.array]
                if not known:
                    arrays.append(flow.array)
                source = ("in", known[0] if known else len(arrays) - 1)
            window.parts.append(flow.step())
            window.sources.append(source)
            window.keeps.append(not joint)
            if not joint:
                latest[flow] = (n, i)
        windows.append(window)
    return windows, arrays, latest


def carrying(body, own, windows, arrays, grid, also, finale):
    ins, outs, held = own

    def kernel(*refs):
        refs = list(refs)

        def take(n):
            got = refs[:n]
            del refs[:n]
            return got

        my_in, arr = take(ins), take(arrays)
        my_out = take(outs)
        given = [[take(1)[0] if k else None for k in w.keeps] for w in windows]
        my_held = take(held)
        made, came, joints = [], [], []
        for w, g in zip(windows, given):
            if w.joint:
                joint, col, views = take(1)[0], 0, []
                for q in w.parts:
                    views.append(joint.at[(slice(None),) * (len(q.after) - 1) + (pl.ds(col, q.after[-1]),)])
                    col += q.after[-1]
                joints.append(joint)
                made.append(views)
            else:
                joints.append(None)
                made.append([ref if ref is not None else take(1)[0] for ref in g])
            came.append([take(len(q.groups)) for q in w.parts])
        mine = my_in + my_out + my_held
        step = pl.program_id(0)
        groups = [g for w in windows for q in w.parts for g in q.groups] + list(also)
        if groups:
            here = place()
            pl.when(step == 0)(lambda: greet(groups, here))
        if windows:
            send, recv, local = refs
        copies, sources, base = [], [], 0
        for w, m, c in zip(windows, made, came):
            now, froms = [], []
            for i, q in enumerate(w.parts):
                kind = w.sources[i]
                if kind[0] == "in":
                    src = arr[kind[1]]
                elif kind[0] == "ref":
                    src = mine[kind[1]]
                elif kind[0] == "joint":
                    src = joints[kind[1]]
                else:
                    src = made[kind[1]][kind[2]]
                held_here = kind[0] != "in"
                froms.append((src, held_here))
                now += q.copies(
                    src, held_here, m[i], c[i], send.at[base], recv.at[base], local.at[base], here
                )
                base += 1
            copies.append(now)
            sources.append(froms)

        def phase(number):
            for n, w in enumerate(windows):
                if w.stop == number:
                    for copy in copies[n]:
                        copy.wait()
                    for q, (src, held_here), m, c in zip(w.parts, sources[n], made[n], came[n]):
                        q.add(src, held_here, m, c, here)
            for n, w in enumerate(windows):
                if w.start == number:
                    for copy in copies[n]:
                        copy.start()

        used = sorted({w.start for w in windows} | {w.stop for w in windows})
        for number in used:
            if number < grid:
                pl.when(step == number)(functools.partial(phase, number))
        body(*mine)
        for number in used:
            if number >= grid:
                pl.when(step == grid - 1)(functools.partial(phase, number))
        if finale:
            pl.when(step == grid - 1)(lambda: finale(*mine))

    return kernel


def run(
    body, name, grid, ins, in_specs, outs, out_specs, held=(), schedule=(), collective=None,
    flops=0, moved=0, also=(), finale=None,
):
    in_specs, outs, out_specs, held = list(in_specs), list(outs), list(out_specs), list(held)
    windows, arrays, latest = plan(schedule)
    own = len(outs)
    kernel = carrying(body, (len(ins), own, len(held)), windows, len(arrays), grid, also, finale)
    in_specs += [pl.BlockSpec(memory_space=pl.ANY)] * len(arrays)
    order, count = [], 0
    for n, w in enumerate(windows):
        if w.joint:
            shape = w.parts[0].after[:-1] + (sum(q.after[-1] for q in w.parts),)
            held.append(pltpu.VMEM(shape, BF16))
        for i, (q, k) in enumerate(zip(w.parts, w.keeps)):
            if w.joint:
                continue
            if k:
                outs.append(jax.ShapeDtypeStruct(q.after, BF16))
                out_specs.append(whole(q.after))
                order.append((n, i))
            else:
                held.append(pltpu.VMEM(q.after, BF16))
        held += [pltpu.VMEM(q.came, BF16) for q in w.parts for _ in q.groups]
        count += len(w.parts)
    if windows:
        held += [pltpu.SemaphoreType.DMA((count, 3))] * 2 + [pltpu.SemaphoreType.DMA((count,))]
    results = pl.pallas_call(
        kernel,
        grid=(grid,),
        in_specs=in_specs,
        out_specs=out_specs,
        out_shape=outs,
        scratch_shapes=held,
        compiler_params=params(collective if windows or also else None),
        cost_estimate=cost(flops, moved),
        name=name,
    )(*ins, *arrays)
    for flow, where in latest.items():
        flow.array = results[own + order.index(where)]
    return results[:own]


def head_masks(dtype):
    lane = lax.broadcasted_iota(jnp.int32, (1, PAIR), 1)
    low = jnp.where(lane < HD, 1.0, 0.0)
    return low.astype(dtype), (1.0 - low).astype(dtype)


def query_code(code):
    lane = lax.broadcasted_iota(jnp.int32, code.shape, 1)
    return jnp.where(lane < 4, (code.astype(F32) - 1.0) * FAR, 0.0).astype(BF16)


def softmax_pieces(scores, values):
    peak = functools.reduce(jnp.maximum, [jnp.max(s, axis=-1, keepdims=True) for s in scores])
    expd = [jnp.exp(s - peak) for s in scores]
    norm = sum(jnp.sum(e, axis=-1, keepdims=True) for e in expd)
    out = sum(nn(e.astype(BF16), v) for e, v in zip(expd, values))
    return out / norm, peak + jnp.log(norm)


def pair_spec(rows, offset):
    return pl.BlockSpec((rows, PAIR), lambda p: (0, p + offset))


def whole(shape):
    return pl.BlockSpec(shape, lambda *_: (0,) * len(shape))


def delta_rows(g, o):
    prod = g.astype(F32) * o.astype(F32)
    upper = prod.astype(BF16)
    lower = (prod - upper.astype(F32)).astype(BF16)
    row = lax.broadcasted_iota(jnp.int32, (8, PAIR), 0)
    lane = lax.broadcasted_iota(jnp.int32, (8, PAIR), 1)
    pick = jnp.where(row == lane // HD, 1.0, 0.0).astype(BF16)
    return nt(pick, upper) + nt(pick, lower)


def back_piece(keys, values, q, g, lse, delta, causal):
    s = nt(keys, q)
    if causal:
        row = lax.broadcasted_iota(jnp.int32, s.shape, 0)
        col = lax.broadcasted_iota(jnp.int32, s.shape, 1)
        s = jnp.where(row <= col, s, -FAR)
    p = jnp.exp(s - lse)
    ds = p * (nt(values, g) - delta)
    return p.astype(BF16), ds.astype(BF16)


def cross_backward_kernel(
    size, pairs, q_ref, k_ref, v_ref, ko_ref, vo_ref, g_ref, o_ref, lse_ref, t_ref, own_ref, oth_ref,
    m_ref, mo_ref, wk_ref, wv_ref, gco_ref, dh2_ref, h1_ref, ctx_ref, wcq_ref, wso_ref, g1_ref, s1_ref,
    dm_ref, dmo_ref, gb_ref, dh1_ref, dsc_ref, late_ref, small_ref, grad_ref,
    dmo_acc, mt_ref, mot_ref, dcq_ref,
):
    step = pl.program_id(0)
    rows, width = m_ref.shape
    lead = (slice(None),) * (len(grad_ref.shape) - 1)

    def put(ref, col, grad):
        to = pl.ds(pl.multiple_of(col, PAIR), grad.shape[1])
        ref[lead + (to,)] = grad.astype(BF16).reshape(ref.shape[:-1] + (grad.shape[1],))

    @pl.when(step == 0)
    def _():
        mt_ref[...] = jnp.transpose(m_ref[...])
        mot_ref[...] = jnp.transpose(mo_ref[...])
        put(grad_ref, 0, gco_ref[...])

    @pl.when(step < pairs)
    def _():
        count = rows // size
        halves = [(k_ref, v_ref, own_ref, mt_ref, dm_ref), (ko_ref, vo_ref, oth_ref, mot_ref, dmo_acc)]
        cols = pl.ds(pl.multiple_of(step * PAIR, PAIR), PAIR)
        dq = [0.0] * count
        gk = gv = gb = 0.0
        for kr, vr, code, mem, acc in halves:
            keys = jnp.concatenate([kr[...], code[...]], axis=1)
            values = vr[...]
            dk = dv = 0.0
            for block, mask, qm, gm, q, lse, delta in backward_pieces(size, q_ref, g_ref, o_ref, lse_ref, t_ref):
                p, ds = back_piece(keys, values, q, gm, lse, delta, False)
                dk = dk + nn(ds, qm)
                dv = dv + nn(p, gm)
                dq[block] = dq[block] + tn(ds, kr[...] * mask)
            both = jnp.concatenate([dk.astype(BF16), dv.astype(BF16)], axis=1)
            grad = nn(mem[...], both)
            gk, gv = gk + grad[:, :PAIR], gv + grad[:, PAIR:]
            gb = gb + total(both[:, PAIR:])
            dm = nt(both, jnp.concatenate([wk_ref[...], wv_ref[...]], axis=1))

            @pl.when(step == 0)
            def _():
                acc[...] = dm

            @pl.when(step > 0)
            def _():
                acc[...] += dm

        for block in range(count):
            dcq_ref[block * size : (block + 1) * size, cols] = dq[block].astype(BF16)
        put(grad_ref, width + step * PAIR, gk)
        put(grad_ref, 2 * width + step * PAIR, gv)
        gb_ref[:, cols] = gb

    @pl.when(step == pairs)
    def _():
        dmo_ref[...] = dmo_acc[...].astype(BF16)
        gain = line(g1_ref)
        n1, r1 = normed(h1_ref[...])
        a1b = (n1 * gain + line(s1_ref)).astype(BF16)
        dcq = dcq_ref[...]
        d1 = dh2_ref[...] + nt(dcq, wcq_ref[...])
        dh1 = norm_back(d1, n1, r1, gain)
        dh1_ref[...] = dh1
        dso = dh1.astype(BF16)
        dsc_ref[...] = nt(dso, wso_ref[...]).astype(BF16)
        put(late_ref, 0, tn(a1b, dcq))
        put(late_ref, width, tn(ctx_ref[...], dso))
        small_ref[0:1] = total(dcq)
        small_ref[1:2] = total(d1 * n1)
        small_ref[2:3] = total(d1)
        small_ref[3:4] = total(dso)
        small_ref[4:8] = jnp.zeros((4, width), F32)


MIDDLE = 30


def cross_backward(block, cq, kv, kvo, g, o, lse, t, own, oth, m, mo, w, gco, dh2, h1, ctx, wcq, wso, gain, shift, schedule):
    rows, width = cq.shape
    pairs = width // PAIR

    def pair_of(size, offset):
        return pl.BlockSpec((size, PAIR), lambda s: (0, jnp.minimum(s, pairs - 1) + offset))

    flat, square = whole((rows, width)), whole((width, width))
    outs = [
        jax.ShapeDtypeStruct((rows, width), F32),
        jax.ShapeDtypeStruct((rows, width), BF16),
        jax.ShapeDtypeStruct((1, width), F32),
        jax.ShapeDtypeStruct((rows, width), F32),
        jax.ShapeDtypeStruct((rows, width), BF16),
        jax.ShapeDtypeStruct(block + (2 * width,), BF16),
        jax.ShapeDtypeStruct((8, width), F32),
    ]
    specs = [flat, flat, whole((1, width)), flat, flat, whole(block + (2 * width,)), whole((8, width))]
    held = []
    if schedule:
        held.append(pltpu.VMEM(block + (3 * width,), BF16))
    else:
        outs.append(jax.ShapeDtypeStruct(block + (3 * width,), BF16))
        specs.append(whole(block + (3 * width,)))
    held += [
        pltpu.VMEM((rows, width), F32),
        pltpu.VMEM((width, rows), BF16),
        pltpu.VMEM((width, rows), BF16),
        pltpu.VMEM((rows, width), BF16),
    ]
    return run(
        functools.partial(cross_backward_kernel, 256, pairs), "cross_backward", pairs + 1,
        (cq, kv, kv, kvo, kvo, g, o, lse, t, own, oth, m, mo, w, w, gco, dh2, h1, ctx, wcq, wso, gain, shift),
        [
            pair_of(rows, 0), pair_of(rows, 0), pair_of(rows, pairs), pair_of(rows, 0), pair_of(rows, pairs),
            pair_of(rows, 0), pair_of(rows, 0),
            pl.BlockSpec((8, rows), lambda s: (jnp.minimum(s, pairs - 1), 0)),
            whole((rows, 128)), whole((rows, 128)), whole((rows, 128)), flat, flat,
            pair_of(width, 0), pair_of(width, pairs),
            square, flat, flat, flat, square, square, whole(gain.shape), whole(shift.shape),
        ],
        outs, specs, held, schedule, 3,
        64 * rows * rows * width + 24 * rows * width * width, 40 * rows * width,
    )


def backward_pieces(size, q_ref, g_ref, o_ref, lse_ref, own_ref):
    masks = head_masks(BF16)
    scale = BF16(HD**-0.5)
    qcode = query_code(own_ref[...])
    delta = delta_rows(g_ref[...], o_ref[...])
    for block in range(q_ref.shape[0] // size):
        at = slice(block * size, (block + 1) * size)
        for head, mask in enumerate(masks):
            qm = q_ref[at] * (mask * scale)
            gm = g_ref[at] * mask
            q = jnp.concatenate([qm, qcode[at]], axis=1)
            yield block, mask * scale, qm, gm, q, lse_ref[head : head + 1, at], delta[head : head + 1, at]


def self_backward_kernel(
    size, q_ref, k_ref, v_ref, ko_ref, vo_ref, g_ref, o_ref, lse_ref, own_ref, oth_ref,
    x_ref, xo_ref, wq_ref, wk_ref, wv_ref, dh1_ref, sa_ref, sb_ref, sc_ref, sd_ref, dmo_ref,
    dx_ref, dmi_ref, grad_ref,
    dq_acc, dx_acc, dxo_acc, dkv_acc, xt_ref, xot_ref, dxo_ref, came_ref, memory_ref, turn_ref, send_ref, recv_ref,
):
    step = pl.program_id(0)
    sp = lax.axis_index("sp")
    second = sp == 1
    rows, width = x_ref.shape
    pairs = width // PAIR
    pair = lax.rem(step, pairs)
    cols = pl.ds(pl.multiple_of(pair * PAIR, PAIR), PAIR)
    count = rows // size
    over = remote(dxo_ref, came_ref, send_ref.at[0], recv_ref.at[0], ("y",))

    def pieces():
        return backward_pieces(size, q_ref, g_ref, o_ref, lse_ref, own_ref)

    @pl.when(step == 0)
    def _():
        remote(dmo_ref, memory_ref, send_ref.at[1], recv_ref.at[1], ("y",)).start()
        xt_ref[...] = jnp.transpose(x_ref[...])
        turn_ref[...] = jnp.zeros(turn_ref.shape, F32)
        turn_ref[0:8] = sa_ref[...]
        turn_ref[8:16] = sb_ref[...]
        turn_ref[16:17] = sc_ref[...]
        turn_ref[17:21] = sd_ref[...]

    @pl.when(jnp.logical_and(step == 0, second))
    def _():
        xot_ref[...] = jnp.transpose(xo_ref[...])

    @pl.when(jnp.logical_and(step < pairs, second))
    def _():
        keys = jnp.concatenate([ko_ref[...], oth_ref[...]], axis=1)
        values = vo_ref[...]
        dk = dv = 0.0
        dq = [0.0] * count
        for block, mask, qm, gm, q, lse, delta in pieces():
            p, ds = back_piece(keys, values, q, gm, lse, delta, False)
            dk = dk + nn(ds, qm)
            dv = dv + nn(p, gm)
            dq[block] = dq[block] + tn(ds, ko_ref[...] * mask)
        for block in range(count):
            dq_acc[pair, block * size : (block + 1) * size] = dq[block]
        both = jnp.concatenate([dk.astype(BF16), dv.astype(BF16)], axis=1)
        dkv_acc[pair] = both
        dxo = nt(both, jnp.concatenate([wk_ref[...], wv_ref[...]], axis=1))

        @pl.when(step == 0)
        def _():
            dxo_acc[...] = dxo

        @pl.when(step > 0)
        def _():
            dxo_acc[...] += dxo

    @pl.when(jnp.logical_and(step == pairs - 1, second))
    def _():
        dxo_ref[...] = dxo_acc[...].astype(BF16)
        over.start()

    @pl.when(step >= pairs)
    def _():
        dq, dk, dv = [0.0] * count, [0.0] * count, [0.0] * count
        for block, mask, qm, gm, q, lse, delta in pieces():
            for part in range(block + 1):
                of = slice(part * size, (part + 1) * size)
                keys = jnp.concatenate([k_ref[of], own_ref[of]], axis=1)
                p, ds = back_piece(keys, v_ref[of], q, gm, lse, delta, part == block)
                dk[part] = dk[part] + nn(ds, qm)
                dv[part] = dv[part] + nn(p, gm)
                dq[block] = dq[block] + tn(ds, k_ref[of] * mask)
        dq, dk, dv = (jnp.concatenate(a, axis=0) for a in (dq, dk, dv))
        dq = jnp.where(second, dq + dq_acc[pair], dq)
        dqk = jnp.concatenate([dq.astype(BF16), dk.astype(BF16)], axis=1)
        dv = dv.astype(BF16)
        grad_qk = nn(xt_ref[...], dqk)
        grad_v = nn(xt_ref[...], dv)
        shape = grad_ref.shape[:-1] + (PAIR,)
        lead = (slice(None),) * (len(shape) - 1)

        def put(n, grad):
            col = pair // 2 * 6 + 2 * n + pair % 2
            to = pl.ds(pl.multiple_of(col * PAIR, PAIR), PAIR)
            grad_ref[lead + (to,)] = grad.astype(BF16).reshape(shape)

        put(0, grad_qk[:, :PAIR])
        turn_ref[21:22, cols] = total(dqk[:, :PAIR])

        @pl.when(second)
        def _():
            grad_o = nn(xot_ref[...], dkv_acc[pair])
            put(1, grad_qk[:, PAIR:] + grad_o[:, :PAIR])
            put(2, grad_v + grad_o[:, PAIR:])
            turn_ref[22:23, cols] = total(dv) + total(dkv_acc[pair, :, PAIR:])

        @pl.when(jnp.logical_not(second))
        def _():
            put(1, grad_qk[:, PAIR:])
            put(2, grad_v)
            turn_ref[22:23, cols] = total(dv)

        dx = nt(dqk, jnp.concatenate([wq_ref[...], wk_ref[...]], axis=1)) + nt(dv, wv_ref[...])

        @pl.when(step == pairs)
        def _():
            dx_acc[...] = dh1_ref[...] + dx

        @pl.when(step > pairs)
        def _():
            dx_acc[...] += dx

    @pl.when(step == 2 * pairs - 1)
    def _():
        shape = grad_ref.shape[:-1] + (2 * PAIR,)
        lead = (slice(None),) * (len(shape) - 1)
        col = 3 * width
        grad_ref[lead + (slice(col, col + 2 * PAIR),)] = jnp.transpose(turn_ref[...]).astype(BF16).reshape(shape)


def self_backward_finale(*refs):
    dmo_ref, dx_ref, dmi_ref = refs[20:23]
    dx_acc, dxo_ref, came_ref, memory_ref, send_ref, recv_ref = (refs[i] for i in (25, 30, 31, 32, 34, 35))
    remote(dmo_ref, memory_ref, send_ref.at[1], recv_ref.at[1], ("y",)).wait()
    dmi_ref[...] = memory_ref[...]
    over = remote(dxo_ref, came_ref, send_ref.at[0], recv_ref.at[0], ("y",))

    @pl.when(lax.axis_index("sp") == 0)
    def _():
        over.wait_recv()
        dx_ref[...] = (dx_acc[...] + came_ref[...].astype(F32)).astype(BF16)

    @pl.when(lax.axis_index("sp") == 1)
    def _():
        over.wait_send()
        dx_ref[...] = dx_acc[...].astype(BF16)


GRADS = 23


def self_backward(block, qkv, kvo, g, o, lse, own, oth, x, xo, w, dh1, small, dmo, schedule):
    rows, width = x.shape
    pairs = width // PAIR

    def pair_of(offset):
        return pl.BlockSpec((rows, PAIR), lambda s: (0, lax.rem(s, pairs) + offset))

    def weight(offset):
        return pl.BlockSpec((width, PAIR), lambda s: (0, lax.rem(s, pairs) + offset))

    made = block + (3 * width + 2 * PAIR,)
    outs = [jax.ShapeDtypeStruct((rows, width), BF16)] * 2
    specs = [whole((rows, width))] * 2
    held = []
    if schedule:
        held += [pltpu.VMEM(made, BF16)]
    else:
        outs += [jax.ShapeDtypeStruct(made, BF16)]
        specs += [whole(made)]
    held += [
        pltpu.VMEM((pairs, rows, PAIR), F32),
        pltpu.VMEM((rows, width), F32),
        pltpu.VMEM((rows, width), F32),
        pltpu.VMEM((pairs, rows, 2 * PAIR), BF16),
        pltpu.VMEM((width, rows), BF16),
        pltpu.VMEM((width, rows), BF16),
        pltpu.VMEM((rows, width), BF16),
        pltpu.VMEM((rows, width), BF16),
        pltpu.VMEM((rows, width), BF16),
        pltpu.VMEM((2 * PAIR, width), F32),
        pltpu.SemaphoreType.DMA((2,)),
        pltpu.SemaphoreType.DMA((2,)),
    ]
    return run(
        functools.partial(self_backward_kernel, 256), "self_backward", 2 * pairs,
        (qkv, qkv, qkv, kvo, kvo, g, o, lse, own, oth, x, xo, w, w, w, dh1) + tuple(small) + (dmo,),
        [
            pair_of(0),
            pair_of(pairs),
            pair_of(2 * pairs),
            pair_of(0),
            pair_of(pairs),
            pair_of(0),
            pair_of(0),
            pl.BlockSpec((8, rows), lambda s: (lax.rem(s, pairs), 0)),
            whole((rows, 128)),
            whole((rows, 128)),
            whole((rows, width)),
            whole((rows, width)),
            weight(0),
            weight(pairs),
            weight(2 * pairs),
            whole((rows, width)),
        ] + [whole(a.shape) for a in small] + [pl.BlockSpec(memory_space=pl.ANY)],
        outs, specs, held, schedule, 5,
        48 * rows * rows * width + 20 * rows * width * width, 12 * width * width + 40 * rows * width,
        (("y",),), self_backward_finale,
    )


def code_of(docs_ref):
    row = lax.broadcasted_iota(jnp.int32, (PAIR, docs_ref.shape[1]), 0)
    return jnp.transpose(jnp.where(docs_ref[...] == row, 1.0, 0.0)).astype(BF16)


def line(ref):
    return ref[...].astype(F32)[None, :]


def front_kernel(
    size, x_hbm, m_hbm, td_ref, md_ref, wx_hbm, wm_hbm, wo_hbm, wq_hbm,
    bq_ref, bv_ref, bcv_ref, bso_ref, g_ref, s_ref, bcq_ref,
    qkv_out, mkv_out, kvo_out, mkvo_out, cq_out, ctx_out, cc_out, h_out, xo_out, mo_out,
    lse_ref, clse_ref, tt_ref, mt_ref, to_ref, mo_ref,
    x_ref, m_ref, wx_ref, wm_ref, wo_ref, wq_ref, xc_ref, mc_ref, tdc_ref, mdc_ref,
    qkv_ref, mkv_ref, kvo_ref, mkvo_ref, cq_ref, ctx_ref, cc_ref, h_ref, acc_ref, held_ref,
    load_ref, store_ref, send_ref, recv_ref,
):
    rows, width = x_ref.shape
    pairs = width // PAIR
    second = lax.axis_index("sp") == 1
    first = jnp.logical_not(second)
    masks = head_masks(BF16)
    keeps = head_masks(F32)
    scale = BF16(HD**-0.5)
    loads = [
        pltpu.make_async_copy(src, dst, load_ref.at[i])
        for i, (src, dst) in enumerate(
            ((x_hbm, x_ref), (wx_hbm, wx_ref), (m_hbm, m_ref), (wm_hbm, wm_ref), (wo_hbm, wo_ref), (wq_hbm, wq_ref))
        )
    ]
    give = [
        pltpu.make_async_copy(src, dst, store_ref.at[i])
        for i, (src, dst) in enumerate(
            (
                (qkv_ref, qkv_out), (mkv_ref, mkv_out), (mkvo_ref, mkvo_out), (cq_ref, cq_out), (ctx_ref, ctx_out),
                (cc_ref, cc_out), (h_ref, h_out), (mc_ref, mo_out), (kvo_ref, kvo_out), (xc_ref, xo_out),
            )
        )
    ]
    x_over = remote(x_hbm, xc_ref, send_ref.at[0], recv_ref.at[0], ("y",))
    m_over = remote(m_hbm, mc_ref, send_ref.at[1], recv_ref.at[1], ("y",))
    docs = [
        remote(td_ref, tdc_ref, send_ref.at[2], recv_ref.at[2], ("y",)),
        remote(md_ref, mdc_ref, send_ref.at[3], recv_ref.at[3], ("y",)),
    ]
    for copy in loads:
        copy.start()
    greet([("y",)])
    for copy in docs:
        copy.start()
    pl.when(first)(x_over.start)
    pl.when(second)(m_over.start)

    def columns(offset, pair):
        return pl.ds(pl.multiple_of(offset + pair * PAIR, PAIR), PAIR)

    def heads(source, offset, pair, code, block):
        at = slice(block * size, (block + 1) * size)
        q = source[at, columns(offset, pair)]
        return [jnp.concatenate([q * (mask * scale), code[at]], axis=1) for mask in masks]

    def keep_lse(block, pair, low, high, out):
        at = slice(block * size, (block + 1) * size)
        lane = lax.broadcasted_iota(jnp.int32, (size, PAIR), 1)
        both = jnp.where(lane == 0, low, high)
        held_ref[pair, at] = both
        out[pl.ds(pl.multiple_of(pair * 8, 8), 8), at] = jnp.transpose(both)[:8]

    def begin(block, pair, results, lse_out, out):
        at = slice(block * size, (block + 1) * size)
        mixed = sum(r * keep for (r, _), keep in zip(results, keeps))
        acc_ref[at, columns(0, pair)] = mixed
        out[at, columns(0, pair)] = mixed.astype(BF16)
        keep_lse(block, pair, results[0][1], results[1][1], lse_out)

    def merge(block, pair, results, lse_out, out):
        at = slice(block * size, (block + 1) * size)
        before = acc_ref[at, columns(0, pair)]
        mixed, lses = 0.0, []
        for head, ((r, lse), keep) in enumerate(zip(results, keeps)):
            old = held_ref[pair, at, head : head + 1]
            peak = jnp.maximum(old, lse)
            both = peak + jnp.log(jnp.exp(old - peak) + jnp.exp(lse - peak))
            mixed = mixed + keep * (before * jnp.exp(old - both) + r * jnp.exp(lse - both))
            lses.append(both)
        out[at, columns(0, pair)] = mixed.astype(BF16)
        keep_lse(block, pair, lses[0], lses[1], lse_out)

    to_ref[...] = code_of(td_ref)
    mo_ref[...] = code_of(md_ref)
    loads[0].wait()
    loads[1].wait()
    for n, bias in enumerate((line(bq_ref), 0.0, line(bv_ref))):
        cols = slice(n * width, (n + 1) * width)
        qkv_ref[:, cols] = (nn(x_ref[...], wx_ref[:, cols]) + bias).astype(BF16)
    give[0].start()
    loads[2].wait()
    loads[3].wait()
    for n, bias in enumerate((0.0, line(bcv_ref))):
        cols = slice(n * width, (n + 1) * width)
        mkv_ref[:, cols] = (nn(m_ref[...], wm_ref[:, cols]) + bias).astype(BF16)
    give[1].start()

    @pl.loop(0, pairs)
    def _(pair):
        code = query_code(to_ref[...])
        for block in range(rows // size):
            results = []
            for q in heads(qkv_ref, 0, pair, code, block):
                scores, values = [], []
                for part in range(block + 1):
                    of = slice(part * size, (part + 1) * size)
                    keys = jnp.concatenate([qkv_ref[of, columns(width, pair)], to_ref[of]], axis=1)
                    sc = nt(q, keys)
                    if part == block:
                        row = lax.broadcasted_iota(jnp.int32, sc.shape, 0)
                        col = lax.broadcasted_iota(jnp.int32, sc.shape, 1)
                        sc = jnp.where(row >= col, sc, -FAR)
                    scores.append(sc)
                    values.append(qkv_ref[of, columns(2 * width, pair)])
                results.append(softmax_pieces(scores, values))
            begin(block, pair, results, lse_ref, ctx_ref)

    for copy in docs:
        copy.wait()
    tt_ref[...] = code_of(tdc_ref)
    mt_ref[...] = code_of(mdc_ref)

    @pl.when(first)
    def _():
        x_over.wait_send()
        m_over.start()

    @pl.when(second)
    def _():
        x_over.wait_recv()
        give[9].start()
        for n, bias in enumerate((0.0, line(bv_ref))):
            cols = slice(n * width, (n + 1) * width)
            from_cols = slice((n + 1) * width, (n + 2) * width)
            kvo_ref[:, cols] = (nn(xc_ref[...], wx_ref[:, from_cols]) + bias).astype(BF16)
        give[8].start()

        @pl.loop(0, pairs)
        def _(pair):
            code = query_code(to_ref[...])
            keys = jnp.concatenate([kvo_ref[:, columns(0, pair)], tt_ref[...]], axis=1)
            values = kvo_ref[:, columns(width, pair)]
            for block in range(rows // size):
                results = [softmax_pieces([nt(q, keys)], [values]) for q in heads(qkv_ref, 0, pair, code, block)]
                merge(block, pair, results, lse_ref, ctx_ref)

    give[4].start()
    loads[4].wait()
    loads[5].wait()
    h = x_ref[...].astype(F32) + nn(ctx_ref[...], wo_ref[...]) + line(bso_ref)
    h_ref[...] = h
    n, _ = normed(h)
    a = (n * line(g_ref) + line(s_ref)).astype(BF16)
    cq_ref[...] = (nn(a, wq_ref[...]) + line(bcq_ref)).astype(BF16)
    give[6].start()
    give[3].start()

    def cross(keys_ref, key_code, finish):
        @pl.loop(0, pairs)
        def _(pair):
            code = query_code(to_ref[...])
            keys = jnp.concatenate([keys_ref[:, columns(0, pair)], key_code[...]], axis=1)
            values = keys_ref[:, columns(width, pair)]
            for block in range(rows // size):
                results = [softmax_pieces([nt(q, keys)], [values]) for q in heads(cq_ref, 0, pair, code, block)]
                finish(block, pair, results, clse_ref, cc_ref)

    cross(mkv_ref, mo_ref, begin)
    m_over.wait()
    give[7].start()
    for n, bias in enumerate((0.0, line(bcv_ref))):
        cols = slice(n * width, (n + 1) * width)
        mkvo_ref[:, cols] = (nn(mc_ref[...], wm_ref[:, cols]) + bias).astype(BF16)
    give[2].start()
    cross(mkvo_ref, mt_ref, merge)
    give[5].start()
    for copy in give[:8]:
        copy.wait()

    @pl.when(second)
    def _():
        give[8].wait()
        give[9].wait()


def front(x, mem, td, md, wx, wm, wo, wq, vectors):
    rows, width = x.shape
    pairs = width // PAIR

    def flat(n):
        return jax.ShapeDtypeStruct((rows, n * width), BF16)

    stats = jax.ShapeDtypeStruct((8 * pairs, rows), F32)
    code = jax.ShapeDtypeStruct((rows, PAIR), BF16)
    far = pl.BlockSpec(memory_space=pl.ANY)
    near = pl.BlockSpec(memory_space=pltpu.VMEM)
    tall = jax.ShapeDtypeStruct((rows, width), F32)
    held = [flat(3), flat(2), flat(2), flat(2), flat(1), flat(1), flat(1), tall, tall]
    return pl.pallas_call(
        functools.partial(front_kernel, 256),
        in_specs=[far, far, near, near, far, far, far, far] + [near] * len(vectors),
        out_specs=[far] * 10 + [near] * 6,
        out_shape=[flat(3), flat(2), flat(2), flat(2), flat(1), flat(1), flat(1), tall, flat(1), flat(1)]
        + [stats, stats, code, code, code, code],
        scratch_shapes=[pltpu.VMEM(a.shape, a.dtype) for a in (flat(1), flat(1))]
        + [pltpu.VMEM(w.shape, BF16) for w in (wx, wm, wo, wq)]
        + [pltpu.VMEM((rows, width), BF16)] * 2
        + [pltpu.VMEM((1, rows), jnp.int32)] * 2
        + [pltpu.VMEM(a.shape, a.dtype) for a in held]
        + [
            pltpu.VMEM((pairs, rows, PAIR), F32),
            pltpu.SemaphoreType.DMA((6,)),
            pltpu.SemaphoreType.DMA((10,)),
            pltpu.SemaphoreType.DMA((4,)),
            pltpu.SemaphoreType.DMA((4,)),
        ],
        compiler_params=params(1),
        cost_estimate=cost(22 * rows * width * width + 36 * rows * rows * width, 60 * rows * width),
        name="front",
    )(x, mem, td, md, wx, wm, wo, wq, *vectors)


def feed_kernel(
    count, comm, h1_ref, cc_ref, ct_ref, wco_ref, wi_ref, wo_ref,
    g1_ref, s1_ref, bco_ref, g2_ref, s2_ref, bfo_ref, g3_ref, s3_ref, bfi_ref, out_ref, dh2_ref, dcc_ref, gco_ref, *refs,
):
    if comm:
        gwi_ref, refs = refs[0], refs[1:]
    else:
        gwi_ref, gwo_ref, refs = refs[0], refs[1], refs[2:]
    small_ref, gib_ref, hid_ref, slope_ref, n2_ref, r2_ref, a2b_ref, acc_ref, df_ref, bias_ref, *refs = refs
    step = pl.program_id(0)
    width = acc_ref.shape[1]

    if comm:
        mi_ref, mo_ref, ci_ref, co_ref, send_ref, recv_ref = refs
        wide = ci_ref.shape[-1]
        here = place()
        c = here[1]

        def chunk_copies(j):
            at = pl.ds(pl.multiple_of(j * width, width), width)
            return [
                remote(mi_ref.at[:, :, at], ci_ref.at[:, :, at], send_ref.at[0, j], recv_ref.at[0, j], ("core",), here),
                remote(mo_ref.at[j], co_ref.at[j], send_ref.at[1, j], recv_ref.at[1, j], ("core",), here),
            ]

    @pl.when(step == 0)
    def _():
        if comm:
            greet([("core",)])
        wide = bfi_ref[...].astype(F32)
        for i in range(count):
            bias_ref[i : i + 1] = wide[None, i * width : (i + 1) * width]
        n1, _ = normed(h1_ref[...])
        a1 = n1 * line(g1_ref) + line(s1_ref)
        h2 = a1 + nn(cc_ref[...], wco_ref[...]) + line(bco_ref)
        n2, r2 = normed(h2)
        n2_ref[...] = n2
        r2_ref[...] = jnp.broadcast_to(r2, r2_ref.shape)
        a2 = n2 * line(g2_ref) + line(s2_ref)
        a2b_ref[...] = a2.astype(BF16)
        acc_ref[...] = a2 + line(bfo_ref)

    @pl.when(step < count)
    def _():
        u = nn(a2b_ref[...], wi_ref[...]) + bias_ref[pl.ds(step, 1)]
        cumul = 0.5 * (1.0 + lax.erf(u * 0.7071067811865476))
        density = jnp.exp(-0.5 * u * u) * 0.3989422804014327
        hid = (u * cumul).astype(BF16)
        hid_ref[step] = hid
        slope_ref[step] = cumul + u * density
        acc_ref[...] += nn(hid, wo_ref[...])

    @pl.when(step == count - 1)
    def _():
        n3, r3 = normed(acc_ref[...])
        gain = line(g3_ref)
        out_ref[...] = (n3 * gain + line(s3_ref)).astype(BF16)
        e = ct_ref[...].astype(F32)
        d3 = norm_back(e, n3, r3, gain)
        df = d3.astype(BF16)
        df_ref[...] = df
        acc_ref[...] = d3
        small_ref[0:1] = total(e * n3)
        small_ref[1:2] = total(e)
        small_ref[2:3] = total(df)

    @pl.when(jnp.logical_and(step >= count, step < 2 * count))
    def _():
        j = step - count
        df = df_ref[...]
        du = (nt(df, wo_ref[...]) * slope_ref[j]).astype(BF16)
        gib_ref[...] = total(du)
        acc_ref[...] += nt(du, wi_ref[...])
        go = tn(hid_ref[j], df).astype(BF16)
        gi = tn(a2b_ref[...], du).astype(BF16)
        if comm:
            at = pl.ds(pl.multiple_of(j * width, width), width)
            eight, narrow = gwi_ref.shape[:2]
            gi = gi.reshape(eight, 2, narrow, width)
            go = go.reshape(2, 2, 4, narrow, width)
            gwi_ref[:, :, at] = jnp.where(c == 0, gi[:, 0], gi[:, 1])
            mi_ref[:, :, at] = jnp.where(c == 0, gi[:, 1], gi[:, 0])
            mo_ref[j] = jnp.where(c == 0, go[:, 1], go[:, 0])
            for i in range(4):
                gwi_ref[pl.ds(2 * j, 2), :, pl.ds(wide + i * width, width)] = jnp.where(c == 0, go[:, 0, i], go[:, 1, i])
            for copy in chunk_copies(j):
                copy.start()
        else:
            gwo_ref[...] = go
            gwi_ref[...] = gi

    @pl.when(step == 2 * count)
    def _():
        d2 = acc_ref[...]
        n2 = n2_ref[...]
        dh2 = norm_back(d2, n2, r2_ref[:, :1], line(g2_ref))
        dh2_ref[...] = dh2
        dco = dh2.astype(BF16)
        dcc_ref[...] = nt(dco, wco_ref[...]).astype(BF16)
        gco_ref[...] = tn(cc_ref[...], dco).astype(BF16)
        small_ref[3:4] = total(d2 * n2)
        small_ref[4:5] = total(d2)
        small_ref[5:6] = total(dco)
        small_ref[6:8] = jnp.zeros((2, d2.shape[1]), F32)

    if comm:

        @pl.when(step > count)
        def _():
            j = step - count - 1
            at = pl.ds(pl.multiple_of(j * width, width), width)
            for copy in chunk_copies(j):
                copy.wait()
            gwi_ref[:, :, at] += ci_ref[:, :, at]
            for i in range(4):
                gwi_ref[pl.ds(2 * j, 2), :, pl.ds(wide + i * width, width)] += co_ref[j, :, i]


def feed(size, comm, h1, cc, ct, wco, wi, wo, vectors):
    rows, width = h1.shape
    wide = wi.shape[1]
    chunk = width
    count = wide // chunk

    def weight(s):
        return jnp.where(s < count, s, jnp.minimum(s - count, count - 1))

    def early(s):
        return jnp.clip(s - count, 0, count - 1)

    flat = whole((rows, width))
    square = whole((width, width))
    scratch = [
        pltpu.VMEM((count, rows, chunk), BF16),
        pltpu.VMEM((count, rows, chunk), F32),
        pltpu.VMEM((rows, width), F32),
        pltpu.VMEM((rows, 128), F32),
        pltpu.VMEM((rows, width), BF16),
        pltpu.VMEM((rows, width), F32),
        pltpu.VMEM((rows, width), BF16),
        pltpu.VMEM((8, width), F32),
    ]
    if comm:
        narrow = width // size
        grad_specs = [whole((size // 2, narrow, 2 * wide))]
        grad_shapes = [(size // 2, narrow, 2 * wide)]
        scratch += [
            pltpu.VMEM((size // 2, narrow, wide), BF16),
            pltpu.VMEM((count, 2, 4, narrow, width), BF16),
            pltpu.VMEM((size // 2, narrow, wide), BF16),
            pltpu.VMEM((count, 2, 4, narrow, width), BF16),
            pltpu.SemaphoreType.DMA((2, count)),
            pltpu.SemaphoreType.DMA((2, count)),
        ]
    else:
        grad_specs = [
            pl.BlockSpec((width, chunk), lambda s: (0, early(s))),
            pl.BlockSpec((chunk, width), lambda s: (early(s), 0)),
        ]
        grad_shapes = [(width, wide), (wide, width)]
    return pl.pallas_call(
        functools.partial(feed_kernel, count, comm),
        grid=(2 * count + 1,),
        in_specs=[
            flat, flat, flat, square,
            pl.BlockSpec((width, chunk), lambda s: (0, weight(s))),
            pl.BlockSpec((chunk, width), lambda s: (weight(s), 0)),
        ]
        + [whole(v.shape) for v in vectors],
        out_specs=[flat, flat, flat, square]
        + grad_specs
        + [whole((8, width)), pl.BlockSpec((1, chunk), lambda s: (0, early(s)))],
        out_shape=[
            jax.ShapeDtypeStruct((rows, width), BF16),
            jax.ShapeDtypeStruct((rows, width), F32),
            jax.ShapeDtypeStruct((rows, width), BF16),
            jax.ShapeDtypeStruct((width, width), BF16),
        ]
        + [jax.ShapeDtypeStruct(a, BF16) for a in grad_shapes]
        + [
            jax.ShapeDtypeStruct((8, width), F32),
            jax.ShapeDtypeStruct((1, wide), F32),
        ],
        scratch_shapes=scratch,
        compiler_params=params(2 if comm else None),
        cost_estimate=cost(
            12 * rows * width * wide + 6 * rows * width * width, 12 * width * wide + 16 * rows * width
        ),
        name="feed",
    )(h1, cc, ct, wco, wi, wo, *vectors)


def outputs_kernel(moves, count, line, *refs):
    pieces, rest = refs[:count], refs[count:]
    out_ref, dx_ref, dm_ref, dmi_ref = rest[:4]
    outs = rest[4:]
    for piece, first, wide, which, row, col in moves:
        ref = pieces[piece]
        outs[which][row : row + ref.shape[0], col : col + wide] = ref[:, first : first + wide].astype(F32)
    turned, result, dx, dm = outs[-4:]
    turned[...] = jnp.transpose(pieces[line[0]][:, line[1] : line[1] + PAIR].astype(F32))
    result[...] = out_ref[...]
    dx[...] = dx_ref[...]
    dm[...] = (dm_ref[...] + dmi_ref[...].astype(F32)).astype(BF16)


def outputs(pieces, moves, line, shapes, out, dx, dm, dmi):
    ins = tuple(pieces) + (out, dx, dm, dmi)
    result = jax.ShapeDtypeStruct(out.shape, BF16)
    return pl.pallas_call(
        functools.partial(outputs_kernel, moves, len(pieces), line),
        out_shape=[jax.ShapeDtypeStruct(a, F32) for a in shapes]
        + [jax.ShapeDtypeStruct((PAIR, pieces[0].shape[0]), F32), result, result, result],
        compiler_params=params(),
        cost_estimate=cost(0, 12 << 20),
        name="outputs",
    )(*ins)


def moved(pieces, targets):
    out = []
    for n, (start, wide) in enumerate(pieces):
        for first, cols, which, row, col in targets:
            low, high = max(start, first), min(start + wide, first + cols)
            if low < high:
                out.append((n, low - start, high - low, which, row, col + low - first))
    return out


def schedule_of(flows, kernel):
    entries = [
        (start, order, name, start, stop)
        for order, name in enumerate(flows)
        for start, stop in PLAN[name][kernel]
    ]
    return tuple(([flows[name]], start, stop) for _, _, name, start, stop in sorted(entries))


def swap_sum(part, axis, pairs):
    came = lax.ppermute(part, axis, pairs)
    return part.astype(F32) + came.astype(F32)


def sum_scatter(grad, size, order):
    rows, cols = grad.shape
    bits = size.bit_length() - 1
    me = lax.axis_index("dp")
    now = grad.reshape((2,) * bits + (rows // size, cols))
    left = list(range(bits))[::-1]
    for bit in [b for b in order if b < bits] + [b for b in range(bits) if b not in order]:
        axis = left.index(bit)
        mine = (me >> bit) & 1
        keep = lax.dynamic_index_in_dim(now, mine, axis, keepdims=False)
        send = lax.dynamic_index_in_dim(now, 1 - mine, axis, keepdims=False)
        came = lax.ppermute(send, "dp", [(i, i ^ (1 << bit)) for i in range(size)])
        now = (keep.astype(F32) + came.astype(F32)).astype(BF16)
        left.pop(axis)
    return swap_sum(now, "sp", [(0, 1), (1, 0)])


def per_device(
    size,
    inputs,
    memory,
    target_docs,
    memory_docs,
    cotangent,
    w_qkv,
    b_q,
    b_v,
    w_so,
    b_so,
    g_one,
    s_one,
    w_cq,
    b_cq,
    w_ckv,
    b_cv,
    w_co,
    b_co,
    g_two,
    s_two,
    w_fi,
    b_fi,
    w_fo,
    b_fo,
    g_three,
    s_three,
):
    rows, width = inputs.shape[1:]
    wide = b_fi.shape[0]
    comm = size == 16
    narrow, broad = width // size, wide // size
    x, mem, ct = inputs[0], memory[0], cotangent[0]
    qkv, mkv, kvo, mkvo, cq, ctx, cc, h1, x_o, mem_o, lse, clse, t_oth, m_oth, t_own, m_own = front(
        x, mem, target_docs, memory_docs, w_qkv, w_ckv, w_so, w_cq, (b_q, b_v, b_cv, b_so, g_one, s_one, b_cq)
    )
    output, dh2, dcc, gco, gwi, *gwo, small_a, gib = feed(
        size, comm, h1, cc, ct, w_co, w_fi, w_fo,
        (g_one, s_one, b_co, g_two, s_two, b_fo, g_three, s_three, b_fi),
    )
    turned = gib.reshape(width, -1).T

    block = (2, 2, 2, 2, narrow) if comm else (width,)
    at_cross, at_self, flows = (), (), {}
    if comm:
        late_shape = block + (2 * width,)
        sources = {
            "T0": (gwi.reshape(block[:3] + gwi.shape[1:]), block[:3] + gwi.shape[1:], BLOCK[:3]),
            "T1a": (("ref", MIDDLE), block + (3 * width,), BLOCK),
            "T1b": (None, late_shape, BLOCK),
            "G": (("ref", GRADS), block + (3 * width + 2 * PAIR,), BLOCK),
        }
        for name, (source, cols, hops, _, _) in PLAN.items():
            array, shape, dims = sources[source]
            flows[name] = Flow(array, shape, hops, dims, cols)
        at_cross = schedule_of(flows, 3)
        at_self = schedule_of(flows, 4)
    dm, dmo, gcvb, dh1, dsc, late, small_b, *early = cross_backward(
        block, cq, mkv, mkvo, dcc, cc, clse, t_own, m_own, m_oth, mem, mem_o, w_ckv,
        gco, dh2, h1, ctx, w_cq, w_so, g_one, s_one, at_cross,
    )
    for name, flow in flows.items():
        if PLAN[name][0] == "T1b":
            flow.array = late
    dx, dm_in, *made = self_backward(
        block, qkv, kvo, dsc, ctx, lse, t_own, t_oth, x, x_o, w_qkv, dh1, (small_a, small_b, gcvb, turned), dmo, at_self
    )
    if comm:
        targets = {
            "T0": [(0, wide, 2, 0, 0)] + [(wide + i * width, width, 3, i * narrow, 0) for i in range(4)],
            "T1a": [(0, width, 4, 0, 0), (width, 2 * width, 1, 0, 0)],
            "T1b": [(0, width, 5, 0, 0), (width, width, 6, 0, 0)],
            "G": [
                (g * 6 * PAIR + i * 2 * PAIR, 2 * PAIR, 0, 0, i * width + g * 2 * PAIR)
                for g in range(width // PAIR // 2)
                for i in range(3)
            ],
        }
        moves, line = [], None
        for n, (source, cols, *_) in enumerate(PLAN.values()):
            moves += [(n,) + m[1:] for m in moved([cols], targets[source])]
            if source == "G" and cols[0] <= 3 * width < sum(cols):
                line = n, 3 * width - cols[0]
        shapes = [(narrow, 3 * width), (narrow, 2 * width), (narrow, wide), (broad, width)] + [(narrow, width)] * 3
        t_qkv, t_cmem, t_fin, t_fout, t_cout, t_cquery, t_out, lines, output, derivative, grad_memory = outputs(
            [f.array for f in flows.values()], moves, line, shapes, output, dx, dm, dm_in
        )
    else:
        (early,), (made,) = early, made
        columns = made[:, 3 * width : 3 * width + PAIR]
        groups = range(width // PAIR // 2)
        gqkv = jnp.concatenate(
            [made[:, (g * 6 + 2 * i) * PAIR : (g * 6 + 2 * i + 2) * PAIR] for i in range(3) for g in groups], axis=1
        )
        t_fin, t_fout, t_cout, t_cquery, t_out, t_cmem, t_qkv, lines = (
            sum_scatter(g, size, (0, 1, 2, 3))
            for g in (
                gwi, gwo[0], early[:, :width], late[:, :width], late[:, width:], early[:, width:], gqkv, columns
            )
        )
        lines, derivative = lines.T, dx
        grad_memory = (dm + dm_in.astype(F32)).astype(BF16)
    t_gthree, t_sthree, t_fobias, t_gtwo, t_stwo, t_cobias = (lines[i] for i in range(6))
    t_cqbias, t_gone, t_sone, t_obias = (lines[i] for i in range(8, 12))
    t_cvbias, t_qbias, t_vbias = lines[16], lines[21], lines[22]
    t_fibias = lines[17:21].T.reshape(-1)
    return (
        output[None],
        derivative[None],
        grad_memory[None],
        t_qkv,
        t_qbias,
        t_vbias,
        t_out,
        t_obias,
        t_gone,
        t_sone,
        t_cquery,
        t_cqbias,
        t_cmem,
        t_cvbias,
        t_cout,
        t_cobias,
        t_gtwo,
        t_stwo,
        t_fin,
        t_fibias,
        t_fout,
        t_fobias,
        t_gthree,
        t_sthree,
    )


def solution(mesh):
    split = P("dp", "sp", None)
    in_specs = (split, split, P("dp", "sp"), P("dp", "sp"), split) + (P(),) * 21
    matrix, vector = P("dp", None), P("dp")
    out_specs = (
        split, split, split,
        matrix, vector, vector,
        matrix, vector, vector, vector,
        matrix, vector,
        matrix, vector,
        matrix, vector, vector, vector,
        matrix, vector,
        matrix, vector, vector, vector,
    )
    return jax.shard_map(
        functools.partial(per_device, mesh.shape["dp"]),
        mesh=mesh, in_specs=in_specs, out_specs=out_specs, check_vma=False,
    )
```

```python
import functools

import jax
import jax.numpy as jnp
from jax import lax
from jax.experimental import pallas as pl
from jax.experimental.pallas import tpu as pltpu
from jax.sharding import PartitionSpec as P

HD = 64
PAIR = 2 * HD
EPS = 1e-05
FAR = 1.0e9
VMEM = 60 * 1024 * 1024
F32 = jnp.float32
BF16 = jnp.bfloat16


def nn(a, b):
    return lax.dot_general(a, b, (((1,), (0,)), ((), ())), preferred_element_type=F32)


def nt(a, b):
    return lax.dot_general(a, b, (((1,), (1,)), ((), ())), preferred_element_type=F32)


def tn(a, b):
    return lax.dot_general(a, b, (((0,), (0,)), ((), ())), preferred_element_type=F32)


def params(collective=None):
    if collective is None:
        return pltpu.CompilerParams(vmem_limit_bytes=VMEM)
    return pltpu.CompilerParams(
        vmem_limit_bytes=VMEM, collective_id=collective, has_side_effects=True
    )


def cost(flops, moved):
    return pl.CostEstimate(flops=int(flops), bytes_accessed=int(moved), transcendentals=0)


def normed(h):
    centred = h - jnp.mean(h, axis=-1, keepdims=True)
    rstd = lax.rsqrt(jnp.mean(centred * centred, axis=-1, keepdims=True) + EPS)
    return centred * rstd, rstd


def norm_back(grad, n, rstd, gain):
    scaled = grad * gain
    centre = jnp.mean(scaled, axis=-1, keepdims=True)
    along = jnp.mean(scaled * n, axis=-1, keepdims=True)
    return rstd * (scaled - centre - n * along)


def total(a):
    return jnp.sum(a.astype(F32), axis=0, keepdims=True)


def place():
    me = lax.axis_index("dp")
    return me, me % 2, (me // 2) % 2, me // 4, lax.axis_index("sp")


def flipped(at, hops):
    me, c, x, z, sp = at
    for hop in hops:
        if hop == "core":
            me, c = me + 1 - 2 * c, 1 - c
        elif hop == "x":
            me, x = me + 2 - 4 * x, 1 - x
        elif hop == "z1":
            me, z = me + 4 - 8 * (z % 2), z + 1 - 2 * (z % 2)
        elif hop == "z2":
            me, z = me + 8 - 16 * (z // 2), z + 2 - 4 * (z // 2)
        else:
            sp = 1 - sp
    return me, c, x, z, sp


def partner(hops, at=None):
    there = flipped(at or place(), hops)
    return {"dp": there[0], "sp": there[4]}


def greet(groups, at=None):
    groups = sorted({tuple("y" if h[0] == "y" else h for h in hops) for hops in groups})
    barrier = pltpu.get_barrier_semaphore()
    for hops in groups:
        pl.semaphore_signal(barrier, inc=1, device_id=partner(hops, at), device_id_type=pl.DeviceIdType.MESH)
    pl.semaphore_wait(barrier, len(groups))


def remote(src, dst, send, recv, hops, at=None):
    return pltpu.make_async_remote_copy(
        src_ref=src, dst_ref=dst, send_sem=send, recv_sem=recv,
        device_id=partner(hops, at), device_id_type=pl.DeviceIdType.MESH,
    )


PLAN = {
    "T00": ("T0", (0, 2304), ("x", "yr", "z1", "z2", "yg"), ((0, 5), (5, 7)), ((0, 6), (6, 8), (8, 11))),
    "T01": ("T0", (2304, 1280), ("z1", "x", "z2", "y"), ((0, 3), (3, 6), (6, 7)), ((0, 3),)),
    "T02": ("T0", (3584, 2560), ("yr", "x", "z1", "z2", "yg"), ((0, 5), (5, 7)), ((0, 7), (7, 9), (9, 12))),
    "T1a0": ("T1a", (0, 1280), ("core", "x", "yr", "z1", "z2", "yg"), ((6, 7),), ((0, 5), (5, 10), (10, 12), (12, 18), (18, 22))),
    "T1a1": ("T1a", (1280, 1024), ("core", "z1", "x", "z2", "y"), ((6, 7),), ((0, 8), (8, 10), (10, 12), (12, 17))),
    "T1b0": ("T1b", (0, 1536), ("core", "x", "z1", "yr", "z2", "yg"), (), ((0, 3), (3, 8), (8, 10), (10, 13), (13, 20), (20, 25))),
    "G10": ("G", (0, 768), ("core", "x", "z1", "z2", "y"), (), ((8, 9), (9, 11), (11, 13), (13, 20), (20, 25))),
    "G20": ("G", (768, 256), ("core", "x", "z1", "z2", "y"), (), ((10, 11), (11, 12), (12, 15), (15, 19), (19, 24))),
    "G21": ("G", (1024, 512), ("core", "x", "yr", "z1", "z2", "yg"), (), ((10, 12), (12, 17), (17, 23), (23, 26), (26, 28), (28, 30))),
    "G30": ("G", (1536, 640), ("core", "x", "z1", ("z2", "y")), (), ((12, 16), (16, 21), (21, 27), (27, 32))),
    "G31": ("G", (2176, 384), ("core", "z1", "x", "z2", "y"), (), ((12, 14), (14, 24), (24, 25), (25, 29), (29, 31))),
}
BLOCK = ("z2", "z1", "x", "core")


class Part:
    def __init__(self, hop, shape, dims, cols=None):
        self.hops = hops = hop if isinstance(hop, tuple) else (hop,)
        self.groups = [(h,) for h in hops] + ([hops] if len(hops) > 1 else [])
        self.dims = dims
        self.cols = cols or (0, shape[-1])
        self.shape = shape = tuple(shape[:-1]) + (self.cols[1],)
        for h in hops:
            if h in dims:
                at = dims.index(h)
                shape, dims = shape[:at] + shape[at + 1 :], dims[:at] + dims[at + 1 :]
            elif h != "y":
                shape = shape[:-1] + (shape[-1] // 2 if h == "yr" else 2 * shape[-1],)
        self.after, self.left = shape, dims
        self.came = self.shape if hops == ("yg",) else shape

    def share(self, at):
        _, c, x, z, sp = at
        first, wide = self.cols
        index = [slice(None)] * (len(self.shape) - 1) + [pl.ds(first, wide)]
        for h in self.hops:
            if h in self.dims:
                index[self.dims.index(h)] = {"core": c, "x": x, "z1": z % 2, "z2": z // 2}[h]
            elif h == "yr":
                half = wide // 2
                index[-1] = pl.ds(pl.multiple_of(first + sp * half, 128), half)
        return tuple(index)

    def copies(self, src, held, made, came, send, recv, local, at):
        out = [
            remote(src.at[self.share(flipped(at, g))], came[i], send.at[i], recv.at[i], g, at)
            for i, g in enumerate(self.groups)
        ]
        if not held:
            out.append(pltpu.make_async_copy(src.at[self.share(at)], made, local))
        return out

    def add(self, src, held, made, came, at):
        if self.hops == ("yg",):
            wide, sp = self.shape[-1], at[4]
            lead = (slice(None),) * (len(self.shape) - 1)
            made[lead + (pl.ds(pl.multiple_of(sp * wide, 128), wide),)] = src[self.share(at)]
            made[lead + (pl.ds(pl.multiple_of((1 - sp) * wide, 128), wide),)] = came[0][...]
        elif len(came) > 1:
            mine = src[self.share(at)] if held else made[...]
            one, two, three = (c[...].astype(F32) for c in came)
            made[...] = ((mine.astype(F32) + one) + (two + three)).astype(BF16)
        elif held:
            made[...] = src[self.share(at)] + came[0][...]
        else:
            made[...] += came[0][...]


class Flow:
    def __init__(self, array, shape, hops, dims=BLOCK, cols=None):
        self.array, self.shape, self.dims, self.cols = array, tuple(shape), dims, cols
        self.hops = list(hops)

    def step(self):
        part = Part(self.hops.pop(0), self.shape, self.dims, self.cols)
        self.shape, self.dims, self.cols = part.after, part.left, None
        return part


class Window:
    def __init__(self, start, stop, joint):
        self.start, self.stop, self.joint = start, stop, joint
        self.parts, self.sources, self.keeps = [], [], []


class Joint:
    def __init__(self):
        self.window = None


def plan(schedule):
    windows, arrays, latest = [], [], {}
    for n, (flows, start, stop, *joint) in enumerate(schedule):
        window = Window(start, stop, bool(joint))
        if joint:
            joint[0].window = n
        for i, flow in enumerate(flows):
            if flow in latest:
                source = ("part",) + latest[flow]
                before = windows[latest[flow][0]]
                before.keeps[latest[flow][1]] = False
            elif isinstance(flow.array, Joint):
                source = ("joint", flow.array.window)
            elif isinstance(flow.array, tuple):
                source = flow.array
            else:
                known = [k for k, a in enumerate(arrays) if a is flow.array]
                if not known:
                    arrays.append(flow.array)
                source = ("in", known[0] if known else len(arrays) - 1)
            window.parts.append(flow.step())
            window.sources.append(source)
            window.keeps.append(not joint)
            if not joint:
                latest[flow] = (n, i)
        windows.append(window)
    return windows, arrays, latest


def carrying(body, own, windows, arrays, grid, also, finale):
    ins, outs, held = own

    def kernel(*refs):
        refs = list(refs)

        def take(n):
            got = refs[:n]
            del refs[:n]
            return got

        my_in, arr = take(ins), take(arrays)
        my_out = take(outs)
        given = [[take(1)[0] if k else None for k in w.keeps] for w in windows]
        my_held = take(held)
        made, came, joints = [], [], []
        for w, g in zip(windows, given):
            if w.joint:
                joint, col, views = take(1)[0], 0, []
                for q in w.parts:
                    views.append(joint.at[(slice(None),) * (len(q.after) - 1) + (pl.ds(col, q.after[-1]),)])
                    col += q.after[-1]
                joints.append(joint)
                made.append(views)
            else:
                joints.append(None)
                made.append([ref if ref is not None else take(1)[0] for ref in g])
            came.append([take(len(q.groups)) for q in w.parts])
        mine = my_in + my_out + my_held
        step = pl.program_id(0)
        groups = [g for w in windows for q in w.parts for g in q.groups] + list(also)
        if groups:
            here = place()
            pl.when(step == 0)(lambda: greet(groups, here))
        if windows:
            send, recv, local = refs
        copies, sources, base = [], [], 0
        for w, m, c in zip(windows, made, came):
            now, froms = [], []
            for i, q in enumerate(w.parts):
                kind = w.sources[i]
                if kind[0] == "in":
                    src = arr[kind[1]]
                elif kind[0] == "ref":
                    src = mine[kind[1]]
                elif kind[0] == "joint":
                    src = joints[kind[1]]
                else:
                    src = made[kind[1]][kind[2]]
                held_here = kind[0] != "in"
                froms.append((src, held_here))
                now += q.copies(
                    src, held_here, m[i], c[i], send.at[base], recv.at[base], local.at[base], here
                )
                base += 1
            copies.append(now)
            sources.append(froms)

        def phase(number):
            for n, w in enumerate(windows):
                if w.stop == number:
                    for copy in copies[n]:
                        copy.wait()
                    for q, (src, held_here), m, c in zip(w.parts, sources[n], made[n], came[n]):
                        q.add(src, held_here, m, c, here)
            for n, w in enumerate(windows):
                if w.start == number:
                    for copy in copies[n]:
                        copy.start()

        used = sorted({w.start for w in windows} | {w.stop for w in windows})
        for number in used:
            if number < grid:
                pl.when(step == number)(functools.partial(phase, number))
        body(*mine)
        for number in used:
            if number >= grid:
                pl.when(step == grid - 1)(functools.partial(phase, number))
        if finale:
            pl.when(step == grid - 1)(lambda: finale(*mine))

    return kernel


def run(
    body, name, grid, ins, in_specs, outs, out_specs, held=(), schedule=(), collective=None,
    flops=0, moved=0, also=(), finale=None,
):
    in_specs, outs, out_specs, held = list(in_specs), list(outs), list(out_specs), list(held)
    windows, arrays, latest = plan(schedule)
    own = len(outs)
    kernel = carrying(body, (len(ins), own, len(held)), windows, len(arrays), grid, also, finale)
    in_specs += [pl.BlockSpec(memory_space=pl.ANY)] * len(arrays)
    order, count = [], 0
    for n, w in enumerate(windows):
        if w.joint:
            shape = w.parts[0].after[:-1] + (sum(q.after[-1] for q in w.parts),)
            held.append(pltpu.VMEM(shape, BF16))
        for i, (q, k) in enumerate(zip(w.parts, w.keeps)):
            if w.joint:
                continue
            if k:
                outs.append(jax.ShapeDtypeStruct(q.after, BF16))
                out_specs.append(whole(q.after))
                order.append((n, i))
            else:
                held.append(pltpu.VMEM(q.after, BF16))
        held += [pltpu.VMEM(q.came, BF16) for q in w.parts for _ in q.groups]
        count += len(w.parts)
    if windows:
        held += [pltpu.SemaphoreType.DMA((count, 3))] * 2 + [pltpu.SemaphoreType.DMA((count,))]
    results = pl.pallas_call(
        kernel,
        grid=(grid,),
        in_specs=in_specs,
        out_specs=out_specs,
        out_shape=outs,
        scratch_shapes=held,
        compiler_params=params(collective if windows or also else None),
        cost_estimate=cost(flops, moved),
        name=name,
    )(*ins, *arrays)
    for flow, where in latest.items():
        flow.array = results[own + order.index(where)]
    return results[:own]


def head_masks(dtype):
    lane = lax.broadcasted_iota(jnp.int32, (1, PAIR), 1)
    low = jnp.where(lane < HD, 1.0, 0.0)
    return low.astype(dtype), (1.0 - low).astype(dtype)


def query_code(code):
    lane = lax.broadcasted_iota(jnp.int32, code.shape, 1)
    return jnp.where(lane < 4, (code.astype(F32) - 1.0) * FAR, 0.0).astype(BF16)


def softmax_over(keys, values_t, q, diagonal=0):
    s = nt(keys, q)
    if diagonal:
        low, high = s[:-diagonal], s[-diagonal:]
        row = lax.broadcasted_iota(jnp.int32, high.shape, 0)
        col = lax.broadcasted_iota(jnp.int32, high.shape, 1)
        high = jnp.where(row <= col, high, -FAR)
        s = jnp.concatenate([low, high], axis=0) if low.shape[0] else high
    peak = jnp.max(s, axis=0, keepdims=True)
    e = jnp.exp(s - peak)
    norm = jnp.sum(e, axis=0, keepdims=True)
    return nn(values_t, e.astype(BF16)) / norm, peak + jnp.log(norm)


def pair_spec(rows, offset):
    return pl.BlockSpec((rows, PAIR), lambda p: (0, p + offset))


def whole(shape):
    return pl.BlockSpec(shape, lambda *_: (0,) * len(shape))


def delta_rows(g, o):
    prod = g.astype(F32) * o.astype(F32)
    upper = prod.astype(BF16)
    lower = (prod - upper.astype(F32)).astype(BF16)
    row = lax.broadcasted_iota(jnp.int32, (8, PAIR), 0)
    lane = lax.broadcasted_iota(jnp.int32, (8, PAIR), 1)
    pick = jnp.where(row == lane // HD, 1.0, 0.0).astype(BF16)
    return nt(pick, upper) + nt(pick, lower)


def back_piece(keys, values, q, g, lse, delta, causal):
    s = nt(keys, q)
    if causal:
        row = lax.broadcasted_iota(jnp.int32, s.shape, 0)
        col = lax.broadcasted_iota(jnp.int32, s.shape, 1)
        s = jnp.where(row <= col, s, -FAR)
    p = jnp.exp(s - lse)
    ds = p * (nt(values, g) - delta)
    return p.astype(BF16), ds.astype(BF16)


def cross_backward_kernel(
    size, pairs, q_ref, k_ref, v_ref, ko_ref, vo_ref, g_ref, o_ref, lse_ref, t_ref, own_ref, oth_ref,
    m_ref, mo_ref, wk_ref, wv_ref, gco_ref, dh2_ref, h1_ref, ctx_ref, wcq_ref, wso_ref, g1_ref, s1_ref,
    dm_ref, dmo_ref, gb_ref, dh1_ref, dsc_ref, late_ref, small_ref, grad_ref,
    dmo_acc, mt_ref, mot_ref, dcq_ref,
):
    step = pl.program_id(0)
    rows, width = m_ref.shape
    lead = (slice(None),) * (len(grad_ref.shape) - 1)

    def put(ref, col, grad):
        to = pl.ds(pl.multiple_of(col, PAIR), grad.shape[1])
        ref[lead + (to,)] = grad.astype(BF16).reshape(ref.shape[:-1] + (grad.shape[1],))

    @pl.when(step == 0)
    def _():
        mt_ref[...] = jnp.transpose(m_ref[...])
        mot_ref[...] = jnp.transpose(mo_ref[...])
        put(grad_ref, 0, gco_ref[...])

    @pl.when(step < pairs)
    def _():
        count = rows // size
        halves = [(k_ref, v_ref, own_ref, mt_ref, dm_ref), (ko_ref, vo_ref, oth_ref, mot_ref, dmo_acc)]
        cols = pl.ds(pl.multiple_of(step * PAIR, PAIR), PAIR)
        dq = [[0.0, 0.0] for _ in range(count)]
        gk = gv = gb = 0.0
        for kr, vr, code, mem, acc in halves:
            keys = jnp.concatenate([kr[...], code[...]], axis=1)
            values = vr[...]
            turned = jnp.transpose(kr[...])
            dk = dv = 0.0
            for block, head, qm, gm, q, lse, delta in backward_pieces(size, q_ref, g_ref, o_ref, lse_ref, t_ref):
                p, ds = back_piece(keys, values, q, gm, lse, delta, False)
                dk = dk + nn(ds, qm)
                dv = dv + nn(p, gm)
                dq[block][head] = dq[block][head] + nn(turned[head * HD : (head + 1) * HD], ds)
            both = jnp.concatenate([dk.astype(BF16), dv.astype(BF16)], axis=1)
            grad = nn(mem[...], both)
            gk, gv = gk + grad[:, :PAIR], gv + grad[:, PAIR:]
            gb = gb + total(both[:, PAIR:])
            dm = nt(both, jnp.concatenate([wk_ref[...], wv_ref[...]], axis=1))

            @pl.when(step == 0)
            def _():
                acc[...] = dm

            @pl.when(step > 0)
            def _():
                acc[...] += dm

        for block in range(count):
            dcq_ref[block * size : (block + 1) * size, cols] = upright(dq[block]).astype(BF16)
        put(grad_ref, width + step * PAIR, gk)
        put(grad_ref, 2 * width + step * PAIR, gv)
        gb_ref[:, cols] = gb

    @pl.when(step == pairs)
    def _():
        dmo_ref[...] = dmo_acc[...].astype(BF16)
        gain = line(g1_ref)
        n1, r1 = normed(h1_ref[...])
        a1b = (n1 * gain + line(s1_ref)).astype(BF16)
        dcq = dcq_ref[...]
        d1 = dh2_ref[...] + nt(dcq, wcq_ref[...])
        dh1 = norm_back(d1, n1, r1, gain)
        dh1_ref[...] = dh1
        dso = dh1.astype(BF16)
        dsc_ref[...] = nt(dso, wso_ref[...]).astype(BF16)
        put(late_ref, 0, tn(a1b, dcq))
        put(late_ref, width, tn(ctx_ref[...], dso))
        small_ref[0:1] = total(dcq)
        small_ref[1:2] = total(d1 * n1)
        small_ref[2:3] = total(d1)
        small_ref[3:4] = total(dso)
        small_ref[4:8] = jnp.zeros((4, width), F32)


MIDDLE = 30


def cross_backward(block, cq, kv, kvo, g, o, lse, t, own, oth, m, mo, w, gco, dh2, h1, ctx, wcq, wso, gain, shift, schedule):
    rows, width = cq.shape
    pairs = width // PAIR

    def pair_of(size, offset):
        return pl.BlockSpec((size, PAIR), lambda s: (0, jnp.minimum(s, pairs - 1) + offset))

    flat, square = whole((rows, width)), whole((width, width))
    outs = [
        jax.ShapeDtypeStruct((rows, width), F32),
        jax.ShapeDtypeStruct((rows, width), BF16),
        jax.ShapeDtypeStruct((1, width), F32),
        jax.ShapeDtypeStruct((rows, width), F32),
        jax.ShapeDtypeStruct((rows, width), BF16),
        jax.ShapeDtypeStruct(block + (2 * width,), BF16),
        jax.ShapeDtypeStruct((8, width), F32),
    ]
    specs = [flat, flat, whole((1, width)), flat, flat, whole(block + (2 * width,)), whole((8, width))]
    held = []
    if schedule:
        held.append(pltpu.VMEM(block + (3 * width,), BF16))
    else:
        outs.append(jax.ShapeDtypeStruct(block + (3 * width,), BF16))
        specs.append(whole(block + (3 * width,)))
    held += [
        pltpu.VMEM((rows, width), F32),
        pltpu.VMEM((width, rows), BF16),
        pltpu.VMEM((width, rows), BF16),
        pltpu.VMEM((rows, width), BF16),
    ]
    return run(
        functools.partial(cross_backward_kernel, 256, pairs), "cross_backward", pairs + 1,
        (cq, kv, kv, kvo, kvo, g, o, lse, t, own, oth, m, mo, w, w, gco, dh2, h1, ctx, wcq, wso, gain, shift),
        [
            pair_of(rows, 0), pair_of(rows, 0), pair_of(rows, pairs), pair_of(rows, 0), pair_of(rows, pairs),
            pair_of(rows, 0), pair_of(rows, 0),
            pl.BlockSpec((8, rows), lambda s: (jnp.minimum(s, pairs - 1), 0)),
            whole((rows, 128)), whole((rows, 128)), whole((rows, 128)), flat, flat,
            pair_of(width, 0), pair_of(width, pairs),
            square, flat, flat, flat, square, square, whole(gain.shape), whole(shift.shape),
        ],
        outs, specs, held, schedule, 3,
        64 * rows * rows * width + 24 * rows * width * width, 40 * rows * width,
    )


def upright(heads):
    return jnp.transpose(jnp.concatenate(heads, axis=0) * HD**-0.5)


def backward_pieces(size, q_ref, g_ref, o_ref, lse_ref, own_ref):
    masks = head_masks(BF16)
    scale = BF16(HD**-0.5)
    qcode = query_code(own_ref[...])
    delta = delta_rows(g_ref[...], o_ref[...])
    for block in range(q_ref.shape[0] // size):
        at = slice(block * size, (block + 1) * size)
        for head, mask in enumerate(masks):
            qm = q_ref[at] * (mask * scale)
            gm = g_ref[at] * mask
            q = jnp.concatenate([qm, qcode[at]], axis=1)
            yield block, head, qm, gm, q, lse_ref[head : head + 1, at], delta[head : head + 1, at]


def self_backward_kernel(
    size, q_ref, k_ref, v_ref, ko_ref, vo_ref, g_ref, o_ref, lse_ref, own_ref, oth_ref,
    x_ref, xo_ref, wq_ref, wk_ref, wv_ref, dh1_ref, sa_ref, sb_ref, sc_ref, sd_ref, dmo_ref,
    dx_ref, dmi_ref, grad_ref,
    dq_acc, dx_acc, dxo_acc, dkv_acc, xt_ref, xot_ref, dxo_ref, came_ref, memory_ref, turn_ref, send_ref, recv_ref,
):
    step = pl.program_id(0)
    sp = lax.axis_index("sp")
    second = sp == 1
    rows, width = x_ref.shape
    pairs = width // PAIR
    pair = lax.rem(step, pairs)
    cols = pl.ds(pl.multiple_of(pair * PAIR, PAIR), PAIR)
    count = rows // size
    over = remote(dxo_ref, came_ref, send_ref.at[0], recv_ref.at[0], ("y",))

    def pieces():
        return backward_pieces(size, q_ref, g_ref, o_ref, lse_ref, own_ref)

    @pl.when(step == 0)
    def _():
        remote(dmo_ref, memory_ref, send_ref.at[1], recv_ref.at[1], ("y",)).start()
        xt_ref[...] = jnp.transpose(x_ref[...])
        turn_ref[...] = jnp.zeros(turn_ref.shape, F32)
        turn_ref[0:8] = sa_ref[...]
        turn_ref[8:16] = sb_ref[...]
        turn_ref[16:17] = sc_ref[...]
        turn_ref[17:21] = sd_ref[...]

    @pl.when(jnp.logical_and(step == 0, second))
    def _():
        xot_ref[...] = jnp.transpose(xo_ref[...])

    @pl.when(jnp.logical_and(step == 0, jnp.logical_not(second)))
    def _():
        dq_acc[...] = jnp.zeros(dq_acc.shape, F32)

    @pl.when(jnp.logical_and(step < pairs, second))
    def _():
        keys = jnp.concatenate([ko_ref[...], oth_ref[...]], axis=1)
        values = vo_ref[...]
        turned = jnp.transpose(ko_ref[...])
        dk = dv = 0.0
        for block, head, qm, gm, q, lse, delta in pieces():
            p, ds = back_piece(keys, values, q, gm, lse, delta, False)
            dk = dk + nn(ds, qm)
            dv = dv + nn(p, gm)
            of_head = slice(head * HD, (head + 1) * HD)
            dq_acc[pair, of_head, block * size : (block + 1) * size] = nn(turned[of_head], ds)
        both = jnp.concatenate([dk.astype(BF16), dv.astype(BF16)], axis=1)
        dkv_acc[pair] = both
        dxo = nt(both, jnp.concatenate([wk_ref[...], wv_ref[...]], axis=1))

        @pl.when(step == 0)
        def _():
            dxo_acc[...] = dxo

        @pl.when(step > 0)
        def _():
            dxo_acc[...] += dxo

    @pl.when(jnp.logical_and(step == pairs - 1, second))
    def _():
        dxo_ref[...] = dxo_acc[...].astype(BF16)
        over.start()

    @pl.when(step >= pairs)
    def _():
        turned = jnp.transpose(k_ref[...])
        dq = [[0.0, 0.0] for _ in range(count)]
        dk, dv = [0.0] * count, [0.0] * count
        for block, head, qm, gm, q, lse, delta in pieces():
            for part in range(block + 1):
                of = slice(part * size, (part + 1) * size)
                keys = jnp.concatenate([k_ref[of], own_ref[of]], axis=1)
                p, ds = back_piece(keys, v_ref[of], q, gm, lse, delta, part == block)
                dk[part] = dk[part] + nn(ds, qm)
                dv[part] = dv[part] + nn(p, gm)
                dq[block][head] = dq[block][head] + nn(turned[head * HD : (head + 1) * HD, of], ds)
        dk, dv = (jnp.concatenate(a, axis=0) for a in (dk, dv))
        before = dq_acc[pair]
        dq = jnp.concatenate(
            [
                upright(
                    [
                        part + before[head * HD : (head + 1) * HD, block * size : (block + 1) * size]
                        for head, part in enumerate(parts)
                    ]
                )
                for block, parts in enumerate(dq)
            ],
            axis=0,
        )
        dqk = jnp.concatenate([dq.astype(BF16), dk.astype(BF16)], axis=1)
        dv = dv.astype(BF16)
        grad_qk = nn(xt_ref[...], dqk)
        grad_v = nn(xt_ref[...], dv)
        shape = grad_ref.shape[:-1] + (PAIR,)
        lead = (slice(None),) * (len(shape) - 1)

        def put(n, grad):
            col = pair // 2 * 6 + 2 * n + pair % 2
            to = pl.ds(pl.multiple_of(col * PAIR, PAIR), PAIR)
            grad_ref[lead + (to,)] = grad.astype(BF16).reshape(shape)

        put(0, grad_qk[:, :PAIR])
        turn_ref[21:22, cols] = total(dqk[:, :PAIR])

        @pl.when(second)
        def _():
            grad_o = nn(xot_ref[...], dkv_acc[pair])
            put(1, grad_qk[:, PAIR:] + grad_o[:, :PAIR])
            put(2, grad_v + grad_o[:, PAIR:])
            turn_ref[22:23, cols] = total(dv) + total(dkv_acc[pair, :, PAIR:])

        @pl.when(jnp.logical_not(second))
        def _():
            put(1, grad_qk[:, PAIR:])
            put(2, grad_v)
            turn_ref[22:23, cols] = total(dv)

        dx = nt(dqk, jnp.concatenate([wq_ref[...], wk_ref[...]], axis=1)) + nt(dv, wv_ref[...])

        @pl.when(step == pairs)
        def _():
            dx_acc[...] = dh1_ref[...] + dx

        @pl.when(step > pairs)
        def _():
            dx_acc[...] += dx

    @pl.when(step == 2 * pairs - 1)
    def _():
        shape = grad_ref.shape[:-1] + (2 * PAIR,)
        lead = (slice(None),) * (len(shape) - 1)
        col = 3 * width
        grad_ref[lead + (slice(col, col + 2 * PAIR),)] = jnp.transpose(turn_ref[...]).astype(BF16).reshape(shape)


def self_backward_finale(*refs):
    dmo_ref, dx_ref, dmi_ref = refs[20:23]
    dx_acc, dxo_ref, came_ref, memory_ref, send_ref, recv_ref = (refs[i] for i in (25, 30, 31, 32, 34, 35))
    remote(dmo_ref, memory_ref, send_ref.at[1], recv_ref.at[1], ("y",)).wait()
    dmi_ref[...] = memory_ref[...]
    over = remote(dxo_ref, came_ref, send_ref.at[0], recv_ref.at[0], ("y",))

    @pl.when(lax.axis_index("sp") == 0)
    def _():
        over.wait_recv()
        dx_ref[...] = (dx_acc[...] + came_ref[...].astype(F32)).astype(BF16)

    @pl.when(lax.axis_index("sp") == 1)
    def _():
        over.wait_send()
        dx_ref[...] = dx_acc[...].astype(BF16)


GRADS = 23


def self_backward(block, qkv, kvo, g, o, lse, own, oth, x, xo, w, dh1, small, dmo, schedule):
    rows, width = x.shape
    pairs = width // PAIR

    def pair_of(offset):
        return pl.BlockSpec((rows, PAIR), lambda s: (0, lax.rem(s, pairs) + offset))

    def weight(offset):
        return pl.BlockSpec((width, PAIR), lambda s: (0, lax.rem(s, pairs) + offset))

    made = block + (3 * width + 2 * PAIR,)
    outs = [jax.ShapeDtypeStruct((rows, width), BF16)] * 2
    specs = [whole((rows, width))] * 2
    held = []
    if schedule:
        held += [pltpu.VMEM(made, BF16)]
    else:
        outs += [jax.ShapeDtypeStruct(made, BF16)]
        specs += [whole(made)]
    held += [
        pltpu.VMEM((pairs, PAIR, rows), F32),
        pltpu.VMEM((rows, width), F32),
        pltpu.VMEM((rows, width), F32),
        pltpu.VMEM((pairs, rows, 2 * PAIR), BF16),
        pltpu.VMEM((width, rows), BF16),
        pltpu.VMEM((width, rows), BF16),
        pltpu.VMEM((rows, width), BF16),
        pltpu.VMEM((rows, width), BF16),
        pltpu.VMEM((rows, width), BF16),
        pltpu.VMEM((2 * PAIR, width), F32),
        pltpu.SemaphoreType.DMA((2,)),
        pltpu.SemaphoreType.DMA((2,)),
    ]
    return run(
        functools.partial(self_backward_kernel, 256), "self_backward", 2 * pairs,
        (qkv, qkv, qkv, kvo, kvo, g, o, lse, own, oth, x, xo, w, w, w, dh1) + tuple(small) + (dmo,),
        [
            pair_of(0),
            pair_of(pairs),
            pair_of(2 * pairs),
            pair_of(0),
            pair_of(pairs),
            pair_of(0),
            pair_of(0),
            pl.BlockSpec((8, rows), lambda s: (lax.rem(s, pairs), 0)),
            whole((rows, 128)),
            whole((rows, 128)),
            whole((rows, width)),
            whole((rows, width)),
            weight(0),
            weight(pairs),
            weight(2 * pairs),
            whole((rows, width)),
        ] + [whole(a.shape) for a in small] + [pl.BlockSpec(memory_space=pl.ANY)],
        outs, specs, held, schedule, 5,
        48 * rows * rows * width + 20 * rows * width * width, 12 * width * width + 40 * rows * width,
        (("y",),), self_backward_finale,
    )


def code_of(docs_ref):
    row = lax.broadcasted_iota(jnp.int32, (PAIR, docs_ref.shape[1]), 0)
    return jnp.transpose(jnp.where(docs_ref[...] == row, 1.0, 0.0)).astype(BF16)


def line(ref):
    return ref[...].astype(F32)[None, :]


def front_kernel(
    size, x_hbm, m_hbm, td_ref, md_ref, wx_hbm, wm_hbm, wo_hbm, wq_hbm,
    bq_ref, bv_ref, bcv_ref, bso_ref, g_ref, s_ref, bcq_ref,
    qkv_out, mkv_out, kvo_out, mkvo_out, cq_out, ctx_out, cc_out, h_out, xo_out, mo_out,
    lse_ref, clse_ref, tt_ref, mt_ref, to_ref, mo_ref,
    x_ref, m_ref, wx_ref, wm_ref, wo_ref, wq_ref, xc_ref, mc_ref, tdc_ref, mdc_ref,
    qkv_ref, mkv_ref, kvo_ref, mkvo_ref, cq_ref, ctx_ref, cc_ref, h_ref, acc_ref,
    load_ref, store_ref, send_ref, recv_ref,
):
    rows, width = x_ref.shape
    pairs = width // PAIR
    second = lax.axis_index("sp") == 1
    first = jnp.logical_not(second)
    masks = head_masks(BF16)
    scale = BF16(HD**-0.5)
    loads = [
        pltpu.make_async_copy(src, dst, load_ref.at[i])
        for i, (src, dst) in enumerate(
            ((x_hbm, x_ref), (wx_hbm, wx_ref), (m_hbm, m_ref), (wm_hbm, wm_ref), (wo_hbm, wo_ref), (wq_hbm, wq_ref))
        )
    ]
    give = [
        pltpu.make_async_copy(src, dst, store_ref.at[i])
        for i, (src, dst) in enumerate(
            (
                (qkv_ref, qkv_out), (mkv_ref, mkv_out), (mkvo_ref, mkvo_out), (cq_ref, cq_out), (ctx_ref, ctx_out),
                (cc_ref, cc_out), (h_ref, h_out), (mc_ref, mo_out), (kvo_ref, kvo_out), (xc_ref, xo_out),
            )
        )
    ]
    x_over = remote(x_hbm, xc_ref, send_ref.at[0], recv_ref.at[0], ("y",))
    m_over = remote(m_hbm, mc_ref, send_ref.at[1], recv_ref.at[1], ("y",))
    docs = [
        remote(td_ref, tdc_ref, send_ref.at[2], recv_ref.at[2], ("y",)),
        remote(md_ref, mdc_ref, send_ref.at[3], recv_ref.at[3], ("y",)),
    ]
    for copy in loads:
        copy.start()
    greet([("y",)])
    for copy in docs:
        copy.start()
    pl.when(first)(x_over.start)
    pl.when(second)(m_over.start)

    def columns(offset, pair):
        return pl.ds(pl.multiple_of(offset + pair * PAIR, PAIR), PAIR)

    def heads(source, offset, pair, code, block):
        at = slice(block * size, (block + 1) * size)
        q = source[at, columns(offset, pair)]
        return [jnp.concatenate([q * (mask * scale), code[at]], axis=1) for mask in masks]

    def keep(block, pair, outs, lses, lse_out, out):
        at = slice(block * size, (block + 1) * size)
        mixed = jnp.concatenate(outs, axis=0)
        acc_ref[pair, :, at] = mixed
        out[at, columns(0, pair)] = jnp.transpose(mixed).astype(BF16)
        row = lax.broadcasted_iota(jnp.int32, (8, size), 0)
        lse_out[pl.ds(pl.multiple_of(pair * 8, 8), 8), at] = jnp.where(row == 0, lses[0], lses[1])

    def begin(block, pair, results, lse_out, out):
        keep(block, pair, [r for r, _ in results], [lse for _, lse in results], lse_out, out)

    def merge(block, pair, results, lse_out, out):
        at = slice(block * size, (block + 1) * size)
        stats = lse_out[pl.ds(pl.multiple_of(pair * 8, 8), 8), at]
        outs, lses = [], []
        for head, (r, lse) in enumerate(results):
            before = acc_ref[pair, head * HD : (head + 1) * HD, at]
            old = stats[head : head + 1]
            peak = jnp.maximum(old, lse)
            both = peak + jnp.log(jnp.exp(old - peak) + jnp.exp(lse - peak))
            outs.append(before * jnp.exp(old - both) + r * jnp.exp(lse - both))
            lses.append(both)
        keep(block, pair, outs, lses, lse_out, out)

    def halves(values):
        turned = jnp.transpose(values)
        return turned[:HD], turned[HD:]

    to_ref[...] = code_of(td_ref)
    mo_ref[...] = code_of(md_ref)
    loads[0].wait()
    loads[1].wait()
    for n, bias in enumerate((line(bq_ref), 0.0, line(bv_ref))):
        cols = slice(n * width, (n + 1) * width)
        qkv_ref[:, cols] = (nn(x_ref[...], wx_ref[:, cols]) + bias).astype(BF16)
    give[0].start()
    loads[2].wait()
    loads[3].wait()
    for n, bias in enumerate((0.0, line(bcv_ref))):
        cols = slice(n * width, (n + 1) * width)
        mkv_ref[:, cols] = (nn(m_ref[...], wm_ref[:, cols]) + bias).astype(BF16)
    give[1].start()

    @pl.loop(0, pairs)
    def _(pair):
        code = query_code(to_ref[...])
        keys = jnp.concatenate([qkv_ref[:, columns(width, pair)], to_ref[...]], axis=1)
        values = halves(qkv_ref[:, columns(2 * width, pair)])
        for block in range(rows // size):
            end = (block + 1) * size
            results = [
                softmax_over(keys[:end], v[:, :end], q, size)
                for q, v in zip(heads(qkv_ref, 0, pair, code, block), values)
            ]
            begin(block, pair, results, lse_ref, ctx_ref)

    for copy in docs:
        copy.wait()
    tt_ref[...] = code_of(tdc_ref)
    mt_ref[...] = code_of(mdc_ref)

    @pl.when(first)
    def _():
        x_over.wait_send()
        m_over.start()

    @pl.when(second)
    def _():
        x_over.wait_recv()
        give[9].start()
        for n, bias in enumerate((0.0, line(bv_ref))):
            cols = slice(n * width, (n + 1) * width)
            from_cols = slice((n + 1) * width, (n + 2) * width)
            kvo_ref[:, cols] = (nn(xc_ref[...], wx_ref[:, from_cols]) + bias).astype(BF16)
        give[8].start()

        @pl.loop(0, pairs)
        def _(pair):
            code = query_code(to_ref[...])
            keys = jnp.concatenate([kvo_ref[:, columns(0, pair)], tt_ref[...]], axis=1)
            values = halves(kvo_ref[:, columns(width, pair)])
            for block in range(rows // size):
                results = [
                    softmax_over(keys, v, q) for q, v in zip(heads(qkv_ref, 0, pair, code, block), values)
                ]
                merge(block, pair, results, lse_ref, ctx_ref)

    give[4].start()
    loads[4].wait()
    loads[5].wait()
    h = x_ref[...].astype(F32) + nn(ctx_ref[...], wo_ref[...]) + line(bso_ref)
    h_ref[...] = h
    n, _ = normed(h)
    a = (n * line(g_ref) + line(s_ref)).astype(BF16)
    cq_ref[...] = (nn(a, wq_ref[...]) + line(bcq_ref)).astype(BF16)
    give[6].start()
    give[3].start()

    def cross(keys_ref, key_code, finish):
        @pl.loop(0, pairs)
        def _(pair):
            code = query_code(to_ref[...])
            keys = jnp.concatenate([keys_ref[:, columns(0, pair)], key_code[...]], axis=1)
            values = halves(keys_ref[:, columns(width, pair)])
            for block in range(rows // size):
                results = [
                    softmax_over(keys, v, q) for q, v in zip(heads(cq_ref, 0, pair, code, block), values)
                ]
                finish(block, pair, results, clse_ref, cc_ref)

    cross(mkv_ref, mo_ref, begin)
    m_over.wait()
    give[7].start()
    for n, bias in enumerate((0.0, line(bcv_ref))):
        cols = slice(n * width, (n + 1) * width)
        mkvo_ref[:, cols] = (nn(mc_ref[...], wm_ref[:, cols]) + bias).astype(BF16)
    give[2].start()
    cross(mkvo_ref, mt_ref, merge)
    give[5].start()
    for copy in give[:8]:
        copy.wait()

    @pl.when(second)
    def _():
        give[8].wait()
        give[9].wait()


def front(x, mem, td, md, wx, wm, wo, wq, vectors):
    rows, width = x.shape
    pairs = width // PAIR

    def flat(n):
        return jax.ShapeDtypeStruct((rows, n * width), BF16)

    stats = jax.ShapeDtypeStruct((8 * pairs, rows), F32)
    code = jax.ShapeDtypeStruct((rows, PAIR), BF16)
    far = pl.BlockSpec(memory_space=pl.ANY)
    near = pl.BlockSpec(memory_space=pltpu.VMEM)
    tall = jax.ShapeDtypeStruct((rows, width), F32)
    held = [flat(3), flat(2), flat(2), flat(2), flat(1), flat(1), flat(1), tall]
    return pl.pallas_call(
        functools.partial(front_kernel, 256),
        in_specs=[far, far, near, near, far, far, far, far] + [near] * len(vectors),
        out_specs=[far] * 10 + [near] * 6,
        out_shape=[flat(3), flat(2), flat(2), flat(2), flat(1), flat(1), flat(1), tall, flat(1), flat(1)]
        + [stats, stats, code, code, code, code],
        scratch_shapes=[pltpu.VMEM(a.shape, a.dtype) for a in (flat(1), flat(1))]
        + [pltpu.VMEM(w.shape, BF16) for w in (wx, wm, wo, wq)]
        + [pltpu.VMEM((rows, width), BF16)] * 2
        + [pltpu.VMEM((1, rows), jnp.int32)] * 2
        + [pltpu.VMEM(a.shape, a.dtype) for a in held]
        + [
            pltpu.VMEM((pairs, PAIR, rows), F32),
            pltpu.SemaphoreType.DMA((6,)),
            pltpu.SemaphoreType.DMA((10,)),
            pltpu.SemaphoreType.DMA((4,)),
            pltpu.SemaphoreType.DMA((4,)),
        ],
        compiler_params=params(1),
        cost_estimate=cost(22 * rows * width * width + 36 * rows * rows * width, 60 * rows * width),
        name="front",
    )(x, mem, td, md, wx, wm, wo, wq, *vectors)


def feed_kernel(
    count, comm, h1_ref, cc_ref, ct_ref, wco_ref, wi_ref, wo_ref,
    g1_ref, s1_ref, bco_ref, g2_ref, s2_ref, bfo_ref, g3_ref, s3_ref, bfi_ref, out_ref, dh2_ref, dcc_ref, gco_ref, *refs,
):
    if comm:
        gwi_ref, refs = refs[0], refs[1:]
    else:
        gwi_ref, gwo_ref, refs = refs[0], refs[1], refs[2:]
    small_ref, gib_ref, hid_ref, slope_ref, n2_ref, r2_ref, a2b_ref, acc_ref, df_ref, bias_ref, *refs = refs
    step = pl.program_id(0)
    width = acc_ref.shape[1]

    if comm:
        mi_ref, mo_ref, ci_ref, co_ref, send_ref, recv_ref = refs
        wide = ci_ref.shape[-1]
        here = place()
        c = here[1]

        def chunk_copies(j):
            at = pl.ds(pl.multiple_of(j * width, width), width)
            return [
                remote(mi_ref.at[:, :, at], ci_ref.at[:, :, at], send_ref.at[0, j], recv_ref.at[0, j], ("core",), here),
                remote(mo_ref.at[j], co_ref.at[j], send_ref.at[1, j], recv_ref.at[1, j], ("core",), here),
            ]

    @pl.when(step == 0)
    def _():
        if comm:
            greet([("core",)])
        wide = bfi_ref[...].astype(F32)
        for i in range(count):
            bias_ref[i : i + 1] = wide[None, i * width : (i + 1) * width]
        n1, _ = normed(h1_ref[...])
        a1 = n1 * line(g1_ref) + line(s1_ref)
        h2 = a1 + nn(cc_ref[...], wco_ref[...]) + line(bco_ref)
        n2, r2 = normed(h2)
        n2_ref[...] = n2
        r2_ref[...] = jnp.broadcast_to(r2, r2_ref.shape)
        a2 = n2 * line(g2_ref) + line(s2_ref)
        a2b_ref[...] = a2.astype(BF16)
        acc_ref[...] = a2 + line(bfo_ref)

    @pl.when(step < count)
    def _():
        u = nn(a2b_ref[...], wi_ref[...]) + bias_ref[pl.ds(step, 1)]
        cumul = 0.5 * (1.0 + lax.erf(u * 0.7071067811865476))
        density = jnp.exp(-0.5 * u * u) * 0.3989422804014327
        hid = (u * cumul).astype(BF16)
        hid_ref[step] = hid
        slope_ref[step] = cumul + u * density
        acc_ref[...] += nn(hid, wo_ref[...])

    @pl.when(step == count - 1)
    def _():
        n3, r3 = normed(acc_ref[...])
        gain = line(g3_ref)
        out_ref[...] = (n3 * gain + line(s3_ref)).astype(BF16)
        e = ct_ref[...].astype(F32)
        d3 = norm_back(e, n3, r3, gain)
        df = d3.astype(BF16)
        df_ref[...] = df
        acc_ref[...] = d3
        small_ref[0:1] = total(e * n3)
        small_ref[1:2] = total(e)
        small_ref[2:3] = total(df)

    @pl.when(jnp.logical_and(step >= count, step < 2 * count))
    def _():
        j = step - count
        df = df_ref[...]
        du = (nt(df, wo_ref[...]) * slope_ref[j]).astype(BF16)
        gib_ref[...] = total(du)
        acc_ref[...] += nt(du, wi_ref[...])
        go = tn(hid_ref[j], df).astype(BF16)
        gi = tn(a2b_ref[...], du).astype(BF16)
        if comm:
            at = pl.ds(pl.multiple_of(j * width, width), width)
            eight, narrow = gwi_ref.shape[:2]
            gi = gi.reshape(eight, 2, narrow, width)
            go = go.reshape(2, 2, 4, narrow, width)
            gwi_ref[:, :, at] = jnp.where(c == 0, gi[:, 0], gi[:, 1])
            mi_ref[:, :, at] = jnp.where(c == 0, gi[:, 1], gi[:, 0])
            mo_ref[j] = jnp.where(c == 0, go[:, 1], go[:, 0])
            for i in range(4):
                gwi_ref[pl.ds(2 * j, 2), :, pl.ds(wide + i * width, width)] = jnp.where(c == 0, go[:, 0, i], go[:, 1, i])
            for copy in chunk_copies(j):
                copy.start()
        else:
            gwo_ref[...] = go
            gwi_ref[...] = gi

    @pl.when(step == 2 * count)
    def _():
        d2 = acc_ref[...]
        n2 = n2_ref[...]
        dh2 = norm_back(d2, n2, r2_ref[:, :1], line(g2_ref))
        dh2_ref[...] = dh2
        dco = dh2.astype(BF16)
        dcc_ref[...] = nt(dco, wco_ref[...]).astype(BF16)
        gco_ref[...] = tn(cc_ref[...], dco).astype(BF16)
        small_ref[3:4] = total(d2 * n2)
        small_ref[4:5] = total(d2)
        small_ref[5:6] = total(dco)
        small_ref[6:8] = jnp.zeros((2, d2.shape[1]), F32)

    if comm:

        @pl.when(step > count)
        def _():
            j = step - count - 1
            at = pl.ds(pl.multiple_of(j * width, width), width)
            for copy in chunk_copies(j):
                copy.wait()
            gwi_ref[:, :, at] += ci_ref[:, :, at]
            for i in range(4):
                gwi_ref[pl.ds(2 * j, 2), :, pl.ds(wide + i * width, width)] += co_ref[j, :, i]


def feed(size, comm, h1, cc, ct, wco, wi, wo, vectors):
    rows, width = h1.shape
    wide = wi.shape[1]
    chunk = width
    count = wide // chunk

    def weight(s):
        return jnp.where(s < count, s, jnp.minimum(s - count, count - 1))

    def early(s):
        return jnp.clip(s - count, 0, count - 1)

    flat = whole((rows, width))
    square = whole((width, width))
    scratch = [
        pltpu.VMEM((count, rows, chunk), BF16),
        pltpu.VMEM((count, rows, chunk), F32),
        pltpu.VMEM((rows, width), F32),
        pltpu.VMEM((rows, 128), F32),
        pltpu.VMEM((rows, width), BF16),
        pltpu.VMEM((rows, width), F32),
        pltpu.VMEM((rows, width), BF16),
        pltpu.VMEM((8, width), F32),
    ]
    if comm:
        narrow = width // size
        grad_specs = [whole((size // 2, narrow, 2 * wide))]
        grad_shapes = [(size // 2, narrow, 2 * wide)]
        scratch += [
            pltpu.VMEM((size // 2, narrow, wide), BF16),
            pltpu.VMEM((count, 2, 4, narrow, width), BF16),
            pltpu.VMEM((size // 2, narrow, wide), BF16),
            pltpu.VMEM((count, 2, 4, narrow, width), BF16),
            pltpu.SemaphoreType.DMA((2, count)),
            pltpu.SemaphoreType.DMA((2, count)),
        ]
    else:
        grad_specs = [
            pl.BlockSpec((width, chunk), lambda s: (0, early(s))),
            pl.BlockSpec((chunk, width), lambda s: (early(s), 0)),
        ]
        grad_shapes = [(width, wide), (wide, width)]
    return pl.pallas_call(
        functools.partial(feed_kernel, count, comm),
        grid=(2 * count + 1,),
        in_specs=[
            flat, flat, flat, square,
            pl.BlockSpec((width, chunk), lambda s: (0, weight(s))),
            pl.BlockSpec((chunk, width), lambda s: (weight(s), 0)),
        ]
        + [whole(v.shape) for v in vectors],
        out_specs=[flat, flat, flat, square]
        + grad_specs
        + [whole((8, width)), pl.BlockSpec((1, chunk), lambda s: (0, early(s)))],
        out_shape=[
            jax.ShapeDtypeStruct((rows, width), BF16),
            jax.ShapeDtypeStruct((rows, width), F32),
            jax.ShapeDtypeStruct((rows, width), BF16),
            jax.ShapeDtypeStruct((width, width), BF16),
        ]
        + [jax.ShapeDtypeStruct(a, BF16) for a in grad_shapes]
        + [
            jax.ShapeDtypeStruct((8, width), F32),
            jax.ShapeDtypeStruct((1, wide), F32),
        ],
        scratch_shapes=scratch,
        compiler_params=params(2 if comm else None),
        cost_estimate=cost(
            12 * rows * width * wide + 6 * rows * width * width, 12 * width * wide + 16 * rows * width
        ),
        name="feed",
    )(h1, cc, ct, wco, wi, wo, *vectors)


def outputs_kernel(moves, count, line, *refs):
    pieces, rest = refs[:count], refs[count:]
    out_ref, dx_ref, dm_ref, dmi_ref = rest[:4]
    outs = rest[4:]
    for piece, first, wide, which, row, col in moves:
        ref = pieces[piece]
        outs[which][row : row + ref.shape[0], col : col + wide] = ref[:, first : first + wide].astype(F32)
    turned, result, dx, dm = outs[-4:]
    turned[...] = jnp.transpose(pieces[line[0]][:, line[1] : line[1] + PAIR].astype(F32))
    result[...] = out_ref[...]
    dx[...] = dx_ref[...]
    dm[...] = (dm_ref[...] + dmi_ref[...].astype(F32)).astype(BF16)


def outputs(pieces, moves, line, shapes, out, dx, dm, dmi):
    ins = tuple(pieces) + (out, dx, dm, dmi)
    result = jax.ShapeDtypeStruct(out.shape, BF16)
    return pl.pallas_call(
        functools.partial(outputs_kernel, moves, len(pieces), line),
        out_shape=[jax.ShapeDtypeStruct(a, F32) for a in shapes]
        + [jax.ShapeDtypeStruct((PAIR, pieces[0].shape[0]), F32), result, result, result],
        compiler_params=params(),
        cost_estimate=cost(0, 12 << 20),
        name="outputs",
    )(*ins)


def moved(pieces, targets):
    out = []
    for n, (start, wide) in enumerate(pieces):
        for first, cols, which, row, col in targets:
            low, high = max(start, first), min(start + wide, first + cols)
            if low < high:
                out.append((n, low - start, high - low, which, row, col + low - first))
    return out


def schedule_of(flows, kernel):
    entries = [
        (start, order, name, start, stop)
        for order, name in enumerate(flows)
        for start, stop in PLAN[name][kernel]
    ]
    return tuple(([flows[name]], start, stop) for _, _, name, start, stop in sorted(entries))


def swap_sum(part, axis, pairs):
    came = lax.ppermute(part, axis, pairs)
    return part.astype(F32) + came.astype(F32)


def sum_scatter(grad, size, order):
    rows, cols = grad.shape
    bits = size.bit_length() - 1
    me = lax.axis_index("dp")
    now = grad.reshape((2,) * bits + (rows // size, cols))
    left = list(range(bits))[::-1]
    for bit in [b for b in order if b < bits] + [b for b in range(bits) if b not in order]:
        axis = left.index(bit)
        mine = (me >> bit) & 1
        keep = lax.dynamic_index_in_dim(now, mine, axis, keepdims=False)
        send = lax.dynamic_index_in_dim(now, 1 - mine, axis, keepdims=False)
        came = lax.ppermute(send, "dp", [(i, i ^ (1 << bit)) for i in range(size)])
        now = (keep.astype(F32) + came.astype(F32)).astype(BF16)
        left.pop(axis)
    return swap_sum(now, "sp", [(0, 1), (1, 0)])


def per_device(
    size,
    inputs,
    memory,
    target_docs,
    memory_docs,
    cotangent,
    w_qkv,
    b_q,
    b_v,
    w_so,
    b_so,
    g_one,
    s_one,
    w_cq,
    b_cq,
    w_ckv,
    b_cv,
    w_co,
    b_co,
    g_two,
    s_two,
    w_fi,
    b_fi,
    w_fo,
    b_fo,
    g_three,
    s_three,
):
    rows, width = inputs.shape[1:]
    wide = b_fi.shape[0]
    comm = size == 16
    narrow, broad = width // size, wide // size
    x, mem, ct = inputs[0], memory[0], cotangent[0]
    qkv, mkv, kvo, mkvo, cq, ctx, cc, h1, x_o, mem_o, lse, clse, t_oth, m_oth, t_own, m_own = front(
        x, mem, target_docs, memory_docs, w_qkv, w_ckv, w_so, w_cq, (b_q, b_v, b_cv, b_so, g_one, s_one, b_cq)
    )
    output, dh2, dcc, gco, gwi, *gwo, small_a, gib = feed(
        size, comm, h1, cc, ct, w_co, w_fi, w_fo,
        (g_one, s_one, b_co, g_two, s_two, b_fo, g_three, s_three, b_fi),
    )
    turned = gib.reshape(width, -1).T

    block = (2, 2, 2, 2, narrow) if comm else (width,)
    at_cross, at_self, flows = (), (), {}
    if comm:
        late_shape = block + (2 * width,)
        sources = {
            "T0": (gwi.reshape(block[:3] + gwi.shape[1:]), block[:3] + gwi.shape[1:], BLOCK[:3]),
            "T1a": (("ref", MIDDLE), block + (3 * width,), BLOCK),
            "T1b": (None, late_shape, BLOCK),
            "G": (("ref", GRADS), block + (3 * width + 2 * PAIR,), BLOCK),
        }
        for name, (source, cols, hops, _, _) in PLAN.items():
            array, shape, dims = sources[source]
            flows[name] = Flow(array, shape, hops, dims, cols)
        at_cross = schedule_of(flows, 3)
        at_self = schedule_of(flows, 4)
    dm, dmo, gcvb, dh1, dsc, late, small_b, *early = cross_backward(
        block, cq, mkv, mkvo, dcc, cc, clse, t_own, m_own, m_oth, mem, mem_o, w_ckv,
        gco, dh2, h1, ctx, w_cq, w_so, g_one, s_one, at_cross,
    )
    for name, flow in flows.items():
        if PLAN[name][0] == "T1b":
            flow.array = late
    dx, dm_in, *made = self_backward(
        block, qkv, kvo, dsc, ctx, lse, t_own, t_oth, x, x_o, w_qkv, dh1, (small_a, small_b, gcvb, turned), dmo, at_self
    )
    if comm:
        targets = {
            "T0": [(0, wide, 2, 0, 0)] + [(wide + i * width, width, 3, i * narrow, 0) for i in range(4)],
            "T1a": [(0, width, 4, 0, 0), (width, 2 * width, 1, 0, 0)],
            "T1b": [(0, width, 5, 0, 0), (width, width, 6, 0, 0)],
            "G": [
                (g * 6 * PAIR + i * 2 * PAIR, 2 * PAIR, 0, 0, i * width + g * 2 * PAIR)
                for g in range(width // PAIR // 2)
                for i in range(3)
            ],
        }
        moves, line = [], None
        for n, (source, cols, *_) in enumerate(PLAN.values()):
            moves += [(n,) + m[1:] for m in moved([cols], targets[source])]
            if source == "G" and cols[0] <= 3 * width < sum(cols):
                line = n, 3 * width - cols[0]
        shapes = [(narrow, 3 * width), (narrow, 2 * width), (narrow, wide), (broad, width)] + [(narrow, width)] * 3
        t_qkv, t_cmem, t_fin, t_fout, t_cout, t_cquery, t_out, lines, output, derivative, grad_memory = outputs(
            [f.array for f in flows.values()], moves, line, shapes, output, dx, dm, dm_in
        )
    else:
        (early,), (made,) = early, made
        columns = made[:, 3 * width : 3 * width + PAIR]
        groups = range(width // PAIR // 2)
        gqkv = jnp.concatenate(
            [made[:, (g * 6 + 2 * i) * PAIR : (g * 6 + 2 * i + 2) * PAIR] for i in range(3) for g in groups], axis=1
        )
        t_fin, t_fout, t_cout, t_cquery, t_out, t_cmem, t_qkv, lines = (
            sum_scatter(g, size, (0, 1, 2, 3))
            for g in (
                gwi, gwo[0], early[:, :width], late[:, :width], late[:, width:], early[:, width:], gqkv, columns
            )
        )
        lines, derivative = lines.T, dx
        grad_memory = (dm + dm_in.astype(F32)).astype(BF16)
    t_gthree, t_sthree, t_fobias, t_gtwo, t_stwo, t_cobias = (lines[i] for i in range(6))
    t_cqbias, t_gone, t_sone, t_obias = (lines[i] for i in range(8, 12))
    t_cvbias, t_qbias, t_vbias = lines[16], lines[21], lines[22]
    t_fibias = lines[17:21].T.reshape(-1)
    return (
        output[None],
        derivative[None],
        grad_memory[None],
        t_qkv,
        t_qbias,
        t_vbias,
        t_out,
        t_obias,
        t_gone,
        t_sone,
        t_cquery,
        t_cqbias,
        t_cmem,
        t_cvbias,
        t_cout,
        t_cobias,
        t_gtwo,
        t_stwo,
        t_fin,
        t_fibias,
        t_fout,
        t_fobias,
        t_gthree,
        t_sthree,
    )


def solution(mesh):
    split = P("dp", "sp", None)
    in_specs = (split, split, P("dp", "sp"), P("dp", "sp"), split) + (P(),) * 21
    matrix, vector = P("dp", None), P("dp")
    out_specs = (
        split, split, split,
        matrix, vector, vector,
        matrix, vector, vector, vector,
        matrix, vector,
        matrix, vector,
        matrix, vector, vector, vector,
        matrix, vector,
        matrix, vector, vector, vector,
    )
    return jax.shard_map(
        functools.partial(per_device, mesh.shape["dp"]),
        mesh=mesh, in_specs=in_specs, out_specs=out_specs, check_vma=False,
    )
```

```python
import functools

import jax
import jax.numpy as jnp
from jax import lax
from jax.experimental import pallas as pl
from jax.experimental.pallas import tpu as pltpu
from jax.sharding import PartitionSpec as P

HD = 64
PAIR = 2 * HD
EPS = 1e-05
FAR = 1.0e9
VMEM = 60 * 1024 * 1024
F32 = jnp.float32
BF16 = jnp.bfloat16


def nn(a, b):
    return lax.dot_general(a, b, (((1,), (0,)), ((), ())), preferred_element_type=F32)


def nt(a, b):
    return lax.dot_general(a, b, (((1,), (1,)), ((), ())), preferred_element_type=F32)


def tn(a, b):
    return lax.dot_general(a, b, (((0,), (0,)), ((), ())), preferred_element_type=F32)


def params(collective=None):
    if collective is None:
        return pltpu.CompilerParams(vmem_limit_bytes=VMEM)
    return pltpu.CompilerParams(
        vmem_limit_bytes=VMEM, collective_id=collective, has_side_effects=True
    )


def cost(flops, moved):
    return pl.CostEstimate(flops=int(flops), bytes_accessed=int(moved), transcendentals=0)


def normed(h):
    centred = h - jnp.mean(h, axis=-1, keepdims=True)
    rstd = lax.rsqrt(jnp.mean(centred * centred, axis=-1, keepdims=True) + EPS)
    return centred * rstd, rstd


def norm_back(grad, n, rstd, gain):
    scaled = grad * gain
    centre = jnp.mean(scaled, axis=-1, keepdims=True)
    along = jnp.mean(scaled * n, axis=-1, keepdims=True)
    return rstd * (scaled - centre - n * along)


def total(a):
    return jnp.sum(a.astype(F32), axis=0, keepdims=True)


def place():
    me = lax.axis_index("dp")
    return me, me % 2, (me // 2) % 2, me // 4, lax.axis_index("sp")


def flipped(at, hops):
    me, c, x, z, sp = at
    for hop in hops:
        if hop == "core":
            me, c = me + 1 - 2 * c, 1 - c
        elif hop == "x":
            me, x = me + 2 - 4 * x, 1 - x
        elif hop == "z1":
            me, z = me + 4 - 8 * (z % 2), z + 1 - 2 * (z % 2)
        elif hop == "z2":
            me, z = me + 8 - 16 * (z // 2), z + 2 - 4 * (z // 2)
        else:
            sp = 1 - sp
    return me, c, x, z, sp


def partner(hops, at=None):
    there = flipped(at or place(), hops)
    return {"dp": there[0], "sp": there[4]}


def greet(groups, at=None):
    groups = sorted({tuple("y" if h[0] == "y" else h for h in hops) for hops in groups})
    barrier = pltpu.get_barrier_semaphore()
    for hops in groups:
        pl.semaphore_signal(barrier, inc=1, device_id=partner(hops, at), device_id_type=pl.DeviceIdType.MESH)
    pl.semaphore_wait(barrier, len(groups))


def remote(src, dst, send, recv, hops, at=None):
    return pltpu.make_async_remote_copy(
        src_ref=src, dst_ref=dst, send_sem=send, recv_sem=recv,
        device_id=partner(hops, at), device_id_type=pl.DeviceIdType.MESH,
    )


PLAN = {
    "T00": ("T0", (0, 2304), ("x", "yr", "z1", "z2", "yg"), ((0, 5), (5, 7)), ((0, 6), (6, 8), (8, 11))),
    "T01": ("T0", (2304, 1280), ("z1", "x", "z2", "y"), ((0, 3), (3, 6), (6, 7)), ((0, 3),)),
    "T02": ("T0", (3584, 2560), ("yr", "x", "z1", "z2", "yg"), ((0, 5), (5, 7)), ((0, 7), (7, 9), (9, 12))),
    "T1a0": ("T1a", (0, 1280), ("core", "x", "yr", "z1", "z2", "yg"), ((6, 7),), ((0, 5), (5, 10), (10, 12), (12, 18), (18, 22))),
    "T1a1": ("T1a", (1280, 1024), ("core", "z1", "x", "z2", "y"), ((6, 7),), ((0, 8), (8, 10), (10, 12), (12, 17))),
    "T1b0": ("T1b", (0, 1536), ("core", "x", "z1", "yr", "z2", "yg"), (), ((0, 3), (3, 8), (8, 10), (10, 13), (13, 20), (20, 25))),
    "G10": ("G", (0, 768), ("core", "x", "z1", "z2", "y"), (), ((8, 9), (9, 11), (11, 13), (13, 20), (20, 25))),
    "G20": ("G", (768, 256), ("core", "x", "z1", "z2", "y"), (), ((10, 11), (11, 12), (12, 15), (15, 19), (19, 24))),
    "G21": ("G", (1024, 512), ("core", "x", "yr", "z1", "z2", "yg"), (), ((10, 12), (12, 17), (17, 23), (23, 26), (26, 28), (28, 30))),
    "G30": ("G", (1536, 640), ("core", "x", "z1", ("z2", "y")), (), ((12, 16), (16, 21), (21, 27), (27, 32))),
    "G31": ("G", (2176, 384), ("core", "z1", "x", "z2", "y"), (), ((12, 14), (14, 24), (24, 25), (25, 29), (29, 31))),
}
BLOCK = ("z2", "z1", "x", "core")


class Part:
    def __init__(self, hop, shape, dims, cols=None):
        self.hops = hops = hop if isinstance(hop, tuple) else (hop,)
        self.groups = [(h,) for h in hops] + ([hops] if len(hops) > 1 else [])
        self.dims = dims
        self.cols = cols or (0, shape[-1])
        self.shape = shape = tuple(shape[:-1]) + (self.cols[1],)
        for h in hops:
            if h in dims:
                at = dims.index(h)
                shape, dims = shape[:at] + shape[at + 1 :], dims[:at] + dims[at + 1 :]
            elif h != "y":
                shape = shape[:-1] + (shape[-1] // 2 if h == "yr" else 2 * shape[-1],)
        self.after, self.left = shape, dims
        self.came = self.shape if hops == ("yg",) else shape

    def share(self, at):
        _, c, x, z, sp = at
        first, wide = self.cols
        index = [slice(None)] * (len(self.shape) - 1) + [pl.ds(first, wide)]
        for h in self.hops:
            if h in self.dims:
                index[self.dims.index(h)] = {"core": c, "x": x, "z1": z % 2, "z2": z // 2}[h]
            elif h == "yr":
                half = wide // 2
                index[-1] = pl.ds(pl.multiple_of(first + sp * half, 128), half)
        return tuple(index)

    def copies(self, src, held, made, came, send, recv, local, at):
        out = [
            remote(src.at[self.share(flipped(at, g))], came[i], send.at[i], recv.at[i], g, at)
            for i, g in enumerate(self.groups)
        ]
        if not held:
            out.append(pltpu.make_async_copy(src.at[self.share(at)], made, local))
        return out

    def add(self, src, held, made, came, at):
        if self.hops == ("yg",):
            wide, sp = self.shape[-1], at[4]
            lead = (slice(None),) * (len(self.shape) - 1)
            made[lead + (pl.ds(pl.multiple_of(sp * wide, 128), wide),)] = src[self.share(at)]
            made[lead + (pl.ds(pl.multiple_of((1 - sp) * wide, 128), wide),)] = came[0][...]
        elif len(came) > 1:
            mine = src[self.share(at)] if held else made[...]
            one, two, three = (c[...].astype(F32) for c in came)
            made[...] = ((mine.astype(F32) + one) + (two + three)).astype(BF16)
        elif held:
            made[...] = src[self.share(at)] + came[0][...]
        else:
            made[...] += came[0][...]


class Flow:
    def __init__(self, array, shape, hops, dims=BLOCK, cols=None):
        self.array, self.shape, self.dims, self.cols = array, tuple(shape), dims, cols
        self.hops = list(hops)

    def step(self):
        part = Part(self.hops.pop(0), self.shape, self.dims, self.cols)
        self.shape, self.dims, self.cols = part.after, part.left, None
        return part


class Window:
    def __init__(self, start, stop, joint):
        self.start, self.stop, self.joint = start, stop, joint
        self.parts, self.sources, self.keeps = [], [], []


class Joint:
    def __init__(self):
        self.window = None


def plan(schedule):
    windows, arrays, latest = [], [], {}
    for n, (flows, start, stop, *joint) in enumerate(schedule):
        window = Window(start, stop, bool(joint))
        if joint:
            joint[0].window = n
        for i, flow in enumerate(flows):
            if flow in latest:
                source = ("part",) + latest[flow]
                before = windows[latest[flow][0]]
                before.keeps[latest[flow][1]] = False
            elif isinstance(flow.array, Joint):
                source = ("joint", flow.array.window)
            elif isinstance(flow.array, tuple):
                source = flow.array
            else:
                known = [k for k, a in enumerate(arrays) if a is flow.array]
                if not known:
                    arrays.append(flow.array)
                source = ("in", known[0] if known else len(arrays) - 1)
            window.parts.append(flow.step())
            window.sources.append(source)
            window.keeps.append(not joint)
            if not joint:
                latest[flow] = (n, i)
        windows.append(window)
    return windows, arrays, latest


def carrying(body, own, windows, arrays, grid, also, finale):
    ins, outs, held = own

    def kernel(*refs):
        refs = list(refs)

        def take(n):
            got = refs[:n]
            del refs[:n]
            return got

        my_in, arr = take(ins), take(arrays)
        my_out = take(outs)
        given = [[take(1)[0] if k else None for k in w.keeps] for w in windows]
        my_held = take(held)
        made, came, joints = [], [], []
        for w, g in zip(windows, given):
            if w.joint:
                joint, col, views = take(1)[0], 0, []
                for q in w.parts:
                    views.append(joint.at[(slice(None),) * (len(q.after) - 1) + (pl.ds(col, q.after[-1]),)])
                    col += q.after[-1]
                joints.append(joint)
                made.append(views)
            else:
                joints.append(None)
                made.append([ref if ref is not None else take(1)[0] for ref in g])
            came.append([take(len(q.groups)) for q in w.parts])
        mine = my_in + my_out + my_held
        step = pl.program_id(0)
        groups = [g for w in windows for q in w.parts for g in q.groups] + list(also)
        if groups:
            here = place()
            pl.when(step == 0)(lambda: greet(groups, here))
        if windows:
            send, recv, local = refs
        copies, sources, base = [], [], 0
        for w, m, c in zip(windows, made, came):
            now, froms = [], []
            for i, q in enumerate(w.parts):
                kind = w.sources[i]
                if kind[0] == "in":
                    src = arr[kind[1]]
                elif kind[0] == "ref":
                    src = mine[kind[1]]
                elif kind[0] == "joint":
                    src = joints[kind[1]]
                else:
                    src = made[kind[1]][kind[2]]
                held_here = kind[0] != "in"
                froms.append((src, held_here))
                now += q.copies(
                    src, held_here, m[i], c[i], send.at[base], recv.at[base], local.at[base], here
                )
                base += 1
            copies.append(now)
            sources.append(froms)

        def phase(number):
            for n, w in enumerate(windows):
                if w.stop == number:
                    for copy in copies[n]:
                        copy.wait()
                    for q, (src, held_here), m, c in zip(w.parts, sources[n], made[n], came[n]):
                        q.add(src, held_here, m, c, here)
            for n, w in enumerate(windows):
                if w.start == number:
                    for copy in copies[n]:
                        copy.start()

        used = sorted({w.start for w in windows} | {w.stop for w in windows})
        for number in used:
            if number < grid:
                pl.when(step == number)(functools.partial(phase, number))
        body(*mine)
        for number in used:
            if number >= grid:
                pl.when(step == grid - 1)(functools.partial(phase, number))
        if finale:
            pl.when(step == grid - 1)(lambda: finale(*mine))

    return kernel


def run(
    body, name, grid, ins, in_specs, outs, out_specs, held=(), schedule=(), collective=None,
    flops=0, moved=0, also=(), finale=None,
):
    in_specs, outs, out_specs, held = list(in_specs), list(outs), list(out_specs), list(held)
    windows, arrays, latest = plan(schedule)
    own = len(outs)
    kernel = carrying(body, (len(ins), own, len(held)), windows, len(arrays), grid, also, finale)
    in_specs += [pl.BlockSpec(memory_space=pl.ANY)] * len(arrays)
    order, count = [], 0
    for n, w in enumerate(windows):
        if w.joint:
            shape = w.parts[0].after[:-1] + (sum(q.after[-1] for q in w.parts),)
            held.append(pltpu.VMEM(shape, BF16))
        for i, (q, k) in enumerate(zip(w.parts, w.keeps)):
            if w.joint:
                continue
            if k:
                outs.append(jax.ShapeDtypeStruct(q.after, BF16))
                out_specs.append(whole(q.after))
                order.append((n, i))
            else:
                held.append(pltpu.VMEM(q.after, BF16))
        held += [pltpu.VMEM(q.came, BF16) for q in w.parts for _ in q.groups]
        count += len(w.parts)
    if windows:
        held += [pltpu.SemaphoreType.DMA((count, 3))] * 2 + [pltpu.SemaphoreType.DMA((count,))]
    results = pl.pallas_call(
        kernel,
        grid=(grid,),
        in_specs=in_specs,
        out_specs=out_specs,
        out_shape=outs,
        scratch_shapes=held,
        compiler_params=params(collective if windows or also else None),
        cost_estimate=cost(flops, moved),
        name=name,
    )(*ins, *arrays)
    for flow, where in latest.items():
        flow.array = results[own + order.index(where)]
    return results[:own]


def head_masks(dtype):
    lane = lax.broadcasted_iota(jnp.int32, (1, PAIR), 1)
    low = jnp.where(lane < HD, 1.0, 0.0)
    return low.astype(dtype), (1.0 - low).astype(dtype)


def query_code(code):
    lane = lax.broadcasted_iota(jnp.int32, code.shape, 1)
    return jnp.where(lane < 4, (code.astype(F32) - 1.0) * FAR, 0.0).astype(BF16)


def masked(s, diagonal):
    low, high = s[:-diagonal], s[-diagonal:]
    row = lax.broadcasted_iota(jnp.int32, high.shape, 0)
    col = lax.broadcasted_iota(jnp.int32, high.shape, 1)
    high = jnp.where(row <= col, high, -FAR)
    return jnp.concatenate([low, high], axis=0) if low.shape[0] else high


def softmax_over(jobs):
    results = []
    ready = nt(jobs[0][0], jobs[0][2])
    for n, (_, values_t, _, diagonal) in enumerate(jobs):
        s = ready
        if n + 1 < len(jobs):
            ready = nt(jobs[n + 1][0], jobs[n + 1][2])
        if diagonal:
            s = masked(s, diagonal)
        peak = jnp.max(s, axis=0, keepdims=True)
        e = jnp.exp(s - peak)
        norm = jnp.sum(e, axis=0, keepdims=True)
        results.append((nn(values_t, e.astype(BF16)) / norm, peak + jnp.log(norm)))
    return results


def pair_spec(rows, offset):
    return pl.BlockSpec((rows, PAIR), lambda p: (0, p + offset))


def whole(shape):
    return pl.BlockSpec(shape, lambda *_: (0,) * len(shape))


def delta_rows(g, o):
    prod = g.astype(F32) * o.astype(F32)
    upper = prod.astype(BF16)
    lower = (prod - upper.astype(F32)).astype(BF16)
    row = lax.broadcasted_iota(jnp.int32, (8, PAIR), 0)
    lane = lax.broadcasted_iota(jnp.int32, (8, PAIR), 1)
    pick = jnp.where(row == lane // HD, 1.0, 0.0).astype(BF16)
    return nt(pick, upper) + nt(pick, lower)


def back_pieces(jobs):
    def products(job):
        keys, values, q, g = job[:4]
        return nt(keys, q), nt(values, g)

    ready = products(jobs[0])
    for n, (_, _, _, _, lse, delta, causal) in enumerate(jobs):
        s, dp = ready
        if n + 1 < len(jobs):
            ready = products(jobs[n + 1])
        if causal:
            s = masked(s, s.shape[0])
        p = jnp.exp(s - lse)
        yield n, p.astype(BF16), (p * (dp - delta)).astype(BF16)


def cross_backward_kernel(
    size, pairs, q_ref, k_ref, v_ref, ko_ref, vo_ref, g_ref, o_ref, lse_ref, t_ref, own_ref, oth_ref,
    m_ref, mo_ref, wk_ref, wv_ref, gco_ref, dh2_ref, h1_ref, ctx_ref, wcq_ref, wso_ref, g1_ref, s1_ref,
    dm_ref, dmo_ref, gb_ref, dh1_ref, dsc_ref, late_ref, small_ref, grad_ref,
    dmo_acc, mt_ref, mot_ref, dcq_ref,
):
    step = pl.program_id(0)
    rows, width = m_ref.shape
    lead = (slice(None),) * (len(grad_ref.shape) - 1)

    def put(ref, col, grad):
        to = pl.ds(pl.multiple_of(col, PAIR), grad.shape[1])
        ref[lead + (to,)] = grad.astype(BF16).reshape(ref.shape[:-1] + (grad.shape[1],))

    @pl.when(step == 0)
    def _():
        mt_ref[...] = jnp.transpose(m_ref[...])
        mot_ref[...] = jnp.transpose(mo_ref[...])
        put(grad_ref, 0, gco_ref[...])

    @pl.when(step < pairs)
    def _():
        count = rows // size
        halves = [(k_ref, v_ref, own_ref, mt_ref, dm_ref), (ko_ref, vo_ref, oth_ref, mot_ref, dmo_acc)]
        cols = pl.ds(pl.multiple_of(step * PAIR, PAIR), PAIR)
        dq = [[0.0, 0.0] for _ in range(count)]
        gk = gv = gb = 0.0
        for kr, vr, code, mem, acc in halves:
            keys = jnp.concatenate([kr[...], code[...]], axis=1)
            values = vr[...]
            turned = jnp.transpose(kr[...])
            dk = dv = 0.0
            jobs = list(backward_pieces(size, q_ref, g_ref, o_ref, lse_ref, t_ref))
            for n, p, ds in back_pieces([(keys, values, q, gm, lse, delta, False) for _, _, _, gm, q, lse, delta in jobs]):
                block, head, qm, gm = jobs[n][:4]
                dk = dk + nn(ds, qm)
                dv = dv + nn(p, gm)
                dq[block][head] = dq[block][head] + nn(turned[head * HD : (head + 1) * HD], ds)
            both = jnp.concatenate([dk.astype(BF16), dv.astype(BF16)], axis=1)
            grad = nn(mem[...], both)
            gk, gv = gk + grad[:, :PAIR], gv + grad[:, PAIR:]
            gb = gb + total(both[:, PAIR:])
            dm = nt(both, jnp.concatenate([wk_ref[...], wv_ref[...]], axis=1))

            @pl.when(step == 0)
            def _():
                acc[...] = dm

            @pl.when(step > 0)
            def _():
                acc[...] += dm

        for block in range(count):
            dcq_ref[block * size : (block + 1) * size, cols] = upright(dq[block]).astype(BF16)
        put(grad_ref, width + step * PAIR, gk)
        put(grad_ref, 2 * width + step * PAIR, gv)
        gb_ref[:, cols] = gb

    @pl.when(step == pairs)
    def _():
        dmo_ref[...] = dmo_acc[...].astype(BF16)
        gain = line(g1_ref)
        n1, r1 = normed(h1_ref[...])
        a1b = (n1 * gain + line(s1_ref)).astype(BF16)
        dcq = dcq_ref[...]
        d1 = dh2_ref[...] + nt(dcq, wcq_ref[...])
        dh1 = norm_back(d1, n1, r1, gain)
        dh1_ref[...] = dh1
        dso = dh1.astype(BF16)
        dsc_ref[...] = nt(dso, wso_ref[...]).astype(BF16)
        put(late_ref, 0, tn(a1b, dcq))
        put(late_ref, width, tn(ctx_ref[...], dso))
        small_ref[0:1] = total(dcq)
        small_ref[1:2] = total(d1 * n1)
        small_ref[2:3] = total(d1)
        small_ref[3:4] = total(dso)
        small_ref[4:8] = jnp.zeros((4, width), F32)


MIDDLE = 30


def cross_backward(block, cq, kv, kvo, g, o, lse, t, own, oth, m, mo, w, gco, dh2, h1, ctx, wcq, wso, gain, shift, schedule):
    rows, width = cq.shape
    pairs = width // PAIR

    def pair_of(size, offset):
        return pl.BlockSpec((size, PAIR), lambda s: (0, jnp.minimum(s, pairs - 1) + offset))

    flat, square = whole((rows, width)), whole((width, width))
    outs = [
        jax.ShapeDtypeStruct((rows, width), F32),
        jax.ShapeDtypeStruct((rows, width), BF16),
        jax.ShapeDtypeStruct((1, width), F32),
        jax.ShapeDtypeStruct((rows, width), F32),
        jax.ShapeDtypeStruct((rows, width), BF16),
        jax.ShapeDtypeStruct(block + (2 * width,), BF16),
        jax.ShapeDtypeStruct((8, width), F32),
    ]
    specs = [flat, flat, whole((1, width)), flat, flat, whole(block + (2 * width,)), whole((8, width))]
    held = []
    if schedule:
        held.append(pltpu.VMEM(block + (3 * width,), BF16))
    else:
        outs.append(jax.ShapeDtypeStruct(block + (3 * width,), BF16))
        specs.append(whole(block + (3 * width,)))
    held += [
        pltpu.VMEM((rows, width), F32),
        pltpu.VMEM((width, rows), BF16),
        pltpu.VMEM((width, rows), BF16),
        pltpu.VMEM((rows, width), BF16),
    ]
    return run(
        functools.partial(cross_backward_kernel, 256, pairs), "cross_backward", pairs + 1,
        (cq, kv, kv, kvo, kvo, g, o, lse, t, own, oth, m, mo, w, w, gco, dh2, h1, ctx, wcq, wso, gain, shift),
        [
            pair_of(rows, 0), pair_of(rows, 0), pair_of(rows, pairs), pair_of(rows, 0), pair_of(rows, pairs),
            pair_of(rows, 0), pair_of(rows, 0),
            pl.BlockSpec((8, rows), lambda s: (jnp.minimum(s, pairs - 1), 0)),
            whole((rows, 128)), whole((rows, 128)), whole((rows, 128)), flat, flat,
            pair_of(width, 0), pair_of(width, pairs),
            square, flat, flat, flat, square, square, whole(gain.shape), whole(shift.shape),
        ],
        outs, specs, held, schedule, 3,
        64 * rows * rows * width + 24 * rows * width * width, 40 * rows * width,
    )


def upright(heads):
    return jnp.transpose(jnp.concatenate(heads, axis=0) * HD**-0.5)


def backward_pieces(size, q_ref, g_ref, o_ref, lse_ref, own_ref):
    masks = head_masks(BF16)
    scale = BF16(HD**-0.5)
    qcode = query_code(own_ref[...])
    delta = delta_rows(g_ref[...], o_ref[...])
    for block in range(q_ref.shape[0] // size):
        at = slice(block * size, (block + 1) * size)
        for head, mask in enumerate(masks):
            qm = q_ref[at] * (mask * scale)
            gm = g_ref[at] * mask
            q = jnp.concatenate([qm, qcode[at]], axis=1)
            yield block, head, qm, gm, q, lse_ref[head : head + 1, at], delta[head : head + 1, at]


def self_backward_kernel(
    size, q_ref, k_ref, v_ref, ko_ref, vo_ref, g_ref, o_ref, lse_ref, own_ref, oth_ref,
    x_ref, xo_ref, wq_ref, wk_ref, wv_ref, dh1_ref, sa_ref, sb_ref, sc_ref, sd_ref, dmo_ref,
    dx_ref, dmi_ref, grad_ref,
    dq_acc, dx_acc, dxo_acc, dkv_acc, xt_ref, xot_ref, dxo_ref, came_ref, memory_ref, turn_ref, send_ref, recv_ref,
):
    step = pl.program_id(0)
    sp = lax.axis_index("sp")
    second = sp == 1
    rows, width = x_ref.shape
    pairs = width // PAIR
    pair = lax.rem(step, pairs)
    cols = pl.ds(pl.multiple_of(pair * PAIR, PAIR), PAIR)
    count = rows // size
    over = remote(dxo_ref, came_ref, send_ref.at[0], recv_ref.at[0], ("y",))

    def pieces():
        return backward_pieces(size, q_ref, g_ref, o_ref, lse_ref, own_ref)

    @pl.when(step == 0)
    def _():
        remote(dmo_ref, memory_ref, send_ref.at[1], recv_ref.at[1], ("y",)).start()
        xt_ref[...] = jnp.transpose(x_ref[...])
        turn_ref[...] = jnp.zeros(turn_ref.shape, F32)
        turn_ref[0:8] = sa_ref[...]
        turn_ref[8:16] = sb_ref[...]
        turn_ref[16:17] = sc_ref[...]

    @pl.when(jnp.logical_and(step == 0, second))
    def _():
        xot_ref[...] = jnp.transpose(xo_ref[...])

    @pl.when(jnp.logical_and(step == 0, jnp.logical_not(second)))
    def _():
        dq_acc[...] = jnp.zeros(dq_acc.shape, F32)

    @pl.when(jnp.logical_and(step < pairs, second))
    def _():
        keys = jnp.concatenate([ko_ref[...], oth_ref[...]], axis=1)
        values = vo_ref[...]
        turned = jnp.transpose(ko_ref[...])
        dk = dv = 0.0
        jobs = list(pieces())
        for n, p, ds in back_pieces([(keys, values, q, gm, lse, delta, False) for _, _, _, gm, q, lse, delta in jobs]):
            block, head, qm, gm = jobs[n][:4]
            dk = dk + nn(ds, qm)
            dv = dv + nn(p, gm)
            of_head = slice(head * HD, (head + 1) * HD)
            dq_acc[pair, of_head, block * size : (block + 1) * size] = nn(turned[of_head], ds)
        both = jnp.concatenate([dk.astype(BF16), dv.astype(BF16)], axis=1)
        dkv_acc[pair] = both
        dxo = nt(both, jnp.concatenate([wk_ref[...], wv_ref[...]], axis=1))

        @pl.when(step == 0)
        def _():
            dxo_acc[...] = dxo

        @pl.when(step > 0)
        def _():
            dxo_acc[...] += dxo

    @pl.when(jnp.logical_and(step == pairs - 1, second))
    def _():
        dxo_ref[...] = dxo_acc[...].astype(BF16)
        over.start()

    @pl.when(step >= pairs)
    def _():
        turned = jnp.transpose(k_ref[...])
        dq = [[0.0, 0.0] for _ in range(count)]
        dk, dv = [0.0] * count, [0.0] * count
        jobs, where = [], []
        keys = jnp.concatenate([k_ref[...], own_ref[...]], axis=1)
        for block, head, qm, gm, q, lse, delta in pieces():
            for part in range(block + 1):
                of = slice(part * size, (part + 1) * size)
                jobs.append((keys[of], v_ref[of], q, gm, lse, delta, part == block))
                where.append((block, part, head, qm, gm))
        for n, p, ds in back_pieces(jobs):
            block, part, head, qm, gm = where[n]
            of = slice(part * size, (part + 1) * size)
            dk[part] = dk[part] + nn(ds, qm)
            dv[part] = dv[part] + nn(p, gm)
            dq[block][head] = dq[block][head] + nn(turned[head * HD : (head + 1) * HD, of], ds)
        dk, dv = (jnp.concatenate(a, axis=0) for a in (dk, dv))
        before = dq_acc[pair]
        dq = jnp.concatenate(
            [
                upright(
                    [
                        part + before[head * HD : (head + 1) * HD, block * size : (block + 1) * size]
                        for head, part in enumerate(parts)
                    ]
                )
                for block, parts in enumerate(dq)
            ],
            axis=0,
        )
        dqk = jnp.concatenate([dq.astype(BF16), dk.astype(BF16)], axis=1)
        dv = dv.astype(BF16)
        grad_qk = nn(xt_ref[...], dqk)
        grad_v = nn(xt_ref[...], dv)
        shape = grad_ref.shape[:-1] + (PAIR,)
        lead = (slice(None),) * (len(shape) - 1)

        def put(n, grad):
            col = pair // 2 * 6 + 2 * n + pair % 2
            to = pl.ds(pl.multiple_of(col * PAIR, PAIR), PAIR)
            grad_ref[lead + (to,)] = grad.astype(BF16).reshape(shape)

        put(0, grad_qk[:, :PAIR])
        turn_ref[21:22, cols] = total(dqk[:, :PAIR])

        @pl.when(second)
        def _():
            grad_o = nn(xot_ref[...], dkv_acc[pair])
            put(1, grad_qk[:, PAIR:] + grad_o[:, :PAIR])
            put(2, grad_v + grad_o[:, PAIR:])
            turn_ref[22:23, cols] = total(dv) + total(dkv_acc[pair, :, PAIR:])

        @pl.when(jnp.logical_not(second))
        def _():
            put(1, grad_qk[:, PAIR:])
            put(2, grad_v)
            turn_ref[22:23, cols] = total(dv)

        dx = nt(dqk, jnp.concatenate([wq_ref[...], wk_ref[...]], axis=1)) + nt(dv, wv_ref[...])

        @pl.when(step == pairs)
        def _():
            dx_acc[...] = dh1_ref[...] + dx

        @pl.when(step > pairs)
        def _():
            dx_acc[...] += dx

    @pl.when(step == 2 * pairs - 1)
    def _():
        shape = grad_ref.shape[:-1] + (2 * PAIR,)
        lead = (slice(None),) * (len(shape) - 1)
        col = 3 * width
        columns = jnp.transpose(turn_ref[...])
        if sd_ref.shape == (width, PAIR):
            columns = columns + jnp.concatenate([sd_ref[...], jnp.zeros((width, PAIR), F32)], axis=1)
        grad_ref[lead + (slice(col, col + 2 * PAIR),)] = columns.astype(BF16).reshape(shape)


def self_backward_finale(*refs):
    dmo_ref, dx_ref, dmi_ref = refs[20:23]
    dx_acc, dxo_ref, came_ref, memory_ref, send_ref, recv_ref = (refs[i] for i in (25, 30, 31, 32, 34, 35))
    remote(dmo_ref, memory_ref, send_ref.at[1], recv_ref.at[1], ("y",)).wait()
    dmi_ref[...] = memory_ref[...]
    over = remote(dxo_ref, came_ref, send_ref.at[0], recv_ref.at[0], ("y",))

    @pl.when(lax.axis_index("sp") == 0)
    def _():
        over.wait_recv()
        dx_ref[...] = (dx_acc[...] + came_ref[...].astype(F32)).astype(BF16)

    @pl.when(lax.axis_index("sp") == 1)
    def _():
        over.wait_send()
        dx_ref[...] = dx_acc[...].astype(BF16)


GRADS = 23


def self_backward(block, qkv, kvo, g, o, lse, own, oth, x, xo, w, dh1, small, dmo, schedule):
    rows, width = x.shape
    pairs = width // PAIR

    def pair_of(offset):
        return pl.BlockSpec((rows, PAIR), lambda s: (0, lax.rem(s, pairs) + offset))

    def weight(offset):
        return pl.BlockSpec((width, PAIR), lambda s: (0, lax.rem(s, pairs) + offset))

    made = block + (3 * width + 2 * PAIR,)
    outs = [jax.ShapeDtypeStruct((rows, width), BF16)] * 2
    specs = [whole((rows, width))] * 2
    held = []
    if schedule:
        held += [pltpu.VMEM(made, BF16)]
    else:
        outs += [jax.ShapeDtypeStruct(made, BF16)]
        specs += [whole(made)]
    held += [
        pltpu.VMEM((pairs, PAIR, rows), F32),
        pltpu.VMEM((rows, width), F32),
        pltpu.VMEM((rows, width), F32),
        pltpu.VMEM((pairs, rows, 2 * PAIR), BF16),
        pltpu.VMEM((width, rows), BF16),
        pltpu.VMEM((width, rows), BF16),
        pltpu.VMEM((rows, width), BF16),
        pltpu.VMEM((rows, width), BF16),
        pltpu.VMEM((rows, width), BF16),
        pltpu.VMEM((2 * PAIR, width), F32),
        pltpu.SemaphoreType.DMA((2,)),
        pltpu.SemaphoreType.DMA((2,)),
    ]
    return run(
        functools.partial(self_backward_kernel, 256), "self_backward", 2 * pairs,
        (qkv, qkv, qkv, kvo, kvo, g, o, lse, own, oth, x, xo, w, w, w, dh1) + tuple(small) + (dmo,),
        [
            pair_of(0),
            pair_of(pairs),
            pair_of(2 * pairs),
            pair_of(0),
            pair_of(pairs),
            pair_of(0),
            pair_of(0),
            pl.BlockSpec((8, rows), lambda s: (lax.rem(s, pairs), 0)),
            whole((rows, 128)),
            whole((rows, 128)),
            whole((rows, width)),
            whole((rows, width)),
            weight(0),
            weight(pairs),
            weight(2 * pairs),
            whole((rows, width)),
        ] + [whole(a.shape) for a in small] + [pl.BlockSpec(memory_space=pl.ANY)],
        outs, specs, held, schedule, 5,
        48 * rows * rows * width + 20 * rows * width * width, 12 * width * width + 40 * rows * width,
        (("y",),), self_backward_finale,
    )


def code_of(docs_ref):
    row = lax.broadcasted_iota(jnp.int32, (PAIR, docs_ref.shape[1]), 0)
    return jnp.transpose(jnp.where(docs_ref[...] == row, 1.0, 0.0)).astype(BF16)


def line(ref):
    return ref[...].astype(F32)[None, :]


def front_kernel(
    size, x_hbm, m_hbm, td_ref, md_ref, wx_hbm, wm_hbm, wo_hbm, wq_hbm,
    bq_ref, bv_ref, bcv_ref, bso_ref, g_ref, s_ref, bcq_ref,
    qkv_out, mkv_out, kvo_out, mkvo_out, cq_out, ctx_out, cc_out, h_out, xo_out, mo_out,
    lse_ref, clse_ref, tt_ref, mt_ref, to_ref, mo_ref,
    x_ref, m_ref, wx_ref, wm_ref, wo_ref, wq_ref, xc_ref, mc_ref, tdc_ref, mdc_ref,
    qkv_ref, mkv_ref, kvo_ref, mkvo_ref, cq_ref, ctx_ref, cc_ref, h_ref, acc_ref,
    load_ref, store_ref, send_ref, recv_ref,
):
    rows, width = x_ref.shape
    pairs = width // PAIR
    second = lax.axis_index("sp") == 1
    first = jnp.logical_not(second)
    masks = head_masks(BF16)
    scale = BF16(HD**-0.5)
    loads = [
        pltpu.make_async_copy(src, dst, load_ref.at[i])
        for i, (src, dst) in enumerate(
            ((x_hbm, x_ref), (wx_hbm, wx_ref), (m_hbm, m_ref), (wm_hbm, wm_ref), (wo_hbm, wo_ref), (wq_hbm, wq_ref))
        )
    ]
    give = [
        pltpu.make_async_copy(src, dst, store_ref.at[i])
        for i, (src, dst) in enumerate(
            (
                (qkv_ref, qkv_out), (mkv_ref, mkv_out), (mkvo_ref, mkvo_out), (cq_ref, cq_out), (ctx_ref, ctx_out),
                (cc_ref, cc_out), (h_ref, h_out), (mc_ref, mo_out), (kvo_ref, kvo_out), (xc_ref, xo_out),
            )
        )
    ]
    x_over = remote(x_hbm, xc_ref, send_ref.at[0], recv_ref.at[0], ("y",))
    m_over = remote(m_hbm, mc_ref, send_ref.at[1], recv_ref.at[1], ("y",))
    docs = [
        remote(td_ref, tdc_ref, send_ref.at[2], recv_ref.at[2], ("y",)),
        remote(md_ref, mdc_ref, send_ref.at[3], recv_ref.at[3], ("y",)),
    ]
    for copy in loads:
        copy.start()
    greet([("y",)])
    for copy in docs:
        copy.start()
    pl.when(first)(x_over.start)
    pl.when(second)(m_over.start)

    def columns(offset, pair):
        return pl.ds(pl.multiple_of(offset + pair * PAIR, PAIR), PAIR)

    def heads(source, offset, pair, code, block):
        at = slice(block * size, (block + 1) * size)
        q = source[at, columns(offset, pair)]
        return [jnp.concatenate([q * (mask * scale), code[at]], axis=1) for mask in masks]

    def keep(block, pair, outs, lses, lse_out, out):
        at = slice(block * size, (block + 1) * size)
        mixed = jnp.concatenate(outs, axis=0)
        acc_ref[pair, :, at] = mixed
        out[at, columns(0, pair)] = jnp.transpose(mixed).astype(BF16)
        row = lax.broadcasted_iota(jnp.int32, (8, size), 0)
        lse_out[pl.ds(pl.multiple_of(pair * 8, 8), 8), at] = jnp.where(row == 0, lses[0], lses[1])

    def begin(block, pair, results, lse_out, out):
        keep(block, pair, [r for r, _ in results], [lse for _, lse in results], lse_out, out)

    def merge(block, pair, results, lse_out, out):
        at = slice(block * size, (block + 1) * size)
        stats = lse_out[pl.ds(pl.multiple_of(pair * 8, 8), 8), at]
        outs, lses = [], []
        for head, (r, lse) in enumerate(results):
            before = acc_ref[pair, head * HD : (head + 1) * HD, at]
            old = stats[head : head + 1]
            peak = jnp.maximum(old, lse)
            both = peak + jnp.log(jnp.exp(old - peak) + jnp.exp(lse - peak))
            outs.append(before * jnp.exp(old - both) + r * jnp.exp(lse - both))
            lses.append(both)
        keep(block, pair, outs, lses, lse_out, out)

    def halves(values):
        turned = jnp.transpose(values)
        return turned[:HD], turned[HD:]

    to_ref[...] = code_of(td_ref)
    mo_ref[...] = code_of(md_ref)
    loads[0].wait()
    loads[1].wait()
    for n, bias in enumerate((line(bq_ref), 0.0, line(bv_ref))):
        cols = slice(n * width, (n + 1) * width)
        qkv_ref[:, cols] = (nn(x_ref[...], wx_ref[:, cols]) + bias).astype(BF16)
    give[0].start()
    loads[2].wait()
    loads[3].wait()
    for n, bias in enumerate((0.0, line(bcv_ref))):
        cols = slice(n * width, (n + 1) * width)
        mkv_ref[:, cols] = (nn(m_ref[...], wm_ref[:, cols]) + bias).astype(BF16)
    give[1].start()

    def attend(query, keys_ref, key_at, value_at, key_code, diagonal, finish, stats, out):
        @pl.loop(0, pairs // 2)
        def _(half):
            code = query_code(to_ref[...])
            jobs, where = [], []
            for pair in (2 * half, 2 * half + 1):
                keys = jnp.concatenate([keys_ref[:, columns(key_at, pair)], key_code[...]], axis=1)
                values = halves(keys_ref[:, columns(value_at, pair)])
                for block in range(rows // size):
                    end = (block + 1) * size if diagonal else rows
                    for q, v in zip(heads(query, 0, pair, code, block), values):
                        jobs.append((keys[:end], v[:, :end], q, size if diagonal else 0))
                    where.append((block, pair))
            results = softmax_over(jobs)
            for n, (block, pair) in enumerate(where):
                finish(block, pair, results[2 * n : 2 * n + 2], stats, out)

    attend(qkv_ref, qkv_ref, width, 2 * width, to_ref, True, begin, lse_ref, ctx_ref)

    for copy in docs:
        copy.wait()
    tt_ref[...] = code_of(tdc_ref)
    mt_ref[...] = code_of(mdc_ref)

    @pl.when(first)
    def _():
        x_over.wait_send()
        m_over.start()

    @pl.when(second)
    def _():
        x_over.wait_recv()
        give[9].start()
        for n, bias in enumerate((0.0, line(bv_ref))):
            cols = slice(n * width, (n + 1) * width)
            from_cols = slice((n + 1) * width, (n + 2) * width)
            kvo_ref[:, cols] = (nn(xc_ref[...], wx_ref[:, from_cols]) + bias).astype(BF16)
        give[8].start()

        attend(qkv_ref, kvo_ref, 0, width, tt_ref, False, merge, lse_ref, ctx_ref)

    give[4].start()
    loads[4].wait()
    loads[5].wait()
    h = x_ref[...].astype(F32) + nn(ctx_ref[...], wo_ref[...]) + line(bso_ref)
    h_ref[...] = h
    n, _ = normed(h)
    a = (n * line(g_ref) + line(s_ref)).astype(BF16)
    cq_ref[...] = (nn(a, wq_ref[...]) + line(bcq_ref)).astype(BF16)
    give[6].start()
    give[3].start()

    attend(cq_ref, mkv_ref, 0, width, mo_ref, False, begin, clse_ref, cc_ref)
    m_over.wait()
    give[7].start()
    for n, bias in enumerate((0.0, line(bcv_ref))):
        cols = slice(n * width, (n + 1) * width)
        mkvo_ref[:, cols] = (nn(mc_ref[...], wm_ref[:, cols]) + bias).astype(BF16)
    give[2].start()
    attend(cq_ref, mkvo_ref, 0, width, mt_ref, False, merge, clse_ref, cc_ref)
    give[5].start()
    for copy in give[:8]:
        copy.wait()

    @pl.when(second)
    def _():
        give[8].wait()
        give[9].wait()


def front(x, mem, td, md, wx, wm, wo, wq, vectors):
    rows, width = x.shape
    pairs = width // PAIR

    def flat(n):
        return jax.ShapeDtypeStruct((rows, n * width), BF16)

    stats = jax.ShapeDtypeStruct((8 * pairs, rows), F32)
    code = jax.ShapeDtypeStruct((rows, PAIR), BF16)
    far = pl.BlockSpec(memory_space=pl.ANY)
    near = pl.BlockSpec(memory_space=pltpu.VMEM)
    tall = jax.ShapeDtypeStruct((rows, width), F32)
    held = [flat(3), flat(2), flat(2), flat(2), flat(1), flat(1), flat(1), tall]
    return pl.pallas_call(
        functools.partial(front_kernel, 256),
        in_specs=[far, far, near, near, far, far, far, far] + [near] * len(vectors),
        out_specs=[far] * 10 + [near] * 6,
        out_shape=[flat(3), flat(2), flat(2), flat(2), flat(1), flat(1), flat(1), tall, flat(1), flat(1)]
        + [stats, stats, code, code, code, code],
        scratch_shapes=[pltpu.VMEM(a.shape, a.dtype) for a in (flat(1), flat(1))]
        + [pltpu.VMEM(w.shape, BF16) for w in (wx, wm, wo, wq)]
        + [pltpu.VMEM((rows, width), BF16)] * 2
        + [pltpu.VMEM((1, rows), jnp.int32)] * 2
        + [pltpu.VMEM(a.shape, a.dtype) for a in held]
        + [
            pltpu.VMEM((pairs, PAIR, rows), F32),
            pltpu.SemaphoreType.DMA((6,)),
            pltpu.SemaphoreType.DMA((10,)),
            pltpu.SemaphoreType.DMA((4,)),
            pltpu.SemaphoreType.DMA((4,)),
        ],
        compiler_params=params(1),
        cost_estimate=cost(22 * rows * width * width + 36 * rows * rows * width, 60 * rows * width),
        name="front",
    )(x, mem, td, md, wx, wm, wo, wq, *vectors)


def feed_kernel(
    count, comm, h1_ref, cc_ref, ct_ref, wco_ref, wi_ref, wo_ref,
    g1_ref, s1_ref, bco_ref, g2_ref, s2_ref, bfo_ref, g3_ref, s3_ref, bfi_ref, out_ref, dh2_ref, dcc_ref, gco_ref, *refs,
):
    if comm:
        gwi_ref, refs = refs[0], refs[1:]
    else:
        gwi_ref, gwo_ref, refs = refs[0], refs[1], refs[2:]
    small_ref, gib_ref, hid_ref, slope_ref, n2_ref, r2_ref, a2b_ref, acc_ref, df_ref, bias_ref, *refs = refs
    step = pl.program_id(0)
    width = acc_ref.shape[1]

    if comm:
        mi_ref, mo_ref, ci_ref, co_ref, send_ref, recv_ref = refs
        wide = ci_ref.shape[-1]
        here = place()
        c = here[1]

        def chunk_copies(j):
            at = pl.ds(pl.multiple_of(j * width, width), width)
            return [
                remote(mi_ref.at[:, :, at], ci_ref.at[:, :, at], send_ref.at[0, j], recv_ref.at[0, j], ("core",), here),
                remote(mo_ref.at[j], co_ref.at[j], send_ref.at[1, j], recv_ref.at[1, j], ("core",), here),
            ]

    @pl.when(step == 0)
    def _():
        if comm:
            greet([("core",)])
        wide = bfi_ref[...].astype(F32)
        for i in range(count):
            bias_ref[i : i + 1] = wide[None, i * width : (i + 1) * width]
        n1, _ = normed(h1_ref[...])
        a1 = n1 * line(g1_ref) + line(s1_ref)
        h2 = a1 + nn(cc_ref[...], wco_ref[...]) + line(bco_ref)
        n2, r2 = normed(h2)
        n2_ref[...] = n2
        r2_ref[...] = jnp.broadcast_to(r2, r2_ref.shape)
        a2 = n2 * line(g2_ref) + line(s2_ref)
        a2b_ref[...] = a2.astype(BF16)
        acc_ref[...] = a2 + line(bfo_ref)

    @pl.when(step < count)
    def _():
        u = nn(a2b_ref[...], wi_ref[...]) + bias_ref[pl.ds(step, 1)]
        cumul = 0.5 * (1.0 + lax.erf(u * 0.7071067811865476))
        density = jnp.exp(-0.5 * u * u) * 0.3989422804014327
        hid = (u * cumul).astype(BF16)
        hid_ref[step] = hid
        slope_ref[step] = cumul + u * density
        acc_ref[...] += nn(hid, wo_ref[...])

    @pl.when(step == count - 1)
    def _():
        n3, r3 = normed(acc_ref[...])
        gain = line(g3_ref)
        out_ref[...] = (n3 * gain + line(s3_ref)).astype(BF16)
        e = ct_ref[...].astype(F32)
        d3 = norm_back(e, n3, r3, gain)
        df = d3.astype(BF16)
        df_ref[...] = df
        acc_ref[...] = d3
        small_ref[0:1] = total(e * n3)
        small_ref[1:2] = total(e)
        small_ref[2:3] = total(df)

    @pl.when(jnp.logical_and(step >= count, step < 2 * count))
    def _():
        j = step - count
        df = df_ref[...]
        du = (nt(df, wo_ref[...]) * slope_ref[j]).astype(BF16)
        sums = tn(du, jnp.ones((du.shape[0], PAIR), BF16))
        quarter = width // gib_ref.shape[0]
        if gib_ref.shape[0] == 4:
            lane = lax.broadcasted_iota(jnp.int32, (quarter // 4, PAIR), 1)
            for i in range(4):
                part = sum(
                    jnp.where(lane == 17 + n, sums[(4 * i + n) * quarter // 4 : (4 * i + n + 1) * quarter // 4], 0.0)
                    for n in range(4)
                )
                gib_ref[i] = part
        else:
            gib_ref[0] = jnp.transpose(sums)[:1]
        acc_ref[...] += nt(du, wi_ref[...])
        go = tn(hid_ref[j], df).astype(BF16)
        gi = tn(a2b_ref[...], du).astype(BF16)
        if comm:
            at = pl.ds(pl.multiple_of(j * width, width), width)
            eight, narrow = gwi_ref.shape[:2]
            gi = gi.reshape(eight, 2, narrow, width)
            go = go.reshape(2, 2, 4, narrow, width)
            gwi_ref[:, :, at] = jnp.where(c == 0, gi[:, 0], gi[:, 1])
            mi_ref[:, :, at] = jnp.where(c == 0, gi[:, 1], gi[:, 0])
            mo_ref[j] = jnp.where(c == 0, go[:, 1], go[:, 0])
            for i in range(4):
                gwi_ref[pl.ds(2 * j, 2), :, pl.ds(wide + i * width, width)] = jnp.where(c == 0, go[:, 0, i], go[:, 1, i])
            for copy in chunk_copies(j):
                copy.start()
        else:
            gwo_ref[...] = go
            gwi_ref[...] = gi

    @pl.when(step == 2 * count)
    def _():
        d2 = acc_ref[...]
        n2 = n2_ref[...]
        dh2 = norm_back(d2, n2, r2_ref[:, :1], line(g2_ref))
        dh2_ref[...] = dh2
        dco = dh2.astype(BF16)
        dcc_ref[...] = nt(dco, wco_ref[...]).astype(BF16)
        gco_ref[...] = tn(cc_ref[...], dco).astype(BF16)
        small_ref[3:4] = total(d2 * n2)
        small_ref[4:5] = total(d2)
        small_ref[5:6] = total(dco)
        small_ref[6:8] = jnp.zeros((2, d2.shape[1]), F32)

    if comm:

        @pl.when(step > count)
        def _():
            j = step - count - 1
            at = pl.ds(pl.multiple_of(j * width, width), width)
            for copy in chunk_copies(j):
                copy.wait()
            gwi_ref[:, :, at] += ci_ref[:, :, at]
            for i in range(4):
                gwi_ref[pl.ds(2 * j, 2), :, pl.ds(wide + i * width, width)] += co_ref[j, :, i]


def feed(size, comm, h1, cc, ct, wco, wi, wo, vectors):
    rows, width = h1.shape
    wide = wi.shape[1]
    chunk = width
    count = wide // chunk

    def weight(s):
        return jnp.where(s < count, s, jnp.minimum(s - count, count - 1))

    def early(s):
        return jnp.clip(s - count, 0, count - 1)

    flat = whole((rows, width))
    square = whole((width, width))
    scratch = [
        pltpu.VMEM((count, rows, chunk), BF16),
        pltpu.VMEM((count, rows, chunk), F32),
        pltpu.VMEM((rows, width), F32),
        pltpu.VMEM((rows, 128), F32),
        pltpu.VMEM((rows, width), BF16),
        pltpu.VMEM((rows, width), F32),
        pltpu.VMEM((rows, width), BF16),
        pltpu.VMEM((8, width), F32),
    ]
    if comm:
        narrow = width // size
        gib_shape = jax.ShapeDtypeStruct((size, narrow, PAIR), F32)
        gib_spec = pl.BlockSpec((4, narrow, PAIR), lambda s: (early(s), 0, 0))
        grad_specs = [whole((size // 2, narrow, 2 * wide))]
        grad_shapes = [(size // 2, narrow, 2 * wide)]
        scratch += [
            pltpu.VMEM((size // 2, narrow, wide), BF16),
            pltpu.VMEM((count, 2, 4, narrow, width), BF16),
            pltpu.VMEM((size // 2, narrow, wide), BF16),
            pltpu.VMEM((count, 2, 4, narrow, width), BF16),
            pltpu.SemaphoreType.DMA((2, count)),
            pltpu.SemaphoreType.DMA((2, count)),
        ]
    else:
        gib_shape = jax.ShapeDtypeStruct((count, 1, width), F32)
        gib_spec = pl.BlockSpec((1, 1, chunk), lambda s: (early(s), 0, 0))
        grad_specs = [
            pl.BlockSpec((width, chunk), lambda s: (0, early(s))),
            pl.BlockSpec((chunk, width), lambda s: (early(s), 0)),
        ]
        grad_shapes = [(width, wide), (wide, width)]
    return pl.pallas_call(
        functools.partial(feed_kernel, count, comm),
        grid=(2 * count + 1,),
        in_specs=[
            flat, flat, flat, square,
            pl.BlockSpec((width, chunk), lambda s: (0, weight(s))),
            pl.BlockSpec((chunk, width), lambda s: (weight(s), 0)),
        ]
        + [whole(v.shape) for v in vectors],
        out_specs=[flat, flat, flat, square]
        + grad_specs
        + [whole((8, width)), gib_spec],
        out_shape=[
            jax.ShapeDtypeStruct((rows, width), BF16),
            jax.ShapeDtypeStruct((rows, width), F32),
            jax.ShapeDtypeStruct((rows, width), BF16),
            jax.ShapeDtypeStruct((width, width), BF16),
        ]
        + [jax.ShapeDtypeStruct(a, BF16) for a in grad_shapes]
        + [
            jax.ShapeDtypeStruct((8, width), F32),
            gib_shape,
        ],
        scratch_shapes=scratch,
        compiler_params=params(2 if comm else None),
        cost_estimate=cost(
            12 * rows * width * wide + 6 * rows * width * width, 12 * width * wide + 16 * rows * width
        ),
        name="feed",
    )(h1, cc, ct, wco, wi, wo, *vectors)


def outputs_kernel(moves, count, line, *refs):
    pieces, rest = refs[:count], refs[count:]
    out_ref, dx_ref, dm_ref, dmi_ref = rest[:4]
    outs = rest[4:]
    for piece, first, wide, which, row, col in moves:
        ref = pieces[piece]
        outs[which][row : row + ref.shape[0], col : col + wide] = ref[:, first : first + wide].astype(F32)
    turned, result, dx, dm = outs[-4:]
    turned[...] = jnp.transpose(pieces[line[0]][:, line[1] : line[1] + PAIR].astype(F32))
    result[...] = out_ref[...]
    dx[...] = dx_ref[...]
    dm[...] = (dm_ref[...] + dmi_ref[...].astype(F32)).astype(BF16)


def outputs(pieces, moves, line, shapes, out, dx, dm, dmi):
    ins = tuple(pieces) + (out, dx, dm, dmi)
    result = jax.ShapeDtypeStruct(out.shape, BF16)
    return pl.pallas_call(
        functools.partial(outputs_kernel, moves, len(pieces), line),
        out_shape=[jax.ShapeDtypeStruct(a, F32) for a in shapes]
        + [jax.ShapeDtypeStruct((PAIR, pieces[0].shape[0]), F32), result, result, result],
        compiler_params=params(),
        cost_estimate=cost(0, 12 << 20),
        name="outputs",
    )(*ins)


def moved(pieces, targets):
    out = []
    for n, (start, wide) in enumerate(pieces):
        for first, cols, which, row, col in targets:
            low, high = max(start, first), min(start + wide, first + cols)
            if low < high:
                out.append((n, low - start, high - low, which, row, col + low - first))
    return out


def schedule_of(flows, kernel):
    entries = [
        (start, order, name, start, stop)
        for order, name in enumerate(flows)
        for start, stop in PLAN[name][kernel]
    ]
    return tuple(([flows[name]], start, stop) for _, _, name, start, stop in sorted(entries))


def swap_sum(part, axis, pairs):
    came = lax.ppermute(part, axis, pairs)
    return part.astype(F32) + came.astype(F32)


def sum_scatter(grad, size, order):
    rows, cols = grad.shape
    bits = size.bit_length() - 1
    me = lax.axis_index("dp")
    now = grad.reshape((2,) * bits + (rows // size, cols))
    left = list(range(bits))[::-1]
    for bit in [b for b in order if b < bits] + [b for b in range(bits) if b not in order]:
        axis = left.index(bit)
        mine = (me >> bit) & 1
        keep = lax.dynamic_index_in_dim(now, mine, axis, keepdims=False)
        send = lax.dynamic_index_in_dim(now, 1 - mine, axis, keepdims=False)
        came = lax.ppermute(send, "dp", [(i, i ^ (1 << bit)) for i in range(size)])
        now = (keep.astype(F32) + came.astype(F32)).astype(BF16)
        left.pop(axis)
    return swap_sum(now, "sp", [(0, 1), (1, 0)])


def per_device(
    size,
    inputs,
    memory,
    target_docs,
    memory_docs,
    cotangent,
    w_qkv,
    b_q,
    b_v,
    w_so,
    b_so,
    g_one,
    s_one,
    w_cq,
    b_cq,
    w_ckv,
    b_cv,
    w_co,
    b_co,
    g_two,
    s_two,
    w_fi,
    b_fi,
    w_fo,
    b_fo,
    g_three,
    s_three,
):
    rows, width = inputs.shape[1:]
    wide = b_fi.shape[0]
    comm = size == 16
    narrow, broad = width // size, wide // size
    x, mem, ct = inputs[0], memory[0], cotangent[0]
    qkv, mkv, kvo, mkvo, cq, ctx, cc, h1, x_o, mem_o, lse, clse, t_oth, m_oth, t_own, m_own = front(
        x, mem, target_docs, memory_docs, w_qkv, w_ckv, w_so, w_cq, (b_q, b_v, b_cv, b_so, g_one, s_one, b_cq)
    )
    output, dh2, dcc, gco, gwi, *gwo, small_a, gib = feed(
        size, comm, h1, cc, ct, w_co, w_fi, w_fo,
        (g_one, s_one, b_co, g_two, s_two, b_fo, g_three, s_three, b_fi),
    )
    gib = gib.reshape(width, PAIR) if comm else gib.reshape(1, wide)

    block = (2, 2, 2, 2, narrow) if comm else (width,)
    at_cross, at_self, flows = (), (), {}
    if comm:
        late_shape = block + (2 * width,)
        sources = {
            "T0": (gwi.reshape(block[:3] + gwi.shape[1:]), block[:3] + gwi.shape[1:], BLOCK[:3]),
            "T1a": (("ref", MIDDLE), block + (3 * width,), BLOCK),
            "T1b": (None, late_shape, BLOCK),
            "G": (("ref", GRADS), block + (3 * width + 2 * PAIR,), BLOCK),
        }
        for name, (source, cols, hops, _, _) in PLAN.items():
            array, shape, dims = sources[source]
            flows[name] = Flow(array, shape, hops, dims, cols)
        at_cross = schedule_of(flows, 3)
        at_self = schedule_of(flows, 4)
    dm, dmo, gcvb, dh1, dsc, late, small_b, *early = cross_backward(
        block, cq, mkv, mkvo, dcc, cc, clse, t_own, m_own, m_oth, mem, mem_o, w_ckv,
        gco, dh2, h1, ctx, w_cq, w_so, g_one, s_one, at_cross,
    )
    for name, flow in flows.items():
        if PLAN[name][0] == "T1b":
            flow.array = late
    dx, dm_in, *made = self_backward(
        block, qkv, kvo, dsc, ctx, lse, t_own, t_oth, x, x_o, w_qkv, dh1, (small_a, small_b, gcvb, gib), dmo, at_self
    )
    if comm:
        targets = {
            "T0": [(0, wide, 2, 0, 0)] + [(wide + i * width, width, 3, i * narrow, 0) for i in range(4)],
            "T1a": [(0, width, 4, 0, 0), (width, 2 * width, 1, 0, 0)],
            "T1b": [(0, width, 5, 0, 0), (width, width, 6, 0, 0)],
            "G": [
                (g * 6 * PAIR + i * 2 * PAIR, 2 * PAIR, 0, 0, i * width + g * 2 * PAIR)
                for g in range(width // PAIR // 2)
                for i in range(3)
            ],
        }
        moves, line = [], None
        for n, (source, cols, *_) in enumerate(PLAN.values()):
            moves += [(n,) + m[1:] for m in moved([cols], targets[source])]
            if source == "G" and cols[0] <= 3 * width < sum(cols):
                line = n, 3 * width - cols[0]
        shapes = [(narrow, 3 * width), (narrow, 2 * width), (narrow, wide), (broad, width)] + [(narrow, width)] * 3
        t_qkv, t_cmem, t_fin, t_fout, t_cout, t_cquery, t_out, lines, output, derivative, grad_memory = outputs(
            [f.array for f in flows.values()], moves, line, shapes, output, dx, dm, dm_in
        )
    else:
        (early,), (made,) = early, made
        columns = made[:, 3 * width : 3 * width + PAIR]
        groups = range(width // PAIR // 2)
        gqkv = jnp.concatenate(
            [made[:, (g * 6 + 2 * i) * PAIR : (g * 6 + 2 * i + 2) * PAIR] for i in range(3) for g in groups], axis=1
        )
        t_fin, t_fout, t_cout, t_cquery, t_out, t_cmem, t_qkv, lines = (
            sum_scatter(g, size, (0, 1, 2, 3))
            for g in (
                gwi, gwo[0], early[:, :width], late[:, :width], late[:, width:], early[:, width:], gqkv, columns
            )
        )
        lines, derivative = lines.T, dx
        grad_memory = (dm + dm_in.astype(F32)).astype(BF16)
    t_gthree, t_sthree, t_fobias, t_gtwo, t_stwo, t_cobias = (lines[i] for i in range(6))
    t_cqbias, t_gone, t_sone, t_obias = (lines[i] for i in range(8, 12))
    t_cvbias, t_qbias, t_vbias = lines[16], lines[21], lines[22]
    if comm:
        t_fibias = lines[17:21].reshape(-1)
    else:
        t_fibias = lax.psum(lax.psum_scatter(gib[0], "dp", scatter_dimension=0, tiled=True), "sp")
    return (
        output[None],
        derivative[None],
        grad_memory[None],
        t_qkv,
        t_qbias,
        t_vbias,
        t_out,
        t_obias,
        t_gone,
        t_sone,
        t_cquery,
        t_cqbias,
        t_cmem,
        t_cvbias,
        t_cout,
        t_cobias,
        t_gtwo,
        t_stwo,
        t_fin,
        t_fibias,
        t_fout,
        t_fobias,
        t_gthree,
        t_sthree,
    )


def solution(mesh):
    split = P("dp", "sp", None)
    in_specs = (split, split, P("dp", "sp"), P("dp", "sp"), split) + (P(),) * 21
    matrix, vector = P("dp", None), P("dp")
    out_specs = (
        split, split, split,
        matrix, vector, vector,
        matrix, vector, vector, vector,
        matrix, vector,
        matrix, vector,
        matrix, vector, vector, vector,
        matrix, vector,
        matrix, vector, vector, vector,
    )
    return jax.shard_map(
        functools.partial(per_device, mesh.shape["dp"]),
        mesh=mesh, in_specs=in_specs, out_specs=out_specs, check_vma=False,
    )
```

```python
import functools

import jax
import jax.numpy as jnp
from jax import lax
from jax.experimental import pallas as pl
from jax.experimental.pallas import tpu as pltpu
from jax.sharding import PartitionSpec as P

HD = 64
PAIR = 2 * HD
EPS = 1e-05
FAR = 1.0e9
VMEM = 60 * 1024 * 1024
F32 = jnp.float32
BF16 = jnp.bfloat16


def nn(a, b):
    return lax.dot_general(a, b, (((1,), (0,)), ((), ())), preferred_element_type=F32)


def nt(a, b):
    return lax.dot_general(a, b, (((1,), (1,)), ((), ())), preferred_element_type=F32)


def tn(a, b):
    return lax.dot_general(a, b, (((0,), (0,)), ((), ())), preferred_element_type=F32)


def params(collective=None):
    if collective is None:
        return pltpu.CompilerParams(vmem_limit_bytes=VMEM)
    return pltpu.CompilerParams(
        vmem_limit_bytes=VMEM, collective_id=collective, has_side_effects=True
    )


def cost(flops, moved):
    return pl.CostEstimate(flops=int(flops), bytes_accessed=int(moved), transcendentals=0)


def normed(h):
    centred = h - jnp.mean(h, axis=-1, keepdims=True)
    rstd = lax.rsqrt(jnp.mean(centred * centred, axis=-1, keepdims=True) + EPS)
    return centred * rstd, rstd


def norm_back(grad, n, rstd, gain):
    scaled = grad * gain
    centre = jnp.mean(scaled, axis=-1, keepdims=True)
    along = jnp.mean(scaled * n, axis=-1, keepdims=True)
    return rstd * (scaled - centre - n * along)


def total(a):
    return jnp.sum(a.astype(F32), axis=0, keepdims=True)


def place():
    me = lax.axis_index("dp")
    return me, me % 2, (me // 2) % 2, me // 4, lax.axis_index("sp")


def flipped(at, hops):
    me, c, x, z, sp = at
    for hop in hops:
        if hop == "core":
            me, c = me + 1 - 2 * c, 1 - c
        elif hop == "x":
            me, x = me + 2 - 4 * x, 1 - x
        elif hop == "z1":
            me, z = me + 4 - 8 * (z % 2), z + 1 - 2 * (z % 2)
        elif hop == "z2":
            me, z = me + 8 - 16 * (z // 2), z + 2 - 4 * (z // 2)
        else:
            sp = 1 - sp
    return me, c, x, z, sp


def partner(hops, at=None):
    there = flipped(at or place(), hops)
    return {"dp": there[0], "sp": there[4]}


def greet(groups, at=None):
    groups = sorted({tuple("y" if h[0] == "y" else h for h in hops) for hops in groups})
    barrier = pltpu.get_barrier_semaphore()
    for hops in groups:
        pl.semaphore_signal(barrier, inc=1, device_id=partner(hops, at), device_id_type=pl.DeviceIdType.MESH)
    pl.semaphore_wait(barrier, len(groups))


def remote(src, dst, send, recv, hops, at=None):
    return pltpu.make_async_remote_copy(
        src_ref=src, dst_ref=dst, send_sem=send, recv_sem=recv,
        device_id=partner(hops, at), device_id_type=pl.DeviceIdType.MESH,
    )


PLAN = {
    "T0_0": ("T0", (0, 256), ("z1", "x", "yr", "z2", "yg"), ((0, 2), (2, 3), (3, 4), (4, 5), (5, 6)), ()),
    "T0_1": ("T0", (256, 2048), ("yr", "z1", "x", "z2", "yg"), ((0, 4), (4, 6), (6, 7)), ((0, 7), (7, 11))),
    "T0_2": ("T0", (2304, 1792), ("x", "yr", "z1", "z2", "yg"), ((0, 4), (4, 6), (6, 7)), ((0, 7), (7, 11))),
    "T0_3": ("T0", (4096, 2048), ("z1", "x", "yr", "z2", "yg"), ((0, 4), (4, 6), (6, 7)), ((0, 7), (7, 11))),
    "T1a_0": ("T1a", (0, 512), ("core", "yr", "z1", "x", "z2", "yg"), ((6, 7),), ((0, 5), (5, 9), (9, 11), (11, 14), (14, 17))),
    "T1a_1": ("T1a", (512, 768), ("core", "z1", "x", "yr", "z2", "yg"), ((6, 7),), ((0, 10), (10, 12), (12, 22), (22, 33), (33, 41))),
    "T1a_2": ("T1a", (1280, 1024), ("core", "x", "z1", "z2", "y"), ((6, 7),), ((0, 7), (7, 11), (11, 21), (21, 40))),
    "T1b_0": ("T1b", (0, 1280), ("core", "x", "z1", "z2", "y"), (), ((0, 3), (3, 9), (9, 12), (12, 28), (28, 47))),
    "T1b_1": ("T1b", (1280, 256), ("core", "z1", "x", "z2", "y"), (), ((0, 2), (2, 8), (8, 10), (10, 11), (11, 13))),
    "G1_0": ("G", (0, 512), ("core", "yr", "x", "z1", "z2", "yg"), (), ((8, 10), (10, 29), (29, 36), (36, 44), (44, 48), (48, 51))),
    "G1_1": ("G", (512, 256), ("core", "x", "z1", "yr", "z2", "yg"), (), ((8, 9), (9, 11), (11, 16), (16, 20), (20, 25), (25, 32))),
    "G2_0": ("G", (768, 256), ("core", "z1", "x", "z2", "y"), (), ((10, 11), (11, 21), (21, 27), (27, 34), (34, 42))),
    "G2_1": ("G", (1024, 512), ("core", "x", "z1", "z2", "y"), (), ((10, 12), (12, 19), (19, 35), (35, 43), (43, 49))),
    "G3_0": ("G", (1536, 128), ("core", "z1", "x", "z2", "y"), (), ((11, 12), (12, 18), (18, 24), (24, 31), (31, 38))),
    "G3_1": ("G", (1664, 256), ("core", "z1", "x", "z2", "y"), (), ((11, 12), (12, 23), (23, 30), (30, 37), (37, 45))),
    "G4_0": ("G", (1920, 512), ("core", "x", "z1", "z2", "y"), (), ((12, 15), (15, 26), (26, 39), (39, 46), (46, 50))),
}
BLOCK = ("z2", "z1", "x", "core")


class Part:
    def __init__(self, hop, shape, dims, cols=None):
        self.hops = hops = hop if isinstance(hop, tuple) else (hop,)
        self.groups = [(h,) for h in hops] + ([hops] if len(hops) > 1 else [])
        self.dims = dims
        self.cols = cols or (0, shape[-1])
        self.shape = shape = tuple(shape[:-1]) + (self.cols[1],)
        for h in hops:
            if h in dims:
                at = dims.index(h)
                shape, dims = shape[:at] + shape[at + 1 :], dims[:at] + dims[at + 1 :]
            elif h != "y":
                shape = shape[:-1] + (shape[-1] // 2 if h == "yr" else 2 * shape[-1],)
        self.after, self.left = shape, dims
        self.came = self.shape if hops == ("yg",) else shape

    def share(self, at):
        _, c, x, z, sp = at
        first, wide = self.cols
        index = [slice(None)] * (len(self.shape) - 1) + [pl.ds(first, wide)]
        for h in self.hops:
            if h in self.dims:
                index[self.dims.index(h)] = {"core": c, "x": x, "z1": z % 2, "z2": z // 2}[h]
            elif h == "yr":
                half = wide // 2
                index[-1] = pl.ds(pl.multiple_of(first + sp * half, 128), half)
        return tuple(index)

    def copies(self, src, held, made, came, send, recv, local, at):
        out = [
            remote(src.at[self.share(flipped(at, g))], came[i], send.at[i], recv.at[i], g, at)
            for i, g in enumerate(self.groups)
        ]
        if not held:
            out.append(pltpu.make_async_copy(src.at[self.share(at)], made, local))
        return out

    def add(self, src, held, made, came, at):
        if self.hops == ("yg",):
            wide, sp = self.shape[-1], at[4]
            lead = (slice(None),) * (len(self.shape) - 1)
            made[lead + (pl.ds(pl.multiple_of(sp * wide, 128), wide),)] = src[self.share(at)]
            made[lead + (pl.ds(pl.multiple_of((1 - sp) * wide, 128), wide),)] = came[0][...]
        elif len(came) > 1:
            mine = src[self.share(at)] if held else made[...]
            one, two, three = (c[...].astype(F32) for c in came)
            made[...] = ((mine.astype(F32) + one) + (two + three)).astype(BF16)
        elif held:
            made[...] = src[self.share(at)] + came[0][...]
        else:
            made[...] += came[0][...]


class Flow:
    def __init__(self, array, shape, hops, dims=BLOCK, cols=None):
        self.array, self.shape, self.dims, self.cols = array, tuple(shape), dims, cols
        self.hops = list(hops)

    def step(self):
        part = Part(self.hops.pop(0), self.shape, self.dims, self.cols)
        self.shape, self.dims, self.cols = part.after, part.left, None
        return part


class Window:
    def __init__(self, start, stop, joint):
        self.start, self.stop, self.joint = start, stop, joint
        self.parts, self.sources, self.keeps = [], [], []


class Joint:
    def __init__(self):
        self.window = None


def plan(schedule):
    windows, arrays, latest = [], [], {}
    for n, (flows, start, stop, *joint) in enumerate(schedule):
        window = Window(start, stop, bool(joint))
        if joint:
            joint[0].window = n
        for i, flow in enumerate(flows):
            if flow in latest:
                source = ("part",) + latest[flow]
                before = windows[latest[flow][0]]
                before.keeps[latest[flow][1]] = False
            elif isinstance(flow.array, Joint):
                source = ("joint", flow.array.window)
            elif isinstance(flow.array, tuple):
                source = flow.array
            else:
                known = [k for k, a in enumerate(arrays) if a is flow.array]
                if not known:
                    arrays.append(flow.array)
                source = ("in", known[0] if known else len(arrays) - 1)
            window.parts.append(flow.step())
            window.sources.append(source)
            window.keeps.append(not joint)
            if not joint:
                latest[flow] = (n, i)
        windows.append(window)
    return windows, arrays, latest


def carrying(body, own, windows, arrays, grid, also, finale):
    ins, outs, held = own

    def kernel(*refs):
        refs = list(refs)

        def take(n):
            got = refs[:n]
            del refs[:n]
            return got

        my_in, arr = take(ins), take(arrays)
        my_out = take(outs)
        given = [[take(1)[0] if k else None for k in w.keeps] for w in windows]
        my_held = take(held)
        made, came, joints = [], [], []
        for w, g in zip(windows, given):
            if w.joint:
                joint, col, views = take(1)[0], 0, []
                for q in w.parts:
                    views.append(joint.at[(slice(None),) * (len(q.after) - 1) + (pl.ds(col, q.after[-1]),)])
                    col += q.after[-1]
                joints.append(joint)
                made.append(views)
            else:
                joints.append(None)
                made.append([ref if ref is not None else take(1)[0] for ref in g])
            came.append([take(len(q.groups)) for q in w.parts])
        mine = my_in + my_out + my_held
        step = pl.program_id(0)
        groups = [g for w in windows for q in w.parts for g in q.groups] + list(also)
        if groups:
            here = place()
            pl.when(step == 0)(lambda: greet(groups, here))
        if windows:
            send, recv, local = refs
        copies, sources, base = [], [], 0
        for w, m, c in zip(windows, made, came):
            now, froms = [], []
            for i, q in enumerate(w.parts):
                kind = w.sources[i]
                if kind[0] == "in":
                    src = arr[kind[1]]
                elif kind[0] == "ref":
                    src = mine[kind[1]]
                elif kind[0] == "joint":
                    src = joints[kind[1]]
                else:
                    src = made[kind[1]][kind[2]]
                held_here = kind[0] != "in"
                froms.append((src, held_here))
                now += q.copies(
                    src, held_here, m[i], c[i], send.at[base], recv.at[base], local.at[base], here
                )
                base += 1
            copies.append(now)
            sources.append(froms)

        def phase(number):
            for n, w in enumerate(windows):
                if w.stop == number:
                    for copy in copies[n]:
                        copy.wait()
                    for q, (src, held_here), m, c in zip(w.parts, sources[n], made[n], came[n]):
                        q.add(src, held_here, m, c, here)
            for n, w in enumerate(windows):
                if w.start == number:
                    for copy in copies[n]:
                        copy.start()

        used = sorted({w.start for w in windows} | {w.stop for w in windows})
        for number in used:
            if number < grid:
                pl.when(step == number)(functools.partial(phase, number))
        body(*mine)
        for number in used:
            if number >= grid:
                pl.when(step == grid - 1)(functools.partial(phase, number))
        if finale:
            pl.when(step == grid - 1)(lambda: finale(*mine))

    return kernel


def run(
    body, name, grid, ins, in_specs, outs, out_specs, held=(), schedule=(), collective=None,
    flops=0, moved=0, also=(), finale=None,
):
    in_specs, outs, out_specs, held = list(in_specs), list(outs), list(out_specs), list(held)
    windows, arrays, latest = plan(schedule)
    own = len(outs)
    kernel = carrying(body, (len(ins), own, len(held)), windows, len(arrays), grid, also, finale)
    in_specs += [pl.BlockSpec(memory_space=pl.ANY)] * len(arrays)
    order, count = [], 0
    for n, w in enumerate(windows):
        if w.joint:
            shape = w.parts[0].after[:-1] + (sum(q.after[-1] for q in w.parts),)
            held.append(pltpu.VMEM(shape, BF16))
        for i, (q, k) in enumerate(zip(w.parts, w.keeps)):
            if w.joint:
                continue
            if k:
                outs.append(jax.ShapeDtypeStruct(q.after, BF16))
                out_specs.append(whole(q.after))
                order.append((n, i))
            else:
                held.append(pltpu.VMEM(q.after, BF16))
        held += [pltpu.VMEM(q.came, BF16) for q in w.parts for _ in q.groups]
        count += len(w.parts)
    if windows:
        held += [pltpu.SemaphoreType.DMA((count, 3))] * 2 + [pltpu.SemaphoreType.DMA((count,))]
    results = pl.pallas_call(
        kernel,
        grid=(grid,),
        in_specs=in_specs,
        out_specs=out_specs,
        out_shape=outs,
        scratch_shapes=held,
        compiler_params=params(collective if windows or also else None),
        cost_estimate=cost(flops, moved),
        name=name,
    )(*ins, *arrays)
    for flow, where in latest.items():
        flow.array = results[own + order.index(where)]
    return results[:own]


def head_masks(dtype):
    lane = lax.broadcasted_iota(jnp.int32, (1, PAIR), 1)
    low = jnp.where(lane < HD, 1.0, 0.0)
    return low.astype(dtype), (1.0 - low).astype(dtype)


def query_code(code):
    lane = lax.broadcasted_iota(jnp.int32, code.shape, 1)
    return jnp.where(lane < 4, (code.astype(F32) - 1.0) * FAR, 0.0).astype(BF16)


def masked(s, diagonal):
    low, high = s[:-diagonal], s[-diagonal:]
    row = lax.broadcasted_iota(jnp.int32, high.shape, 0)
    col = lax.broadcasted_iota(jnp.int32, high.shape, 1)
    high = jnp.where(row <= col, high, -FAR)
    return jnp.concatenate([low, high], axis=0) if low.shape[0] else high


def softmax_over(jobs):
    results = []
    ready = nt(jobs[0][0], jobs[0][2])
    for n, (_, values_t, _, diagonal) in enumerate(jobs):
        s = ready
        if n + 1 < len(jobs):
            ready = nt(jobs[n + 1][0], jobs[n + 1][2])
        if diagonal:
            s = masked(s, diagonal)
        peak = jnp.max(s, axis=0, keepdims=True)
        e = jnp.exp(s - peak)
        norm = jnp.sum(e, axis=0, keepdims=True)
        results.append((nn(values_t, e.astype(BF16)) / norm, peak + jnp.log(norm)))
    return results


def pair_spec(rows, offset):
    return pl.BlockSpec((rows, PAIR), lambda p: (0, p + offset))


def whole(shape):
    return pl.BlockSpec(shape, lambda *_: (0,) * len(shape))


def delta_rows(g, o):
    prod = g.astype(F32) * o.astype(F32)
    upper = prod.astype(BF16)
    lower = (prod - upper.astype(F32)).astype(BF16)
    row = lax.broadcasted_iota(jnp.int32, (8, PAIR), 0)
    lane = lax.broadcasted_iota(jnp.int32, (8, PAIR), 1)
    pick = jnp.where(row == lane // HD, 1.0, 0.0).astype(BF16)
    return nt(pick, upper) + nt(pick, lower)


def back_pieces(jobs):
    def products(job):
        keys, values, q, g = job[:4]
        return nt(keys, q), nt(values, g)

    ready = products(jobs[0])
    for n, (_, _, _, _, lse, delta, causal) in enumerate(jobs):
        s, dp = ready
        if n + 1 < len(jobs):
            ready = products(jobs[n + 1])
        if causal:
            s = masked(s, s.shape[0])
        p = jnp.exp(s - lse)
        yield n, p.astype(BF16), (p * (dp - delta)).astype(BF16)


def cross_backward_kernel(
    size, pairs, q_ref, k_ref, v_ref, ko_ref, vo_ref, g_ref, o_ref, lse_ref, t_ref, own_ref, oth_ref,
    m_ref, mo_ref, wk_ref, wv_ref, gco_hbm, dh2_hbm, h1_hbm, ctx_hbm, wcq_hbm, wso_hbm, g1_ref, s1_ref,
    dm_out, dmo_out, gb_ref, dh1_ref, dsc_ref, late_ref, small_ref, grad_ref,
    dm_ref, dmo_acc, mt_ref, mot_ref, dcq_ref, dmo_ref, gco_ref, dh2_ref, h1_ref, ctx_ref, wcq_ref, wso_ref, move_ref,
):
    step = pl.program_id(0)
    rows, width = m_ref.shape
    lead = (slice(None),) * (len(grad_ref.shape) - 1)

    loads = [
        pltpu.make_async_copy(src, dst, move_ref.at[i])
        for i, (src, dst) in enumerate(
            (
                (gco_hbm, gco_ref), (dh2_hbm, dh2_ref), (h1_hbm, h1_ref), (ctx_hbm, ctx_ref), (wcq_hbm, wcq_ref),
                (wso_hbm, wso_ref),
            )
        )
    ]
    gives = [
        pltpu.make_async_copy(src, dst, move_ref.at[6 + i])
        for i, (src, dst) in enumerate(((dm_ref, dm_out), (dmo_ref, dmo_out)))
    ]

    def put(ref, col, grad):
        to = pl.ds(pl.multiple_of(col, PAIR), grad.shape[1])
        ref[lead + (to,)] = grad.astype(BF16).reshape(ref.shape[:-1] + (grad.shape[1],))

    @pl.when(step == 0)
    def _():
        for copy in loads:
            copy.start()
        mt_ref[...] = jnp.transpose(m_ref[...])
        mot_ref[...] = jnp.transpose(mo_ref[...])

    @pl.when(step == 1)
    def _():
        loads[0].wait()
        put(grad_ref, 0, gco_ref[...])

    @pl.when(step < pairs)
    def _():
        count = rows // size
        halves = [(k_ref, v_ref, own_ref, mt_ref, dm_ref), (ko_ref, vo_ref, oth_ref, mot_ref, dmo_acc)]
        cols = pl.ds(pl.multiple_of(step * PAIR, PAIR), PAIR)
        dq = [[0.0, 0.0] for _ in range(count)]
        gk = gv = gb = 0.0
        for kr, vr, code, mem, acc in halves:
            keys = jnp.concatenate([kr[...], code[...]], axis=1)
            values = vr[...]
            turned = jnp.transpose(kr[...])
            dk = dv = 0.0
            jobs = list(backward_pieces(size, q_ref, g_ref, o_ref, lse_ref, t_ref))
            for n, p, ds in back_pieces([(keys, values, q, gm, lse, delta, False) for _, _, _, gm, q, lse, delta in jobs]):
                block, head, qm, gm = jobs[n][:4]
                dk = dk + nn(ds, qm)
                dv = dv + nn(p, gm)
                dq[block][head] = dq[block][head] + nn(turned[head * HD : (head + 1) * HD], ds)
            both = jnp.concatenate([dk.astype(BF16), dv.astype(BF16)], axis=1)
            grad = nn(mem[...], both)
            gk, gv = gk + grad[:, :PAIR], gv + grad[:, PAIR:]
            gb = gb + total(both[:, PAIR:])
            dm = nt(both, jnp.concatenate([wk_ref[...], wv_ref[...]], axis=1))

            @pl.when(step == 0)
            def _():
                acc[...] = dm

            @pl.when(step > 0)
            def _():
                acc[...] += dm

        for block in range(count):
            dcq_ref[block * size : (block + 1) * size, cols] = upright(dq[block]).astype(BF16)
        put(grad_ref, width + step * PAIR, gk)
        put(grad_ref, 2 * width + step * PAIR, gv)
        gb_ref[:, cols] = gb

    @pl.when(step == pairs)
    def _():
        dmo_ref[...] = dmo_acc[...].astype(BF16)
        for copy in gives:
            copy.start()
        for copy in loads[1:]:
            copy.wait()
        gain = line(g1_ref)
        n1, r1 = normed(h1_ref[...])
        a1b = (n1 * gain + line(s1_ref)).astype(BF16)
        dcq = dcq_ref[...]
        d1 = dh2_ref[...] + nt(dcq, wcq_ref[...])
        dh1 = norm_back(d1, n1, r1, gain)
        dh1_ref[...] = dh1
        dso = dh1.astype(BF16)
        dsc_ref[...] = nt(dso, wso_ref[...]).astype(BF16)
        put(late_ref, 0, tn(a1b, dcq))
        put(late_ref, width, tn(ctx_ref[...], dso))
        small_ref[0:1] = total(dcq)
        small_ref[1:2] = total(d1 * n1)
        small_ref[2:3] = total(d1)
        small_ref[3:4] = total(dso)
        small_ref[4:8] = jnp.zeros((4, width), F32)
        for copy in gives:
            copy.wait()


MIDDLE = 30


def cross_backward(block, cq, kv, kvo, g, o, lse, t, own, oth, m, mo, w, gco, dh2, h1, ctx, wcq, wso, gain, shift, schedule):
    rows, width = cq.shape
    pairs = width // PAIR

    def pair_of(size, offset):
        return pl.BlockSpec((size, PAIR), lambda s: (0, jnp.minimum(s, pairs - 1) + offset))

    flat, square = whole((rows, width)), whole((width, width))
    outs = [
        jax.ShapeDtypeStruct((rows, width), F32),
        jax.ShapeDtypeStruct((rows, width), BF16),
        jax.ShapeDtypeStruct((1, width), F32),
        jax.ShapeDtypeStruct((rows, width), F32),
        jax.ShapeDtypeStruct((rows, width), BF16),
        jax.ShapeDtypeStruct(block + (2 * width,), BF16),
        jax.ShapeDtypeStruct((8, width), F32),
    ]
    far = pl.BlockSpec(memory_space=pl.ANY)
    specs = [far, far, whole((1, width)), flat, flat, whole(block + (2 * width,)), whole((8, width))]
    held = []
    if schedule:
        held.append(pltpu.VMEM(block + (3 * width,), BF16))
    else:
        outs.append(jax.ShapeDtypeStruct(block + (3 * width,), BF16))
        specs.append(whole(block + (3 * width,)))
    held += [
        pltpu.VMEM((rows, width), F32),
        pltpu.VMEM((rows, width), F32),
        pltpu.VMEM((width, rows), BF16),
        pltpu.VMEM((width, rows), BF16),
        pltpu.VMEM((rows, width), BF16),
        pltpu.VMEM((rows, width), BF16),
    ]
    held += [pltpu.VMEM(a.shape, a.dtype) for a in (gco, dh2, h1, ctx, wcq, wso)] + [pltpu.SemaphoreType.DMA((8,))]
    return run(
        functools.partial(cross_backward_kernel, 256, pairs), "cross_backward", pairs + 1,
        (cq, kv, kv, kvo, kvo, g, o, lse, t, own, oth, m, mo, w, w, gco, dh2, h1, ctx, wcq, wso, gain, shift),
        [
            pair_of(rows, 0), pair_of(rows, 0), pair_of(rows, pairs), pair_of(rows, 0), pair_of(rows, pairs),
            pair_of(rows, 0), pair_of(rows, 0),
            pl.BlockSpec((8, rows), lambda s: (jnp.minimum(s, pairs - 1), 0)),
            whole((rows, 128)), whole((rows, 128)), whole((rows, 128)), flat, flat,
            pair_of(width, 0), pair_of(width, pairs),
            far, far, far, far, far, far, whole(gain.shape), whole(shift.shape),
        ],
        outs, specs, held, schedule, 3,
        64 * rows * rows * width + 24 * rows * width * width, 40 * rows * width,
    )


def upright(heads):
    return jnp.transpose(jnp.concatenate(heads, axis=0) * HD**-0.5)


def backward_pieces(size, q_ref, g_ref, o_ref, lse_ref, own_ref):
    masks = head_masks(BF16)
    scale = BF16(HD**-0.5)
    qcode = query_code(own_ref[...])
    delta = delta_rows(g_ref[...], o_ref[...])
    for block in range(q_ref.shape[0] // size):
        at = slice(block * size, (block + 1) * size)
        for head, mask in enumerate(masks):
            qm = q_ref[at] * (mask * scale)
            gm = g_ref[at] * mask
            q = jnp.concatenate([qm, qcode[at]], axis=1)
            yield block, head, qm, gm, q, lse_ref[head : head + 1, at], delta[head : head + 1, at]


def self_backward_kernel(
    size, q_ref, k_ref, v_ref, ko_ref, vo_ref, g_ref, o_ref, lse_ref, own_ref, oth_ref,
    x_ref, xo_ref, wq_ref, wk_ref, wv_ref, dh1_ref, sa_ref, sb_ref, sc_ref, sd_ref, dmo_ref,
    dx_ref, dmi_ref, grad_ref,
    dq_acc, dx_acc, dxo_acc, dkv_acc, xt_ref, xot_ref, dxo_ref, came_ref, memory_ref, turn_ref, send_ref, recv_ref,
):
    step = pl.program_id(0)
    sp = lax.axis_index("sp")
    second = sp == 1
    rows, width = x_ref.shape
    pairs = width // PAIR
    pair = lax.rem(step, pairs)
    cols = pl.ds(pl.multiple_of(pair * PAIR, PAIR), PAIR)
    count = rows // size
    over = remote(dxo_ref, came_ref, send_ref.at[0], recv_ref.at[0], ("y",))

    def pieces():
        return backward_pieces(size, q_ref, g_ref, o_ref, lse_ref, own_ref)

    @pl.when(step == 0)
    def _():
        remote(dmo_ref, memory_ref, send_ref.at[1], recv_ref.at[1], ("y",)).start()
        xt_ref[...] = jnp.transpose(x_ref[...])
        turn_ref[...] = jnp.zeros(turn_ref.shape, F32)
        turn_ref[0:8] = sa_ref[...]
        turn_ref[8:16] = sb_ref[...]
        turn_ref[16:17] = sc_ref[...]

    @pl.when(jnp.logical_and(step == 0, second))
    def _():
        xot_ref[...] = jnp.transpose(xo_ref[...])

    @pl.when(jnp.logical_and(step == 0, jnp.logical_not(second)))
    def _():
        dq_acc[...] = jnp.zeros(dq_acc.shape, F32)

    @pl.when(jnp.logical_and(step < pairs, second))
    def _():
        keys = jnp.concatenate([ko_ref[...], oth_ref[...]], axis=1)
        values = vo_ref[...]
        turned = jnp.transpose(ko_ref[...])
        dk = dv = 0.0
        jobs = list(pieces())
        for n, p, ds in back_pieces([(keys, values, q, gm, lse, delta, False) for _, _, _, gm, q, lse, delta in jobs]):
            block, head, qm, gm = jobs[n][:4]
            dk = dk + nn(ds, qm)
            dv = dv + nn(p, gm)
            of_head = slice(head * HD, (head + 1) * HD)
            dq_acc[pair, of_head, block * size : (block + 1) * size] = nn(turned[of_head], ds)
        both = jnp.concatenate([dk.astype(BF16), dv.astype(BF16)], axis=1)
        dkv_acc[pair] = both
        dxo = nt(both, jnp.concatenate([wk_ref[...], wv_ref[...]], axis=1))

        @pl.when(step == 0)
        def _():
            dxo_acc[...] = dxo

        @pl.when(step > 0)
        def _():
            dxo_acc[...] += dxo

    @pl.when(jnp.logical_and(step == pairs - 1, second))
    def _():
        dxo_ref[...] = dxo_acc[...].astype(BF16)
        over.start()

    @pl.when(step >= pairs)
    def _():
        turned = jnp.transpose(k_ref[...])
        dq = [[0.0, 0.0] for _ in range(count)]
        dk, dv = [0.0] * count, [0.0] * count
        jobs, where = [], []
        keys = jnp.concatenate([k_ref[...], own_ref[...]], axis=1)
        for block, head, qm, gm, q, lse, delta in pieces():
            for part in range(block + 1):
                of = slice(part * size, (part + 1) * size)
                jobs.append((keys[of], v_ref[of], q, gm, lse, delta, part == block))
                where.append((block, part, head, qm, gm))
        for n, p, ds in back_pieces(jobs):
            block, part, head, qm, gm = where[n]
            of = slice(part * size, (part + 1) * size)
            dk[part] = dk[part] + nn(ds, qm)
            dv[part] = dv[part] + nn(p, gm)
            dq[block][head] = dq[block][head] + nn(turned[head * HD : (head + 1) * HD, of], ds)
        dk, dv = (jnp.concatenate(a, axis=0) for a in (dk, dv))
        before = dq_acc[pair]
        dq = jnp.concatenate(
            [
                upright(
                    [
                        part + before[head * HD : (head + 1) * HD, block * size : (block + 1) * size]
                        for head, part in enumerate(parts)
                    ]
                )
                for block, parts in enumerate(dq)
            ],
            axis=0,
        )
        dqk = jnp.concatenate([dq.astype(BF16), dk.astype(BF16)], axis=1)
        dv = dv.astype(BF16)
        grad_qk = nn(xt_ref[...], dqk)
        grad_v = nn(xt_ref[...], dv)
        shape = grad_ref.shape[:-1] + (PAIR,)
        lead = (slice(None),) * (len(shape) - 1)

        def put(n, grad):
            col = pair * 3 + n
            to = pl.ds(pl.multiple_of(col * PAIR, PAIR), PAIR)
            grad_ref[lead + (to,)] = grad.astype(BF16).reshape(shape)

        put(0, grad_qk[:, :PAIR])
        turn_ref[21:22, cols] = total(dqk[:, :PAIR])

        @pl.when(second)
        def _():
            grad_o = nn(xot_ref[...], dkv_acc[pair])
            put(1, grad_qk[:, PAIR:] + grad_o[:, :PAIR])
            put(2, grad_v + grad_o[:, PAIR:])
            turn_ref[22:23, cols] = total(dv) + total(dkv_acc[pair, :, PAIR:])

        @pl.when(jnp.logical_not(second))
        def _():
            put(1, grad_qk[:, PAIR:])
            put(2, grad_v)
            turn_ref[22:23, cols] = total(dv)

        dx = nt(dqk, jnp.concatenate([wq_ref[...], wk_ref[...]], axis=1)) + nt(dv, wv_ref[...])

        @pl.when(step == pairs)
        def _():
            dx_acc[...] = dh1_ref[...] + dx

        @pl.when(step > pairs)
        def _():
            dx_acc[...] += dx

    @pl.when(step == 2 * pairs - 1)
    def _():
        shape = grad_ref.shape[:-1] + (PAIR,)
        lead = (slice(None),) * (len(shape) - 1)
        columns = jnp.transpose(turn_ref[...])
        if sd_ref.shape == columns.shape:
            columns = columns + sd_ref[...]
        grad_ref[lead + (slice(3 * width, 3 * width + PAIR),)] = columns.astype(BF16).reshape(shape)


def self_backward_finale(*refs):
    dmo_ref, dx_ref, dmi_ref = refs[20:23]
    dx_acc, dxo_ref, came_ref, memory_ref, send_ref, recv_ref = (refs[i] for i in (25, 30, 31, 32, 34, 35))
    remote(dmo_ref, memory_ref, send_ref.at[1], recv_ref.at[1], ("y",)).wait()
    dmi_ref[...] = memory_ref[...]
    over = remote(dxo_ref, came_ref, send_ref.at[0], recv_ref.at[0], ("y",))

    @pl.when(lax.axis_index("sp") == 0)
    def _():
        over.wait_recv()
        dx_ref[...] = (dx_acc[...] + came_ref[...].astype(F32)).astype(BF16)

    @pl.when(lax.axis_index("sp") == 1)
    def _():
        over.wait_send()
        dx_ref[...] = dx_acc[...].astype(BF16)


GRADS = 23


def self_backward(block, qkv, kvo, g, o, lse, own, oth, x, xo, w, dh1, small, dmo, schedule):
    rows, width = x.shape
    pairs = width // PAIR

    def pair_of(offset):
        return pl.BlockSpec((rows, PAIR), lambda s: (0, lax.rem(s, pairs) + offset))

    def weight(offset):
        return pl.BlockSpec((width, PAIR), lambda s: (0, lax.rem(s, pairs) + offset))

    made = block + (3 * width + PAIR,)
    outs = [jax.ShapeDtypeStruct((rows, width), BF16)] * 2
    specs = [whole((rows, width))] * 2
    held = []
    if schedule:
        held += [pltpu.VMEM(made, BF16)]
    else:
        outs += [jax.ShapeDtypeStruct(made, BF16)]
        specs += [whole(made)]
    held += [
        pltpu.VMEM((pairs, PAIR, rows), F32),
        pltpu.VMEM((rows, width), F32),
        pltpu.VMEM((rows, width), F32),
        pltpu.VMEM((pairs, rows, 2 * PAIR), BF16),
        pltpu.VMEM((width, rows), BF16),
        pltpu.VMEM((width, rows), BF16),
        pltpu.VMEM((rows, width), BF16),
        pltpu.VMEM((rows, width), BF16),
        pltpu.VMEM((rows, width), BF16),
        pltpu.VMEM((PAIR, width), F32),
        pltpu.SemaphoreType.DMA((2,)),
        pltpu.SemaphoreType.DMA((2,)),
    ]
    return run(
        functools.partial(self_backward_kernel, 256), "self_backward", 2 * pairs,
        (qkv, qkv, qkv, kvo, kvo, g, o, lse, own, oth, x, xo, w, w, w, dh1) + tuple(small) + (dmo,),
        [
            pair_of(0),
            pair_of(pairs),
            pair_of(2 * pairs),
            pair_of(0),
            pair_of(pairs),
            pair_of(0),
            pair_of(0),
            pl.BlockSpec((8, rows), lambda s: (lax.rem(s, pairs), 0)),
            whole((rows, 128)),
            whole((rows, 128)),
            whole((rows, width)),
            whole((rows, width)),
            weight(0),
            weight(pairs),
            weight(2 * pairs),
            whole((rows, width)),
        ] + [whole(a.shape) for a in small] + [pl.BlockSpec(memory_space=pl.ANY)],
        outs, specs, held, schedule, 5,
        48 * rows * rows * width + 20 * rows * width * width, 12 * width * width + 40 * rows * width,
        (("y",),), self_backward_finale,
    )


def code_of(docs_ref):
    row = lax.broadcasted_iota(jnp.int32, (PAIR, docs_ref.shape[1]), 0)
    return jnp.transpose(jnp.where(docs_ref[...] == row, 1.0, 0.0)).astype(BF16)


def line(ref):
    return ref[...].astype(F32)[None, :]


def front_kernel(
    size, x_hbm, m_hbm, td_ref, md_ref, wx_hbm, wm_hbm, wo_hbm, wq_hbm,
    bq_ref, bv_ref, bcv_ref, bso_ref, g_ref, s_ref, bcq_ref,
    qkv_out, mkv_out, kvo_out, mkvo_out, cq_out, ctx_out, cc_out, h_out, xo_out, mo_out,
    lse_ref, clse_ref, tt_ref, mt_ref, to_ref, mo_ref,
    x_ref, m_ref, wx_ref, wm_ref, wo_ref, wq_ref, xc_ref, mc_ref, tdc_ref, mdc_ref,
    qkv_ref, mkv_ref, kvo_ref, mkvo_ref, cq_ref, ctx_ref, cc_ref, h_ref, acc_ref,
    load_ref, store_ref, send_ref, recv_ref,
):
    rows, width = x_ref.shape
    pairs = width // PAIR
    second = lax.axis_index("sp") == 1
    first = jnp.logical_not(second)
    masks = head_masks(BF16)
    scale = BF16(HD**-0.5)
    loads = [
        pltpu.make_async_copy(src, dst, load_ref.at[i])
        for i, (src, dst) in enumerate(
            ((x_hbm, x_ref), (wx_hbm, wx_ref), (m_hbm, m_ref), (wm_hbm, wm_ref), (wo_hbm, wo_ref), (wq_hbm, wq_ref))
        )
    ]
    give = [
        pltpu.make_async_copy(src, dst, store_ref.at[i])
        for i, (src, dst) in enumerate(
            (
                (qkv_ref, qkv_out), (mkv_ref, mkv_out), (mkvo_ref, mkvo_out), (cq_ref, cq_out), (ctx_ref, ctx_out),
                (cc_ref, cc_out), (h_ref, h_out), (mc_ref, mo_out), (kvo_ref, kvo_out), (xc_ref, xo_out),
            )
        )
    ]
    x_over = remote(x_hbm, xc_ref, send_ref.at[0], recv_ref.at[0], ("y",))
    m_over = remote(m_hbm, mc_ref, send_ref.at[1], recv_ref.at[1], ("y",))
    docs = [
        remote(td_ref, tdc_ref, send_ref.at[2], recv_ref.at[2], ("y",)),
        remote(md_ref, mdc_ref, send_ref.at[3], recv_ref.at[3], ("y",)),
    ]
    for copy in loads:
        copy.start()
    greet([("y",)])
    for copy in docs:
        copy.start()
    pl.when(first)(x_over.start)
    pl.when(second)(m_over.start)

    def columns(offset, pair):
        return pl.ds(pl.multiple_of(offset + pair * PAIR, PAIR), PAIR)

    def heads(source, offset, pair, code, block):
        at = slice(block * size, (block + 1) * size)
        q = source[at, columns(offset, pair)]
        return [jnp.concatenate([q * (mask * scale), code[at]], axis=1) for mask in masks]

    def keep(block, pair, outs, lses, lse_out, out):
        at = slice(block * size, (block + 1) * size)
        mixed = jnp.concatenate(outs, axis=0)
        acc_ref[pair, :, at] = mixed
        out[at, columns(0, pair)] = jnp.transpose(mixed).astype(BF16)
        row = lax.broadcasted_iota(jnp.int32, (8, size), 0)
        lse_out[pl.ds(pl.multiple_of(pair * 8, 8), 8), at] = jnp.where(row == 0, lses[0], lses[1])

    def begin(block, pair, results, lse_out, out):
        keep(block, pair, [r for r, _ in results], [lse for _, lse in results], lse_out, out)

    def merge(block, pair, results, lse_out, out):
        at = slice(block * size, (block + 1) * size)
        stats = lse_out[pl.ds(pl.multiple_of(pair * 8, 8), 8), at]
        outs, lses = [], []
        for head, (r, lse) in enumerate(results):
            before = acc_ref[pair, head * HD : (head + 1) * HD, at]
            old = stats[head : head + 1]
            peak = jnp.maximum(old, lse)
            both = peak + jnp.log(jnp.exp(old - peak) + jnp.exp(lse - peak))
            outs.append(before * jnp.exp(old - both) + r * jnp.exp(lse - both))
            lses.append(both)
        keep(block, pair, outs, lses, lse_out, out)

    def halves(values):
        turned = jnp.transpose(values)
        return turned[:HD], turned[HD:]

    to_ref[...] = code_of(td_ref)
    mo_ref[...] = code_of(md_ref)
    loads[0].wait()
    loads[1].wait()
    for n, bias in enumerate((line(bq_ref), 0.0, line(bv_ref))):
        cols = slice(n * width, (n + 1) * width)
        qkv_ref[:, cols] = (nn(x_ref[...], wx_ref[:, cols]) + bias).astype(BF16)
    give[0].start()
    loads[2].wait()
    loads[3].wait()
    for n, bias in enumerate((0.0, line(bcv_ref))):
        cols = slice(n * width, (n + 1) * width)
        mkv_ref[:, cols] = (nn(m_ref[...], wm_ref[:, cols]) + bias).astype(BF16)
    give[1].start()

    def attend(query, keys_ref, key_at, value_at, key_code, diagonal, finish, stats, out):
        @pl.loop(0, pairs // 2)
        def _(half):
            code = query_code(to_ref[...])
            jobs, where = [], []
            for pair in (2 * half, 2 * half + 1):
                keys = jnp.concatenate([keys_ref[:, columns(key_at, pair)], key_code[...]], axis=1)
                values = halves(keys_ref[:, columns(value_at, pair)])
                for block in range(rows // size):
                    end = (block + 1) * size if diagonal else rows
                    for q, v in zip(heads(query, 0, pair, code, block), values):
                        jobs.append((keys[:end], v[:, :end], q, size if diagonal else 0))
                    where.append((block, pair))
            results = softmax_over(jobs)
            for n, (block, pair) in enumerate(where):
                finish(block, pair, results[2 * n : 2 * n + 2], stats, out)

    attend(qkv_ref, qkv_ref, width, 2 * width, to_ref, True, begin, lse_ref, ctx_ref)

    for copy in docs:
        copy.wait()
    tt_ref[...] = code_of(tdc_ref)
    mt_ref[...] = code_of(mdc_ref)

    @pl.when(first)
    def _():
        x_over.wait_send()
        m_over.start()

    @pl.when(second)
    def _():
        x_over.wait_recv()
        give[9].start()
        for n, bias in enumerate((0.0, line(bv_ref))):
            cols = slice(n * width, (n + 1) * width)
            from_cols = slice((n + 1) * width, (n + 2) * width)
            kvo_ref[:, cols] = (nn(xc_ref[...], wx_ref[:, from_cols]) + bias).astype(BF16)
        give[8].start()

        attend(qkv_ref, kvo_ref, 0, width, tt_ref, False, merge, lse_ref, ctx_ref)

    give[4].start()
    loads[4].wait()
    loads[5].wait()
    h = x_ref[...].astype(F32) + nn(ctx_ref[...], wo_ref[...]) + line(bso_ref)
    h_ref[...] = h
    n, _ = normed(h)
    a = (n * line(g_ref) + line(s_ref)).astype(BF16)
    cq_ref[...] = (nn(a, wq_ref[...]) + line(bcq_ref)).astype(BF16)
    give[6].start()
    give[3].start()

    attend(cq_ref, mkv_ref, 0, width, mo_ref, False, begin, clse_ref, cc_ref)
    m_over.wait()
    give[7].start()
    for n, bias in enumerate((0.0, line(bcv_ref))):
        cols = slice(n * width, (n + 1) * width)
        mkvo_ref[:, cols] = (nn(mc_ref[...], wm_ref[:, cols]) + bias).astype(BF16)
    give[2].start()
    attend(cq_ref, mkvo_ref, 0, width, mt_ref, False, merge, clse_ref, cc_ref)
    give[5].start()
    for copy in give[:8]:
        copy.wait()

    @pl.when(second)
    def _():
        give[8].wait()
        give[9].wait()


def front(x, mem, td, md, wx, wm, wo, wq, vectors):
    rows, width = x.shape
    pairs = width // PAIR

    def flat(n):
        return jax.ShapeDtypeStruct((rows, n * width), BF16)

    stats = jax.ShapeDtypeStruct((8 * pairs, rows), F32)
    code = jax.ShapeDtypeStruct((rows, PAIR), BF16)
    far = pl.BlockSpec(memory_space=pl.ANY)
    near = pl.BlockSpec(memory_space=pltpu.VMEM)
    tall = jax.ShapeDtypeStruct((rows, width), F32)
    held = [flat(3), flat(2), flat(2), flat(2), flat(1), flat(1), flat(1), tall]
    return pl.pallas_call(
        functools.partial(front_kernel, 256),
        in_specs=[far, far, near, near, far, far, far, far] + [near] * len(vectors),
        out_specs=[far] * 10 + [near] * 6,
        out_shape=[flat(3), flat(2), flat(2), flat(2), flat(1), flat(1), flat(1), tall, flat(1), flat(1)]
        + [stats, stats, code, code, code, code],
        scratch_shapes=[pltpu.VMEM(a.shape, a.dtype) for a in (flat(1), flat(1))]
        + [pltpu.VMEM(w.shape, BF16) for w in (wx, wm, wo, wq)]
        + [pltpu.VMEM((rows, width), BF16)] * 2
        + [pltpu.VMEM((1, rows), jnp.int32)] * 2
        + [pltpu.VMEM(a.shape, a.dtype) for a in held]
        + [
            pltpu.VMEM((pairs, PAIR, rows), F32),
            pltpu.SemaphoreType.DMA((6,)),
            pltpu.SemaphoreType.DMA((10,)),
            pltpu.SemaphoreType.DMA((4,)),
            pltpu.SemaphoreType.DMA((4,)),
        ],
        compiler_params=params(1),
        cost_estimate=cost(22 * rows * width * width + 36 * rows * rows * width, 60 * rows * width),
        name="front",
    )(x, mem, td, md, wx, wm, wo, wq, *vectors)


def feed_kernel(
    count, comm, h1_ref, cc_ref, ct_ref, wco_ref, wi_ref, wo_ref,
    g1_ref, s1_ref, bco_ref, g2_ref, s2_ref, bfo_ref, g3_ref, s3_ref, bfi_ref, out_ref, dh2_ref, dcc_ref, gco_ref, *refs,
):
    if comm:
        gwi_ref, refs = refs[0], refs[1:]
    else:
        gwi_ref, gwo_ref, refs = refs[0], refs[1], refs[2:]
    small_ref, gib_ref, hid_ref, slope_ref, n2_ref, r2_ref, a2b_ref, acc_ref, df_ref, bias_ref, *refs = refs
    step = pl.program_id(0)
    width = acc_ref.shape[1]

    if comm:
        mi_ref, mo_ref, ci_ref, co_ref, send_ref, recv_ref = refs
        wide = ci_ref.shape[-1]
        here = place()
        c = here[1]

        def chunk_copies(j):
            at = pl.ds(pl.multiple_of(j * width, width), width)
            return [
                remote(mi_ref.at[:, :, at], ci_ref.at[:, :, at], send_ref.at[0, j], recv_ref.at[0, j], ("core",), here),
                remote(mo_ref.at[j], co_ref.at[j], send_ref.at[1, j], recv_ref.at[1, j], ("core",), here),
            ]

    @pl.when(step == 0)
    def _():
        if comm:
            greet([("core",)])
        wide = bfi_ref[...].astype(F32)
        for i in range(count):
            bias_ref[i : i + 1] = wide[None, i * width : (i + 1) * width]
        n1, _ = normed(h1_ref[...])
        a1 = n1 * line(g1_ref) + line(s1_ref)
        h2 = a1 + nn(cc_ref[...], wco_ref[...]) + line(bco_ref)
        n2, r2 = normed(h2)
        n2_ref[...] = n2
        r2_ref[...] = jnp.broadcast_to(r2, r2_ref.shape)
        a2 = n2 * line(g2_ref) + line(s2_ref)
        a2b_ref[...] = a2.astype(BF16)
        acc_ref[...] = a2 + line(bfo_ref)

    piece = 2 * PAIR
    pieces = [slice(i, i + piece) for i in range(0, width, piece)]

    @pl.when(step < count)
    def _():
        def product(at):
            return nn(a2b_ref[...], wi_ref[:, at])

        bias = bias_ref[pl.ds(step, 1)]
        ready = product(pieces[0])
        more = 0.0
        for i, at in enumerate(pieces):
            u = ready + bias[:, at]
            if i + 1 < len(pieces):
                ready = product(pieces[i + 1])
            cumul = 0.5 * (1.0 + lax.erf(u * 0.7071067811865476))
            density = jnp.exp(-0.5 * u * u) * 0.3989422804014327
            hid = (u * cumul).astype(BF16)
            hid_ref[step, :, at] = hid
            slope_ref[step, :, at] = cumul + u * density
            more = more + nn(hid, wo_ref[at])
        acc_ref[...] += more

    @pl.when(step == count - 1)
    def _():
        n3, r3 = normed(acc_ref[...])
        gain = line(g3_ref)
        out_ref[...] = (n3 * gain + line(s3_ref)).astype(BF16)
        e = ct_ref[...].astype(F32)
        d3 = norm_back(e, n3, r3, gain)
        df = d3.astype(BF16)
        df_ref[...] = df
        acc_ref[...] = d3
        small_ref[0:1] = total(e * n3)
        small_ref[1:2] = total(e)
        small_ref[2:3] = total(df)

    @pl.when(jnp.logical_and(step >= count, step < 2 * count))
    def _():
        j = step - count
        df = df_ref[...]

        def product(at):
            return nt(df, wo_ref[at])

        ready = product(pieces[0])
        more, go, gi, sums = 0.0, [], [], []
        for i, at in enumerate(pieces):
            du = (ready * slope_ref[j, :, at]).astype(BF16)
            if i + 1 < len(pieces):
                ready = product(pieces[i + 1])
            go.append(tn(hid_ref[j, :, at], df).astype(BF16))
            more = more + nt(du, wi_ref[:, at])
            gi.append(tn(a2b_ref[...], du).astype(BF16))
            sums.append(tn(du, jnp.ones((du.shape[0], PAIR), BF16)))
        acc_ref[...] += more
        go, gi, sums = (jnp.concatenate(a, axis=n) for a, n in ((go, 0), (gi, 1), (sums, 0)))
        quarter = width // gib_ref.shape[0]
        if gib_ref.shape[0] == 4:
            lane = lax.broadcasted_iota(jnp.int32, (quarter // 4, PAIR), 1)
            for i in range(4):
                part = sum(
                    jnp.where(lane == 17 + n, sums[(4 * i + n) * quarter // 4 : (4 * i + n + 1) * quarter // 4], 0.0)
                    for n in range(4)
                )
                gib_ref[i] = part
        else:
            gib_ref[0] = jnp.transpose(sums)[:1]
        if comm:
            at = pl.ds(pl.multiple_of(j * width, width), width)
            eight, narrow = gwi_ref.shape[:2]
            gi = gi.reshape(eight, 2, narrow, width)
            go = go.reshape(2, 2, 4, narrow, width)
            gwi_ref[:, :, at] = jnp.where(c == 0, gi[:, 0], gi[:, 1])
            mi_ref[:, :, at] = jnp.where(c == 0, gi[:, 1], gi[:, 0])
            mo_ref[j] = jnp.where(c == 0, go[:, 1], go[:, 0])
            for i in range(4):
                gwi_ref[pl.ds(2 * j, 2), :, pl.ds(wide + i * width, width)] = jnp.where(c == 0, go[:, 0, i], go[:, 1, i])
            for copy in chunk_copies(j):
                copy.start()
        else:
            gwo_ref[...] = go
            gwi_ref[...] = gi

    @pl.when(step == 2 * count)
    def _():
        d2 = acc_ref[...]
        n2 = n2_ref[...]
        dh2 = norm_back(d2, n2, r2_ref[:, :1], line(g2_ref))
        dh2_ref[...] = dh2
        dco = dh2.astype(BF16)
        dcc_ref[...] = nt(dco, wco_ref[...]).astype(BF16)
        gco_ref[...] = tn(cc_ref[...], dco).astype(BF16)
        small_ref[3:4] = total(d2 * n2)
        small_ref[4:5] = total(d2)
        small_ref[5:6] = total(dco)
        small_ref[6:8] = jnp.zeros((2, d2.shape[1]), F32)

    if comm:

        @pl.when(step > count)
        def _():
            j = step - count - 1
            at = pl.ds(pl.multiple_of(j * width, width), width)
            for copy in chunk_copies(j):
                copy.wait()
            gwi_ref[:, :, at] += ci_ref[:, :, at]
            for i in range(4):
                gwi_ref[pl.ds(2 * j, 2), :, pl.ds(wide + i * width, width)] += co_ref[j, :, i]


def feed(size, comm, h1, cc, ct, wco, wi, wo, vectors):
    rows, width = h1.shape
    wide = wi.shape[1]
    chunk = width
    count = wide // chunk

    def weight(s):
        return jnp.where(s < count, s, jnp.minimum(s - count, count - 1))

    def early(s):
        return jnp.clip(s - count, 0, count - 1)

    flat = whole((rows, width))
    square = whole((width, width))
    scratch = [
        pltpu.VMEM((count, rows, chunk), BF16),
        pltpu.VMEM((count, rows, chunk), F32),
        pltpu.VMEM((rows, width), F32),
        pltpu.VMEM((rows, 128), F32),
        pltpu.VMEM((rows, width), BF16),
        pltpu.VMEM((rows, width), F32),
        pltpu.VMEM((rows, width), BF16),
        pltpu.VMEM((8, width), F32),
    ]
    if comm:
        narrow = width // size
        gib_shape = jax.ShapeDtypeStruct((size, narrow, PAIR), F32)
        gib_spec = pl.BlockSpec((4, narrow, PAIR), lambda s: (early(s), 0, 0))
        grad_specs = [whole((size // 2, narrow, 2 * wide))]
        grad_shapes = [(size // 2, narrow, 2 * wide)]
        scratch += [
            pltpu.VMEM((size // 2, narrow, wide), BF16),
            pltpu.VMEM((count, 2, 4, narrow, width), BF16),
            pltpu.VMEM((size // 2, narrow, wide), BF16),
            pltpu.VMEM((count, 2, 4, narrow, width), BF16),
            pltpu.SemaphoreType.DMA((2, count)),
            pltpu.SemaphoreType.DMA((2, count)),
        ]
    else:
        gib_shape = jax.ShapeDtypeStruct((count, 1, width), F32)
        gib_spec = pl.BlockSpec((1, 1, chunk), lambda s: (early(s), 0, 0))
        grad_specs = [
            pl.BlockSpec((width, chunk), lambda s: (0, early(s))),
            pl.BlockSpec((chunk, width), lambda s: (early(s), 0)),
        ]
        grad_shapes = [(width, wide), (wide, width)]
    return pl.pallas_call(
        functools.partial(feed_kernel, count, comm),
        grid=(2 * count + 1,),
        in_specs=[
            flat, flat, flat, square,
            pl.BlockSpec((width, chunk), lambda s: (0, weight(s))),
            pl.BlockSpec((chunk, width), lambda s: (weight(s), 0)),
        ]
        + [whole(v.shape) for v in vectors],
        out_specs=[flat, flat, flat, square]
        + grad_specs
        + [whole((8, width)), gib_spec],
        out_shape=[
            jax.ShapeDtypeStruct((rows, width), BF16),
            jax.ShapeDtypeStruct((rows, width), F32),
            jax.ShapeDtypeStruct((rows, width), BF16),
            jax.ShapeDtypeStruct((width, width), BF16),
        ]
        + [jax.ShapeDtypeStruct(a, BF16) for a in grad_shapes]
        + [
            jax.ShapeDtypeStruct((8, width), F32),
            gib_shape,
        ],
        scratch_shapes=scratch,
        compiler_params=params(2 if comm else None),
        cost_estimate=cost(
            12 * rows * width * wide + 6 * rows * width * width, 12 * width * wide + 16 * rows * width
        ),
        name="feed",
    )(h1, cc, ct, wco, wi, wo, *vectors)


def outputs_kernel(moves, count, line, *refs):
    pieces, rest = refs[:count], refs[count:]
    out_ref, dx_ref, dm_ref, dmi_ref = rest[:4]
    outs = rest[4:]
    for piece, first, wide, which, row, col in moves:
        ref = pieces[piece]
        outs[which][row : row + ref.shape[0], col : col + wide] = ref[:, first : first + wide].astype(F32)
    turned, result, dx, dm = outs[-4:]
    turned[...] = jnp.transpose(pieces[line[0]][:, line[1] : line[1] + PAIR].astype(F32))
    result[...] = out_ref[...]
    dx[...] = dx_ref[...]
    dm[...] = (dm_ref[...] + dmi_ref[...].astype(F32)).astype(BF16)


def outputs(pieces, moves, line, shapes, out, dx, dm, dmi):
    ins = tuple(pieces) + (out, dx, dm, dmi)
    result = jax.ShapeDtypeStruct(out.shape, BF16)
    return pl.pallas_call(
        functools.partial(outputs_kernel, moves, len(pieces), line),
        out_shape=[jax.ShapeDtypeStruct(a, F32) for a in shapes]
        + [jax.ShapeDtypeStruct((PAIR, pieces[0].shape[0]), F32), result, result, result],
        compiler_params=params(),
        cost_estimate=cost(0, 12 << 20),
        name="outputs",
    )(*ins)


def moved(pieces, targets):
    out = []
    for n, (start, wide) in enumerate(pieces):
        for first, cols, which, row, col in targets:
            low, high = max(start, first), min(start + wide, first + cols)
            if low < high:
                out.append((n, low - start, high - low, which, row, col + low - first))
    return out


def schedule_of(flows, kernel):
    entries = [
        (start, order, name, start, stop)
        for order, name in enumerate(flows)
        for start, stop in PLAN[name][kernel]
    ]
    return tuple(([flows[name]], start, stop) for _, _, name, start, stop in sorted(entries))


def swap_sum(part, axis, pairs):
    came = lax.ppermute(part, axis, pairs)
    return part.astype(F32) + came.astype(F32)


def sum_scatter(grad, size, order):
    rows, cols = grad.shape
    bits = size.bit_length() - 1
    me = lax.axis_index("dp")
    now = grad.reshape((2,) * bits + (rows // size, cols))
    left = list(range(bits))[::-1]
    for bit in [b for b in order if b < bits] + [b for b in range(bits) if b not in order]:
        axis = left.index(bit)
        mine = (me >> bit) & 1
        keep = lax.dynamic_index_in_dim(now, mine, axis, keepdims=False)
        send = lax.dynamic_index_in_dim(now, 1 - mine, axis, keepdims=False)
        came = lax.ppermute(send, "dp", [(i, i ^ (1 << bit)) for i in range(size)])
        now = (keep.astype(F32) + came.astype(F32)).astype(BF16)
        left.pop(axis)
    return swap_sum(now, "sp", [(0, 1), (1, 0)])


def per_device(
    size,
    inputs,
    memory,
    target_docs,
    memory_docs,
    cotangent,
    w_qkv,
    b_q,
    b_v,
    w_so,
    b_so,
    g_one,
    s_one,
    w_cq,
    b_cq,
    w_ckv,
    b_cv,
    w_co,
    b_co,
    g_two,
    s_two,
    w_fi,
    b_fi,
    w_fo,
    b_fo,
    g_three,
    s_three,
):
    rows, width = inputs.shape[1:]
    wide = b_fi.shape[0]
    comm = size == 16
    narrow, broad = width // size, wide // size
    x, mem, ct = inputs[0], memory[0], cotangent[0]
    qkv, mkv, kvo, mkvo, cq, ctx, cc, h1, x_o, mem_o, lse, clse, t_oth, m_oth, t_own, m_own = front(
        x, mem, target_docs, memory_docs, w_qkv, w_ckv, w_so, w_cq, (b_q, b_v, b_cv, b_so, g_one, s_one, b_cq)
    )
    output, dh2, dcc, gco, gwi, *gwo, small_a, gib = feed(
        size, comm, h1, cc, ct, w_co, w_fi, w_fo,
        (g_one, s_one, b_co, g_two, s_two, b_fo, g_three, s_three, b_fi),
    )
    gib = gib.reshape(width, PAIR) if comm else gib.reshape(1, wide)

    block = (2, 2, 2, 2, narrow) if comm else (width,)
    at_cross, at_self, flows = (), (), {}
    if comm:
        late_shape = block + (2 * width,)
        sources = {
            "T0": (gwi.reshape(block[:3] + gwi.shape[1:]), block[:3] + gwi.shape[1:], BLOCK[:3]),
            "T1a": (("ref", MIDDLE), block + (3 * width,), BLOCK),
            "T1b": (None, late_shape, BLOCK),
            "G": (("ref", GRADS), block + (3 * width + PAIR,), BLOCK),
        }
        for name, (source, cols, hops, _, _) in PLAN.items():
            array, shape, dims = sources[source]
            flows[name] = Flow(array, shape, hops, dims, cols)
        at_cross = schedule_of(flows, 3)
        at_self = schedule_of(flows, 4)
    dm, dmo, gcvb, dh1, dsc, late, small_b, *early = cross_backward(
        block, cq, mkv, mkvo, dcc, cc, clse, t_own, m_own, m_oth, mem, mem_o, w_ckv,
        gco, dh2, h1, ctx, w_cq, w_so, g_one, s_one, at_cross,
    )
    for name, flow in flows.items():
        if PLAN[name][0] == "T1b":
            flow.array = late
    dx, dm_in, *made = self_backward(
        block, qkv, kvo, dsc, ctx, lse, t_own, t_oth, x, x_o, w_qkv, dh1, (small_a, small_b, gcvb, gib), dmo, at_self
    )
    if comm:
        targets = {
            "T0": [(0, wide, 2, 0, 0)] + [(wide + i * width, width, 3, i * narrow, 0) for i in range(4)],
            "T1a": [(0, width, 4, 0, 0), (width, 2 * width, 1, 0, 0)],
            "T1b": [(0, width, 5, 0, 0), (width, width, 6, 0, 0)],
            "G": [
                ((3 * pair + i) * PAIR, PAIR, 0, 0, i * width + pair * PAIR)
                for pair in range(width // PAIR)
                for i in range(3)
            ],
        }
        moves, line = [], None
        for n, (source, cols, *_) in enumerate(PLAN.values()):
            moves += [(n,) + m[1:] for m in moved([cols], targets[source])]
            if source == "G" and cols[0] <= 3 * width < sum(cols):
                line = n, 3 * width - cols[0]
        shapes = [(narrow, 3 * width), (narrow, 2 * width), (narrow, wide), (broad, width)] + [(narrow, width)] * 3
        t_qkv, t_cmem, t_fin, t_fout, t_cout, t_cquery, t_out, lines, output, derivative, grad_memory = outputs(
            [f.array for f in flows.values()], moves, line, shapes, output, dx, dm, dm_in
        )
    else:
        (early,), (made,) = early, made
        columns = made[:, 3 * width : 3 * width + PAIR]
        gqkv = made[:, : 3 * width].reshape(width, -1, 3, PAIR).swapaxes(1, 2).reshape(width, 3 * width)
        t_fin, t_fout, t_cout, t_cquery, t_out, t_cmem, t_qkv, lines = (
            sum_scatter(g, size, (0, 1, 2, 3))
            for g in (
                gwi, gwo[0], early[:, :width], late[:, :width], late[:, width:], early[:, width:], gqkv, columns
            )
        )
        lines, derivative = lines.T, dx
        grad_memory = (dm + dm_in.astype(F32)).astype(BF16)
    t_gthree, t_sthree, t_fobias, t_gtwo, t_stwo, t_cobias = (lines[i] for i in range(6))
    t_cqbias, t_gone, t_sone, t_obias = (lines[i] for i in range(8, 12))
    t_cvbias, t_qbias, t_vbias = lines[16], lines[21], lines[22]
    if comm:
        t_fibias = lines[17:21].reshape(-1)
    else:
        t_fibias = lax.psum(lax.psum_scatter(gib[0], "dp", scatter_dimension=0, tiled=True), "sp")
    return (
        output[None],
        derivative[None],
        grad_memory[None],
        t_qkv,
        t_qbias,
        t_vbias,
        t_out,
        t_obias,
        t_gone,
        t_sone,
        t_cquery,
        t_cqbias,
        t_cmem,
        t_cvbias,
        t_cout,
        t_cobias,
        t_gtwo,
        t_stwo,
        t_fin,
        t_fibias,
        t_fout,
        t_fobias,
        t_gthree,
        t_sthree,
    )


def solution(mesh):
    split = P("dp", "sp", None)
    in_specs = (split, split, P("dp", "sp"), P("dp", "sp"), split) + (P(),) * 21
    matrix, vector = P("dp", None), P("dp")
    out_specs = (
        split, split, split,
        matrix, vector, vector,
        matrix, vector, vector, vector,
        matrix, vector,
        matrix, vector,
        matrix, vector, vector, vector,
        matrix, vector,
        matrix, vector, vector, vector,
    )
    return jax.shard_map(
        functools.partial(per_device, mesh.shape["dp"]),
        mesh=mesh, in_specs=in_specs, out_specs=out_specs, check_vma=False,
    )
```

```python
import functools

import jax
import jax.numpy as jnp
from jax import lax
from jax.experimental import pallas as pl
from jax.experimental.pallas import tpu as pltpu
from jax.sharding import PartitionSpec as P

HD = 64
PAIR = 2 * HD
EPS = 1e-05
FAR = 1.0e9
VMEM = 60 * 1024 * 1024
F32 = jnp.float32
BF16 = jnp.bfloat16


def nn(a, b):
    return lax.dot_general(a, b, (((1,), (0,)), ((), ())), preferred_element_type=F32)


def nt(a, b):
    return lax.dot_general(a, b, (((1,), (1,)), ((), ())), preferred_element_type=F32)


def tn(a, b):
    return lax.dot_general(a, b, (((0,), (0,)), ((), ())), preferred_element_type=F32)


def params(collective=None):
    if collective is None:
        return pltpu.CompilerParams(vmem_limit_bytes=VMEM)
    return pltpu.CompilerParams(
        vmem_limit_bytes=VMEM, collective_id=collective, has_side_effects=True
    )


def cost(flops, moved):
    return pl.CostEstimate(flops=int(flops), bytes_accessed=int(moved), transcendentals=0)


def normed(h):
    centred = h - jnp.mean(h, axis=-1, keepdims=True)
    rstd = lax.rsqrt(jnp.mean(centred * centred, axis=-1, keepdims=True) + EPS)
    return centred * rstd, rstd


def norm_back(grad, n, rstd, gain):
    scaled = grad * gain
    centre = jnp.mean(scaled, axis=-1, keepdims=True)
    along = jnp.mean(scaled * n, axis=-1, keepdims=True)
    return rstd * (scaled - centre - n * along)


def total(a):
    return jnp.sum(a.astype(F32), axis=0, keepdims=True)


def place():
    me = lax.axis_index("dp")
    return me, me % 2, (me // 2) % 2, me // 4, lax.axis_index("sp")


def flipped(at, hops):
    me, c, x, z, sp = at
    for hop in hops:
        if hop == "core":
            me, c = me + 1 - 2 * c, 1 - c
        elif hop == "x":
            me, x = me + 2 - 4 * x, 1 - x
        elif hop == "z1":
            me, z = me + 4 - 8 * (z % 2), z + 1 - 2 * (z % 2)
        elif hop == "z2":
            me, z = me + 8 - 16 * (z // 2), z + 2 - 4 * (z // 2)
        else:
            sp = 1 - sp
    return me, c, x, z, sp


def partner(hops, at=None):
    there = flipped(at or place(), hops)
    return {"dp": there[0], "sp": there[4]}


def greet(groups, at=None):
    groups = sorted({tuple("y" if h[0] == "y" else h for h in hops) for hops in groups})
    barrier = pltpu.get_barrier_semaphore()
    for hops in groups:
        pl.semaphore_signal(barrier, inc=1, device_id=partner(hops, at), device_id_type=pl.DeviceIdType.MESH)
    pl.semaphore_wait(barrier, len(groups))


def remote(src, dst, send, recv, hops, at=None):
    return pltpu.make_async_remote_copy(
        src_ref=src, dst_ref=dst, send_sem=send, recv_sem=recv,
        device_id=partner(hops, at), device_id_type=pl.DeviceIdType.MESH,
    )


PLAN = {
    "T0_0": ("T0", (0, 1536), ("yr", "x", "z1", "z2", "yg"), ((0, 3), (3, 6), (6, 7)), ((0, 2), (2, 4))),
    "T0_1": ("T0", (1536, 1536), ("z1", "x", "yr", "z2", "yg"), ((0, 5), (5, 7)), ((0, 2), (2, 4), (4, 6))),
    "T0_2": ("T0", (3072, 1024), ("z1", "yr", "x", "z2", "yg"), ((0, 4), (4, 6), (6, 7)), ((0, 2), (2, 4))),
    "T0_3": ("T0", (4096, 2048), ("x", "yr", "z1", "z2", "yg"), ((0, 5), (5, 7)), ((0, 4), (4, 6), (6, 8))),
    "T1a_0": ("T1a", (0, 1536), ("core", "x", "z1", "z2", "y"), ((6, 7),), ((0, 5), (5, 9), (9, 20), (20, 35))),
    "T1a_1": ("T1a", (1536, 768), ("core", "z1", "x", "z2", "y"), ((6, 7),), ((0, 5), (5, 7), (7, 9), (9, 16))),
    "T1b_0": ("T1b", (0, 768), ("core", "z1", "x", "yr", "z2", "yg"), (), ((0, 2), (2, 7), (7, 9), (9, 16), (16, 23), (23, 30))),
    "T1b_1": ("T1b", (768, 768), ("core", "x", "z1", "z2", "y"), (), ((0, 2), (2, 5), (5, 8), (8, 10), (10, 18))),
    "G1_0": ("G", (0, 768), ("core", "x", "z1", "z2", "y"), (), ((5, 6), (6, 9), (9, 20), (20, 28), (28, 38))),
    "G2_0": ("G", (768, 512), ("core", "x", "yr", "z1", "z2", "yg"), (), ((7, 8), (8, 13), (13, 22), (22, 29), (29, 34), (34, 40))),
    "G2_1": ("G", (1280, 256), ("core", "z1", "x", "z2", "y"), (), ((7, 8), (8, 11), (11, 14), (14, 19), (19, 24))),
    "G3_0": ("G", (1536, 384), ("core", "x", "z1", "z2", "y"), (), ((8, 9), (9, 15), (15, 25), (25, 32), (32, 39))),
    "G4_0": ("G", (1920, 256), ("core", "z1", "x", "yr", "z2", "yg"), (), ((9, 12), (12, 21), (21, 26), (26, 31), (31, 36), (36, 41))),
    "G4_1": ("G", (2176, 256), ("core", "x", "yr", "z1", "z2", "yg"), (), ((9, 12), (12, 17), (17, 27), (27, 33), (33, 37), (37, 42))),
}
BLOCK = ("z2", "z1", "x", "core")


class Part:
    def __init__(self, hop, shape, dims, cols=None):
        self.hops = hops = hop if isinstance(hop, tuple) else (hop,)
        self.groups = [(h,) for h in hops] + ([hops] if len(hops) > 1 else [])
        self.dims = dims
        self.cols = cols or (0, shape[-1])
        self.shape = shape = tuple(shape[:-1]) + (self.cols[1],)
        for h in hops:
            if h in dims:
                at = dims.index(h)
                shape, dims = shape[:at] + shape[at + 1 :], dims[:at] + dims[at + 1 :]
            elif h != "y":
                shape = shape[:-1] + (shape[-1] // 2 if h == "yr" else 2 * shape[-1],)
        self.after, self.left = shape, dims
        self.came = self.shape if hops == ("yg",) else shape

    def share(self, at):
        _, c, x, z, sp = at
        first, wide = self.cols
        index = [slice(None)] * (len(self.shape) - 1) + [pl.ds(first, wide)]
        for h in self.hops:
            if h in self.dims:
                index[self.dims.index(h)] = {"core": c, "x": x, "z1": z % 2, "z2": z // 2}[h]
            elif h == "yr":
                half = wide // 2
                index[-1] = pl.ds(pl.multiple_of(first + sp * half, 128), half)
        return tuple(index)

    def copies(self, src, held, made, came, send, recv, local, at):
        out = [
            remote(src.at[self.share(flipped(at, g))], came[i], send.at[i], recv.at[i], g, at)
            for i, g in enumerate(self.groups)
        ]
        if not held:
            out.append(pltpu.make_async_copy(src.at[self.share(at)], made, local))
        return out

    def add(self, src, held, made, came, at):
        if self.hops == ("yg",):
            wide, sp = self.shape[-1], at[4]
            lead = (slice(None),) * (len(self.shape) - 1)
            made[lead + (pl.ds(pl.multiple_of(sp * wide, 128), wide),)] = src[self.share(at)]
            made[lead + (pl.ds(pl.multiple_of((1 - sp) * wide, 128), wide),)] = came[0][...]
        elif len(came) > 1:
            mine = src[self.share(at)] if held else made[...]
            one, two, three = (c[...].astype(F32) for c in came)
            made[...] = ((mine.astype(F32) + one) + (two + three)).astype(BF16)
        elif held:
            made[...] = src[self.share(at)] + came[0][...]
        else:
            made[...] += came[0][...]


class Flow:
    def __init__(self, array, shape, hops, dims=BLOCK, cols=None):
        self.array, self.shape, self.dims, self.cols = array, tuple(shape), dims, cols
        self.hops = list(hops)

    def step(self):
        part = Part(self.hops.pop(0), self.shape, self.dims, self.cols)
        self.shape, self.dims, self.cols = part.after, part.left, None
        return part


class Window:
    def __init__(self, start, stop, joint):
        self.start, self.stop, self.joint = start, stop, joint
        self.parts, self.sources, self.keeps = [], [], []


class Joint:
    def __init__(self):
        self.window = None


def plan(schedule):
    windows, arrays, latest = [], [], {}
    for n, (flows, start, stop, *joint) in enumerate(schedule):
        window = Window(start, stop, bool(joint))
        if joint:
            joint[0].window = n
        for i, flow in enumerate(flows):
            if flow in latest:
                source = ("part",) + latest[flow]
                before = windows[latest[flow][0]]
                before.keeps[latest[flow][1]] = False
            elif isinstance(flow.array, Joint):
                source = ("joint", flow.array.window)
            elif isinstance(flow.array, tuple):
                source = flow.array
            else:
                known = [k for k, a in enumerate(arrays) if a is flow.array]
                if not known:
                    arrays.append(flow.array)
                source = ("in", known[0] if known else len(arrays) - 1)
            window.parts.append(flow.step())
            window.sources.append(source)
            window.keeps.append(not joint)
            if not joint:
                latest[flow] = (n, i)
        windows.append(window)
    return windows, arrays, latest


def carrying(body, own, windows, arrays, grid, also, finale):
    ins, outs, held = own

    def kernel(*refs):
        refs = list(refs)

        def take(n):
            got = refs[:n]
            del refs[:n]
            return got

        my_in, arr = take(ins), take(arrays)
        my_out = take(outs)
        given = [[take(1)[0] if k else None for k in w.keeps] for w in windows]
        my_held = take(held)
        made, came, joints = [], [], []
        for w, g in zip(windows, given):
            if w.joint:
                joint, col, views = take(1)[0], 0, []
                for q in w.parts:
                    views.append(joint.at[(slice(None),) * (len(q.after) - 1) + (pl.ds(col, q.after[-1]),)])
                    col += q.after[-1]
                joints.append(joint)
                made.append(views)
            else:
                joints.append(None)
                made.append([ref if ref is not None else take(1)[0] for ref in g])
            came.append([take(len(q.groups)) for q in w.parts])
        mine = my_in + my_out + my_held
        step = pl.program_id(0)
        groups = [g for w in windows for q in w.parts for g in q.groups] + list(also)
        if groups:
            here = place()
            pl.when(step == 0)(lambda: greet(groups, here))
        if windows:
            send, recv, local = refs
        copies, sources, base = [], [], 0
        for w, m, c in zip(windows, made, came):
            now, froms = [], []
            for i, q in enumerate(w.parts):
                kind = w.sources[i]
                if kind[0] == "in":
                    src = arr[kind[1]]
                elif kind[0] == "ref":
                    src = mine[kind[1]]
                elif kind[0] == "joint":
                    src = joints[kind[1]]
                else:
                    src = made[kind[1]][kind[2]]
                held_here = kind[0] != "in"
                froms.append((src, held_here))
                now += q.copies(
                    src, held_here, m[i], c[i], send.at[base], recv.at[base], local.at[base], here
                )
                base += 1
            copies.append(now)
            sources.append(froms)

        def phase(number):
            for n, w in enumerate(windows):
                if w.stop == number:
                    for copy in copies[n]:
                        copy.wait()
                    for q, (src, held_here), m, c in zip(w.parts, sources[n], made[n], came[n]):
                        q.add(src, held_here, m, c, here)
            for n, w in enumerate(windows):
                if w.start == number:
                    for copy in copies[n]:
                        copy.start()

        used = sorted({w.start for w in windows} | {w.stop for w in windows})
        for number in used:
            if number < grid:
                pl.when(step == number)(functools.partial(phase, number))
        body(*mine)
        for number in used:
            if number >= grid:
                pl.when(step == grid - 1)(functools.partial(phase, number))
        if finale:
            pl.when(step == grid - 1)(lambda: finale(*mine))

    return kernel


def run(
    body, name, grid, ins, in_specs, outs, out_specs, held=(), schedule=(), collective=None,
    flops=0, moved=0, also=(), finale=None,
):
    in_specs, outs, out_specs, held = list(in_specs), list(outs), list(out_specs), list(held)
    windows, arrays, latest = plan(schedule)
    own = len(outs)
    kernel = carrying(body, (len(ins), own, len(held)), windows, len(arrays), grid, also, finale)
    in_specs += [pl.BlockSpec(memory_space=pl.ANY)] * len(arrays)
    order, count = [], 0
    for n, w in enumerate(windows):
        if w.joint:
            shape = w.parts[0].after[:-1] + (sum(q.after[-1] for q in w.parts),)
            held.append(pltpu.VMEM(shape, BF16))
        for i, (q, k) in enumerate(zip(w.parts, w.keeps)):
            if w.joint:
                continue
            if k:
                outs.append(jax.ShapeDtypeStruct(q.after, BF16))
                out_specs.append(whole(q.after))
                order.append((n, i))
            else:
                held.append(pltpu.VMEM(q.after, BF16))
        held += [pltpu.VMEM(q.came, BF16) for q in w.parts for _ in q.groups]
        count += len(w.parts)
    if windows:
        held += [pltpu.SemaphoreType.DMA((count, 3))] * 2 + [pltpu.SemaphoreType.DMA((count,))]
    results = pl.pallas_call(
        kernel,
        grid=(grid,),
        in_specs=in_specs,
        out_specs=out_specs,
        out_shape=outs,
        scratch_shapes=held,
        compiler_params=params(collective if windows or also else None),
        cost_estimate=cost(flops, moved),
        name=name,
    )(*ins, *arrays)
    for flow, where in latest.items():
        flow.array = results[own + order.index(where)]
    return results[:own]


def head_masks(dtype):
    lane = lax.broadcasted_iota(jnp.int32, (1, PAIR), 1)
    low = jnp.where(lane < HD, 1.0, 0.0)
    return low.astype(dtype), (1.0 - low).astype(dtype)


def query_code(code):
    lane = lax.broadcasted_iota(jnp.int32, code.shape, 1)
    return jnp.where(lane < 4, (code.astype(F32) - 1.0) * FAR, 0.0).astype(BF16)


def masked(s, diagonal):
    low, high = s[:-diagonal], s[-diagonal:]
    row = lax.broadcasted_iota(jnp.int32, high.shape, 0)
    col = lax.broadcasted_iota(jnp.int32, high.shape, 1)
    high = jnp.where(row <= col, high, -FAR)
    return jnp.concatenate([low, high], axis=0) if low.shape[0] else high


def softmax_over(jobs):
    results = []
    ready = nt(jobs[0][0], jobs[0][2])
    for n, (_, values_t, _, diagonal) in enumerate(jobs):
        s = ready
        if n + 1 < len(jobs):
            ready = nt(jobs[n + 1][0], jobs[n + 1][2])
        if diagonal:
            s = masked(s, diagonal)
        peak = jnp.max(s, axis=0, keepdims=True)
        e = jnp.exp(s - peak)
        norm = jnp.sum(e, axis=0, keepdims=True)
        results.append((nn(values_t, e.astype(BF16)) / norm, peak + jnp.log(norm)))
    return results


def pair_spec(rows, offset):
    return pl.BlockSpec((rows, PAIR), lambda p: (0, p + offset))


def whole(shape):
    return pl.BlockSpec(shape, lambda *_: (0,) * len(shape))


def delta_rows(g, o):
    prod = g.astype(F32) * o.astype(F32)
    upper = prod.astype(BF16)
    lower = (prod - upper.astype(F32)).astype(BF16)
    row = lax.broadcasted_iota(jnp.int32, (8, PAIR), 0)
    lane = lax.broadcasted_iota(jnp.int32, (8, PAIR), 1)
    pick = jnp.where(row == lane // HD, 1.0, 0.0).astype(BF16)
    return nt(pick, upper) + nt(pick, lower)


def back_pieces(jobs):
    def products(job):
        keys, values, q, g = job[:4]
        return nt(keys, q), nt(values, g)

    ready = products(jobs[0])
    for n, (_, _, _, _, lse, delta, causal) in enumerate(jobs):
        s, dp = ready
        if n + 1 < len(jobs):
            ready = products(jobs[n + 1])
        if causal:
            s = masked(s, s.shape[0])
        p = jnp.exp(s - lse)
        yield n, p.astype(BF16), (p * (dp - delta)).astype(BF16)


def cross_backward_kernel(
    size, pairs, q_ref, k_ref, v_ref, ko_ref, vo_ref, g_ref, o_ref, lse_ref, t_ref, own_ref, oth_ref,
    m_ref, mo_ref, wk_ref, wv_ref, gco_hbm, dh2_hbm, h1_hbm, ctx_hbm, wcq_hbm, wso_hbm, g1_ref, s1_ref,
    dm_out, dmo_out, gb_ref, dh1_ref, dsc_ref, late_ref, small_ref, grad_ref,
    dm_ref, dmo_acc, mt_ref, mot_ref, dcq_ref, dmo_ref, gco_ref, dh2_ref, h1_ref, ctx_ref, wcq_ref, wso_ref, move_ref,
):
    step = pl.program_id(0)
    rows, width = m_ref.shape
    lead = (slice(None),) * (len(grad_ref.shape) - 1)

    loads = [
        pltpu.make_async_copy(src, dst, move_ref.at[i])
        for i, (src, dst) in enumerate(
            (
                (gco_hbm, gco_ref), (dh2_hbm, dh2_ref), (h1_hbm, h1_ref), (ctx_hbm, ctx_ref), (wcq_hbm, wcq_ref),
                (wso_hbm, wso_ref),
            )
        )
    ]
    gives = [
        pltpu.make_async_copy(src, dst, move_ref.at[6 + i])
        for i, (src, dst) in enumerate(((dm_ref, dm_out), (dmo_ref, dmo_out)))
    ]

    def put(ref, col, grad):
        to = pl.ds(pl.multiple_of(col, PAIR), grad.shape[1])
        ref[lead + (to,)] = grad.astype(BF16).reshape(ref.shape[:-1] + (grad.shape[1],))

    @pl.when(step == 0)
    def _():
        for copy in loads:
            copy.start()
        mt_ref[...] = jnp.transpose(m_ref[...])
        mot_ref[...] = jnp.transpose(mo_ref[...])
        dm_ref[...] = jnp.zeros(dm_ref.shape, F32)
        dmo_acc[...] = jnp.zeros(dmo_acc.shape, F32)

    @pl.when(step == 1)
    def _():
        loads[0].wait()
        put(grad_ref, 0, gco_ref[...])

    @pl.when(step < pairs)
    def _():
        count = rows // size
        cols = pl.ds(pl.multiple_of(step * PAIR, PAIR), PAIR)
        sides = [(k_ref, v_ref, own_ref, mt_ref, dm_ref), (ko_ref, vo_ref, oth_ref, mot_ref, dmo_acc)]
        blocks = list(backward_pieces(size, q_ref, g_ref, o_ref, lse_ref, t_ref))
        weights = jnp.concatenate([wk_ref[...], wv_ref[...]], axis=1)
        jobs, where, turned = [], [], []
        for side, (kr, vr, code, _, _) in enumerate(sides):
            keys = jnp.concatenate([kr[...], code[...]], axis=1)
            turned.append(jnp.transpose(kr[...]))
            for block, head, qm, gm, q, lse, delta in blocks:
                jobs.append((keys, vr[...], q, gm, lse, delta, False))
                where.append((side, block, head, qm, gm))
        dq = [[0.0, 0.0] for _ in range(count)]
        dk, dv = [0.0, 0.0], [0.0, 0.0]
        grad = gb = 0.0
        for n, p, ds in back_pieces(jobs):
            side, block, head, qm, gm = where[n]
            dk[side] = dk[side] + nn(ds, qm)
            dv[side] = dv[side] + nn(p, gm)
            dq[block][head] = dq[block][head] + nn(turned[side][head * HD : (head + 1) * HD], ds)
            if n + 1 == len(jobs) or where[n + 1][0] != side:
                both = jnp.concatenate([dk[side].astype(BF16), dv[side].astype(BF16)], axis=1)
                mem, acc = sides[side][3:]
                grad = grad + nn(mem[...], both)
                gb = gb + total(both[:, PAIR:])
                acc[...] += nt(both, weights)
        for block in range(count):
            dcq_ref[block * size : (block + 1) * size, cols] = upright(dq[block]).astype(BF16)
        put(grad_ref, width + step * PAIR, grad[:, :PAIR])
        put(grad_ref, 2 * width + step * PAIR, grad[:, PAIR:])
        gb_ref[:, cols] = gb

    @pl.when(step == pairs)
    def _():
        dmo_ref[...] = dmo_acc[...].astype(BF16)
        for copy in gives:
            copy.start()
        for copy in loads[1:]:
            copy.wait()
        gain = line(g1_ref)
        n1, r1 = normed(h1_ref[...])
        a1b = (n1 * gain + line(s1_ref)).astype(BF16)
        dcq = dcq_ref[...]
        d1 = dh2_ref[...] + nt(dcq, wcq_ref[...])
        dh1 = norm_back(d1, n1, r1, gain)
        dh1_ref[...] = dh1
        dso = dh1.astype(BF16)
        dsc_ref[...] = nt(dso, wso_ref[...]).astype(BF16)
        put(late_ref, 0, tn(a1b, dcq))
        put(late_ref, width, tn(ctx_ref[...], dso))
        small_ref[0:1] = total(dcq)
        small_ref[1:2] = total(d1 * n1)
        small_ref[2:3] = total(d1)
        small_ref[3:4] = total(dso)
        small_ref[4:8] = jnp.zeros((4, width), F32)
        for copy in gives:
            copy.wait()


MIDDLE = 30


def cross_backward(block, cq, kv, kvo, g, o, lse, t, own, oth, m, mo, w, gco, dh2, h1, ctx, wcq, wso, gain, shift, schedule):
    rows, width = cq.shape
    pairs = width // PAIR

    def pair_of(size, offset):
        return pl.BlockSpec((size, PAIR), lambda s: (0, jnp.minimum(s, pairs - 1) + offset))

    flat, square = whole((rows, width)), whole((width, width))
    outs = [
        jax.ShapeDtypeStruct((rows, width), F32),
        jax.ShapeDtypeStruct((rows, width), BF16),
        jax.ShapeDtypeStruct((1, width), F32),
        jax.ShapeDtypeStruct((rows, width), F32),
        jax.ShapeDtypeStruct((rows, width), BF16),
        jax.ShapeDtypeStruct(block + (2 * width,), BF16),
        jax.ShapeDtypeStruct((8, width), F32),
    ]
    far = pl.BlockSpec(memory_space=pl.ANY)
    specs = [far, far, whole((1, width)), flat, flat, whole(block + (2 * width,)), whole((8, width))]
    held = []
    if schedule:
        held.append(pltpu.VMEM(block + (3 * width,), BF16))
    else:
        outs.append(jax.ShapeDtypeStruct(block + (3 * width,), BF16))
        specs.append(whole(block + (3 * width,)))
    held += [
        pltpu.VMEM((rows, width), F32),
        pltpu.VMEM((rows, width), F32),
        pltpu.VMEM((width, rows), BF16),
        pltpu.VMEM((width, rows), BF16),
        pltpu.VMEM((rows, width), BF16),
        pltpu.VMEM((rows, width), BF16),
    ]
    held += [pltpu.VMEM(a.shape, a.dtype) for a in (gco, dh2, h1, ctx, wcq, wso)] + [pltpu.SemaphoreType.DMA((8,))]
    return run(
        functools.partial(cross_backward_kernel, 256, pairs), "cross_backward", pairs + 1,
        (cq, kv, kv, kvo, kvo, g, o, lse, t, own, oth, m, mo, w, w, gco, dh2, h1, ctx, wcq, wso, gain, shift),
        [
            pair_of(rows, 0), pair_of(rows, 0), pair_of(rows, pairs), pair_of(rows, 0), pair_of(rows, pairs),
            pair_of(rows, 0), pair_of(rows, 0),
            pl.BlockSpec((8, rows), lambda s: (jnp.minimum(s, pairs - 1), 0)),
            whole((rows, 128)), whole((rows, 128)), whole((rows, 128)), flat, flat,
            pair_of(width, 0), pair_of(width, pairs),
            far, far, far, far, far, far, whole(gain.shape), whole(shift.shape),
        ],
        outs, specs, held, schedule, 3,
        64 * rows * rows * width + 24 * rows * width * width, 40 * rows * width,
    )


def upright(heads):
    return jnp.transpose(jnp.concatenate(heads, axis=0) * HD**-0.5)


def backward_pieces(size, q_ref, g_ref, o_ref, lse_ref, own_ref):
    masks = head_masks(BF16)
    scale = BF16(HD**-0.5)
    qcode = query_code(own_ref[...])
    delta = delta_rows(g_ref[...], o_ref[...])
    for block in range(q_ref.shape[0] // size):
        at = slice(block * size, (block + 1) * size)
        for head, mask in enumerate(masks):
            qm = q_ref[at] * (mask * scale)
            gm = g_ref[at] * mask
            q = jnp.concatenate([qm, qcode[at]], axis=1)
            yield block, head, qm, gm, q, lse_ref[head : head + 1, at], delta[head : head + 1, at]


def self_backward_kernel(
    size, *refs,
):
    (q2_ref, ko_ref, vo_ref, g2_ref, o2_ref, lse2_ref, wk2_ref, wv2_ref,
     q_ref, k_ref, v_ref, g_ref, o_ref, lse_ref, wq_ref, wk_ref, wv_ref,
     own_ref, oth_ref, x_ref, xo_ref, dh1_ref, sa_ref, sb_ref, sc_ref, sd_ref, dmo_ref,
     dx_ref, dmi_ref, grad_ref,
     dq_acc, dx_acc, dxo_acc, dkv_acc, xt_ref, xot_ref, dxo_ref, came_ref, memory_ref, turn_ref, send_ref, recv_ref) = refs
    step = pl.program_id(0)
    sp = lax.axis_index("sp")
    second = sp == 1
    rows, width = x_ref.shape
    pairs = width // PAIR
    early = pairs // 2
    count = rows // size
    over = remote(dxo_ref, came_ref, send_ref.at[0], recv_ref.at[0], ("y",))

    @pl.when(step == 0)
    def _():
        remote(dmo_ref, memory_ref, send_ref.at[1], recv_ref.at[1], ("y",)).start()
        xt_ref[...] = jnp.transpose(x_ref[...])
        turn_ref[...] = jnp.zeros(turn_ref.shape, F32)
        turn_ref[0:8] = sa_ref[...]
        turn_ref[8:16] = sb_ref[...]
        turn_ref[16:17] = sc_ref[...]
        dx_acc[...] = dh1_ref[...]

    @pl.when(jnp.logical_and(step == 0, second))
    def _():
        xot_ref[...] = jnp.transpose(xo_ref[...])
        dxo_acc[...] = jnp.zeros(dxo_acc.shape, F32)

    @pl.when(jnp.logical_and(step == 0, jnp.logical_not(second)))
    def _():
        dq_acc[...] = jnp.zeros(dq_acc.shape, F32)
        dkv_acc[...] = jnp.zeros(dkv_acc.shape, BF16)
        xot_ref[...] = jnp.zeros(xot_ref.shape, BF16)

    @pl.when(jnp.logical_and(step < early, second))
    def _():
        jobs, where, turned = [], [], []
        for two in range(2):
            at = slice(two * PAIR, (two + 1) * PAIR)
            keys = jnp.concatenate([ko_ref[:, at], oth_ref[...]], axis=1)
            turned.append(jnp.transpose(ko_ref[:, at]))
            stats = lse2_ref.at[8 * two : 8 * two + 8]
            for block, head, qm, gm, q, lse, delta in backward_pieces(
                size, q2_ref.at[:, at], g2_ref.at[:, at], o2_ref.at[:, at], stats, own_ref
            ):
                jobs.append((keys, vo_ref[:, at], q, gm, lse, delta, False))
                where.append((two, block, head, qm, gm))
        dk, dv = [0.0, 0.0], [0.0, 0.0]
        for n, p, ds in back_pieces(jobs):
            two, block, head, qm, gm = where[n]
            dk[two] = dk[two] + nn(ds, qm)
            dv[two] = dv[two] + nn(p, gm)
            of_head = slice(head * HD, (head + 1) * HD)
            dq_acc[2 * step + two, of_head, block * size : (block + 1) * size] = nn(turned[two][of_head], ds)
        for two in range(2):
            at = slice(two * PAIR, (two + 1) * PAIR)
            both = jnp.concatenate([dk[two].astype(BF16), dv[two].astype(BF16)], axis=1)
            dkv_acc[2 * step + two] = both
            dxo_acc[...] += nt(both, jnp.concatenate([wk2_ref[:, at], wv2_ref[:, at]], axis=1))

    @pl.when(jnp.logical_and(step == early - 1, second))
    def _():
        dxo_ref[...] = dxo_acc[...].astype(BF16)
        over.start()

    @pl.when(step >= early)
    def _():
        pair = step - early
        cols = pl.ds(pl.multiple_of(pair * PAIR, PAIR), PAIR)
        dkvo = dkv_acc[pair]
        grad_o = nn(xot_ref[...], dkvo)
        turned = jnp.transpose(k_ref[...])
        dq = [[0.0, 0.0] for _ in range(count)]
        dk, dv = [0.0] * count, [0.0] * count
        jobs, where = [], []
        keys = jnp.concatenate([k_ref[...], own_ref[...]], axis=1)
        for block, head, qm, gm, q, lse, delta in backward_pieces(size, q_ref, g_ref, o_ref, lse_ref, own_ref):
            for part in range(block + 1):
                of = slice(part * size, (part + 1) * size)
                jobs.append((keys[of], v_ref[of], q, gm, lse, delta, part == block))
                where.append((block, part, head, qm, gm))
        for n, p, ds in back_pieces(jobs):
            block, part, head, qm, gm = where[n]
            of = slice(part * size, (part + 1) * size)
            dk[part] = dk[part] + nn(ds, qm)
            dv[part] = dv[part] + nn(p, gm)
            dq[block][head] = dq[block][head] + nn(turned[head * HD : (head + 1) * HD, of], ds)
        dk, dv = (jnp.concatenate(a, axis=0).astype(BF16) for a in (dk, dv))
        before = dq_acc[pair]
        dq = jnp.concatenate(
            [
                upright(
                    [
                        part + before[head * HD : (head + 1) * HD, block * size : (block + 1) * size]
                        for head, part in enumerate(parts)
                    ]
                )
                for block, parts in enumerate(dq)
            ],
            axis=0,
        ).astype(BF16)
        dkv = jnp.concatenate([dk, dv], axis=1)
        grad_kv = nn(xt_ref[...], dkv) + grad_o
        grad_q = nn(xt_ref[...], dq)
        dx_acc[...] += nt(dkv, jnp.concatenate([wk_ref[...], wv_ref[...]], axis=1)) + nt(dq, wq_ref[...])
        lead = (slice(None),) * (len(grad_ref.shape) - 1)
        for n, grad in enumerate((grad_q, grad_kv[:, :PAIR], grad_kv[:, PAIR:])):
            to = pl.ds(pl.multiple_of((pair * 3 + n) * PAIR, PAIR), PAIR)
            grad_ref[lead + (to,)] = grad.astype(BF16).reshape(grad_ref.shape[:-1] + (PAIR,))
        turn_ref[21:22, cols] = total(dq)
        turn_ref[22:23, cols] = total(dv) + total(dkvo[:, PAIR:])

    @pl.when(step == early + pairs - 1)
    def _():
        shape = grad_ref.shape[:-1] + (PAIR,)
        lead = (slice(None),) * (len(shape) - 1)
        columns = jnp.transpose(turn_ref[...])
        if sd_ref.shape == columns.shape:
            columns = columns + sd_ref[...]
        grad_ref[lead + (slice(3 * width, 3 * width + PAIR),)] = columns.astype(BF16).reshape(shape)


def self_backward_finale(*refs):
    dmo_ref, dx_ref, dmi_ref = refs[26:29]
    dx_acc, dxo_ref, came_ref, memory_ref, send_ref, recv_ref = (refs[i] for i in (31, 36, 37, 38, 40, 41))
    remote(dmo_ref, memory_ref, send_ref.at[1], recv_ref.at[1], ("y",)).wait()
    dmi_ref[...] = memory_ref[...]
    over = remote(dxo_ref, came_ref, send_ref.at[0], recv_ref.at[0], ("y",))

    @pl.when(lax.axis_index("sp") == 0)
    def _():
        over.wait_recv()
        dx_ref[...] = (dx_acc[...] + came_ref[...].astype(F32)).astype(BF16)

    @pl.when(lax.axis_index("sp") == 1)
    def _():
        over.wait_send()
        dx_ref[...] = dx_acc[...].astype(BF16)


GRADS = 29


def self_backward(block, qkv, kvo, g, o, lse, own, oth, x, xo, w, dh1, small, dmo, schedule):
    rows, width = x.shape
    pairs = width // PAIR
    early = pairs // 2

    def two_of(size, offset):
        return pl.BlockSpec((size, 2 * PAIR), lambda s: (0, jnp.minimum(s, early - 1) + offset))

    def pair_of(size, offset):
        return pl.BlockSpec((size, PAIR), lambda s: (0, jnp.maximum(s - early, 0) + offset))

    made = block + (3 * width + PAIR,)
    outs = [jax.ShapeDtypeStruct((rows, width), BF16)] * 2
    specs = [whole((rows, width))] * 2
    held = []
    if schedule:
        held += [pltpu.VMEM(made, BF16)]
    else:
        outs += [jax.ShapeDtypeStruct(made, BF16)]
        specs += [whole(made)]
    held += [
        pltpu.VMEM((pairs, PAIR, rows), F32),
        pltpu.VMEM((rows, width), F32),
        pltpu.VMEM((rows, width), F32),
        pltpu.VMEM((pairs, rows, 2 * PAIR), BF16),
        pltpu.VMEM((width, rows), BF16),
        pltpu.VMEM((width, rows), BF16),
        pltpu.VMEM((rows, width), BF16),
        pltpu.VMEM((rows, width), BF16),
        pltpu.VMEM((rows, width), BF16),
        pltpu.VMEM((PAIR, width), F32),
        pltpu.SemaphoreType.DMA((2,)),
        pltpu.SemaphoreType.DMA((2,)),
    ]
    return run(
        functools.partial(self_backward_kernel, 256), "self_backward", early + pairs,
        (qkv, kvo, kvo, g, o, lse, w, w, qkv, qkv, qkv, g, o, lse, w, w, w, own, oth, x, xo, dh1) + tuple(small) + (dmo,),
        [
            two_of(rows, 0), two_of(rows, 0), two_of(rows, early), two_of(rows, 0), two_of(rows, 0),
            pl.BlockSpec((16, rows), lambda s: (jnp.minimum(s, early - 1), 0)),
            two_of(width, early), two_of(width, 2 * early),
            pair_of(rows, 0), pair_of(rows, pairs), pair_of(rows, 2 * pairs), pair_of(rows, 0), pair_of(rows, 0),
            pl.BlockSpec((8, rows), lambda s: (jnp.maximum(s - early, 0), 0)),
            pair_of(width, 0), pair_of(width, pairs), pair_of(width, 2 * pairs),
            whole((rows, 128)), whole((rows, 128)), whole((rows, width)), whole((rows, width)), whole((rows, width)),
        ] + [whole(a.shape) for a in small] + [pl.BlockSpec(memory_space=pl.ANY)],
        outs, specs, held, schedule, 5,
        48 * rows * rows * width + 20 * rows * width * width, 12 * width * width + 40 * rows * width,
        (("y",),), self_backward_finale,
    )


def code_of(docs_ref):
    row = lax.broadcasted_iota(jnp.int32, (PAIR, docs_ref.shape[1]), 0)
    return jnp.transpose(jnp.where(docs_ref[...] == row, 1.0, 0.0)).astype(BF16)


def line(ref):
    return ref[...].astype(F32)[None, :]


def front_kernel(
    size, x_hbm, m_hbm, td_ref, md_ref, wx_hbm, wm_hbm, wo_hbm, wq_hbm,
    bq_ref, bv_ref, bcv_ref, bso_ref, g_ref, s_ref, bcq_ref,
    qkv_out, mkv_out, kvo_out, mkvo_out, cq_out, ctx_out, cc_out, h_out, xo_out, mo_out,
    lse_ref, clse_ref, tt_ref, mt_ref, to_ref, mo_ref,
    x_ref, m_ref, wx_ref, wm_ref, wo_ref, wq_ref, xc_ref, mc_ref, tdc_ref, mdc_ref,
    qkv_ref, mkv_ref, kvo_ref, mkvo_ref, cq_ref, ctx_ref, cc_ref, h_ref, acc_ref,
    load_ref, store_ref, send_ref, recv_ref,
):
    rows, width = x_ref.shape
    pairs = width // PAIR
    second = lax.axis_index("sp") == 1
    first = jnp.logical_not(second)
    masks = head_masks(BF16)
    scale = BF16(HD**-0.5)
    loads = [
        pltpu.make_async_copy(src, dst, load_ref.at[i])
        for i, (src, dst) in enumerate(
            ((x_hbm, x_ref), (wx_hbm, wx_ref), (m_hbm, m_ref), (wm_hbm, wm_ref), (wo_hbm, wo_ref), (wq_hbm, wq_ref))
        )
    ]
    give = [
        pltpu.make_async_copy(src, dst, store_ref.at[i])
        for i, (src, dst) in enumerate(
            (
                (qkv_ref, qkv_out), (mkv_ref, mkv_out), (mkvo_ref, mkvo_out), (cq_ref, cq_out), (ctx_ref, ctx_out),
                (cc_ref, cc_out), (h_ref, h_out), (mc_ref, mo_out), (kvo_ref, kvo_out), (xc_ref, xo_out),
            )
        )
    ]
    x_over = remote(x_hbm, xc_ref, send_ref.at[0], recv_ref.at[0], ("y",))
    m_over = remote(m_hbm, mc_ref, send_ref.at[1], recv_ref.at[1], ("y",))
    docs = [
        remote(td_ref, tdc_ref, send_ref.at[2], recv_ref.at[2], ("y",)),
        remote(md_ref, mdc_ref, send_ref.at[3], recv_ref.at[3], ("y",)),
    ]
    for copy in loads:
        copy.start()
    greet([("y",)])
    for copy in docs:
        copy.start()
    pl.when(first)(x_over.start)
    pl.when(second)(m_over.start)

    def columns(offset, pair):
        return pl.ds(pl.multiple_of(offset + pair * PAIR, PAIR), PAIR)

    def heads(source, offset, pair, code, block):
        at = slice(block * size, (block + 1) * size)
        q = source[at, columns(offset, pair)]
        return [jnp.concatenate([q * (mask * scale), code[at]], axis=1) for mask in masks]

    def keep(block, pair, outs, lses, lse_out, out):
        at = slice(block * size, (block + 1) * size)
        mixed = jnp.concatenate(outs, axis=0)
        acc_ref[pair, :, at] = mixed
        out[at, columns(0, pair)] = jnp.transpose(mixed).astype(BF16)
        row = lax.broadcasted_iota(jnp.int32, (8, size), 0)
        lse_out[pl.ds(pl.multiple_of(pair * 8, 8), 8), at] = jnp.where(row == 0, lses[0], lses[1])

    def begin(block, pair, results, lse_out, out):
        keep(block, pair, [r for r, _ in results], [lse for _, lse in results], lse_out, out)

    def merge(block, pair, results, lse_out, out):
        at = slice(block * size, (block + 1) * size)
        stats = lse_out[pl.ds(pl.multiple_of(pair * 8, 8), 8), at]
        outs, lses = [], []
        for head, (r, lse) in enumerate(results):
            before = acc_ref[pair, head * HD : (head + 1) * HD, at]
            old = stats[head : head + 1]
            peak = jnp.maximum(old, lse)
            both = peak + jnp.log(jnp.exp(old - peak) + jnp.exp(lse - peak))
            outs.append(before * jnp.exp(old - both) + r * jnp.exp(lse - both))
            lses.append(both)
        keep(block, pair, outs, lses, lse_out, out)

    def halves(values):
        turned = jnp.transpose(values)
        return turned[:HD], turned[HD:]

    to_ref[...] = code_of(td_ref)
    mo_ref[...] = code_of(md_ref)
    loads[0].wait()
    loads[1].wait()
    for n, bias in enumerate((line(bq_ref), 0.0, line(bv_ref))):
        cols = slice(n * width, (n + 1) * width)
        qkv_ref[:, cols] = (nn(x_ref[...], wx_ref[:, cols]) + bias).astype(BF16)
    give[0].start()
    loads[2].wait()
    loads[3].wait()
    for n, bias in enumerate((0.0, line(bcv_ref))):
        cols = slice(n * width, (n + 1) * width)
        mkv_ref[:, cols] = (nn(m_ref[...], wm_ref[:, cols]) + bias).astype(BF16)
    give[1].start()

    def attend(query, keys_ref, key_at, value_at, key_code, diagonal, finish, stats, out):
        @pl.loop(0, pairs // 3)
        def _(third):
            code = query_code(to_ref[...])
            jobs, where = [], []
            for pair in (3 * third, 3 * third + 1, 3 * third + 2):
                keys = jnp.concatenate([keys_ref[:, columns(key_at, pair)], key_code[...]], axis=1)
                values = halves(keys_ref[:, columns(value_at, pair)])
                for block in range(rows // size):
                    end = (block + 1) * size if diagonal else rows
                    for q, v in zip(heads(query, 0, pair, code, block), values):
                        jobs.append((keys[:end], v[:, :end], q, size if diagonal else 0))
                    where.append((block, pair))
            results = softmax_over(jobs)
            for n, (block, pair) in enumerate(where):
                finish(block, pair, results[2 * n : 2 * n + 2], stats, out)

    attend(qkv_ref, qkv_ref, width, 2 * width, to_ref, True, begin, lse_ref, ctx_ref)

    for copy in docs:
        copy.wait()
    tt_ref[...] = code_of(tdc_ref)
    mt_ref[...] = code_of(mdc_ref)

    @pl.when(first)
    def _():
        x_over.wait_send()
        m_over.start()

    @pl.when(second)
    def _():
        x_over.wait_recv()
        give[9].start()
        for n, bias in enumerate((0.0, line(bv_ref))):
            cols = slice(n * width, (n + 1) * width)
            from_cols = slice((n + 1) * width, (n + 2) * width)
            kvo_ref[:, cols] = (nn(xc_ref[...], wx_ref[:, from_cols]) + bias).astype(BF16)
        give[8].start()

        attend(qkv_ref, kvo_ref, 0, width, tt_ref, False, merge, lse_ref, ctx_ref)

    give[4].start()
    loads[4].wait()
    loads[5].wait()
    h = x_ref[...].astype(F32) + nn(ctx_ref[...], wo_ref[...]) + line(bso_ref)
    h_ref[...] = h
    n, _ = normed(h)
    a = (n * line(g_ref) + line(s_ref)).astype(BF16)
    cq_ref[...] = (nn(a, wq_ref[...]) + line(bcq_ref)).astype(BF16)
    give[6].start()
    give[3].start()

    attend(cq_ref, mkv_ref, 0, width, mo_ref, False, begin, clse_ref, cc_ref)
    m_over.wait()
    give[7].start()
    for n, bias in enumerate((0.0, line(bcv_ref))):
        cols = slice(n * width, (n + 1) * width)
        mkvo_ref[:, cols] = (nn(mc_ref[...], wm_ref[:, cols]) + bias).astype(BF16)
    give[2].start()
    attend(cq_ref, mkvo_ref, 0, width, mt_ref, False, merge, clse_ref, cc_ref)
    give[5].start()
    for copy in give[:8]:
        copy.wait()

    @pl.when(second)
    def _():
        give[8].wait()
        give[9].wait()


def front(x, mem, td, md, wx, wm, wo, wq, vectors):
    rows, width = x.shape
    pairs = width // PAIR

    def flat(n):
        return jax.ShapeDtypeStruct((rows, n * width), BF16)

    stats = jax.ShapeDtypeStruct((8 * pairs, rows), F32)
    code = jax.ShapeDtypeStruct((rows, PAIR), BF16)
    far = pl.BlockSpec(memory_space=pl.ANY)
    near = pl.BlockSpec(memory_space=pltpu.VMEM)
    tall = jax.ShapeDtypeStruct((rows, width), F32)
    held = [flat(3), flat(2), flat(2), flat(2), flat(1), flat(1), flat(1), tall]
    return pl.pallas_call(
        functools.partial(front_kernel, 256),
        in_specs=[far, far, near, near, far, far, far, far] + [near] * len(vectors),
        out_specs=[far] * 10 + [near] * 6,
        out_shape=[flat(3), flat(2), flat(2), flat(2), flat(1), flat(1), flat(1), tall, flat(1), flat(1)]
        + [stats, stats, code, code, code, code],
        scratch_shapes=[pltpu.VMEM(a.shape, a.dtype) for a in (flat(1), flat(1))]
        + [pltpu.VMEM(w.shape, BF16) for w in (wx, wm, wo, wq)]
        + [pltpu.VMEM((rows, width), BF16)] * 2
        + [pltpu.VMEM((1, rows), jnp.int32)] * 2
        + [pltpu.VMEM(a.shape, a.dtype) for a in held]
        + [
            pltpu.VMEM((pairs, PAIR, rows), F32),
            pltpu.SemaphoreType.DMA((6,)),
            pltpu.SemaphoreType.DMA((10,)),
            pltpu.SemaphoreType.DMA((4,)),
            pltpu.SemaphoreType.DMA((4,)),
        ],
        compiler_params=params(1),
        cost_estimate=cost(22 * rows * width * width + 36 * rows * rows * width, 60 * rows * width),
        name="front",
    )(x, mem, td, md, wx, wm, wo, wq, *vectors)


def feed_kernel(
    count, comm, h1_ref, cc_ref, ct_ref, wco_ref, wi_ref, wo_ref,
    g1_ref, s1_ref, bco_ref, g2_ref, s2_ref, bfo_ref, g3_ref, s3_ref, bfi_ref, out_ref, dh2_ref, dcc_ref, gco_ref, *refs,
):
    if comm:
        gwi_ref, refs = refs[0], refs[1:]
    else:
        gwi_ref, gwo_ref, refs = refs[0], refs[1], refs[2:]
    small_ref, gib_ref, hid_ref, slope_ref, n2_ref, r2_ref, a2b_ref, acc_ref, df_ref, bias_ref, *refs = refs
    step = pl.program_id(0)
    width = acc_ref.shape[1]

    if comm:
        mi_ref, mo_ref, ci_ref, co_ref, send_ref, recv_ref = refs
        wide = ci_ref.shape[-1]
        here = place()
        c = here[1]

        def chunk_copies(j):
            at = pl.ds(pl.multiple_of(j * width, width), width)
            return [
                remote(mi_ref.at[:, :, at], ci_ref.at[:, :, at], send_ref.at[0, j], recv_ref.at[0, j], ("core",), here),
                remote(mo_ref.at[j], co_ref.at[j], send_ref.at[1, j], recv_ref.at[1, j], ("core",), here),
            ]

    @pl.when(step == 0)
    def _():
        if comm:
            greet([("core",)])
        wide = bfi_ref[...].astype(F32)
        for i in range(count):
            bias_ref[i : i + 1] = wide[None, i * width : (i + 1) * width]
        n1, _ = normed(h1_ref[...])
        a1 = n1 * line(g1_ref) + line(s1_ref)
        h2 = a1 + nn(cc_ref[...], wco_ref[...]) + line(bco_ref)
        n2, r2 = normed(h2)
        n2_ref[...] = n2
        r2_ref[...] = jnp.broadcast_to(r2, r2_ref.shape)
        a2 = n2 * line(g2_ref) + line(s2_ref)
        a2b_ref[...] = a2.astype(BF16)
        acc_ref[...] = a2 + line(bfo_ref)

    piece = 2 * PAIR
    pieces = [slice(i, i + piece) for i in range(0, width, piece)]

    @pl.when(step < count)
    def _():
        def product(at):
            return nn(a2b_ref[...], wi_ref[:, at])

        bias = bias_ref[pl.ds(step, 1)]
        ready = product(pieces[0])
        more = 0.0
        for i, at in enumerate(pieces):
            u = ready + bias[:, at]
            if i + 1 < len(pieces):
                ready = product(pieces[i + 1])
            cumul = 0.5 * (1.0 + lax.erf(u * 0.7071067811865476))
            density = jnp.exp(-0.5 * u * u) * 0.3989422804014327
            hid = (u * cumul).astype(BF16)
            hid_ref[step, :, at] = hid
            slope_ref[step, :, at] = cumul + u * density
            more = more + nn(hid, wo_ref[at])
        acc_ref[...] += more

    @pl.when(step == count - 1)
    def _():
        n3, r3 = normed(acc_ref[...])
        gain = line(g3_ref)
        out_ref[...] = (n3 * gain + line(s3_ref)).astype(BF16)
        e = ct_ref[...].astype(F32)
        d3 = norm_back(e, n3, r3, gain)
        df = d3.astype(BF16)
        df_ref[...] = df
        acc_ref[...] = d3
        small_ref[0:1] = total(e * n3)
        small_ref[1:2] = total(e)
        small_ref[2:3] = total(df)

    @pl.when(jnp.logical_and(step >= count, step < 2 * count))
    def _():
        j = step - count
        df = df_ref[...]

        def product(at):
            return nt(df, wo_ref[at])

        ready = product(pieces[0])
        more, go, gi, sums = 0.0, [], [], []
        for i, at in enumerate(pieces):
            du = (ready * slope_ref[j, :, at]).astype(BF16)
            if i + 1 < len(pieces):
                ready = product(pieces[i + 1])
            go.append(tn(hid_ref[j, :, at], df).astype(BF16))
            more = more + nt(du, wi_ref[:, at])
            gi.append(tn(a2b_ref[...], du).astype(BF16))
            sums.append(tn(du, jnp.ones((du.shape[0], PAIR), BF16)))
        acc_ref[...] += more
        go, gi, sums = (jnp.concatenate(a, axis=n) for a, n in ((go, 0), (gi, 1), (sums, 0)))
        quarter = width // gib_ref.shape[0]
        if gib_ref.shape[0] == 4:
            lane = lax.broadcasted_iota(jnp.int32, (quarter // 4, PAIR), 1)
            for i in range(4):
                part = sum(
                    jnp.where(lane == 17 + n, sums[(4 * i + n) * quarter // 4 : (4 * i + n + 1) * quarter // 4], 0.0)
                    for n in range(4)
                )
                gib_ref[i] = part
        else:
            gib_ref[0] = jnp.transpose(sums)[:1]
        if comm:
            at = pl.ds(pl.multiple_of(j * width, width), width)
            eight, narrow = gwi_ref.shape[:2]
            gi = gi.reshape(eight, 2, narrow, width)
            go = go.reshape(2, 2, 4, narrow, width)
            gwi_ref[:, :, at] = jnp.where(c == 0, gi[:, 0], gi[:, 1])
            mi_ref[:, :, at] = jnp.where(c == 0, gi[:, 1], gi[:, 0])
            mo_ref[j] = jnp.where(c == 0, go[:, 1], go[:, 0])
            for i in range(4):
                gwi_ref[pl.ds(2 * j, 2), :, pl.ds(wide + i * width, width)] = jnp.where(c == 0, go[:, 0, i], go[:, 1, i])
            for copy in chunk_copies(j):
                copy.start()
        else:
            gwo_ref[...] = go
            gwi_ref[...] = gi

    @pl.when(step == 2 * count)
    def _():
        d2 = acc_ref[...]
        n2 = n2_ref[...]
        dh2 = norm_back(d2, n2, r2_ref[:, :1], line(g2_ref))
        dh2_ref[...] = dh2
        dco = dh2.astype(BF16)
        dcc_ref[...] = nt(dco, wco_ref[...]).astype(BF16)
        gco_ref[...] = tn(cc_ref[...], dco).astype(BF16)
        small_ref[3:4] = total(d2 * n2)
        small_ref[4:5] = total(d2)
        small_ref[5:6] = total(dco)
        small_ref[6:8] = jnp.zeros((2, d2.shape[1]), F32)

    if comm:

        @pl.when(step > count)
        def _():
            j = step - count - 1
            at = pl.ds(pl.multiple_of(j * width, width), width)
            for copy in chunk_copies(j):
                copy.wait()
            gwi_ref[:, :, at] += ci_ref[:, :, at]
            for i in range(4):
                gwi_ref[pl.ds(2 * j, 2), :, pl.ds(wide + i * width, width)] += co_ref[j, :, i]


def feed(size, comm, h1, cc, ct, wco, wi, wo, vectors):
    rows, width = h1.shape
    wide = wi.shape[1]
    chunk = width
    count = wide // chunk

    def weight(s):
        return jnp.where(s < count, s, jnp.minimum(s - count, count - 1))

    def early(s):
        return jnp.clip(s - count, 0, count - 1)

    flat = whole((rows, width))
    square = whole((width, width))
    scratch = [
        pltpu.VMEM((count, rows, chunk), BF16),
        pltpu.VMEM((count, rows, chunk), F32),
        pltpu.VMEM((rows, width), F32),
        pltpu.VMEM((rows, 128), F32),
        pltpu.VMEM((rows, width), BF16),
        pltpu.VMEM((rows, width), F32),
        pltpu.VMEM((rows, width), BF16),
        pltpu.VMEM((8, width), F32),
    ]
    if comm:
        narrow = width // size
        gib_shape = jax.ShapeDtypeStruct((size, narrow, PAIR), F32)
        gib_spec = pl.BlockSpec((4, narrow, PAIR), lambda s: (early(s), 0, 0))
        grad_specs = [whole((size // 2, narrow, 2 * wide))]
        grad_shapes = [(size // 2, narrow, 2 * wide)]
        scratch += [
            pltpu.VMEM((size // 2, narrow, wide), BF16),
            pltpu.VMEM((count, 2, 4, narrow, width), BF16),
            pltpu.VMEM((size // 2, narrow, wide), BF16),
            pltpu.VMEM((count, 2, 4, narrow, width), BF16),
            pltpu.SemaphoreType.DMA((2, count)),
            pltpu.SemaphoreType.DMA((2, count)),
        ]
    else:
        gib_shape = jax.ShapeDtypeStruct((count, 1, width), F32)
        gib_spec = pl.BlockSpec((1, 1, chunk), lambda s: (early(s), 0, 0))
        grad_specs = [
            pl.BlockSpec((width, chunk), lambda s: (0, early(s))),
            pl.BlockSpec((chunk, width), lambda s: (early(s), 0)),
        ]
        grad_shapes = [(width, wide), (wide, width)]
    return pl.pallas_call(
        functools.partial(feed_kernel, count, comm),
        grid=(2 * count + 1,),
        in_specs=[
            flat, flat, flat, square,
            pl.BlockSpec((width, chunk), lambda s: (0, weight(s))),
            pl.BlockSpec((chunk, width), lambda s: (weight(s), 0)),
        ]
        + [whole(v.shape) for v in vectors],
        out_specs=[flat, flat, flat, square]
        + grad_specs
        + [whole((8, width)), gib_spec],
        out_shape=[
            jax.ShapeDtypeStruct((rows, width), BF16),
            jax.ShapeDtypeStruct((rows, width), F32),
            jax.ShapeDtypeStruct((rows, width), BF16),
            jax.ShapeDtypeStruct((width, width), BF16),
        ]
        + [jax.ShapeDtypeStruct(a, BF16) for a in grad_shapes]
        + [
            jax.ShapeDtypeStruct((8, width), F32),
            gib_shape,
        ],
        scratch_shapes=scratch,
        compiler_params=params(2 if comm else None),
        cost_estimate=cost(
            12 * rows * width * wide + 6 * rows * width * width, 12 * width * wide + 16 * rows * width
        ),
        name="feed",
    )(h1, cc, ct, wco, wi, wo, *vectors)


def outputs_kernel(moves, count, line, *refs):
    pieces, rest = refs[:count], refs[count:]
    out_ref, dx_ref, dm_ref, dmi_ref = rest[:4]
    outs = rest[4:]
    for piece, first, wide, which, row, col in moves:
        ref = pieces[piece]
        outs[which][row : row + ref.shape[0], col : col + wide] = ref[:, first : first + wide].astype(F32)
    turned, result, dx, dm = outs[-4:]
    turned[...] = jnp.transpose(pieces[line[0]][:, line[1] : line[1] + PAIR].astype(F32))
    result[...] = out_ref[...]
    dx[...] = dx_ref[...]
    dm[...] = (dm_ref[...] + dmi_ref[...].astype(F32)).astype(BF16)


def outputs(pieces, moves, line, shapes, out, dx, dm, dmi):
    ins = tuple(pieces) + (out, dx, dm, dmi)
    result = jax.ShapeDtypeStruct(out.shape, BF16)
    return pl.pallas_call(
        functools.partial(outputs_kernel, moves, len(pieces), line),
        out_shape=[jax.ShapeDtypeStruct(a, F32) for a in shapes]
        + [jax.ShapeDtypeStruct((PAIR, pieces[0].shape[0]), F32), result, result, result],
        compiler_params=params(),
        cost_estimate=cost(0, 12 << 20),
        name="outputs",
    )(*ins)


def moved(pieces, targets):
    out = []
    for n, (start, wide) in enumerate(pieces):
        for first, cols, which, row, col in targets:
            low, high = max(start, first), min(start + wide, first + cols)
            if low < high:
                out.append((n, low - start, high - low, which, row, col + low - first))
    return out


def schedule_of(flows, kernel):
    entries = [
        (start, order, name, start, stop)
        for order, name in enumerate(flows)
        for start, stop in PLAN[name][kernel]
    ]
    return tuple(([flows[name]], start, stop) for _, _, name, start, stop in sorted(entries))


def swap_sum(part, axis, pairs):
    came = lax.ppermute(part, axis, pairs)
    return part.astype(F32) + came.astype(F32)


def sum_scatter(grad, size, order):
    rows, cols = grad.shape
    bits = size.bit_length() - 1
    me = lax.axis_index("dp")
    now = grad.reshape((2,) * bits + (rows // size, cols))
    left = list(range(bits))[::-1]
    for bit in [b for b in order if b < bits] + [b for b in range(bits) if b not in order]:
        axis = left.index(bit)
        mine = (me >> bit) & 1
        keep = lax.dynamic_index_in_dim(now, mine, axis, keepdims=False)
        send = lax.dynamic_index_in_dim(now, 1 - mine, axis, keepdims=False)
        came = lax.ppermute(send, "dp", [(i, i ^ (1 << bit)) for i in range(size)])
        now = (keep.astype(F32) + came.astype(F32)).astype(BF16)
        left.pop(axis)
    return swap_sum(now, "sp", [(0, 1), (1, 0)])


def per_device(
    size,
    inputs,
    memory,
    target_docs,
    memory_docs,
    cotangent,
    w_qkv,
    b_q,
    b_v,
    w_so,
    b_so,
    g_one,
    s_one,
    w_cq,
    b_cq,
    w_ckv,
    b_cv,
    w_co,
    b_co,
    g_two,
    s_two,
    w_fi,
    b_fi,
    w_fo,
    b_fo,
    g_three,
    s_three,
):
    rows, width = inputs.shape[1:]
    wide = b_fi.shape[0]
    comm = size == 16
    narrow, broad = width // size, wide // size
    x, mem, ct = inputs[0], memory[0], cotangent[0]
    qkv, mkv, kvo, mkvo, cq, ctx, cc, h1, x_o, mem_o, lse, clse, t_oth, m_oth, t_own, m_own = front(
        x, mem, target_docs, memory_docs, w_qkv, w_ckv, w_so, w_cq, (b_q, b_v, b_cv, b_so, g_one, s_one, b_cq)
    )
    output, dh2, dcc, gco, gwi, *gwo, small_a, gib = feed(
        size, comm, h1, cc, ct, w_co, w_fi, w_fo,
        (g_one, s_one, b_co, g_two, s_two, b_fo, g_three, s_three, b_fi),
    )
    gib = gib.reshape(width, PAIR) if comm else gib.reshape(1, wide)

    block = (2, 2, 2, 2, narrow) if comm else (width,)
    at_cross, at_self, flows = (), (), {}
    if comm:
        late_shape = block + (2 * width,)
        sources = {
            "T0": (gwi.reshape(block[:3] + gwi.shape[1:]), block[:3] + gwi.shape[1:], BLOCK[:3]),
            "T1a": (("ref", MIDDLE), block + (3 * width,), BLOCK),
            "T1b": (None, late_shape, BLOCK),
            "G": (("ref", GRADS), block + (3 * width + PAIR,), BLOCK),
        }
        for name, (source, cols, hops, _, _) in PLAN.items():
            array, shape, dims = sources[source]
            flows[name] = Flow(array, shape, hops, dims, cols)
        at_cross = schedule_of(flows, 3)
        at_self = schedule_of(flows, 4)
    dm, dmo, gcvb, dh1, dsc, late, small_b, *early = cross_backward(
        block, cq, mkv, mkvo, dcc, cc, clse, t_own, m_own, m_oth, mem, mem_o, w_ckv,
        gco, dh2, h1, ctx, w_cq, w_so, g_one, s_one, at_cross,
    )
    for name, flow in flows.items():
        if PLAN[name][0] == "T1b":
            flow.array = late
    dx, dm_in, *made = self_backward(
        block, qkv, kvo, dsc, ctx, lse, t_own, t_oth, x, x_o, w_qkv, dh1, (small_a, small_b, gcvb, gib), dmo, at_self
    )
    if comm:
        targets = {
            "T0": [(0, wide, 2, 0, 0)] + [(wide + i * width, width, 3, i * narrow, 0) for i in range(4)],
            "T1a": [(0, width, 4, 0, 0), (width, 2 * width, 1, 0, 0)],
            "T1b": [(0, width, 5, 0, 0), (width, width, 6, 0, 0)],
            "G": [
                ((3 * pair + i) * PAIR, PAIR, 0, 0, i * width + pair * PAIR)
                for pair in range(width // PAIR)
                for i in range(3)
            ],
        }
        moves, line = [], None
        for n, (source, cols, *_) in enumerate(PLAN.values()):
            moves += [(n,) + m[1:] for m in moved([cols], targets[source])]
            if source == "G" and cols[0] <= 3 * width < sum(cols):
                line = n, 3 * width - cols[0]
        shapes = [(narrow, 3 * width), (narrow, 2 * width), (narrow, wide), (broad, width)] + [(narrow, width)] * 3
        t_qkv, t_cmem, t_fin, t_fout, t_cout, t_cquery, t_out, lines, output, derivative, grad_memory = outputs(
            [f.array for f in flows.values()], moves, line, shapes, output, dx, dm, dm_in
        )
    else:
        (early,), (made,) = early, made
        columns = made[:, 3 * width : 3 * width + PAIR]
        gqkv = made[:, : 3 * width].reshape(width, -1, 3, PAIR).swapaxes(1, 2).reshape(width, 3 * width)
        t_fin, t_fout, t_cout, t_cquery, t_out, t_cmem, t_qkv, lines = (
            sum_scatter(g, size, (0, 1, 2, 3))
            for g in (
                gwi, gwo[0], early[:, :width], late[:, :width], late[:, width:], early[:, width:], gqkv, columns
            )
        )
        lines, derivative = lines.T, dx
        grad_memory = (dm + dm_in.astype(F32)).astype(BF16)
    t_gthree, t_sthree, t_fobias, t_gtwo, t_stwo, t_cobias = (lines[i] for i in range(6))
    t_cqbias, t_gone, t_sone, t_obias = (lines[i] for i in range(8, 12))
    t_cvbias, t_qbias, t_vbias = lines[16], lines[21], lines[22]
    if comm:
        t_fibias = lines[17:21].reshape(-1)
    else:
        t_fibias = lax.psum(lax.psum_scatter(gib[0], "dp", scatter_dimension=0, tiled=True), "sp")
    return (
        output[None],
        derivative[None],
        grad_memory[None],
        t_qkv,
        t_qbias,
        t_vbias,
        t_out,
        t_obias,
        t_gone,
        t_sone,
        t_cquery,
        t_cqbias,
        t_cmem,
        t_cvbias,
        t_cout,
        t_cobias,
        t_gtwo,
        t_stwo,
        t_fin,
        t_fibias,
        t_fout,
        t_fobias,
        t_gthree,
        t_sthree,
    )


def solution(mesh):
    split = P("dp", "sp", None)
    in_specs = (split, split, P("dp", "sp"), P("dp", "sp"), split) + (P(),) * 21
    matrix, vector = P("dp", None), P("dp")
    out_specs = (
        split, split, split,
        matrix, vector, vector,
        matrix, vector, vector, vector,
        matrix, vector,
        matrix, vector,
        matrix, vector, vector, vector,
        matrix, vector,
        matrix, vector, vector, vector,
    )
    return jax.shard_map(
        functools.partial(per_device, mesh.shape["dp"]),
        mesh=mesh, in_specs=in_specs, out_specs=out_specs, check_vma=False,
    )
```

```python
import functools

import jax
import jax.numpy as jnp
from jax import lax
from jax.experimental import pallas as pl
from jax.experimental.pallas import tpu as pltpu
from jax.sharding import PartitionSpec as P

HD = 64
PAIR = 2 * HD
EPS = 1e-05
FAR = 1.0e9
VMEM = 60 * 1024 * 1024
F32 = jnp.float32
BF16 = jnp.bfloat16


def nn(a, b):
    return lax.dot_general(a, b, (((1,), (0,)), ((), ())), preferred_element_type=F32)


def nt(a, b):
    return lax.dot_general(a, b, (((1,), (1,)), ((), ())), preferred_element_type=F32)


def tn(a, b):
    return lax.dot_general(a, b, (((0,), (0,)), ((), ())), preferred_element_type=F32)


def params(collective=None):
    if collective is None:
        return pltpu.CompilerParams(vmem_limit_bytes=VMEM)
    return pltpu.CompilerParams(
        vmem_limit_bytes=VMEM, collective_id=collective, has_side_effects=True
    )


def cost(flops, moved):
    return pl.CostEstimate(flops=int(flops), bytes_accessed=int(moved), transcendentals=0)


def normed(h):
    centred = h - jnp.mean(h, axis=-1, keepdims=True)
    rstd = lax.rsqrt(jnp.mean(centred * centred, axis=-1, keepdims=True) + EPS)
    return centred * rstd, rstd


def norm_back(grad, n, rstd, gain):
    scaled = grad * gain
    centre = jnp.mean(scaled, axis=-1, keepdims=True)
    along = jnp.mean(scaled * n, axis=-1, keepdims=True)
    return rstd * (scaled - centre - n * along)


def total(a):
    return jnp.sum(a.astype(F32), axis=0, keepdims=True)


def place():
    me = lax.axis_index("dp")
    return me, me % 2, (me // 2) % 2, me // 4, lax.axis_index("sp")


def flipped(at, hops):
    me, c, x, z, sp = at
    for hop in hops:
        if hop == "core":
            me, c = me + 1 - 2 * c, 1 - c
        elif hop == "x":
            me, x = me + 2 - 4 * x, 1 - x
        elif hop == "z1":
            me, z = me + 4 - 8 * (z % 2), z + 1 - 2 * (z % 2)
        elif hop == "z2":
            me, z = me + 8 - 16 * (z // 2), z + 2 - 4 * (z // 2)
        else:
            sp = 1 - sp
    return me, c, x, z, sp


def partner(hops, at=None):
    there = flipped(at or place(), hops)
    return {"dp": there[0], "sp": there[4]}


def greet(groups, at=None):
    groups = sorted({tuple("y" if h[0] == "y" else h for h in hops) for hops in groups})
    barrier = pltpu.get_barrier_semaphore()
    for hops in groups:
        pl.semaphore_signal(barrier, inc=1, device_id=partner(hops, at), device_id_type=pl.DeviceIdType.MESH)
    pl.semaphore_wait(barrier, len(groups))


def remote(src, dst, send, recv, hops, at=None):
    return pltpu.make_async_remote_copy(
        src_ref=src, dst_ref=dst, send_sem=send, recv_sem=recv,
        device_id=partner(hops, at), device_id_type=pl.DeviceIdType.MESH,
    )


PLAN = {
    "T0_0": ("T0", (0, 2048), ("yr", "x", "z1", "z2", "yg"), ((0, 4), (4, 7)), ((0, 4), (4, 6), (6, 9))),
    "T0_1": ("T0", (2048, 1408), ("x", "z1", "z2", "y"), ((0, 5), (5, 7)), ((0, 3), (3, 6))),
    "T0_2": ("T0", (3456, 1792), ("z1", "yr", "x", "z2", "yg"), ((0, 4), (4, 6), (6, 7)), ((0, 3), (3, 5))),
    "T0_3": ("T0", (5248, 896), ("x", "z1", "z2", "y"), ((0, 4), (4, 6), (6, 7)), ((0, 2),)),
    "T1a_0": ("T1a", (0, 256), ("core", "yr", "x", "z1", "z2", "yg"), ((6, 7),), ((0, 2), (2, 4), (4, 5), (5, 6), (6, 7))),
    "T1a_1": ("T1a", (256, 1536), ("core", "x", "z1", "z2", "y"), ((6, 7),), ((0, 6), (6, 9), (9, 20), (20, 37))),
    "T1a_2": ("T1a", (1792, 512), ("core", "x", "yr", "z1", "z2", "yg"), ((6, 7),), ((0, 4), (4, 6), (6, 7), (7, 8), (8, 9))),
    "T1b_0": ("T1b", (0, 512), ("core", "x", "z1", "z2", "y"), (), ((0, 1), (1, 5), (5, 7), (7, 9), (9, 15))),
    "T1b_1": ("T1b", (512, 1024), ("core", "z1", "yr", "x", "z2", "yg"), (), ((0, 2), (2, 6), (6, 10), (10, 18), (18, 29), (29, 38))),
    "G1_0": ("G", (0, 768), ("core", "x", "z1", "yr", "z2", "yg"), (), ((5, 6), (6, 8), (8, 13), (13, 17), (17, 26), (26, 35))),
    "G2_0": ("G", (768, 512), ("core", "x", "yr", "z1", "z2", "yg"), (), ((7, 8), (8, 12), (12, 19), (19, 28), (28, 34), (34, 41))),
    "G2_1": ("G", (1280, 256), ("core", "yr", "x", "z1", "z2", "yg"), (), ((7, 8), (8, 11), (11, 16), (16, 23), (23, 27), (27, 32))),
    "G3_0": ("G", (1536, 384), ("core", ("x", "z1"), "z2", "y"), (), ((8, 9), (9, 24), (24, 31), (31, 40))),
    "G4_0": ("G", (1920, 256), ("core", "z1", "x", "z2", "y"), (), ((9, 14), (14, 22), (22, 25), (25, 33), (33, 39))),
    "G4_1": ("G", (2176, 256), ("core", "x", "z1", "z2", "y"), (), ((9, 14), (14, 21), (21, 30), (30, 36), (36, 42))),
}
BLOCK = ("z2", "z1", "x", "core")


class Part:
    def __init__(self, hop, shape, dims, cols=None):
        self.hops = hops = hop if isinstance(hop, tuple) else (hop,)
        self.groups = [(h,) for h in hops] + ([hops] if len(hops) > 1 else [])
        self.dims = dims
        self.cols = cols or (0, shape[-1])
        self.shape = shape = tuple(shape[:-1]) + (self.cols[1],)
        for h in hops:
            if h in dims:
                at = dims.index(h)
                shape, dims = shape[:at] + shape[at + 1 :], dims[:at] + dims[at + 1 :]
            elif h != "y":
                shape = shape[:-1] + (shape[-1] // 2 if h == "yr" else 2 * shape[-1],)
        self.after, self.left = shape, dims
        self.came = self.shape if hops == ("yg",) else shape

    def share(self, at):
        _, c, x, z, sp = at
        first, wide = self.cols
        index = [slice(None)] * (len(self.shape) - 1) + [pl.ds(first, wide)]
        for h in self.hops:
            if h in self.dims:
                index[self.dims.index(h)] = {"core": c, "x": x, "z1": z % 2, "z2": z // 2}[h]
            elif h == "yr":
                half = wide // 2
                index[-1] = pl.ds(pl.multiple_of(first + sp * half, 128), half)
        return tuple(index)

    def copies(self, src, held, made, came, send, recv, local, at):
        out = [
            remote(src.at[self.share(flipped(at, g))], came[i], send.at[i], recv.at[i], g, at)
            for i, g in enumerate(self.groups)
        ]
        if not held:
            out.append(pltpu.make_async_copy(src.at[self.share(at)], made, local))
        return out

    def add(self, src, held, made, came, at):
        if self.hops == ("yg",):
            wide, sp = self.shape[-1], at[4]
            lead = (slice(None),) * (len(self.shape) - 1)
            made[lead + (pl.ds(pl.multiple_of(sp * wide, 128), wide),)] = src[self.share(at)]
            made[lead + (pl.ds(pl.multiple_of((1 - sp) * wide, 128), wide),)] = came[0][...]
        elif len(came) > 1:
            mine = src[self.share(at)] if held else made[...]
            one, two, three = (c[...].astype(F32) for c in came)
            made[...] = ((mine.astype(F32) + one) + (two + three)).astype(BF16)
        elif held:
            made[...] = src[self.share(at)] + came[0][...]
        else:
            made[...] += came[0][...]


class Flow:
    def __init__(self, array, shape, hops, dims=BLOCK, cols=None):
        self.array, self.shape, self.dims, self.cols = array, tuple(shape), dims, cols
        self.hops = list(hops)

    def step(self):
        part = Part(self.hops.pop(0), self.shape, self.dims, self.cols)
        self.shape, self.dims, self.cols = part.after, part.left, None
        return part


class Window:
    def __init__(self, start, stop, joint):
        self.start, self.stop, self.joint = start, stop, joint
        self.parts, self.sources, self.keeps = [], [], []


class Joint:
    def __init__(self):
        self.window = None


def plan(schedule):
    windows, arrays, latest = [], [], {}
    for n, (flows, start, stop, *joint) in enumerate(schedule):
        window = Window(start, stop, bool(joint))
        if joint:
            joint[0].window = n
        for i, flow in enumerate(flows):
            if flow in latest:
                source = ("part",) + latest[flow]
                before = windows[latest[flow][0]]
                before.keeps[latest[flow][1]] = False
            elif isinstance(flow.array, Joint):
                source = ("joint", flow.array.window)
            elif isinstance(flow.array, tuple):
                source = flow.array
            else:
                known = [k for k, a in enumerate(arrays) if a is flow.array]
                if not known:
                    arrays.append(flow.array)
                source = ("in", known[0] if known else len(arrays) - 1)
            window.parts.append(flow.step())
            window.sources.append(source)
            window.keeps.append(not joint)
            if not joint:
                latest[flow] = (n, i)
        windows.append(window)
    return windows, arrays, latest


def carrying(body, own, windows, arrays, grid, also, finale):
    ins, outs, held = own

    def kernel(*refs):
        refs = list(refs)

        def take(n):
            got = refs[:n]
            del refs[:n]
            return got

        my_in, arr = take(ins), take(arrays)
        my_out = take(outs)
        given = [[take(1)[0] if k else None for k in w.keeps] for w in windows]
        my_held = take(held)
        made, came, joints = [], [], []
        for w, g in zip(windows, given):
            if w.joint:
                joint, col, views = take(1)[0], 0, []
                for q in w.parts:
                    views.append(joint.at[(slice(None),) * (len(q.after) - 1) + (pl.ds(col, q.after[-1]),)])
                    col += q.after[-1]
                joints.append(joint)
                made.append(views)
            else:
                joints.append(None)
                made.append([ref if ref is not None else take(1)[0] for ref in g])
            came.append([take(len(q.groups)) for q in w.parts])
        mine = my_in + my_out + my_held
        step = pl.program_id(0)
        groups = [g for w in windows for q in w.parts for g in q.groups] + list(also)
        if groups:
            here = place()
            pl.when(step == 0)(lambda: greet(groups, here))
        if windows:
            send, recv, local = refs
        copies, sources, base = [], [], 0
        for w, m, c in zip(windows, made, came):
            now, froms = [], []
            for i, q in enumerate(w.parts):
                kind = w.sources[i]
                if kind[0] == "in":
                    src = arr[kind[1]]
                elif kind[0] == "ref":
                    src = mine[kind[1]]
                elif kind[0] == "joint":
                    src = joints[kind[1]]
                else:
                    src = made[kind[1]][kind[2]]
                held_here = kind[0] != "in"
                froms.append((src, held_here))
                now += q.copies(
                    src, held_here, m[i], c[i], send.at[base], recv.at[base], local.at[base], here
                )
                base += 1
            copies.append(now)
            sources.append(froms)

        def phase(number):
            for n, w in enumerate(windows):
                if w.stop == number:
                    for copy in copies[n]:
                        copy.wait()
                    for q, (src, held_here), m, c in zip(w.parts, sources[n], made[n], came[n]):
                        q.add(src, held_here, m, c, here)
            for n, w in enumerate(windows):
                if w.start == number:
                    for copy in copies[n]:
                        copy.start()

        used = sorted({w.start for w in windows} | {w.stop for w in windows})
        for number in used:
            if number < grid:
                pl.when(step == number)(functools.partial(phase, number))
        body(*mine)
        for number in used:
            if number >= grid:
                pl.when(step == grid - 1)(functools.partial(phase, number))
        if finale:
            pl.when(step == grid - 1)(lambda: finale(*mine))

    return kernel


def run(
    body, name, grid, ins, in_specs, outs, out_specs, held=(), schedule=(), collective=None,
    flops=0, moved=0, also=(), finale=None,
):
    in_specs, outs, out_specs, held = list(in_specs), list(outs), list(out_specs), list(held)
    windows, arrays, latest = plan(schedule)
    own = len(outs)
    kernel = carrying(body, (len(ins), own, len(held)), windows, len(arrays), grid, also, finale)
    in_specs += [pl.BlockSpec(memory_space=pl.ANY)] * len(arrays)
    order, count = [], 0
    for n, w in enumerate(windows):
        if w.joint:
            shape = w.parts[0].after[:-1] + (sum(q.after[-1] for q in w.parts),)
            held.append(pltpu.VMEM(shape, BF16))
        for i, (q, k) in enumerate(zip(w.parts, w.keeps)):
            if w.joint:
                continue
            if k:
                outs.append(jax.ShapeDtypeStruct(q.after, BF16))
                out_specs.append(whole(q.after))
                order.append((n, i))
            else:
                held.append(pltpu.VMEM(q.after, BF16))
        held += [pltpu.VMEM(q.came, BF16) for q in w.parts for _ in q.groups]
        count += len(w.parts)
    if windows:
        held += [pltpu.SemaphoreType.DMA((count, 3))] * 2 + [pltpu.SemaphoreType.DMA((count,))]
    results = pl.pallas_call(
        kernel,
        grid=(grid,),
        in_specs=in_specs,
        out_specs=out_specs,
        out_shape=outs,
        scratch_shapes=held,
        compiler_params=params(collective if windows or also else None),
        cost_estimate=cost(flops, moved),
        name=name,
    )(*ins, *arrays)
    for flow, where in latest.items():
        flow.array = results[own + order.index(where)]
    return results[:own]


def head_masks(dtype):
    lane = lax.broadcasted_iota(jnp.int32, (1, PAIR), 1)
    low = jnp.where(lane < HD, 1.0, 0.0)
    return low.astype(dtype), (1.0 - low).astype(dtype)


def query_code(code):
    lane = lax.broadcasted_iota(jnp.int32, code.shape, 1)
    return jnp.where(lane < 4, (code.astype(F32) - 1.0) * FAR, 0.0).astype(BF16)


def masked(s, diagonal):
    low, high = s[:-diagonal], s[-diagonal:]
    row = lax.broadcasted_iota(jnp.int32, high.shape, 0)
    col = lax.broadcasted_iota(jnp.int32, high.shape, 1)
    high = jnp.where(row <= col, high, -FAR)
    return jnp.concatenate([low, high], axis=0) if low.shape[0] else high


def softmax_over(jobs):
    results = []
    ready = nt(jobs[0][0], jobs[0][2])
    for n, (_, values_t, _, diagonal) in enumerate(jobs):
        s = ready
        if n + 1 < len(jobs):
            ready = nt(jobs[n + 1][0], jobs[n + 1][2])
        if diagonal:
            s = masked(s, diagonal)
        peak = jnp.max(s, axis=0, keepdims=True)
        e = jnp.exp(s - peak)
        norm = jnp.sum(e, axis=0, keepdims=True)
        results.append((nn(values_t, e.astype(BF16)) / norm, peak + jnp.log(norm)))
    return results


def pair_spec(rows, offset):
    return pl.BlockSpec((rows, PAIR), lambda p: (0, p + offset))


def whole(shape):
    return pl.BlockSpec(shape, lambda *_: (0,) * len(shape))


def delta_rows(g, o):
    prod = g.astype(F32) * o.astype(F32)
    upper = prod.astype(BF16)
    lower = (prod - upper.astype(F32)).astype(BF16)
    row = lax.broadcasted_iota(jnp.int32, (8, PAIR), 0)
    lane = lax.broadcasted_iota(jnp.int32, (8, PAIR), 1)
    pick = jnp.where(row == lane // HD, 1.0, 0.0).astype(BF16)
    return nt(pick, upper) + nt(pick, lower)


def back_pieces(jobs):
    def products(job):
        keys, values, q, g = job[:4]
        return nt(keys, q), nt(values, g)

    ready = products(jobs[0])
    for n, (_, _, _, _, lse, delta, causal) in enumerate(jobs):
        s, dp = ready
        if n + 1 < len(jobs):
            ready = products(jobs[n + 1])
        if causal:
            s = masked(s, s.shape[0])
        p = jnp.exp(s - lse)
        yield n, p.astype(BF16), (p * (dp - delta)).astype(BF16)


def cross_backward_kernel(
    size, pairs, q_ref, k_ref, v_ref, ko_ref, vo_ref, g_ref, o_ref, lse_ref, t_ref, own_ref, oth_ref,
    m_ref, mo_ref, wk_ref, wv_ref, gco_hbm, dh2_hbm, h1_hbm, ctx_hbm, wcq_hbm, wso_hbm, g1_ref, s1_ref,
    dm_out, dmo_out, gb_ref, dh1_ref, dsc_ref, late_ref, small_ref, grad_ref,
    dm_ref, dmo_acc, mt_ref, mot_ref, dcq_ref, dmo_ref, gco_ref, dh2_ref, h1_ref, ctx_ref, wcq_ref, wso_ref, move_ref,
):
    step = pl.program_id(0)
    rows, width = m_ref.shape
    lead = (slice(None),) * (len(grad_ref.shape) - 1)

    loads = [
        pltpu.make_async_copy(src, dst, move_ref.at[i])
        for i, (src, dst) in enumerate(
            (
                (gco_hbm, gco_ref), (dh2_hbm, dh2_ref), (h1_hbm, h1_ref), (ctx_hbm, ctx_ref), (wcq_hbm, wcq_ref),
                (wso_hbm, wso_ref),
            )
        )
    ]
    gives = [
        pltpu.make_async_copy(src, dst, move_ref.at[6 + i])
        for i, (src, dst) in enumerate(((dm_ref, dm_out), (dmo_ref, dmo_out)))
    ]

    def put(ref, col, grad):
        to = pl.ds(pl.multiple_of(col, PAIR), grad.shape[1])
        ref[lead + (to,)] = grad.astype(BF16).reshape(ref.shape[:-1] + (grad.shape[1],))

    @pl.when(step == 0)
    def _():
        for copy in loads:
            copy.start()
        mt_ref[...] = jnp.transpose(m_ref[...])
        mot_ref[...] = jnp.transpose(mo_ref[...])
        dm_ref[...] = jnp.zeros(dm_ref.shape, F32)
        dmo_acc[...] = jnp.zeros(dmo_acc.shape, F32)

    @pl.when(step == 1)
    def _():
        loads[0].wait()
        put(grad_ref, 0, gco_ref[...])

    @pl.when(step < pairs)
    def _():
        count = rows // size
        cols = pl.ds(pl.multiple_of(step * PAIR, PAIR), PAIR)
        sides = [(k_ref, v_ref, own_ref, mt_ref, dm_ref), (ko_ref, vo_ref, oth_ref, mot_ref, dmo_acc)]
        blocks = list(backward_pieces(size, q_ref, g_ref, o_ref, lse_ref, t_ref))
        weights = jnp.concatenate([wk_ref[...], wv_ref[...]], axis=1)
        jobs, where, turned = [], [], []
        for side, (kr, vr, code, _, _) in enumerate(sides):
            keys = jnp.concatenate([kr[...], code[...]], axis=1)
            turned.append(jnp.transpose(kr[...]))
            for block, head, qm, gm, q, lse, delta in blocks:
                jobs.append((keys, vr[...], q, gm, lse, delta, False))
                where.append((side, block, head, qm, gm))
        dq = [[0.0, 0.0] for _ in range(count)]
        dk, dv = [0.0, 0.0], [0.0, 0.0]
        grad = gb = 0.0
        for n, p, ds in back_pieces(jobs):
            side, block, head, qm, gm = where[n]
            dk[side] = dk[side] + nn(ds, qm)
            dv[side] = dv[side] + nn(p, gm)
            dq[block][head] = dq[block][head] + nn(turned[side][head * HD : (head + 1) * HD], ds)
            if n + 1 == len(jobs) or where[n + 1][0] != side:
                both = jnp.concatenate([dk[side].astype(BF16), dv[side].astype(BF16)], axis=1)
                mem, acc = sides[side][3:]
                grad = grad + nn(mem[...], both)
                gb = gb + total(both[:, PAIR:])
                acc[...] += nt(both, weights)
        for block in range(count):
            dcq_ref[block * size : (block + 1) * size, cols] = upright(dq[block]).astype(BF16)
        put(grad_ref, width + step * PAIR, grad[:, :PAIR])
        put(grad_ref, 2 * width + step * PAIR, grad[:, PAIR:])
        gb_ref[:, cols] = gb

    @pl.when(step == pairs)
    def _():
        dmo_ref[...] = dmo_acc[...].astype(BF16)
        for copy in gives:
            copy.start()
        for copy in loads[1:]:
            copy.wait()
        gain = line(g1_ref)
        n1, r1 = normed(h1_ref[...])
        a1b = (n1 * gain + line(s1_ref)).astype(BF16)
        dcq = dcq_ref[...]
        d1 = dh2_ref[...] + nt(dcq, wcq_ref[...])
        dh1 = norm_back(d1, n1, r1, gain)
        dh1_ref[...] = dh1
        dso = dh1.astype(BF16)
        dsc_ref[...] = nt(dso, wso_ref[...]).astype(BF16)
        put(late_ref, 0, tn(a1b, dcq))
        put(late_ref, width, tn(ctx_ref[...], dso))
        small_ref[0:1] = total(dcq)
        small_ref[1:2] = total(d1 * n1)
        small_ref[2:3] = total(d1)
        small_ref[3:4] = total(dso)
        small_ref[4:8] = jnp.zeros((4, width), F32)
        for copy in gives:
            copy.wait()


MIDDLE = 30


def cross_backward(block, cq, kv, kvo, g, o, lse, t, own, oth, m, mo, w, gco, dh2, h1, ctx, wcq, wso, gain, shift, schedule):
    rows, width = cq.shape
    pairs = width // PAIR

    def pair_of(size, offset):
        return pl.BlockSpec((size, PAIR), lambda s: (0, jnp.minimum(s, pairs - 1) + offset))

    flat, square = whole((rows, width)), whole((width, width))
    outs = [
        jax.ShapeDtypeStruct((rows, width), F32),
        jax.ShapeDtypeStruct((rows, width), BF16),
        jax.ShapeDtypeStruct((1, width), F32),
        jax.ShapeDtypeStruct((rows, width), F32),
        jax.ShapeDtypeStruct((rows, width), BF16),
        jax.ShapeDtypeStruct(block + (2 * width,), BF16),
        jax.ShapeDtypeStruct((8, width), F32),
    ]
    far = pl.BlockSpec(memory_space=pl.ANY)
    specs = [far, far, whole((1, width)), flat, flat, whole(block + (2 * width,)), whole((8, width))]
    held = []
    if schedule:
        held.append(pltpu.VMEM(block + (3 * width,), BF16))
    else:
        outs.append(jax.ShapeDtypeStruct(block + (3 * width,), BF16))
        specs.append(whole(block + (3 * width,)))
    held += [
        pltpu.VMEM((rows, width), F32),
        pltpu.VMEM((rows, width), F32),
        pltpu.VMEM((width, rows), BF16),
        pltpu.VMEM((width, rows), BF16),
        pltpu.VMEM((rows, width), BF16),
        pltpu.VMEM((rows, width), BF16),
    ]
    held += [pltpu.VMEM(a.shape, a.dtype) for a in (gco, dh2, h1, ctx, wcq, wso)] + [pltpu.SemaphoreType.DMA((8,))]
    return run(
        functools.partial(cross_backward_kernel, 256, pairs), "cross_backward", pairs + 1,
        (cq, kv, kv, kvo, kvo, g, o, lse, t, own, oth, m, mo, w, w, gco, dh2, h1, ctx, wcq, wso, gain, shift),
        [
            pair_of(rows, 0), pair_of(rows, 0), pair_of(rows, pairs), pair_of(rows, 0), pair_of(rows, pairs),
            pair_of(rows, 0), pair_of(rows, 0),
            pl.BlockSpec((8, rows), lambda s: (jnp.minimum(s, pairs - 1), 0)),
            whole((rows, 128)), whole((rows, 128)), whole((rows, 128)), flat, flat,
            pair_of(width, 0), pair_of(width, pairs),
            far, far, far, far, far, far, whole(gain.shape), whole(shift.shape),
        ],
        outs, specs, held, schedule, 3,
        64 * rows * rows * width + 24 * rows * width * width, 40 * rows * width,
    )


def upright(heads):
    return jnp.transpose(jnp.concatenate(heads, axis=0) * HD**-0.5)


def backward_pieces(size, q_ref, g_ref, o_ref, lse_ref, own_ref):
    masks = head_masks(BF16)
    scale = BF16(HD**-0.5)
    qcode = query_code(own_ref[...])
    delta = delta_rows(g_ref[...], o_ref[...])
    for block in range(q_ref.shape[0] // size):
        at = slice(block * size, (block + 1) * size)
        for head, mask in enumerate(masks):
            qm = q_ref[at] * (mask * scale)
            gm = g_ref[at] * mask
            q = jnp.concatenate([qm, qcode[at]], axis=1)
            yield block, head, qm, gm, q, lse_ref[head : head + 1, at], delta[head : head + 1, at]


def self_backward_kernel(
    size, *refs,
):
    (q2_ref, ko_ref, vo_ref, g2_ref, o2_ref, lse2_ref, wk2_ref, wv2_ref,
     q_ref, k_ref, v_ref, g_ref, o_ref, lse_ref, wq_ref, wk_ref, wv_ref,
     own_ref, oth_ref, x_ref, xo_ref, dh1_ref, sa_ref, sb_ref, sc_ref, sd_ref, dm_hbm, dmo_hbm, out_hbm,
     dx_out, dm_out, out_out, grad_ref,
     dq_acc, dx_acc, dxo_acc, dkv_acc, xt_ref, xot_ref, dxo_ref, came_ref, memory_ref, dm_ref, gm_ref, dx_ref, turn_ref,
     send_ref, recv_ref) = refs
    step = pl.program_id(0)
    second = lax.axis_index("dp") % 2 == 1
    rows, width = x_ref.shape
    pairs = width // PAIR
    early = pairs // 2
    count = rows // size
    over = remote(dxo_ref, came_ref, send_ref.at[0], recv_ref.at[0], ("core",))
    m_over = remote(dmo_hbm, memory_ref, send_ref.at[1], recv_ref.at[1], ("core",))
    dm_load = pltpu.make_async_copy(dm_hbm, dm_ref, send_ref.at[5])

    @pl.when(step == 0)
    def _():
        m_over.start()
        dm_load.start()
        Swap(out_hbm, out_out, send_ref.at[2], recv_ref.at[2]).start()
        xt_ref[...] = jnp.transpose(x_ref[...])
        turn_ref[...] = jnp.zeros(turn_ref.shape, F32)
        turn_ref[0:8] = sa_ref[...]
        turn_ref[8:16] = sb_ref[...]
        turn_ref[16:17] = sc_ref[...]
        dx_acc[...] = dh1_ref[...]

    @pl.when(jnp.logical_and(step == 0, second))
    def _():
        xot_ref[...] = jnp.transpose(xo_ref[...])
        dxo_acc[...] = jnp.zeros(dxo_acc.shape, F32)

    @pl.when(jnp.logical_and(step == 0, jnp.logical_not(second)))
    def _():
        dq_acc[...] = jnp.zeros(dq_acc.shape, F32)
        dkv_acc[...] = jnp.zeros(dkv_acc.shape, BF16)
        xot_ref[...] = jnp.zeros(xot_ref.shape, BF16)

    @pl.when(jnp.logical_and(step < early, second))
    def _():
        jobs, where, turned = [], [], []
        for two in range(2):
            at = slice(two * PAIR, (two + 1) * PAIR)
            keys = jnp.concatenate([ko_ref[:, at], oth_ref[...]], axis=1)
            turned.append(jnp.transpose(ko_ref[:, at]))
            stats = lse2_ref.at[8 * two : 8 * two + 8]
            for block, head, qm, gm, q, lse, delta in backward_pieces(
                size, q2_ref.at[:, at], g2_ref.at[:, at], o2_ref.at[:, at], stats, own_ref
            ):
                jobs.append((keys, vo_ref[:, at], q, gm, lse, delta, False))
                where.append((two, block, head, qm, gm))
        dk, dv = [0.0, 0.0], [0.0, 0.0]
        for n, p, ds in back_pieces(jobs):
            two, block, head, qm, gm = where[n]
            dk[two] = dk[two] + nn(ds, qm)
            dv[two] = dv[two] + nn(p, gm)
            of_head = slice(head * HD, (head + 1) * HD)
            dq_acc[2 * step + two, of_head, block * size : (block + 1) * size] = nn(turned[two][of_head], ds)
        for two in range(2):
            at = slice(two * PAIR, (two + 1) * PAIR)
            both = jnp.concatenate([dk[two].astype(BF16), dv[two].astype(BF16)], axis=1)
            dkv_acc[2 * step + two] = both
            dxo_acc[...] += nt(both, jnp.concatenate([wk2_ref[:, at], wv2_ref[:, at]], axis=1))

    @pl.when(jnp.logical_and(step == early - 1, second))
    def _():
        dxo_ref[...] = dxo_acc[...].astype(BF16)
        over.start()

    @pl.when(step == early)
    def _():
        m_over.wait()
        dm_load.wait()
        gm_ref[...] = (dm_ref[...] + memory_ref[...].astype(F32)).astype(BF16)
        Swap(gm_ref, dm_out, send_ref.at[3], recv_ref.at[3]).start()

    @pl.when(step >= early)
    def _():
        pair = step - early
        cols = pl.ds(pl.multiple_of(pair * PAIR, PAIR), PAIR)
        dkvo = dkv_acc[pair]
        grad_o = nn(xot_ref[...], dkvo)
        turned = jnp.transpose(k_ref[...])
        dq = [[0.0, 0.0] for _ in range(count)]
        dk, dv = [0.0] * count, [0.0] * count
        jobs, where = [], []
        keys = jnp.concatenate([k_ref[...], own_ref[...]], axis=1)
        for block, head, qm, gm, q, lse, delta in backward_pieces(size, q_ref, g_ref, o_ref, lse_ref, own_ref):
            for part in range(block + 1):
                of = slice(part * size, (part + 1) * size)
                jobs.append((keys[of], v_ref[of], q, gm, lse, delta, part == block))
                where.append((block, part, head, qm, gm))
        for n, p, ds in back_pieces(jobs):
            block, part, head, qm, gm = where[n]
            of = slice(part * size, (part + 1) * size)
            dk[part] = dk[part] + nn(ds, qm)
            dv[part] = dv[part] + nn(p, gm)
            dq[block][head] = dq[block][head] + nn(turned[head * HD : (head + 1) * HD, of], ds)
        dk, dv = (jnp.concatenate(a, axis=0).astype(BF16) for a in (dk, dv))
        before = dq_acc[pair]
        dq = jnp.concatenate(
            [
                upright(
                    [
                        part + before[head * HD : (head + 1) * HD, block * size : (block + 1) * size]
                        for head, part in enumerate(parts)
                    ]
                )
                for block, parts in enumerate(dq)
            ],
            axis=0,
        ).astype(BF16)
        dkv = jnp.concatenate([dk, dv], axis=1)
        grad_kv = nn(xt_ref[...], dkv) + grad_o
        grad_q = nn(xt_ref[...], dq)
        dx_acc[...] += nt(dkv, jnp.concatenate([wk_ref[...], wv_ref[...]], axis=1)) + nt(dq, wq_ref[...])
        lead = (slice(None),) * (len(grad_ref.shape) - 1)
        for n, grad in enumerate((grad_q, grad_kv[:, :PAIR], grad_kv[:, PAIR:])):
            to = pl.ds(pl.multiple_of((pair * 3 + n) * PAIR, PAIR), PAIR)
            grad_ref[lead + (to,)] = grad.astype(BF16).reshape(grad_ref.shape[:-1] + (PAIR,))
        turn_ref[21:22, cols] = total(dq)
        turn_ref[22:23, cols] = total(dv) + total(dkvo[:, PAIR:])

    @pl.when(step == early + pairs - 1)
    def _():
        shape = grad_ref.shape[:-1] + (PAIR,)
        lead = (slice(None),) * (len(shape) - 1)
        columns = jnp.transpose(turn_ref[...])
        if sd_ref.shape == columns.shape:
            columns = columns + sd_ref[...]
        grad_ref[lead + (slice(3 * width, 3 * width + PAIR),)] = columns.astype(BF16).reshape(shape)

        @pl.when(second)
        def _():
            over.wait_send()
            dx_ref[...] = dx_acc[...].astype(BF16)

        @pl.when(jnp.logical_not(second))
        def _():
            over.wait_recv()
            dx_ref[...] = (dx_acc[...] + came_ref[...].astype(F32)).astype(BF16)

        Swap(dx_ref, dx_out, send_ref.at[4], recv_ref.at[4]).start()


def self_backward_finale(*refs):
    out_hbm, dx_out, dm_out, out_out = refs[28:32]
    gm_ref, dx_ref, _, send_ref, recv_ref = refs[43:48]
    Swap(out_hbm, out_out, send_ref.at[2], recv_ref.at[2]).wait()
    Swap(gm_ref, dm_out, send_ref.at[3], recv_ref.at[3]).wait()
    Swap(dx_ref, dx_out, send_ref.at[4], recv_ref.at[4]).wait()


GRADS = 32


def self_backward(block, qkv, kvo, g, o, lse, own, oth, x, xo, w, dh1, small, dm, dmo, out, schedule):
    rows, width = x.shape
    pairs = width // PAIR
    early = pairs // 2

    def two_of(size, offset):
        return pl.BlockSpec((size, 2 * PAIR), lambda s: (0, jnp.minimum(s, early - 1) + offset))

    def pair_of(size, offset):
        return pl.BlockSpec((size, PAIR), lambda s: (0, jnp.maximum(s - early, 0) + offset))

    made = block + (3 * width + PAIR,)
    far = pl.BlockSpec(memory_space=pl.ANY)
    outs = [jax.ShapeDtypeStruct((rows, width), BF16)] * 3
    specs = [far] * 3
    held = []
    if schedule:
        held += [pltpu.VMEM(made, BF16)]
    else:
        outs += [jax.ShapeDtypeStruct(made, BF16)]
        specs += [whole(made)]
    held += [
        pltpu.VMEM((pairs, PAIR, rows), F32),
        pltpu.VMEM((rows, width), F32),
        pltpu.VMEM((rows, width), F32),
        pltpu.VMEM((pairs, rows, 2 * PAIR), BF16),
        pltpu.VMEM((width, rows), BF16),
        pltpu.VMEM((width, rows), BF16),
        pltpu.VMEM((rows, width), BF16),
        pltpu.VMEM((rows, width), BF16),
        pltpu.VMEM((rows, width), BF16),
        pltpu.VMEM((rows, width), F32),
        pltpu.VMEM((rows, width), BF16),
        pltpu.VMEM((rows, width), BF16),
        pltpu.VMEM((PAIR, width), F32),
        pltpu.SemaphoreType.DMA((6,)),
        pltpu.SemaphoreType.DMA((5,)),
    ]
    return run(
        functools.partial(self_backward_kernel, 256), "self_backward", early + pairs,
        (qkv, kvo, kvo, g, o, lse, w, w, qkv, qkv, qkv, g, o, lse, w, w, w, own, oth, x, xo, dh1) + tuple(small) + (dm, dmo, out),
        [
            two_of(rows, 0), two_of(rows, 0), two_of(rows, early), two_of(rows, 0), two_of(rows, 0),
            pl.BlockSpec((16, rows), lambda s: (jnp.minimum(s, early - 1), 0)),
            two_of(width, early), two_of(width, 2 * early),
            pair_of(rows, 0), pair_of(rows, pairs), pair_of(rows, 2 * pairs), pair_of(rows, 0), pair_of(rows, 0),
            pl.BlockSpec((8, rows), lambda s: (jnp.maximum(s - early, 0), 0)),
            pair_of(width, 0), pair_of(width, pairs), pair_of(width, 2 * pairs),
            whole((rows, 128)), whole((rows, 128)), whole((rows, width)), whole((rows, width)), whole((rows, width)),
        ] + [whole(a.shape) for a in small] + [far] * 3,
        outs, specs, held, schedule, 5,
        48 * rows * rows * width + 20 * rows * width * width, 12 * width * width + 40 * rows * width,
        (("core",), ("core", "y")), self_backward_finale,
    )


def code_of(docs_ref):
    row = lax.broadcasted_iota(jnp.int32, (PAIR, docs_ref.shape[1]), 0)
    return jnp.transpose(jnp.where(docs_ref[...] == row, 1.0, 0.0)).astype(BF16)


def line(ref):
    return ref[...].astype(F32)[None, :]


def moving():
    return lax.axis_index("dp") % 2 != lax.axis_index("sp")


class Swap:
    def __init__(self, src, dst, send, recv):
        self.there = remote(src, dst, send, recv, ("core", "y"))
        self.here = pltpu.make_async_copy(src, dst, recv)

    def start(self):
        pl.when(moving())(self.there.start)
        pl.when(jnp.logical_not(moving()))(self.here.start)

    def wait_recv(self):
        pl.when(moving())(self.there.wait_recv)
        pl.when(jnp.logical_not(moving()))(self.here.wait)

    def wait_send(self):
        pl.when(moving())(self.there.wait_send)

    def wait(self):
        self.wait_send()
        self.wait_recv()


def front_kernel(
    size, x_hbm, m_hbm, c_hbm, td_hbm, md_hbm, wx_hbm, wm_hbm, wo_hbm, wq_hbm,
    bq_ref, bv_ref, bcv_ref, bso_ref, g_ref, s_ref, bcq_ref,
    qkv_out, mkv_out, kvo_out, mkvo_out, cq_out, ctx_out, cc_out, h_out, xo_out, mo_out, x_out, m_out, c_out,
    lse_ref, clse_ref, tt_ref, mt_ref, to_ref, mo_ref,
    x_ref, m_ref, wx_ref, wm_ref, wo_ref, wq_ref, xc_ref, mc_ref, td_ref, md_ref, tdc_ref, mdc_ref,
    qkv_ref, mkv_ref, kvo_ref, mkvo_ref, cq_ref, ctx_ref, cc_ref, h_ref, acc_ref,
    load_ref, store_ref, send_ref, recv_ref,
):
    rows, width = x_ref.shape
    pairs = width // PAIR
    second = lax.axis_index("dp") % 2 == 1
    first = jnp.logical_not(second)
    masks = head_masks(BF16)
    scale = BF16(HD**-0.5)
    loads = [
        pltpu.make_async_copy(src, dst, load_ref.at[i])
        for i, (src, dst) in enumerate(((wx_hbm, wx_ref), (wm_hbm, wm_ref), (wo_hbm, wo_ref), (wq_hbm, wq_ref)))
    ]
    give = [
        pltpu.make_async_copy(src, dst, store_ref.at[i])
        for i, (src, dst) in enumerate(
            (
                (qkv_ref, qkv_out), (mkv_ref, mkv_out), (mkvo_ref, mkvo_out), (cq_ref, cq_out), (ctx_ref, ctx_out),
                (cc_ref, cc_out), (h_ref, h_out), (mc_ref, mo_out), (x_ref, x_out), (m_ref, m_out),
                (kvo_ref, kvo_out), (xc_ref, xo_out),
            )
        )
    ]
    swaps = [
        Swap(src, dst, send_ref.at[i], recv_ref.at[i])
        for i, (src, dst) in enumerate(
            ((td_hbm, td_ref), (md_hbm, md_ref), (x_hbm, x_ref), (m_hbm, m_ref), (c_hbm, c_out))
        )
    ]
    x_over = remote(x_ref, xc_ref, send_ref.at[5], recv_ref.at[5], ("core",))
    m_over = remote(m_ref, mc_ref, send_ref.at[6], recv_ref.at[6], ("core",))
    docs = [
        remote(td_ref, tdc_ref, send_ref.at[7], recv_ref.at[7], ("core",)),
        remote(md_ref, mdc_ref, send_ref.at[8], recv_ref.at[8], ("core",)),
    ]
    for copy in loads:
        copy.start()
    greet([("core", "y"), ("core",)])
    for copy in swaps[:3]:
        copy.start()

    def columns(offset, pair):
        return pl.ds(pl.multiple_of(offset + pair * PAIR, PAIR), PAIR)

    def heads(source, offset, pair, code, block):
        at = slice(block * size, (block + 1) * size)
        q = source[at, columns(offset, pair)]
        return [jnp.concatenate([q * (mask * scale), code[at]], axis=1) for mask in masks]

    def keep(block, pair, outs, lses, lse_out, out):
        at = slice(block * size, (block + 1) * size)
        mixed = jnp.concatenate(outs, axis=0)
        acc_ref[pair, :, at] = mixed
        out[at, columns(0, pair)] = jnp.transpose(mixed).astype(BF16)
        row = lax.broadcasted_iota(jnp.int32, (8, size), 0)
        lse_out[pl.ds(pl.multiple_of(pair * 8, 8), 8), at] = jnp.where(row == 0, lses[0], lses[1])

    def begin(block, pair, results, lse_out, out):
        keep(block, pair, [r for r, _ in results], [lse for _, lse in results], lse_out, out)

    def merge(block, pair, results, lse_out, out):
        at = slice(block * size, (block + 1) * size)
        stats = lse_out[pl.ds(pl.multiple_of(pair * 8, 8), 8), at]
        outs, lses = [], []
        for head, (r, lse) in enumerate(results):
            before = acc_ref[pair, head * HD : (head + 1) * HD, at]
            old = stats[head : head + 1]
            peak = jnp.maximum(old, lse)
            both = peak + jnp.log(jnp.exp(old - peak) + jnp.exp(lse - peak))
            outs.append(before * jnp.exp(old - both) + r * jnp.exp(lse - both))
            lses.append(both)
        keep(block, pair, outs, lses, lse_out, out)

    def halves(values):
        turned = jnp.transpose(values)
        return turned[:HD], turned[HD:]

    for copy in swaps[:2]:
        copy.wait_recv()
    for copy in docs:
        copy.start()
    to_ref[...] = code_of(td_ref)
    mo_ref[...] = code_of(md_ref)
    loads[0].wait()
    swaps[2].wait()
    swaps[3].start()
    pl.when(first)(x_over.start)
    give[8].start()
    for n, bias in enumerate((line(bq_ref), 0.0, line(bv_ref))):
        cols = slice(n * width, (n + 1) * width)
        qkv_ref[:, cols] = (nn(x_ref[...], wx_ref[:, cols]) + bias).astype(BF16)
    give[0].start()

    def attend(query, keys_ref, key_at, value_at, key_code, diagonal, finish, stats, out):
        @pl.loop(0, pairs // 3)
        def _(third):
            code = query_code(to_ref[...])
            jobs, where = [], []
            for pair in (3 * third, 3 * third + 1, 3 * third + 2):
                keys = jnp.concatenate([keys_ref[:, columns(key_at, pair)], key_code[...]], axis=1)
                values = halves(keys_ref[:, columns(value_at, pair)])
                for block in range(rows // size):
                    end = (block + 1) * size if diagonal else rows
                    for q, v in zip(heads(query, 0, pair, code, block), values):
                        jobs.append((keys[:end], v[:, :end], q, size if diagonal else 0))
                    where.append((block, pair))
            results = softmax_over(jobs)
            for n, (block, pair) in enumerate(where):
                finish(block, pair, results[2 * n : 2 * n + 2], stats, out)

    attend(qkv_ref, qkv_ref, width, 2 * width, to_ref, True, begin, lse_ref, ctx_ref)

    for copy in docs:
        copy.wait()
    tt_ref[...] = code_of(tdc_ref)
    mt_ref[...] = code_of(mdc_ref)
    swaps[3].wait()
    m_over.start()
    swaps[4].start()
    give[9].start()
    pl.when(first)(x_over.wait_send)

    @pl.when(second)
    def _():
        x_over.wait_recv()
        give[11].start()
        for n, bias in enumerate((0.0, line(bv_ref))):
            cols = slice(n * width, (n + 1) * width)
            from_cols = slice((n + 1) * width, (n + 2) * width)
            kvo_ref[:, cols] = (nn(xc_ref[...], wx_ref[:, from_cols]) + bias).astype(BF16)
        give[10].start()

        attend(qkv_ref, kvo_ref, 0, width, tt_ref, False, merge, lse_ref, ctx_ref)

    give[4].start()
    loads[2].wait()
    loads[3].wait()
    h = x_ref[...].astype(F32) + nn(ctx_ref[...], wo_ref[...]) + line(bso_ref)
    h_ref[...] = h
    n, _ = normed(h)
    a = (n * line(g_ref) + line(s_ref)).astype(BF16)
    cq_ref[...] = (nn(a, wq_ref[...]) + line(bcq_ref)).astype(BF16)
    give[6].start()
    give[3].start()

    loads[1].wait()
    for n, bias in enumerate((0.0, line(bcv_ref))):
        cols = slice(n * width, (n + 1) * width)
        mkv_ref[:, cols] = (nn(m_ref[...], wm_ref[:, cols]) + bias).astype(BF16)
    give[1].start()
    attend(cq_ref, mkv_ref, 0, width, mo_ref, False, begin, clse_ref, cc_ref)
    m_over.wait()
    give[7].start()
    for n, bias in enumerate((0.0, line(bcv_ref))):
        cols = slice(n * width, (n + 1) * width)
        mkvo_ref[:, cols] = (nn(mc_ref[...], wm_ref[:, cols]) + bias).astype(BF16)
    give[2].start()
    attend(cq_ref, mkvo_ref, 0, width, mt_ref, False, merge, clse_ref, cc_ref)
    give[5].start()
    for copy in give[:10]:
        copy.wait()
    for copy in swaps[:2]:
        copy.wait_send()
    swaps[4].wait()

    @pl.when(second)
    def _():
        give[10].wait()
        give[11].wait()


def front(x, mem, ct, td, md, wx, wm, wo, wq, vectors):
    rows, width = x.shape
    pairs = width // PAIR

    def flat(n):
        return jax.ShapeDtypeStruct((rows, n * width), BF16)

    stats = jax.ShapeDtypeStruct((8 * pairs, rows), F32)
    code = jax.ShapeDtypeStruct((rows, PAIR), BF16)
    far = pl.BlockSpec(memory_space=pl.ANY)
    near = pl.BlockSpec(memory_space=pltpu.VMEM)
    tall = jax.ShapeDtypeStruct((rows, width), F32)
    held = [flat(3), flat(2), flat(2), flat(2), flat(1), flat(1), flat(1), tall]
    return pl.pallas_call(
        functools.partial(front_kernel, 256),
        in_specs=[far] * 9 + [near] * len(vectors),
        out_specs=[far] * 13 + [near] * 6,
        out_shape=[flat(3), flat(2), flat(2), flat(2), flat(1), flat(1), flat(1), tall] + [flat(1)] * 5
        + [stats, stats, code, code, code, code],
        scratch_shapes=[pltpu.VMEM((rows, width), BF16)] * 2
        + [pltpu.VMEM(w.shape, BF16) for w in (wx, wm, wo, wq)]
        + [pltpu.VMEM((rows, width), BF16)] * 2
        + [pltpu.VMEM((1, rows), jnp.int32)] * 4
        + [pltpu.VMEM(a.shape, a.dtype) for a in held]
        + [
            pltpu.VMEM((pairs, PAIR, rows), F32),
            pltpu.SemaphoreType.DMA((4,)),
            pltpu.SemaphoreType.DMA((12,)),
            pltpu.SemaphoreType.DMA((9,)),
            pltpu.SemaphoreType.DMA((9,)),
        ],
        compiler_params=params(1),
        cost_estimate=cost(22 * rows * width * width + 36 * rows * rows * width, 60 * rows * width),
        name="front",
    )(x, mem, ct, td, md, wx, wm, wo, wq, *vectors)


def feed_kernel(
    count, comm, h1_ref, cc_ref, ct_ref, wco_ref, wi_ref, wo_ref,
    g1_ref, s1_ref, bco_ref, g2_ref, s2_ref, bfo_ref, g3_ref, s3_ref, bfi_ref, out_ref, dh2_ref, dcc_ref, gco_ref, *refs,
):
    if comm:
        gwi_ref, refs = refs[0], refs[1:]
    else:
        gwi_ref, gwo_ref, refs = refs[0], refs[1], refs[2:]
    small_ref, gib_ref, hid_ref, slope_ref, n2_ref, r2_ref, a2b_ref, acc_ref, df_ref, bias_ref, *refs = refs
    step = pl.program_id(0)
    width = acc_ref.shape[1]

    if comm:
        mi_ref, mo_ref, ci_ref, co_ref, send_ref, recv_ref = refs
        wide = ci_ref.shape[-1]
        here = place()
        c = here[1]

        def chunk_copies(j):
            at = pl.ds(pl.multiple_of(j * width, width), width)
            return [
                remote(mi_ref.at[:, :, at], ci_ref.at[:, :, at], send_ref.at[0, j], recv_ref.at[0, j], ("core",), here),
                remote(mo_ref.at[j], co_ref.at[j], send_ref.at[1, j], recv_ref.at[1, j], ("core",), here),
            ]

    @pl.when(step == 0)
    def _():
        if comm:
            greet([("core",)])
        wide = bfi_ref[...].astype(F32)
        for i in range(count):
            bias_ref[i : i + 1] = wide[None, i * width : (i + 1) * width]
        n1, _ = normed(h1_ref[...])
        a1 = n1 * line(g1_ref) + line(s1_ref)
        h2 = a1 + nn(cc_ref[...], wco_ref[...]) + line(bco_ref)
        n2, r2 = normed(h2)
        n2_ref[...] = n2
        r2_ref[...] = jnp.broadcast_to(r2, r2_ref.shape)
        a2 = n2 * line(g2_ref) + line(s2_ref)
        a2b_ref[...] = a2.astype(BF16)
        acc_ref[...] = a2 + line(bfo_ref)

    piece = 2 * PAIR
    pieces = [slice(i, i + piece) for i in range(0, width, piece)]

    @pl.when(step < count)
    def _():
        def product(at):
            return nn(a2b_ref[...], wi_ref[:, at])

        bias = bias_ref[pl.ds(step, 1)]
        ready = product(pieces[0])
        more = 0.0
        for i, at in enumerate(pieces):
            u = ready + bias[:, at]
            if i + 1 < len(pieces):
                ready = product(pieces[i + 1])
            cumul = 0.5 * (1.0 + lax.erf(u * 0.7071067811865476))
            density = jnp.exp(-0.5 * u * u) * 0.3989422804014327
            hid = (u * cumul).astype(BF16)
            hid_ref[step, :, at] = hid
            slope_ref[step, :, at] = cumul + u * density
            more = more + nn(hid, wo_ref[at])
        acc_ref[...] += more

    @pl.when(step == count - 1)
    def _():
        n3, r3 = normed(acc_ref[...])
        gain = line(g3_ref)
        out_ref[...] = (n3 * gain + line(s3_ref)).astype(BF16)
        e = ct_ref[...].astype(F32)
        d3 = norm_back(e, n3, r3, gain)
        df = d3.astype(BF16)
        df_ref[...] = df
        acc_ref[...] = d3
        small_ref[0:1] = total(e * n3)
        small_ref[1:2] = total(e)
        small_ref[2:3] = total(df)

    @pl.when(jnp.logical_and(step >= count, step < 2 * count))
    def _():
        j = step - count
        df = df_ref[...]

        def product(at):
            return nt(df, wo_ref[at])

        ready = product(pieces[0])
        more, go, gi, sums = 0.0, [], [], []
        for i, at in enumerate(pieces):
            du = (ready * slope_ref[j, :, at]).astype(BF16)
            if i + 1 < len(pieces):
                ready = product(pieces[i + 1])
            go.append(tn(hid_ref[j, :, at], df).astype(BF16))
            more = more + nt(du, wi_ref[:, at])
            gi.append(tn(a2b_ref[...], du).astype(BF16))
            sums.append(tn(du, jnp.ones((du.shape[0], PAIR), BF16)))
        acc_ref[...] += more
        go, gi, sums = (jnp.concatenate(a, axis=n) for a, n in ((go, 0), (gi, 1), (sums, 0)))
        quarter = width // gib_ref.shape[0]
        if gib_ref.shape[0] == 4:
            lane = lax.broadcasted_iota(jnp.int32, (quarter // 4, PAIR), 1)
            for i in range(4):
                part = sum(
                    jnp.where(lane == 17 + n, sums[(4 * i + n) * quarter // 4 : (4 * i + n + 1) * quarter // 4], 0.0)
                    for n in range(4)
                )
                gib_ref[i] = part
        else:
            gib_ref[0] = jnp.transpose(sums)[:1]
        if comm:
            at = pl.ds(pl.multiple_of(j * width, width), width)
            eight, narrow = gwi_ref.shape[:2]
            gi = gi.reshape(eight, 2, narrow, width)
            go = go.reshape(2, 2, 4, narrow, width)
            gwi_ref[:, :, at] = jnp.where(c == 0, gi[:, 0], gi[:, 1])
            mi_ref[:, :, at] = jnp.where(c == 0, gi[:, 1], gi[:, 0])
            mo_ref[j] = jnp.where(c == 0, go[:, 1], go[:, 0])
            for i in range(4):
                gwi_ref[pl.ds(2 * j, 2), :, pl.ds(wide + i * width, width)] = jnp.where(c == 0, go[:, 0, i], go[:, 1, i])
            for copy in chunk_copies(j):
                copy.start()
        else:
            gwo_ref[...] = go
            gwi_ref[...] = gi

    @pl.when(step == 2 * count)
    def _():
        d2 = acc_ref[...]
        n2 = n2_ref[...]
        dh2 = norm_back(d2, n2, r2_ref[:, :1], line(g2_ref))
        dh2_ref[...] = dh2
        dco = dh2.astype(BF16)
        dcc_ref[...] = nt(dco, wco_ref[...]).astype(BF16)
        gco_ref[...] = tn(cc_ref[...], dco).astype(BF16)
        small_ref[3:4] = total(d2 * n2)
        small_ref[4:5] = total(d2)
        small_ref[5:6] = total(dco)
        small_ref[6:8] = jnp.zeros((2, d2.shape[1]), F32)

    if comm:

        @pl.when(step > count)
        def _():
            j = step - count - 1
            at = pl.ds(pl.multiple_of(j * width, width), width)
            for copy in chunk_copies(j):
                copy.wait()
            gwi_ref[:, :, at] += ci_ref[:, :, at]
            for i in range(4):
                gwi_ref[pl.ds(2 * j, 2), :, pl.ds(wide + i * width, width)] += co_ref[j, :, i]


def feed(size, comm, h1, cc, ct, wco, wi, wo, vectors):
    rows, width = h1.shape
    wide = wi.shape[1]
    chunk = width
    count = wide // chunk

    def weight(s):
        return jnp.where(s < count, s, jnp.minimum(s - count, count - 1))

    def early(s):
        return jnp.clip(s - count, 0, count - 1)

    flat = whole((rows, width))
    square = whole((width, width))
    scratch = [
        pltpu.VMEM((count, rows, chunk), BF16),
        pltpu.VMEM((count, rows, chunk), F32),
        pltpu.VMEM((rows, width), F32),
        pltpu.VMEM((rows, 128), F32),
        pltpu.VMEM((rows, width), BF16),
        pltpu.VMEM((rows, width), F32),
        pltpu.VMEM((rows, width), BF16),
        pltpu.VMEM((8, width), F32),
    ]
    if comm:
        narrow = width // size
        gib_shape = jax.ShapeDtypeStruct((size, narrow, PAIR), F32)
        gib_spec = pl.BlockSpec((4, narrow, PAIR), lambda s: (early(s), 0, 0))
        grad_specs = [whole((size // 2, narrow, 2 * wide))]
        grad_shapes = [(size // 2, narrow, 2 * wide)]
        scratch += [
            pltpu.VMEM((size // 2, narrow, wide), BF16),
            pltpu.VMEM((count, 2, 4, narrow, width), BF16),
            pltpu.VMEM((size // 2, narrow, wide), BF16),
            pltpu.VMEM((count, 2, 4, narrow, width), BF16),
            pltpu.SemaphoreType.DMA((2, count)),
            pltpu.SemaphoreType.DMA((2, count)),
        ]
    else:
        gib_shape = jax.ShapeDtypeStruct((count, 1, width), F32)
        gib_spec = pl.BlockSpec((1, 1, chunk), lambda s: (early(s), 0, 0))
        grad_specs = [
            pl.BlockSpec((width, chunk), lambda s: (0, early(s))),
            pl.BlockSpec((chunk, width), lambda s: (early(s), 0)),
        ]
        grad_shapes = [(width, wide), (wide, width)]
    return pl.pallas_call(
        functools.partial(feed_kernel, count, comm),
        grid=(2 * count + 1,),
        in_specs=[
            flat, flat, flat, square,
            pl.BlockSpec((width, chunk), lambda s: (0, weight(s))),
            pl.BlockSpec((chunk, width), lambda s: (weight(s), 0)),
        ]
        + [whole(v.shape) for v in vectors],
        out_specs=[flat, flat, flat, square]
        + grad_specs
        + [whole((8, width)), gib_spec],
        out_shape=[
            jax.ShapeDtypeStruct((rows, width), BF16),
            jax.ShapeDtypeStruct((rows, width), F32),
            jax.ShapeDtypeStruct((rows, width), BF16),
            jax.ShapeDtypeStruct((width, width), BF16),
        ]
        + [jax.ShapeDtypeStruct(a, BF16) for a in grad_shapes]
        + [
            jax.ShapeDtypeStruct((8, width), F32),
            gib_shape,
        ],
        scratch_shapes=scratch,
        compiler_params=params(2 if comm else None),
        cost_estimate=cost(
            12 * rows * width * wide + 6 * rows * width * width, 12 * width * wide + 16 * rows * width
        ),
        name="feed",
    )(h1, cc, ct, wco, wi, wo, *vectors)


def outputs_kernel(moves, count, line, *refs):
    pieces, rest = refs[:count], refs[count:]
    out_ref, dx_ref, dm_ref = rest[:3]
    outs = rest[3:]
    for piece, first, wide, which, row, col in moves:
        ref = pieces[piece]
        outs[which][row : row + ref.shape[0], col : col + wide] = ref[:, first : first + wide].astype(F32)
    turned, result, dx, dm = outs[-4:]
    turned[...] = jnp.transpose(pieces[line[0]][:, line[1] : line[1] + PAIR].astype(F32))
    result[...] = out_ref[...]
    dx[...] = dx_ref[...]
    dm[...] = dm_ref[...]


def outputs(pieces, moves, line, shapes, out, dx, dm):
    ins = tuple(pieces) + (out, dx, dm)
    result = jax.ShapeDtypeStruct(out.shape, BF16)
    return pl.pallas_call(
        functools.partial(outputs_kernel, moves, len(pieces), line),
        out_shape=[jax.ShapeDtypeStruct(a, F32) for a in shapes]
        + [jax.ShapeDtypeStruct((PAIR, pieces[0].shape[0]), F32), result, result, result],
        compiler_params=params(),
        cost_estimate=cost(0, 12 << 20),
        name="outputs",
    )(*ins)


def moved(pieces, targets):
    out = []
    for n, (start, wide) in enumerate(pieces):
        for first, cols, which, row, col in targets:
            low, high = max(start, first), min(start + wide, first + cols)
            if low < high:
                out.append((n, low - start, high - low, which, row, col + low - first))
    return out


def schedule_of(flows, kernel):
    entries = [
        (start, order, name, start, stop)
        for order, name in enumerate(flows)
        for start, stop in PLAN[name][kernel]
    ]
    return tuple(([flows[name]], start, stop) for _, _, name, start, stop in sorted(entries))


def swap_sum(part, axis, pairs):
    came = lax.ppermute(part, axis, pairs)
    return part.astype(F32) + came.astype(F32)


def sum_scatter(grad, size, order):
    rows, cols = grad.shape
    bits = size.bit_length() - 1
    me = lax.axis_index("dp")
    now = grad.reshape((2,) * bits + (rows // size, cols))
    left = list(range(bits))[::-1]
    for bit in [b for b in order if b < bits] + [b for b in range(bits) if b not in order]:
        axis = left.index(bit)
        mine = (me >> bit) & 1
        keep = lax.dynamic_index_in_dim(now, mine, axis, keepdims=False)
        send = lax.dynamic_index_in_dim(now, 1 - mine, axis, keepdims=False)
        came = lax.ppermute(send, "dp", [(i, i ^ (1 << bit)) for i in range(size)])
        now = (keep.astype(F32) + came.astype(F32)).astype(BF16)
        left.pop(axis)
    return swap_sum(now, "sp", [(0, 1), (1, 0)])


def per_device(
    size,
    inputs,
    memory,
    target_docs,
    memory_docs,
    cotangent,
    w_qkv,
    b_q,
    b_v,
    w_so,
    b_so,
    g_one,
    s_one,
    w_cq,
    b_cq,
    w_ckv,
    b_cv,
    w_co,
    b_co,
    g_two,
    s_two,
    w_fi,
    b_fi,
    w_fo,
    b_fo,
    g_three,
    s_three,
):
    rows, width = inputs.shape[1:]
    wide = b_fi.shape[0]
    comm = size == 16
    narrow, broad = width // size, wide // size
    x, mem, ct = inputs[0], memory[0], cotangent[0]
    qkv, mkv, kvo, mkvo, cq, ctx, cc, h1, x_o, mem_o, x, mem, ct, lse, clse, t_oth, m_oth, t_own, m_own = front(
        x, mem, ct, target_docs, memory_docs, w_qkv, w_ckv, w_so, w_cq, (b_q, b_v, b_cv, b_so, g_one, s_one, b_cq)
    )
    output, dh2, dcc, gco, gwi, *gwo, small_a, gib = feed(
        size, comm, h1, cc, ct, w_co, w_fi, w_fo,
        (g_one, s_one, b_co, g_two, s_two, b_fo, g_three, s_three, b_fi),
    )
    gib = gib.reshape(width, PAIR) if comm else gib.reshape(1, wide)

    block = (2, 2, 2, 2, narrow) if comm else (width,)
    at_cross, at_self, flows = (), (), {}
    if comm:
        late_shape = block + (2 * width,)
        sources = {
            "T0": (gwi.reshape(block[:3] + gwi.shape[1:]), block[:3] + gwi.shape[1:], BLOCK[:3]),
            "T1a": (("ref", MIDDLE), block + (3 * width,), BLOCK),
            "T1b": (None, late_shape, BLOCK),
            "G": (("ref", GRADS), block + (3 * width + PAIR,), BLOCK),
        }
        for name, (source, cols, hops, _, _) in PLAN.items():
            array, shape, dims = sources[source]
            flows[name] = Flow(array, shape, hops, dims, cols)
        at_cross = schedule_of(flows, 3)
        at_self = schedule_of(flows, 4)
    dm, dmo, gcvb, dh1, dsc, late, small_b, *early = cross_backward(
        block, cq, mkv, mkvo, dcc, cc, clse, t_own, m_own, m_oth, mem, mem_o, w_ckv,
        gco, dh2, h1, ctx, w_cq, w_so, g_one, s_one, at_cross,
    )
    for name, flow in flows.items():
        if PLAN[name][0] == "T1b":
            flow.array = late
    derivative, grad_memory, output, *made = self_backward(
        block, qkv, kvo, dsc, ctx, lse, t_own, t_oth, x, x_o, w_qkv, dh1, (small_a, small_b, gcvb, gib), dm, dmo, output, at_self
    )
    if comm:
        targets = {
            "T0": [(0, wide, 2, 0, 0)] + [(wide + i * width, width, 3, i * narrow, 0) for i in range(4)],
            "T1a": [(0, width, 4, 0, 0), (width, 2 * width, 1, 0, 0)],
            "T1b": [(0, width, 5, 0, 0), (width, width, 6, 0, 0)],
            "G": [
                ((3 * pair + i) * PAIR, PAIR, 0, 0, i * width + pair * PAIR)
                for pair in range(width // PAIR)
                for i in range(3)
            ],
        }
        moves, line = [], None
        for n, (source, cols, *_) in enumerate(PLAN.values()):
            moves += [(n,) + m[1:] for m in moved([cols], targets[source])]
            if source == "G" and cols[0] <= 3 * width < sum(cols):
                line = n, 3 * width - cols[0]
        shapes = [(narrow, 3 * width), (narrow, 2 * width), (narrow, wide), (broad, width)] + [(narrow, width)] * 3
        t_qkv, t_cmem, t_fin, t_fout, t_cout, t_cquery, t_out, lines, output, derivative, grad_memory = outputs(
            [f.array for f in flows.values()], moves, line, shapes, output, derivative, grad_memory
        )
    else:
        (early,), (made,) = early, made
        columns = made[:, 3 * width : 3 * width + PAIR]
        gqkv = made[:, : 3 * width].reshape(width, -1, 3, PAIR).swapaxes(1, 2).reshape(width, 3 * width)
        t_fin, t_fout, t_cout, t_cquery, t_out, t_cmem, t_qkv, lines = (
            sum_scatter(g, size, (0, 1, 2, 3))
            for g in (
                gwi, gwo[0], early[:, :width], late[:, :width], late[:, width:], early[:, width:], gqkv, columns
            )
        )
        lines = lines.T
    t_gthree, t_sthree, t_fobias, t_gtwo, t_stwo, t_cobias = (lines[i] for i in range(6))
    t_cqbias, t_gone, t_sone, t_obias = (lines[i] for i in range(8, 12))
    t_cvbias, t_qbias, t_vbias = lines[16], lines[21], lines[22]
    if comm:
        t_fibias = lines[17:21].reshape(-1)
    else:
        t_fibias = lax.psum(lax.psum_scatter(gib[0], "dp", scatter_dimension=0, tiled=True), "sp")
    return (
        output[None],
        derivative[None],
        grad_memory[None],
        t_qkv,
        t_qbias,
        t_vbias,
        t_out,
        t_obias,
        t_gone,
        t_sone,
        t_cquery,
        t_cqbias,
        t_cmem,
        t_cvbias,
        t_cout,
        t_cobias,
        t_gtwo,
        t_stwo,
        t_fin,
        t_fibias,
        t_fout,
        t_fobias,
        t_gthree,
        t_sthree,
    )


def solution(mesh):
    split = P("dp", "sp", None)
    in_specs = (split, split, P("dp", "sp"), P("dp", "sp"), split) + (P(),) * 21
    matrix, vector = P("dp", None), P("dp")
    out_specs = (
        split, split, split,
        matrix, vector, vector,
        matrix, vector, vector, vector,
        matrix, vector,
        matrix, vector,
        matrix, vector, vector, vector,
        matrix, vector,
        matrix, vector, vector, vector,
    )
    return jax.shard_map(
        functools.partial(per_device, mesh.shape["dp"]),
        mesh=mesh, in_specs=in_specs, out_specs=out_specs, check_vma=False,
    )
```

```python
import functools

import jax
import jax.numpy as jnp
from jax import lax
from jax.experimental import pallas as pl
from jax.experimental.pallas import tpu as pltpu
from jax.sharding import PartitionSpec as P

HD = 64
PAIR = 2 * HD
EPS = 1e-05
FAR = 1.0e9
VMEM = 60 * 1024 * 1024
F32 = jnp.float32
BF16 = jnp.bfloat16


def nn(a, b):
    return lax.dot_general(a, b, (((1,), (0,)), ((), ())), preferred_element_type=F32)


def nt(a, b):
    return lax.dot_general(a, b, (((1,), (1,)), ((), ())), preferred_element_type=F32)


def tn(a, b):
    return lax.dot_general(a, b, (((0,), (0,)), ((), ())), preferred_element_type=F32)


def params(collective=None):
    if collective is None:
        return pltpu.CompilerParams(vmem_limit_bytes=VMEM)
    return pltpu.CompilerParams(
        vmem_limit_bytes=VMEM, collective_id=collective, has_side_effects=True
    )


def cost(flops, moved):
    return pl.CostEstimate(flops=int(flops), bytes_accessed=int(moved), transcendentals=0)


def normed(h):
    centred = h - jnp.mean(h, axis=-1, keepdims=True)
    rstd = lax.rsqrt(jnp.mean(centred * centred, axis=-1, keepdims=True) + EPS)
    return centred * rstd, rstd


def norm_back(grad, n, rstd, gain):
    scaled = grad * gain
    centre = jnp.mean(scaled, axis=-1, keepdims=True)
    along = jnp.mean(scaled * n, axis=-1, keepdims=True)
    return rstd * (scaled - centre - n * along)


def total(a):
    return jnp.sum(a.astype(F32), axis=0, keepdims=True)


def place():
    me = lax.axis_index("dp")
    return me, me % 2, (me // 2) % 2, me // 4, lax.axis_index("sp")


def flipped(at, hops):
    me, c, x, z, sp = at
    for hop in hops:
        if hop == "core":
            me, c = me + 1 - 2 * c, 1 - c
        elif hop == "x":
            me, x = me + 2 - 4 * x, 1 - x
        elif hop == "z1":
            me, z = me + 4 - 8 * (z % 2), z + 1 - 2 * (z % 2)
        elif hop == "z2":
            me, z = me + 8 - 16 * (z // 2), z + 2 - 4 * (z // 2)
        else:
            sp = 1 - sp
    return me, c, x, z, sp


def partner(hops, at=None):
    there = flipped(at or place(), hops)
    return {"dp": there[0], "sp": there[4]}


def greet(groups, at=None):
    groups = sorted({tuple("y" if h[0] == "y" else h for h in hops) for hops in groups})
    barrier = pltpu.get_barrier_semaphore()
    for hops in groups:
        pl.semaphore_signal(barrier, inc=1, device_id=partner(hops, at), device_id_type=pl.DeviceIdType.MESH)
    pl.semaphore_wait(barrier, len(groups))


def remote(src, dst, send, recv, hops, at=None):
    return pltpu.make_async_remote_copy(
        src_ref=src, dst_ref=dst, send_sem=send, recv_sem=recv,
        device_id=partner(hops, at), device_id_type=pl.DeviceIdType.MESH,
    )


PLAN = {
    "T0i_0": ("T0i", (0, 1536), ("z1", "x", "yr", "z2", "yg"), ((0, 5), (5, 7)), ((0, 3), (3, 5), (5, 7))),
    "T0i_1": ("T0i", (1536, 1536), ("x", "z1", "z2", "y"), ((0, 5), (5, 7)), ((0, 2), (2, 5))),
    "T0o_0": ("T0o", (3072, 1024), ("x", "z1", "z2", "y"), ((0, 3), (3, 5), (5, 6)), (), ((6, 9),)),
    "T0o_1": ("T0o", (4096, 1024), ("yr", "x", "z1", "z2", "yg"), ((0, 4), (4, 6), (6, 7)), ((0, 2),), ((6, 9),)),
    "T0o_2": ("T0o", (5120, 1024), ("z1", "x", "z2", "y"), ((0, 4), (4, 6), (6, 7)), (), ((6, 9),)),
    "T1a_0": ("T1a", (0, 1536), ("core", "z1", "x", "z2", "y"), ((6, 7),), ((0, 6), (6, 8), (8, 14), (14, 25))),
    "T1a_1": ("T1a", (1536, 768), ("core", "x", "z1", "z2", "y"), ((6, 7),), ((0, 2), (2, 5), (5, 7), (7, 9))),
    "T1b_0": ("T1b", (0, 1536), ("core", "x", "z1", "z2", "y"), (), ((0, 2), (2, 6), (6, 8), (8, 14), (14, 25))),
    "G1_0": ("G", (0, 768), ("core", "yr", "x", "z1", "z2", "yg"), (), ((5, 6), (6, 9), (9, 11), (11, 16), (16, 20), (20, 24))),
    "G2_0": ("G", (768, 768), ("core", "yr", "x", "z1", "z2", "yg"), (), ((7, 8), (8, 12), (12, 17), (17, 21), (21, 26), (26, 29))),
    "G3_0": ("G", (1536, 384), ("core", "z1", "x", "z2", "y"), (), ((8, 9), (9, 15), (15, 19), (19, 23), (23, 28))),
    "G4_0": ("G", (1920, 512), ("core", "x", "z1", "z2", "y"), (), ((9, 10), (10, 13), (13, 18), (18, 22), (22, 27))),
}
BLOCK = ("z2", "z1", "x", "core")


class Part:
    def __init__(self, hop, shape, dims, cols=None):
        self.hops = hops = hop if isinstance(hop, tuple) else (hop,)
        self.groups = [(h,) for h in hops] + ([hops] if len(hops) > 1 else [])
        self.dims = dims
        self.cols = cols or (0, shape[-1])
        self.shape = shape = tuple(shape[:-1]) + (self.cols[1],)
        for h in hops:
            if h in dims:
                at = dims.index(h)
                shape, dims = shape[:at] + shape[at + 1 :], dims[:at] + dims[at + 1 :]
            elif h != "y":
                shape = shape[:-1] + (shape[-1] // 2 if h == "yr" else 2 * shape[-1],)
        self.after, self.left = shape, dims
        self.came = self.shape if hops == ("yg",) else shape

    def share(self, at):
        _, c, x, z, sp = at
        first, wide = self.cols
        index = [slice(None)] * (len(self.shape) - 1) + [pl.ds(first, wide)]
        for h in self.hops:
            if h in self.dims:
                index[self.dims.index(h)] = {"core": c, "x": x, "z1": z % 2, "z2": z // 2}[h]
            elif h == "yr":
                half = wide // 2
                index[-1] = pl.ds(pl.multiple_of(first + sp * half, 128), half)
        return tuple(index)

    def copies(self, src, held, made, came, send, recv, local, at):
        out = [
            remote(src.at[self.share(flipped(at, g))], came[i], send.at[i], recv.at[i], g, at)
            for i, g in enumerate(self.groups)
        ]
        if not held:
            to = made.at[self.part_of(at[4])] if self.hops == ("yg",) else made
            out.append(pltpu.make_async_copy(src.at[self.share(at)], to, local))
        return out

    def part_of(self, sp):
        wide = self.shape[-1]
        return (slice(None),) * (len(self.shape) - 1) + (pl.ds(pl.multiple_of(sp * wide, 128), wide),)

    def add(self, src, held, made, came, at):
        if self.hops == ("yg",):
            if held:
                made[self.part_of(at[4])] = src[self.share(at)]
            made[self.part_of(1 - at[4])] = came[0][...]
        elif len(came) > 1:
            mine = src[self.share(at)] if held else made[...]
            one, two, three = (c[...].astype(F32) for c in came)
            made[...] = ((mine.astype(F32) + one) + (two + three)).astype(BF16)
        elif held:
            made[...] = src[self.share(at)] + came[0][...]
        else:
            made[...] += came[0][...]


class Flow:
    def __init__(self, array, shape, hops, dims=BLOCK, cols=None):
        self.array, self.shape, self.dims, self.cols = array, tuple(shape), dims, cols
        self.hops = list(hops)

    def step(self):
        part = Part(self.hops.pop(0), self.shape, self.dims, self.cols)
        self.shape, self.dims, self.cols = part.after, part.left, None
        return part


class Window:
    def __init__(self, start, stop, joint):
        self.start, self.stop, self.joint = start, stop, joint
        self.parts, self.sources, self.keeps = [], [], []


class Joint:
    def __init__(self):
        self.window = None


def plan(schedule):
    windows, arrays, latest = [], [], {}
    for n, (flows, start, stop, *joint) in enumerate(schedule):
        window = Window(start, stop, bool(joint))
        if joint:
            joint[0].window = n
        for i, flow in enumerate(flows):
            if flow in latest:
                source = ("part",) + latest[flow]
                before = windows[latest[flow][0]]
                before.keeps[latest[flow][1]] = False
            elif isinstance(flow.array, Joint):
                source = ("joint", flow.array.window)
            elif isinstance(flow.array, tuple):
                source = flow.array
            else:
                known = [k for k, a in enumerate(arrays) if a is flow.array]
                if not known:
                    arrays.append(flow.array)
                source = ("in", known[0] if known else len(arrays) - 1)
            window.parts.append(flow.step())
            window.sources.append(source)
            window.keeps.append(not joint)
            if not joint:
                latest[flow] = (n, i)
        windows.append(window)
    return windows, arrays, latest


def carrying(body, own, windows, arrays, grid, also, finale):
    ins, outs, held = own

    def kernel(*refs):
        refs = list(refs)

        def take(n):
            got = refs[:n]
            del refs[:n]
            return got

        my_in, arr = take(ins), take(arrays)
        my_out = take(outs)
        given = [[take(1)[0] if k else None for k in w.keeps] for w in windows]
        my_held = take(held)
        made, came, joints = [], [], []
        for w, g in zip(windows, given):
            if w.joint:
                joint, col, views = take(1)[0], 0, []
                for q in w.parts:
                    views.append(joint.at[(slice(None),) * (len(q.after) - 1) + (pl.ds(col, q.after[-1]),)])
                    col += q.after[-1]
                joints.append(joint)
                made.append(views)
            else:
                joints.append(None)
                made.append([ref if ref is not None else take(1)[0] for ref in g])
            came.append([take(len(q.groups)) for q in w.parts])
        mine = my_in + my_out + my_held
        step = pl.program_id(0)
        groups = [g for w in windows for q in w.parts for g in q.groups] + list(also)
        if groups:
            here = place()
            pl.when(step == 0)(lambda: greet(groups, here))
        if windows:
            send, recv, local = refs
        copies, sources, base = [], [], 0
        for w, m, c in zip(windows, made, came):
            now, froms = [], []
            for i, q in enumerate(w.parts):
                kind = w.sources[i]
                if kind[0] == "in":
                    src = arr[kind[1]]
                elif kind[0] == "ref":
                    src = mine[kind[1]]
                elif kind[0] == "joint":
                    src = joints[kind[1]]
                else:
                    src = made[kind[1]][kind[2]]
                held_here = kind[0] != "in"
                froms.append((src, held_here))
                now += q.copies(
                    src, held_here, m[i], c[i], send.at[base], recv.at[base], local.at[base], here
                )
                base += 1
            copies.append(now)
            sources.append(froms)

        def phase(number):
            for n, w in enumerate(windows):
                if w.stop == number:
                    for copy in copies[n]:
                        copy.wait()
                    for q, (src, held_here), m, c in zip(w.parts, sources[n], made[n], came[n]):
                        q.add(src, held_here, m, c, here)
            for n, w in enumerate(windows):
                if w.start == number:
                    for copy in copies[n]:
                        copy.start()

        used = sorted({w.start for w in windows} | {w.stop for w in windows})
        for number in used:
            if number < grid:
                pl.when(step == number)(functools.partial(phase, number))
        body(*mine)
        for number in used:
            if number >= grid:
                pl.when(step == grid - 1)(functools.partial(phase, number))
        if finale:
            pl.when(step == grid - 1)(lambda: finale(*mine))

    return kernel


def run(
    body, name, grid, ins, in_specs, outs, out_specs, held=(), schedule=(), collective=None,
    flops=0, moved=0, also=(), finale=None,
):
    in_specs, outs, out_specs, held = list(in_specs), list(outs), list(out_specs), list(held)
    windows, arrays, latest = plan(schedule)
    own = len(outs)
    kernel = carrying(body, (len(ins), own, len(held)), windows, len(arrays), grid, also, finale)
    in_specs += [pl.BlockSpec(memory_space=pl.ANY)] * len(arrays)
    order, count = [], 0
    for n, w in enumerate(windows):
        if w.joint:
            shape = w.parts[0].after[:-1] + (sum(q.after[-1] for q in w.parts),)
            held.append(pltpu.VMEM(shape, BF16))
        for i, (q, k) in enumerate(zip(w.parts, w.keeps)):
            if w.joint:
                continue
            if k:
                outs.append(jax.ShapeDtypeStruct(q.after, BF16))
                out_specs.append(whole(q.after))
                order.append((n, i))
            else:
                held.append(pltpu.VMEM(q.after, BF16))
        held += [pltpu.VMEM(q.came, BF16) for q in w.parts for _ in q.groups]
        count += len(w.parts)
    if windows:
        held += [pltpu.SemaphoreType.DMA((count, 3))] * 2 + [pltpu.SemaphoreType.DMA((count,))]
    results = pl.pallas_call(
        kernel,
        grid=(grid,),
        in_specs=in_specs,
        out_specs=out_specs,
        out_shape=outs,
        scratch_shapes=held,
        compiler_params=params(collective if windows or also else None),
        cost_estimate=cost(flops, moved),
        name=name,
    )(*ins, *arrays)
    for flow, where in latest.items():
        flow.array = results[own + order.index(where)]
    return results[:own]


def head_masks(dtype):
    lane = lax.broadcasted_iota(jnp.int32, (1, PAIR), 1)
    low = jnp.where(lane < HD, 1.0, 0.0)
    return low.astype(dtype), (1.0 - low).astype(dtype)


def query_code(code):
    lane = lax.broadcasted_iota(jnp.int32, code.shape, 1)
    return jnp.where(lane < 4, (code.astype(F32) - 1.0) * FAR, 0.0).astype(BF16)


def masked(s, diagonal):
    low, high = s[:-diagonal], s[-diagonal:]
    row = lax.broadcasted_iota(jnp.int32, high.shape, 0)
    col = lax.broadcasted_iota(jnp.int32, high.shape, 1)
    high = jnp.where(row <= col, high, -FAR)
    return jnp.concatenate([low, high], axis=0) if low.shape[0] else high


def softmax_over(jobs):
    results = []
    ready = nt(jobs[0][0], jobs[0][2])
    for n, (_, values_t, _, diagonal) in enumerate(jobs):
        s = ready
        if n + 1 < len(jobs):
            ready = nt(jobs[n + 1][0], jobs[n + 1][2])
        if diagonal:
            s = masked(s, diagonal)
        peak = jnp.max(s, axis=0, keepdims=True)
        e = jnp.exp(s - peak)
        norm = jnp.sum(e, axis=0, keepdims=True)
        results.append((nn(values_t, e.astype(BF16)) / norm, peak + jnp.log(norm)))
    return results


def pair_spec(rows, offset):
    return pl.BlockSpec((rows, PAIR), lambda p: (0, p + offset))


def whole(shape):
    return pl.BlockSpec(shape, lambda *_: (0,) * len(shape))


def delta_rows(g, o):
    prod = g.astype(F32) * o.astype(F32)
    upper = prod.astype(BF16)
    lower = (prod - upper.astype(F32)).astype(BF16)
    row = lax.broadcasted_iota(jnp.int32, (8, PAIR), 0)
    lane = lax.broadcasted_iota(jnp.int32, (8, PAIR), 1)
    pick = jnp.where(row == lane // HD, 1.0, 0.0).astype(BF16)
    return nt(pick, upper) + nt(pick, lower)


def back_pieces(jobs):
    def products(job):
        keys, values, q, g = job[:4]
        return nt(keys, q), nt(values, g)

    ready = products(jobs[0])
    for n, (_, _, _, _, lse, delta, causal) in enumerate(jobs):
        s, dp = ready
        if n + 1 < len(jobs):
            ready = products(jobs[n + 1])
        if causal:
            s = masked(s, s.shape[0])
        p = jnp.exp(s - lse)
        yield n, p.astype(BF16), (p * (dp - delta)).astype(BF16)


def cross_backward_kernel(
    size, pairs, q_ref, k_ref, v_ref, ko_ref, vo_ref, g_ref, o_ref, lse_ref, t_ref, own_ref, oth_ref,
    m_ref, mo_ref, wk_ref, wv_ref, gco_hbm, dh2_hbm, h1_hbm, ctx_hbm, wcq_hbm, wso_hbm, g1_ref, s1_ref,
    dm_out, dmo_out, gb_ref, dh1_ref, dsc_ref, late_ref, small_ref, grad_ref,
    dm_ref, dmo_acc, mt_ref, mot_ref, dcq_ref, dmo_ref, gco_ref, dh2_ref, h1_ref, ctx_ref, wcq_ref, wso_ref, move_ref,
):
    step = pl.program_id(0)
    rows, width = m_ref.shape
    lead = (slice(None),) * (len(grad_ref.shape) - 1)

    loads = [
        pltpu.make_async_copy(src, dst, move_ref.at[i])
        for i, (src, dst) in enumerate(
            (
                (gco_hbm, gco_ref), (dh2_hbm, dh2_ref), (h1_hbm, h1_ref), (ctx_hbm, ctx_ref), (wcq_hbm, wcq_ref),
                (wso_hbm, wso_ref),
            )
        )
    ]
    gives = [
        pltpu.make_async_copy(src, dst, move_ref.at[6 + i])
        for i, (src, dst) in enumerate(((dm_ref, dm_out), (dmo_ref, dmo_out)))
    ]

    def put(ref, col, grad):
        to = pl.ds(pl.multiple_of(col, PAIR), grad.shape[1])
        ref[lead + (to,)] = grad.astype(BF16).reshape(ref.shape[:-1] + (grad.shape[1],))

    @pl.when(step == 0)
    def _():
        for copy in loads:
            copy.start()
        mt_ref[...] = jnp.transpose(m_ref[...])
        mot_ref[...] = jnp.transpose(mo_ref[...])
        dm_ref[...] = jnp.zeros(dm_ref.shape, F32)
        dmo_acc[...] = jnp.zeros(dmo_acc.shape, F32)

    @pl.when(step == 1)
    def _():
        loads[0].wait()
        put(grad_ref, 0, gco_ref[...])

    @pl.when(step < pairs)
    def _():
        count = rows // size
        cols = pl.ds(pl.multiple_of(step * PAIR, PAIR), PAIR)
        sides = [(k_ref, v_ref, own_ref, mt_ref, dm_ref), (ko_ref, vo_ref, oth_ref, mot_ref, dmo_acc)]
        blocks = list(backward_pieces(size, q_ref, g_ref, o_ref, lse_ref, t_ref))
        weights = jnp.concatenate([wk_ref[...], wv_ref[...]], axis=1)
        jobs, where, turned = [], [], []
        for side, (kr, vr, code, _, _) in enumerate(sides):
            keys = jnp.concatenate([kr[...], code[...]], axis=1)
            turned.append(jnp.transpose(kr[...]))
            for block, head, qm, gm, q, lse, delta in blocks:
                jobs.append((keys, vr[...], q, gm, lse, delta, False))
                where.append((side, block, head, qm, gm))
        dq = [[0.0, 0.0] for _ in range(count)]
        dk, dv = [0.0, 0.0], [0.0, 0.0]
        grad = gb = 0.0
        for n, p, ds in back_pieces(jobs):
            side, block, head, qm, gm = where[n]
            dk[side] = dk[side] + nn(ds, qm)
            dv[side] = dv[side] + nn(p, gm)
            dq[block][head] = dq[block][head] + nn(turned[side][head * HD : (head + 1) * HD], ds)
            if n + 1 == len(jobs) or where[n + 1][0] != side:
                both = jnp.concatenate([dk[side].astype(BF16), dv[side].astype(BF16)], axis=1)
                mem, acc = sides[side][3:]
                grad = grad + nn(mem[...], both)
                gb = gb + total(both[:, PAIR:])
                acc[...] += nt(both, weights)
        for block in range(count):
            dcq_ref[block * size : (block + 1) * size, cols] = upright(dq[block]).astype(BF16)
        put(grad_ref, width + step * PAIR, grad[:, :PAIR])
        put(grad_ref, 2 * width + step * PAIR, grad[:, PAIR:])
        gb_ref[:, cols] = gb

    @pl.when(step == pairs)
    def _():
        dmo_ref[...] = dmo_acc[...].astype(BF16)
        for copy in gives:
            copy.start()
        for copy in loads[1:]:
            copy.wait()
        gain = line(g1_ref)
        n1, r1 = normed(h1_ref[...])
        a1b = (n1 * gain + line(s1_ref)).astype(BF16)
        dcq = dcq_ref[...]
        d1 = dh2_ref[...] + nt(dcq, wcq_ref[...])
        dh1 = norm_back(d1, n1, r1, gain)
        dh1_ref[...] = dh1
        dso = dh1.astype(BF16)
        dsc_ref[...] = nt(dso, wso_ref[...]).astype(BF16)
        put(late_ref, 0, tn(a1b, dcq))
        put(late_ref, width, tn(ctx_ref[...], dso))
        small_ref[0:1] = total(dcq)
        small_ref[1:2] = total(d1 * n1)
        small_ref[2:3] = total(d1)
        small_ref[3:4] = total(dso)
        small_ref[4:8] = jnp.zeros((4, width), F32)
        for copy in gives:
            copy.wait()


MIDDLE = 30


def cross_backward(block, cq, kv, kvo, g, o, lse, t, own, oth, m, mo, w, gco, dh2, h1, ctx, wcq, wso, gain, shift, schedule):
    rows, width = cq.shape
    pairs = width // PAIR

    def pair_of(size, offset):
        return pl.BlockSpec((size, PAIR), lambda s: (0, jnp.minimum(s, pairs - 1) + offset))

    flat, square = whole((rows, width)), whole((width, width))
    outs = [
        jax.ShapeDtypeStruct((rows, width), F32),
        jax.ShapeDtypeStruct((rows, width), BF16),
        jax.ShapeDtypeStruct((1, width), F32),
        jax.ShapeDtypeStruct((rows, width), F32),
        jax.ShapeDtypeStruct((rows, width), BF16),
        jax.ShapeDtypeStruct(block + (2 * width,), BF16),
        jax.ShapeDtypeStruct((8, width), F32),
    ]
    far = pl.BlockSpec(memory_space=pl.ANY)
    specs = [far, far, whole((1, width)), flat, flat, whole(block + (2 * width,)), whole((8, width))]
    held = []
    if schedule:
        held.append(pltpu.VMEM(block + (3 * width,), BF16))
    else:
        outs.append(jax.ShapeDtypeStruct(block + (3 * width,), BF16))
        specs.append(whole(block + (3 * width,)))
    held += [
        pltpu.VMEM((rows, width), F32),
        pltpu.VMEM((rows, width), F32),
        pltpu.VMEM((width, rows), BF16),
        pltpu.VMEM((width, rows), BF16),
        pltpu.VMEM((rows, width), BF16),
        pltpu.VMEM((rows, width), BF16),
    ]
    held += [pltpu.VMEM(a.shape, a.dtype) for a in (gco, dh2, h1, ctx, wcq, wso)] + [pltpu.SemaphoreType.DMA((8,))]
    return run(
        functools.partial(cross_backward_kernel, 256, pairs), "cross_backward", pairs + 1,
        (cq, kv, kv, kvo, kvo, g, o, lse, t, own, oth, m, mo, w, w, gco, dh2, h1, ctx, wcq, wso, gain, shift),
        [
            pair_of(rows, 0), pair_of(rows, 0), pair_of(rows, pairs), pair_of(rows, 0), pair_of(rows, pairs),
            pair_of(rows, 0), pair_of(rows, 0),
            pl.BlockSpec((8, rows), lambda s: (jnp.minimum(s, pairs - 1), 0)),
            whole((rows, 128)), whole((rows, 128)), whole((rows, 128)), flat, flat,
            pair_of(width, 0), pair_of(width, pairs),
            far, far, far, far, far, far, whole(gain.shape), whole(shift.shape),
        ],
        outs, specs, held, schedule, 3,
        64 * rows * rows * width + 24 * rows * width * width, 40 * rows * width,
    )


def upright(heads):
    return jnp.transpose(jnp.concatenate(heads, axis=0) * HD**-0.5)


def backward_pieces(size, q_ref, g_ref, o_ref, lse_ref, own_ref):
    masks = head_masks(BF16)
    scale = BF16(HD**-0.5)
    qcode = query_code(own_ref[...])
    delta = delta_rows(g_ref[...], o_ref[...])
    for block in range(q_ref.shape[0] // size):
        at = slice(block * size, (block + 1) * size)
        for head, mask in enumerate(masks):
            qm = q_ref[at] * (mask * scale)
            gm = g_ref[at] * mask
            q = jnp.concatenate([qm, qcode[at]], axis=1)
            yield block, head, qm, gm, q, lse_ref[head : head + 1, at], delta[head : head + 1, at]


def self_backward_kernel(
    size, *refs,
):
    (q2_ref, ko_ref, vo_ref, g2_ref, o2_ref, lse2_ref, wk2_ref, wv2_ref,
     q_ref, k_ref, v_ref, g_ref, o_ref, lse_ref, wq_ref, wk_ref, wv_ref,
     own_ref, oth_ref, x_ref, xo_ref, dh1_ref, sa_ref, sb_ref, sc_ref, sd_ref, dm_hbm, dmo_hbm, out_hbm,
     dx_out, dm_out, out_out, grad_ref,
     dq_acc, dx_acc, dxo_acc, dkv_acc, xt_ref, xot_ref, dxo_ref, came_ref, memory_ref, dm_ref, gm_ref, dx_ref, turn_ref,
     send_ref, recv_ref) = refs
    step = pl.program_id(0)
    second = lax.axis_index("dp") % 2 == 1
    rows, width = x_ref.shape
    pairs = width // PAIR
    early = pairs // 2
    count = rows // size
    over = remote(dxo_ref, came_ref, send_ref.at[0], recv_ref.at[0], ("core",))
    m_over = remote(dmo_hbm, memory_ref, send_ref.at[1], recv_ref.at[1], ("core",))
    dm_load = pltpu.make_async_copy(dm_hbm, dm_ref, send_ref.at[5])

    @pl.when(step == 0)
    def _():
        m_over.start()
        dm_load.start()
        Swap(out_hbm, out_out, send_ref.at[2], recv_ref.at[2]).start()
        xt_ref[...] = jnp.transpose(x_ref[...])
        turn_ref[...] = jnp.zeros(turn_ref.shape, F32)
        turn_ref[0:8] = sa_ref[...]
        turn_ref[8:16] = sb_ref[...]
        turn_ref[16:17] = sc_ref[...]
        dx_acc[...] = dh1_ref[...]

    @pl.when(jnp.logical_and(step == 0, second))
    def _():
        xot_ref[...] = jnp.transpose(xo_ref[...])
        dxo_acc[...] = jnp.zeros(dxo_acc.shape, F32)

    @pl.when(jnp.logical_and(step == 0, jnp.logical_not(second)))
    def _():
        dq_acc[...] = jnp.zeros(dq_acc.shape, F32)
        dkv_acc[...] = jnp.zeros(dkv_acc.shape, BF16)
        xot_ref[...] = jnp.zeros(xot_ref.shape, BF16)

    @pl.when(jnp.logical_and(step < early, second))
    def _():
        jobs, where, turned = [], [], []
        for two in range(2):
            at = slice(two * PAIR, (two + 1) * PAIR)
            keys = jnp.concatenate([ko_ref[:, at], oth_ref[...]], axis=1)
            turned.append(jnp.transpose(ko_ref[:, at]))
            stats = lse2_ref.at[8 * two : 8 * two + 8]
            for block, head, qm, gm, q, lse, delta in backward_pieces(
                size, q2_ref.at[:, at], g2_ref.at[:, at], o2_ref.at[:, at], stats, own_ref
            ):
                jobs.append((keys, vo_ref[:, at], q, gm, lse, delta, False))
                where.append((two, block, head, qm, gm))
        dk, dv = [0.0, 0.0], [0.0, 0.0]
        for n, p, ds in back_pieces(jobs):
            two, block, head, qm, gm = where[n]
            dk[two] = dk[two] + nn(ds, qm)
            dv[two] = dv[two] + nn(p, gm)
            of_head = slice(head * HD, (head + 1) * HD)
            dq_acc[2 * step + two, of_head, block * size : (block + 1) * size] = nn(turned[two][of_head], ds)
        for two in range(2):
            at = slice(two * PAIR, (two + 1) * PAIR)
            both = jnp.concatenate([dk[two].astype(BF16), dv[two].astype(BF16)], axis=1)
            dkv_acc[2 * step + two] = both
            dxo_acc[...] += nt(both, jnp.concatenate([wk2_ref[:, at], wv2_ref[:, at]], axis=1))

    @pl.when(jnp.logical_and(step == early - 1, second))
    def _():
        dxo_ref[...] = dxo_acc[...].astype(BF16)
        over.start()

    @pl.when(step == early)
    def _():
        m_over.wait()
        dm_load.wait()
        gm_ref[...] = (dm_ref[...] + memory_ref[...].astype(F32)).astype(BF16)
        Swap(gm_ref, dm_out, send_ref.at[3], recv_ref.at[3]).start()

    @pl.when(step >= early)
    def _():
        pair = step - early
        cols = pl.ds(pl.multiple_of(pair * PAIR, PAIR), PAIR)
        dkvo = dkv_acc[pair]
        grad_o = nn(xot_ref[...], dkvo)
        turned = jnp.transpose(k_ref[...])
        dq = [[0.0, 0.0] for _ in range(count)]
        dk, dv = [0.0] * count, [0.0] * count
        jobs, where = [], []
        keys = jnp.concatenate([k_ref[...], own_ref[...]], axis=1)
        for block, head, qm, gm, q, lse, delta in backward_pieces(size, q_ref, g_ref, o_ref, lse_ref, own_ref):
            for part in range(block + 1):
                of = slice(part * size, (part + 1) * size)
                jobs.append((keys[of], v_ref[of], q, gm, lse, delta, part == block))
                where.append((block, part, head, qm, gm))
        for n, p, ds in back_pieces(jobs):
            block, part, head, qm, gm = where[n]
            of = slice(part * size, (part + 1) * size)
            dk[part] = dk[part] + nn(ds, qm)
            dv[part] = dv[part] + nn(p, gm)
            dq[block][head] = dq[block][head] + nn(turned[head * HD : (head + 1) * HD, of], ds)
        dk, dv = (jnp.concatenate(a, axis=0).astype(BF16) for a in (dk, dv))
        before = dq_acc[pair]
        dq = jnp.concatenate(
            [
                upright(
                    [
                        part + before[head * HD : (head + 1) * HD, block * size : (block + 1) * size]
                        for head, part in enumerate(parts)
                    ]
                )
                for block, parts in enumerate(dq)
            ],
            axis=0,
        ).astype(BF16)
        dkv = jnp.concatenate([dk, dv], axis=1)
        grad_kv = nn(xt_ref[...], dkv) + grad_o
        grad_q = nn(xt_ref[...], dq)
        dx_acc[...] += nt(dkv, jnp.concatenate([wk_ref[...], wv_ref[...]], axis=1)) + nt(dq, wq_ref[...])
        lead = (slice(None),) * (len(grad_ref.shape) - 1)
        for n, grad in enumerate((grad_q, grad_kv[:, :PAIR], grad_kv[:, PAIR:])):
            to = pl.ds(pl.multiple_of((pair * 3 + n) * PAIR, PAIR), PAIR)
            grad_ref[lead + (to,)] = grad.astype(BF16).reshape(grad_ref.shape[:-1] + (PAIR,))
        turn_ref[21:22, cols] = total(dq)
        turn_ref[22:23, cols] = total(dv) + total(dkvo[:, PAIR:])

    @pl.when(step == early + pairs - 1)
    def _():
        shape = grad_ref.shape[:-1] + (PAIR,)
        lead = (slice(None),) * (len(shape) - 1)
        columns = jnp.transpose(turn_ref[...])
        if sd_ref.shape == columns.shape:
            columns = columns + sd_ref[...]
        grad_ref[lead + (slice(3 * width, 3 * width + PAIR),)] = columns.astype(BF16).reshape(shape)

        @pl.when(second)
        def _():
            over.wait_send()
            dx_ref[...] = dx_acc[...].astype(BF16)

        @pl.when(jnp.logical_not(second))
        def _():
            over.wait_recv()
            dx_ref[...] = (dx_acc[...] + came_ref[...].astype(F32)).astype(BF16)

        Swap(dx_ref, dx_out, send_ref.at[4], recv_ref.at[4]).start()


def self_backward_finale(*refs):
    out_hbm, dx_out, dm_out, out_out = refs[28:32]
    gm_ref, dx_ref, _, send_ref, recv_ref = refs[43:48]
    Swap(out_hbm, out_out, send_ref.at[2], recv_ref.at[2]).wait()
    Swap(gm_ref, dm_out, send_ref.at[3], recv_ref.at[3]).wait()
    Swap(dx_ref, dx_out, send_ref.at[4], recv_ref.at[4]).wait()


GRADS = 32


def self_backward(block, qkv, kvo, g, o, lse, own, oth, x, xo, w, dh1, small, dm, dmo, out, schedule):
    rows, width = x.shape
    pairs = width // PAIR
    early = pairs // 2

    def two_of(size, offset):
        return pl.BlockSpec((size, 2 * PAIR), lambda s: (0, jnp.minimum(s, early - 1) + offset))

    def pair_of(size, offset):
        return pl.BlockSpec((size, PAIR), lambda s: (0, jnp.maximum(s - early, 0) + offset))

    made = block + (3 * width + PAIR,)
    far = pl.BlockSpec(memory_space=pl.ANY)
    outs = [jax.ShapeDtypeStruct((rows, width), BF16)] * 3
    specs = [far] * 3
    held = []
    if schedule:
        held += [pltpu.VMEM(made, BF16)]
    else:
        outs += [jax.ShapeDtypeStruct(made, BF16)]
        specs += [whole(made)]
    held += [
        pltpu.VMEM((pairs, PAIR, rows), F32),
        pltpu.VMEM((rows, width), F32),
        pltpu.VMEM((rows, width), F32),
        pltpu.VMEM((pairs, rows, 2 * PAIR), BF16),
        pltpu.VMEM((width, rows), BF16),
        pltpu.VMEM((width, rows), BF16),
        pltpu.VMEM((rows, width), BF16),
        pltpu.VMEM((rows, width), BF16),
        pltpu.VMEM((rows, width), BF16),
        pltpu.VMEM((rows, width), F32),
        pltpu.VMEM((rows, width), BF16),
        pltpu.VMEM((rows, width), BF16),
        pltpu.VMEM((PAIR, width), F32),
        pltpu.SemaphoreType.DMA((6,)),
        pltpu.SemaphoreType.DMA((5,)),
    ]
    return run(
        functools.partial(self_backward_kernel, 256), "self_backward", early + pairs,
        (qkv, kvo, kvo, g, o, lse, w, w, qkv, qkv, qkv, g, o, lse, w, w, w, own, oth, x, xo, dh1) + tuple(small) + (dm, dmo, out),
        [
            two_of(rows, 0), two_of(rows, 0), two_of(rows, early), two_of(rows, 0), two_of(rows, 0),
            pl.BlockSpec((16, rows), lambda s: (jnp.minimum(s, early - 1), 0)),
            two_of(width, early), two_of(width, 2 * early),
            pair_of(rows, 0), pair_of(rows, pairs), pair_of(rows, 2 * pairs), pair_of(rows, 0), pair_of(rows, 0),
            pl.BlockSpec((8, rows), lambda s: (jnp.maximum(s - early, 0), 0)),
            pair_of(width, 0), pair_of(width, pairs), pair_of(width, 2 * pairs),
            whole((rows, 128)), whole((rows, 128)), whole((rows, width)), whole((rows, width)), whole((rows, width)),
        ] + [whole(a.shape) for a in small] + [far] * 3,
        outs, specs, held, schedule, 5,
        48 * rows * rows * width + 20 * rows * width * width, 12 * width * width + 40 * rows * width,
        (("core",), ("core", "y")), self_backward_finale,
    )


def code_of(docs_ref):
    row = lax.broadcasted_iota(jnp.int32, (PAIR, docs_ref.shape[1]), 0)
    return jnp.transpose(jnp.where(docs_ref[...] == row, 1.0, 0.0)).astype(BF16)


def line(ref):
    return ref[...].astype(F32)[None, :]


def moving():
    return lax.axis_index("dp") % 2 != lax.axis_index("sp")


class Swap:
    def __init__(self, src, dst, send, recv):
        self.there = remote(src, dst, send, recv, ("core", "y"))
        self.here = pltpu.make_async_copy(src, dst, recv)

    def start(self):
        pl.when(moving())(self.there.start)
        pl.when(jnp.logical_not(moving()))(self.here.start)

    def wait_recv(self):
        pl.when(moving())(self.there.wait_recv)
        pl.when(jnp.logical_not(moving()))(self.here.wait)

    def wait_send(self):
        pl.when(moving())(self.there.wait_send)

    def wait(self):
        self.wait_send()
        self.wait_recv()


def front_kernel(
    size, x_hbm, m_hbm, c_hbm, td_hbm, md_hbm, wx_hbm, wm_hbm, wo_hbm, wq_hbm,
    bq_ref, bv_ref, bcv_ref, bso_ref, g_ref, s_ref, bcq_ref,
    qkv_out, mkv_out, kvo_out, mkvo_out, cq_out, ctx_out, cc_out, h_out, xo_out, mo_out, x_out, m_out, c_out,
    lse_ref, clse_ref, tt_ref, mt_ref, to_ref, mo_ref,
    x_ref, m_ref, wx_ref, wm_ref, wo_ref, wq_ref, xc_ref, mc_ref, td_ref, md_ref, tdc_ref, mdc_ref,
    qkv_ref, mkv_ref, kvo_ref, mkvo_ref, cq_ref, ctx_ref, cc_ref, h_ref, acc_ref,
    load_ref, store_ref, send_ref, recv_ref,
):
    rows, width = x_ref.shape
    pairs = width // PAIR
    second = lax.axis_index("dp") % 2 == 1
    first = jnp.logical_not(second)
    masks = head_masks(BF16)
    scale = BF16(HD**-0.5)
    loads = [
        pltpu.make_async_copy(src, dst, load_ref.at[i])
        for i, (src, dst) in enumerate(((wx_hbm, wx_ref), (wm_hbm, wm_ref), (wo_hbm, wo_ref), (wq_hbm, wq_ref)))
    ]
    give = [
        pltpu.make_async_copy(src, dst, store_ref.at[i])
        for i, (src, dst) in enumerate(
            (
                (qkv_ref, qkv_out), (mkv_ref, mkv_out), (mkvo_ref, mkvo_out), (cq_ref, cq_out), (ctx_ref, ctx_out),
                (cc_ref, cc_out), (h_ref, h_out), (mc_ref, mo_out), (x_ref, x_out), (m_ref, m_out),
                (kvo_ref, kvo_out), (xc_ref, xo_out),
            )
        )
    ]
    swaps = [
        Swap(src, dst, send_ref.at[i], recv_ref.at[i])
        for i, (src, dst) in enumerate(
            ((td_hbm, td_ref), (md_hbm, md_ref), (m_hbm, m_ref), (c_hbm, c_out))
            + tuple((x_hbm.at[at], x_ref.at[at]) for at in (pl.ds(0, rows // 2), pl.ds(rows // 2, rows // 2)))
        )
    ]
    x_over = remote(x_ref, xc_ref, send_ref.at[6], recv_ref.at[6], ("core",))
    m_over = remote(m_ref, mc_ref, send_ref.at[7], recv_ref.at[7], ("core",))
    docs = [
        remote(td_ref, tdc_ref, send_ref.at[8], recv_ref.at[8], ("core",)),
        remote(md_ref, mdc_ref, send_ref.at[9], recv_ref.at[9], ("core",)),
    ]
    for copy in loads:
        copy.start()
    greet([("core", "y"), ("core",)])
    for copy in swaps[:2] + swaps[4:]:
        copy.start()

    def columns(offset, pair):
        return pl.ds(pl.multiple_of(offset + pair * PAIR, PAIR), PAIR)

    def heads(source, offset, pair, code, block):
        at = slice(block * size, (block + 1) * size)
        q = source[at, columns(offset, pair)]
        return [jnp.concatenate([q * (mask * scale), code[at]], axis=1) for mask in masks]

    def keep(block, pair, outs, lses, lse_out, out):
        at = slice(block * size, (block + 1) * size)
        mixed = jnp.concatenate(outs, axis=0)
        acc_ref[pair, :, at] = mixed
        out[at, columns(0, pair)] = jnp.transpose(mixed).astype(BF16)
        row = lax.broadcasted_iota(jnp.int32, (8, size), 0)
        lse_out[pl.ds(pl.multiple_of(pair * 8, 8), 8), at] = jnp.where(row == 0, lses[0], lses[1])

    def begin(block, pair, results, lse_out, out):
        keep(block, pair, [r for r, _ in results], [lse for _, lse in results], lse_out, out)

    def merge(block, pair, results, lse_out, out):
        at = slice(block * size, (block + 1) * size)
        stats = lse_out[pl.ds(pl.multiple_of(pair * 8, 8), 8), at]
        outs, lses = [], []
        for head, (r, lse) in enumerate(results):
            before = acc_ref[pair, head * HD : (head + 1) * HD, at]
            old = stats[head : head + 1]
            peak = jnp.maximum(old, lse)
            both = peak + jnp.log(jnp.exp(old - peak) + jnp.exp(lse - peak))
            outs.append(before * jnp.exp(old - both) + r * jnp.exp(lse - both))
            lses.append(both)
        keep(block, pair, outs, lses, lse_out, out)

    def halves(values):
        turned = jnp.transpose(values)
        return turned[:HD], turned[HD:]

    for copy in swaps[:2]:
        copy.wait_recv()
    for copy in docs:
        copy.start()
    to_ref[...] = code_of(td_ref)
    mo_ref[...] = code_of(md_ref)
    loads[0].wait()
    for half, copy in enumerate(swaps[4:]):
        copy.wait()
        at = slice(half * rows // 2, (half + 1) * rows // 2)
        if half:
            swaps[2].start()
            pl.when(first)(x_over.start)
            give[8].start()
        for n, bias in enumerate((line(bq_ref), 0.0, line(bv_ref))):
            cols = slice(n * width, (n + 1) * width)
            qkv_ref[at, cols] = (nn(x_ref[at], wx_ref[:, cols]) + bias).astype(BF16)
    give[0].start()

    def attend(query, keys_ref, key_at, value_at, key_code, diagonal, finish, stats, out):
        @pl.loop(0, pairs // 3)
        def _(third):
            code = query_code(to_ref[...])
            jobs, where = [], []
            for pair in (3 * third, 3 * third + 1, 3 * third + 2):
                keys = jnp.concatenate([keys_ref[:, columns(key_at, pair)], key_code[...]], axis=1)
                values = halves(keys_ref[:, columns(value_at, pair)])
                for block in range(rows // size):
                    end = (block + 1) * size if diagonal else rows
                    for q, v in zip(heads(query, 0, pair, code, block), values):
                        jobs.append((keys[:end], v[:, :end], q, size if diagonal else 0))
                    where.append((block, pair))
            results = softmax_over(jobs)
            for n, (block, pair) in enumerate(where):
                finish(block, pair, results[2 * n : 2 * n + 2], stats, out)

    attend(qkv_ref, qkv_ref, width, 2 * width, to_ref, True, begin, lse_ref, ctx_ref)

    for copy in docs:
        copy.wait()
    tt_ref[...] = code_of(tdc_ref)
    mt_ref[...] = code_of(mdc_ref)
    swaps[2].wait()
    m_over.start()
    swaps[3].start()
    give[9].start()
    pl.when(first)(x_over.wait_send)

    @pl.when(second)
    def _():
        x_over.wait_recv()
        give[11].start()
        for n, bias in enumerate((0.0, line(bv_ref))):
            cols = slice(n * width, (n + 1) * width)
            from_cols = slice((n + 1) * width, (n + 2) * width)
            kvo_ref[:, cols] = (nn(xc_ref[...], wx_ref[:, from_cols]) + bias).astype(BF16)
        give[10].start()

        attend(qkv_ref, kvo_ref, 0, width, tt_ref, False, merge, lse_ref, ctx_ref)

    give[4].start()
    loads[2].wait()
    loads[3].wait()
    h = x_ref[...].astype(F32) + nn(ctx_ref[...], wo_ref[...]) + line(bso_ref)
    h_ref[...] = h
    n, _ = normed(h)
    a = (n * line(g_ref) + line(s_ref)).astype(BF16)
    cq_ref[...] = (nn(a, wq_ref[...]) + line(bcq_ref)).astype(BF16)
    give[6].start()
    give[3].start()

    loads[1].wait()
    for n, bias in enumerate((0.0, line(bcv_ref))):
        cols = slice(n * width, (n + 1) * width)
        mkv_ref[:, cols] = (nn(m_ref[...], wm_ref[:, cols]) + bias).astype(BF16)
    give[1].start()
    attend(cq_ref, mkv_ref, 0, width, mo_ref, False, begin, clse_ref, cc_ref)
    m_over.wait()
    give[7].start()
    for n, bias in enumerate((0.0, line(bcv_ref))):
        cols = slice(n * width, (n + 1) * width)
        mkvo_ref[:, cols] = (nn(mc_ref[...], wm_ref[:, cols]) + bias).astype(BF16)
    give[2].start()
    attend(cq_ref, mkvo_ref, 0, width, mt_ref, False, merge, clse_ref, cc_ref)
    give[5].start()
    for copy in give[:10]:
        copy.wait()
    for copy in swaps[:2]:
        copy.wait_send()
    swaps[3].wait()

    @pl.when(second)
    def _():
        give[10].wait()
        give[11].wait()


def front(x, mem, ct, td, md, wx, wm, wo, wq, vectors):
    rows, width = x.shape
    pairs = width // PAIR

    def flat(n):
        return jax.ShapeDtypeStruct((rows, n * width), BF16)

    stats = jax.ShapeDtypeStruct((8 * pairs, rows), F32)
    code = jax.ShapeDtypeStruct((rows, PAIR), BF16)
    far = pl.BlockSpec(memory_space=pl.ANY)
    near = pl.BlockSpec(memory_space=pltpu.VMEM)
    tall = jax.ShapeDtypeStruct((rows, width), F32)
    held = [flat(3), flat(2), flat(2), flat(2), flat(1), flat(1), flat(1), tall]
    return pl.pallas_call(
        functools.partial(front_kernel, 256),
        in_specs=[far] * 9 + [near] * len(vectors),
        out_specs=[far] * 13 + [near] * 6,
        out_shape=[flat(3), flat(2), flat(2), flat(2), flat(1), flat(1), flat(1), tall] + [flat(1)] * 5
        + [stats, stats, code, code, code, code],
        scratch_shapes=[pltpu.VMEM((rows, width), BF16)] * 2
        + [pltpu.VMEM(w.shape, BF16) for w in (wx, wm, wo, wq)]
        + [pltpu.VMEM((rows, width), BF16)] * 2
        + [pltpu.VMEM((1, rows), jnp.int32)] * 4
        + [pltpu.VMEM(a.shape, a.dtype) for a in held]
        + [
            pltpu.VMEM((pairs, PAIR, rows), F32),
            pltpu.SemaphoreType.DMA((4,)),
            pltpu.SemaphoreType.DMA((12,)),
            pltpu.SemaphoreType.DMA((10,)),
            pltpu.SemaphoreType.DMA((10,)),
        ],
        compiler_params=params(1),
        cost_estimate=cost(22 * rows * width * width + 36 * rows * rows * width, 60 * rows * width),
        name="front",
    )(x, mem, ct, td, md, wx, wm, wo, wq, *vectors)


def feed_kernel(
    count, comm, h1_ref, cc_ref, ct_ref, wco_ref, wi_ref, wo_ref,
    g1_ref, s1_ref, bco_ref, g2_ref, s2_ref, bfo_ref, g3_ref, s3_ref, bfi_ref, out_ref, dh2_ref, dcc_ref, gco_ref, *refs,
):
    if comm:
        gwi_ref, refs = refs[0], refs[1:]
    else:
        gwi_ref, gwo_ref, refs = refs[0], refs[1], refs[2:]
    small_ref, gib_ref, hid_ref, slope_ref, n2_ref, r2_ref, a2b_ref, acc_ref, df_ref, bias_ref, *refs = refs
    step = pl.program_id(0)
    width = acc_ref.shape[1]

    if comm:
        mi_ref, mo_ref, ci_ref, co_ref, send_ref, recv_ref = refs
        wide = ci_ref.shape[-1]
        here = place()
        c = here[1]

        def chunk_copies(j):
            at = pl.ds(pl.multiple_of(j * width, width), width)
            return remote(mi_ref.at[:, :, at], ci_ref.at[:, :, at], send_ref.at[0, j], recv_ref.at[0, j], ("core",), here)

        def block_copies(j):
            return remote(mo_ref.at[j], co_ref.at[j], send_ref.at[1, j], recv_ref.at[1, j], ("core",), here)

        def place_of(j, i):
            return (j // 2, j % 2, slice(None), slice(None), slice(wide + i * width, wide + (i + 1) * width))

    @pl.when(step == 0)
    def _():
        wide = bfi_ref[...].astype(F32)
        for i in range(count):
            bias_ref[i : i + 1] = wide[None, i * width : (i + 1) * width]
        n1, _ = normed(h1_ref[...])
        a1 = n1 * line(g1_ref) + line(s1_ref)
        h2 = a1 + nn(cc_ref[...], wco_ref[...]) + line(bco_ref)
        n2, r2 = normed(h2)
        n2_ref[...] = n2
        r2_ref[...] = jnp.broadcast_to(r2, r2_ref.shape)
        a2 = n2 * line(g2_ref) + line(s2_ref)
        a2b_ref[...] = a2.astype(BF16)
        acc_ref[...] = a2 + line(bfo_ref)

    piece = 2 * PAIR
    pieces = [slice(i, i + piece) for i in range(0, width, piece)]

    @pl.when(step < count)
    def _():
        def product(at):
            return nn(a2b_ref[...], wi_ref[:, at])

        bias = bias_ref[pl.ds(step, 1)]
        ready = product(pieces[0])
        more = 0.0
        for i, at in enumerate(pieces):
            u = ready + bias[:, at]
            if i + 1 < len(pieces):
                ready = product(pieces[i + 1])
            cumul = 0.5 * (1.0 + lax.erf(u * 0.7071067811865476))
            density = jnp.exp(-0.5 * u * u) * 0.3989422804014327
            hid = (u * cumul).astype(BF16)
            hid_ref[step, :, at] = hid
            slope_ref[step, :, at] = cumul + u * density
            more = more + nn(hid, wo_ref[at])
        acc_ref[...] += more

    @pl.when(step == count - 1)
    def _():
        n3, r3 = normed(acc_ref[...])
        gain = line(g3_ref)
        out_ref[...] = (n3 * gain + line(s3_ref)).astype(BF16)
        e = ct_ref[...].astype(F32)
        d3 = norm_back(e, n3, r3, gain)
        df = d3.astype(BF16)
        df_ref[...] = df
        acc_ref[...] = d3
        small_ref[0:1] = total(e * n3)
        small_ref[1:2] = total(e)
        small_ref[2:3] = total(df)

    @pl.when(jnp.logical_and(step >= count, step < 2 * count))
    def _():
        j = step - count
        df = df_ref[...]

        def product(at):
            return nt(df, wo_ref[at])

        ready = product(pieces[0])
        more, go, gi, sums = 0.0, [], [], []
        for i, at in enumerate(pieces):
            du = (ready * slope_ref[j, :, at]).astype(BF16)
            if i + 1 < len(pieces):
                ready = product(pieces[i + 1])
            if not comm:
                go.append(tn(hid_ref[j, :, at], df).astype(BF16))
            more = more + nt(du, wi_ref[:, at])
            gi.append(tn(a2b_ref[...], du).astype(BF16))
            sums.append(tn(du, jnp.ones((du.shape[0], PAIR), BF16)))
        acc_ref[...] += more
        gi, sums = jnp.concatenate(gi, axis=1), jnp.concatenate(sums, axis=0)
        quarter = width // gib_ref.shape[0]
        if gib_ref.shape[0] == 4:
            lane = lax.broadcasted_iota(jnp.int32, (quarter // 4, PAIR), 1)
            for i in range(4):
                part = sum(
                    jnp.where(lane == 17 + n, sums[(4 * i + n) * quarter // 4 : (4 * i + n + 1) * quarter // 4], 0.0)
                    for n in range(4)
                )
                gib_ref[i] = part
        else:
            gib_ref[0] = jnp.transpose(sums)[:1]
        if comm:
            at = pl.ds(pl.multiple_of(j * width, width), width)
            narrow = gwi_ref.shape[3]
            gi = gi.reshape(2, 2, 2, 2, narrow, width)
            gwi_ref[:, :, :, :, at] = jnp.where(c == 0, gi[:, :, :, 0], gi[:, :, :, 1])
            mi_ref[:, :, at] = jnp.where(c == 0, gi[:, :, :, 1], gi[:, :, :, 0]).reshape(8, narrow, width)
            chunk_copies(j).start()
        else:
            gwo_ref[...] = jnp.concatenate(go, axis=0)
            gwi_ref[...] = gi

    @pl.when(step == 2 * count)
    def _():
        d2 = acc_ref[...]
        n2 = n2_ref[...]
        dh2 = norm_back(d2, n2, r2_ref[:, :1], line(g2_ref))
        dh2_ref[...] = dh2
        dco = dh2.astype(BF16)
        dcc_ref[...] = nt(dco, wco_ref[...]).astype(BF16)
        gco_ref[...] = tn(cc_ref[...], dco).astype(BF16)
        small_ref[3:4] = total(d2 * n2)
        small_ref[4:5] = total(d2)
        small_ref[5:6] = total(dco)
        small_ref[6:8] = jnp.zeros((2, d2.shape[1]), F32)

    if comm:

        @pl.when(step == count)
        def _():
            narrow = gwi_ref.shape[3]
            for j in range(count):
                go = tn(hid_ref[j], df_ref[...]).astype(BF16).reshape(2, 2, 4, narrow, width)
                mo_ref[j] = jnp.where(c == 0, go[:, 1], go[:, 0])
                block_copies(j).start()
                for i in range(4):
                    gwi_ref[place_of(j, i)] = jnp.where(c == 0, go[:, 0, i], go[:, 1, i])

        @pl.when(step == count + 1)
        def _():
            for j in range(count):
                block_copies(j).wait()
                for i in range(4):
                    gwi_ref[place_of(j, i)] += co_ref[j, :, i]

        @pl.when(step > count)
        def _():
            j = step - count - 1
            at = pl.ds(pl.multiple_of(j * width, width), width)
            chunk_copies(j).wait()
            gwi_ref[:, :, :, :, at] += ci_ref[:, :, at].reshape(gwi_ref.shape[:-1] + (width,))


FEEDS = 19


def feed(size, comm, h1, cc, ct, wco, wi, wo, vectors, schedule):
    rows, width = h1.shape
    wide = wi.shape[1]
    chunk = width
    count = wide // chunk

    def weight(s):
        return jnp.where(s < count, s, jnp.minimum(s - count, count - 1))

    def early(s):
        return jnp.clip(s - count, 0, count - 1)

    flat = whole((rows, width))
    square = whole((width, width))
    scratch = [
        pltpu.VMEM((count, rows, chunk), BF16),
        pltpu.VMEM((count, rows, chunk), F32),
        pltpu.VMEM((rows, width), F32),
        pltpu.VMEM((rows, 128), F32),
        pltpu.VMEM((rows, width), BF16),
        pltpu.VMEM((rows, width), F32),
        pltpu.VMEM((rows, width), BF16),
        pltpu.VMEM((8, width), F32),
    ]
    if comm:
        narrow = width // size
        gib_shape = jax.ShapeDtypeStruct((size, narrow, PAIR), F32)
        gib_spec = pl.BlockSpec((4, narrow, PAIR), lambda s: (early(s), 0, 0))
        grad_specs = [whole((2, 2, 2, narrow, 2 * wide))]
        grad_shapes = [(2, 2, 2, narrow, 2 * wide)]
        scratch += [
            pltpu.VMEM((size // 2, narrow, wide), BF16),
            pltpu.VMEM((count, 2, 4, narrow, width), BF16),
            pltpu.VMEM((size // 2, narrow, wide), BF16),
            pltpu.VMEM((count, 2, 4, narrow, width), BF16),
            pltpu.SemaphoreType.DMA((2, count)),
            pltpu.SemaphoreType.DMA((2, count)),
        ]
    else:
        gib_shape = jax.ShapeDtypeStruct((count, 1, width), F32)
        gib_spec = pl.BlockSpec((1, 1, chunk), lambda s: (early(s), 0, 0))
        grad_specs = [
            pl.BlockSpec((width, chunk), lambda s: (0, early(s))),
            pl.BlockSpec((chunk, width), lambda s: (early(s), 0)),
        ]
        grad_shapes = [(width, wide), (wide, width)]
    return run(
        functools.partial(feed_kernel, count, comm), "feed", 2 * count + 1,
        (h1, cc, ct, wco, wi, wo) + tuple(vectors),
        [
            flat, flat, flat, square,
            pl.BlockSpec((width, chunk), lambda s: (0, weight(s))),
            pl.BlockSpec((chunk, width), lambda s: (weight(s), 0)),
        ]
        + [whole(v.shape) for v in vectors],
        [
            jax.ShapeDtypeStruct((rows, width), BF16),
            jax.ShapeDtypeStruct((rows, width), F32),
            jax.ShapeDtypeStruct((rows, width), BF16),
            jax.ShapeDtypeStruct((width, width), BF16),
        ]
        + [jax.ShapeDtypeStruct(a, BF16) for a in grad_shapes]
        + [jax.ShapeDtypeStruct((8, width), F32), gib_shape],
        [flat, flat, flat, square] + grad_specs + [whole((8, width)), gib_spec],
        scratch, schedule, 2,
        12 * rows * width * wide + 6 * rows * width * width, 12 * width * wide + 16 * rows * width,
        (("core",),) if comm else (),
    )


def outputs_kernel(moves, count, line, *refs):
    pieces, rest = refs[:count], refs[count:]
    out_ref, dx_ref, dm_ref = rest[:3]
    outs = rest[3:]
    for piece, first, wide, which, row, col in moves:
        ref = pieces[piece]
        outs[which][row : row + ref.shape[0], col : col + wide] = ref[:, first : first + wide].astype(F32)
    turned, result, dx, dm = outs[-4:]
    turned[...] = jnp.transpose(pieces[line[0]][:, line[1] : line[1] + PAIR].astype(F32))
    result[...] = out_ref[...]
    dx[...] = dx_ref[...]
    dm[...] = dm_ref[...]


def outputs(pieces, moves, line, shapes, out, dx, dm):
    ins = tuple(pieces) + (out, dx, dm)
    result = jax.ShapeDtypeStruct(out.shape, BF16)
    return pl.pallas_call(
        functools.partial(outputs_kernel, moves, len(pieces), line),
        out_shape=[jax.ShapeDtypeStruct(a, F32) for a in shapes]
        + [jax.ShapeDtypeStruct((PAIR, pieces[0].shape[0]), F32), result, result, result],
        compiler_params=params(),
        cost_estimate=cost(0, 12 << 20),
        name="outputs",
    )(*ins)


def moved(pieces, targets):
    out = []
    for n, (start, wide) in enumerate(pieces):
        for first, cols, which, row, col in targets:
            low, high = max(start, first), min(start + wide, first + cols)
            if low < high:
                out.append((n, low - start, high - low, which, row, col + low - first))
    return out


def schedule_of(flows, kernel):
    entries = [
        (start, order, name, start, stop)
        for order, name in enumerate(flows)
        for start, stop in (PLAN[name] + ((), (), ()))[kernel]
    ]
    return tuple(([flows[name]], start, stop) for _, _, name, start, stop in sorted(entries))


def swap_sum(part, axis, pairs):
    came = lax.ppermute(part, axis, pairs)
    return part.astype(F32) + came.astype(F32)


def sum_scatter(grad, size, order):
    rows, cols = grad.shape
    bits = size.bit_length() - 1
    me = lax.axis_index("dp")
    now = grad.reshape((2,) * bits + (rows // size, cols))
    left = list(range(bits))[::-1]
    for bit in [b for b in order if b < bits] + [b for b in range(bits) if b not in order]:
        axis = left.index(bit)
        mine = (me >> bit) & 1
        keep = lax.dynamic_index_in_dim(now, mine, axis, keepdims=False)
        send = lax.dynamic_index_in_dim(now, 1 - mine, axis, keepdims=False)
        came = lax.ppermute(send, "dp", [(i, i ^ (1 << bit)) for i in range(size)])
        now = (keep.astype(F32) + came.astype(F32)).astype(BF16)
        left.pop(axis)
    return swap_sum(now, "sp", [(0, 1), (1, 0)])


def per_device(
    size,
    inputs,
    memory,
    target_docs,
    memory_docs,
    cotangent,
    w_qkv,
    b_q,
    b_v,
    w_so,
    b_so,
    g_one,
    s_one,
    w_cq,
    b_cq,
    w_ckv,
    b_cv,
    w_co,
    b_co,
    g_two,
    s_two,
    w_fi,
    b_fi,
    w_fo,
    b_fo,
    g_three,
    s_three,
):
    rows, width = inputs.shape[1:]
    wide = b_fi.shape[0]
    comm = size == 16
    narrow, broad = width // size, wide // size
    x, mem, ct = inputs[0], memory[0], cotangent[0]
    qkv, mkv, kvo, mkvo, cq, ctx, cc, h1, x_o, mem_o, x, mem, ct, lse, clse, t_oth, m_oth, t_own, m_own = front(
        x, mem, ct, target_docs, memory_docs, w_qkv, w_ckv, w_so, w_cq, (b_q, b_v, b_cv, b_so, g_one, s_one, b_cq)
    )
    block = (2, 2, 2, 2, narrow) if comm else (width,)
    at_feed, at_cross, at_self, flows = (), (), (), {}
    if comm:
        joint = block[:3] + (narrow, 2 * wide)
        sources = {
            "T0i": (None, joint, BLOCK[:3]),
            "T0o": (("ref", FEEDS), joint, BLOCK[:3]),
            "T1a": (("ref", MIDDLE), block + (3 * width,), BLOCK),
            "T1b": (None, block + (2 * width,), BLOCK),
            "G": (("ref", GRADS), block + (3 * width + PAIR,), BLOCK),
        }
        for name, (source, cols, hops, *_) in PLAN.items():
            array, shape, dims = sources[source]
            flows[name] = Flow(array, shape, hops, dims, cols)
        at_feed = schedule_of(flows, 5)
    output, dh2, dcc, gco, gwi, *gwo, small_a, gib = feed(
        size, comm, h1, cc, ct, w_co, w_fi, w_fo,
        (g_one, s_one, b_co, g_two, s_two, b_fo, g_three, s_three, b_fi), at_feed,
    )
    for name, flow in flows.items():
        if PLAN[name][0] == "T0i":
            flow.array = gwi
    gib = gib.reshape(width, PAIR) if comm else gib.reshape(1, wide)

    if comm:
        at_cross = schedule_of(flows, 3)
        at_self = schedule_of(flows, 4)
    dm, dmo, gcvb, dh1, dsc, late, small_b, *early = cross_backward(
        block, cq, mkv, mkvo, dcc, cc, clse, t_own, m_own, m_oth, mem, mem_o, w_ckv,
        gco, dh2, h1, ctx, w_cq, w_so, g_one, s_one, at_cross,
    )
    for name, flow in flows.items():
        if PLAN[name][0] == "T1b":
            flow.array = late
    derivative, grad_memory, output, *made = self_backward(
        block, qkv, kvo, dsc, ctx, lse, t_own, t_oth, x, x_o, w_qkv, dh1, (small_a, small_b, gcvb, gib), dm, dmo, output, at_self
    )
    if comm:
        targets = {
            "T0i": [(0, wide, 2, 0, 0)],
            "T0o": [(wide + i * width, width, 3, i * narrow, 0) for i in range(4)],
            "T1a": [(0, width, 4, 0, 0), (width, 2 * width, 1, 0, 0)],
            "T1b": [(0, width, 5, 0, 0), (width, width, 6, 0, 0)],
            "G": [
                ((3 * pair + i) * PAIR, PAIR, 0, 0, i * width + pair * PAIR)
                for pair in range(width // PAIR)
                for i in range(3)
            ],
        }
        moves, line = [], None
        for n, (source, cols, *_) in enumerate(PLAN.values()):
            moves += [(n,) + m[1:] for m in moved([cols], targets[source])]
            if source == "G" and cols[0] <= 3 * width < sum(cols):
                line = n, 3 * width - cols[0]
        shapes = [(narrow, 3 * width), (narrow, 2 * width), (narrow, wide), (broad, width)] + [(narrow, width)] * 3
        t_qkv, t_cmem, t_fin, t_fout, t_cout, t_cquery, t_out, lines, output, derivative, grad_memory = outputs(
            [f.array for f in flows.values()], moves, line, shapes, output, derivative, grad_memory
        )
    else:
        (early,), (made,) = early, made
        columns = made[:, 3 * width : 3 * width + PAIR]
        gqkv = made[:, : 3 * width].reshape(width, -1, 3, PAIR).swapaxes(1, 2).reshape(width, 3 * width)
        t_fin, t_fout, t_cout, t_cquery, t_out, t_cmem, t_qkv, lines = (
            sum_scatter(g, size, (0, 1, 2, 3))
            for g in (
                gwi, gwo[0], early[:, :width], late[:, :width], late[:, width:], early[:, width:], gqkv, columns
            )
        )
        lines = lines.T
    t_gthree, t_sthree, t_fobias, t_gtwo, t_stwo, t_cobias = (lines[i] for i in range(6))
    t_cqbias, t_gone, t_sone, t_obias = (lines[i] for i in range(8, 12))
    t_cvbias, t_qbias, t_vbias = lines[16], lines[21], lines[22]
    if comm:
        t_fibias = lines[17:21].reshape(-1)
    else:
        t_fibias = lax.psum(lax.psum_scatter(gib[0], "dp", scatter_dimension=0, tiled=True), "sp")
    return (
        output[None],
        derivative[None],
        grad_memory[None],
        t_qkv,
        t_qbias,
        t_vbias,
        t_out,
        t_obias,
        t_gone,
        t_sone,
        t_cquery,
        t_cqbias,
        t_cmem,
        t_cvbias,
        t_cout,
        t_cobias,
        t_gtwo,
        t_stwo,
        t_fin,
        t_fibias,
        t_fout,
        t_fobias,
        t_gthree,
        t_sthree,
    )


def solution(mesh):
    split = P("dp", "sp", None)
    in_specs = (split, split, P("dp", "sp"), P("dp", "sp"), split) + (P(),) * 21
    matrix, vector = P("dp", None), P("dp")
    out_specs = (
        split, split, split,
        matrix, vector, vector,
        matrix, vector, vector, vector,
        matrix, vector,
        matrix, vector,
        matrix, vector, vector, vector,
        matrix, vector,
        matrix, vector, vector, vector,
    )
    return jax.shard_map(
        functools.partial(per_device, mesh.shape["dp"]),
        mesh=mesh, in_specs=in_specs, out_specs=out_specs, check_vma=False,
    )
```

```python
import functools

import jax
import jax.numpy as jnp
from jax import lax
from jax.experimental import pallas as pl
from jax.experimental.pallas import tpu as pltpu
from jax.sharding import PartitionSpec as P

HD = 64
PAIR = 2 * HD
EPS = 1e-05
FAR = 1.0e9
VMEM = 60 * 1024 * 1024
F32 = jnp.float32
BF16 = jnp.bfloat16


def nn(a, b):
    return lax.dot_general(a, b, (((1,), (0,)), ((), ())), preferred_element_type=F32)


def nt(a, b):
    return lax.dot_general(a, b, (((1,), (1,)), ((), ())), preferred_element_type=F32)


def tn(a, b):
    return lax.dot_general(a, b, (((0,), (0,)), ((), ())), preferred_element_type=F32)


def params(collective=None):
    if collective is None:
        return pltpu.CompilerParams(vmem_limit_bytes=VMEM)
    return pltpu.CompilerParams(
        vmem_limit_bytes=VMEM, collective_id=collective, has_side_effects=True
    )


def cost(flops, moved):
    return pl.CostEstimate(flops=int(flops), bytes_accessed=int(moved), transcendentals=0)


def normed(h):
    centred = h - jnp.mean(h, axis=-1, keepdims=True)
    rstd = lax.rsqrt(jnp.mean(centred * centred, axis=-1, keepdims=True) + EPS)
    return centred * rstd, rstd


def norm_back(grad, n, rstd, gain):
    scaled = grad * gain
    centre = jnp.mean(scaled, axis=-1, keepdims=True)
    along = jnp.mean(scaled * n, axis=-1, keepdims=True)
    return rstd * (scaled - centre - n * along)


def total(a):
    return jnp.sum(a.astype(F32), axis=0, keepdims=True)


def place():
    me = lax.axis_index("dp")
    return me, me % 2, (me // 2) % 2, me // 4, lax.axis_index("sp")


def flipped(at, hops):
    me, c, x, z, sp = at
    for hop in hops:
        if hop == "core":
            me, c = me + 1 - 2 * c, 1 - c
        elif hop == "x":
            me, x = me + 2 - 4 * x, 1 - x
        elif hop == "z1":
            me, z = me + 4 - 8 * (z % 2), z + 1 - 2 * (z % 2)
        elif hop == "z2":
            me, z = me + 8 - 16 * (z // 2), z + 2 - 4 * (z // 2)
        else:
            sp = 1 - sp
    return me, c, x, z, sp


def partner(hops, at=None):
    there = flipped(at or place(), hops)
    return {"dp": there[0], "sp": there[4]}


def greet(groups, at=None):
    groups = sorted({tuple("y" if h[0] == "y" else h for h in hops) for hops in groups})
    barrier = pltpu.get_barrier_semaphore()
    for hops in groups:
        pl.semaphore_signal(barrier, inc=1, device_id=partner(hops, at), device_id_type=pl.DeviceIdType.MESH)
    pl.semaphore_wait(barrier, len(groups))


def remote(src, dst, send, recv, hops, at=None):
    return pltpu.make_async_remote_copy(
        src_ref=src, dst_ref=dst, send_sem=send, recv_sem=recv,
        device_id=partner(hops, at), device_id_type=pl.DeviceIdType.MESH,
    )


PLAN = {
    "T0i_0": ("T0i", (0, 768), ("z1", "x", "yr", "z2", "yg"), ((0, 4), (4, 6), (6, 7)), ((0, 2), (2, 4))),
    "T0i_1": ("T0i", (768, 1024), ("z1", "x", "z2", "y"), ((0, 5), (5, 7)), ((0, 2), (2, 4))),
    "T0i_2": ("T0i", (1792, 1280), ("x", "z1", "yr", "z2", "yg"), ((0, 4), (4, 7)), ((0, 2), (2, 4), (4, 6))),
    "T0o_0": ("T0o", (3072, 512), ("x", "yr", "z1", "z2", "yg"), ((0, 2), (2, 4), (4, 5), (5, 6)), (), ((6, 9),)),
    "T0o_1": ("T0o", (3584, 512), ("yr", "x", "z1", "z2", "yg"), ((0, 2), (2, 4), (4, 5), (5, 6)), (), ((6, 9),)),
    "T0o_2": ("T0o", (4096, 512), ("z1", "yr", "x", "z2", "yg"), ((0, 2), (2, 3), (3, 4), (4, 5)), (), ((6, 9),)),
    "T0p_0": ("T0p", (4608, 1536), ("yr", "z1", "x", "z2", "yg"), ((0, 4), (4, 7)), ((0, 3), (3, 5), (5, 7))),
    "T1a_0": ("T1a", (0, 768), ("core", "x", "z1", "z2", "y"), ((6, 7),), ((0, 4), (4, 6), (6, 8), (8, 9))),
    "T1a_1": ("T1a", (768, 1536), ("core", "z1", "x", "z2", "y"), ((6, 7),), ((0, 6), (6, 9), (9, 14), (14, 18))),
    "T1b_0": ("T1b", (0, 1536), ("core", "x", "yr", "z1", "z2", "yg"), (), ((0, 2), (2, 6), (6, 9), (9, 14), (14, 17), (17, 19))),
    "G1_0": ("G", (0, 768), ("core", "z1", "yr", "x", "z2", "yg"), (), ((5, 6), (6, 9), (9, 12), (12, 14), (14, 16), (16, 17))),
    "G2_0": ("G", (768, 768), ("core", "x", "yr", "z1", "z2", "yg"), (), ((7, 8), (8, 11), (11, 15), (15, 17), (17, 19), (19, 20))),
    "G3_0": ("G", (1536, 384), ("core", "z1", "x", "z2", "y"), (), ((8, 9), (9, 14), (14, 16), (16, 18), (18, 19))),
    "G4_0": ("G", (1920, 512), ("core", "x", "z1", "z2", "y"), (), ((9, 10), (10, 13), (13, 16), (16, 18), (18, 20))),
}
BLOCK = ("z2", "z1", "x", "core")


class Part:
    def __init__(self, hop, shape, dims, cols=None):
        self.hops = hops = hop if isinstance(hop, tuple) else (hop,)
        self.groups = [(h,) for h in hops] + ([hops] if len(hops) > 1 else [])
        self.dims = dims
        self.cols = cols or (0, shape[-1])
        self.shape = shape = tuple(shape[:-1]) + (self.cols[1],)
        for h in hops:
            if h in dims:
                at = dims.index(h)
                shape, dims = shape[:at] + shape[at + 1 :], dims[:at] + dims[at + 1 :]
            elif h != "y":
                shape = shape[:-1] + (shape[-1] // 2 if h == "yr" else 2 * shape[-1],)
        self.after, self.left = shape, dims
        self.came = self.shape if hops == ("yg",) else shape

    def share(self, at):
        _, c, x, z, sp = at
        first, wide = self.cols
        index = [slice(None)] * (len(self.shape) - 1) + [pl.ds(first, wide)]
        for h in self.hops:
            if h in self.dims:
                index[self.dims.index(h)] = {"core": c, "x": x, "z1": z % 2, "z2": z // 2}[h]
            elif h == "yr":
                half = wide // 2
                index[-1] = pl.ds(pl.multiple_of(first + sp * half, 128), half)
        return tuple(index)

    def copies(self, src, held, made, came, send, recv, local, at):
        out = [
            remote(src.at[self.share(flipped(at, g))], came[i], send.at[i], recv.at[i], g, at)
            for i, g in enumerate(self.groups)
        ]
        if not held:
            to = made.at[self.part_of(at[4])] if self.hops == ("yg",) else made
            out.append(pltpu.make_async_copy(src.at[self.share(at)], to, local))
        return out

    def part_of(self, sp):
        wide = self.shape[-1]
        return (slice(None),) * (len(self.shape) - 1) + (pl.ds(pl.multiple_of(sp * wide, 128), wide),)

    def add(self, src, held, made, came, at):
        if self.hops == ("yg",):
            if held:
                made[self.part_of(at[4])] = src[self.share(at)]
            made[self.part_of(1 - at[4])] = came[0][...]
        elif len(came) > 1:
            mine = src[self.share(at)] if held else made[...]
            one, two, three = (c[...].astype(F32) for c in came)
            made[...] = ((mine.astype(F32) + one) + (two + three)).astype(BF16)
        elif held:
            made[...] = src[self.share(at)] + came[0][...]
        else:
            made[...] += came[0][...]


class Flow:
    def __init__(self, array, shape, hops, dims=BLOCK, cols=None):
        self.array, self.shape, self.dims, self.cols = array, tuple(shape), dims, cols
        self.hops = list(hops)

    def step(self):
        part = Part(self.hops.pop(0), self.shape, self.dims, self.cols)
        self.shape, self.dims, self.cols = part.after, part.left, None
        return part


class Window:
    def __init__(self, start, stop, joint):
        self.start, self.stop, self.joint = start, stop, joint
        self.parts, self.sources, self.keeps = [], [], []


class Joint:
    def __init__(self):
        self.window = None


def plan(schedule):
    windows, arrays, latest = [], [], {}
    for n, (flows, start, stop, *joint) in enumerate(schedule):
        window = Window(start, stop, bool(joint))
        if joint:
            joint[0].window = n
        for i, flow in enumerate(flows):
            if flow in latest:
                source = ("part",) + latest[flow]
                before = windows[latest[flow][0]]
                before.keeps[latest[flow][1]] = False
            elif isinstance(flow.array, Joint):
                source = ("joint", flow.array.window)
            elif isinstance(flow.array, tuple):
                source = flow.array
            else:
                known = [k for k, a in enumerate(arrays) if a is flow.array]
                if not known:
                    arrays.append(flow.array)
                source = ("in", known[0] if known else len(arrays) - 1)
            window.parts.append(flow.step())
            window.sources.append(source)
            window.keeps.append(not joint)
            if not joint:
                latest[flow] = (n, i)
        windows.append(window)
    return windows, arrays, latest


def carrying(body, own, windows, arrays, grid, also, finale):
    ins, outs, held = own

    def kernel(*refs):
        refs = list(refs)

        def take(n):
            got = refs[:n]
            del refs[:n]
            return got

        my_in, arr = take(ins), take(arrays)
        my_out = take(outs)
        given = [[take(1)[0] if k else None for k in w.keeps] for w in windows]
        my_held = take(held)
        made, came, joints = [], [], []
        for w, g in zip(windows, given):
            if w.joint:
                joint, col, views = take(1)[0], 0, []
                for q in w.parts:
                    views.append(joint.at[(slice(None),) * (len(q.after) - 1) + (pl.ds(col, q.after[-1]),)])
                    col += q.after[-1]
                joints.append(joint)
                made.append(views)
            else:
                joints.append(None)
                made.append([ref if ref is not None else take(1)[0] for ref in g])
            came.append([take(len(q.groups)) for q in w.parts])
        mine = my_in + my_out + my_held
        step = pl.program_id(0)
        groups = [g for w in windows for q in w.parts for g in q.groups] + list(also)
        if groups:
            here = place()
            pl.when(step == 0)(lambda: greet(groups, here))
        if windows:
            send, recv, local = refs
        copies, sources, base = [], [], 0
        for w, m, c in zip(windows, made, came):
            now, froms = [], []
            for i, q in enumerate(w.parts):
                kind = w.sources[i]
                if kind[0] == "in":
                    src = arr[kind[1]]
                elif kind[0] == "ref":
                    src = mine[kind[1]]
                elif kind[0] == "joint":
                    src = joints[kind[1]]
                else:
                    src = made[kind[1]][kind[2]]
                held_here = kind[0] != "in"
                froms.append((src, held_here))
                now += q.copies(
                    src, held_here, m[i], c[i], send.at[base], recv.at[base], local.at[base], here
                )
                base += 1
            copies.append(now)
            sources.append(froms)

        def phase(number):
            for n, w in enumerate(windows):
                if w.stop == number:
                    for copy in copies[n]:
                        copy.wait()
                    for q, (src, held_here), m, c in zip(w.parts, sources[n], made[n], came[n]):
                        q.add(src, held_here, m, c, here)
            for n, w in enumerate(windows):
                if w.start == number:
                    for copy in copies[n]:
                        copy.start()

        used = sorted({w.start for w in windows} | {w.stop for w in windows})
        for number in used:
            if number < grid:
                pl.when(step == number)(functools.partial(phase, number))
        body(*mine)
        for number in used:
            if number >= grid:
                pl.when(step == grid - 1)(functools.partial(phase, number))
        if finale:
            pl.when(step == grid - 1)(lambda: finale(*mine))

    return kernel


def run(
    body, name, grid, ins, in_specs, outs, out_specs, held=(), schedule=(), collective=None,
    flops=0, moved=0, also=(), finale=None,
):
    in_specs, outs, out_specs, held = list(in_specs), list(outs), list(out_specs), list(held)
    windows, arrays, latest = plan(schedule)
    own = len(outs)
    kernel = carrying(body, (len(ins), own, len(held)), windows, len(arrays), grid, also, finale)
    in_specs += [pl.BlockSpec(memory_space=pl.ANY)] * len(arrays)
    order, count = [], 0
    for n, w in enumerate(windows):
        if w.joint:
            shape = w.parts[0].after[:-1] + (sum(q.after[-1] for q in w.parts),)
            held.append(pltpu.VMEM(shape, BF16))
        for i, (q, k) in enumerate(zip(w.parts, w.keeps)):
            if w.joint:
                continue
            if k:
                outs.append(jax.ShapeDtypeStruct(q.after, BF16))
                out_specs.append(whole(q.after))
                order.append((n, i))
            else:
                held.append(pltpu.VMEM(q.after, BF16))
        held += [pltpu.VMEM(q.came, BF16) for q in w.parts for _ in q.groups]
        count += len(w.parts)
    if windows:
        held += [pltpu.SemaphoreType.DMA((count, 3))] * 2 + [pltpu.SemaphoreType.DMA((count,))]
    results = pl.pallas_call(
        kernel,
        grid=(grid,),
        in_specs=in_specs,
        out_specs=out_specs,
        out_shape=outs,
        scratch_shapes=held,
        compiler_params=params(collective if windows or also else None),
        cost_estimate=cost(flops, moved),
        name=name,
    )(*ins, *arrays)
    for flow, where in latest.items():
        flow.array = results[own + order.index(where)]
    return results[:own]


def head_masks(dtype):
    lane = lax.broadcasted_iota(jnp.int32, (1, PAIR), 1)
    low = jnp.where(lane < HD, 1.0, 0.0)
    return low.astype(dtype), (1.0 - low).astype(dtype)


def query_code(code):
    lane = lax.broadcasted_iota(jnp.int32, code.shape, 1)
    return jnp.where(lane < 4, (code.astype(F32) - 1.0) * FAR, 0.0).astype(BF16)


def masked(s, diagonal):
    low, high = s[:-diagonal], s[-diagonal:]
    row = lax.broadcasted_iota(jnp.int32, high.shape, 0)
    col = lax.broadcasted_iota(jnp.int32, high.shape, 1)
    high = jnp.where(row <= col, high, -FAR)
    return jnp.concatenate([low, high], axis=0) if low.shape[0] else high


def softmax_over(jobs):
    results = []
    ready = nt(jobs[0][0], jobs[0][2])
    for n, (_, values_t, _, diagonal) in enumerate(jobs):
        s = ready
        if n + 1 < len(jobs):
            ready = nt(jobs[n + 1][0], jobs[n + 1][2])
        if diagonal:
            s = masked(s, diagonal)
        peak = jnp.max(s, axis=0, keepdims=True)
        e = jnp.exp(s - peak)
        norm = jnp.sum(e, axis=0, keepdims=True)
        results.append((nn(values_t, e.astype(BF16)) / norm, peak + jnp.log(norm)))
    return results


def pair_spec(rows, offset):
    return pl.BlockSpec((rows, PAIR), lambda p: (0, p + offset))


def whole(shape):
    return pl.BlockSpec(shape, lambda *_: (0,) * len(shape))


def delta_rows(g, o):
    prod = g.astype(F32) * o.astype(F32)
    upper = prod.astype(BF16)
    lower = (prod - upper.astype(F32)).astype(BF16)
    row = lax.broadcasted_iota(jnp.int32, (8, PAIR), 0)
    lane = lax.broadcasted_iota(jnp.int32, (8, PAIR), 1)
    pick = jnp.where(row == lane // HD, 1.0, 0.0).astype(BF16)
    return nt(pick, upper) + nt(pick, lower)


def back_pieces(jobs):
    def products(job):
        keys, values, q, g = job[:4]
        return nt(keys, q), nt(values, g)

    ready = products(jobs[0])
    for n, (_, _, _, _, lse, delta, causal) in enumerate(jobs):
        s, dp = ready
        if n + 1 < len(jobs):
            ready = products(jobs[n + 1])
        if causal:
            s = masked(s, s.shape[0])
        p = jnp.exp(s - lse)
        yield n, p.astype(BF16), (p * (dp - delta)).astype(BF16)


def cross_backward_kernel(
    size, pairs, q_ref, k_ref, v_ref, ko_ref, vo_ref, g_ref, o_ref, lse_ref, t_ref, own_ref, oth_ref,
    m_ref, mo_ref, wk_ref, wv_ref, gco_hbm, dh2_hbm, h1_hbm, ctx_hbm, wcq_hbm, wso_hbm, g1_ref, s1_ref,
    dm_out, dmo_out, gb_ref, dh1_ref, dsc_ref, late_ref, small_ref, grad_ref,
    dm_ref, dmo_acc, mt_ref, mot_ref, dcq_ref, dmo_ref, gco_ref, dh2_ref, h1_ref, ctx_ref, wcq_ref, wso_ref, move_ref,
):
    step = pl.program_id(0)
    rows, width = m_ref.shape
    lead = (slice(None),) * (len(grad_ref.shape) - 1)

    loads = [
        pltpu.make_async_copy(src, dst, move_ref.at[i])
        for i, (src, dst) in enumerate(
            (
                (gco_hbm, gco_ref), (dh2_hbm, dh2_ref), (h1_hbm, h1_ref), (ctx_hbm, ctx_ref), (wcq_hbm, wcq_ref),
                (wso_hbm, wso_ref),
            )
        )
    ]
    gives = [
        pltpu.make_async_copy(src, dst, move_ref.at[6 + i])
        for i, (src, dst) in enumerate(((dm_ref, dm_out), (dmo_ref, dmo_out)))
    ]

    def put(ref, col, grad):
        to = pl.ds(pl.multiple_of(col, PAIR), grad.shape[1])
        ref[lead + (to,)] = grad.astype(BF16).reshape(ref.shape[:-1] + (grad.shape[1],))

    @pl.when(step == 0)
    def _():
        for copy in loads:
            copy.start()
        mt_ref[...] = jnp.transpose(m_ref[...])
        mot_ref[...] = jnp.transpose(mo_ref[...])
        dm_ref[...] = jnp.zeros(dm_ref.shape, F32)
        dmo_acc[...] = jnp.zeros(dmo_acc.shape, F32)

    @pl.when(step == 1)
    def _():
        loads[0].wait()
        put(grad_ref, 0, gco_ref[...])

    @pl.when(step < pairs)
    def _():
        count = rows // size
        cols = pl.ds(pl.multiple_of(step * PAIR, PAIR), PAIR)
        sides = [(k_ref, v_ref, own_ref, mt_ref, dm_ref), (ko_ref, vo_ref, oth_ref, mot_ref, dmo_acc)]
        blocks = list(backward_pieces(size, q_ref, g_ref, o_ref, lse_ref, t_ref))
        weights = jnp.concatenate([wk_ref[...], wv_ref[...]], axis=1)
        jobs, where, turned = [], [], []
        for side, (kr, vr, code, _, _) in enumerate(sides):
            keys = jnp.concatenate([kr[...], code[...]], axis=1)
            turned.append(jnp.transpose(kr[...]))
            for block, head, qm, gm, q, lse, delta in blocks:
                jobs.append((keys, vr[...], q, gm, lse, delta, False))
                where.append((side, block, head, qm, gm))
        dq = [[0.0, 0.0] for _ in range(count)]
        dk, dv = [0.0, 0.0], [0.0, 0.0]
        grad = gb = 0.0
        for n, p, ds in back_pieces(jobs):
            side, block, head, qm, gm = where[n]
            dk[side] = dk[side] + nn(ds, qm)
            dv[side] = dv[side] + nn(p, gm)
            dq[block][head] = dq[block][head] + nn(turned[side][head * HD : (head + 1) * HD], ds)
            if n + 1 == len(jobs) or where[n + 1][0] != side:
                both = jnp.concatenate([dk[side].astype(BF16), dv[side].astype(BF16)], axis=1)
                mem, acc = sides[side][3:]
                grad = grad + nn(mem[...], both)
                gb = gb + total(both[:, PAIR:])
                acc[...] += nt(both, weights)
        for block in range(count):
            dcq_ref[block * size : (block + 1) * size, cols] = upright(dq[block]).astype(BF16)
        put(grad_ref, width + step * PAIR, grad[:, :PAIR])
        put(grad_ref, 2 * width + step * PAIR, grad[:, PAIR:])
        gb_ref[:, cols] = gb

    @pl.when(step == pairs)
    def _():
        dmo_ref[...] = dmo_acc[...].astype(BF16)
        for copy in gives:
            copy.start()
        for copy in loads[1:]:
            copy.wait()
        gain = line(g1_ref)
        n1, r1 = normed(h1_ref[...])
        a1b = (n1 * gain + line(s1_ref)).astype(BF16)
        dcq = dcq_ref[...]
        d1 = dh2_ref[...] + nt(dcq, wcq_ref[...])
        dh1 = norm_back(d1, n1, r1, gain)
        dh1_ref[...] = dh1
        dso = dh1.astype(BF16)
        dsc_ref[...] = nt(dso, wso_ref[...]).astype(BF16)
        put(late_ref, 0, tn(a1b, dcq))
        put(late_ref, width, tn(ctx_ref[...], dso))
        small_ref[0:1] = total(dcq)
        small_ref[1:2] = total(d1 * n1)
        small_ref[2:3] = total(d1)
        small_ref[3:4] = total(dso)
        small_ref[4:8] = jnp.zeros((4, width), F32)
        for copy in gives:
            copy.wait()


MIDDLE = 30


def cross_backward(block, cq, kv, kvo, g, o, lse, t, own, oth, m, mo, w, gco, dh2, h1, ctx, wcq, wso, gain, shift, schedule):
    rows, width = cq.shape
    pairs = width // PAIR

    def pair_of(size, offset):
        return pl.BlockSpec((size, PAIR), lambda s: (0, jnp.minimum(s, pairs - 1) + offset))

    flat, square = whole((rows, width)), whole((width, width))
    outs = [
        jax.ShapeDtypeStruct((rows, width), F32),
        jax.ShapeDtypeStruct((rows, width), BF16),
        jax.ShapeDtypeStruct((1, width), F32),
        jax.ShapeDtypeStruct((rows, width), F32),
        jax.ShapeDtypeStruct((rows, width), BF16),
        jax.ShapeDtypeStruct(block + (2 * width,), BF16),
        jax.ShapeDtypeStruct((8, width), F32),
    ]
    far = pl.BlockSpec(memory_space=pl.ANY)
    specs = [far, far, whole((1, width)), flat, flat, whole(block + (2 * width,)), whole((8, width))]
    held = []
    if schedule:
        held.append(pltpu.VMEM(block + (3 * width,), BF16))
    else:
        outs.append(jax.ShapeDtypeStruct(block + (3 * width,), BF16))
        specs.append(whole(block + (3 * width,)))
    held += [
        pltpu.VMEM((rows, width), F32),
        pltpu.VMEM((rows, width), F32),
        pltpu.VMEM((width, rows), BF16),
        pltpu.VMEM((width, rows), BF16),
        pltpu.VMEM((rows, width), BF16),
        pltpu.VMEM((rows, width), BF16),
    ]
    held += [pltpu.VMEM(a.shape, a.dtype) for a in (gco, dh2, h1, ctx, wcq, wso)] + [pltpu.SemaphoreType.DMA((8,))]
    return run(
        functools.partial(cross_backward_kernel, 256, pairs), "cross_backward", pairs + 1,
        (cq, kv, kv, kvo, kvo, g, o, lse, t, own, oth, m, mo, w, w, gco, dh2, h1, ctx, wcq, wso, gain, shift),
        [
            pair_of(rows, 0), pair_of(rows, 0), pair_of(rows, pairs), pair_of(rows, 0), pair_of(rows, pairs),
            pair_of(rows, 0), pair_of(rows, 0),
            pl.BlockSpec((8, rows), lambda s: (jnp.minimum(s, pairs - 1), 0)),
            whole((rows, 128)), whole((rows, 128)), whole((rows, 128)), flat, flat,
            pair_of(width, 0), pair_of(width, pairs),
            far, far, far, far, far, far, whole(gain.shape), whole(shift.shape),
        ],
        outs, specs, held, schedule, 3,
        64 * rows * rows * width + 24 * rows * width * width, 40 * rows * width,
    )


def upright(heads):
    return jnp.transpose(jnp.concatenate(heads, axis=0) * HD**-0.5)


def backward_pieces(size, q_ref, g_ref, o_ref, lse_ref, own_ref):
    masks = head_masks(BF16)
    scale = BF16(HD**-0.5)
    qcode = query_code(own_ref[...])
    delta = delta_rows(g_ref[...], o_ref[...])
    for block in range(q_ref.shape[0] // size):
        at = slice(block * size, (block + 1) * size)
        for head, mask in enumerate(masks):
            qm = q_ref[at] * (mask * scale)
            gm = g_ref[at] * mask
            q = jnp.concatenate([qm, qcode[at]], axis=1)
            yield block, head, qm, gm, q, lse_ref[head : head + 1, at], delta[head : head + 1, at]


def self_backward_kernel(
    size, *refs,
):
    (q2_ref, ko_ref, vo_ref, g2_ref, o2_ref, lse2_ref, wk2_ref, wv2_ref,
     q_ref, k_ref, v_ref, g_ref, o_ref, lse_ref, wq_ref, wk_ref, wv_ref,
     own_ref, oth_ref, x_ref, xo_ref, dh1_ref, sa_ref, sb_ref, sc_ref, sd_ref, dm_hbm, dmo_hbm, out_hbm,
     dx_out, dm_out, out_out, grad_ref,
     dq_acc, dx_acc, dxo_acc, dkv_acc, xt_ref, xot_ref, dxo_ref, came_ref, memory_ref, dm_ref, gm_ref, dx_ref, turn_ref,
     send_ref, recv_ref) = refs
    step = pl.program_id(0)
    second = lax.axis_index("dp") % 2 == 1
    rows, width = x_ref.shape
    pairs = width // PAIR
    early = pairs // 2
    count = rows // size
    over = remote(dxo_ref, came_ref, send_ref.at[0], recv_ref.at[0], ("core",))
    m_over = remote(dmo_hbm, memory_ref, send_ref.at[1], recv_ref.at[1], ("core",))
    dm_load = pltpu.make_async_copy(dm_hbm, dm_ref, send_ref.at[5])

    @pl.when(step == 0)
    def _():
        m_over.start()
        dm_load.start()
        Swap(out_hbm, out_out, send_ref.at[2], recv_ref.at[2]).start()
        xt_ref[...] = jnp.transpose(x_ref[...])
        turn_ref[...] = jnp.zeros(turn_ref.shape, F32)
        turn_ref[0:8] = sa_ref[...]
        turn_ref[8:16] = sb_ref[...]
        turn_ref[16:17] = sc_ref[...]
        dx_acc[...] = dh1_ref[...]

    @pl.when(jnp.logical_and(step == 0, second))
    def _():
        xot_ref[...] = jnp.transpose(xo_ref[...])
        dxo_acc[...] = jnp.zeros(dxo_acc.shape, F32)

    @pl.when(jnp.logical_and(step == 0, jnp.logical_not(second)))
    def _():
        dq_acc[...] = jnp.zeros(dq_acc.shape, F32)
        dkv_acc[...] = jnp.zeros(dkv_acc.shape, BF16)
        xot_ref[...] = jnp.zeros(xot_ref.shape, BF16)

    @pl.when(jnp.logical_and(step < early, second))
    def _():
        jobs, where, turned = [], [], []
        for two in range(2):
            at = slice(two * PAIR, (two + 1) * PAIR)
            keys = jnp.concatenate([ko_ref[:, at], oth_ref[...]], axis=1)
            turned.append(jnp.transpose(ko_ref[:, at]))
            stats = lse2_ref.at[8 * two : 8 * two + 8]
            for block, head, qm, gm, q, lse, delta in backward_pieces(
                size, q2_ref.at[:, at], g2_ref.at[:, at], o2_ref.at[:, at], stats, own_ref
            ):
                jobs.append((keys, vo_ref[:, at], q, gm, lse, delta, False))
                where.append((two, block, head, qm, gm))
        dk, dv = [0.0, 0.0], [0.0, 0.0]
        for n, p, ds in back_pieces(jobs):
            two, block, head, qm, gm = where[n]
            dk[two] = dk[two] + nn(ds, qm)
            dv[two] = dv[two] + nn(p, gm)
            of_head = slice(head * HD, (head + 1) * HD)
            dq_acc[2 * step + two, of_head, block * size : (block + 1) * size] = nn(turned[two][of_head], ds)
        for two in range(2):
            at = slice(two * PAIR, (two + 1) * PAIR)
            both = jnp.concatenate([dk[two].astype(BF16), dv[two].astype(BF16)], axis=1)
            dkv_acc[2 * step + two] = both
            dxo_acc[...] += nt(both, jnp.concatenate([wk2_ref[:, at], wv2_ref[:, at]], axis=1))

    @pl.when(jnp.logical_and(step == early - 1, second))
    def _():
        dxo_ref[...] = dxo_acc[...].astype(BF16)
        over.start()

    @pl.when(step == early)
    def _():
        m_over.wait()
        dm_load.wait()
        gm_ref[...] = (dm_ref[...] + memory_ref[...].astype(F32)).astype(BF16)
        Swap(gm_ref, dm_out, send_ref.at[3], recv_ref.at[3]).start()

    @pl.when(step >= early)
    def _():
        pair = step - early
        cols = pl.ds(pl.multiple_of(pair * PAIR, PAIR), PAIR)
        dkvo = dkv_acc[pair]
        grad_o = nn(xot_ref[...], dkvo)
        turned = jnp.transpose(k_ref[...])
        dq = [[0.0, 0.0] for _ in range(count)]
        dk, dv = [0.0] * count, [0.0] * count
        jobs, where = [], []
        keys = jnp.concatenate([k_ref[...], own_ref[...]], axis=1)
        for block, head, qm, gm, q, lse, delta in backward_pieces(size, q_ref, g_ref, o_ref, lse_ref, own_ref):
            for part in range(block + 1):
                of = slice(part * size, (part + 1) * size)
                jobs.append((keys[of], v_ref[of], q, gm, lse, delta, part == block))
                where.append((block, part, head, qm, gm))
        for n, p, ds in back_pieces(jobs):
            block, part, head, qm, gm = where[n]
            of = slice(part * size, (part + 1) * size)
            dk[part] = dk[part] + nn(ds, qm)
            dv[part] = dv[part] + nn(p, gm)
            dq[block][head] = dq[block][head] + nn(turned[head * HD : (head + 1) * HD, of], ds)
        dk, dv = (jnp.concatenate(a, axis=0).astype(BF16) for a in (dk, dv))
        before = dq_acc[pair]
        dq = jnp.concatenate(
            [
                upright(
                    [
                        part + before[head * HD : (head + 1) * HD, block * size : (block + 1) * size]
                        for head, part in enumerate(parts)
                    ]
                )
                for block, parts in enumerate(dq)
            ],
            axis=0,
        ).astype(BF16)
        dkv = jnp.concatenate([dk, dv], axis=1)
        grad_kv = nn(xt_ref[...], dkv) + grad_o
        grad_q = nn(xt_ref[...], dq)
        dx_acc[...] += nt(dkv, jnp.concatenate([wk_ref[...], wv_ref[...]], axis=1)) + nt(dq, wq_ref[...])
        lead = (slice(None),) * (len(grad_ref.shape) - 1)
        for n, grad in enumerate((grad_q, grad_kv[:, :PAIR], grad_kv[:, PAIR:])):
            to = pl.ds(pl.multiple_of((pair * 3 + n) * PAIR, PAIR), PAIR)
            grad_ref[lead + (to,)] = grad.astype(BF16).reshape(grad_ref.shape[:-1] + (PAIR,))
        turn_ref[21:22, cols] = total(dq)
        turn_ref[22:23, cols] = total(dv) + total(dkvo[:, PAIR:])

    @pl.when(step == early + pairs - 1)
    def _():
        shape = grad_ref.shape[:-1] + (PAIR,)
        lead = (slice(None),) * (len(shape) - 1)
        columns = jnp.transpose(turn_ref[...])
        if sd_ref.shape == columns.shape:
            columns = columns + sd_ref[...]
        grad_ref[lead + (slice(3 * width, 3 * width + PAIR),)] = columns.astype(BF16).reshape(shape)

        @pl.when(second)
        def _():
            over.wait_send()
            dx_ref[...] = dx_acc[...].astype(BF16)

        @pl.when(jnp.logical_not(second))
        def _():
            over.wait_recv()
            dx_ref[...] = (dx_acc[...] + came_ref[...].astype(F32)).astype(BF16)

        Swap(dx_ref, dx_out, send_ref.at[4], recv_ref.at[4]).start()


def self_backward_finale(*refs):
    out_hbm, dx_out, dm_out, out_out = refs[28:32]
    gm_ref, dx_ref, _, send_ref, recv_ref = refs[43:48]
    Swap(out_hbm, out_out, send_ref.at[2], recv_ref.at[2]).wait()
    Swap(gm_ref, dm_out, send_ref.at[3], recv_ref.at[3]).wait()
    Swap(dx_ref, dx_out, send_ref.at[4], recv_ref.at[4]).wait()


GRADS = 32


def self_backward(block, qkv, kvo, g, o, lse, own, oth, x, xo, w, dh1, small, dm, dmo, out, schedule):
    rows, width = x.shape
    pairs = width // PAIR
    early = pairs // 2

    def two_of(size, offset):
        return pl.BlockSpec((size, 2 * PAIR), lambda s: (0, jnp.minimum(s, early - 1) + offset))

    def pair_of(size, offset):
        return pl.BlockSpec((size, PAIR), lambda s: (0, jnp.maximum(s - early, 0) + offset))

    made = block + (3 * width + PAIR,)
    far = pl.BlockSpec(memory_space=pl.ANY)
    outs = [jax.ShapeDtypeStruct((rows, width), BF16)] * 3
    specs = [far] * 3
    held = []
    if schedule:
        held += [pltpu.VMEM(made, BF16)]
    else:
        outs += [jax.ShapeDtypeStruct(made, BF16)]
        specs += [whole(made)]
    held += [
        pltpu.VMEM((pairs, PAIR, rows), F32),
        pltpu.VMEM((rows, width), F32),
        pltpu.VMEM((rows, width), F32),
        pltpu.VMEM((pairs, rows, 2 * PAIR), BF16),
        pltpu.VMEM((width, rows), BF16),
        pltpu.VMEM((width, rows), BF16),
        pltpu.VMEM((rows, width), BF16),
        pltpu.VMEM((rows, width), BF16),
        pltpu.VMEM((rows, width), BF16),
        pltpu.VMEM((rows, width), F32),
        pltpu.VMEM((rows, width), BF16),
        pltpu.VMEM((rows, width), BF16),
        pltpu.VMEM((PAIR, width), F32),
        pltpu.SemaphoreType.DMA((6,)),
        pltpu.SemaphoreType.DMA((5,)),
    ]
    return run(
        functools.partial(self_backward_kernel, 256), "self_backward", early + pairs,
        (qkv, kvo, kvo, g, o, lse, w, w, qkv, qkv, qkv, g, o, lse, w, w, w, own, oth, x, xo, dh1) + tuple(small) + (dm, dmo, out),
        [
            two_of(rows, 0), two_of(rows, 0), two_of(rows, early), two_of(rows, 0), two_of(rows, 0),
            pl.BlockSpec((16, rows), lambda s: (jnp.minimum(s, early - 1), 0)),
            two_of(width, early), two_of(width, 2 * early),
            pair_of(rows, 0), pair_of(rows, pairs), pair_of(rows, 2 * pairs), pair_of(rows, 0), pair_of(rows, 0),
            pl.BlockSpec((8, rows), lambda s: (jnp.maximum(s - early, 0), 0)),
            pair_of(width, 0), pair_of(width, pairs), pair_of(width, 2 * pairs),
            whole((rows, 128)), whole((rows, 128)), whole((rows, width)), whole((rows, width)), whole((rows, width)),
        ] + [whole(a.shape) for a in small] + [far] * 3,
        outs, specs, held, schedule, 5,
        48 * rows * rows * width + 20 * rows * width * width, 12 * width * width + 40 * rows * width,
        (("core",), ("core", "y")), self_backward_finale,
    )


def code_of(docs_ref):
    row = lax.broadcasted_iota(jnp.int32, (PAIR, docs_ref.shape[1]), 0)
    return jnp.transpose(jnp.where(docs_ref[...] == row, 1.0, 0.0)).astype(BF16)


def line(ref):
    return ref[...].astype(F32)[None, :]


def moving():
    return lax.axis_index("dp") % 2 != lax.axis_index("sp")


class Swap:
    def __init__(self, src, dst, send, recv):
        self.there = remote(src, dst, send, recv, ("core", "y"))
        self.here = pltpu.make_async_copy(src, dst, recv)

    def start(self):
        pl.when(moving())(self.there.start)
        pl.when(jnp.logical_not(moving()))(self.here.start)

    def wait_recv(self):
        pl.when(moving())(self.there.wait_recv)
        pl.when(jnp.logical_not(moving()))(self.here.wait)

    def wait_send(self):
        pl.when(moving())(self.there.wait_send)

    def wait(self):
        self.wait_send()
        self.wait_recv()


def front_kernel(
    size, x_hbm, m_hbm, c_hbm, td_hbm, md_hbm, wx_hbm, wm_hbm, wo_hbm, wq_hbm,
    bq_ref, bv_ref, bcv_ref, bso_ref, g_ref, s_ref, bcq_ref,
    qkv_out, mkv_out, kvo_out, mkvo_out, cq_out, ctx_out, cc_out, h_out, xo_out, mo_out, x_out, m_out, c_out,
    lse_ref, clse_ref, tt_ref, mt_ref, to_ref, mo_ref,
    x_ref, m_ref, wx_ref, wm_ref, wo_ref, wq_ref, xc_ref, mc_ref, td_ref, md_ref, tdc_ref, mdc_ref,
    qkv_ref, mkv_ref, kvo_ref, mkvo_ref, cq_ref, ctx_ref, cc_ref, h_ref, acc_ref,
    load_ref, store_ref, send_ref, recv_ref,
):
    rows, width = x_ref.shape
    pairs = width // PAIR
    second = lax.axis_index("dp") % 2 == 1
    first = jnp.logical_not(second)
    masks = head_masks(BF16)
    scale = BF16(HD**-0.5)
    loads = [
        pltpu.make_async_copy(src, dst, load_ref.at[i])
        for i, (src, dst) in enumerate(((wx_hbm, wx_ref), (wm_hbm, wm_ref), (wo_hbm, wo_ref), (wq_hbm, wq_ref)))
    ]
    give = [
        pltpu.make_async_copy(src, dst, store_ref.at[i])
        for i, (src, dst) in enumerate(
            (
                (qkv_ref, qkv_out), (mkv_ref, mkv_out), (mkvo_ref, mkvo_out), (cq_ref, cq_out), (ctx_ref, ctx_out),
                (cc_ref, cc_out), (h_ref, h_out), (mc_ref, mo_out), (x_ref, x_out), (m_ref, m_out),
                (kvo_ref, kvo_out), (xc_ref, xo_out),
            )
        )
    ]
    swaps = [
        Swap(src, dst, send_ref.at[i], recv_ref.at[i])
        for i, (src, dst) in enumerate(
            ((td_hbm, td_ref), (md_hbm, md_ref), (m_hbm, m_ref), (c_hbm, c_out))
            + tuple((x_hbm.at[at], x_ref.at[at]) for at in (pl.ds(0, rows // 2), pl.ds(rows // 2, rows // 2)))
        )
    ]
    x_over = remote(x_ref, xc_ref, send_ref.at[6], recv_ref.at[6], ("core",))
    m_over = remote(m_ref, mc_ref, send_ref.at[7], recv_ref.at[7], ("core",))
    docs = [
        remote(td_ref, tdc_ref, send_ref.at[8], recv_ref.at[8], ("core",)),
        remote(md_ref, mdc_ref, send_ref.at[9], recv_ref.at[9], ("core",)),
    ]
    for copy in loads:
        copy.start()
    greet([("core", "y"), ("core",)])
    for copy in swaps[:2] + swaps[4:]:
        copy.start()

    def columns(offset, pair):
        return pl.ds(pl.multiple_of(offset + pair * PAIR, PAIR), PAIR)

    def heads(source, offset, pair, code, block):
        at = slice(block * size, (block + 1) * size)
        q = source[at, columns(offset, pair)]
        return [jnp.concatenate([q * (mask * scale), code[at]], axis=1) for mask in masks]

    def keep(block, pair, outs, lses, lse_out, out):
        at = slice(block * size, (block + 1) * size)
        mixed = jnp.concatenate(outs, axis=0)
        acc_ref[pair, :, at] = mixed
        out[at, columns(0, pair)] = jnp.transpose(mixed).astype(BF16)
        row = lax.broadcasted_iota(jnp.int32, (8, size), 0)
        lse_out[pl.ds(pl.multiple_of(pair * 8, 8), 8), at] = jnp.where(row == 0, lses[0], lses[1])

    def begin(block, pair, results, lse_out, out):
        keep(block, pair, [r for r, _ in results], [lse for _, lse in results], lse_out, out)

    def merge(block, pair, results, lse_out, out):
        at = slice(block * size, (block + 1) * size)
        stats = lse_out[pl.ds(pl.multiple_of(pair * 8, 8), 8), at]
        outs, lses = [], []
        for head, (r, lse) in enumerate(results):
            before = acc_ref[pair, head * HD : (head + 1) * HD, at]
            old = stats[head : head + 1]
            peak = jnp.maximum(old, lse)
            both = peak + jnp.log(jnp.exp(old - peak) + jnp.exp(lse - peak))
            outs.append(before * jnp.exp(old - both) + r * jnp.exp(lse - both))
            lses.append(both)
        keep(block, pair, outs, lses, lse_out, out)

    def halves(values):
        turned = jnp.transpose(values)
        return turned[:HD], turned[HD:]

    waiting = jnp.logical_and(second, moving())

    def other_keys():
        for n, bias in enumerate((0.0, line(bv_ref))):
            cols = slice(n * width, (n + 1) * width)
            from_cols = slice((n + 1) * width, (n + 2) * width)
            kvo_ref[:, cols] = (nn(xc_ref[...], wx_ref[:, from_cols]) + bias).astype(BF16)
        give[10].start()

    def other_memory():
        for n, bias in enumerate((0.0, line(bcv_ref))):
            cols = slice(n * width, (n + 1) * width)
            mkvo_ref[:, cols] = (nn(mc_ref[...], wm_ref[:, cols]) + bias).astype(BF16)
        give[2].start()

    @pl.when(jnp.logical_not(moving()))
    def _():
        swaps[2].start()
        swaps[4].wait()
        swaps[5].wait()
        pl.when(first)(x_over.start)
        swaps[2].wait()
        m_over.start()

    for copy in swaps[:2]:
        copy.wait_recv()
    for copy in docs:
        copy.start()
    to_ref[...] = code_of(td_ref)
    mo_ref[...] = code_of(md_ref)
    loads[0].wait()
    loads[1].wait()

    @pl.when(waiting)
    def _():
        x_over.wait_recv()
        give[11].start()
        other_keys()
        m_over.wait_recv()
        give[7].start()
        other_memory()

    for half, copy in enumerate(swaps[4:]):
        pl.when(moving())(copy.wait)
        at = slice(half * rows // 2, (half + 1) * rows // 2)
        if half:

            @pl.when(moving())
            def _():
                swaps[2].start()
                pl.when(first)(x_over.start)

            give[8].start()
        for n, bias in enumerate((line(bq_ref), 0.0, line(bv_ref))):
            cols = slice(n * width, (n + 1) * width)
            qkv_ref[at, cols] = (nn(x_ref[at], wx_ref[:, cols]) + bias).astype(BF16)
    give[0].start()

    def attend(query, keys_ref, key_at, value_at, key_code, diagonal, finish, stats, out):
        @pl.loop(0, pairs // 3)
        def _(third):
            code = query_code(to_ref[...])
            jobs, where = [], []
            for pair in (3 * third, 3 * third + 1, 3 * third + 2):
                keys = jnp.concatenate([keys_ref[:, columns(key_at, pair)], key_code[...]], axis=1)
                values = halves(keys_ref[:, columns(value_at, pair)])
                for block in range(rows // size):
                    end = (block + 1) * size if diagonal else rows
                    for q, v in zip(heads(query, 0, pair, code, block), values):
                        jobs.append((keys[:end], v[:, :end], q, size if diagonal else 0))
                    where.append((block, pair))
            results = softmax_over(jobs)
            for n, (block, pair) in enumerate(where):
                finish(block, pair, results[2 * n : 2 * n + 2], stats, out)

    attend(qkv_ref, qkv_ref, width, 2 * width, to_ref, True, begin, lse_ref, ctx_ref)

    for copy in docs:
        copy.wait()
    tt_ref[...] = code_of(tdc_ref)
    mt_ref[...] = code_of(mdc_ref)
    @pl.when(moving())
    def _():
        swaps[2].wait()
        m_over.start()

    swaps[3].start()
    give[9].start()
    pl.when(first)(x_over.wait_send)

    @pl.when(jnp.logical_and(second, jnp.logical_not(waiting)))
    def _():
        x_over.wait_recv()
        give[11].start()
        other_keys()

    @pl.when(second)
    def _():
        attend(qkv_ref, kvo_ref, 0, width, tt_ref, False, merge, lse_ref, ctx_ref)

    give[4].start()
    loads[2].wait()
    loads[3].wait()
    h = x_ref[...].astype(F32) + nn(ctx_ref[...], wo_ref[...]) + line(bso_ref)
    h_ref[...] = h
    n, _ = normed(h)
    a = (n * line(g_ref) + line(s_ref)).astype(BF16)
    cq_ref[...] = (nn(a, wq_ref[...]) + line(bcq_ref)).astype(BF16)
    give[6].start()
    give[3].start()

    for n, bias in enumerate((0.0, line(bcv_ref))):
        cols = slice(n * width, (n + 1) * width)
        mkv_ref[:, cols] = (nn(m_ref[...], wm_ref[:, cols]) + bias).astype(BF16)
    give[1].start()
    attend(cq_ref, mkv_ref, 0, width, mo_ref, False, begin, clse_ref, cc_ref)
    m_over.wait_send()

    @pl.when(jnp.logical_not(waiting))
    def _():
        m_over.wait_recv()
        give[7].start()
        other_memory()

    attend(cq_ref, mkvo_ref, 0, width, mt_ref, False, merge, clse_ref, cc_ref)
    give[5].start()
    for copy in give[:10]:
        copy.wait()
    for copy in swaps[:2]:
        copy.wait_send()
    swaps[3].wait()

    @pl.when(second)
    def _():
        give[10].wait()
        give[11].wait()


def front(x, mem, ct, td, md, wx, wm, wo, wq, vectors):
    rows, width = x.shape
    pairs = width // PAIR

    def flat(n):
        return jax.ShapeDtypeStruct((rows, n * width), BF16)

    stats = jax.ShapeDtypeStruct((8 * pairs, rows), F32)
    code = jax.ShapeDtypeStruct((rows, PAIR), BF16)
    far = pl.BlockSpec(memory_space=pl.ANY)
    near = pl.BlockSpec(memory_space=pltpu.VMEM)
    tall = jax.ShapeDtypeStruct((rows, width), F32)
    held = [flat(3), flat(2), flat(2), flat(2), flat(1), flat(1), flat(1), tall]
    return pl.pallas_call(
        functools.partial(front_kernel, 256),
        in_specs=[far] * 9 + [near] * len(vectors),
        out_specs=[far] * 13 + [near] * 6,
        out_shape=[flat(3), flat(2), flat(2), flat(2), flat(1), flat(1), flat(1), tall] + [flat(1)] * 5
        + [stats, stats, code, code, code, code],
        scratch_shapes=[pltpu.VMEM((rows, width), BF16)] * 2
        + [pltpu.VMEM(w.shape, BF16) for w in (wx, wm, wo, wq)]
        + [pltpu.VMEM((rows, width), BF16)] * 2
        + [pltpu.VMEM((1, rows), jnp.int32)] * 4
        + [pltpu.VMEM(a.shape, a.dtype) for a in held]
        + [
            pltpu.VMEM((pairs, PAIR, rows), F32),
            pltpu.SemaphoreType.DMA((4,)),
            pltpu.SemaphoreType.DMA((12,)),
            pltpu.SemaphoreType.DMA((10,)),
            pltpu.SemaphoreType.DMA((10,)),
        ],
        compiler_params=params(1),
        cost_estimate=cost(22 * rows * width * width + 36 * rows * rows * width, 60 * rows * width),
        name="front",
    )(x, mem, ct, td, md, wx, wm, wo, wq, *vectors)


def feed_kernel(
    count, comm, h1_ref, cc_ref, ct_ref, wco_ref, wi_ref, wo_ref,
    g1_ref, s1_ref, bco_ref, g2_ref, s2_ref, bfo_ref, g3_ref, s3_ref, bfi_ref, out_ref, dh2_ref, dcc_ref, gco_ref, *refs,
):
    if comm:
        gwi_ref, refs = refs[0], refs[1:]
    else:
        gwi_ref, gwo_ref, refs = refs[0], refs[1], refs[2:]
    small_ref, gib_ref, hid_ref, slope_ref, n2_ref, r2_ref, a2b_ref, acc_ref, df_ref, bias_ref, *refs = refs
    step = pl.program_id(0)
    width = acc_ref.shape[1]

    if comm:
        mi_ref, mo_ref, ci_ref, co_ref, send_ref, recv_ref = refs
        wide = ci_ref.shape[-1]
        here = place()
        c = here[1]

        def chunk_copies(j):
            at = pl.ds(pl.multiple_of(j * width, width), width)
            return remote(mi_ref.at[:, :, at], ci_ref.at[:, :, at], send_ref.at[0, j], recv_ref.at[0, j], ("core",), here)

        def block_copies(j):
            return remote(mo_ref.at[j], co_ref.at[j], send_ref.at[1, j], recv_ref.at[1, j], ("core",), here)

        def place_of(j, i):
            return (j // 2, j % 2, slice(None), slice(None), slice(wide + i * width, wide + (i + 1) * width))

    @pl.when(step == 0)
    def _():
        wide = bfi_ref[...].astype(F32)
        for i in range(count):
            bias_ref[i : i + 1] = wide[None, i * width : (i + 1) * width]
        n1, _ = normed(h1_ref[...])
        a1 = n1 * line(g1_ref) + line(s1_ref)
        h2 = a1 + nn(cc_ref[...], wco_ref[...]) + line(bco_ref)
        n2, r2 = normed(h2)
        n2_ref[...] = n2
        r2_ref[...] = jnp.broadcast_to(r2, r2_ref.shape)
        a2 = n2 * line(g2_ref) + line(s2_ref)
        a2b_ref[...] = a2.astype(BF16)
        acc_ref[...] = a2 + line(bfo_ref)

    piece = 2 * PAIR
    pieces = [slice(i, i + piece) for i in range(0, width, piece)]

    @pl.when(step < count)
    def _():
        def product(at):
            return nn(a2b_ref[...], wi_ref[:, at])

        bias = bias_ref[pl.ds(step, 1)]
        ready = product(pieces[0])
        more = 0.0
        for i, at in enumerate(pieces):
            u = ready + bias[:, at]
            if i + 1 < len(pieces):
                ready = product(pieces[i + 1])
            cumul = 0.5 * (1.0 + lax.erf(u * 0.7071067811865476))
            density = jnp.exp(-0.5 * u * u) * 0.3989422804014327
            hid = (u * cumul).astype(BF16)
            hid_ref[step, :, at] = hid
            slope_ref[step, :, at] = cumul + u * density
            more = more + nn(hid, wo_ref[at])
        acc_ref[...] += more

    @pl.when(step == count - 1)
    def _():
        n3, r3 = normed(acc_ref[...])
        gain = line(g3_ref)
        out_ref[...] = (n3 * gain + line(s3_ref)).astype(BF16)
        e = ct_ref[...].astype(F32)
        d3 = norm_back(e, n3, r3, gain)
        df = d3.astype(BF16)
        df_ref[...] = df
        acc_ref[...] = d3
        small_ref[0:1] = total(e * n3)
        small_ref[1:2] = total(e)
        small_ref[2:3] = total(df)

    @pl.when(jnp.logical_and(step >= count, step < 2 * count))
    def _():
        j = step - count
        df = df_ref[...]

        def product(at):
            return nt(df, wo_ref[at])

        ready = product(pieces[0])
        more, go, gi, sums = 0.0, [], [], []
        for i, at in enumerate(pieces):
            du = (ready * slope_ref[j, :, at]).astype(BF16)
            if i + 1 < len(pieces):
                ready = product(pieces[i + 1])
            if not comm:
                go.append(tn(hid_ref[j, :, at], df).astype(BF16))
            more = more + nt(du, wi_ref[:, at])
            gi.append(tn(a2b_ref[...], du).astype(BF16))
            sums.append(tn(du, jnp.ones((du.shape[0], PAIR), BF16)))
        acc_ref[...] += more
        gi, sums = jnp.concatenate(gi, axis=1), jnp.concatenate(sums, axis=0)
        quarter = width // gib_ref.shape[0]
        if gib_ref.shape[0] == 4:
            lane = lax.broadcasted_iota(jnp.int32, (quarter // 4, PAIR), 1)
            for i in range(4):
                part = sum(
                    jnp.where(lane == 17 + n, sums[(4 * i + n) * quarter // 4 : (4 * i + n + 1) * quarter // 4], 0.0)
                    for n in range(4)
                )
                gib_ref[i] = part
        else:
            gib_ref[0] = jnp.transpose(sums)[:1]
        if comm:
            at = pl.ds(pl.multiple_of(j * width, width), width)
            narrow = gwi_ref.shape[3]
            gi = gi.reshape(2, 2, 2, 2, narrow, width)
            gwi_ref[:, :, :, :, at] = jnp.where(c == 0, gi[:, :, :, 0], gi[:, :, :, 1])
            mi_ref[:, :, at] = jnp.where(c == 0, gi[:, :, :, 1], gi[:, :, :, 0]).reshape(8, narrow, width)
            chunk_copies(j).start()
        else:
            gwo_ref[...] = jnp.concatenate(go, axis=0)
            gwi_ref[...] = gi

    @pl.when(step == 2 * count)
    def _():
        d2 = acc_ref[...]
        n2 = n2_ref[...]
        dh2 = norm_back(d2, n2, r2_ref[:, :1], line(g2_ref))
        dh2_ref[...] = dh2
        dco = dh2.astype(BF16)
        dcc_ref[...] = nt(dco, wco_ref[...]).astype(BF16)
        gco_ref[...] = tn(cc_ref[...], dco).astype(BF16)
        small_ref[3:4] = total(d2 * n2)
        small_ref[4:5] = total(d2)
        small_ref[5:6] = total(dco)
        small_ref[6:8] = jnp.zeros((2, d2.shape[1]), F32)

    if comm:

        @pl.when(step == count)
        def _():
            narrow = gwi_ref.shape[3]
            for j in range(count):
                go = tn(hid_ref[j], df_ref[...]).astype(BF16).reshape(2, 2, 4, narrow, width)
                mo_ref[j] = jnp.where(c == 0, go[:, 1], go[:, 0])
                block_copies(j).start()
                for i in range(4):
                    gwi_ref[place_of(j, i)] = jnp.where(c == 0, go[:, 0, i], go[:, 1, i])

        @pl.when(step == count + 1)
        def _():
            for j in range(count):
                block_copies(j).wait()
                for i in range(4):
                    gwi_ref[place_of(j, i)] += co_ref[j, :, i]

        @pl.when(step > count)
        def _():
            j = step - count - 1
            at = pl.ds(pl.multiple_of(j * width, width), width)
            chunk_copies(j).wait()
            gwi_ref[:, :, :, :, at] += ci_ref[:, :, at].reshape(gwi_ref.shape[:-1] + (width,))


FEEDS = 19


def feed(size, comm, h1, cc, ct, wco, wi, wo, vectors, schedule):
    rows, width = h1.shape
    wide = wi.shape[1]
    chunk = width
    count = wide // chunk

    def weight(s):
        return jnp.where(s < count, s, jnp.minimum(s - count, count - 1))

    def early(s):
        return jnp.clip(s - count, 0, count - 1)

    flat = whole((rows, width))
    square = whole((width, width))
    scratch = [
        pltpu.VMEM((count, rows, chunk), BF16),
        pltpu.VMEM((count, rows, chunk), F32),
        pltpu.VMEM((rows, width), F32),
        pltpu.VMEM((rows, 128), F32),
        pltpu.VMEM((rows, width), BF16),
        pltpu.VMEM((rows, width), F32),
        pltpu.VMEM((rows, width), BF16),
        pltpu.VMEM((8, width), F32),
    ]
    if comm:
        narrow = width // size
        gib_shape = jax.ShapeDtypeStruct((size, narrow, PAIR), F32)
        gib_spec = pl.BlockSpec((4, narrow, PAIR), lambda s: (early(s), 0, 0))
        grad_specs = [whole((2, 2, 2, narrow, 2 * wide))]
        grad_shapes = [(2, 2, 2, narrow, 2 * wide)]
        scratch += [
            pltpu.VMEM((size // 2, narrow, wide), BF16),
            pltpu.VMEM((count, 2, 4, narrow, width), BF16),
            pltpu.VMEM((size // 2, narrow, wide), BF16),
            pltpu.VMEM((count, 2, 4, narrow, width), BF16),
            pltpu.SemaphoreType.DMA((2, count)),
            pltpu.SemaphoreType.DMA((2, count)),
        ]
    else:
        gib_shape = jax.ShapeDtypeStruct((count, 1, width), F32)
        gib_spec = pl.BlockSpec((1, 1, chunk), lambda s: (early(s), 0, 0))
        grad_specs = [
            pl.BlockSpec((width, chunk), lambda s: (0, early(s))),
            pl.BlockSpec((chunk, width), lambda s: (early(s), 0)),
        ]
        grad_shapes = [(width, wide), (wide, width)]
    return run(
        functools.partial(feed_kernel, count, comm), "feed", 2 * count + 1,
        (h1, cc, ct, wco, wi, wo) + tuple(vectors),
        [
            flat, flat, flat, square,
            pl.BlockSpec((width, chunk), lambda s: (0, weight(s))),
            pl.BlockSpec((chunk, width), lambda s: (weight(s), 0)),
        ]
        + [whole(v.shape) for v in vectors],
        [
            jax.ShapeDtypeStruct((rows, width), BF16),
            jax.ShapeDtypeStruct((rows, width), F32),
            jax.ShapeDtypeStruct((rows, width), BF16),
            jax.ShapeDtypeStruct((width, width), BF16),
        ]
        + [jax.ShapeDtypeStruct(a, BF16) for a in grad_shapes]
        + [jax.ShapeDtypeStruct((8, width), F32), gib_shape],
        [flat, flat, flat, square] + grad_specs + [whole((8, width)), gib_spec],
        scratch, schedule, 2,
        12 * rows * width * wide + 6 * rows * width * width, 12 * width * wide + 16 * rows * width,
        (("core",),) if comm else (),
    )


def outputs_kernel(moves, count, line, *refs):
    pieces, rest = refs[:count], refs[count:]
    out_ref, dx_ref, dm_ref = rest[:3]
    outs = rest[3:]
    for piece, first, wide, which, row, col in moves:
        ref = pieces[piece]
        outs[which][row : row + ref.shape[0], col : col + wide] = ref[:, first : first + wide].astype(F32)
    vectors, (turned, result, dx, dm) = outs[-4 - len(LINES) : -4], outs[-4:]
    lines = jnp.transpose(pieces[line[0]][:, line[1] : line[1] + PAIR].astype(F32))
    turned[...] = lines
    for ref, i in zip(vectors, LINES):
        ref[...] = lines[i]
    result[...] = out_ref[...]
    dx[...] = dx_ref[...]
    dm[...] = dm_ref[...]


LINES = (0, 1, 2, 3, 4, 5, 8, 9, 10, 11, 16, 21, 22)


def outputs(pieces, moves, line, shapes, out, dx, dm):
    ins = tuple(pieces) + (out, dx, dm)
    result = jax.ShapeDtypeStruct(out.shape, BF16)
    return pl.pallas_call(
        functools.partial(outputs_kernel, moves, len(pieces), line),
        out_shape=[jax.ShapeDtypeStruct(a, F32) for a in shapes]
        + [jax.ShapeDtypeStruct((pieces[0].shape[0],), F32)] * len(LINES)
        + [jax.ShapeDtypeStruct((PAIR, pieces[0].shape[0]), F32), result, result, result],
        compiler_params=params(),
        cost_estimate=cost(0, 12 << 20),
        name="outputs",
    )(*ins)


def moved(pieces, targets):
    out = []
    for n, (start, wide) in enumerate(pieces):
        for first, cols, which, row, col in targets:
            low, high = max(start, first), min(start + wide, first + cols)
            if low < high:
                out.append((n, low - start, high - low, which, row, col + low - first))
    return out


def schedule_of(flows, kernel):
    entries = [
        (start, order, name, start, stop)
        for order, name in enumerate(flows)
        for start, stop in (PLAN[name] + ((), (), ()))[kernel]
    ]
    return tuple(([flows[name]], start, stop) for _, _, name, start, stop in sorted(entries))


def swap_sum(part, axis, pairs):
    came = lax.ppermute(part, axis, pairs)
    return part.astype(F32) + came.astype(F32)


def sum_scatter(grad, size, order):
    rows, cols = grad.shape
    bits = size.bit_length() - 1
    me = lax.axis_index("dp")
    now = grad.reshape((2,) * bits + (rows // size, cols))
    left = list(range(bits))[::-1]
    for bit in [b for b in order if b < bits] + [b for b in range(bits) if b not in order]:
        axis = left.index(bit)
        mine = (me >> bit) & 1
        keep = lax.dynamic_index_in_dim(now, mine, axis, keepdims=False)
        send = lax.dynamic_index_in_dim(now, 1 - mine, axis, keepdims=False)
        came = lax.ppermute(send, "dp", [(i, i ^ (1 << bit)) for i in range(size)])
        now = (keep.astype(F32) + came.astype(F32)).astype(BF16)
        left.pop(axis)
    return swap_sum(now, "sp", [(0, 1), (1, 0)])


def per_device(
    size,
    inputs,
    memory,
    target_docs,
    memory_docs,
    cotangent,
    w_qkv,
    b_q,
    b_v,
    w_so,
    b_so,
    g_one,
    s_one,
    w_cq,
    b_cq,
    w_ckv,
    b_cv,
    w_co,
    b_co,
    g_two,
    s_two,
    w_fi,
    b_fi,
    w_fo,
    b_fo,
    g_three,
    s_three,
):
    rows, width = inputs.shape[1:]
    wide = b_fi.shape[0]
    comm = size == 16
    narrow, broad = width // size, wide // size
    x, mem, ct = inputs[0], memory[0], cotangent[0]
    qkv, mkv, kvo, mkvo, cq, ctx, cc, h1, x_o, mem_o, x, mem, ct, lse, clse, t_oth, m_oth, t_own, m_own = front(
        x, mem, ct, target_docs, memory_docs, w_qkv, w_ckv, w_so, w_cq, (b_q, b_v, b_cv, b_so, g_one, s_one, b_cq)
    )
    block = (2, 2, 2, 2, narrow) if comm else (width,)
    at_feed, at_cross, at_self, flows = (), (), (), {}
    if comm:
        joint = block[:3] + (narrow, 2 * wide)
        sources = {
            "T0i": (None, joint, BLOCK[:3]),
            "T0p": (None, joint, BLOCK[:3]),
            "T0o": (("ref", FEEDS), joint, BLOCK[:3]),
            "T1a": (("ref", MIDDLE), block + (3 * width,), BLOCK),
            "T1b": (None, block + (2 * width,), BLOCK),
            "G": (("ref", GRADS), block + (3 * width + PAIR,), BLOCK),
        }
        for name, (source, cols, hops, *_) in PLAN.items():
            array, shape, dims = sources[source]
            flows[name] = Flow(array, shape, hops, dims, cols)
        at_feed = schedule_of(flows, 5)
    output, dh2, dcc, gco, gwi, *gwo, small_a, gib = feed(
        size, comm, h1, cc, ct, w_co, w_fi, w_fo,
        (g_one, s_one, b_co, g_two, s_two, b_fo, g_three, s_three, b_fi), at_feed,
    )
    for name, flow in flows.items():
        if PLAN[name][0] in ("T0i", "T0p"):
            flow.array = gwi
    gib = gib.reshape(width, PAIR) if comm else gib.reshape(1, wide)

    if comm:
        at_cross = schedule_of(flows, 3)
        at_self = schedule_of(flows, 4)
    dm, dmo, gcvb, dh1, dsc, late, small_b, *early = cross_backward(
        block, cq, mkv, mkvo, dcc, cc, clse, t_own, m_own, m_oth, mem, mem_o, w_ckv,
        gco, dh2, h1, ctx, w_cq, w_so, g_one, s_one, at_cross,
    )
    for name, flow in flows.items():
        if PLAN[name][0] == "T1b":
            flow.array = late
    derivative, grad_memory, output, *made = self_backward(
        block, qkv, kvo, dsc, ctx, lse, t_own, t_oth, x, x_o, w_qkv, dh1, (small_a, small_b, gcvb, gib), dm, dmo, output, at_self
    )
    if comm:
        targets = {
            "T0i": [(0, wide, 2, 0, 0)],
            "T0o": [(wide + i * width, width, 3, i * narrow, 0) for i in range(4)],
            "T0p": [(wide + i * width, width, 3, i * narrow, 0) for i in range(4)],
            "T1a": [(0, width, 4, 0, 0), (width, 2 * width, 1, 0, 0)],
            "T1b": [(0, width, 5, 0, 0), (width, width, 6, 0, 0)],
            "G": [
                ((3 * pair + i) * PAIR, PAIR, 0, 0, i * width + pair * PAIR)
                for pair in range(width // PAIR)
                for i in range(3)
            ],
        }
        moves, line = [], None
        for n, (source, cols, *_) in enumerate(PLAN.values()):
            moves += [(n,) + m[1:] for m in moved([cols], targets[source])]
            if source == "G" and cols[0] <= 3 * width < sum(cols):
                line = n, 3 * width - cols[0]
        shapes = [(narrow, 3 * width), (narrow, 2 * width), (narrow, wide), (broad, width)] + [(narrow, width)] * 3
        t_qkv, t_cmem, t_fin, t_fout, t_cout, t_cquery, t_out, *vectors, lines, output, derivative, grad_memory = outputs(
            [f.array for f in flows.values()], moves, line, shapes, output, derivative, grad_memory
        )
    else:
        (early,), (made,) = early, made
        columns = made[:, 3 * width : 3 * width + PAIR]
        gqkv = made[:, : 3 * width].reshape(width, -1, 3, PAIR).swapaxes(1, 2).reshape(width, 3 * width)
        t_fin, t_fout, t_cout, t_cquery, t_out, t_cmem, t_qkv, lines = (
            sum_scatter(g, size, (0, 1, 2, 3))
            for g in (
                gwi, gwo[0], early[:, :width], late[:, :width], late[:, width:], early[:, width:], gqkv, columns
            )
        )
        lines = lines.T
    if not comm:
        vectors = [lines[i] for i in LINES]
    (t_gthree, t_sthree, t_fobias, t_gtwo, t_stwo, t_cobias, t_cqbias, t_gone, t_sone, t_obias, t_cvbias, t_qbias,
     t_vbias) = vectors
    if comm:
        t_fibias = lines[17:21].reshape(-1)
    else:
        t_fibias = lax.psum(lax.psum_scatter(gib[0], "dp", scatter_dimension=0, tiled=True), "sp")
    return (
        output[None],
        derivative[None],
        grad_memory[None],
        t_qkv,
        t_qbias,
        t_vbias,
        t_out,
        t_obias,
        t_gone,
        t_sone,
        t_cquery,
        t_cqbias,
        t_cmem,
        t_cvbias,
        t_cout,
        t_cobias,
        t_gtwo,
        t_stwo,
        t_fin,
        t_fibias,
        t_fout,
        t_fobias,
        t_gthree,
        t_sthree,
    )


def solution(mesh):
    split = P("dp", "sp", None)
    in_specs = (split, split, P("dp", "sp"), P("dp", "sp"), split) + (P(),) * 21
    matrix, vector = P("dp", None), P("dp")
    out_specs = (
        split, split, split,
        matrix, vector, vector,
        matrix, vector, vector, vector,
        matrix, vector,
        matrix, vector,
        matrix, vector, vector, vector,
        matrix, vector,
        matrix, vector, vector, vector,
    )
    return jax.shard_map(
        functools.partial(per_device, mesh.shape["dp"]),
        mesh=mesh, in_specs=in_specs, out_specs=out_specs, check_vma=False,
    )
```

```python
import functools

import jax
import jax.numpy as jnp
from jax import lax
from jax.experimental import pallas as pl
from jax.experimental.pallas import tpu as pltpu
from jax.sharding import PartitionSpec as P

HD = 64
PAIR = 2 * HD
EPS = 1e-05
FAR = 1.0e9
VMEM = 60 * 1024 * 1024
F32 = jnp.float32
BF16 = jnp.bfloat16


def nn(a, b):
    return lax.dot_general(a, b, (((1,), (0,)), ((), ())), preferred_element_type=F32)


def nt(a, b):
    return lax.dot_general(a, b, (((1,), (1,)), ((), ())), preferred_element_type=F32)


def tn(a, b):
    return lax.dot_general(a, b, (((0,), (0,)), ((), ())), preferred_element_type=F32)


def params(collective=None):
    if collective is None:
        return pltpu.CompilerParams(vmem_limit_bytes=VMEM)
    return pltpu.CompilerParams(
        vmem_limit_bytes=VMEM, collective_id=collective, has_side_effects=True
    )


def cost(flops, moved):
    return pl.CostEstimate(flops=int(flops), bytes_accessed=int(moved), transcendentals=0)


def normed(h):
    centred = h - jnp.mean(h, axis=-1, keepdims=True)
    rstd = lax.rsqrt(jnp.mean(centred * centred, axis=-1, keepdims=True) + EPS)
    return centred * rstd, rstd


def norm_back(grad, n, rstd, gain):
    scaled = grad * gain
    centre = jnp.mean(scaled, axis=-1, keepdims=True)
    along = jnp.mean(scaled * n, axis=-1, keepdims=True)
    return rstd * (scaled - centre - n * along)


def total(a):
    return jnp.sum(a.astype(F32), axis=0, keepdims=True)


def place():
    me = lax.axis_index("dp")
    return me, me % 2, (me // 2) % 2, me // 4, lax.axis_index("sp")


def flipped(at, hops):
    me, c, x, z, sp = at
    for hop in hops:
        if hop == "core":
            me, c = me + 1 - 2 * c, 1 - c
        elif hop == "x":
            me, x = me + 2 - 4 * x, 1 - x
        elif hop == "z1":
            me, z = me + 4 - 8 * (z % 2), z + 1 - 2 * (z % 2)
        elif hop == "z2":
            me, z = me + 8 - 16 * (z // 2), z + 2 - 4 * (z // 2)
        else:
            sp = 1 - sp
    return me, c, x, z, sp


def partner(hops, at=None):
    there = flipped(at or place(), hops)
    return {"dp": there[0], "sp": there[4]}


def greet(groups, at=None):
    groups = sorted({tuple("y" if h[0] == "y" else h for h in hops) for hops in groups})
    barrier = pltpu.get_barrier_semaphore()
    for hops in groups:
        pl.semaphore_signal(barrier, inc=1, device_id=partner(hops, at), device_id_type=pl.DeviceIdType.MESH)
    pl.semaphore_wait(barrier, len(groups))


def remote(src, dst, send, recv, hops, at=None):
    return pltpu.make_async_remote_copy(
        src_ref=src, dst_ref=dst, send_sem=send, recv_sem=recv,
        device_id=partner(hops, at), device_id_type=pl.DeviceIdType.MESH,
    )


PLAN = {
    "T0i_0": ("T0i", (0, 1536), ("z1", "x", "yr", "z2", "yg"), ((0, 5), (5, 7)), ((0, 3), (3, 5), (5, 7))),
    "T0i_1": ("T0i", (1536, 1536), ("x", "z1", "z2", "y"), ((0, 5), (5, 7)), ((0, 2), (2, 5))),
    "T0o_0": ("T0o", (3072, 1024), ("x", "z1", "z2", "y"), ((0, 3), (3, 5), (5, 6)), (), ((6, 9),)),
    "T0o_1": ("T0o", (4096, 1024), ("yr", "x", "z1", "z2", "yg"), ((0, 4), (4, 6), (6, 7)), ((0, 2),), ((6, 9),)),
    "T0o_2": ("T0o", (5120, 1024), ("z1", "x", "z2", "y"), ((0, 4), (4, 6), (6, 7)), (), ((6, 9),)),
    "T1a_0": ("T1a", (0, 1536), ("core", "z1", "x", "z2", "y"), ((6, 7),), ((0, 6), (6, 8), (8, 14), (14, 25))),
    "T1a_1": ("T1a", (1536, 768), ("core", "x", "z1", "z2", "y"), ((6, 7),), ((0, 2), (2, 5), (5, 7), (7, 9))),
    "T1b_0": ("T1b", (0, 1536), ("core", "x", "z1", "z2", "y"), (), ((0, 2), (2, 6), (6, 8), (8, 14), (14, 25))),
    "G1_0": ("G", (0, 768), ("core", "yr", "x", "z1", "z2", "yg"), (), ((5, 6), (6, 9), (9, 11), (11, 16), (16, 20), (20, 24))),
    "G2_0": ("G", (768, 768), ("core", "yr", "x", "z1", "z2", "yg"), (), ((7, 8), (8, 12), (12, 17), (17, 21), (21, 26), (26, 29))),
    "G3_0": ("G", (1536, 384), ("core", "z1", "x", "z2", "y"), (), ((8, 9), (9, 15), (15, 19), (19, 23), (23, 28))),
    "G4_0": ("G", (1920, 512), ("core", "x", "z1", "z2", "y"), (), ((9, 10), (10, 13), (13, 18), (18, 22), (22, 27))),
}
BLOCK = ("z2", "z1", "x", "core")


class Part:
    def __init__(self, hop, shape, dims, cols=None):
        self.hops = hops = hop if isinstance(hop, tuple) else (hop,)
        self.groups = [(h,) for h in hops] + ([hops] if len(hops) > 1 else [])
        self.dims = dims
        self.cols = cols or (0, shape[-1])
        self.shape = shape = tuple(shape[:-1]) + (self.cols[1],)
        for h in hops:
            if h in dims:
                at = dims.index(h)
                shape, dims = shape[:at] + shape[at + 1 :], dims[:at] + dims[at + 1 :]
            elif h != "y":
                shape = shape[:-1] + (shape[-1] // 2 if h == "yr" else 2 * shape[-1],)
        self.after, self.left = shape, dims
        self.came = self.shape if hops == ("yg",) else shape

    def share(self, at):
        _, c, x, z, sp = at
        first, wide = self.cols
        index = [slice(None)] * (len(self.shape) - 1) + [pl.ds(first, wide)]
        for h in self.hops:
            if h in self.dims:
                index[self.dims.index(h)] = {"core": c, "x": x, "z1": z % 2, "z2": z // 2}[h]
            elif h == "yr":
                half = wide // 2
                index[-1] = pl.ds(pl.multiple_of(first + sp * half, 128), half)
        return tuple(index)

    def copies(self, src, held, made, came, send, recv, local, at):
        out = [
            remote(src.at[self.share(flipped(at, g))], came[i], send.at[i], recv.at[i], g, at)
            for i, g in enumerate(self.groups)
        ]
        if not held:
            to = made.at[self.part_of(at[4])] if self.hops == ("yg",) else made
            out.append(pltpu.make_async_copy(src.at[self.share(at)], to, local))
        return out

    def part_of(self, sp):
        wide = self.shape[-1]
        return (slice(None),) * (len(self.shape) - 1) + (pl.ds(pl.multiple_of(sp * wide, 128), wide),)

    def add(self, src, held, made, came, at):
        if self.hops == ("yg",):
            if held:
                made[self.part_of(at[4])] = src[self.share(at)]
            made[self.part_of(1 - at[4])] = came[0][...]
        elif len(came) > 1:
            mine = src[self.share(at)] if held else made[...]
            one, two, three = (c[...].astype(F32) for c in came)
            made[...] = ((mine.astype(F32) + one) + (two + three)).astype(BF16)
        elif held:
            made[...] = src[self.share(at)] + came[0][...]
        else:
            made[...] += came[0][...]


class Flow:
    def __init__(self, array, shape, hops, dims=BLOCK, cols=None):
        self.array, self.shape, self.dims, self.cols = array, tuple(shape), dims, cols
        self.hops = list(hops)

    def step(self):
        part = Part(self.hops.pop(0), self.shape, self.dims, self.cols)
        self.shape, self.dims, self.cols = part.after, part.left, None
        return part


class Window:
    def __init__(self, start, stop, joint):
        self.start, self.stop, self.joint = start, stop, joint
        self.parts, self.sources, self.keeps = [], [], []


class Joint:
    def __init__(self):
        self.window = None


def plan(schedule):
    windows, arrays, latest = [], [], {}
    for n, (flows, start, stop, *joint) in enumerate(schedule):
        window = Window(start, stop, bool(joint))
        if joint:
            joint[0].window = n
        for i, flow in enumerate(flows):
            if flow in latest:
                source = ("part",) + latest[flow]
                before = windows[latest[flow][0]]
                before.keeps[latest[flow][1]] = False
            elif isinstance(flow.array, Joint):
                source = ("joint", flow.array.window)
            elif isinstance(flow.array, tuple):
                source = flow.array
            else:
                known = [k for k, a in enumerate(arrays) if a is flow.array]
                if not known:
                    arrays.append(flow.array)
                source = ("in", known[0] if known else len(arrays) - 1)
            window.parts.append(flow.step())
            window.sources.append(source)
            window.keeps.append(not joint)
            if not joint:
                latest[flow] = (n, i)
        windows.append(window)
    return windows, arrays, latest


def carrying(body, own, windows, arrays, grid, also, finale):
    ins, outs, held = own

    def kernel(*refs):
        refs = list(refs)

        def take(n):
            got = refs[:n]
            del refs[:n]
            return got

        my_in, arr = take(ins), take(arrays)
        my_out = take(outs)
        given = [[take(1)[0] if k else None for k in w.keeps] for w in windows]
        my_held = take(held)
        made, came, joints = [], [], []
        for w, g in zip(windows, given):
            if w.joint:
                joint, col, views = take(1)[0], 0, []
                for q in w.parts:
                    views.append(joint.at[(slice(None),) * (len(q.after) - 1) + (pl.ds(col, q.after[-1]),)])
                    col += q.after[-1]
                joints.append(joint)
                made.append(views)
            else:
                joints.append(None)
                made.append([ref if ref is not None else take(1)[0] for ref in g])
            came.append([take(len(q.groups)) for q in w.parts])
        mine = my_in + my_out + my_held
        step = pl.program_id(0)
        groups = [g for w in windows for q in w.parts for g in q.groups] + list(also)
        if groups:
            here = place()
            pl.when(step == 0)(lambda: greet(groups, here))
        if windows:
            send, recv, local = refs
        copies, sources, base = [], [], 0
        for w, m, c in zip(windows, made, came):
            now, froms = [], []
            for i, q in enumerate(w.parts):
                kind = w.sources[i]
                if kind[0] == "in":
                    src = arr[kind[1]]
                elif kind[0] == "ref":
                    src = mine[kind[1]]
                elif kind[0] == "joint":
                    src = joints[kind[1]]
                else:
                    src = made[kind[1]][kind[2]]
                held_here = kind[0] != "in"
                froms.append((src, held_here))
                now += q.copies(
                    src, held_here, m[i], c[i], send.at[base], recv.at[base], local.at[base], here
                )
                base += 1
            copies.append(now)
            sources.append(froms)

        def phase(number):
            for n, w in enumerate(windows):
                if w.stop == number:
                    for copy in copies[n]:
                        copy.wait()
                    for q, (src, held_here), m, c in zip(w.parts, sources[n], made[n], came[n]):
                        q.add(src, held_here, m, c, here)
            for n, w in enumerate(windows):
                if w.start == number:
                    for copy in copies[n]:
                        copy.start()

        used = sorted({w.start for w in windows} | {w.stop for w in windows})
        for number in used:
            if number < grid:
                pl.when(step == number)(functools.partial(phase, number))
        body(*mine)
        for number in used:
            if number >= grid:
                pl.when(step == grid - 1)(functools.partial(phase, number))
        if finale:
            pl.when(step == grid - 1)(lambda: finale(*mine))

    return kernel


def run(
    body, name, grid, ins, in_specs, outs, out_specs, held=(), schedule=(), collective=None,
    flops=0, moved=0, also=(), finale=None,
):
    in_specs, outs, out_specs, held = list(in_specs), list(outs), list(out_specs), list(held)
    windows, arrays, latest = plan(schedule)
    own = len(outs)
    kernel = carrying(body, (len(ins), own, len(held)), windows, len(arrays), grid, also, finale)
    in_specs += [pl.BlockSpec(memory_space=pl.ANY)] * len(arrays)
    order, count = [], 0
    for n, w in enumerate(windows):
        if w.joint:
            shape = w.parts[0].after[:-1] + (sum(q.after[-1] for q in w.parts),)
            held.append(pltpu.VMEM(shape, BF16))
        for i, (q, k) in enumerate(zip(w.parts, w.keeps)):
            if w.joint:
                continue
            if k:
                outs.append(jax.ShapeDtypeStruct(q.after, BF16))
                out_specs.append(whole(q.after))
                order.append((n, i))
            else:
                held.append(pltpu.VMEM(q.after, BF16))
        held += [pltpu.VMEM(q.came, BF16) for q in w.parts for _ in q.groups]
        count += len(w.parts)
    if windows:
        held += [pltpu.SemaphoreType.DMA((count, 3))] * 2 + [pltpu.SemaphoreType.DMA((count,))]
    results = pl.pallas_call(
        kernel,
        grid=(grid,),
        in_specs=in_specs,
        out_specs=out_specs,
        out_shape=outs,
        scratch_shapes=held,
        compiler_params=params(collective if windows or also else None),
        cost_estimate=cost(flops, moved),
        name=name,
    )(*ins, *arrays)
    for flow, where in latest.items():
        flow.array = results[own + order.index(where)]
    return results[:own]


def head_masks(dtype):
    lane = lax.broadcasted_iota(jnp.int32, (1, PAIR), 1)
    low = jnp.where(lane < HD, 1.0, 0.0)
    return low.astype(dtype), (1.0 - low).astype(dtype)


def query_code(code):
    lane = lax.broadcasted_iota(jnp.int32, code.shape, 1)
    return jnp.where(lane < 4, (code.astype(F32) - 1.0) * FAR, 0.0).astype(BF16)


def masked(s, diagonal):
    low, high = s[:-diagonal], s[-diagonal:]
    row = lax.broadcasted_iota(jnp.int32, high.shape, 0)
    col = lax.broadcasted_iota(jnp.int32, high.shape, 1)
    high = jnp.where(row <= col, high, -FAR)
    return jnp.concatenate([low, high], axis=0) if low.shape[0] else high


def softmax_over(jobs):
    results = []
    ready = nt(jobs[0][0], jobs[0][2])
    for n, (_, values_t, _, diagonal) in enumerate(jobs):
        s = ready
        if n + 1 < len(jobs):
            ready = nt(jobs[n + 1][0], jobs[n + 1][2])
        if diagonal:
            s = masked(s, diagonal)
        peak = jnp.max(s, axis=0, keepdims=True)
        e = jnp.exp(s - peak)
        norm = jnp.sum(e, axis=0, keepdims=True)
        results.append((nn(values_t, e.astype(BF16)) / norm, peak + jnp.log(norm)))
    return results


def pair_spec(rows, offset):
    return pl.BlockSpec((rows, PAIR), lambda p: (0, p + offset))


def whole(shape):
    return pl.BlockSpec(shape, lambda *_: (0,) * len(shape))


def delta_rows(g, o):
    prod = g.astype(F32) * o.astype(F32)
    upper = prod.astype(BF16)
    lower = (prod - upper.astype(F32)).astype(BF16)
    row = lax.broadcasted_iota(jnp.int32, (8, PAIR), 0)
    lane = lax.broadcasted_iota(jnp.int32, (8, PAIR), 1)
    pick = jnp.where(row == lane // HD, 1.0, 0.0).astype(BF16)
    return nt(pick, upper) + nt(pick, lower)


def back_pieces(jobs):
    def products(job):
        keys, values, q, g = job[:4]
        return nt(keys, q), nt(values, g)

    ready = products(jobs[0])
    for n, (_, _, _, _, lse, delta, causal) in enumerate(jobs):
        s, dp = ready
        if n + 1 < len(jobs):
            ready = products(jobs[n + 1])
        if causal:
            s = masked(s, s.shape[0])
        p = jnp.exp(s - lse)
        yield n, p.astype(BF16), (p * (dp - delta)).astype(BF16)


def cross_backward_kernel(
    size, pairs, q_ref, k_ref, v_ref, ko_ref, vo_ref, g_ref, o_ref, lse_ref, t_ref, own_ref, oth_ref,
    m_ref, mo_ref, wk_ref, wv_ref, gco_hbm, dh2_hbm, h1_hbm, ctx_hbm, wcq_hbm, wso_hbm, g1_ref, s1_ref,
    dm_out, dmo_out, gb_ref, dh1_ref, dsc_ref, late_ref, small_ref, grad_ref,
    dm_ref, dmo_acc, mt_ref, mot_ref, dcq_ref, dmo_ref, gco_ref, dh2_ref, h1_ref, ctx_ref, wcq_ref, wso_ref, move_ref,
):
    step = pl.program_id(0)
    rows, width = m_ref.shape
    lead = (slice(None),) * (len(grad_ref.shape) - 1)

    loads = [
        pltpu.make_async_copy(src, dst, move_ref.at[i])
        for i, (src, dst) in enumerate(
            (
                (gco_hbm, gco_ref), (dh2_hbm, dh2_ref), (h1_hbm, h1_ref), (ctx_hbm, ctx_ref), (wcq_hbm, wcq_ref),
                (wso_hbm, wso_ref),
            )
        )
    ]
    gives = [
        pltpu.make_async_copy(src, dst, move_ref.at[6 + i])
        for i, (src, dst) in enumerate(((dm_ref, dm_out), (dmo_ref, dmo_out)))
    ]

    def put(ref, col, grad):
        to = pl.ds(pl.multiple_of(col, PAIR), grad.shape[1])
        ref[lead + (to,)] = grad.astype(BF16).reshape(ref.shape[:-1] + (grad.shape[1],))

    @pl.when(step == 0)
    def _():
        for copy in loads:
            copy.start()
        mt_ref[...] = jnp.transpose(m_ref[...])
        mot_ref[...] = jnp.transpose(mo_ref[...])
        dm_ref[...] = jnp.zeros(dm_ref.shape, F32)
        dmo_acc[...] = jnp.zeros(dmo_acc.shape, F32)

    @pl.when(step == 1)
    def _():
        loads[0].wait()
        put(grad_ref, 0, gco_ref[...])

    @pl.when(step < pairs)
    def _():
        count = rows // size
        cols = pl.ds(pl.multiple_of(step * PAIR, PAIR), PAIR)
        sides = [(k_ref, v_ref, own_ref, mt_ref, dm_ref), (ko_ref, vo_ref, oth_ref, mot_ref, dmo_acc)]
        blocks = list(backward_pieces(size, q_ref, g_ref, o_ref, lse_ref, t_ref))
        weights = jnp.concatenate([wk_ref[...], wv_ref[...]], axis=1)
        jobs, where, turned = [], [], []
        for side, (kr, vr, code, _, _) in enumerate(sides):
            keys = jnp.concatenate([kr[...], code[...]], axis=1)
            turned.append(jnp.transpose(kr[...]))
            for block, head, qm, gm, q, lse, delta in blocks:
                jobs.append((keys, vr[...], q, gm, lse, delta, False))
                where.append((side, block, head, qm, gm))
        dq = [[0.0, 0.0] for _ in range(count)]
        dk, dv = [0.0, 0.0], [0.0, 0.0]
        grad = gb = 0.0
        for n, p, ds in back_pieces(jobs):
            side, block, head, qm, gm = where[n]
            dk[side] = dk[side] + nn(ds, qm)
            dv[side] = dv[side] + nn(p, gm)
            dq[block][head] = dq[block][head] + nn(turned[side][head * HD : (head + 1) * HD], ds)
            if n + 1 == len(jobs) or where[n + 1][0] != side:
                both = jnp.concatenate([dk[side].astype(BF16), dv[side].astype(BF16)], axis=1)
                mem, acc = sides[side][3:]
                grad = grad + nn(mem[...], both)
                gb = gb + total(both[:, PAIR:])
                acc[...] += nt(both, weights)
        for block in range(count):
            dcq_ref[block * size : (block + 1) * size, cols] = upright(dq[block]).astype(BF16)
        put(grad_ref, width + step * PAIR, grad[:, :PAIR])
        put(grad_ref, 2 * width + step * PAIR, grad[:, PAIR:])
        gb_ref[:, cols] = gb

    @pl.when(step == pairs)
    def _():
        dmo_ref[...] = dmo_acc[...].astype(BF16)
        for copy in gives:
            copy.start()
        for copy in loads[1:]:
            copy.wait()
        gain = line(g1_ref)
        n1, r1 = normed(h1_ref[...])
        a1b = (n1 * gain + line(s1_ref)).astype(BF16)
        dcq = dcq_ref[...]
        d1 = dh2_ref[...] + nt(dcq, wcq_ref[...])
        dh1 = norm_back(d1, n1, r1, gain)
        dh1_ref[...] = dh1
        dso = dh1.astype(BF16)
        dsc_ref[...] = nt(dso, wso_ref[...]).astype(BF16)
        put(late_ref, 0, tn(a1b, dcq))
        put(late_ref, width, tn(ctx_ref[...], dso))
        small_ref[0:1] = total(dcq)
        small_ref[1:2] = total(d1 * n1)
        small_ref[2:3] = total(d1)
        small_ref[3:4] = total(dso)
        small_ref[4:8] = jnp.zeros((4, width), F32)
        for copy in gives:
            copy.wait()


MIDDLE = 30


def cross_backward(block, cq, kv, kvo, g, o, lse, t, own, oth, m, mo, w, gco, dh2, h1, ctx, wcq, wso, gain, shift, schedule):
    rows, width = cq.shape
    pairs = width // PAIR

    def pair_of(size, offset):
        return pl.BlockSpec((size, PAIR), lambda s: (0, jnp.minimum(s, pairs - 1) + offset))

    flat, square = whole((rows, width)), whole((width, width))
    outs = [
        jax.ShapeDtypeStruct((rows, width), F32),
        jax.ShapeDtypeStruct((rows, width), BF16),
        jax.ShapeDtypeStruct((1, width), F32),
        jax.ShapeDtypeStruct((rows, width), F32),
        jax.ShapeDtypeStruct((rows, width), BF16),
        jax.ShapeDtypeStruct(block + (2 * width,), BF16),
        jax.ShapeDtypeStruct((8, width), F32),
    ]
    far = pl.BlockSpec(memory_space=pl.ANY)
    specs = [far, far, whole((1, width)), flat, flat, whole(block + (2 * width,)), whole((8, width))]
    held = []
    if schedule:
        held.append(pltpu.VMEM(block + (3 * width,), BF16))
    else:
        outs.append(jax.ShapeDtypeStruct(block + (3 * width,), BF16))
        specs.append(whole(block + (3 * width,)))
    held += [
        pltpu.VMEM((rows, width), F32),
        pltpu.VMEM((rows, width), F32),
        pltpu.VMEM((width, rows), BF16),
        pltpu.VMEM((width, rows), BF16),
        pltpu.VMEM((rows, width), BF16),
        pltpu.VMEM((rows, width), BF16),
    ]
    held += [pltpu.VMEM(a.shape, a.dtype) for a in (gco, dh2, h1, ctx, wcq, wso)] + [pltpu.SemaphoreType.DMA((8,))]
    return run(
        functools.partial(cross_backward_kernel, 256, pairs), "cross_backward", pairs + 1,
        (cq, kv, kv, kvo, kvo, g, o, lse, t, own, oth, m, mo, w, w, gco, dh2, h1, ctx, wcq, wso, gain, shift),
        [
            pair_of(rows, 0), pair_of(rows, 0), pair_of(rows, pairs), pair_of(rows, 0), pair_of(rows, pairs),
            pair_of(rows, 0), pair_of(rows, 0),
            pl.BlockSpec((8, rows), lambda s: (jnp.minimum(s, pairs - 1), 0)),
            whole((rows, 128)), whole((rows, 128)), whole((rows, 128)), flat, flat,
            pair_of(width, 0), pair_of(width, pairs),
            far, far, far, far, far, far, whole(gain.shape), whole(shift.shape),
        ],
        outs, specs, held, schedule, 3,
        64 * rows * rows * width + 24 * rows * width * width, 40 * rows * width,
    )


def upright(heads):
    return jnp.transpose(jnp.concatenate(heads, axis=0) * HD**-0.5)


def backward_pieces(size, q_ref, g_ref, o_ref, lse_ref, own_ref):
    masks = head_masks(BF16)
    scale = BF16(HD**-0.5)
    qcode = query_code(own_ref[...])
    delta = delta_rows(g_ref[...], o_ref[...])
    for block in range(q_ref.shape[0] // size):
        at = slice(block * size, (block + 1) * size)
        for head, mask in enumerate(masks):
            qm = q_ref[at] * (mask * scale)
            gm = g_ref[at] * mask
            q = jnp.concatenate([qm, qcode[at]], axis=1)
            yield block, head, qm, gm, q, lse_ref[head : head + 1, at], delta[head : head + 1, at]


def self_backward_kernel(
    size, *refs,
):
    (q2_ref, ko_ref, vo_ref, g2_ref, o2_ref, lse2_ref, wk2_ref, wv2_ref,
     q_ref, k_ref, v_ref, g_ref, o_ref, lse_ref, wq_ref, wk_ref, wv_ref,
     own_ref, oth_ref, x_ref, xo_ref, dh1_ref, sa_ref, sb_ref, sc_ref, sd_ref, dm_hbm, dmo_hbm, out_hbm,
     dx_out, dm_out, out_out, grad_ref,
     dq_acc, dx_acc, dxo_acc, dkv_acc, xt_ref, xot_ref, dxo_ref, came_ref, memory_ref, dm_ref, gm_ref, dx_ref, turn_ref,
     send_ref, recv_ref) = refs
    step = pl.program_id(0)
    second = lax.axis_index("dp") % 2 == 1
    rows, width = x_ref.shape
    pairs = width // PAIR
    early = pairs // 2
    count = rows // size
    over = remote(dxo_ref, came_ref, send_ref.at[0], recv_ref.at[0], ("core",))
    m_over = remote(dmo_hbm, memory_ref, send_ref.at[1], recv_ref.at[1], ("core",))
    dm_load = pltpu.make_async_copy(dm_hbm, dm_ref, send_ref.at[5])

    @pl.when(step == 0)
    def _():
        m_over.start()
        dm_load.start()
        Swap(out_hbm, out_out, send_ref.at[2], recv_ref.at[2]).start()
        xt_ref[...] = jnp.transpose(x_ref[...])
        turn_ref[...] = jnp.zeros(turn_ref.shape, F32)
        turn_ref[0:8] = sa_ref[...]
        turn_ref[8:16] = sb_ref[...]
        turn_ref[16:17] = sc_ref[...]
        dx_acc[...] = dh1_ref[...]

    @pl.when(jnp.logical_and(step == 0, second))
    def _():
        xot_ref[...] = jnp.transpose(xo_ref[...])
        dxo_acc[...] = jnp.zeros(dxo_acc.shape, F32)

    @pl.when(jnp.logical_and(step == 0, jnp.logical_not(second)))
    def _():
        dq_acc[...] = jnp.zeros(dq_acc.shape, F32)
        dkv_acc[...] = jnp.zeros(dkv_acc.shape, BF16)
        xot_ref[...] = jnp.zeros(xot_ref.shape, BF16)

    @pl.when(jnp.logical_and(step < early, second))
    def _():
        jobs, where, turned = [], [], []
        for two in range(2):
            at = slice(two * PAIR, (two + 1) * PAIR)
            keys = jnp.concatenate([ko_ref[:, at], oth_ref[...]], axis=1)
            turned.append(jnp.transpose(ko_ref[:, at]))
            stats = lse2_ref.at[8 * two : 8 * two + 8]
            for block, head, qm, gm, q, lse, delta in backward_pieces(
                size, q2_ref.at[:, at], g2_ref.at[:, at], o2_ref.at[:, at], stats, own_ref
            ):
                jobs.append((keys, vo_ref[:, at], q, gm, lse, delta, False))
                where.append((two, block, head, qm, gm))
        dk, dv = [0.0, 0.0], [0.0, 0.0]
        for n, p, ds in back_pieces(jobs):
            two, block, head, qm, gm = where[n]
            dk[two] = dk[two] + nn(ds, qm)
            dv[two] = dv[two] + nn(p, gm)
            of_head = slice(head * HD, (head + 1) * HD)
            dq_acc[2 * step + two, of_head, block * size : (block + 1) * size] = nn(turned[two][of_head], ds)
        for two in range(2):
            at = slice(two * PAIR, (two + 1) * PAIR)
            both = jnp.concatenate([dk[two].astype(BF16), dv[two].astype(BF16)], axis=1)
            dkv_acc[2 * step + two] = both
            dxo_acc[...] += nt(both, jnp.concatenate([wk2_ref[:, at], wv2_ref[:, at]], axis=1))

    @pl.when(jnp.logical_and(step == early - 1, second))
    def _():
        dxo_ref[...] = dxo_acc[...].astype(BF16)
        over.start()

    @pl.when(step == early)
    def _():
        m_over.wait()
        dm_load.wait()
        gm_ref[...] = (dm_ref[...] + memory_ref[...].astype(F32)).astype(BF16)
        Swap(gm_ref, dm_out, send_ref.at[3], recv_ref.at[3]).start()

    @pl.when(step >= early)
    def _():
        pair = step - early
        cols = pl.ds(pl.multiple_of(pair * PAIR, PAIR), PAIR)
        dkvo = dkv_acc[pair]
        grad_o = nn(xot_ref[...], dkvo)
        turned = jnp.transpose(k_ref[...])
        dq = [[0.0, 0.0] for _ in range(count)]
        dk, dv = [0.0] * count, [0.0] * count
        jobs, where = [], []
        keys = jnp.concatenate([k_ref[...], own_ref[...]], axis=1)
        for block, head, qm, gm, q, lse, delta in backward_pieces(size, q_ref, g_ref, o_ref, lse_ref, own_ref):
            for part in range(block + 1):
                of = slice(part * size, (part + 1) * size)
                jobs.append((keys[of], v_ref[of], q, gm, lse, delta, part == block))
                where.append((block, part, head, qm, gm))
        for n, p, ds in back_pieces(jobs):
            block, part, head, qm, gm = where[n]
            of = slice(part * size, (part + 1) * size)
            dk[part] = dk[part] + nn(ds, qm)
            dv[part] = dv[part] + nn(p, gm)
            dq[block][head] = dq[block][head] + nn(turned[head * HD : (head + 1) * HD, of], ds)
        dk, dv = (jnp.concatenate(a, axis=0).astype(BF16) for a in (dk, dv))
        before = dq_acc[pair]
        dq = jnp.concatenate(
            [
                upright(
                    [
                        part + before[head * HD : (head + 1) * HD, block * size : (block + 1) * size]
                        for head, part in enumerate(parts)
                    ]
                )
                for block, parts in enumerate(dq)
            ],
            axis=0,
        ).astype(BF16)
        dkv = jnp.concatenate([dk, dv], axis=1)
        grad_kv = nn(xt_ref[...], dkv) + grad_o
        grad_q = nn(xt_ref[...], dq)
        dx_acc[...] += nt(dkv, jnp.concatenate([wk_ref[...], wv_ref[...]], axis=1)) + nt(dq, wq_ref[...])
        lead = (slice(None),) * (len(grad_ref.shape) - 1)
        for n, grad in enumerate((grad_q, grad_kv[:, :PAIR], grad_kv[:, PAIR:])):
            to = pl.ds(pl.multiple_of((pair * 3 + n) * PAIR, PAIR), PAIR)
            grad_ref[lead + (to,)] = grad.astype(BF16).reshape(grad_ref.shape[:-1] + (PAIR,))
        turn_ref[21:22, cols] = total(dq)
        turn_ref[22:23, cols] = total(dv) + total(dkvo[:, PAIR:])

    @pl.when(step == early + pairs - 1)
    def _():
        shape = grad_ref.shape[:-1] + (PAIR,)
        lead = (slice(None),) * (len(shape) - 1)
        columns = jnp.transpose(turn_ref[...])
        if sd_ref.shape == columns.shape:
            columns = columns + sd_ref[...]
        grad_ref[lead + (slice(3 * width, 3 * width + PAIR),)] = columns.astype(BF16).reshape(shape)

        @pl.when(second)
        def _():
            over.wait_send()
            dx_ref[...] = dx_acc[...].astype(BF16)

        @pl.when(jnp.logical_not(second))
        def _():
            over.wait_recv()
            dx_ref[...] = (dx_acc[...] + came_ref[...].astype(F32)).astype(BF16)

        Swap(dx_ref, dx_out, send_ref.at[4], recv_ref.at[4]).start()


def self_backward_finale(*refs):
    out_hbm, dx_out, dm_out, out_out = refs[28:32]
    gm_ref, dx_ref, _, send_ref, recv_ref = refs[43:48]
    Swap(out_hbm, out_out, send_ref.at[2], recv_ref.at[2]).wait()
    Swap(gm_ref, dm_out, send_ref.at[3], recv_ref.at[3]).wait()
    Swap(dx_ref, dx_out, send_ref.at[4], recv_ref.at[4]).wait()


GRADS = 32


def self_backward(block, qkv, kvo, g, o, lse, own, oth, x, xo, w, dh1, small, dm, dmo, out, schedule):
    rows, width = x.shape
    pairs = width // PAIR
    early = pairs // 2

    def two_of(size, offset):
        return pl.BlockSpec((size, 2 * PAIR), lambda s: (0, jnp.minimum(s, early - 1) + offset))

    def pair_of(size, offset):
        return pl.BlockSpec((size, PAIR), lambda s: (0, jnp.maximum(s - early, 0) + offset))

    made = block + (3 * width + PAIR,)
    far = pl.BlockSpec(memory_space=pl.ANY)
    outs = [jax.ShapeDtypeStruct((rows, width), BF16)] * 3
    specs = [far] * 3
    held = []
    if schedule:
        held += [pltpu.VMEM(made, BF16)]
    else:
        outs += [jax.ShapeDtypeStruct(made, BF16)]
        specs += [whole(made)]
    held += [
        pltpu.VMEM((pairs, PAIR, rows), F32),
        pltpu.VMEM((rows, width), F32),
        pltpu.VMEM((rows, width), F32),
        pltpu.VMEM((pairs, rows, 2 * PAIR), BF16),
        pltpu.VMEM((width, rows), BF16),
        pltpu.VMEM((width, rows), BF16),
        pltpu.VMEM((rows, width), BF16),
        pltpu.VMEM((rows, width), BF16),
        pltpu.VMEM((rows, width), BF16),
        pltpu.VMEM((rows, width), F32),
        pltpu.VMEM((rows, width), BF16),
        pltpu.VMEM((rows, width), BF16),
        pltpu.VMEM((PAIR, width), F32),
        pltpu.SemaphoreType.DMA((6,)),
        pltpu.SemaphoreType.DMA((5,)),
    ]
    return run(
        functools.partial(self_backward_kernel, 256), "self_backward", early + pairs,
        (qkv, kvo, kvo, g, o, lse, w, w, qkv, qkv, qkv, g, o, lse, w, w, w, own, oth, x, xo, dh1) + tuple(small) + (dm, dmo, out),
        [
            two_of(rows, 0), two_of(rows, 0), two_of(rows, early), two_of(rows, 0), two_of(rows, 0),
            pl.BlockSpec((16, rows), lambda s: (jnp.minimum(s, early - 1), 0)),
            two_of(width, early), two_of(width, 2 * early),
            pair_of(rows, 0), pair_of(rows, pairs), pair_of(rows, 2 * pairs), pair_of(rows, 0), pair_of(rows, 0),
            pl.BlockSpec((8, rows), lambda s: (jnp.maximum(s - early, 0), 0)),
            pair_of(width, 0), pair_of(width, pairs), pair_of(width, 2 * pairs),
            whole((rows, 128)), whole((rows, 128)), whole((rows, width)), whole((rows, width)), whole((rows, width)),
        ] + [whole(a.shape) for a in small] + [far] * 3,
        outs, specs, held, schedule, 5,
        48 * rows * rows * width + 20 * rows * width * width, 12 * width * width + 40 * rows * width,
        (("core",), ("core", "y")), self_backward_finale,
    )


def code_of(docs_ref):
    row = lax.broadcasted_iota(jnp.int32, (PAIR, docs_ref.shape[1]), 0)
    return jnp.transpose(jnp.where(docs_ref[...] == row, 1.0, 0.0)).astype(BF16)


def line(ref):
    return ref[...].astype(F32)[None, :]


def moving():
    return lax.axis_index("dp") % 2 != lax.axis_index("sp")


class Swap:
    def __init__(self, src, dst, send, recv):
        self.there = remote(src, dst, send, recv, ("core", "y"))
        self.here = pltpu.make_async_copy(src, dst, recv)

    def start(self):
        pl.when(moving())(self.there.start)
        pl.when(jnp.logical_not(moving()))(self.here.start)

    def wait_recv(self):
        pl.when(moving())(self.there.wait_recv)
        pl.when(jnp.logical_not(moving()))(self.here.wait)

    def wait_send(self):
        pl.when(moving())(self.there.wait_send)

    def wait(self):
        self.wait_send()
        self.wait_recv()


def front_kernel(
    size, x_hbm, m_hbm, c_hbm, td_hbm, md_hbm, wx_hbm, wm_hbm, wo_hbm, wq_hbm,
    bq_ref, bv_ref, bcv_ref, bso_ref, g_ref, s_ref, bcq_ref,
    qkv_out, mkv_out, kvo_out, mkvo_out, cq_out, ctx_out, cc_out, h_out, xo_out, mo_out, x_out, m_out, c_out,
    lse_ref, clse_ref, tt_ref, mt_ref, to_ref, mo_ref,
    x_ref, m_ref, wx_ref, wm_ref, wo_ref, wq_ref, xc_ref, mc_ref, td_ref, md_ref, tdc_ref, mdc_ref,
    qkv_ref, mkv_ref, kvo_ref, mkvo_ref, cq_ref, ctx_ref, cc_ref, h_ref, acc_ref,
    load_ref, store_ref, send_ref, recv_ref,
):
    rows, width = x_ref.shape
    pairs = width // PAIR
    second = lax.axis_index("dp") % 2 == 1
    first = jnp.logical_not(second)
    masks = head_masks(BF16)
    scale = BF16(HD**-0.5)
    loads = [
        pltpu.make_async_copy(src, dst, load_ref.at[i])
        for i, (src, dst) in enumerate(((wx_hbm, wx_ref), (wm_hbm, wm_ref), (wo_hbm, wo_ref), (wq_hbm, wq_ref)))
    ]
    give = [
        pltpu.make_async_copy(src, dst, store_ref.at[i])
        for i, (src, dst) in enumerate(
            (
                (qkv_ref, qkv_out), (mkv_ref, mkv_out), (mkvo_ref, mkvo_out), (cq_ref, cq_out), (ctx_ref, ctx_out),
                (cc_ref, cc_out), (h_ref, h_out), (mc_ref, mo_out), (x_ref, x_out), (m_ref, m_out),
                (kvo_ref, kvo_out), (xc_ref, xo_out),
            )
        )
    ]
    swaps = [
        Swap(src, dst, send_ref.at[i], recv_ref.at[i])
        for i, (src, dst) in enumerate(
            ((td_hbm, td_ref), (md_hbm, md_ref), (m_hbm, m_ref), (c_hbm, c_out))
            + tuple((x_hbm.at[at], x_ref.at[at]) for at in (pl.ds(0, rows // 2), pl.ds(rows // 2, rows // 2)))
        )
    ]
    x_over = remote(x_ref, xc_ref, send_ref.at[6], recv_ref.at[6], ("core",))
    m_over = remote(m_ref, mc_ref, send_ref.at[7], recv_ref.at[7], ("core",))
    docs = [
        remote(td_ref, tdc_ref, send_ref.at[8], recv_ref.at[8], ("core",)),
        remote(md_ref, mdc_ref, send_ref.at[9], recv_ref.at[9], ("core",)),
    ]
    for copy in loads:
        copy.start()
    greet([("core", "y"), ("core",)])
    for copy in swaps[:2] + swaps[4:]:
        copy.start()

    def columns(offset, pair):
        return pl.ds(pl.multiple_of(offset + pair * PAIR, PAIR), PAIR)

    def heads(source, offset, pair, code, block):
        at = slice(block * size, (block + 1) * size)
        q = source[at, columns(offset, pair)]
        return [jnp.concatenate([q * (mask * scale), code[at]], axis=1) for mask in masks]

    def keep(block, pair, outs, lses, lse_out, out):
        at = slice(block * size, (block + 1) * size)
        mixed = jnp.concatenate(outs, axis=0)
        acc_ref[pair, :, at] = mixed
        out[at, columns(0, pair)] = jnp.transpose(mixed).astype(BF16)
        row = lax.broadcasted_iota(jnp.int32, (8, size), 0)
        lse_out[pl.ds(pl.multiple_of(pair * 8, 8), 8), at] = jnp.where(row == 0, lses[0], lses[1])

    def begin(block, pair, results, lse_out, out):
        keep(block, pair, [r for r, _ in results], [lse for _, lse in results], lse_out, out)

    def merge(block, pair, results, lse_out, out):
        at = slice(block * size, (block + 1) * size)
        stats = lse_out[pl.ds(pl.multiple_of(pair * 8, 8), 8), at]
        outs, lses = [], []
        for head, (r, lse) in enumerate(results):
            before = acc_ref[pair, head * HD : (head + 1) * HD, at]
            old = stats[head : head + 1]
            peak = jnp.maximum(old, lse)
            both = peak + jnp.log(jnp.exp(old - peak) + jnp.exp(lse - peak))
            outs.append(before * jnp.exp(old - both) + r * jnp.exp(lse - both))
            lses.append(both)
        keep(block, pair, outs, lses, lse_out, out)

    def halves(values):
        turned = jnp.transpose(values)
        return turned[:HD], turned[HD:]

    waiting = jnp.logical_and(second, moving())

    def other_keys():
        for n, bias in enumerate((0.0, line(bv_ref))):
            cols = slice(n * width, (n + 1) * width)
            from_cols = slice((n + 1) * width, (n + 2) * width)
            kvo_ref[:, cols] = (nn(xc_ref[...], wx_ref[:, from_cols]) + bias).astype(BF16)
        give[10].start()

    def other_memory():
        for n, bias in enumerate((0.0, line(bcv_ref))):
            cols = slice(n * width, (n + 1) * width)
            mkvo_ref[:, cols] = (nn(mc_ref[...], wm_ref[:, cols]) + bias).astype(BF16)
        give[2].start()

    @pl.when(jnp.logical_not(moving()))
    def _():
        swaps[2].start()
        swaps[4].wait()
        swaps[5].wait()
        pl.when(first)(x_over.start)
        swaps[2].wait()
        m_over.start()

    for copy in swaps[:2]:
        copy.wait_recv()
    for copy in docs:
        copy.start()
    to_ref[...] = code_of(td_ref)
    mo_ref[...] = code_of(md_ref)
    loads[0].wait()
    loads[1].wait()

    @pl.when(waiting)
    def _():
        x_over.wait_recv()
        give[11].start()
        other_keys()
        m_over.wait_recv()
        give[7].start()
        other_memory()

    for half, copy in enumerate(swaps[4:]):
        pl.when(moving())(copy.wait)
        at = slice(half * rows // 2, (half + 1) * rows // 2)
        if half:

            @pl.when(moving())
            def _():
                swaps[2].start()
                pl.when(first)(x_over.start)

            give[8].start()
        for n, bias in enumerate((line(bq_ref), 0.0, line(bv_ref))):
            cols = slice(n * width, (n + 1) * width)
            qkv_ref[at, cols] = (nn(x_ref[at], wx_ref[:, cols]) + bias).astype(BF16)
    give[0].start()

    def attend(query, keys_ref, key_at, value_at, key_code, diagonal, finish, stats, out):
        @pl.loop(0, pairs // 3)
        def _(third):
            code = query_code(to_ref[...])
            jobs, where = [], []
            for pair in (3 * third, 3 * third + 1, 3 * third + 2):
                keys = jnp.concatenate([keys_ref[:, columns(key_at, pair)], key_code[...]], axis=1)
                values = halves(keys_ref[:, columns(value_at, pair)])
                for block in range(rows // size):
                    end = (block + 1) * size if diagonal else rows
                    for q, v in zip(heads(query, 0, pair, code, block), values):
                        jobs.append((keys[:end], v[:, :end], q, size if diagonal else 0))
                    where.append((block, pair))
            results = softmax_over(jobs)
            for n, (block, pair) in enumerate(where):
                finish(block, pair, results[2 * n : 2 * n + 2], stats, out)

    attend(qkv_ref, qkv_ref, width, 2 * width, to_ref, True, begin, lse_ref, ctx_ref)

    for copy in docs:
        copy.wait()
    tt_ref[...] = code_of(tdc_ref)
    mt_ref[...] = code_of(mdc_ref)
    @pl.when(moving())
    def _():
        swaps[2].wait()
        m_over.start()

    swaps[3].start()
    give[9].start()
    pl.when(first)(x_over.wait_send)

    @pl.when(jnp.logical_and(second, jnp.logical_not(waiting)))
    def _():
        x_over.wait_recv()
        give[11].start()
        other_keys()

    @pl.when(second)
    def _():
        attend(qkv_ref, kvo_ref, 0, width, tt_ref, False, merge, lse_ref, ctx_ref)

    give[4].start()
    loads[2].wait()
    loads[3].wait()
    h = x_ref[...].astype(F32) + nn(ctx_ref[...], wo_ref[...]) + line(bso_ref)
    h_ref[...] = h
    n, _ = normed(h)
    a = (n * line(g_ref) + line(s_ref)).astype(BF16)
    cq_ref[...] = (nn(a, wq_ref[...]) + line(bcq_ref)).astype(BF16)
    give[6].start()
    give[3].start()

    for n, bias in enumerate((0.0, line(bcv_ref))):
        cols = slice(n * width, (n + 1) * width)
        mkv_ref[:, cols] = (nn(m_ref[...], wm_ref[:, cols]) + bias).astype(BF16)
    give[1].start()
    attend(cq_ref, mkv_ref, 0, width, mo_ref, False, begin, clse_ref, cc_ref)
    m_over.wait_send()

    @pl.when(jnp.logical_not(waiting))
    def _():
        m_over.wait_recv()
        give[7].start()
        other_memory()

    attend(cq_ref, mkvo_ref, 0, width, mt_ref, False, merge, clse_ref, cc_ref)
    give[5].start()
    for copy in give[:10]:
        copy.wait()
    for copy in swaps[:2]:
        copy.wait_send()
    swaps[3].wait()

    @pl.when(second)
    def _():
        give[10].wait()
        give[11].wait()


def front(x, mem, ct, td, md, wx, wm, wo, wq, vectors):
    rows, width = x.shape
    pairs = width // PAIR

    def flat(n):
        return jax.ShapeDtypeStruct((rows, n * width), BF16)

    stats = jax.ShapeDtypeStruct((8 * pairs, rows), F32)
    code = jax.ShapeDtypeStruct((rows, PAIR), BF16)
    far = pl.BlockSpec(memory_space=pl.ANY)
    near = pl.BlockSpec(memory_space=pltpu.VMEM)
    tall = jax.ShapeDtypeStruct((rows, width), F32)
    held = [flat(3), flat(2), flat(2), flat(2), flat(1), flat(1), flat(1), tall]
    return pl.pallas_call(
        functools.partial(front_kernel, 256),
        in_specs=[far] * 9 + [near] * len(vectors),
        out_specs=[far] * 13 + [near] * 6,
        out_shape=[flat(3), flat(2), flat(2), flat(2), flat(1), flat(1), flat(1), tall] + [flat(1)] * 5
        + [stats, stats, code, code, code, code],
        scratch_shapes=[pltpu.VMEM((rows, width), BF16)] * 2
        + [pltpu.VMEM(w.shape, BF16) for w in (wx, wm, wo, wq)]
        + [pltpu.VMEM((rows, width), BF16)] * 2
        + [pltpu.VMEM((1, rows), jnp.int32)] * 4
        + [pltpu.VMEM(a.shape, a.dtype) for a in held]
        + [
            pltpu.VMEM((pairs, PAIR, rows), F32),
            pltpu.SemaphoreType.DMA((4,)),
            pltpu.SemaphoreType.DMA((12,)),
            pltpu.SemaphoreType.DMA((10,)),
            pltpu.SemaphoreType.DMA((10,)),
        ],
        compiler_params=params(1),
        cost_estimate=cost(22 * rows * width * width + 36 * rows * rows * width, 60 * rows * width),
        name="front",
    )(x, mem, ct, td, md, wx, wm, wo, wq, *vectors)


def feed_kernel(
    count, comm, h1_ref, cc_ref, ct_ref, wco_ref, wi_ref, wo_ref,
    g1_ref, s1_ref, bco_ref, g2_ref, s2_ref, bfo_ref, g3_ref, s3_ref, bfi_ref, out_ref, dh2_ref, dcc_ref, gco_ref, *refs,
):
    if comm:
        gwi_ref, refs = refs[0], refs[1:]
    else:
        gwi_ref, gwo_ref, refs = refs[0], refs[1], refs[2:]
    small_ref, gib_ref, hid_ref, slope_ref, n2_ref, r2_ref, a2b_ref, acc_ref, df_ref, bias_ref, *refs = refs
    step = pl.program_id(0)
    width = acc_ref.shape[1]

    if comm:
        mi_ref, mo_ref, ci_ref, co_ref, send_ref, recv_ref = refs
        wide = ci_ref.shape[-1]
        here = place()
        c = here[1]

        def chunk_copies(j):
            at = pl.ds(pl.multiple_of(j * width, width), width)
            return remote(mi_ref.at[:, :, at], ci_ref.at[:, :, at], send_ref.at[0, j], recv_ref.at[0, j], ("core",), here)

        def block_copies(j):
            return remote(mo_ref.at[j], co_ref.at[j], send_ref.at[1, j], recv_ref.at[1, j], ("core",), here)

        def place_of(j, i):
            return (j // 2, j % 2, slice(None), slice(None), slice(wide + i * width, wide + (i + 1) * width))

    @pl.when(step == 0)
    def _():
        wide = bfi_ref[...].astype(F32)
        for i in range(count):
            bias_ref[i : i + 1] = wide[None, i * width : (i + 1) * width]
        n1, _ = normed(h1_ref[...])
        a1 = n1 * line(g1_ref) + line(s1_ref)
        h2 = a1 + nn(cc_ref[...], wco_ref[...]) + line(bco_ref)
        n2, r2 = normed(h2)
        n2_ref[...] = n2
        r2_ref[...] = jnp.broadcast_to(r2, r2_ref.shape)
        a2 = n2 * line(g2_ref) + line(s2_ref)
        a2b_ref[...] = a2.astype(BF16)
        acc_ref[...] = a2 + line(bfo_ref)

    piece = 2 * PAIR
    pieces = [slice(i, i + piece) for i in range(0, width, piece)]

    @pl.when(step < count)
    def _():
        def product(at):
            return nn(a2b_ref[...], wi_ref[:, at])

        bias = bias_ref[pl.ds(step, 1)]
        ready = product(pieces[0])
        more = 0.0
        for i, at in enumerate(pieces):
            u = ready + bias[:, at]
            if i + 1 < len(pieces):
                ready = product(pieces[i + 1])
            cumul = 0.5 * (1.0 + lax.erf(u * 0.7071067811865476))
            density = jnp.exp(-0.5 * u * u) * 0.3989422804014327
            hid = (u * cumul).astype(BF16)
            hid_ref[step, :, at] = hid
            slope_ref[step, :, at] = cumul + u * density
            more = more + nn(hid, wo_ref[at])
        acc_ref[...] += more

    @pl.when(step == count - 1)
    def _():
        n3, r3 = normed(acc_ref[...])
        gain = line(g3_ref)
        out_ref[...] = (n3 * gain + line(s3_ref)).astype(BF16)
        e = ct_ref[...].astype(F32)
        d3 = norm_back(e, n3, r3, gain)
        df = d3.astype(BF16)
        df_ref[...] = df
        acc_ref[...] = d3
        small_ref[0:1] = total(e * n3)
        small_ref[1:2] = total(e)
        small_ref[2:3] = total(df)

    @pl.when(jnp.logical_and(step >= count, step < 2 * count))
    def _():
        j = step - count
        df = df_ref[...]

        def product(at):
            return nt(df, wo_ref[at])

        ready = product(pieces[0])
        more, go, gi, sums = 0.0, [], [], []
        for i, at in enumerate(pieces):
            du = (ready * slope_ref[j, :, at]).astype(BF16)
            if i + 1 < len(pieces):
                ready = product(pieces[i + 1])
            if not comm:
                go.append(tn(hid_ref[j, :, at], df).astype(BF16))
            more = more + nt(du, wi_ref[:, at])
            gi.append(tn(a2b_ref[...], du).astype(BF16))
            sums.append(tn(du, jnp.ones((du.shape[0], PAIR), BF16)))
        acc_ref[...] += more
        gi, sums = jnp.concatenate(gi, axis=1), jnp.concatenate(sums, axis=0)
        quarter = width // gib_ref.shape[0]
        if gib_ref.shape[0] == 4:
            lane = lax.broadcasted_iota(jnp.int32, (quarter // 4, PAIR), 1)
            for i in range(4):
                part = sum(
                    jnp.where(lane == 17 + n, sums[(4 * i + n) * quarter // 4 : (4 * i + n + 1) * quarter // 4], 0.0)
                    for n in range(4)
                )
                gib_ref[i] = part
        else:
            gib_ref[0] = jnp.transpose(sums)[:1]
        if comm:
            at = pl.ds(pl.multiple_of(j * width, width), width)
            narrow = gwi_ref.shape[3]
            gi = gi.reshape(2, 2, 2, 2, narrow, width)
            gwi_ref[:, :, :, :, at] = jnp.where(c == 0, gi[:, :, :, 0], gi[:, :, :, 1])
            mi_ref[:, :, at] = jnp.where(c == 0, gi[:, :, :, 1], gi[:, :, :, 0]).reshape(8, narrow, width)
            chunk_copies(j).start()
        else:
            gwo_ref[...] = jnp.concatenate(go, axis=0)
            gwi_ref[...] = gi

    @pl.when(step == 2 * count)
    def _():
        d2 = acc_ref[...]
        n2 = n2_ref[...]
        dh2 = norm_back(d2, n2, r2_ref[:, :1], line(g2_ref))
        dh2_ref[...] = dh2
        dco = dh2.astype(BF16)
        dcc_ref[...] = nt(dco, wco_ref[...]).astype(BF16)
        gco_ref[...] = tn(cc_ref[...], dco).astype(BF16)
        small_ref[3:4] = total(d2 * n2)
        small_ref[4:5] = total(d2)
        small_ref[5:6] = total(dco)
        small_ref[6:8] = jnp.zeros((2, d2.shape[1]), F32)

    if comm:

        @pl.when(step == count)
        def _():
            narrow = gwi_ref.shape[3]
            for j in range(count):
                go = tn(hid_ref[j], df_ref[...]).astype(BF16).reshape(2, 2, 4, narrow, width)
                mo_ref[j] = jnp.where(c == 0, go[:, 1], go[:, 0])
                block_copies(j).start()
                for i in range(4):
                    gwi_ref[place_of(j, i)] = jnp.where(c == 0, go[:, 0, i], go[:, 1, i])

        @pl.when(step == count + 1)
        def _():
            for j in range(count):
                block_copies(j).wait()
                for i in range(4):
                    gwi_ref[place_of(j, i)] += co_ref[j, :, i]

        @pl.when(step > count)
        def _():
            j = step - count - 1
            at = pl.ds(pl.multiple_of(j * width, width), width)
            chunk_copies(j).wait()
            gwi_ref[:, :, :, :, at] += ci_ref[:, :, at].reshape(gwi_ref.shape[:-1] + (width,))


FEEDS = 19


def feed(size, comm, h1, cc, ct, wco, wi, wo, vectors, schedule):
    rows, width = h1.shape
    wide = wi.shape[1]
    chunk = width
    count = wide // chunk

    def weight(s):
        return jnp.where(s < count, s, jnp.minimum(s - count, count - 1))

    def early(s):
        return jnp.clip(s - count, 0, count - 1)

    flat = whole((rows, width))
    square = whole((width, width))
    scratch = [
        pltpu.VMEM((count, rows, chunk), BF16),
        pltpu.VMEM((count, rows, chunk), F32),
        pltpu.VMEM((rows, width), F32),
        pltpu.VMEM((rows, 128), F32),
        pltpu.VMEM((rows, width), BF16),
        pltpu.VMEM((rows, width), F32),
        pltpu.VMEM((rows, width), BF16),
        pltpu.VMEM((8, width), F32),
    ]
    if comm:
        narrow = width // size
        gib_shape = jax.ShapeDtypeStruct((size, narrow, PAIR), F32)
        gib_spec = pl.BlockSpec((4, narrow, PAIR), lambda s: (early(s), 0, 0))
        grad_specs = [whole((2, 2, 2, narrow, 2 * wide))]
        grad_shapes = [(2, 2, 2, narrow, 2 * wide)]
        scratch += [
            pltpu.VMEM((size // 2, narrow, wide), BF16),
            pltpu.VMEM((count, 2, 4, narrow, width), BF16),
            pltpu.VMEM((size // 2, narrow, wide), BF16),
            pltpu.VMEM((count, 2, 4, narrow, width), BF16),
            pltpu.SemaphoreType.DMA((2, count)),
            pltpu.SemaphoreType.DMA((2, count)),
        ]
    else:
        gib_shape = jax.ShapeDtypeStruct((count, 1, width), F32)
        gib_spec = pl.BlockSpec((1, 1, chunk), lambda s: (early(s), 0, 0))
        grad_specs = [
            pl.BlockSpec((width, chunk), lambda s: (0, early(s))),
            pl.BlockSpec((chunk, width), lambda s: (early(s), 0)),
        ]
        grad_shapes = [(width, wide), (wide, width)]
    return run(
        functools.partial(feed_kernel, count, comm), "feed", 2 * count + 1,
        (h1, cc, ct, wco, wi, wo) + tuple(vectors),
        [
            flat, flat, flat, square,
            pl.BlockSpec((width, chunk), lambda s: (0, weight(s))),
            pl.BlockSpec((chunk, width), lambda s: (weight(s), 0)),
        ]
        + [whole(v.shape) for v in vectors],
        [
            jax.ShapeDtypeStruct((rows, width), BF16),
            jax.ShapeDtypeStruct((rows, width), F32),
            jax.ShapeDtypeStruct((rows, width), BF16),
            jax.ShapeDtypeStruct((width, width), BF16),
        ]
        + [jax.ShapeDtypeStruct(a, BF16) for a in grad_shapes]
        + [jax.ShapeDtypeStruct((8, width), F32), gib_shape],
        [flat, flat, flat, square] + grad_specs + [whole((8, width)), gib_spec],
        scratch, schedule, 2,
        12 * rows * width * wide + 6 * rows * width * width, 12 * width * wide + 16 * rows * width,
        (("core",),) if comm else (),
    )


def outputs_kernel(moves, count, line, *refs):
    pieces, rest = refs[:count], refs[count:]
    out_ref, dx_ref, dm_ref = rest[:3]
    outs = rest[3:]
    for piece, first, wide, which, row, col in moves:
        ref = pieces[piece]
        outs[which][row : row + ref.shape[0], col : col + wide] = ref[:, first : first + wide].astype(F32)
    vectors, (turned, result, dx, dm) = outs[-4 - len(LINES) : -4], outs[-4:]
    lines = jnp.transpose(pieces[line[0]][:, line[1] : line[1] + PAIR].astype(F32))
    turned[...] = lines
    for ref, i in zip(vectors, LINES):
        ref[...] = lines[i]
    result[...] = out_ref[...]
    dx[...] = dx_ref[...]
    dm[...] = dm_ref[...]


LINES = (0, 1, 2, 3, 4, 5, 8, 9, 10, 11, 16, 21, 22)


def outputs(pieces, moves, line, shapes, out, dx, dm):
    ins = tuple(pieces) + (out, dx, dm)
    result = jax.ShapeDtypeStruct(out.shape, BF16)
    return pl.pallas_call(
        functools.partial(outputs_kernel, moves, len(pieces), line),
        out_shape=[jax.ShapeDtypeStruct(a, F32) for a in shapes]
        + [jax.ShapeDtypeStruct((pieces[0].shape[0],), F32)] * len(LINES)
        + [jax.ShapeDtypeStruct((PAIR, pieces[0].shape[0]), F32), result, result, result],
        compiler_params=params(),
        cost_estimate=cost(0, 12 << 20),
        name="outputs",
    )(*ins)


def moved(pieces, targets):
    out = []
    for n, (start, wide) in enumerate(pieces):
        for first, cols, which, row, col in targets:
            low, high = max(start, first), min(start + wide, first + cols)
            if low < high:
                out.append((n, low - start, high - low, which, row, col + low - first))
    return out


def schedule_of(flows, kernel):
    entries = [
        (start, order, name, start, stop)
        for order, name in enumerate(flows)
        for start, stop in (PLAN[name] + ((), (), ()))[kernel]
    ]
    return tuple(([flows[name]], start, stop) for _, _, name, start, stop in sorted(entries))


def swap_sum(part, axis, pairs):
    came = lax.ppermute(part, axis, pairs)
    return part.astype(F32) + came.astype(F32)


def sum_scatter(grad, size, order):
    rows, cols = grad.shape
    bits = size.bit_length() - 1
    me = lax.axis_index("dp")
    now = grad.reshape((2,) * bits + (rows // size, cols))
    left = list(range(bits))[::-1]
    for bit in [b for b in order if b < bits] + [b for b in range(bits) if b not in order]:
        axis = left.index(bit)
        mine = (me >> bit) & 1
        keep = lax.dynamic_index_in_dim(now, mine, axis, keepdims=False)
        send = lax.dynamic_index_in_dim(now, 1 - mine, axis, keepdims=False)
        came = lax.ppermute(send, "dp", [(i, i ^ (1 << bit)) for i in range(size)])
        now = (keep.astype(F32) + came.astype(F32)).astype(BF16)
        left.pop(axis)
    return swap_sum(now, "sp", [(0, 1), (1, 0)])


def per_device(
    size,
    inputs,
    memory,
    target_docs,
    memory_docs,
    cotangent,
    w_qkv,
    b_q,
    b_v,
    w_so,
    b_so,
    g_one,
    s_one,
    w_cq,
    b_cq,
    w_ckv,
    b_cv,
    w_co,
    b_co,
    g_two,
    s_two,
    w_fi,
    b_fi,
    w_fo,
    b_fo,
    g_three,
    s_three,
):
    rows, width = inputs.shape[1:]
    wide = b_fi.shape[0]
    comm = size == 16
    narrow, broad = width // size, wide // size
    x, mem, ct = inputs[0], memory[0], cotangent[0]
    qkv, mkv, kvo, mkvo, cq, ctx, cc, h1, x_o, mem_o, x, mem, ct, lse, clse, t_oth, m_oth, t_own, m_own = front(
        x, mem, ct, target_docs, memory_docs, w_qkv, w_ckv, w_so, w_cq, (b_q, b_v, b_cv, b_so, g_one, s_one, b_cq)
    )
    block = (2, 2, 2, 2, narrow) if comm else (width,)
    at_feed, at_cross, at_self, flows = (), (), (), {}
    if comm:
        joint = block[:3] + (narrow, 2 * wide)
        sources = {
            "T0i": (None, joint, BLOCK[:3]),
            "T0p": (None, joint, BLOCK[:3]),
            "T0o": (("ref", FEEDS), joint, BLOCK[:3]),
            "T1a": (("ref", MIDDLE), block + (3 * width,), BLOCK),
            "T1b": (None, block + (2 * width,), BLOCK),
            "G": (("ref", GRADS), block + (3 * width + PAIR,), BLOCK),
        }
        for name, (source, cols, hops, *_) in PLAN.items():
            array, shape, dims = sources[source]
            flows[name] = Flow(array, shape, hops, dims, cols)
        at_feed = schedule_of(flows, 5)
    output, dh2, dcc, gco, gwi, *gwo, small_a, gib = feed(
        size, comm, h1, cc, ct, w_co, w_fi, w_fo,
        (g_one, s_one, b_co, g_two, s_two, b_fo, g_three, s_three, b_fi), at_feed,
    )
    for name, flow in flows.items():
        if PLAN[name][0] in ("T0i", "T0p"):
            flow.array = gwi
    gib = gib.reshape(width, PAIR) if comm else gib.reshape(1, wide)

    if comm:
        at_cross = schedule_of(flows, 3)
        at_self = schedule_of(flows, 4)
    dm, dmo, gcvb, dh1, dsc, late, small_b, *early = cross_backward(
        block, cq, mkv, mkvo, dcc, cc, clse, t_own, m_own, m_oth, mem, mem_o, w_ckv,
        gco, dh2, h1, ctx, w_cq, w_so, g_one, s_one, at_cross,
    )
    for name, flow in flows.items():
        if PLAN[name][0] == "T1b":
            flow.array = late
    derivative, grad_memory, output, *made = self_backward(
        block, qkv, kvo, dsc, ctx, lse, t_own, t_oth, x, x_o, w_qkv, dh1, (small_a, small_b, gcvb, gib), dm, dmo, output, at_self
    )
    if comm:
        targets = {
            "T0i": [(0, wide, 2, 0, 0)],
            "T0o": [(wide + i * width, width, 3, i * narrow, 0) for i in range(4)],
            "T0p": [(wide + i * width, width, 3, i * narrow, 0) for i in range(4)],
            "T1a": [(0, width, 4, 0, 0), (width, 2 * width, 1, 0, 0)],
            "T1b": [(0, width, 5, 0, 0), (width, width, 6, 0, 0)],
            "G": [
                ((3 * pair + i) * PAIR, PAIR, 0, 0, i * width + pair * PAIR)
                for pair in range(width // PAIR)
                for i in range(3)
            ],
        }
        moves, line = [], None
        for n, (source, cols, *_) in enumerate(PLAN.values()):
            moves += [(n,) + m[1:] for m in moved([cols], targets[source])]
            if source == "G" and cols[0] <= 3 * width < sum(cols):
                line = n, 3 * width - cols[0]
        shapes = [(narrow, 3 * width), (narrow, 2 * width), (narrow, wide), (broad, width)] + [(narrow, width)] * 3
        t_qkv, t_cmem, t_fin, t_fout, t_cout, t_cquery, t_out, *vectors, lines, output, derivative, grad_memory = outputs(
            [f.array for f in flows.values()], moves, line, shapes, output, derivative, grad_memory
        )
    else:
        (early,), (made,) = early, made
        columns = made[:, 3 * width : 3 * width + PAIR]
        gqkv = made[:, : 3 * width].reshape(width, -1, 3, PAIR).swapaxes(1, 2).reshape(width, 3 * width)
        t_fin, t_fout, t_cout, t_cquery, t_out, t_cmem, t_qkv, lines = (
            sum_scatter(g, size, (0, 1, 2, 3))
            for g in (
                gwi, gwo[0], early[:, :width], late[:, :width], late[:, width:], early[:, width:], gqkv, columns
            )
        )
        lines = lines.T
    if not comm:
        vectors = [lines[i] for i in LINES]
    (t_gthree, t_sthree, t_fobias, t_gtwo, t_stwo, t_cobias, t_cqbias, t_gone, t_sone, t_obias, t_cvbias, t_qbias,
     t_vbias) = vectors
    if comm:
        t_fibias = lines[17:21].reshape(-1)
    else:
        t_fibias = lax.psum(lax.psum_scatter(gib[0], "dp", scatter_dimension=0, tiled=True), "sp")
    return (
        output[None],
        derivative[None],
        grad_memory[None],
        t_qkv,
        t_qbias,
        t_vbias,
        t_out,
        t_obias,
        t_gone,
        t_sone,
        t_cquery,
        t_cqbias,
        t_cmem,
        t_cvbias,
        t_cout,
        t_cobias,
        t_gtwo,
        t_stwo,
        t_fin,
        t_fibias,
        t_fout,
        t_fobias,
        t_gthree,
        t_sthree,
    )


def solution(mesh):
    split = P("dp", "sp", None)
    in_specs = (split, split, P("dp", "sp"), P("dp", "sp"), split) + (P(),) * 21
    matrix, vector = P("dp", None), P("dp")
    out_specs = (
        split, split, split,
        matrix, vector, vector,
        matrix, vector, vector, vector,
        matrix, vector,
        matrix, vector,
        matrix, vector, vector, vector,
        matrix, vector,
        matrix, vector, vector, vector,
    )
    return jax.shard_map(
        functools.partial(per_device, mesh.shape["dp"]),
        mesh=mesh, in_specs=in_specs, out_specs=out_specs, check_vma=False,
    )
```
